32 devices in a mesh: page: 8 (over z, core), query: 2 (over y), head: 2 (over x).
Axes of the slice: x: 2, y: 2, z: 4, core: 2. Of those that a mesh axis runs over, the one named last changes fastest.
Arguments:
- queries: float32 [8, 512, 128], P('head', 'query'), may hold values from -40 to 40
- compact_keys: float32 [8, 2048, 128], P('head', 'page'), may hold values from -4 to 4
- compact_values: float32 [8, 2048, 128], P('head', 'page'), may hold values from -6 to 6
- slot_bias: float32 [8, 2048], P('head', 'page'), may hold values from -0.25 to 0.25
- targets: float32 [8, 512, 128], P('head', 'query'), may hold values from -4 to 4
- positions: int32 [8, 512], P('head', 'query'), may hold values from 0 to 262143
- assignment: int32 [8], replicated, may hold values from 0 to 7, as said below
Outputs:
- new_keys: float32 [8, 2048, 128], P('head', 'page')
- new_values: float32 [8, 2048, 128], P('head', 'page')
- new_bias: float32 [8, 2048], P('head', 'page')
The draws below stay inside these ranges and needn't reach their ends.
Inputs may be any that keep to these rules, and one draw needn't show every extreme that they name: `assignment`: a permutation: every page 0 to 7 is held by exactly one page-axis block.
All inputs are finite; a program needn't handle non-finite values.
Results may differ from the reference program's by a relative error of at most 0.0003.
Values sent between devices are 32-bit elements; how exact they have to be, the bound alone decides.
No kernel may reach another device: no remote copies, remote signals or barrier semaphores. Data moves between devices by JAX's collectives and lax.ppermute only.
A program may use at most 64 MiB of HBM per device.

```python
import math
import jax
import jax.numpy as jnp
from jax import lax

KV_HEADS = 8
HD = 128
SLOT_DEV = 256
STEPS = 2
PAGE_LEN = 32768
SLOTS = 2048
QN = 512
CONTEXT = 262144
N_PAGE = 8


def common_draw(key):
    assign_order = jax.random.permutation(jax.random.fold_in(key, 11), N_PAGE).astype(jnp.int32)
    key_seed = jax.random.fold_in(key, 12)
    query_seed = jax.random.fold_in(key, 13)
    slot_keys = jax.random.truncated_normal(key_seed, -4.0, 4.0, (KV_HEADS, SLOTS, HD), jnp.float32)
    query_rows = jax.random.truncated_normal(query_seed, -4.0, 4.0, (KV_HEADS, QN, HD), jnp.float32)
    return (assign_order, slot_keys, query_rows)


def draw_assignment(key, part):
    return common_draw(key)[0]


def draw_compact_keys(key, part):
    return common_draw(key)[1]


def draw_queries(key, part):
    return common_draw(key)[2]


def with_ends(result, key, least, largest):
    place = [jax.random.randint(jax.random.fold_in(key, axis), (), 0, length) for axis, length in enumerate(result.shape)]
    main_axis = result.shape.index(max(result.shape))
    next_to = place[:main_axis] + [(place[main_axis] + 1) % result.shape[main_axis]] + place[main_axis + 1:]
    return result.at[tuple(place)].set(least).at[tuple(next_to)].set(largest)


def level_of(own_key, shape, shards, smallest, top_value):
    level, own = 1.0, jax.random.fold_in(own_key, 6)
    for axis_at, parts in shards:
        draws = jnp.exp(jax.random.uniform(jax.random.fold_in(own, axis_at), (parts,), jnp.float32, smallest / len(shards), top_value / len(shards)))
        level = level * jnp.repeat(draws, shape[axis_at] // parts).reshape([-1 if axis == axis_at else 1 for axis in range(len(shape))])
    return level


def gaussian(own_key, dims, deviation, most, shards=(), kind=jnp.bfloat16):
    level = level_of(own_key, dims, shards, -0.22, 0.18) if shards else 1.0
    result = jax.random.normal(own_key, dims, jnp.float32) * deviation * level
    return jnp.minimum(jnp.maximum(result, -most), most).astype(kind)


def setup_inputs(seed: int = 0) -> dict:
    key_of = jax.random.split(jax.random.key(seed), 8)
    return {
        "queries": draw_queries(jax.random.fold_in(key_of[7], 71), 0),
        "compact_keys": draw_compact_keys(jax.random.fold_in(key_of[7], 71), 0),
        "compact_values": gaussian(key_of[2], (KV_HEADS, SLOTS, HD), 1.0, 6.0, ((0, 2), (1, 8)), jnp.float32),
        "slot_bias": jnp.clip(jax.random.uniform(key_of[3], (KV_HEADS, SLOTS), jnp.float32, -0.25, 0.25) * level_of(key_of[3], (KV_HEADS, SLOTS), ((0, 2), (1, 8)), -0.4, 0.0), -0.25, 0.25),
        "targets": gaussian(key_of[4], (KV_HEADS, QN, HD), 0.5, 4.0, ((0, 2), (1, 2)), jnp.float32),
        "positions": with_ends(jax.random.randint(key_of[5], (KV_HEADS, QN), 0, CONTEXT), jax.random.fold_in(key_of[5], 1), 0, CONTEXT - 1).astype(jnp.int32),
        "assignment": draw_assignment(jax.random.fold_in(key_of[7], 71), 0),
    }


MASKED = -1e+30
EPSILON = 1e-06
RATE_KEYS = 0.05
RATE_VALUES = 0.05
RATE_BIAS = 0.2
HIGHEST = lax.Precision.HIGHEST

def reference(queries, compact_keys, compact_values, slot_bias, targets, positions, assignment):
    score_scale = 1.0 / math.sqrt(HD)
    slot_page = assignment[jnp.arange(SLOTS, dtype=jnp.int32) // SLOT_DEV]

    def head_gradients(inputs):
        query_rows, key_rows, value_rows, bias_row, target_rows, position_row = inputs
        visible = slot_page[None, :] <= (position_row // PAGE_LEN)[:, None]
        scores = jnp.dot(query_rows, key_rows.T, precision=HIGHEST) * score_scale + bias_row[None, :]
        scores = jnp.where(visible, scores, MASKED)
        row_max = lax.optimization_barrier(jnp.max(scores, axis=1))
        weights = jnp.where(visible, jnp.exp(scores - row_max[:, None]), 0.0)
        row_total = lax.optimization_barrier(jnp.sum(weights, axis=1))
        attention = weights / row_total[:, None]
        output = jnp.dot(attention, value_rows, precision=HIGHEST)
        residual = output - target_rows
        grad_values = jnp.dot(attention.T, residual, precision=HIGHEST)
        row_delta = lax.optimization_barrier(jnp.sum(residual * output, axis=1))
        grad_probs = jnp.dot(residual, value_rows.T, precision=HIGHEST)
        grad_scores = attention * (grad_probs - row_delta[:, None])
        grad_bias = lax.optimization_barrier(jnp.sum(grad_scores, axis=0))
        grad_keys = jnp.dot(grad_scores.T, query_rows, precision=HIGHEST) * score_scale
        return (grad_keys, grad_values, grad_bias)
    key_state, value_state, bias_state = (compact_keys, compact_values, slot_bias)
    for repeat in range(STEPS):
        grad_keys, grad_values, grad_bias = lax.map(head_gradients, (queries, key_state, value_state, bias_state, targets, positions))
        rms_keys = jnp.sqrt(jnp.sum(grad_keys * grad_keys) / (KV_HEADS * SLOTS * HD) + EPSILON)
        rms_values = jnp.sqrt(jnp.sum(grad_values * grad_values) / (KV_HEADS * SLOTS * HD) + EPSILON)
        rms_bias = jnp.sqrt(jnp.sum(grad_bias * grad_bias) / (KV_HEADS * SLOTS) + EPSILON)
        key_state = key_state - RATE_KEYS * grad_keys / rms_keys
        value_state = value_state - RATE_VALUES * grad_values / rms_values
        bias_state = bias_state - RATE_BIAS * grad_bias / rms_bias
    return (key_state, value_state, bias_state)
```

```python
import itertools
import math

import jax
import jax.numpy as jnp
from jax import lax
from jax.experimental import pallas as pl
from jax.experimental.pallas import tpu as pltpu
from jax.sharding import PartitionSpec as P

STEPS = 2
PAGE_LEN = 32768


MASKED = -1e30
EPSILON = 1e-06
RATE_KEYS = 0.05
RATE_VALUES = 0.05
RATE_BIAS = 0.2
HIGHEST = lax.Precision.HIGHEST
TAIL = 8
CORES = 2


def send(value, axes, move):
    sizes = [lax.axis_size(axis) for axis in axes]

    def flat(place):
        index = 0
        for size, at in zip(sizes, place):
            index = index * size + at % size
        return index

    pairs = [
        (flat(place), flat(move(*place))) for place in itertools.product(*map(range, sizes))
    ]
    return lax.ppermute(value, axes, pairs)


def dot(left, right, left_dim, right_dim):
    return lax.dot_general(
        left,
        right,
        (((left_dim,), (right_dim,)), ((), ())),
        precision=HIGHEST,
        preferred_element_type=jnp.float32,
    )


def call(body, out_shapes, name, cost, scalars, blocks, scratch=()):
    def whole(shape):
        return pl.BlockSpec(shape, lambda step, numbers: (0,) * len(shape))

    arrays, specs = [], []
    for block in blocks:
        if isinstance(block, tuple):
            array, shape, index = block
            arrays.append(array)
            specs.append(pl.BlockSpec(shape, index))
        else:
            arrays.append(block)
            specs.append(whole(block.shape))
    return pl.pallas_call(
        body,
        out_shape=[jax.ShapeDtypeStruct(shape, jnp.float32) for shape in out_shapes],
        grid_spec=pltpu.PrefetchScalarGridSpec(
            num_scalar_prefetch=1,
            grid=(1,),
            in_specs=specs,
            out_specs=[whole(shape) for shape in out_shapes],
            scratch_shapes=scratch,
        ),
        compiler_params=pltpu.CompilerParams(vmem_limit_bytes=48 * 2**20),
        cost_estimate=pl.CostEstimate(flops=cost, bytes_accessed=2**20, transcendentals=0),
        name=name,
    )(scalars, *arrays)


def row_as_tail(row, width):
    rows = [row[:, at : at + width] for at in range(0, row.shape[1], width)]
    rows.append(jnp.zeros((TAIL - len(rows), width), row.dtype))
    return jnp.concatenate(rows, axis=0)


def tail_as_row(ref, start, count):
    return jnp.concatenate([ref[start + at : start + at + 1, :] for at in range(count)], axis=1)


def row_as_column(row, width):
    parts = []
    for at in range(0, row.shape[1], width):
        parts.append(jnp.broadcast_to(row[:, at : at + width], (width, width)).T)
    return jnp.concatenate(parts, axis=0)


def direct_plan_fits(mesh, queries, compact_keys):
    pages, query_devices, head_devices = (mesh.shape[axis] for axis in ("page", "query", "head"))
    local_heads = queries.shape[0] // head_devices
    part_rows = queries.shape[1] // query_devices
    slot_rows = compact_keys.shape[1] // pages
    width = queries.shape[2]
    if pages % CORES or local_heads != CORES * query_devices or width % 128:
        return False
    ranks = pages // CORES
    chunk = part_rows * query_devices // ranks
    return (
        part_rows * query_devices % ranks == 0
        and chunk % 128 == 0
        and part_rows % chunk == 0
        and slot_rows % width == 0
        and part_rows % width == 0
        and max(slot_rows, part_rows) <= TAIL * width
    )


def direct_per_device(
    queries, compact_keys, compact_values, slot_bias, targets, positions, assignment
):
    local_heads, part_rows, width = queries.shape
    slot_rows = compact_keys.shape[1]
    query_devices = lax.axis_size("query")
    head_devices = lax.axis_size("head")
    ranks = lax.axis_size("page") // CORES
    query_rows = part_rows * query_devices
    chunk = query_rows // ranks
    slot_total = local_heads * head_devices * slot_rows * lax.axis_size("page")
    entry_total = slot_total * width
    score_scale = 1.0 / math.sqrt(width)
    slots = CORES * slot_rows
    pos_rows = part_rows // width
    bias_rows = slot_rows // width
    packed_rows = 2 * slot_rows + TAIL
    matmul_cost = 2 * slots * query_rows * width

    page = lax.axis_index("page")
    rank, core = page // CORES, page % CORES
    me = lax.axis_index("query")
    own_head = CORES * me + core

    def part_of(z):
        return z * chunk // part_rows

    chunk_part = rank * chunk // part_rows
    target_head = CORES * lax.rem(me - chunk_part + query_devices, query_devices) + core
    target_block = lax.rem(rank, part_rows // chunk)
    send_heads = [
        CORES * lax.rem(me - turn + query_devices, query_devices) + core
        for turn in range(1, query_devices)
    ]
    mate_head = CORES * me + (CORES - 1 - core)
    mate_page = CORES * rank + (CORES - 1 - core)

    prep_numbers = jnp.stack(
        [own_head, mate_head, target_head, target_block, *send_heads]
    ).astype(jnp.int32)

    def prep_body(numbers, *refs):
        positions_ref, bias_ref, targets_ref, *refs = refs
        key_refs, refs = refs[:2], refs[2:]
        value_refs, refs = refs[:2], refs[2:]
        query_refs, refs = refs[:query_devices], refs[query_devices:]
        state_outs, refs = refs[:2], refs[2:]
        query_outs, (targets_out,) = refs[:query_devices], refs[query_devices:]
        for turn in range(query_devices):
            head = numbers[0] if turn == 0 else numbers[3 + turn]
            query_outs[turn][:part_rows, :] = query_refs[turn][0]
            row = positions_ref[pl.ds(head, 1), :].astype(jnp.float32)
            query_outs[turn][part_rows:, :] = row_as_tail(row, width)
        for at in range(2):
            state_outs[at][:slot_rows, :] = key_refs[at][0]
            state_outs[at][slot_rows : 2 * slot_rows, :] = value_refs[at][0]
            row = bias_ref[pl.ds(numbers[at], 1), :]
            state_outs[at][2 * slot_rows :, :] = row_as_tail(row, width)
        targets_out[...] = targets_ref[0]

    def head_block(array, number):
        shape = (1,) + array.shape[1:]
        return (array, shape, lambda step, numbers: (numbers[number], 0, 0))

    targets_block = (
        targets,
        (1, chunk, width),
        lambda step, numbers: (numbers[2], numbers[3], 0),
    )
    packed = call(
        prep_body,
        [(packed_rows, width)] * 2 + [(part_rows + TAIL, width)] * query_devices + [(chunk, width)],
        "pack",
        2**20,
        prep_numbers,
        [positions, slot_bias, targets_block]
        + [head_block(compact_keys, at) for at in range(2)]
        + [head_block(compact_values, at) for at in range(2)]
        + [head_block(queries, 0)]
        + [head_block(queries, 3 + turn) for turn in range(1, query_devices)],
    )
    own_state, mate_state = packed[0], packed[1]
    query_parts = [packed[2]] + [
        send(packed[2 + turn], ("query",), lambda y, turn=turn: (y - turn,))
        for turn in range(1, query_devices)
    ]
    states = [own_state, send(mate_state, ("page",), lambda p: (p + 1 - 2 * (p % CORES),))]
    chunk_targets = send(
        packed[2 + query_devices],
        ("page", "query"),
        lambda p, y: (p, y - part_of(p // CORES)),
    )

    to_chunks = [lax.rem(rank + turn, ranks) for turn in range(ranks)]
    from_chunks = [lax.rem(rank - turn + ranks, ranks) for turn in range(ranks)]
    numbers = jnp.stack(
        [assignment[page] * PAGE_LEN, assignment[mate_page] * PAGE_LEN, *to_chunks, *from_chunks]
    ).astype(jnp.int32)

    def along_rank(value, turn):
        return send(value, ("page",), lambda p: (p + CORES * turn,))

    def step_sizes(tile_refs):
        tile = tile_refs[0][...]
        for ref in tile_refs[1:]:
            tile = tile + ref[...]
        sums = jnp.sum(tile, axis=1, keepdims=True)
        return (
            RATE_KEYS / jnp.sqrt(sums[0:1] / entry_total + EPSILON),
            RATE_VALUES / jnp.sqrt(sums[1:2] / entry_total + EPSILON),
            RATE_BIAS / jnp.sqrt(sums[2:3] / slot_total + EPSILON),
        )

    def updated(state_ref, grad_ref, sizes):
        key_end, value_end = slot_rows, 2 * slot_rows
        return (
            state_ref[:key_end, :] - sizes[0] * grad_ref[:key_end, :],
            state_ref[key_end:value_end, :] - sizes[1] * grad_ref[key_end:value_end, :],
            state_ref[value_end:, :] - sizes[2] * grad_ref[value_end:, :],
        )

    def forward(state_refs, query_refs, number_ref, chunk_outs, weights_out, max_out, chunks):
        all_queries = jnp.concatenate([ref[:part_rows, :] for ref in query_refs], axis=0)
        position_row = jnp.concatenate(
            [tail_as_row(ref, part_rows, pos_rows) for ref in query_refs], axis=1
        )
        all_scores, all_visible = [], []
        for at, ref in enumerate(state_refs):
            scores = dot(ref[:slot_rows, :], all_queries, 1, 1) * score_scale
            bias = row_as_column(tail_as_row(ref, 2 * slot_rows, bias_rows), width)
            scores = scores + jnp.concatenate([bias] * (query_rows // width), axis=1)
            page_start = number_ref[at].astype(jnp.float32)
            visible = jnp.broadcast_to(position_row, scores.shape) >= page_start
            all_scores.append(jnp.where(visible, scores, MASKED))
            all_visible.append(visible)
        row_max = jnp.max(all_scores[0], axis=0, keepdims=True)
        for scores in all_scores[1:]:
            row_max = jnp.maximum(row_max, jnp.max(scores, axis=0, keepdims=True))
        row_total = jnp.zeros_like(row_max)
        row_sum = jnp.zeros((width, query_rows), jnp.float32)
        for at, ref in enumerate(state_refs):
            weights = jnp.where(all_visible[at], jnp.exp(all_scores[at] - row_max), 0.0)
            weights_out[at * slot_rows : (at + 1) * slot_rows, :] = weights
            row_total = row_total + jnp.sum(weights, axis=0, keepdims=True)
            row_sum = row_sum + dot(ref[slot_rows : 2 * slot_rows, :], weights, 0, 0)
        max_out[...] = jnp.broadcast_to(row_max, (TAIL, query_rows))
        tail = jnp.concatenate(
            [row_max, row_total, jnp.zeros((TAIL - 2, query_rows), jnp.float32)], axis=0
        )
        for at in range(ranks):
            columns = slice(at * chunk, (at + 1) * chunk)
            chunks[at, :width, :] = row_sum[:, columns]
            chunks[at, width:, :] = tail[:, columns]
        for turn in range(ranks):
            chunk_outs[turn][...] = chunks[number_ref[2 + turn]]

    forward_shapes = (
        [(width + TAIL, chunk)] * ranks + [(slots, query_rows), (TAIL, query_rows)]
    )
    chunk_scratch = [pltpu.VMEM((ranks, width + TAIL, chunk), jnp.float32)]

    def first_body(number_ref, *refs):
        state_refs, refs = refs[:2], refs[2:]
        query_refs, refs = refs[:query_devices], refs[query_devices:]
        chunk_outs, (weights_out, max_out, chunks) = refs[:ranks], refs[ranks:]
        forward(state_refs, query_refs, number_ref, chunk_outs, weights_out, max_out, chunks)

    def next_body(number_ref, *refs):
        state_refs, refs = refs[:2], refs[2:]
        query_refs, refs = refs[:query_devices], refs[query_devices:]
        grad_refs, refs = refs[:2], refs[2:]
        tile_refs, refs = refs[:ranks], refs[ranks:]
        state_outs, refs = refs[:2], refs[2:]
        chunk_outs, (weights_out, max_out, chunks) = refs[:ranks], refs[ranks:]
        sizes = step_sizes(tile_refs)
        for at in range(2):
            keys, values, bias = updated(state_refs[at], grad_refs[at], sizes)
            state_outs[at][:slot_rows, :] = keys
            state_outs[at][slot_rows : 2 * slot_rows, :] = values
            state_outs[at][2 * slot_rows :, :] = bias
        forward(state_outs, query_refs, number_ref, chunk_outs, weights_out, max_out, chunks)

    def merge_body(number_ref, targets_ref, *refs):
        chunk_refs, (merged_out,) = refs[:ranks], refs[ranks:]
        row_max = chunk_refs[0][width : width + 1, :]
        for ref in chunk_refs[1:]:
            row_max = jnp.maximum(row_max, ref[width : width + 1, :])
        row_total = jnp.zeros_like(row_max)
        row_sum = jnp.zeros((width, chunk), jnp.float32)
        for ref in chunk_refs:
            factor = jnp.exp(ref[width : width + 1, :] - row_max)
            row_total = row_total + ref[width + 1 : width + 2, :] * factor
            row_sum = row_sum + ref[:width, :] * factor
        output = row_sum / row_total
        residual = output - targets_ref[...].T
        row_delta = jnp.sum(residual * output, axis=0, keepdims=True)
        merged_out[:width, :] = residual
        merged_out[width:, :] = jnp.concatenate(
            [row_max, row_total, row_delta, jnp.zeros((TAIL - 3, chunk), jnp.float32)], axis=0
        )

    def backward_body(number_ref, *refs):
        weights_ref, max_ref, *refs = refs
        state_refs, refs = refs[:2], refs[2:]
        query_refs, refs = refs[:query_devices], refs[query_devices:]
        merged_refs, refs = refs[:ranks], refs[ranks:]
        grad_outs, (squares_out, chunks) = refs[:2], refs[2:]
        for turn in range(ranks):
            chunks[number_ref[2 + ranks + turn]] = merged_refs[turn][...]
        joined = jnp.concatenate([chunks[at] for at in range(ranks)], axis=1)
        residual = joined[:width, :]
        row_max, row_total, row_delta = (
            joined[width + at : width + at + 1, :] for at in range(3)
        )
        all_queries = jnp.concatenate([ref[:part_rows, :] for ref in query_refs], axis=0)
        factor = jnp.exp(max_ref[0:1, :] - row_max) / row_total
        ones = jnp.ones((TAIL, query_rows), jnp.float32)
        squares = [jnp.zeros((1, width), jnp.float32)] * 3
        for at, ref in enumerate(state_refs):
            attention = weights_ref[at * slot_rows : (at + 1) * slot_rows, :] * factor
            grad_values = dot(attention, residual, 1, 1)
            grad_probs = dot(ref[slot_rows : 2 * slot_rows, :], residual, 1, 0)
            grad_scores = attention * (grad_probs - row_delta)
            grad_keys = dot(grad_scores, all_queries, 1, 0) * score_scale
            grad_bias = row_as_tail(dot(ones, grad_scores, 1, 1)[0:1, :], width)
            grad_outs[at][:slot_rows, :] = grad_keys
            grad_outs[at][slot_rows : 2 * slot_rows, :] = grad_values
            grad_outs[at][2 * slot_rows :, :] = grad_bias
            for which, grad in enumerate((grad_keys, grad_values, grad_bias)):
                squares[which] = squares[which] + jnp.sum(grad * grad, axis=0, keepdims=True)
        squares_out[...] = jnp.concatenate(
            squares + [jnp.zeros((TAIL - 3, width), jnp.float32)], axis=0
        )

    def to_outputs(packs):
        received = []
        for turn in range(query_devices):
            for flip in range(CORES):
                if turn == 0 and flip == 0:
                    received.append(packs[0])
                else:
                    received.append(
                        send(
                            packs[flip],
                            ("page", "query"),
                            lambda p, y, turn=turn, flip=flip: (
                                p + flip * (1 - 2 * (p % CORES)),
                                y + turn,
                            ),
                        )
                    )
        return received

    def over_block(tile):
        total = tile
        for dc, dy, dx in itertools.product(
            range(CORES), range(query_devices), range(head_devices)
        ):
            if dc or dy or dx:
                total = total + send(
                    tile,
                    ("page", "query", "head"),
                    lambda p, y, x, dc=dc, dy=dy, dx=dx: (
                        p + dc * (1 - 2 * (p % CORES)),
                        y + dy,
                        x + dx,
                    ),
                )
        return total

    state_copies, grads, tiles = None, None, None
    for repeat in range(STEPS):
        if repeat == 0:
            *chunk_parts, weights, maxima = call(
                first_body,
                forward_shapes,
                "forward",
                6 * 2 * matmul_cost,
                numbers,
                states + query_parts,
                chunk_scratch,
            )
        else:
            own_new, mate_new, *chunk_parts, weights, maxima = call(
                next_body,
                [(packed_rows, width)] * 2 + forward_shapes,
                "update_forward",
                6 * 2 * matmul_cost,
                numbers,
                states + query_parts + grads + tiles,
                chunk_scratch,
            )
            states = [own_new, mate_new]
            state_copies = states
        arrived = [chunk_parts[0]] + [
            along_rank(chunk_parts[turn], turn) for turn in range(1, ranks)
        ]
        (merged,) = call(
            merge_body,
            [(width + TAIL, chunk)],
            "merge",
            2**20,
            numbers,
            [chunk_targets] + arrived,
        )
        all_merged = [merged] + [along_rank(merged, turn) for turn in range(1, ranks)]
        own_grad, mate_grad, squares = call(
            backward_body,
            [(packed_rows, width)] * 2 + [(TAIL, width)],
            "backward",
            6 * 3 * matmul_cost,
            numbers,
            [weights, maxima] + states + query_parts + all_merged,
            chunk_scratch,
        )
        grads = [own_grad, mate_grad]
        block_squares = over_block(squares)
        tiles = [block_squares] + [
            along_rank(block_squares, turn) for turn in range(1, ranks)
        ]

    all_states = to_outputs(state_copies)
    all_grads = to_outputs(grads)
    out_heads = jnp.stack(
        [
            CORES * lax.rem(me - turn + query_devices, query_devices)
            + (core if flip == 0 else CORES - 1 - core)
            for turn in range(query_devices)
            for flip in range(CORES)
        ]
    ).astype(jnp.int32)

    def last_body(number_ref, *refs):
        state_refs, refs = refs[:local_heads], refs[local_heads:]
        grad_refs, refs = refs[:local_heads], refs[local_heads:]
        tile_refs, (keys_out, values_out, bias_out) = refs[:ranks], refs[ranks:]
        sizes = step_sizes(tile_refs)
        for at in range(local_heads):
            keys, values, bias = updated(state_refs[at], grad_refs[at], sizes)
            head = number_ref[at]
            keys_out[head] = keys
            values_out[head] = values
            bias_row = jnp.concatenate([bias[row : row + 1] for row in range(bias_rows)], axis=1)
            bias_out[pl.ds(head, 1), :] = bias_row

    return tuple(
        call(
            last_body,
            [compact_keys.shape, compact_values.shape, slot_bias.shape],
            "last_update",
            2**20,
            out_heads,
            all_states + all_grads + tiles,
        )
    )


def from_partner(value, axis, stride):
    mask = 2**stride
    pairs = [(source, source ^ mask) for source in range(lax.axis_size(axis))]
    return lax.ppermute(value, axis, pairs)


def squared_sums(grad_keys, grad_values, grad_bias):
    return jnp.stack(
        [
            jnp.sum(grad_keys * grad_keys),
            jnp.sum(grad_values * grad_values),
            jnp.sum(grad_bias * grad_bias),
        ]
    )


def apply_update(states, grads, totals, entry_count, slot_total):
    key_state, value_state, bias_state = states
    grad_keys, grad_values, grad_bias = grads
    rms_keys = jnp.sqrt(totals[0] / entry_count + EPSILON)
    rms_values = jnp.sqrt(totals[1] / entry_count + EPSILON)
    rms_bias = jnp.sqrt(totals[2] / slot_total + EPSILON)
    return (
        key_state - RATE_KEYS * grad_keys / rms_keys,
        value_state - RATE_VALUES * grad_values / rms_values,
        bias_state - RATE_BIAS * grad_bias / rms_bias,
    )


def local_gradients(queries, targets, visible, compact_keys, compact_values, slot_bias):
    score_scale = 1.0 / math.sqrt(queries.shape[2])
    scores = jnp.einsum("hqd,hsd->hqs", queries, compact_keys, precision=HIGHEST) * score_scale
    scores = jnp.where(visible, scores + slot_bias[:, None, :], MASKED)
    local_max = jnp.max(scores, axis=2)
    row_max = lax.pmax(local_max, "page")
    weights = jnp.where(visible, jnp.exp(scores - row_max[:, :, None]), 0.0)
    local_sum = jnp.einsum("hqs,hsd->hqd", weights, compact_values, precision=HIGHEST)
    row_total, row_sum = lax.psum((jnp.sum(weights, axis=2), local_sum), "page")
    attention = weights / row_total[:, :, None]
    output = row_sum / row_total[:, :, None]
    residual = output - targets
    grad_values = jnp.einsum("hqs,hqd->hsd", attention, residual, precision=HIGHEST)
    row_delta = jnp.sum(residual * output, axis=2)
    grad_probs = jnp.einsum("hqd,hsd->hqs", residual, compact_values, precision=HIGHEST)
    grad_scores = attention * (grad_probs - row_delta[:, :, None])
    grad_bias = jnp.sum(grad_scores, axis=1)
    grad_keys = jnp.einsum("hqs,hqd->hsd", grad_scores, queries, precision=HIGHEST) * score_scale
    return (grad_keys, grad_values, grad_bias)


def per_device(queries, compact_keys, compact_values, slot_bias, targets, positions, assignment):
    page_number = assignment[lax.axis_index("page")]
    local_heads = compact_keys.shape[0]
    slot_total = local_heads * lax.axis_size("head") * compact_keys.shape[1] * lax.axis_size("page")
    entry_count = slot_total * compact_keys.shape[2]
    query_count = lax.axis_size("query")
    heads_kept = max(local_heads // query_count, 1)
    query_parts = max(query_count // local_heads, 1)
    part_rows = queries.shape[1] // query_parts

    def split_items(array):
        width = array.shape[2]
        array = array.reshape(local_heads // heads_kept, heads_kept, query_parts, part_rows, width)
        array = jnp.transpose(array, (0, 2, 1, 3, 4))
        return array.reshape(query_count, heads_kept, part_rows, width)

    def join_items(array):
        width = array.shape[3]
        array = jnp.transpose(array, (1, 0, 2, 3))
        return array.reshape(heads_kept, query_count * part_rows, width)

    position_column = positions.astype(jnp.float32)[:, :, None]
    got_queries, got_targets, got_positions = (
        lax.all_to_all(split_items(queries), "query", split_axis=0, concat_axis=0, tiled=True),
        lax.all_to_all(split_items(targets), "query", split_axis=0, concat_axis=0, tiled=True),
        lax.all_to_all(
            split_items(position_column), "query", split_axis=0, concat_axis=0, tiled=True
        ),
    )
    group_queries = join_items(got_queries)
    group_targets = join_items(got_targets)
    group_positions = join_items(got_positions)[:, :, 0]
    visible = (page_number.astype(jnp.float32) <= jnp.floor(group_positions / PAGE_LEN))[:, :, None]
    query_index = lax.axis_index("query")
    first_head = query_index // query_parts * heads_kept
    key_state = lax.dynamic_slice_in_dim(compact_keys, first_head, heads_kept, 0)
    value_state = lax.dynamic_slice_in_dim(compact_values, first_head, heads_kept, 0)
    bias_state = lax.dynamic_slice_in_dim(slot_bias, first_head, heads_kept, 0)
    counted = (query_index % query_parts == 0).astype(jnp.float32)
    for repeat in range(STEPS):
        grads = local_gradients(
            group_queries, group_targets, visible, key_state, value_state, bias_state
        )
        for bit in range(query_parts.bit_length() - 1):
            partner = from_partner((grads[0], grads[1], grads[2]), "query", bit)
            grads = (grads[0] + partner[0], grads[1] + partner[1], grads[2] + partner[2])
        totals = lax.psum(
            squared_sums(grads[0], grads[1], grads[2]) * counted, ("page", "query", "head")
        )
        key_state, value_state, bias_state = apply_update(
            (key_state, value_state, bias_state), grads, totals, entry_count, slot_total
        )
    all_keys, all_values, all_bias = (
        lax.all_gather(key_state, "query", axis=0, tiled=True),
        lax.all_gather(value_state, "query", axis=0, tiled=True),
        lax.all_gather(bias_state, "query", axis=0, tiled=True),
    )
    slot_rows = compact_keys.shape[1]
    head_width = compact_keys.shape[2]
    all_keys = all_keys.reshape(
        local_heads // heads_kept, query_parts, heads_kept, slot_rows, head_width
    )[:, 0]
    all_values = all_values.reshape(
        local_heads // heads_kept, query_parts, heads_kept, slot_rows, head_width
    )[:, 0]
    all_bias = all_bias.reshape(local_heads // heads_kept, query_parts, heads_kept, slot_rows)[:, 0]
    return (
        all_keys.reshape(local_heads, slot_rows, head_width),
        all_values.reshape(local_heads, slot_rows, head_width),
        all_bias.reshape(local_heads, slot_rows),
    )


def solution(mesh):
    placed = (
        P("head", "query", None),
        P("head", "page", None),
        P("head", "page", None),
        P("head", "page"),
        P("head", "query", None),
        P("head", "query"),
        P(),
    )

    def program(*args):
        plan = direct_per_device if direct_plan_fits(mesh, args[0], args[1]) else per_device
        return jax.shard_map(
            plan,
            mesh=mesh,
            in_specs=placed,
            out_specs=(P("head", "page", None), P("head", "page", None), P("head", "page")),
            check_vma=False,
        )(*args)

    return program
```

```python
import itertools
import math

import jax
import jax.numpy as jnp
from jax import lax
from jax.experimental import pallas as pl
from jax.experimental.pallas import tpu as pltpu
from jax.sharding import PartitionSpec as P

STEPS = 2
PAGE_LEN = 32768


MASKED = -1e30
EPSILON = 1e-06
RATE_KEYS = 0.05
RATE_VALUES = 0.05
RATE_BIAS = 0.2
HIGHEST = lax.Precision.HIGHEST
TAIL = 8
CORES = 2


def exchange(value, **masks):
    axes = tuple(masks)
    sizes = [lax.axis_size(axis) for axis in axes]

    def flat(place):
        index = 0
        for size, at in zip(sizes, place):
            index = index * size + at
        return index

    pairs = [
        (flat(place), flat([at ^ mask for at, mask in zip(place, masks.values())]))
        for place in itertools.product(*map(range, sizes))
    ]
    return lax.ppermute(value, axes, pairs)


def dot(left, right, left_dim, right_dim):
    return lax.dot_general(
        left,
        right,
        (((left_dim,), (right_dim,)), ((), ())),
        precision=HIGHEST,
        preferred_element_type=jnp.float32,
    )


def call(body, out_shapes, name, cost, operands, spaces=(), scratch=(), after=()):
    spaces = list(spaces) + [pltpu.VMEM] * (len(operands) - len(spaces)) + [pl.ANY] * len(after)
    count = len(operands)

    def without_after(*refs):
        body(*refs[:count], *refs[count + len(after) :])

    return pl.pallas_call(
        without_after,
        out_shape=[jax.ShapeDtypeStruct(shape, jnp.float32) for shape in out_shapes],
        in_specs=[pl.BlockSpec(memory_space=space) for space in spaces],
        out_specs=[pl.BlockSpec(memory_space=pltpu.VMEM) for _ in out_shapes],
        scratch_shapes=scratch,
        compiler_params=pltpu.CompilerParams(vmem_limit_bytes=32 * 2**20),
        cost_estimate=pl.CostEstimate(flops=cost, bytes_accessed=2**20, transcendentals=0),
        name=name,
    )(*operands, *after)


def row_as_tail(row, width):
    rows = [row[:, at : at + width] for at in range(0, row.shape[1], width)]
    rows.append(jnp.zeros((TAIL - len(rows), width), row.dtype))
    return jnp.concatenate(rows, axis=0)


def tail_as_row(ref, start, count):
    return jnp.concatenate([ref[start + at : start + at + 1, :] for at in range(count)], axis=1)


def row_as_column(row, width):
    parts = []
    for at in range(0, row.shape[1], width):
        parts.append(jnp.broadcast_to(row[:, at : at + width], (width, width)).T)
    return jnp.concatenate(parts, axis=0)


def direct_plan_fits(mesh, queries, compact_keys):
    sizes = [mesh.shape[axis] for axis in ("page", "query", "head")]
    pages, query_devices, head_devices = sizes
    local_heads = queries.shape[0] // head_devices
    part_rows = queries.shape[1] // query_devices
    slot_rows = compact_keys.shape[1] // pages
    width = queries.shape[2]
    if any(size & (size - 1) for size in sizes) or pages < CORES or width % 128:
        return False
    if local_heads != CORES * query_devices:
        return False
    ranks = pages // CORES
    chunk = part_rows * query_devices // ranks
    return (
        part_rows * query_devices % ranks == 0
        and chunk % 128 == 0
        and part_rows % chunk == 0
        and slot_rows % width == 0
        and part_rows % width == 0
        and max(slot_rows, part_rows) <= TAIL * width
    )


def direct_per_device(
    queries, compact_keys, compact_values, slot_bias, targets, positions, assignment
):
    local_heads, part_rows, width = queries.shape
    slot_rows = compact_keys.shape[1]
    query_devices = lax.axis_size("query")
    head_devices = lax.axis_size("head")
    ranks = lax.axis_size("page") // CORES
    query_rows = part_rows * query_devices
    chunk = query_rows // ranks
    slot_total = local_heads * head_devices * slot_rows * lax.axis_size("page")
    entry_total = slot_total * width
    score_scale = 1.0 / math.sqrt(width)
    slots = CORES * slot_rows
    pos_rows = part_rows // width
    bias_rows = slot_rows // width
    packed_rows = 2 * slot_rows + TAIL
    packed_shapes = [(packed_rows, width)] * 2
    matmul_cost = 6 * 2 * slots * query_rows * width

    def places():
        page = lax.axis_index("page")
        return page // CORES, page % CORES, lax.axis_index("query")

    def prep_body(queries, keys, values, bias_ref, targets, positions_ref, *refs):
        state_outs, refs = refs[:2], refs[2:]
        query_outs, (targets_out, sems) = refs[:query_devices], refs[query_devices:]
        rank, core, me = places()
        copies = []
        for turn in range(query_devices):
            head = CORES * (me ^ turn) + core
            copies.append((queries.at[head], query_outs[turn].at[pl.ds(0, part_rows)]))
        for at in range(2):
            head = CORES * me + (core ^ at)
            copies.append((keys.at[head], state_outs[at].at[pl.ds(0, slot_rows)]))
            copies.append((values.at[head], state_outs[at].at[pl.ds(slot_rows, slot_rows)]))
        first = rank * chunk
        head = CORES * (me ^ (first // part_rows)) + core
        rows = pl.ds(pl.multiple_of(first % part_rows, chunk), chunk)
        copies.append((targets.at[head, rows], targets_out))
        copies = [
            pltpu.make_async_copy(source, target, sems.at[at])
            for at, (source, target) in enumerate(copies)
        ]
        for copy in copies:
            copy.start()
        for turn in range(query_devices):
            row = positions_ref[pl.ds(CORES * (me ^ turn) + core, 1), :].astype(jnp.float32)
            query_outs[turn][part_rows:, :] = row_as_tail(row, width)
        for at in range(2):
            row = bias_ref[pl.ds(CORES * me + (core ^ at), 1), :]
            state_outs[at][2 * slot_rows :, :] = row_as_tail(row, width)
        for copy in copies:
            copy.wait()

    own_state, mate_state, *packed_queries, packed_targets = call(
        prep_body,
        packed_shapes + [(part_rows + TAIL, width)] * query_devices + [(chunk, width)],
        "pack",
        2**20,
        [queries, compact_keys, compact_values, slot_bias, targets, positions],
        [pltpu.HBM] * 3 + [pltpu.VMEM, pltpu.HBM],
        [pltpu.SemaphoreType.DMA((query_devices + 5,))],
    )
    query_parts = packed_queries[:1] + [
        exchange(packed_queries[turn], query=turn) for turn in range(1, query_devices)
    ]
    states = [own_state, exchange(mate_state, page=1)]
    chunk_targets = lax.ppermute(
        packed_targets,
        ("page", "query"),
        [
            (p * query_devices + y, p * query_devices + (y ^ (p // CORES * chunk // part_rows)))
            for p in range(ranks * CORES)
            for y in range(query_devices)
        ],
    )

    def step_sizes(tile_refs):
        tile = tile_refs[0][...]
        for ref in tile_refs[1:]:
            tile = tile + ref[...]
        sums = jnp.sum(tile, axis=1, keepdims=True)
        return (
            RATE_KEYS / jnp.sqrt(sums[0:1] / entry_total + EPSILON),
            RATE_VALUES / jnp.sqrt(sums[1:2] / entry_total + EPSILON),
            RATE_BIAS / jnp.sqrt(sums[2:3] / slot_total + EPSILON),
        )

    def updated(state_ref, grad_ref, sizes):
        key_end, value_end = slot_rows, 2 * slot_rows
        return (
            state_ref[:key_end, :] - sizes[0] * grad_ref[:key_end, :],
            state_ref[key_end:value_end, :] - sizes[1] * grad_ref[key_end:value_end, :],
            state_ref[value_end:, :] - sizes[2] * grad_ref[value_end:, :],
        )

    def forward(assignment_ref, state_refs, query_refs, chunk_outs, weights_out, max_out, chunks):
        rank, core, _ = places()
        all_queries = jnp.concatenate([ref[:part_rows, :] for ref in query_refs], axis=0)
        position_row = jnp.concatenate(
            [tail_as_row(ref, part_rows, pos_rows) for ref in query_refs], axis=1
        )
        all_scores, all_visible = [], []
        for at, ref in enumerate(state_refs):
            scores = dot(ref[:slot_rows, :], all_queries, 1, 1) * score_scale
            bias = row_as_column(tail_as_row(ref, 2 * slot_rows, bias_rows), width)
            scores = scores + jnp.concatenate([bias] * (query_rows // width), axis=1)
            page_start = assignment_ref[CORES * rank + (core ^ at)] * PAGE_LEN
            visible = jnp.broadcast_to(position_row, scores.shape) >= page_start.astype(jnp.float32)
            all_scores.append(jnp.where(visible, scores, MASKED))
            all_visible.append(visible)
        row_max = jnp.max(all_scores[0], axis=0, keepdims=True)
        for scores in all_scores[1:]:
            row_max = jnp.maximum(row_max, jnp.max(scores, axis=0, keepdims=True))
        row_total = jnp.zeros_like(row_max)
        row_sum = jnp.zeros((width, query_rows), jnp.float32)
        for at, ref in enumerate(state_refs):
            weights = jnp.where(all_visible[at], jnp.exp(all_scores[at] - row_max), 0.0)
            weights_out[at * slot_rows : (at + 1) * slot_rows, :] = weights
            row_total = row_total + jnp.sum(weights, axis=0, keepdims=True)
            row_sum = row_sum + dot(ref[slot_rows : 2 * slot_rows, :], weights, 0, 0)
        max_out[...] = jnp.broadcast_to(row_max, (TAIL, query_rows))
        tail = jnp.concatenate(
            [row_max, row_total, jnp.zeros((TAIL - 2, query_rows), jnp.float32)], axis=0
        )
        for at in range(ranks):
            columns = slice(at * chunk, (at + 1) * chunk)
            chunks[at, :width, :] = row_sum[:, columns]
            chunks[at, width:, :] = tail[:, columns]
        for turn in range(ranks):
            chunk_outs[turn][...] = chunks[rank ^ turn]

    chunk_shape = (width + TAIL, chunk)
    forward_shapes = [chunk_shape] * ranks + [(slots, query_rows), (TAIL, query_rows)]
    chunk_scratch = [pltpu.VMEM((ranks,) + chunk_shape, jnp.float32)]

    def first_body(assignment_ref, *refs):
        state_refs, refs = refs[:2], refs[2:]
        query_refs, refs = refs[:query_devices], refs[query_devices:]
        chunk_outs, refs = refs[:ranks], refs[ranks:]
        forward(assignment_ref, state_refs, query_refs, chunk_outs, *refs)

    def next_body(assignment_ref, *refs):
        state_refs, refs = refs[:2], refs[2:]
        query_refs, refs = refs[:query_devices], refs[query_devices:]
        grad_refs, tile_refs, refs = refs[:2], refs[2:4], refs[4:]
        state_outs, refs = refs[:2], refs[2:]
        chunk_outs, refs = refs[:ranks], refs[ranks:]
        sizes = step_sizes(tile_refs)
        for at in range(2):
            keys, values, bias = updated(state_refs[at], grad_refs[at], sizes)
            state_outs[at][:slot_rows, :] = keys
            state_outs[at][slot_rows : 2 * slot_rows, :] = values
            state_outs[at][2 * slot_rows :, :] = bias
        forward(assignment_ref, state_outs, query_refs, chunk_outs, *refs)

    def merge_body(targets_ref, *refs):
        chunk_refs, (merged_out,) = refs[:ranks], refs[ranks:]
        row_max = chunk_refs[0][width : width + 1, :]
        for ref in chunk_refs[1:]:
            row_max = jnp.maximum(row_max, ref[width : width + 1, :])
        row_total = jnp.zeros_like(row_max)
        row_sum = jnp.zeros((width, chunk), jnp.float32)
        for ref in chunk_refs:
            factor = jnp.exp(ref[width : width + 1, :] - row_max)
            row_total = row_total + ref[width + 1 : width + 2, :] * factor
            row_sum = row_sum + ref[:width, :] * factor
        output = row_sum / row_total
        residual = output - targets_ref[...].T
        row_delta = jnp.sum(residual * output, axis=0, keepdims=True)
        merged_out[:width, :] = residual
        merged_out[width:, :] = jnp.concatenate(
            [row_max, row_total, row_delta, jnp.zeros((TAIL - 3, chunk), jnp.float32)], axis=0
        )

    def backward_body(weights_ref, max_ref, *refs):
        state_refs, refs = refs[:2], refs[2:]
        query_refs, refs = refs[:query_devices], refs[query_devices:]
        merged_refs, refs = refs[:ranks], refs[ranks:]
        grad_outs, (squares_out, chunks) = refs[:2], refs[2:]
        rank, _, _ = places()
        for turn in range(ranks):
            chunks[rank ^ turn] = merged_refs[turn][...]
        joined = jnp.concatenate([chunks[at] for at in range(ranks)], axis=1)
        residual = joined[:width, :]
        row_max, row_total, row_delta = (
            joined[width + at : width + at + 1, :] for at in range(3)
        )
        all_queries = jnp.concatenate([ref[:part_rows, :] for ref in query_refs], axis=0)
        factor = jnp.exp(max_ref[0:1, :] - row_max) / row_total
        ones = jnp.ones((TAIL, query_rows), jnp.float32)
        squares = [jnp.zeros((1, width), jnp.float32)] * 3
        for at, ref in enumerate(state_refs):
            attention = weights_ref[at * slot_rows : (at + 1) * slot_rows, :] * factor
            grad_values = dot(attention, residual, 1, 1)
            grad_probs = dot(ref[slot_rows : 2 * slot_rows, :], residual, 1, 0)
            grad_scores = attention * (grad_probs - row_delta)
            grad_keys = dot(grad_scores, all_queries, 1, 0) * score_scale
            grad_bias = row_as_tail(dot(ones, grad_scores, 1, 1)[0:1, :], width)
            grad_outs[at][:slot_rows, :] = grad_keys
            grad_outs[at][slot_rows : 2 * slot_rows, :] = grad_values
            grad_outs[at][2 * slot_rows :, :] = grad_bias
            for which, grad in enumerate((grad_keys, grad_values, grad_bias)):
                squares[which] = squares[which] + jnp.sum(grad * grad, axis=0, keepdims=True)
        squares_out[...] = jnp.concatenate(
            squares + [jnp.zeros((TAIL - 3, width), jnp.float32)], axis=0
        )

    def join_body(left_ref, right_ref, out_ref):
        out_ref[...] = left_ref[...] + right_ref[...]

    def axis_rounds(axis, size, least=1):
        return [{axis: 1 << bit} for bit in range(size.bit_length() - 1) if 1 << bit >= least]

    rounds = (
        axis_rounds("query", query_devices)
        + [{"page": 1}]
        + axis_rounds("head", head_devices)
        + axis_rounds("page", ranks * CORES, CORES)
    )

    out_masks = list(itertools.product(range(query_devices), range(CORES)))

    def to_output(packs, mask):
        if mask == (0, 0):
            return packs[0]
        return exchange(packs[mask[1]], page=mask[1], query=mask[0])

    for repeat in range(STEPS):
        last = repeat == STEPS - 1
        before_merge, before_backward = [], []
        if repeat == 0:
            *chunk_parts, weights, maxima = call(
                first_body,
                forward_shapes,
                "forward",
                2 * matmul_cost,
                [assignment] + states + query_parts,
                [pltpu.SMEM],
                chunk_scratch,
            )
        else:
            own_new, mate_new, *chunk_parts, weights, maxima = call(
                next_body,
                packed_shapes + forward_shapes,
                "update_forward",
                2 * matmul_cost,
                [assignment] + states + query_parts + grads + tiles,
                [pltpu.SMEM],
                chunk_scratch,
            )
            states = [own_new, mate_new]
        if last:
            all_states = [to_output(states, mask) for mask in out_masks]
            if repeat:
                before_merge, before_backward = all_states[2:3], all_states[1:2] + all_states[3:]
        arrived = chunk_parts[:1] + [
            exchange(chunk_parts[turn], page=CORES * turn) for turn in range(1, ranks)
        ]
        (merged,) = call(
            merge_body,
            [chunk_shape],
            "merge",
            2**20,
            [chunk_targets] + arrived,
            after=before_merge,
        )
        all_merged = [merged] + [
            exchange(merged, page=CORES * turn) for turn in range(1, ranks)
        ]
        own_grad, mate_grad, squares = call(
            backward_body,
            packed_shapes + [(TAIL, width)],
            "backward",
            3 * matmul_cost,
            [weights, maxima] + states + query_parts + all_merged,
            scratch=chunk_scratch,
            after=before_backward,
        )
        grads = [own_grad, mate_grad]
        if last:
            all_grads = [to_output(grads, mask) for mask in out_masks]
        tiles = [squares, exchange(squares, **rounds[0])]
        for at, masks in enumerate(rounds[1:], 1):
            if last and at == len(rounds) - 1:
                (joined,) = call(
                    join_body, [squares.shape], "join", 2**10, tiles, after=all_grads[2:3]
                )
            else:
                joined = tiles[0] + tiles[1]
            tiles = [joined, exchange(joined, **masks)]

    def last_body(*refs):
        state_refs, refs = refs[:local_heads], refs[local_heads:]
        grad_refs, refs = refs[:local_heads], refs[local_heads:]
        tile_refs, (keys_out, values_out, bias_out) = refs[:2], refs[2:]
        _, core, me = places()
        sizes = step_sizes(tile_refs)
        for at, (turn, flip) in enumerate(out_masks):
            keys, values, bias = updated(state_refs[at], grad_refs[at], sizes)
            head = CORES * (me ^ turn) + (core ^ flip)
            keys_out[head] = keys
            values_out[head] = values
            bias_row = jnp.concatenate([bias[row : row + 1] for row in range(bias_rows)], axis=1)
            bias_out[pl.ds(head, 1), :] = bias_row

    return tuple(
        call(
            last_body,
            [compact_keys.shape, compact_values.shape, slot_bias.shape],
            "last_update",
            2**20,
            all_states + all_grads + tiles,
        )
    )


def from_partner(value, axis, stride):
    mask = 2**stride
    pairs = [(source, source ^ mask) for source in range(lax.axis_size(axis))]
    return lax.ppermute(value, axis, pairs)


def squared_sums(grad_keys, grad_values, grad_bias):
    return jnp.stack(
        [
            jnp.sum(grad_keys * grad_keys),
            jnp.sum(grad_values * grad_values),
            jnp.sum(grad_bias * grad_bias),
        ]
    )


def apply_update(states, grads, totals, entry_count, slot_total):
    key_state, value_state, bias_state = states
    grad_keys, grad_values, grad_bias = grads
    rms_keys = jnp.sqrt(totals[0] / entry_count + EPSILON)
    rms_values = jnp.sqrt(totals[1] / entry_count + EPSILON)
    rms_bias = jnp.sqrt(totals[2] / slot_total + EPSILON)
    return (
        key_state - RATE_KEYS * grad_keys / rms_keys,
        value_state - RATE_VALUES * grad_values / rms_values,
        bias_state - RATE_BIAS * grad_bias / rms_bias,
    )


def local_gradients(queries, targets, visible, compact_keys, compact_values, slot_bias):
    score_scale = 1.0 / math.sqrt(queries.shape[2])
    scores = jnp.einsum("hqd,hsd->hqs", queries, compact_keys, precision=HIGHEST) * score_scale
    scores = jnp.where(visible, scores + slot_bias[:, None, :], MASKED)
    local_max = jnp.max(scores, axis=2)
    row_max = lax.pmax(local_max, "page")
    weights = jnp.where(visible, jnp.exp(scores - row_max[:, :, None]), 0.0)
    local_sum = jnp.einsum("hqs,hsd->hqd", weights, compact_values, precision=HIGHEST)
    row_total, row_sum = lax.psum((jnp.sum(weights, axis=2), local_sum), "page")
    attention = weights / row_total[:, :, None]
    output = row_sum / row_total[:, :, None]
    residual = output - targets
    grad_values = jnp.einsum("hqs,hqd->hsd", attention, residual, precision=HIGHEST)
    row_delta = jnp.sum(residual * output, axis=2)
    grad_probs = jnp.einsum("hqd,hsd->hqs", residual, compact_values, precision=HIGHEST)
    grad_scores = attention * (grad_probs - row_delta[:, :, None])
    grad_bias = jnp.sum(grad_scores, axis=1)
    grad_keys = jnp.einsum("hqs,hqd->hsd", grad_scores, queries, precision=HIGHEST) * score_scale
    return (grad_keys, grad_values, grad_bias)


def per_device(queries, compact_keys, compact_values, slot_bias, targets, positions, assignment):
    page_number = assignment[lax.axis_index("page")]
    local_heads = compact_keys.shape[0]
    slot_total = local_heads * lax.axis_size("head") * compact_keys.shape[1] * lax.axis_size("page")
    entry_count = slot_total * compact_keys.shape[2]
    query_count = lax.axis_size("query")
    heads_kept = max(local_heads // query_count, 1)
    query_parts = max(query_count // local_heads, 1)
    part_rows = queries.shape[1] // query_parts

    def split_items(array):
        width = array.shape[2]
        array = array.reshape(local_heads // heads_kept, heads_kept, query_parts, part_rows, width)
        array = jnp.transpose(array, (0, 2, 1, 3, 4))
        return array.reshape(query_count, heads_kept, part_rows, width)

    def join_items(array):
        width = array.shape[3]
        array = jnp.transpose(array, (1, 0, 2, 3))
        return array.reshape(heads_kept, query_count * part_rows, width)

    position_column = positions.astype(jnp.float32)[:, :, None]
    got_queries, got_targets, got_positions = (
        lax.all_to_all(split_items(queries), "query", split_axis=0, concat_axis=0, tiled=True),
        lax.all_to_all(split_items(targets), "query", split_axis=0, concat_axis=0, tiled=True),
        lax.all_to_all(
            split_items(position_column), "query", split_axis=0, concat_axis=0, tiled=True
        ),
    )
    group_queries = join_items(got_queries)
    group_targets = join_items(got_targets)
    group_positions = join_items(got_positions)[:, :, 0]
    visible = (page_number.astype(jnp.float32) <= jnp.floor(group_positions / PAGE_LEN))[:, :, None]
    query_index = lax.axis_index("query")
    first_head = query_index // query_parts * heads_kept
    key_state = lax.dynamic_slice_in_dim(compact_keys, first_head, heads_kept, 0)
    value_state = lax.dynamic_slice_in_dim(compact_values, first_head, heads_kept, 0)
    bias_state = lax.dynamic_slice_in_dim(slot_bias, first_head, heads_kept, 0)
    counted = (query_index % query_parts == 0).astype(jnp.float32)
    for repeat in range(STEPS):
        grads = local_gradients(
            group_queries, group_targets, visible, key_state, value_state, bias_state
        )
        for bit in range(query_parts.bit_length() - 1):
            partner = from_partner((grads[0], grads[1], grads[2]), "query", bit)
            grads = (grads[0] + partner[0], grads[1] + partner[1], grads[2] + partner[2])
        totals = lax.psum(
            squared_sums(grads[0], grads[1], grads[2]) * counted, ("page", "query", "head")
        )
        key_state, value_state, bias_state = apply_update(
            (key_state, value_state, bias_state), grads, totals, entry_count, slot_total
        )
    all_keys, all_values, all_bias = (
        lax.all_gather(key_state, "query", axis=0, tiled=True),
        lax.all_gather(value_state, "query", axis=0, tiled=True),
        lax.all_gather(bias_state, "query", axis=0, tiled=True),
    )
    slot_rows = compact_keys.shape[1]
    head_width = compact_keys.shape[2]
    all_keys = all_keys.reshape(
        local_heads // heads_kept, query_parts, heads_kept, slot_rows, head_width
    )[:, 0]
    all_values = all_values.reshape(
        local_heads // heads_kept, query_parts, heads_kept, slot_rows, head_width
    )[:, 0]
    all_bias = all_bias.reshape(local_heads // heads_kept, query_parts, heads_kept, slot_rows)[:, 0]
    return (
        all_keys.reshape(local_heads, slot_rows, head_width),
        all_values.reshape(local_heads, slot_rows, head_width),
        all_bias.reshape(local_heads, slot_rows),
    )


def solution(mesh):
    placed = (
        P("head", "query", None),
        P("head", "page", None),
        P("head", "page", None),
        P("head", "page"),
        P("head", "query", None),
        P("head", "query"),
        P(),
    )

    def program(*args):
        plan = direct_per_device if direct_plan_fits(mesh, args[0], args[1]) else per_device
        return jax.shard_map(
            plan,
            mesh=mesh,
            in_specs=placed,
            out_specs=(P("head", "page", None), P("head", "page", None), P("head", "page")),
            check_vma=False,
        )(*args)

    return program
```

```python
import itertools
import math

import jax
import jax.numpy as jnp
from jax import lax
from jax.experimental import pallas as pl
from jax.experimental.pallas import tpu as pltpu
from jax.sharding import PartitionSpec as P

STEPS = 2
PAGE_LEN = 32768


MASKED = -1e30
EPSILON = 1e-06
RATE_KEYS = 0.05
RATE_VALUES = 0.05
RATE_BIAS = 0.2
HIGHEST = lax.Precision.HIGHEST
TAIL = 8
CORES = 2


def exchange(value, **masks):
    axes = tuple(masks)
    sizes = [lax.axis_size(axis) for axis in axes]

    def flat(place):
        index = 0
        for size, at in zip(sizes, place):
            index = index * size + at
        return index

    pairs = [
        (flat(place), flat([at ^ mask for at, mask in zip(place, masks.values())]))
        for place in itertools.product(*map(range, sizes))
    ]
    return lax.ppermute(value, axes, pairs)


def halves(value):
    high = value.astype(jnp.bfloat16)
    return high, (value - high.astype(jnp.float32)).astype(jnp.bfloat16)


def dot(left, right, left_dim, right_dim):
    def one_pass(left_half, right_half):
        return lax.dot_general(
            left_half,
            right_half,
            (((left_dim,), (right_dim,)), ((), ())),
            preferred_element_type=jnp.float32,
        )

    cross = one_pass(left[0], right[1]) + one_pass(left[1], right[0])
    return one_pass(left[0], right[0]) + cross


def call(body, out_shapes, name, cost, operands, scratch=(), after=(), space=pltpu.VMEM, vmem=32):
    spaces = [space] * len(operands) + [pl.ANY] * len(after)
    count = len(operands)

    def without_after(*refs):
        body(*refs[:count], *refs[count + len(after) :])

    return pl.pallas_call(
        without_after,
        out_shape=[jax.ShapeDtypeStruct(shape, jnp.float32) for shape in out_shapes],
        in_specs=[pl.BlockSpec(memory_space=space) for space in spaces],
        out_specs=[pl.BlockSpec(memory_space=pltpu.VMEM) for _ in out_shapes],
        scratch_shapes=scratch,
        compiler_params=pltpu.CompilerParams(vmem_limit_bytes=vmem * 2**20),
        cost_estimate=pl.CostEstimate(flops=cost, bytes_accessed=2**20, transcendentals=0),
        name=name,
    )(*operands, *after)


def row_as_tail(row, width):
    rows = [row[:, at : at + width] for at in range(0, row.shape[1], width)]
    rows.append(jnp.zeros((TAIL - len(rows), width), row.dtype))
    return jnp.concatenate(rows, axis=0)


def tail_as_row(ref, start, count):
    return jnp.concatenate([ref[start + at : start + at + 1, :] for at in range(count)], axis=1)


def row_as_column(row, width):
    parts = []
    for at in range(0, row.shape[1], width):
        parts.append(jnp.broadcast_to(row[:, at : at + width], (width, width)).T)
    return jnp.concatenate(parts, axis=0)


def direct_plan_fits(mesh, queries, compact_keys):
    sizes = [mesh.shape[axis] for axis in ("page", "query", "head")]
    pages, query_devices, head_devices = sizes
    local_heads = queries.shape[0] // head_devices
    part_rows = queries.shape[1] // query_devices
    slot_rows = compact_keys.shape[1] // pages
    width = queries.shape[2]
    if any(size & (size - 1) for size in sizes) or pages < CORES or width % 128:
        return False
    if local_heads != CORES * query_devices:
        return False
    ranks = pages // CORES
    chunk = part_rows * query_devices // ranks
    return (
        part_rows * query_devices % ranks == 0
        and chunk % 128 == 0
        and part_rows % chunk == 0
        and slot_rows % width == 0
        and part_rows % width == 0
        and max(slot_rows, part_rows) < TAIL * width
    )


def direct_per_device(
    queries, compact_keys, compact_values, slot_bias, targets, positions, assignment
):
    local_heads, part_rows, width = queries.shape
    slot_rows = compact_keys.shape[1]
    query_devices = lax.axis_size("query")
    head_devices = lax.axis_size("head")
    ranks = lax.axis_size("page") // CORES
    query_rows = part_rows * query_devices
    chunk = query_rows // ranks
    slot_total = local_heads * head_devices * slot_rows * lax.axis_size("page")
    entry_total = slot_total * width
    score_scale = 1.0 / math.sqrt(width)
    slots = CORES * slot_rows
    pos_rows = part_rows // width
    bias_rows = slot_rows // width
    packed_rows = 2 * slot_rows + TAIL
    packed_shapes = [(packed_rows, width)] * 2
    matmul_cost = 3 * 2 * slots * query_rows * width

    def places():
        page = lax.axis_index("page")
        return page // CORES, page % CORES, lax.axis_index("query")

    def prep_body(
        queries, keys, values, biases, targets, positions, assignment, *refs
    ):
        state_outs, refs = refs[:2], refs[2:]
        query_outs, (targets_out, *refs) = refs[:query_devices], refs[query_devices:]
        bias_ref, positions_ref, assignment_ref, sems = refs
        rank, core, me = places()
        copies = [
            (assignment, assignment_ref),
            (positions, positions_ref),
            (biases, bias_ref),
        ]
        for turn in range(query_devices):
            head = CORES * (me ^ turn) + core
            copies.append((queries.at[head], query_outs[turn].at[pl.ds(0, part_rows)]))
        for at in range(2):
            head = CORES * me + (core ^ at)
            copies.append((keys.at[head], state_outs[at].at[pl.ds(0, slot_rows)]))
            copies.append((values.at[head], state_outs[at].at[pl.ds(slot_rows, slot_rows)]))
        first = rank * chunk
        head = CORES * (me ^ (first // part_rows)) + core
        rows = pl.ds(pl.multiple_of(first % part_rows, chunk), chunk)
        copies.append((targets.at[head, rows], targets_out))
        copies = [
            pltpu.make_async_copy(source, target, sems.at[at])
            for at, (source, target) in enumerate(copies)
        ]
        for copy in copies:
            copy.start()
        for copy in copies[:3]:
            copy.wait()
        for turn in range(query_devices):
            row = positions_ref[pl.ds(CORES * (me ^ turn) + core, 1), :].astype(jnp.float32)
            query_outs[turn][part_rows:, :] = row_as_tail(row, width)
        page_start = assignment_ref[CORES * rank + core] * PAGE_LEN
        for at in range(2):
            row = bias_ref[pl.ds(CORES * me + (core ^ at), 1), :]
            state_outs[at][2 * slot_rows :, :] = row_as_tail(row, width)
            state_outs[at][packed_rows - 1 :, :] = jnp.full(
                (1, width), page_start.astype(jnp.float32)
            )
        for copy in copies[3:]:
            copy.wait()

    own_state, mate_state, *packed_queries, packed_targets = call(
        prep_body,
        packed_shapes + [(part_rows + TAIL, width)] * query_devices + [(chunk, width)],
        "pack",
        2**20,
        [queries, compact_keys, compact_values, slot_bias, targets, positions, assignment],
        [
            pltpu.VMEM(slot_bias.shape, jnp.float32),
            pltpu.VMEM(positions.shape, jnp.int32),
            pltpu.SMEM(assignment.shape, jnp.int32),
            pltpu.SemaphoreType.DMA((query_devices + 8,)),
        ],
        space=pl.ANY,
        vmem=60,
    )
    query_parts = packed_queries[:1] + [
        exchange(packed_queries[turn], query=turn) for turn in range(1, query_devices)
    ]
    states = [own_state, exchange(mate_state, page=1)]
    chunk_targets = lax.ppermute(
        packed_targets,
        ("page", "query"),
        [
            (p * query_devices + y, p * query_devices + (y ^ (p // CORES * chunk // part_rows)))
            for p in range(ranks * CORES)
            for y in range(query_devices)
        ],
    )

    def step_sizes(tile_refs):
        tile = tile_refs[0][...]
        for ref in tile_refs[1:]:
            tile = tile + ref[...]
        sums = jnp.sum(tile, axis=1, keepdims=True)
        return (
            RATE_KEYS / jnp.sqrt(sums[0:1] / entry_total + EPSILON),
            RATE_VALUES / jnp.sqrt(sums[1:2] / entry_total + EPSILON),
            RATE_BIAS / jnp.sqrt(sums[2:3] / slot_total + EPSILON),
        )

    def updated(state_ref, grad_ref, sizes):
        key_end, value_end = slot_rows, 2 * slot_rows
        return (
            state_ref[:key_end, :] - sizes[0] * grad_ref[:key_end, :],
            state_ref[key_end:value_end, :] - sizes[1] * grad_ref[key_end:value_end, :],
            state_ref[value_end:, :] - sizes[2] * grad_ref[value_end:, :],
        )

    def forward(state_refs, query_refs, chunk_outs, weights_out, max_out, chunks):
        rank, _, _ = places()
        all_queries = halves(jnp.concatenate([ref[:part_rows, :] for ref in query_refs], axis=0))
        position_row = jnp.concatenate(
            [tail_as_row(ref, part_rows, pos_rows) for ref in query_refs], axis=1
        )
        all_scores, all_visible = [], []
        for at, ref in enumerate(state_refs):
            scores = dot(halves(ref[:slot_rows, :]), all_queries, 1, 1) * score_scale
            bias = row_as_column(tail_as_row(ref, 2 * slot_rows, bias_rows), width)
            scores = scores + jnp.concatenate([bias] * (query_rows // width), axis=1)
            page_start = ref[packed_rows - 1 : packed_rows, 0:1]
            visible = jnp.broadcast_to(position_row >= page_start, scores.shape)
            all_scores.append(jnp.where(visible, scores, MASKED))
            all_visible.append(visible)
        row_max = jnp.max(all_scores[0], axis=0, keepdims=True)
        for scores in all_scores[1:]:
            row_max = jnp.maximum(row_max, jnp.max(scores, axis=0, keepdims=True))
        row_total = jnp.zeros_like(row_max)
        row_sum = jnp.zeros((width, query_rows), jnp.float32)
        for at, ref in enumerate(state_refs):
            weights = jnp.where(all_visible[at], jnp.exp(all_scores[at] - row_max), 0.0)
            weights_out[at * slot_rows : (at + 1) * slot_rows, :] = weights
            row_total = row_total + jnp.sum(weights, axis=0, keepdims=True)
            values = halves(ref[slot_rows : 2 * slot_rows, :])
            row_sum = row_sum + dot(values, halves(weights), 0, 0)
        max_out[...] = jnp.broadcast_to(row_max, (TAIL, query_rows))
        tail = jnp.concatenate(
            [row_max, row_total, jnp.zeros((TAIL - 2, query_rows), jnp.float32)], axis=0
        )
        for at in range(ranks):
            columns = slice(at * chunk, (at + 1) * chunk)
            chunks[at, :width, :] = row_sum[:, columns]
            chunks[at, width:, :] = tail[:, columns]
        for turn in range(ranks):
            chunk_outs[turn][...] = chunks[rank ^ turn]

    chunk_shape = (width + TAIL, chunk)
    forward_shapes = [chunk_shape] * ranks + [(slots, query_rows), (TAIL, query_rows)]
    chunk_scratch = [pltpu.VMEM((ranks,) + chunk_shape, jnp.float32)]

    def first_body(*refs):
        state_refs, refs = refs[:2], refs[2:]
        query_refs, refs = refs[:query_devices], refs[query_devices:]
        chunk_outs, refs = refs[:ranks], refs[ranks:]
        forward(state_refs, query_refs, chunk_outs, *refs)

    def next_body(*refs):
        state_refs, refs = refs[:2], refs[2:]
        query_refs, refs = refs[:query_devices], refs[query_devices:]
        grad_refs, refs = refs[:2], refs[2:]
        tile_refs, refs = refs[: len(tiles)], refs[len(tiles) :]
        state_outs, refs = refs[:2], refs[2:]
        chunk_outs, refs = refs[:ranks], refs[ranks:]
        sizes = step_sizes(tile_refs)
        for at in range(2):
            keys, values, bias = updated(state_refs[at], grad_refs[at], sizes)
            state_outs[at][:slot_rows, :] = keys
            state_outs[at][slot_rows : 2 * slot_rows, :] = values
            state_outs[at][2 * slot_rows :, :] = bias
        forward(state_outs, query_refs, chunk_outs, *refs)

    def merge_body(targets_ref, *refs):
        chunk_refs, (merged_out,) = refs[:ranks], refs[ranks:]
        row_max = chunk_refs[0][width : width + 1, :]
        for ref in chunk_refs[1:]:
            row_max = jnp.maximum(row_max, ref[width : width + 1, :])
        row_total = jnp.zeros_like(row_max)
        row_sum = jnp.zeros((width, chunk), jnp.float32)
        for ref in chunk_refs:
            factor = jnp.exp(ref[width : width + 1, :] - row_max)
            row_total = row_total + ref[width + 1 : width + 2, :] * factor
            row_sum = row_sum + ref[:width, :] * factor
        output = row_sum / row_total
        residual = output - targets_ref[...].T
        row_delta = jnp.sum(residual * output, axis=0, keepdims=True)
        merged_out[:width, :] = residual
        merged_out[width:, :] = jnp.concatenate(
            [row_max, row_total, row_delta, jnp.zeros((TAIL - 3, chunk), jnp.float32)], axis=0
        )

    def backward_body(weights_ref, max_ref, *refs):
        state_refs, refs = refs[:2], refs[2:]
        query_refs, refs = refs[:query_devices], refs[query_devices:]
        merged_refs, refs = refs[:ranks], refs[ranks:]
        grad_outs, (squares_out, chunks) = refs[:2], refs[2:]
        rank, _, _ = places()
        for turn in range(ranks):
            chunks[rank ^ turn] = merged_refs[turn][...]
        joined = jnp.concatenate([chunks[at] for at in range(ranks)], axis=1)
        residual = joined[:width, :]
        row_max, row_total, row_delta = (
            joined[width + at : width + at + 1, :] for at in range(3)
        )
        all_queries = halves(jnp.concatenate([ref[:part_rows, :] for ref in query_refs], axis=0))
        residual = halves(residual)
        factor = jnp.exp(max_ref[0:1, :] - row_max) / row_total
        ones = jnp.ones((TAIL, query_rows), jnp.bfloat16)
        ones = (ones, jnp.zeros_like(ones))
        squares = [jnp.zeros((1, width), jnp.float32)] * 3
        for at, ref in enumerate(state_refs):
            attention = weights_ref[at * slot_rows : (at + 1) * slot_rows, :] * factor
            grad_values = dot(halves(attention), residual, 1, 1)
            grad_probs = dot(halves(ref[slot_rows : 2 * slot_rows, :]), residual, 1, 0)
            grad_scores = halves(attention * (grad_probs - row_delta))
            grad_keys = dot(grad_scores, all_queries, 1, 0) * score_scale
            grad_bias = row_as_tail(dot(ones, grad_scores, 1, 1)[0:1, :], width)
            grad_outs[at][:slot_rows, :] = grad_keys
            grad_outs[at][slot_rows : 2 * slot_rows, :] = grad_values
            grad_outs[at][2 * slot_rows :, :] = grad_bias
            for which, grad in enumerate((grad_keys, grad_values, grad_bias)):
                squares[which] = squares[which] + jnp.sum(grad * grad, axis=0, keepdims=True)
        squares_out[...] = jnp.concatenate(
            squares + [jnp.zeros((TAIL - 3, width), jnp.float32)], axis=0
        )

    def join_body(*refs):
        total = refs[0][...]
        for ref in refs[1:-1]:
            total = total + ref[...]
        refs[-1][...] = total

    def group(**sizes):
        masks = itertools.product(*(range(0, size, step) for size, step in sizes.values()))
        return [dict(zip(sizes, mask)) for mask in masks if any(mask)]

    core_round = group(page=(CORES, 1))
    rank_round = group(page=(ranks * CORES, CORES))
    first_rounds = [
        core_round,
        group(query=(query_devices, 1), head=(head_devices, 1)),
        rank_round,
    ]
    last_rounds = [
        core_round,
        group(head=(head_devices, 1)),
        rank_round,
        group(query=(query_devices, 1)),
    ]

    out_masks = list(itertools.product(range(query_devices), range(CORES)))

    def to_output(packs, mask):
        if mask == (0, 0):
            return packs[0]
        return exchange(packs[mask[1]], page=mask[1], query=mask[0])

    for repeat in range(STEPS):
        last = repeat == STEPS - 1
        before_merge, before_backward = [], []
        if repeat == 0:
            *chunk_parts, weights, maxima = call(
                first_body,
                forward_shapes,
                "forward",
                2 * matmul_cost,
                states + query_parts,
                chunk_scratch,
            )
        else:
            own_new, mate_new, *chunk_parts, weights, maxima = call(
                next_body,
                packed_shapes + forward_shapes,
                "update_forward",
                2 * matmul_cost,
                states + query_parts + grads + tiles,
                chunk_scratch,
            )
            states = [own_new, mate_new]
        if last:
            all_states = [to_output(states, mask) for mask in out_masks]
            if repeat:
                before_merge, before_backward = all_states[2:3], all_states[1:2] + all_states[3:]
        arrived = chunk_parts[:1] + [
            exchange(chunk_parts[turn], page=CORES * turn) for turn in range(1, ranks)
        ]
        (merged,) = call(
            merge_body,
            [chunk_shape],
            "merge",
            2**20,
            [chunk_targets] + arrived,
            after=before_merge,
        )
        all_merged = [merged] + [
            exchange(merged, page=CORES * turn) for turn in range(1, ranks)
        ]
        own_grad, mate_grad, squares = call(
            backward_body,
            packed_shapes + [(TAIL, width)],
            "backward",
            3 * matmul_cost,
            [weights, maxima] + states + query_parts + all_merged,
            scratch=chunk_scratch,
            after=before_backward,
        )
        grads = [own_grad, mate_grad]
        if last:
            all_grads = [to_output(grads, mask) for mask in out_masks]
        rounds = last_rounds if last else first_rounds
        tiles = [squares]
        for at, masks in enumerate(rounds):
            joined = tiles[0]
            if last and at == len(rounds) - 1:
                (joined,) = call(
                    join_body, [squares.shape], "join", 2**10, tiles, after=all_grads[2:3]
                )
            else:
                for tile in tiles[1:]:
                    joined = joined + tile
            tiles = [joined] + [exchange(joined, **mask) for mask in masks]

    def last_body(*refs):
        state_refs, refs = refs[:local_heads], refs[local_heads:]
        grad_refs, refs = refs[:local_heads], refs[local_heads:]
        tile_refs, (keys_out, values_out, bias_out) = refs[: len(tiles)], refs[len(tiles) :]
        _, core, me = places()
        sizes = step_sizes(tile_refs)
        for at, (turn, flip) in enumerate(out_masks):
            keys, values, bias = updated(state_refs[at], grad_refs[at], sizes)
            head = CORES * (me ^ turn) + (core ^ flip)
            keys_out[head] = keys
            values_out[head] = values
            bias_row = jnp.concatenate([bias[row : row + 1] for row in range(bias_rows)], axis=1)
            bias_out[pl.ds(head, 1), :] = bias_row

    return tuple(
        call(
            last_body,
            [compact_keys.shape, compact_values.shape, slot_bias.shape],
            "last_update",
            2**20,
            all_states + all_grads + tiles,
        )
    )


def from_partner(value, axis, stride):
    mask = 2**stride
    pairs = [(source, source ^ mask) for source in range(lax.axis_size(axis))]
    return lax.ppermute(value, axis, pairs)


def squared_sums(grad_keys, grad_values, grad_bias):
    return jnp.stack(
        [
            jnp.sum(grad_keys * grad_keys),
            jnp.sum(grad_values * grad_values),
            jnp.sum(grad_bias * grad_bias),
        ]
    )


def apply_update(states, grads, totals, entry_count, slot_total):
    key_state, value_state, bias_state = states
    grad_keys, grad_values, grad_bias = grads
    rms_keys = jnp.sqrt(totals[0] / entry_count + EPSILON)
    rms_values = jnp.sqrt(totals[1] / entry_count + EPSILON)
    rms_bias = jnp.sqrt(totals[2] / slot_total + EPSILON)
    return (
        key_state - RATE_KEYS * grad_keys / rms_keys,
        value_state - RATE_VALUES * grad_values / rms_values,
        bias_state - RATE_BIAS * grad_bias / rms_bias,
    )


def local_gradients(queries, targets, visible, compact_keys, compact_values, slot_bias):
    score_scale = 1.0 / math.sqrt(queries.shape[2])
    scores = jnp.einsum("hqd,hsd->hqs", queries, compact_keys, precision=HIGHEST) * score_scale
    scores = jnp.where(visible, scores + slot_bias[:, None, :], MASKED)
    local_max = jnp.max(scores, axis=2)
    row_max = lax.pmax(local_max, "page")
    weights = jnp.where(visible, jnp.exp(scores - row_max[:, :, None]), 0.0)
    local_sum = jnp.einsum("hqs,hsd->hqd", weights, compact_values, precision=HIGHEST)
    row_total, row_sum = lax.psum((jnp.sum(weights, axis=2), local_sum), "page")
    attention = weights / row_total[:, :, None]
    output = row_sum / row_total[:, :, None]
    residual = output - targets
    grad_values = jnp.einsum("hqs,hqd->hsd", attention, residual, precision=HIGHEST)
    row_delta = jnp.sum(residual * output, axis=2)
    grad_probs = jnp.einsum("hqd,hsd->hqs", residual, compact_values, precision=HIGHEST)
    grad_scores = attention * (grad_probs - row_delta[:, :, None])
    grad_bias = jnp.sum(grad_scores, axis=1)
    grad_keys = jnp.einsum("hqs,hqd->hsd", grad_scores, queries, precision=HIGHEST) * score_scale
    return (grad_keys, grad_values, grad_bias)


def per_device(queries, compact_keys, compact_values, slot_bias, targets, positions, assignment):
    page_number = assignment[lax.axis_index("page")]
    local_heads = compact_keys.shape[0]
    slot_total = local_heads * lax.axis_size("head") * compact_keys.shape[1] * lax.axis_size("page")
    entry_count = slot_total * compact_keys.shape[2]
    query_count = lax.axis_size("query")
    heads_kept = max(local_heads // query_count, 1)
    query_parts = max(query_count // local_heads, 1)
    part_rows = queries.shape[1] // query_parts

    def split_items(array):
        width = array.shape[2]
        array = array.reshape(local_heads // heads_kept, heads_kept, query_parts, part_rows, width)
        array = jnp.transpose(array, (0, 2, 1, 3, 4))
        return array.reshape(query_count, heads_kept, part_rows, width)

    def join_items(array):
        width = array.shape[3]
        array = jnp.transpose(array, (1, 0, 2, 3))
        return array.reshape(heads_kept, query_count * part_rows, width)

    position_column = positions.astype(jnp.float32)[:, :, None]
    got_queries, got_targets, got_positions = (
        lax.all_to_all(split_items(queries), "query", split_axis=0, concat_axis=0, tiled=True),
        lax.all_to_all(split_items(targets), "query", split_axis=0, concat_axis=0, tiled=True),
        lax.all_to_all(
            split_items(position_column), "query", split_axis=0, concat_axis=0, tiled=True
        ),
    )
    group_queries = join_items(got_queries)
    group_targets = join_items(got_targets)
    group_positions = join_items(got_positions)[:, :, 0]
    visible = (page_number.astype(jnp.float32) <= jnp.floor(group_positions / PAGE_LEN))[:, :, None]
    query_index = lax.axis_index("query")
    first_head = query_index // query_parts * heads_kept
    key_state = lax.dynamic_slice_in_dim(compact_keys, first_head, heads_kept, 0)
    value_state = lax.dynamic_slice_in_dim(compact_values, first_head, heads_kept, 0)
    bias_state = lax.dynamic_slice_in_dim(slot_bias, first_head, heads_kept, 0)
    counted = (query_index % query_parts == 0).astype(jnp.float32)
    for repeat in range(STEPS):
        grads = local_gradients(
            group_queries, group_targets, visible, key_state, value_state, bias_state
        )
        for bit in range(query_parts.bit_length() - 1):
            partner = from_partner((grads[0], grads[1], grads[2]), "query", bit)
            grads = (grads[0] + partner[0], grads[1] + partner[1], grads[2] + partner[2])
        totals = lax.psum(
            squared_sums(grads[0], grads[1], grads[2]) * counted, ("page", "query", "head")
        )
        key_state, value_state, bias_state = apply_update(
            (key_state, value_state, bias_state), grads, totals, entry_count, slot_total
        )
    all_keys, all_values, all_bias = (
        lax.all_gather(key_state, "query", axis=0, tiled=True),
        lax.all_gather(value_state, "query", axis=0, tiled=True),
        lax.all_gather(bias_state, "query", axis=0, tiled=True),
    )
    slot_rows = compact_keys.shape[1]
    head_width = compact_keys.shape[2]
    all_keys = all_keys.reshape(
        local_heads // heads_kept, query_parts, heads_kept, slot_rows, head_width
    )[:, 0]
    all_values = all_values.reshape(
        local_heads // heads_kept, query_parts, heads_kept, slot_rows, head_width
    )[:, 0]
    all_bias = all_bias.reshape(local_heads // heads_kept, query_parts, heads_kept, slot_rows)[:, 0]
    return (
        all_keys.reshape(local_heads, slot_rows, head_width),
        all_values.reshape(local_heads, slot_rows, head_width),
        all_bias.reshape(local_heads, slot_rows),
    )


def solution(mesh):
    placed = (
        P("head", "query", None),
        P("head", "page", None),
        P("head", "page", None),
        P("head", "page"),
        P("head", "query", None),
        P("head", "query"),
        P(),
    )

    def program(*args):
        plan = direct_per_device if direct_plan_fits(mesh, args[0], args[1]) else per_device
        return jax.shard_map(
            plan,
            mesh=mesh,
            in_specs=placed,
            out_specs=(P("head", "page", None), P("head", "page", None), P("head", "page")),
            check_vma=False,
        )(*args)

    return program
```

```python
import itertools
import math

import jax
import jax.numpy as jnp
from jax import lax
from jax.experimental import pallas as pl
from jax.experimental.pallas import tpu as pltpu
from jax.sharding import PartitionSpec as P

STEPS = 2
PAGE_LEN = 32768


MASKED = -1e30
EPSILON = 1e-06
RATE_KEYS = 0.05
RATE_VALUES = 0.05
RATE_BIAS = 0.2
HIGHEST = lax.Precision.HIGHEST
TAIL = 8
CORES = 2


def exchange(value, **masks):
    axes = tuple(masks)
    sizes = [lax.axis_size(axis) for axis in axes]

    def flat(place):
        index = 0
        for size, at in zip(sizes, place):
            index = index * size + at
        return index

    pairs = [
        (flat(place), flat([at ^ mask for at, mask in zip(place, masks.values())]))
        for place in itertools.product(*map(range, sizes))
    ]
    return lax.ppermute(value, axes, pairs)


def halves(value):
    high = value.astype(jnp.bfloat16)
    return high, (value - high.astype(jnp.float32)).astype(jnp.bfloat16)


def dot(left, right, left_dim, right_dim):
    def one_pass(left_half, right_half):
        return lax.dot_general(
            left_half,
            right_half,
            (((left_dim,), (right_dim,)), ((), ())),
            preferred_element_type=jnp.float32,
        )

    cross = one_pass(left[0], right[1]) + one_pass(left[1], right[0])
    return one_pass(left[0], right[0]) + cross


def call(body, out_shapes, name, cost, operands, scratch=(), after=(), space=pltpu.VMEM, vmem=32):
    spaces = [space] * len(operands) + [pl.ANY] * len(after)
    count = len(operands)

    def without_after(*refs):
        body(*refs[:count], *refs[count + len(after) :])

    return pl.pallas_call(
        without_after,
        out_shape=[jax.ShapeDtypeStruct(shape, jnp.float32) for shape in out_shapes],
        in_specs=[pl.BlockSpec(memory_space=space) for space in spaces],
        out_specs=[pl.BlockSpec(memory_space=pltpu.VMEM) for _ in out_shapes],
        scratch_shapes=scratch,
        compiler_params=pltpu.CompilerParams(vmem_limit_bytes=vmem * 2**20),
        cost_estimate=pl.CostEstimate(flops=cost, bytes_accessed=2**20, transcendentals=0),
        name=name,
    )(*operands, *after)


def row_as_tail(row, width):
    rows = [row[:, at : at + width] for at in range(0, row.shape[1], width)]
    rows.append(jnp.zeros((TAIL - len(rows), width), row.dtype))
    return jnp.concatenate(rows, axis=0)


def tail_as_row(ref, start, count):
    return jnp.concatenate([ref[start + at : start + at + 1, :] for at in range(count)], axis=1)


def row_as_column(row, width):
    parts = []
    for at in range(0, row.shape[1], width):
        parts.append(jnp.broadcast_to(row[:, at : at + width], (width, width)).T)
    return jnp.concatenate(parts, axis=0)


def direct_plan_fits(mesh, queries, compact_keys):
    sizes = [mesh.shape[axis] for axis in ("page", "query", "head")]
    pages, query_devices, head_devices = sizes
    local_heads = queries.shape[0] // head_devices
    part_rows = queries.shape[1] // query_devices
    slot_rows = compact_keys.shape[1] // pages
    width = queries.shape[2]
    if any(size & (size - 1) for size in sizes) or pages < CORES or width % 128:
        return False
    if local_heads != CORES * query_devices:
        return False
    ranks = pages // CORES
    chunk = part_rows * query_devices // ranks
    return (
        part_rows * query_devices % ranks == 0
        and chunk % 128 == 0
        and part_rows % chunk == 0
        and slot_rows % width == 0
        and part_rows % width == 0
        and max(slot_rows, part_rows) < TAIL * width
    )


def direct_per_device(
    queries, compact_keys, compact_values, slot_bias, targets, positions, assignment
):
    local_heads, part_rows, width = queries.shape
    slot_rows = compact_keys.shape[1]
    query_devices = lax.axis_size("query")
    head_devices = lax.axis_size("head")
    ranks = lax.axis_size("page") // CORES
    query_rows = part_rows * query_devices
    chunk = query_rows // ranks
    slot_total = local_heads * head_devices * slot_rows * lax.axis_size("page")
    entry_total = slot_total * width
    score_scale = 1.0 / math.sqrt(width)
    slots = CORES * slot_rows
    devices = ranks * CORES * query_devices * head_devices
    pos_rows = part_rows // width
    bias_rows = slot_rows // width
    packed_rows = 2 * slot_rows + TAIL
    packed_shapes = [(packed_rows, width)] * 2
    matmul_cost = 3 * 2 * slots * query_rows * width

    def places():
        page = lax.axis_index("page")
        return page // CORES, page % CORES, lax.axis_index("query")

    def prep_body(
        queries, keys, values, biases, targets, positions, assignment, *refs
    ):
        state_outs, refs = refs[:2], refs[2:]
        query_outs, (targets_out, *refs) = refs[:query_devices], refs[query_devices:]
        bias_ref, positions_ref, assignment_ref, sems = refs
        rank, core, me = places()
        copies = [
            (assignment, assignment_ref),
            (positions, positions_ref),
            (biases, bias_ref),
        ]
        for turn in range(query_devices):
            head = CORES * (me ^ turn) + core
            copies.append((queries.at[head], query_outs[turn].at[pl.ds(0, part_rows)]))
        for at in range(2):
            head = CORES * me + (core ^ at)
            copies.append((keys.at[head], state_outs[at].at[pl.ds(0, slot_rows)]))
            copies.append((values.at[head], state_outs[at].at[pl.ds(slot_rows, slot_rows)]))
        first = rank * chunk
        head = CORES * (me ^ (first // part_rows)) + core
        rows = pl.ds(pl.multiple_of(first % part_rows, chunk), chunk)
        copies.append((targets.at[head, rows], targets_out))
        copies = [
            pltpu.make_async_copy(source, target, sems.at[at])
            for at, (source, target) in enumerate(copies)
        ]
        for copy in copies:
            copy.start()
        for copy in copies[:3]:
            copy.wait()
        for turn in range(query_devices):
            row = positions_ref[pl.ds(CORES * (me ^ turn) + core, 1), :].astype(jnp.float32)
            query_outs[turn][part_rows:, :] = row_as_tail(row, width)
        page_start = assignment_ref[CORES * rank + core] * PAGE_LEN
        for at in range(2):
            row = bias_ref[pl.ds(CORES * me + (core ^ at), 1), :]
            state_outs[at][2 * slot_rows :, :] = row_as_tail(row, width)
            state_outs[at][packed_rows - 1 :, :] = jnp.full(
                (1, width), page_start.astype(jnp.float32)
            )
        for copy in copies[3:]:
            copy.wait()

    own_state, mate_state, *packed_queries, packed_targets = call(
        prep_body,
        packed_shapes + [(part_rows + TAIL, width)] * query_devices + [(chunk, width)],
        "pack",
        2**20,
        [queries, compact_keys, compact_values, slot_bias, targets, positions, assignment],
        [
            pltpu.VMEM(slot_bias.shape, jnp.float32),
            pltpu.VMEM(positions.shape, jnp.int32),
            pltpu.SMEM(assignment.shape, jnp.int32),
            pltpu.SemaphoreType.DMA((query_devices + 8,)),
        ],
        space=pl.ANY,
        vmem=60,
    )
    query_parts = packed_queries[:1] + [
        exchange(packed_queries[turn], query=turn) for turn in range(1, query_devices)
    ]
    states = [own_state, exchange(mate_state, page=1)]
    chunk_targets = lax.ppermute(
        packed_targets,
        ("page", "query"),
        [
            (p * query_devices + y, p * query_devices + (y ^ (p // CORES * chunk // part_rows)))
            for p in range(ranks * CORES)
            for y in range(query_devices)
        ],
    )

    def step_sizes(tile_refs):
        tile = jnp.sum(tile_refs[0][...], axis=0)
        sums = jnp.sum(tile, axis=1, keepdims=True)
        return (
            RATE_KEYS / jnp.sqrt(sums[0:1] / entry_total + EPSILON),
            RATE_VALUES / jnp.sqrt(sums[1:2] / entry_total + EPSILON),
            RATE_BIAS / jnp.sqrt(sums[2:3] / slot_total + EPSILON),
        )

    def updated(state_ref, grad_ref, sizes):
        key_end, value_end = slot_rows, 2 * slot_rows
        return (
            state_ref[:key_end, :] - sizes[0] * grad_ref[:key_end, :],
            state_ref[key_end:value_end, :] - sizes[1] * grad_ref[key_end:value_end, :],
            state_ref[value_end:, :] - sizes[2] * grad_ref[value_end:, :],
        )

    def forward(state_refs, query_refs, chunk_outs, weights_out, max_out, chunks):
        rank, _, _ = places()
        all_queries = halves(jnp.concatenate([ref[:part_rows, :] for ref in query_refs], axis=0))
        position_row = jnp.concatenate(
            [tail_as_row(ref, part_rows, pos_rows) for ref in query_refs], axis=1
        )
        all_scores, all_visible = [], []
        for at, ref in enumerate(state_refs):
            scores = dot(halves(ref[:slot_rows, :]), all_queries, 1, 1) * score_scale
            bias = row_as_column(tail_as_row(ref, 2 * slot_rows, bias_rows), width)
            scores = scores + jnp.concatenate([bias] * (query_rows // width), axis=1)
            page_start = ref[packed_rows - 1 : packed_rows, 0:1]
            visible = jnp.broadcast_to(position_row >= page_start, scores.shape)
            all_scores.append(jnp.where(visible, scores, MASKED))
            all_visible.append(visible)
        row_max = jnp.max(all_scores[0], axis=0, keepdims=True)
        for scores in all_scores[1:]:
            row_max = jnp.maximum(row_max, jnp.max(scores, axis=0, keepdims=True))
        row_total = jnp.zeros_like(row_max)
        row_sum = jnp.zeros((width, query_rows), jnp.float32)
        for at, ref in enumerate(state_refs):
            weights = jnp.where(all_visible[at], jnp.exp(all_scores[at] - row_max), 0.0)
            weights_out[at * slot_rows : (at + 1) * slot_rows, :] = weights
            row_total = row_total + jnp.sum(weights, axis=0, keepdims=True)
            values = halves(ref[slot_rows : 2 * slot_rows, :])
            row_sum = row_sum + dot(values, halves(weights), 0, 0)
        max_out[...] = jnp.broadcast_to(row_max, (TAIL, query_rows))
        tail = jnp.concatenate(
            [row_max, row_total, jnp.zeros((TAIL - 2, query_rows), jnp.float32)], axis=0
        )
        for at in range(ranks):
            columns = slice(at * chunk, (at + 1) * chunk)
            chunks[at, :width, :] = row_sum[:, columns]
            chunks[at, width:, :] = tail[:, columns]
        for turn in range(ranks):
            chunk_outs[turn][...] = chunks[rank ^ turn]

    chunk_shape = (width + TAIL, chunk)
    forward_shapes = [chunk_shape] * ranks + [(slots, query_rows), (TAIL, query_rows)]
    chunk_scratch = [pltpu.VMEM((ranks,) + chunk_shape, jnp.float32)]

    def first_body(*refs):
        state_refs, refs = refs[:2], refs[2:]
        query_refs, refs = refs[:query_devices], refs[query_devices:]
        chunk_outs, refs = refs[:ranks], refs[ranks:]
        forward(state_refs, query_refs, chunk_outs, *refs)

    def next_body(*refs):
        state_refs, refs = refs[:2], refs[2:]
        query_refs, refs = refs[:query_devices], refs[query_devices:]
        grad_refs, refs = refs[:2], refs[2:]
        tile_refs, refs = refs[: len(tiles)], refs[len(tiles) :]
        state_outs, refs = refs[:2], refs[2:]
        chunk_outs, refs = refs[:ranks], refs[ranks:]
        sizes = step_sizes(tile_refs)
        for at in range(2):
            keys, values, bias = updated(state_refs[at], grad_refs[at], sizes)
            state_outs[at][:slot_rows, :] = keys
            state_outs[at][slot_rows : 2 * slot_rows, :] = values
            state_outs[at][2 * slot_rows :, :] = bias
        forward(state_outs, query_refs, chunk_outs, *refs)

    def merge_body(targets_ref, *refs):
        chunk_refs, (merged_out,) = refs[:ranks], refs[ranks:]
        row_max = chunk_refs[0][width : width + 1, :]
        for ref in chunk_refs[1:]:
            row_max = jnp.maximum(row_max, ref[width : width + 1, :])
        row_total = jnp.zeros_like(row_max)
        row_sum = jnp.zeros((width, chunk), jnp.float32)
        for ref in chunk_refs:
            factor = jnp.exp(ref[width : width + 1, :] - row_max)
            row_total = row_total + ref[width + 1 : width + 2, :] * factor
            row_sum = row_sum + ref[:width, :] * factor
        output = row_sum / row_total
        residual = output - targets_ref[...].T
        row_delta = jnp.sum(residual * output, axis=0, keepdims=True)
        merged_out[:width, :] = residual
        merged_out[width:, :] = jnp.concatenate(
            [row_max, row_total, row_delta, jnp.zeros((TAIL - 3, chunk), jnp.float32)], axis=0
        )

    def backward_body(weights_ref, max_ref, *refs):
        state_refs, refs = refs[:2], refs[2:]
        query_refs, refs = refs[:query_devices], refs[query_devices:]
        merged_refs, refs = refs[:ranks], refs[ranks:]
        grad_outs, (squares_out, chunks) = refs[:2], refs[2:]
        rank, _, _ = places()
        for turn in range(ranks):
            chunks[rank ^ turn] = merged_refs[turn][...]
        joined = jnp.concatenate([chunks[at] for at in range(ranks)], axis=1)
        residual = joined[:width, :]
        row_max, row_total, row_delta = (
            joined[width + at : width + at + 1, :] for at in range(3)
        )
        all_queries = halves(jnp.concatenate([ref[:part_rows, :] for ref in query_refs], axis=0))
        residual = halves(residual)
        factor = jnp.exp(max_ref[0:1, :] - row_max) / row_total
        ones = jnp.ones((TAIL, query_rows), jnp.bfloat16)
        ones = (ones, jnp.zeros_like(ones))
        squares = [jnp.zeros((1, width), jnp.float32)] * 3
        for at, ref in enumerate(state_refs):
            attention = weights_ref[at * slot_rows : (at + 1) * slot_rows, :] * factor
            grad_values = dot(halves(attention), residual, 1, 1)
            grad_probs = dot(halves(ref[slot_rows : 2 * slot_rows, :]), residual, 1, 0)
            grad_scores = halves(attention * (grad_probs - row_delta))
            grad_keys = dot(grad_scores, all_queries, 1, 0) * score_scale
            grad_bias = row_as_tail(dot(ones, grad_scores, 1, 1)[0:1, :], width)
            grad_outs[at][:slot_rows, :] = grad_keys
            grad_outs[at][slot_rows : 2 * slot_rows, :] = grad_values
            grad_outs[at][2 * slot_rows :, :] = grad_bias
            for which, grad in enumerate((grad_keys, grad_values, grad_bias)):
                squares[which] = squares[which] + jnp.sum(grad * grad, axis=0, keepdims=True)
        tile = jnp.concatenate(squares + [jnp.zeros((TAIL - 3, width), jnp.float32)], axis=0)
        for at in range(devices):
            squares_out[at] = tile

    out_masks = list(itertools.product(range(query_devices), range(CORES)))

    def to_output(packs, mask):
        if mask == (0, 0):
            return packs[0]
        return exchange(packs[mask[1]], page=mask[1], query=mask[0])

    for repeat in range(STEPS):
        last = repeat == STEPS - 1
        before_merge, before_backward = [], []
        if repeat == 0:
            *chunk_parts, weights, maxima = call(
                first_body,
                forward_shapes,
                "forward",
                2 * matmul_cost,
                states + query_parts,
                chunk_scratch,
            )
        else:
            own_new, mate_new, *chunk_parts, weights, maxima = call(
                next_body,
                packed_shapes + forward_shapes,
                "update_forward",
                2 * matmul_cost,
                states + query_parts + grads + tiles,
                chunk_scratch,
            )
            states = [own_new, mate_new]
        if last:
            all_states = [to_output(states, mask) for mask in out_masks]
            if repeat:
                before_merge, before_backward = all_states[2:3], all_states[1:2] + all_states[3:]
        arrived = chunk_parts[:1] + [
            exchange(chunk_parts[turn], page=CORES * turn) for turn in range(1, ranks)
        ]
        (merged,) = call(
            merge_body,
            [chunk_shape],
            "merge",
            2**20,
            [chunk_targets] + arrived,
            after=before_merge,
        )
        all_merged = [merged] + [
            exchange(merged, page=CORES * turn) for turn in range(1, ranks)
        ]
        own_grad, mate_grad, squares = call(
            backward_body,
            packed_shapes + [(devices, TAIL, width)],
            "backward",
            3 * matmul_cost,
            [weights, maxima] + states + query_parts + all_merged,
            scratch=chunk_scratch,
            after=before_backward,
        )
        grads = [own_grad, mate_grad]
        if last:
            all_grads = [to_output(grads, mask) for mask in out_masks]
        tiles = [
            lax.all_to_all(
                squares, ("page", "query", "head"), split_axis=0, concat_axis=0, tiled=True
            )
        ]

    def last_body(*refs):
        state_refs, refs = refs[:local_heads], refs[local_heads:]
        grad_refs, refs = refs[:local_heads], refs[local_heads:]
        tile_refs, (keys_out, values_out, bias_out) = refs[: len(tiles)], refs[len(tiles) :]
        _, core, me = places()
        sizes = step_sizes(tile_refs)
        for at, (turn, flip) in enumerate(out_masks):
            keys, values, bias = updated(state_refs[at], grad_refs[at], sizes)
            head = CORES * (me ^ turn) + (core ^ flip)
            keys_out[head] = keys
            values_out[head] = values
            bias_row = jnp.concatenate([bias[row : row + 1] for row in range(bias_rows)], axis=1)
            bias_out[pl.ds(head, 1), :] = bias_row

    return tuple(
        call(
            last_body,
            [compact_keys.shape, compact_values.shape, slot_bias.shape],
            "last_update",
            2**20,
            all_states + all_grads + tiles,
        )
    )


def from_partner(value, axis, stride):
    mask = 2**stride
    pairs = [(source, source ^ mask) for source in range(lax.axis_size(axis))]
    return lax.ppermute(value, axis, pairs)


def squared_sums(grad_keys, grad_values, grad_bias):
    return jnp.stack(
        [
            jnp.sum(grad_keys * grad_keys),
            jnp.sum(grad_values * grad_values),
            jnp.sum(grad_bias * grad_bias),
        ]
    )


def apply_update(states, grads, totals, entry_count, slot_total):
    key_state, value_state, bias_state = states
    grad_keys, grad_values, grad_bias = grads
    rms_keys = jnp.sqrt(totals[0] / entry_count + EPSILON)
    rms_values = jnp.sqrt(totals[1] / entry_count + EPSILON)
    rms_bias = jnp.sqrt(totals[2] / slot_total + EPSILON)
    return (
        key_state - RATE_KEYS * grad_keys / rms_keys,
        value_state - RATE_VALUES * grad_values / rms_values,
        bias_state - RATE_BIAS * grad_bias / rms_bias,
    )


def local_gradients(queries, targets, visible, compact_keys, compact_values, slot_bias):
    score_scale = 1.0 / math.sqrt(queries.shape[2])
    scores = jnp.einsum("hqd,hsd->hqs", queries, compact_keys, precision=HIGHEST) * score_scale
    scores = jnp.where(visible, scores + slot_bias[:, None, :], MASKED)
    local_max = jnp.max(scores, axis=2)
    row_max = lax.pmax(local_max, "page")
    weights = jnp.where(visible, jnp.exp(scores - row_max[:, :, None]), 0.0)
    local_sum = jnp.einsum("hqs,hsd->hqd", weights, compact_values, precision=HIGHEST)
    row_total, row_sum = lax.psum((jnp.sum(weights, axis=2), local_sum), "page")
    attention = weights / row_total[:, :, None]
    output = row_sum / row_total[:, :, None]
    residual = output - targets
    grad_values = jnp.einsum("hqs,hqd->hsd", attention, residual, precision=HIGHEST)
    row_delta = jnp.sum(residual * output, axis=2)
    grad_probs = jnp.einsum("hqd,hsd->hqs", residual, compact_values, precision=HIGHEST)
    grad_scores = attention * (grad_probs - row_delta[:, :, None])
    grad_bias = jnp.sum(grad_scores, axis=1)
    grad_keys = jnp.einsum("hqs,hqd->hsd", grad_scores, queries, precision=HIGHEST) * score_scale
    return (grad_keys, grad_values, grad_bias)


def per_device(queries, compact_keys, compact_values, slot_bias, targets, positions, assignment):
    page_number = assignment[lax.axis_index("page")]
    local_heads = compact_keys.shape[0]
    slot_total = local_heads * lax.axis_size("head") * compact_keys.shape[1] * lax.axis_size("page")
    entry_count = slot_total * compact_keys.shape[2]
    query_count = lax.axis_size("query")
    heads_kept = max(local_heads // query_count, 1)
    query_parts = max(query_count // local_heads, 1)
    part_rows = queries.shape[1] // query_parts

    def split_items(array):
        width = array.shape[2]
        array = array.reshape(local_heads // heads_kept, heads_kept, query_parts, part_rows, width)
        array = jnp.transpose(array, (0, 2, 1, 3, 4))
        return array.reshape(query_count, heads_kept, part_rows, width)

    def join_items(array):
        width = array.shape[3]
        array = jnp.transpose(array, (1, 0, 2, 3))
        return array.reshape(heads_kept, query_count * part_rows, width)

    position_column = positions.astype(jnp.float32)[:, :, None]
    got_queries, got_targets, got_positions = (
        lax.all_to_all(split_items(queries), "query", split_axis=0, concat_axis=0, tiled=True),
        lax.all_to_all(split_items(targets), "query", split_axis=0, concat_axis=0, tiled=True),
        lax.all_to_all(
            split_items(position_column), "query", split_axis=0, concat_axis=0, tiled=True
        ),
    )
    group_queries = join_items(got_queries)
    group_targets = join_items(got_targets)
    group_positions = join_items(got_positions)[:, :, 0]
    visible = (page_number.astype(jnp.float32) <= jnp.floor(group_positions / PAGE_LEN))[:, :, None]
    query_index = lax.axis_index("query")
    first_head = query_index // query_parts * heads_kept
    key_state = lax.dynamic_slice_in_dim(compact_keys, first_head, heads_kept, 0)
    value_state = lax.dynamic_slice_in_dim(compact_values, first_head, heads_kept, 0)
    bias_state = lax.dynamic_slice_in_dim(slot_bias, first_head, heads_kept, 0)
    counted = (query_index % query_parts == 0).astype(jnp.float32)
    for repeat in range(STEPS):
        grads = local_gradients(
            group_queries, group_targets, visible, key_state, value_state, bias_state
        )
        for bit in range(query_parts.bit_length() - 1):
            partner = from_partner((grads[0], grads[1], grads[2]), "query", bit)
            grads = (grads[0] + partner[0], grads[1] + partner[1], grads[2] + partner[2])
        totals = lax.psum(
            squared_sums(grads[0], grads[1], grads[2]) * counted, ("page", "query", "head")
        )
        key_state, value_state, bias_state = apply_update(
            (key_state, value_state, bias_state), grads, totals, entry_count, slot_total
        )
    all_keys, all_values, all_bias = (
        lax.all_gather(key_state, "query", axis=0, tiled=True),
        lax.all_gather(value_state, "query", axis=0, tiled=True),
        lax.all_gather(bias_state, "query", axis=0, tiled=True),
    )
    slot_rows = compact_keys.shape[1]
    head_width = compact_keys.shape[2]
    all_keys = all_keys.reshape(
        local_heads // heads_kept, query_parts, heads_kept, slot_rows, head_width
    )[:, 0]
    all_values = all_values.reshape(
        local_heads // heads_kept, query_parts, heads_kept, slot_rows, head_width
    )[:, 0]
    all_bias = all_bias.reshape(local_heads // heads_kept, query_parts, heads_kept, slot_rows)[:, 0]
    return (
        all_keys.reshape(local_heads, slot_rows, head_width),
        all_values.reshape(local_heads, slot_rows, head_width),
        all_bias.reshape(local_heads, slot_rows),
    )


def solution(mesh):
    placed = (
        P("head", "query", None),
        P("head", "page", None),
        P("head", "page", None),
        P("head", "page"),
        P("head", "query", None),
        P("head", "query"),
        P(),
    )

    def program(*args):
        plan = direct_per_device if direct_plan_fits(mesh, args[0], args[1]) else per_device
        return jax.shard_map(
            plan,
            mesh=mesh,
            in_specs=placed,
            out_specs=(P("head", "page", None), P("head", "page", None), P("head", "page")),
            check_vma=False,
        )(*args)

    return program
```

```python
import itertools
import math

import jax
import jax.numpy as jnp
from jax import lax
from jax.experimental import pallas as pl
from jax.experimental.pallas import tpu as pltpu
from jax.sharding import PartitionSpec as P

STEPS = 2
PAGE_LEN = 32768


MASKED = -1e30
EPSILON = 1e-06
RATE_KEYS = 0.05
RATE_VALUES = 0.05
RATE_BIAS = 0.2
HIGHEST = lax.Precision.HIGHEST
TAIL = 8
CORES = 2


def exchange(value, **masks):
    axes = tuple(masks)
    sizes = [lax.axis_size(axis) for axis in axes]

    def flat(place):
        index = 0
        for size, at in zip(sizes, place):
            index = index * size + at
        return index

    pairs = [
        (flat(place), flat([at ^ mask for at, mask in zip(place, masks.values())]))
        for place in itertools.product(*map(range, sizes))
    ]
    return lax.ppermute(value, axes, pairs)


def halves(value):
    high = value.astype(jnp.bfloat16)
    return high, (value - high.astype(jnp.float32)).astype(jnp.bfloat16)


def dot(left, right, left_dim, right_dim):
    def one_pass(left_half, right_half):
        return lax.dot_general(
            left_half,
            right_half,
            (((left_dim,), (right_dim,)), ((), ())),
            preferred_element_type=jnp.float32,
        )

    cross = one_pass(left[0], right[1]) + one_pass(left[1], right[0])
    return one_pass(left[0], right[0]) + cross


def call(body, out_shapes, name, cost, operands, scratch=(), after=(), space=pltpu.VMEM,
         out_space=pltpu.VMEM, vmem=32):
    spaces = [space] * len(operands) + [pl.ANY] * len(after)
    count = len(operands)

    def without_after(*refs):
        body(*refs[:count], *refs[count + len(after) :])

    return pl.pallas_call(
        without_after,
        out_shape=[jax.ShapeDtypeStruct(shape, jnp.float32) for shape in out_shapes],
        in_specs=[pl.BlockSpec(memory_space=space) for space in spaces],
        out_specs=[pl.BlockSpec(memory_space=out_space) for _ in out_shapes],
        scratch_shapes=scratch,
        compiler_params=pltpu.CompilerParams(vmem_limit_bytes=vmem * 2**20),
        cost_estimate=pl.CostEstimate(flops=cost, bytes_accessed=2**20, transcendentals=0),
        name=name,
    )(*operands, *after)


def row_as_tail(row, width):
    rows = [row[:, at : at + width] for at in range(0, row.shape[1], width)]
    rows.append(jnp.zeros((TAIL - len(rows), width), row.dtype))
    return jnp.concatenate(rows, axis=0)


def tail_as_row(ref, start, count):
    return jnp.concatenate([ref[start + at : start + at + 1, :] for at in range(count)], axis=1)


def row_as_column(row, width):
    parts = []
    for at in range(0, row.shape[1], width):
        parts.append(jnp.broadcast_to(row[:, at : at + width], (width, width)).T)
    return jnp.concatenate(parts, axis=0)


def direct_plan_fits(mesh, queries, compact_keys):
    sizes = [mesh.shape[axis] for axis in ("page", "query", "head")]
    pages, query_devices, head_devices = sizes
    local_heads = queries.shape[0] // head_devices
    part_rows = queries.shape[1] // query_devices
    slot_rows = compact_keys.shape[1] // pages
    width = queries.shape[2]
    if any(size & (size - 1) for size in sizes) or pages < CORES or width % 128:
        return False
    if local_heads != CORES * query_devices:
        return False
    ranks = pages // CORES
    chunk = part_rows * query_devices // ranks
    return (
        part_rows * query_devices % ranks == 0
        and chunk % 128 == 0
        and part_rows % (8 * ranks) == 0
        and slot_rows % width == 0
        and part_rows % width == 0
        and max(slot_rows, part_rows) < TAIL * width
    )


def direct_per_device(
    queries, compact_keys, compact_values, slot_bias, targets, positions, assignment
):
    local_heads, part_rows, width = queries.shape
    slot_rows = compact_keys.shape[1]
    query_devices = lax.axis_size("query")
    head_devices = lax.axis_size("head")
    ranks = lax.axis_size("page") // CORES
    query_rows = part_rows * query_devices
    chunk, piece = query_rows // ranks, part_rows // ranks
    slot_total = local_heads * head_devices * slot_rows * lax.axis_size("page")
    entry_total = slot_total * width
    score_scale = 1.0 / math.sqrt(width)
    slots = CORES * slot_rows
    devices = ranks * CORES * query_devices * head_devices
    pos_rows = part_rows // width
    bias_rows = slot_rows // width
    packed_rows = 2 * slot_rows + TAIL
    packed_shapes = [(packed_rows, width)] * 2
    matmul_cost = 3 * 2 * slots * query_rows * width

    def places():
        page = lax.axis_index("page")
        return page // CORES, page % CORES, lax.axis_index("query")

    def pack_queries(head, rank, queries, targets, out):
        rows = pl.ds(pl.multiple_of(rank * piece, piece), piece)
        return [
            (queries.at[head], out.at[pl.ds(0, part_rows)]),
            (targets.at[head, rows], out.at[pl.ds(part_rows, piece)]),
        ]

    def pack_state(head, keys, values, out):
        return [
            (keys.at[head], out.at[pl.ds(0, slot_rows)]),
            (values.at[head], out.at[pl.ds(slot_rows, slot_rows)]),
        ]

    def start_all(copies, sems, first=0):
        copies = [
            pltpu.make_async_copy(source, target, sems.at[first + at])
            for at, (source, target) in enumerate(copies)
        ]
        for copy in copies:
            copy.start()
        return copies

    def position_tail(head, positions_ref):
        return row_as_tail(positions_ref[pl.ds(head, 1), :].astype(jnp.float32), width)

    def state_tail(head, page, bias_ref, assignment_ref):
        page_start = (assignment_ref[page] * PAGE_LEN).astype(jnp.float32)
        tail = row_as_tail(bias_ref[pl.ds(head, 1), :], width)
        return jnp.concatenate(
            [tail[: TAIL - 1], jnp.full((1, width), page_start, jnp.float32)], axis=0
        )

    def send_body(
        queries, keys, values, biases, targets, positions, assignment, state_out, *refs
    ):
        query_outs = refs[: query_devices - 1]
        bias_ref, positions_ref, assignment_ref, tails, sems = refs[query_devices - 1 :]
        rank, core, me = places()
        heads = [CORES * (me ^ turn) + core for turn in range(1, query_devices)]
        mate_head = CORES * me + (core ^ 1)
        small = start_all(
            [(assignment, assignment_ref), (positions, positions_ref), (biases, bias_ref)], sems
        )
        copies = pack_state(mate_head, keys, values, state_out)
        for head, out in zip(heads, query_outs):
            copies += pack_queries(head, rank, queries, targets, out)
        copies = start_all(copies, sems, 3)
        for copy in small:
            copy.wait()
        tails[0] = state_tail(mate_head, CORES * rank + core, bias_ref, assignment_ref)
        for at, head in enumerate(heads):
            tails[1 + at] = position_tail(head, positions_ref)
        ends = [(tails.at[0], state_out.at[pl.ds(2 * slot_rows, TAIL)])]
        for at, out in enumerate(query_outs):
            ends.append((tails.at[1 + at], out.at[pl.ds(part_rows + piece, TAIL)]))
        copies += start_all(ends, sems, 3 + len(copies))
        for copy in copies:
            copy.wait()

    def own_body(
        queries, keys, values, biases, targets, positions, assignment, state_out, query_out, *refs
    ):
        bias_ref, positions_ref, assignment_ref, sems = refs
        rank, core, me = places()
        head = CORES * me + core
        small = start_all(
            [(assignment, assignment_ref), (positions, positions_ref), (biases, bias_ref)], sems
        )
        copies = pack_state(head, keys, values, state_out)
        copies += pack_queries(head, rank, queries, targets, query_out)
        copies = start_all(copies, sems, 3)
        for copy in small:
            copy.wait()
        state_out[2 * slot_rows :, :] = state_tail(
            head, CORES * rank + core, bias_ref, assignment_ref
        )
        query_out[part_rows + piece :, :] = position_tail(head, positions_ref)
        for copy in copies:
            copy.wait()

    state_shape, query_shape = (packed_rows, width), (part_rows + piece + TAIL, width)
    small_scratch = [
        pltpu.VMEM(slot_bias.shape, jnp.float32),
        pltpu.VMEM(positions.shape, jnp.int32),
        pltpu.SMEM(assignment.shape, jnp.int32),
    ]
    arguments = [
        queries, compact_keys, compact_values, slot_bias, targets, positions, assignment
    ]
    mate_state, *sent_queries = call(
        send_body,
        [state_shape] + [query_shape] * (query_devices - 1),
        "pack",
        2**20,
        arguments,
        small_scratch
        + [
            pltpu.VMEM((query_devices, TAIL, width), jnp.float32),
            pltpu.SemaphoreType.DMA((5 + 3 * query_devices,)),
        ],
        space=pl.ANY,
        out_space=pl.ANY,
        vmem=60,
    )
    own_state, own_queries = call(
        own_body,
        [state_shape, query_shape],
        "own",
        2**24,
        arguments,
        small_scratch + [pltpu.SemaphoreType.DMA((7,))],
        space=pl.ANY,
    )
    query_parts = [own_queries] + [
        exchange(sent_queries[turn - 1], query=turn) for turn in range(1, query_devices)
    ]
    states = [own_state, exchange(mate_state, page=1)]

    def in_columns(parts, axis):
        return jnp.concatenate(
            [
                lax.slice_in_dim(part, at * piece, (at + 1) * piece, axis=axis)
                for at in range(ranks)
                for part in parts
            ],
            axis=axis,
        )

    def read_queries(query_refs):
        return halves(in_columns([ref[:part_rows, :] for ref in query_refs], 0))

    def part_of(ref, at):
        return ref.at[pl.ds(at * packed_rows, packed_rows)]

    def parts_of(refs):
        return refs if len(refs) == CORES else [part_of(refs[0], at) for at in range(CORES)]

    def step_sizes(tile_refs):
        tile = jnp.sum(tile_refs[0][...], axis=0)
        sums = jnp.sum(tile, axis=1, keepdims=True)
        return (
            RATE_KEYS / jnp.sqrt(sums[0:1] / entry_total + EPSILON),
            RATE_VALUES / jnp.sqrt(sums[1:2] / entry_total + EPSILON),
            RATE_BIAS / jnp.sqrt(sums[2:3] / slot_total + EPSILON),
        )

    def updated(state_ref, grad_ref, sizes):
        key_end, value_end = slot_rows, 2 * slot_rows
        return (
            state_ref[:key_end, :] - sizes[0] * grad_ref[:key_end, :],
            state_ref[key_end:value_end, :] - sizes[1] * grad_ref[key_end:value_end, :],
            state_ref[value_end:, :] - sizes[2] * grad_ref[value_end:, :],
        )

    def forward(state_refs, query_refs, chunk_outs, weights_out, max_out, chunks):
        rank, _, _ = places()
        all_queries = read_queries(query_refs)
        position_row = in_columns(
            [tail_as_row(ref, part_rows + piece, pos_rows) for ref in query_refs], 1
        )
        all_scores, all_visible = [], []
        for at, ref in enumerate(state_refs):
            scores = dot(halves(ref[:slot_rows, :]), all_queries, 1, 1) * score_scale
            bias = row_as_column(tail_as_row(ref, 2 * slot_rows, bias_rows), width)
            scores = scores + jnp.concatenate([bias] * (query_rows // width), axis=1)
            page_start = ref[packed_rows - 1 : packed_rows, 0:1]
            visible = jnp.broadcast_to(position_row >= page_start, scores.shape)
            all_scores.append(jnp.where(visible, scores, MASKED))
            all_visible.append(visible)
        row_max = jnp.max(all_scores[0], axis=0, keepdims=True)
        for scores in all_scores[1:]:
            row_max = jnp.maximum(row_max, jnp.max(scores, axis=0, keepdims=True))
        row_total = jnp.zeros_like(row_max)
        row_sum = jnp.zeros((width, query_rows), jnp.float32)
        for at, ref in enumerate(state_refs):
            weights = jnp.where(all_visible[at], jnp.exp(all_scores[at] - row_max), 0.0)
            weights_out[at * slot_rows : (at + 1) * slot_rows, :] = weights
            row_total = row_total + jnp.sum(weights, axis=0, keepdims=True)
            values = halves(ref[slot_rows : 2 * slot_rows, :])
            row_sum = row_sum + dot(values, halves(weights), 0, 0)
        max_out[...] = jnp.broadcast_to(row_max, (TAIL, query_rows))
        tail = jnp.concatenate(
            [row_max, row_total, jnp.zeros((TAIL - 2, query_rows), jnp.float32)], axis=0
        )
        for at in range(ranks):
            columns = slice(at * chunk, (at + 1) * chunk)
            chunks[at, :width, :] = row_sum[:, columns]
            chunks[at, width:, :] = tail[:, columns]
        for turn in range(ranks):
            chunk_outs[turn][...] = chunks[rank ^ turn]

    chunk_shape = (width + TAIL, chunk)
    forward_shapes = [chunk_shape] * ranks + [(slots, query_rows), (TAIL, query_rows)]
    chunk_scratch = [pltpu.VMEM((ranks,) + chunk_shape, jnp.float32)]

    def first_body(*refs):
        state_refs, refs = refs[:2], refs[2:]
        query_refs, refs = refs[:query_devices], refs[query_devices:]
        chunk_outs, refs = refs[:ranks], refs[ranks:]
        forward(state_refs, query_refs, chunk_outs, *refs)

    def next_body(*refs):
        state_refs, refs = refs[:2], refs[2:]
        query_refs, refs = refs[:query_devices], refs[query_devices:]
        grad_refs, refs = refs[:2], refs[2:]
        tile_refs, refs = refs[: len(tiles)], refs[len(tiles) :]
        state_outs, refs = parts_of(refs[:1]), refs[1:]
        chunk_outs, refs = refs[:ranks], refs[ranks:]
        sizes = step_sizes(tile_refs)
        for at in range(2):
            keys, values, bias = updated(state_refs[at], grad_refs[at], sizes)
            state_outs[at][:slot_rows, :] = keys
            state_outs[at][slot_rows : 2 * slot_rows, :] = values
            state_outs[at][2 * slot_rows :, :] = bias
        forward(state_outs, query_refs, chunk_outs, *refs)

    def merge_body(*refs):
        query_refs, refs = refs[:query_devices], refs[query_devices:]
        chunk_refs, (merged_out,) = refs[:ranks], refs[ranks:]
        targets = jnp.concatenate(
            [ref[part_rows : part_rows + piece, :] for ref in query_refs], axis=0
        )
        row_max = chunk_refs[0][width : width + 1, :]
        for ref in chunk_refs[1:]:
            row_max = jnp.maximum(row_max, ref[width : width + 1, :])
        row_total = jnp.zeros_like(row_max)
        row_sum = jnp.zeros((width, chunk), jnp.float32)
        for ref in chunk_refs:
            factor = jnp.exp(ref[width : width + 1, :] - row_max)
            row_total = row_total + ref[width + 1 : width + 2, :] * factor
            row_sum = row_sum + ref[:width, :] * factor
        output = row_sum / row_total
        residual = output - targets.T
        row_delta = jnp.sum(residual * output, axis=0, keepdims=True)
        merged_out[:width, :] = residual
        merged_out[width:, :] = jnp.concatenate(
            [row_max, row_total, row_delta, jnp.zeros((TAIL - 3, chunk), jnp.float32)], axis=0
        )

    def backward_body(weights_ref, max_ref, *refs):
        state_refs, refs = parts_of(refs[: len(states)]), refs[len(states) :]
        query_refs, refs = refs[:query_devices], refs[query_devices:]
        merged_refs, refs = refs[:ranks], refs[ranks:]
        grad_outs, (squares_out, chunks) = refs[:2], refs[2:]
        rank, _, _ = places()
        for turn in range(ranks):
            chunks[rank ^ turn] = merged_refs[turn][...]
        joined = jnp.concatenate([chunks[at] for at in range(ranks)], axis=1)
        residual = joined[:width, :]
        row_max, row_total, row_delta = (
            joined[width + at : width + at + 1, :] for at in range(3)
        )
        all_queries = read_queries(query_refs)
        residual = halves(residual)
        factor = jnp.exp(max_ref[0:1, :] - row_max) / row_total
        ones = jnp.ones((TAIL, query_rows), jnp.bfloat16)
        ones = (ones, jnp.zeros_like(ones))
        squares = [jnp.zeros((1, width), jnp.float32)] * 3
        for at, ref in enumerate(state_refs):
            attention = weights_ref[at * slot_rows : (at + 1) * slot_rows, :] * factor
            grad_values = dot(halves(attention), residual, 1, 1)
            grad_probs = dot(halves(ref[slot_rows : 2 * slot_rows, :]), residual, 1, 0)
            grad_scores = halves(attention * (grad_probs - row_delta))
            grad_keys = dot(grad_scores, all_queries, 1, 0) * score_scale
            grad_bias = row_as_tail(dot(ones, grad_scores, 1, 1)[0:1, :], width)
            grad_outs[at][:slot_rows, :] = grad_keys
            grad_outs[at][slot_rows : 2 * slot_rows, :] = grad_values
            grad_outs[at][2 * slot_rows :, :] = grad_bias
            for which, grad in enumerate((grad_keys, grad_values, grad_bias)):
                squares[which] = squares[which] + jnp.sum(grad * grad, axis=0, keepdims=True)
        tile = jnp.concatenate(squares + [jnp.zeros((TAIL - 3, width), jnp.float32)], axis=0)
        for at in range(devices):
            squares_out[at] = tile

    def mate_body(*refs):
        *state_refs, out_ref = refs
        for at, ref in enumerate(state_refs):
            out_ref[pl.ds(at * packed_rows, packed_rows), :] = part_of(ref, 1)[...]

    out_masks = list(itertools.product(range(query_devices), range(CORES)))

    def to_output(packs, mask):
        if mask == (0, 0):
            return packs[0]
        return exchange(packs[mask[1]], page=mask[1], query=mask[0])

    for repeat in range(STEPS):
        last = repeat == STEPS - 1
        if repeat == 0:
            *chunk_parts, weights, maxima = call(
                first_body,
                forward_shapes,
                "forward",
                2 * matmul_cost,
                states + query_parts,
                chunk_scratch,
            )
        else:
            new_state, *chunk_parts, weights, maxima = call(
                next_body,
                [(CORES * packed_rows, width)] + forward_shapes,
                "update_forward",
                2 * matmul_cost,
                states + query_parts + grads + tiles,
                chunk_scratch,
            )
            states = [new_state]
        arrived = {
            turn: exchange(chunk_parts[turn], page=CORES * turn)
            for turn in reversed(range(1, ranks))
        }
        if repeat:
            new_states = states + [
                exchange(states[0], query=turn) for turn in range(1, query_devices)
            ]
        (merged,) = call(
            merge_body,
            [chunk_shape],
            "merge",
            2**20,
            query_parts + chunk_parts[:1] + list(arrived.values()),
        )
        all_merged = [merged] + [
            exchange(merged, page=CORES * turn) for turn in range(1, ranks)
        ]
        if repeat:
            (for_mate,) = call(
                mate_body,
                [(query_devices * packed_rows, width)],
                "mate_parts",
                2**20,
                new_states,
                after=all_merged[1:],
            )
            from_mate = exchange(for_mate, page=1)
        own_grad, mate_grad, squares = call(
            backward_body,
            packed_shapes + [(devices, TAIL, width)],
            "backward",
            3 * matmul_cost,
            [weights, maxima] + states + query_parts + all_merged,
            scratch=chunk_scratch,
        )
        grads = [own_grad, mate_grad]
        if last:
            all_grads = [to_output(grads, mask) for mask in out_masks]
        tiles = [
            lax.all_to_all(
                squares, ("page", "query", "head"), split_axis=0, concat_axis=0, tiled=True
            )
        ]

    def last_body(*refs):
        state_refs, (mate_ref, *refs) = refs[:query_devices], refs[query_devices:]
        state_refs = [
            part_of(mate_ref, turn) if flip else part_of(state_refs[turn], 0)
            for turn, flip in out_masks
        ]
        grad_refs, refs = refs[:local_heads], refs[local_heads:]
        tile_refs, (keys_out, values_out, bias_out) = refs[: len(tiles)], refs[len(tiles) :]
        _, core, me = places()
        sizes = step_sizes(tile_refs)
        for at, (turn, flip) in enumerate(out_masks):
            keys, values, bias = updated(state_refs[at], grad_refs[at], sizes)
            head = CORES * (me ^ turn) + (core ^ flip)
            keys_out[head] = keys
            values_out[head] = values
            bias_row = jnp.concatenate([bias[row : row + 1] for row in range(bias_rows)], axis=1)
            bias_out[pl.ds(head, 1), :] = bias_row

    return tuple(
        call(
            last_body,
            [compact_keys.shape, compact_values.shape, slot_bias.shape],
            "last_update",
            2**20,
            new_states + [from_mate] + all_grads + tiles,
        )
    )


def from_partner(value, axis, stride):
    mask = 2**stride
    pairs = [(source, source ^ mask) for source in range(lax.axis_size(axis))]
    return lax.ppermute(value, axis, pairs)


def squared_sums(grad_keys, grad_values, grad_bias):
    return jnp.stack(
        [
            jnp.sum(grad_keys * grad_keys),
            jnp.sum(grad_values * grad_values),
            jnp.sum(grad_bias * grad_bias),
        ]
    )


def apply_update(states, grads, totals, entry_count, slot_total):
    key_state, value_state, bias_state = states
    grad_keys, grad_values, grad_bias = grads
    rms_keys = jnp.sqrt(totals[0] / entry_count + EPSILON)
    rms_values = jnp.sqrt(totals[1] / entry_count + EPSILON)
    rms_bias = jnp.sqrt(totals[2] / slot_total + EPSILON)
    return (
        key_state - RATE_KEYS * grad_keys / rms_keys,
        value_state - RATE_VALUES * grad_values / rms_values,
        bias_state - RATE_BIAS * grad_bias / rms_bias,
    )


def local_gradients(queries, targets, visible, compact_keys, compact_values, slot_bias):
    score_scale = 1.0 / math.sqrt(queries.shape[2])
    scores = jnp.einsum("hqd,hsd->hqs", queries, compact_keys, precision=HIGHEST) * score_scale
    scores = jnp.where(visible, scores + slot_bias[:, None, :], MASKED)
    local_max = jnp.max(scores, axis=2)
    row_max = lax.pmax(local_max, "page")
    weights = jnp.where(visible, jnp.exp(scores - row_max[:, :, None]), 0.0)
    local_sum = jnp.einsum("hqs,hsd->hqd", weights, compact_values, precision=HIGHEST)
    row_total, row_sum = lax.psum((jnp.sum(weights, axis=2), local_sum), "page")
    attention = weights / row_total[:, :, None]
    output = row_sum / row_total[:, :, None]
    residual = output - targets
    grad_values = jnp.einsum("hqs,hqd->hsd", attention, residual, precision=HIGHEST)
    row_delta = jnp.sum(residual * output, axis=2)
    grad_probs = jnp.einsum("hqd,hsd->hqs", residual, compact_values, precision=HIGHEST)
    grad_scores = attention * (grad_probs - row_delta[:, :, None])
    grad_bias = jnp.sum(grad_scores, axis=1)
    grad_keys = jnp.einsum("hqs,hqd->hsd", grad_scores, queries, precision=HIGHEST) * score_scale
    return (grad_keys, grad_values, grad_bias)


def per_device(queries, compact_keys, compact_values, slot_bias, targets, positions, assignment):
    page_number = assignment[lax.axis_index("page")]
    local_heads = compact_keys.shape[0]
    slot_total = local_heads * lax.axis_size("head") * compact_keys.shape[1] * lax.axis_size("page")
    entry_count = slot_total * compact_keys.shape[2]
    query_count = lax.axis_size("query")
    heads_kept = max(local_heads // query_count, 1)
    query_parts = max(query_count // local_heads, 1)
    part_rows = queries.shape[1] // query_parts

    def split_items(array):
        width = array.shape[2]
        array = array.reshape(local_heads // heads_kept, heads_kept, query_parts, part_rows, width)
        array = jnp.transpose(array, (0, 2, 1, 3, 4))
        return array.reshape(query_count, heads_kept, part_rows, width)

    def join_items(array):
        width = array.shape[3]
        array = jnp.transpose(array, (1, 0, 2, 3))
        return array.reshape(heads_kept, query_count * part_rows, width)

    position_column = positions.astype(jnp.float32)[:, :, None]
    got_queries, got_targets, got_positions = (
        lax.all_to_all(split_items(queries), "query", split_axis=0, concat_axis=0, tiled=True),
        lax.all_to_all(split_items(targets), "query", split_axis=0, concat_axis=0, tiled=True),
        lax.all_to_all(
            split_items(position_column), "query", split_axis=0, concat_axis=0, tiled=True
        ),
    )
    group_queries = join_items(got_queries)
    group_targets = join_items(got_targets)
    group_positions = join_items(got_positions)[:, :, 0]
    visible = (page_number.astype(jnp.float32) <= jnp.floor(group_positions / PAGE_LEN))[:, :, None]
    query_index = lax.axis_index("query")
    first_head = query_index // query_parts * heads_kept
    key_state = lax.dynamic_slice_in_dim(compact_keys, first_head, heads_kept, 0)
    value_state = lax.dynamic_slice_in_dim(compact_values, first_head, heads_kept, 0)
    bias_state = lax.dynamic_slice_in_dim(slot_bias, first_head, heads_kept, 0)
    counted = (query_index % query_parts == 0).astype(jnp.float32)
    for repeat in range(STEPS):
        grads = local_gradients(
            group_queries, group_targets, visible, key_state, value_state, bias_state
        )
        for bit in range(query_parts.bit_length() - 1):
            partner = from_partner((grads[0], grads[1], grads[2]), "query", bit)
            grads = (grads[0] + partner[0], grads[1] + partner[1], grads[2] + partner[2])
        totals = lax.psum(
            squared_sums(grads[0], grads[1], grads[2]) * counted, ("page", "query", "head")
        )
        key_state, value_state, bias_state = apply_update(
            (key_state, value_state, bias_state), grads, totals, entry_count, slot_total
        )
    all_keys, all_values, all_bias = (
        lax.all_gather(key_state, "query", axis=0, tiled=True),
        lax.all_gather(value_state, "query", axis=0, tiled=True),
        lax.all_gather(bias_state, "query", axis=0, tiled=True),
    )
    slot_rows = compact_keys.shape[1]
    head_width = compact_keys.shape[2]
    all_keys = all_keys.reshape(
        local_heads // heads_kept, query_parts, heads_kept, slot_rows, head_width
    )[:, 0]
    all_values = all_values.reshape(
        local_heads // heads_kept, query_parts, heads_kept, slot_rows, head_width
    )[:, 0]
    all_bias = all_bias.reshape(local_heads // heads_kept, query_parts, heads_kept, slot_rows)[:, 0]
    return (
        all_keys.reshape(local_heads, slot_rows, head_width),
        all_values.reshape(local_heads, slot_rows, head_width),
        all_bias.reshape(local_heads, slot_rows),
    )


def solution(mesh):
    placed = (
        P("head", "query", None),
        P("head", "page", None),
        P("head", "page", None),
        P("head", "page"),
        P("head", "query", None),
        P("head", "query"),
        P(),
    )

    def program(*args):
        plan = direct_per_device if direct_plan_fits(mesh, args[0], args[1]) else per_device
        return jax.shard_map(
            plan,
            mesh=mesh,
            in_specs=placed,
            out_specs=(P("head", "page", None), P("head", "page", None), P("head", "page")),
            check_vma=False,
        )(*args)

    return program
```

```python
import itertools
import math

import jax
import jax.numpy as jnp
from jax import lax
from jax.experimental import pallas as pl
from jax.experimental.pallas import tpu as pltpu
from jax.sharding import PartitionSpec as P

STEPS = 2
PAGE_LEN = 32768


MASKED = -1e30
EPSILON = 1e-06
RATE_KEYS = 0.05
RATE_VALUES = 0.05
RATE_BIAS = 0.2
HIGHEST = lax.Precision.HIGHEST
TAIL = 8
CORES = 2


def exchange(value, **masks):
    axes = tuple(masks)
    sizes = [lax.axis_size(axis) for axis in axes]

    def flat(place):
        index = 0
        for size, at in zip(sizes, place):
            index = index * size + at
        return index

    pairs = [
        (flat(place), flat([at ^ mask for at, mask in zip(place, masks.values())]))
        for place in itertools.product(*map(range, sizes))
    ]
    return lax.ppermute(value, axes, pairs)


def halves(value):
    high = value.astype(jnp.bfloat16)
    return high, (value - high.astype(jnp.float32)).astype(jnp.bfloat16)


def dot(left, right, left_dim, right_dim):
    def one_pass(left_half, right_half):
        return lax.dot_general(
            left_half,
            right_half,
            (((left_dim,), (right_dim,)), ((), ())),
            preferred_element_type=jnp.float32,
        )

    cross = one_pass(left[0], right[1]) + one_pass(left[1], right[0])
    return one_pass(left[0], right[0]) + cross


def call(body, out_shapes, name, cost, operands, scratch=(), after=(), space=pltpu.VMEM, vmem=32):
    spaces = [space] * len(operands) + [pl.ANY] * len(after)
    count = len(operands)

    def without_after(*refs):
        body(*refs[:count], *refs[count + len(after) :])

    return pl.pallas_call(
        without_after,
        out_shape=[jax.ShapeDtypeStruct(shape, jnp.float32) for shape in out_shapes],
        in_specs=[pl.BlockSpec(memory_space=space) for space in spaces],
        out_specs=[pl.BlockSpec(memory_space=pltpu.VMEM) for _ in out_shapes],
        scratch_shapes=scratch,
        compiler_params=pltpu.CompilerParams(vmem_limit_bytes=vmem * 2**20),
        cost_estimate=pl.CostEstimate(flops=cost, bytes_accessed=2**20, transcendentals=0),
        name=name,
    )(*operands, *after)


def row_as_tail(row, width):
    rows = [row[:, at : at + width] for at in range(0, row.shape[1], width)]
    rows.append(jnp.zeros((TAIL - len(rows), width), row.dtype))
    return jnp.concatenate(rows, axis=0)


def tail_as_row(ref, start, count):
    return jnp.concatenate([ref[start + at : start + at + 1, :] for at in range(count)], axis=1)


def row_as_column(row, width):
    parts = []
    for at in range(0, row.shape[1], width):
        parts.append(jnp.broadcast_to(row[:, at : at + width], (width, width)).T)
    return jnp.concatenate(parts, axis=0)


def direct_plan_fits(mesh, queries, compact_keys):
    sizes = [mesh.shape[axis] for axis in ("page", "query", "head")]
    pages, query_devices, head_devices = sizes
    local_heads = queries.shape[0] // head_devices
    part_rows = queries.shape[1] // query_devices
    slot_rows = compact_keys.shape[1] // pages
    width = queries.shape[2]
    if any(size & (size - 1) for size in sizes) or pages < CORES or width % 128:
        return False
    if local_heads != CORES * query_devices:
        return False
    ranks = pages // CORES
    chunk = part_rows * query_devices // ranks
    return (
        part_rows * query_devices % ranks == 0
        and chunk % 128 == 0
        and part_rows % (8 * ranks) == 0
        and slot_rows % width == 0
        and part_rows % width == 0
        and max(slot_rows, part_rows) < TAIL * width
    )


def direct_per_device(
    queries, compact_keys, compact_values, slot_bias, targets, positions, assignment
):
    local_heads, part_rows, width = queries.shape
    slot_rows = compact_keys.shape[1]
    query_devices = lax.axis_size("query")
    head_devices = lax.axis_size("head")
    ranks = lax.axis_size("page") // CORES
    query_rows = part_rows * query_devices
    chunk, piece = query_rows // ranks, part_rows // ranks
    slot_total = local_heads * head_devices * slot_rows * lax.axis_size("page")
    entry_total = slot_total * width
    score_scale = 1.0 / math.sqrt(width)
    slots = CORES * slot_rows
    devices = ranks * CORES * query_devices * head_devices
    pos_rows = part_rows // width
    bias_rows = slot_rows // width
    packed_rows = 2 * slot_rows + TAIL
    packed_shapes = [(packed_rows, width)] * 2
    matmul_cost = 3 * 2 * slots * query_rows * width

    def places():
        page = lax.axis_index("page")
        return page // CORES, page % CORES, lax.axis_index("query")

    def pack_queries(head, rank, queries, targets, out):
        rows = pl.ds(pl.multiple_of(rank * piece, piece), piece)
        return [
            (queries.at[head], out.at[pl.ds(0, part_rows)]),
            (targets.at[head, rows], out.at[pl.ds(part_rows, piece)]),
        ]

    def pack_state(head, keys, values, out):
        return [
            (keys.at[head], out.at[pl.ds(0, slot_rows)]),
            (values.at[head], out.at[pl.ds(slot_rows, slot_rows)]),
        ]

    def start_all(copies, sems, first=0):
        copies = [
            pltpu.make_async_copy(source, target, sems.at[first + at])
            for at, (source, target) in enumerate(copies)
        ]
        for copy in copies:
            copy.start()
        return copies

    def position_tail(head, positions_ref):
        return row_as_tail(positions_ref[pl.ds(head, 1), :].astype(jnp.float32), width)

    def state_tail(head, page, bias_ref, assignment_ref):
        page_start = (assignment_ref[page] * PAGE_LEN).astype(jnp.float32)
        tail = row_as_tail(bias_ref[pl.ds(head, 1), :], width)
        return jnp.concatenate(
            [tail[: TAIL - 1], jnp.full((1, width), page_start, jnp.float32)], axis=0
        )

    def send_body(
        queries, keys, values, biases, targets, positions, assignment, state_out, *refs
    ):
        query_outs = refs[: query_devices - 1]
        bias_ref, positions_ref, assignment_ref, sems = refs[query_devices - 1 :]
        rank, core, me = places()
        heads = [CORES * (me ^ turn) + core for turn in range(1, query_devices)]
        mate_head = CORES * me + (core ^ 1)
        small = start_all(
            [(assignment, assignment_ref), (positions, positions_ref), (biases, bias_ref)], sems
        )
        copies = pack_state(mate_head, keys, values, state_out)
        for head, out in zip(heads, query_outs):
            copies += pack_queries(head, rank, queries, targets, out)
        copies = start_all(copies, sems, 3)
        for copy in small:
            copy.wait()
        state_out[2 * slot_rows :, :] = state_tail(
            mate_head, CORES * rank + core, bias_ref, assignment_ref
        )
        for head, out in zip(heads, query_outs):
            out[part_rows + piece :, :] = position_tail(head, positions_ref)
        for copy in copies:
            copy.wait()

    def own_body(
        queries, keys, values, biases, targets, positions, assignment, state_out, query_out, *refs
    ):
        bias_ref, positions_ref, assignment_ref, sems = refs
        rank, core, me = places()
        head = CORES * me + core
        small = start_all(
            [(assignment, assignment_ref), (positions, positions_ref), (biases, bias_ref)], sems
        )
        copies = pack_state(head, keys, values, state_out)
        copies += pack_queries(head, rank, queries, targets, query_out)
        copies = start_all(copies, sems, 3)
        for copy in small:
            copy.wait()
        state_out[2 * slot_rows :, :] = state_tail(
            head, CORES * rank + core, bias_ref, assignment_ref
        )
        query_out[part_rows + piece :, :] = position_tail(head, positions_ref)
        for copy in copies:
            copy.wait()

    state_shape, query_shape = (packed_rows, width), (part_rows + piece + TAIL, width)
    small_scratch = [
        pltpu.VMEM(slot_bias.shape, jnp.float32),
        pltpu.VMEM(positions.shape, jnp.int32),
        pltpu.SMEM(assignment.shape, jnp.int32),
    ]
    arguments = [
        queries, compact_keys, compact_values, slot_bias, targets, positions, assignment
    ]
    mate_state, *sent_queries = call(
        send_body,
        [state_shape] + [query_shape] * (query_devices - 1),
        "pack",
        2**20,
        arguments,
        small_scratch + [pltpu.SemaphoreType.DMA((3 + 2 * query_devices,))],
        space=pl.ANY,
        vmem=60,
    )
    own_state, own_queries = call(
        own_body,
        [state_shape, query_shape],
        "own",
        2**24,
        arguments,
        small_scratch + [pltpu.SemaphoreType.DMA((7,))],
        space=pl.ANY,
    )
    query_parts = [own_queries] + [
        exchange(sent_queries[turn - 1], query=turn) for turn in range(1, query_devices)
    ]
    states = [own_state, exchange(mate_state, page=1)]

    def in_columns(parts, axis):
        return jnp.concatenate(
            [
                lax.slice_in_dim(part, at * piece, (at + 1) * piece, axis=axis)
                for at in range(ranks)
                for part in parts
            ],
            axis=axis,
        )

    def read_queries(query_refs):
        return halves(in_columns([ref[:part_rows, :] for ref in query_refs], 0))

    def part_of(ref, at):
        return ref.at[pl.ds(at * packed_rows, packed_rows)]

    def parts_of(refs):
        return refs if len(refs) == CORES else [part_of(refs[0], at) for at in range(CORES)]

    def step_sizes(tile_refs):
        tile = jnp.sum(tile_refs[0][...], axis=0)
        sums = jnp.sum(tile, axis=1, keepdims=True)
        return (
            RATE_KEYS / jnp.sqrt(sums[0:1] / entry_total + EPSILON),
            RATE_VALUES / jnp.sqrt(sums[1:2] / entry_total + EPSILON),
            RATE_BIAS / jnp.sqrt(sums[2:3] / slot_total + EPSILON),
        )

    def updated(state_ref, grad_ref, sizes):
        key_end, value_end = slot_rows, 2 * slot_rows
        return (
            state_ref[:key_end, :] - sizes[0] * grad_ref[:key_end, :],
            state_ref[key_end:value_end, :] - sizes[1] * grad_ref[key_end:value_end, :],
            state_ref[value_end:, :] - sizes[2] * grad_ref[value_end:, :],
        )

    def forward(state_refs, query_refs, chunk_outs, weights_out, max_out, chunks):
        rank, _, _ = places()
        all_queries = read_queries(query_refs)
        position_row = in_columns(
            [tail_as_row(ref, part_rows + piece, pos_rows) for ref in query_refs], 1
        )
        all_scores, all_visible = [], []
        for at, ref in enumerate(state_refs):
            scores = dot(halves(ref[:slot_rows, :]), all_queries, 1, 1) * score_scale
            bias = row_as_column(tail_as_row(ref, 2 * slot_rows, bias_rows), width)
            scores = scores + jnp.concatenate([bias] * (query_rows // width), axis=1)
            page_start = ref[packed_rows - 1 : packed_rows, 0:1]
            visible = jnp.broadcast_to(position_row >= page_start, scores.shape)
            all_scores.append(jnp.where(visible, scores, MASKED))
            all_visible.append(visible)
        row_max = jnp.max(all_scores[0], axis=0, keepdims=True)
        for scores in all_scores[1:]:
            row_max = jnp.maximum(row_max, jnp.max(scores, axis=0, keepdims=True))
        row_total = jnp.zeros_like(row_max)
        row_sum = jnp.zeros((width, query_rows), jnp.float32)
        for at, ref in enumerate(state_refs):
            weights = jnp.where(all_visible[at], jnp.exp(all_scores[at] - row_max), 0.0)
            weights_out[at * slot_rows : (at + 1) * slot_rows, :] = weights
            row_total = row_total + jnp.sum(weights, axis=0, keepdims=True)
            values = halves(ref[slot_rows : 2 * slot_rows, :])
            row_sum = row_sum + dot(values, halves(weights), 0, 0)
        max_out[...] = jnp.broadcast_to(row_max, (TAIL, query_rows))
        tail = jnp.concatenate(
            [row_max, row_total, jnp.zeros((TAIL - 2, query_rows), jnp.float32)], axis=0
        )
        for at in range(ranks):
            columns = slice(at * chunk, (at + 1) * chunk)
            chunks[at, :width, :] = row_sum[:, columns]
            chunks[at, width:, :] = tail[:, columns]
        for turn in range(ranks):
            chunk_outs[turn][...] = chunks[rank ^ turn]

    chunk_shape = (width + TAIL, chunk)
    forward_shapes = [chunk_shape] * ranks + [(slots, query_rows), (TAIL, query_rows)]
    chunk_scratch = [pltpu.VMEM((ranks,) + chunk_shape, jnp.float32)]

    def first_body(*refs):
        state_refs, refs = refs[:2], refs[2:]
        query_refs, refs = refs[:query_devices], refs[query_devices:]
        chunk_outs, refs = refs[:ranks], refs[ranks:]
        forward(state_refs, query_refs, chunk_outs, *refs)

    def next_body(*refs):
        state_refs, refs = refs[:2], refs[2:]
        query_refs, refs = refs[:query_devices], refs[query_devices:]
        grad_refs, refs = refs[:2], refs[2:]
        tile_refs, refs = refs[: len(tiles)], refs[len(tiles) :]
        state_outs, refs = parts_of(refs[:1]), refs[1:]
        chunk_outs, refs = refs[:ranks], refs[ranks:]
        sizes = step_sizes(tile_refs)
        for at in range(2):
            keys, values, bias = updated(state_refs[at], grad_refs[at], sizes)
            state_outs[at][:slot_rows, :] = keys
            state_outs[at][slot_rows : 2 * slot_rows, :] = values
            state_outs[at][2 * slot_rows :, :] = bias
        forward(state_outs, query_refs, chunk_outs, *refs)

    def merge_body(*refs):
        query_refs, refs = refs[:query_devices], refs[query_devices:]
        chunk_refs, (merged_out,) = refs[:ranks], refs[ranks:]
        targets = jnp.concatenate(
            [ref[part_rows : part_rows + piece, :] for ref in query_refs], axis=0
        )
        row_max = chunk_refs[0][width : width + 1, :]
        for ref in chunk_refs[1:]:
            row_max = jnp.maximum(row_max, ref[width : width + 1, :])
        row_total = jnp.zeros_like(row_max)
        row_sum = jnp.zeros((width, chunk), jnp.float32)
        for ref in chunk_refs:
            factor = jnp.exp(ref[width : width + 1, :] - row_max)
            row_total = row_total + ref[width + 1 : width + 2, :] * factor
            row_sum = row_sum + ref[:width, :] * factor
        output = row_sum / row_total
        residual = output - targets.T
        row_delta = jnp.sum(residual * output, axis=0, keepdims=True)
        merged_out[:width, :] = residual
        merged_out[width:, :] = jnp.concatenate(
            [row_max, row_total, row_delta, jnp.zeros((TAIL - 3, chunk), jnp.float32)], axis=0
        )

    def backward_body(weights_ref, max_ref, *refs):
        state_refs, refs = parts_of(refs[: len(states)]), refs[len(states) :]
        query_refs, refs = refs[:query_devices], refs[query_devices:]
        merged_refs, refs = refs[:ranks], refs[ranks:]
        grad_outs, (squares_out, chunks) = refs[:2], refs[2:]
        rank, _, _ = places()
        for turn in range(ranks):
            chunks[rank ^ turn] = merged_refs[turn][...]
        joined = jnp.concatenate([chunks[at] for at in range(ranks)], axis=1)
        residual = joined[:width, :]
        row_max, row_total, row_delta = (
            joined[width + at : width + at + 1, :] for at in range(3)
        )
        all_queries = read_queries(query_refs)
        residual = halves(residual)
        factor = jnp.exp(max_ref[0:1, :] - row_max) / row_total
        ones = jnp.ones((TAIL, query_rows), jnp.bfloat16)
        ones = (ones, jnp.zeros_like(ones))
        squares = [jnp.zeros((1, width), jnp.float32)] * 3
        for at, ref in enumerate(state_refs):
            attention = weights_ref[at * slot_rows : (at + 1) * slot_rows, :] * factor
            grad_values = dot(halves(attention), residual, 1, 1)
            grad_probs = dot(halves(ref[slot_rows : 2 * slot_rows, :]), residual, 1, 0)
            grad_scores = halves(attention * (grad_probs - row_delta))
            grad_keys = dot(grad_scores, all_queries, 1, 0) * score_scale
            grad_bias = row_as_tail(dot(ones, grad_scores, 1, 1)[0:1, :], width)
            grad_outs[at][:slot_rows, :] = grad_keys
            grad_outs[at][slot_rows : 2 * slot_rows, :] = grad_values
            grad_outs[at][2 * slot_rows :, :] = grad_bias
            for which, grad in enumerate((grad_keys, grad_values, grad_bias)):
                squares[which] = squares[which] + jnp.sum(grad * grad, axis=0, keepdims=True)
        tile = jnp.concatenate(squares + [jnp.zeros((TAIL - 3, width), jnp.float32)], axis=0)
        for at in range(devices):
            squares_out[at] = tile

    def mate_body(*refs):
        *state_refs, out_ref = refs
        for at, ref in enumerate(state_refs):
            out_ref[pl.ds(at * packed_rows, packed_rows), :] = part_of(ref, 1)[...]

    out_masks = list(itertools.product(range(query_devices), range(CORES)))

    def to_output(packs, mask):
        if mask == (0, 0):
            return packs[0]
        return exchange(packs[mask[1]], page=mask[1], query=mask[0])

    for repeat in range(STEPS):
        last = repeat == STEPS - 1
        if repeat == 0:
            *chunk_parts, weights, maxima = call(
                first_body,
                forward_shapes,
                "forward",
                2 * matmul_cost,
                states + query_parts,
                chunk_scratch,
            )
        else:
            new_state, *chunk_parts, weights, maxima = call(
                next_body,
                [(CORES * packed_rows, width)] + forward_shapes,
                "update_forward",
                2 * matmul_cost,
                states + query_parts + grads + tiles,
                chunk_scratch,
            )
            states = [new_state]
        arrived = {
            turn: exchange(chunk_parts[turn], page=CORES * turn)
            for turn in reversed(range(1, ranks))
        }
        if repeat:
            new_states = states + [
                exchange(states[0], query=turn) for turn in range(1, query_devices)
            ]
        (merged,) = call(
            merge_body,
            [chunk_shape],
            "merge",
            2**20,
            query_parts + chunk_parts[:1] + list(arrived.values()),
        )
        all_merged = [merged] + [
            exchange(merged, page=CORES * turn) for turn in range(1, ranks)
        ]
        if repeat:
            (for_mate,) = call(
                mate_body,
                [(query_devices * packed_rows, width)],
                "mate_parts",
                2**20,
                new_states,
                after=all_merged[1:],
            )
            from_mate = exchange(for_mate, page=1)
        own_grad, mate_grad, squares = call(
            backward_body,
            packed_shapes + [(devices, TAIL, width)],
            "backward",
            3 * matmul_cost,
            [weights, maxima] + states + query_parts + all_merged,
            scratch=chunk_scratch,
        )
        grads = [own_grad, mate_grad]
        if last:
            all_grads = [to_output(grads, mask) for mask in out_masks]
        tiles = [
            lax.all_to_all(
                squares, ("page", "query", "head"), split_axis=0, concat_axis=0, tiled=True
            )
        ]

    def last_body(*refs):
        state_refs, (mate_ref, *refs) = refs[:query_devices], refs[query_devices:]
        state_refs = [
            part_of(mate_ref, turn) if flip else part_of(state_refs[turn], 0)
            for turn, flip in out_masks
        ]
        grad_refs, refs = refs[:local_heads], refs[local_heads:]
        tile_refs, (keys_out, values_out, bias_out) = refs[: len(tiles)], refs[len(tiles) :]
        _, core, me = places()
        sizes = step_sizes(tile_refs)
        for at, (turn, flip) in enumerate(out_masks):
            keys, values, bias = updated(state_refs[at], grad_refs[at], sizes)
            head = CORES * (me ^ turn) + (core ^ flip)
            keys_out[head] = keys
            values_out[head] = values
            bias_row = jnp.concatenate([bias[row : row + 1] for row in range(bias_rows)], axis=1)
            bias_out[pl.ds(head, 1), :] = bias_row

    return tuple(
        call(
            last_body,
            [compact_keys.shape, compact_values.shape, slot_bias.shape],
            "last_update",
            2**20,
            new_states + [from_mate] + all_grads + tiles,
        )
    )


def from_partner(value, axis, stride):
    mask = 2**stride
    pairs = [(source, source ^ mask) for source in range(lax.axis_size(axis))]
    return lax.ppermute(value, axis, pairs)


def squared_sums(grad_keys, grad_values, grad_bias):
    return jnp.stack(
        [
            jnp.sum(grad_keys * grad_keys),
            jnp.sum(grad_values * grad_values),
            jnp.sum(grad_bias * grad_bias),
        ]
    )


def apply_update(states, grads, totals, entry_count, slot_total):
    key_state, value_state, bias_state = states
    grad_keys, grad_values, grad_bias = grads
    rms_keys = jnp.sqrt(totals[0] / entry_count + EPSILON)
    rms_values = jnp.sqrt(totals[1] / entry_count + EPSILON)
    rms_bias = jnp.sqrt(totals[2] / slot_total + EPSILON)
    return (
        key_state - RATE_KEYS * grad_keys / rms_keys,
        value_state - RATE_VALUES * grad_values / rms_values,
        bias_state - RATE_BIAS * grad_bias / rms_bias,
    )


def local_gradients(queries, targets, visible, compact_keys, compact_values, slot_bias):
    score_scale = 1.0 / math.sqrt(queries.shape[2])
    scores = jnp.einsum("hqd,hsd->hqs", queries, compact_keys, precision=HIGHEST) * score_scale
    scores = jnp.where(visible, scores + slot_bias[:, None, :], MASKED)
    local_max = jnp.max(scores, axis=2)
    row_max = lax.pmax(local_max, "page")
    weights = jnp.where(visible, jnp.exp(scores - row_max[:, :, None]), 0.0)
    local_sum = jnp.einsum("hqs,hsd->hqd", weights, compact_values, precision=HIGHEST)
    row_total, row_sum = lax.psum((jnp.sum(weights, axis=2), local_sum), "page")
    attention = weights / row_total[:, :, None]
    output = row_sum / row_total[:, :, None]
    residual = output - targets
    grad_values = jnp.einsum("hqs,hqd->hsd", attention, residual, precision=HIGHEST)
    row_delta = jnp.sum(residual * output, axis=2)
    grad_probs = jnp.einsum("hqd,hsd->hqs", residual, compact_values, precision=HIGHEST)
    grad_scores = attention * (grad_probs - row_delta[:, :, None])
    grad_bias = jnp.sum(grad_scores, axis=1)
    grad_keys = jnp.einsum("hqs,hqd->hsd", grad_scores, queries, precision=HIGHEST) * score_scale
    return (grad_keys, grad_values, grad_bias)


def per_device(queries, compact_keys, compact_values, slot_bias, targets, positions, assignment):
    page_number = assignment[lax.axis_index("page")]
    local_heads = compact_keys.shape[0]
    slot_total = local_heads * lax.axis_size("head") * compact_keys.shape[1] * lax.axis_size("page")
    entry_count = slot_total * compact_keys.shape[2]
    query_count = lax.axis_size("query")
    heads_kept = max(local_heads // query_count, 1)
    query_parts = max(query_count // local_heads, 1)
    part_rows = queries.shape[1] // query_parts

    def split_items(array):
        width = array.shape[2]
        array = array.reshape(local_heads // heads_kept, heads_kept, query_parts, part_rows, width)
        array = jnp.transpose(array, (0, 2, 1, 3, 4))
        return array.reshape(query_count, heads_kept, part_rows, width)

    def join_items(array):
        width = array.shape[3]
        array = jnp.transpose(array, (1, 0, 2, 3))
        return array.reshape(heads_kept, query_count * part_rows, width)

    position_column = positions.astype(jnp.float32)[:, :, None]
    got_queries, got_targets, got_positions = (
        lax.all_to_all(split_items(queries), "query", split_axis=0, concat_axis=0, tiled=True),
        lax.all_to_all(split_items(targets), "query", split_axis=0, concat_axis=0, tiled=True),
        lax.all_to_all(
            split_items(position_column), "query", split_axis=0, concat_axis=0, tiled=True
        ),
    )
    group_queries = join_items(got_queries)
    group_targets = join_items(got_targets)
    group_positions = join_items(got_positions)[:, :, 0]
    visible = (page_number.astype(jnp.float32) <= jnp.floor(group_positions / PAGE_LEN))[:, :, None]
    query_index = lax.axis_index("query")
    first_head = query_index // query_parts * heads_kept
    key_state = lax.dynamic_slice_in_dim(compact_keys, first_head, heads_kept, 0)
    value_state = lax.dynamic_slice_in_dim(compact_values, first_head, heads_kept, 0)
    bias_state = lax.dynamic_slice_in_dim(slot_bias, first_head, heads_kept, 0)
    counted = (query_index % query_parts == 0).astype(jnp.float32)
    for repeat in range(STEPS):
        grads = local_gradients(
            group_queries, group_targets, visible, key_state, value_state, bias_state
        )
        for bit in range(query_parts.bit_length() - 1):
            partner = from_partner((grads[0], grads[1], grads[2]), "query", bit)
            grads = (grads[0] + partner[0], grads[1] + partner[1], grads[2] + partner[2])
        totals = lax.psum(
            squared_sums(grads[0], grads[1], grads[2]) * counted, ("page", "query", "head")
        )
        key_state, value_state, bias_state = apply_update(
            (key_state, value_state, bias_state), grads, totals, entry_count, slot_total
        )
    all_keys, all_values, all_bias = (
        lax.all_gather(key_state, "query", axis=0, tiled=True),
        lax.all_gather(value_state, "query", axis=0, tiled=True),
        lax.all_gather(bias_state, "query", axis=0, tiled=True),
    )
    slot_rows = compact_keys.shape[1]
    head_width = compact_keys.shape[2]
    all_keys = all_keys.reshape(
        local_heads // heads_kept, query_parts, heads_kept, slot_rows, head_width
    )[:, 0]
    all_values = all_values.reshape(
        local_heads // heads_kept, query_parts, heads_kept, slot_rows, head_width
    )[:, 0]
    all_bias = all_bias.reshape(local_heads // heads_kept, query_parts, heads_kept, slot_rows)[:, 0]
    return (
        all_keys.reshape(local_heads, slot_rows, head_width),
        all_values.reshape(local_heads, slot_rows, head_width),
        all_bias.reshape(local_heads, slot_rows),
    )


def solution(mesh):
    placed = (
        P("head", "query", None),
        P("head", "page", None),
        P("head", "page", None),
        P("head", "page"),
        P("head", "query", None),
        P("head", "query"),
        P(),
    )

    def program(*args):
        plan = direct_per_device if direct_plan_fits(mesh, args[0], args[1]) else per_device
        return jax.shard_map(
            plan,
            mesh=mesh,
            in_specs=placed,
            out_specs=(P("head", "page", None), P("head", "page", None), P("head", "page")),
            check_vma=False,
        )(*args)

    return program
```

```python
import itertools
import math

import jax
import jax.numpy as jnp
from jax import lax
from jax.experimental import pallas as pl
from jax.experimental.pallas import tpu as pltpu
from jax.sharding import PartitionSpec as P

STEPS = 2
PAGE_LEN = 32768


MASKED = -1e30
EPSILON = 1e-06
RATE_KEYS = 0.05
RATE_VALUES = 0.05
RATE_BIAS = 0.2
HIGHEST = lax.Precision.HIGHEST
TAIL = 8
CORES = 2


def exchange(value, **masks):
    axes = tuple(masks)
    sizes = [lax.axis_size(axis) for axis in axes]

    def flat(place):
        index = 0
        for size, at in zip(sizes, place):
            index = index * size + at
        return index

    pairs = [
        (flat(place), flat([at ^ mask for at, mask in zip(place, masks.values())]))
        for place in itertools.product(*map(range, sizes))
    ]
    return lax.ppermute(value, axes, pairs)


def halves(value):
    high = value.astype(jnp.bfloat16)
    return high, (value - high.astype(jnp.float32)).astype(jnp.bfloat16)


def dot(left, right, left_dim, right_dim):
    def one_pass(left_half, right_half):
        return lax.dot_general(
            left_half,
            right_half,
            (((left_dim,), (right_dim,)), ((), ())),
            preferred_element_type=jnp.float32,
        )

    cross = one_pass(left[0], right[1]) + one_pass(left[1], right[0])
    return one_pass(left[0], right[0]) + cross


def call(body, out_shapes, name, cost, operands, scratch=(), after=(), space=pltpu.VMEM, vmem=32):
    spaces = [space] * len(operands) + [pl.ANY] * len(after)
    count = len(operands)

    def without_after(*refs):
        body(*refs[:count], *refs[count + len(after) :])

    return pl.pallas_call(
        without_after,
        out_shape=[jax.ShapeDtypeStruct(shape, jnp.float32) for shape in out_shapes],
        in_specs=[pl.BlockSpec(memory_space=space) for space in spaces],
        out_specs=[pl.BlockSpec(memory_space=pltpu.VMEM) for _ in out_shapes],
        scratch_shapes=scratch,
        compiler_params=pltpu.CompilerParams(vmem_limit_bytes=vmem * 2**20),
        cost_estimate=pl.CostEstimate(flops=cost, bytes_accessed=2**20, transcendentals=0),
        name=name,
    )(*operands, *after)


def row_as_tail(row, width):
    rows = [row[:, at : at + width] for at in range(0, row.shape[1], width)]
    rows.append(jnp.zeros((TAIL - len(rows), width), row.dtype))
    return jnp.concatenate(rows, axis=0)


def tail_as_row(ref, start, count):
    return jnp.concatenate([ref[start + at : start + at + 1, :] for at in range(count)], axis=1)


def row_as_column(row, width):
    parts = []
    for at in range(0, row.shape[1], width):
        parts.append(jnp.broadcast_to(row[:, at : at + width], (width, width)).T)
    return jnp.concatenate(parts, axis=0)


def direct_plan_fits(mesh, queries, compact_keys):
    sizes = [mesh.shape[axis] for axis in ("page", "query", "head")]
    pages, query_devices, head_devices = sizes
    local_heads = queries.shape[0] // head_devices
    part_rows = queries.shape[1] // query_devices
    slot_rows = compact_keys.shape[1] // pages
    width = queries.shape[2]
    if any(size & (size - 1) for size in sizes) or pages < CORES or width % 128:
        return False
    if local_heads != CORES * query_devices:
        return False
    ranks = pages // CORES
    chunk = part_rows * query_devices // ranks
    return (
        part_rows * query_devices % ranks == 0
        and chunk % 128 == 0
        and part_rows % (8 * ranks) == 0
        and (part_rows // ranks % 128 == 0 or 1024 % (part_rows // ranks * 8) == 0)
        and slot_rows % width == 0
        and part_rows % width == 0
        and max(slot_rows, part_rows) < TAIL * width
    )


def direct_per_device(
    queries, compact_keys, compact_values, slot_bias, targets, positions, assignment
):
    local_heads, part_rows, width = queries.shape
    slot_rows = compact_keys.shape[1]
    query_devices = lax.axis_size("query")
    head_devices = lax.axis_size("head")
    ranks = lax.axis_size("page") // CORES
    query_rows = part_rows * query_devices
    chunk, piece = query_rows // ranks, part_rows // ranks
    slot_total = local_heads * head_devices * slot_rows * lax.axis_size("page")
    entry_total = slot_total * width
    score_scale = 1.0 / math.sqrt(width)
    slots = CORES * slot_rows
    devices = ranks * CORES * query_devices * head_devices
    pos_rows = part_rows // width
    bias_rows = slot_rows // width
    packed_rows = 2 * slot_rows + TAIL
    packed_shapes = [(packed_rows, width)] * CORES
    matmul_cost = 3 * 2 * slots * query_rows * width

    def places():
        page = lax.axis_index("page")
        return page // CORES, page % CORES, lax.axis_index("query")

    def pack_queries(head, rank, queries, targets, out):
        rows = pl.ds(pl.multiple_of(rank * piece, piece), piece)
        return [
            (queries.at[head], out.at[pl.ds(0, part_rows)]),
            (targets.at[head, rows], out.at[pl.ds(part_rows, piece)]),
        ]

    def pack_state(head, keys, values, out):
        return [
            (keys.at[head], out.at[pl.ds(0, slot_rows)]),
            (values.at[head], out.at[pl.ds(slot_rows, slot_rows)]),
        ]

    def start_all(copies, sems, first=0):
        copies = [
            pltpu.make_async_copy(source, target, sems.at[first + at])
            for at, (source, target) in enumerate(copies)
        ]
        for copy in copies:
            copy.start()
        return copies

    def position_tail(head, positions_ref):
        return row_as_tail(positions_ref[pl.ds(head, 1), :].astype(jnp.float32), width)

    def state_tail(head, page, bias_ref, assignment_ref):
        page_start = (assignment_ref[page] * PAGE_LEN).astype(jnp.float32)
        tail = row_as_tail(bias_ref[pl.ds(head, 1), :], width)
        return jnp.concatenate(
            [tail[: TAIL - 1], jnp.full((1, width), page_start, jnp.float32)], axis=0
        )

    def pack_tails(refs, heads, page, bias_ref, assignment_ref):
        for ref, head in zip(refs, heads):
            ref[2 * slot_rows :, :] = state_tail(head, page, bias_ref, assignment_ref)

    def part_of(ref, at):
        return ref.at[pl.ds(at * packed_rows, packed_rows)]

    def send_body(keys, values, biases, assignment, states_out, bias_ref, assignment_ref, sems):
        rank, core, me = places()
        heads = [CORES * (me ^ turn) + (core ^ 1) for turn in range(query_devices)]
        outs = [part_of(states_out, turn) for turn in range(query_devices)]
        small = start_all([(assignment, assignment_ref), (biases, bias_ref)], sems)
        copies = [pair for head, out in zip(heads, outs) for pair in pack_state(head, keys, values, out)]
        copies = start_all(copies, sems, 2)
        for copy in small:
            copy.wait()
        pack_tails(outs, heads, CORES * rank + core, bias_ref, assignment_ref)
        for copy in copies:
            copy.wait()

    def own_body(
        queries, keys, values, biases, targets, positions, assignment, states_out, *refs
    ):
        query_outs, refs = refs[:query_devices], refs[query_devices:]
        bias_ref, assignment_ref, positions_ref, sems = refs
        rank, core, me = places()
        heads = [CORES * (me ^ turn) + core for turn in range(query_devices)]
        outs = [part_of(states_out, turn) for turn in range(query_devices)]
        small = start_all(
            [(assignment, assignment_ref), (biases, bias_ref), (positions, positions_ref)], sems
        )
        copies = []
        for head, out, query_out in zip(heads, outs, query_outs):
            copies += pack_state(head, keys, values, out)
            copies += pack_queries(head, rank, queries, targets, query_out)
        copies = start_all(copies, sems, 3)
        for copy in small:
            copy.wait()
        pack_tails(outs, heads, CORES * rank + core, bias_ref, assignment_ref)
        for head, query_out in zip(heads, query_outs):
            query_out[part_rows + piece :, :] = position_tail(head, positions_ref)
        for copy in copies:
            copy.wait()

    states_shape = (query_devices * packed_rows, width)
    query_shape = (part_rows + piece + TAIL, width)
    small_scratch = [
        pltpu.VMEM(slot_bias.shape, jnp.float32),
        pltpu.SMEM(assignment.shape, jnp.int32),
    ]
    (sent_states,) = call(
        send_body,
        [states_shape],
        "pack",
        2**20,
        [compact_keys, compact_values, slot_bias, assignment],
        small_scratch + [pltpu.SemaphoreType.DMA((2 + 2 * query_devices,))],
        space=pl.ANY,
        vmem=60,
    )
    mate_states = exchange(sent_states, page=1)
    own_states, *own_queries = call(
        own_body,
        [states_shape] + [query_shape] * query_devices,
        "own",
        2**24,
        [queries, compact_keys, compact_values, slot_bias, targets, positions, assignment],
        small_scratch
        + [
            pltpu.VMEM(positions.shape, jnp.int32),
            pltpu.SemaphoreType.DMA((3 + 4 * query_devices,)),
        ],
        space=pl.ANY,
    )
    query_parts = own_queries[:1] + [
        exchange(own_queries[turn], query=turn) for turn in range(1, query_devices)
    ]
    states = [own_states, mate_states]

    def in_columns(parts, axis):
        return jnp.concatenate(
            [
                lax.slice_in_dim(part, at * piece, (at + 1) * piece, axis=axis)
                for at in range(ranks)
                for part in parts
            ],
            axis=axis,
        )

    def read_queries(query_refs):
        return halves(in_columns([ref[:part_rows, :] for ref in query_refs], 0))

    def pages_of(refs):
        if len(refs) == CORES:
            return [part_of(ref, 0) for ref in refs]
        return [part_of(refs[0], at) for at in range(CORES)]

    def step_sizes(tile_refs):
        tile = jnp.sum(tile_refs[0][...], axis=0)
        sums = jnp.sum(tile, axis=1, keepdims=True)
        return (
            RATE_KEYS / jnp.sqrt(sums[0:1] / entry_total + EPSILON),
            RATE_VALUES / jnp.sqrt(sums[1:2] / entry_total + EPSILON),
            RATE_BIAS / jnp.sqrt(sums[2:3] / slot_total + EPSILON),
        )

    def updated(state_ref, grad_ref, sizes):
        key_end, value_end = slot_rows, 2 * slot_rows
        return (
            state_ref[:key_end, :] - sizes[0] * grad_ref[:key_end, :],
            state_ref[key_end:value_end, :] - sizes[1] * grad_ref[key_end:value_end, :],
            state_ref[value_end:, :] - sizes[2] * grad_ref[value_end:, :],
        )

    def position_row(ref):
        return tail_as_row(ref, part_rows + piece, pos_rows)

    def local_weights(state_refs, queries, positions):
        columns = positions.shape[1]
        all_scores, all_visible = [], []
        for ref in state_refs:
            scores = dot(halves(ref[:slot_rows, :]), queries, 1, 1) * score_scale
            bias = row_as_column(tail_as_row(ref, 2 * slot_rows, bias_rows), width)
            scores = scores + jnp.concatenate([bias] * (columns // width), axis=1)
            page_start = ref[packed_rows - 1 : packed_rows, 0:1]
            visible = jnp.broadcast_to(positions >= page_start, scores.shape)
            all_scores.append(jnp.where(visible, scores, MASKED))
            all_visible.append(visible)
        row_max = jnp.max(all_scores[0], axis=0, keepdims=True)
        for scores in all_scores[1:]:
            row_max = jnp.maximum(row_max, jnp.max(scores, axis=0, keepdims=True))
        weights = [
            jnp.where(visible, jnp.exp(scores - row_max), 0.0)
            for scores, visible in zip(all_scores, all_visible)
        ]
        return weights, row_max

    def local_sums(state_refs, weights, row_max):
        row_total = jnp.zeros_like(row_max)
        row_sum = jnp.zeros((width, row_max.shape[1]), jnp.float32)
        for ref, part in zip(state_refs, weights):
            row_total = row_total + jnp.sum(part, axis=0, keepdims=True)
            values = halves(ref[slot_rows : 2 * slot_rows, :])
            row_sum = row_sum + dot(values, halves(part), 0, 0)
        empty = jnp.zeros((TAIL - 2, row_max.shape[1]), jnp.float32)
        return jnp.concatenate([row_sum, row_max, row_total, empty], axis=0)

    def store_chunks(sums, chunk_outs, chunks):
        rank, _, _ = places()
        for at in range(ranks):
            chunks[at] = sums[:, at * chunk : (at + 1) * chunk]
        for turn in range(ranks):
            chunk_outs[turn][...] = chunks[rank ^ turn]

    def store_weights(weights, row_max, weights_out, max_out):
        for at, part in enumerate(weights):
            weights_out[at * slot_rows : (at + 1) * slot_rows, :] = part
        max_out[...] = jnp.broadcast_to(row_max, (TAIL, query_rows))

    chunk_shape = (width + TAIL, chunk)
    weight_shapes = [(slots, query_rows), (TAIL, query_rows)]
    chunk_scratch = [pltpu.VMEM((ranks,) + chunk_shape, jnp.float32)]

    def first_body(own_ref, mate_ref, *refs):
        query_refs, refs = refs[:query_devices], refs[query_devices:]
        chunk_outs, (chunks,) = refs[:ranks], refs[ranks:]
        sums = []
        for turn, ref in enumerate(query_refs):
            state_refs = [part_of(own_ref, turn), part_of(mate_ref, turn)]
            weights, row_max = local_weights(
                state_refs, halves(ref[:part_rows, :]), position_row(ref)
            )
            sums.append(local_sums(state_refs, weights, row_max))
        store_chunks(in_columns(sums, 1), chunk_outs, chunks)

    def all_weights(state_refs, query_refs):
        positions = in_columns([position_row(ref) for ref in query_refs], 1)
        return local_weights(state_refs, read_queries(query_refs), positions)

    def weights_body(*refs):
        state_refs, refs = pages_of(refs[:2]), refs[2:]
        query_refs, outs = refs[:query_devices], refs[query_devices:]
        store_weights(*all_weights(state_refs, query_refs), *outs)

    def next_body(*refs):
        state_refs, refs = pages_of(refs[:2]), refs[2:]
        query_refs, refs = refs[:query_devices], refs[query_devices:]
        grad_refs, refs = refs[:2], refs[2:]
        tile_refs, refs = refs[: len(tiles)], refs[len(tiles) :]
        state_outs, refs = pages_of(refs[:1]), refs[1:]
        chunk_outs, (weights_out, max_out, chunks) = refs[:ranks], refs[ranks:]
        sizes = step_sizes(tile_refs)
        for at in range(2):
            keys, values, bias = updated(state_refs[at], grad_refs[at], sizes)
            state_outs[at][:slot_rows, :] = keys
            state_outs[at][slot_rows : 2 * slot_rows, :] = values
            state_outs[at][2 * slot_rows :, :] = bias
        weights, row_max = all_weights(state_outs, query_refs)
        store_weights(weights, row_max, weights_out, max_out)
        store_chunks(local_sums(state_outs, weights, row_max), chunk_outs, chunks)

    def merged_chunk(query_refs, chunk_refs):
        targets = jnp.concatenate(
            [ref[part_rows : part_rows + piece, :] for ref in query_refs], axis=0
        )
        row_max = chunk_refs[0][width : width + 1, :]
        for ref in chunk_refs[1:]:
            row_max = jnp.maximum(row_max, ref[width : width + 1, :])
        row_total = jnp.zeros_like(row_max)
        row_sum = jnp.zeros((width, chunk), jnp.float32)
        for ref in chunk_refs:
            factor = jnp.exp(ref[width : width + 1, :] - row_max)
            row_total = row_total + ref[width + 1 : width + 2, :] * factor
            row_sum = row_sum + ref[:width, :] * factor
        output = row_sum / row_total
        residual = output - targets.T
        row_delta = jnp.sum(residual * output, axis=0, keepdims=True)
        empty = jnp.zeros((TAIL - 3, chunk), jnp.float32)
        return residual, jnp.concatenate([row_max, row_total, row_delta, empty], axis=0)

    fold = max(1, 128 // piece)
    folded = width // fold
    piece_shape = (folded + TAIL, fold * piece)

    def first_merge_body(*refs):
        query_refs, refs = refs[:query_devices], refs[query_devices:]
        chunk_refs, piece_outs = refs[:ranks], refs[ranks:]
        residual, tail = merged_chunk(query_refs, chunk_refs)
        for turn, out in enumerate(piece_outs):
            columns = slice(turn * piece, (turn + 1) * piece)
            out[:folded, :] = jnp.concatenate(
                [residual[at * folded : (at + 1) * folded, columns] for at in range(fold)], axis=1
            )
            out[folded:, :] = jnp.concatenate([tail[:, columns]] * fold, axis=1)

    def merge_body(*refs):
        query_refs, refs = refs[:query_devices], refs[query_devices:]
        chunk_refs, (merged_out,) = refs[:ranks], refs[ranks:]
        residual, tail = merged_chunk(query_refs, chunk_refs)
        merged_out[:width, :] = residual
        merged_out[width:, :] = tail

    def join_pieces(piece_refs, pieces):
        rank, _, _ = places()
        for at, ref in enumerate(piece_refs):
            pieces[rank ^ (at % ranks), at // ranks] = ref[...]
        joined = []
        for at in range(ranks):
            for turn in range(query_devices):
                groups = [
                    pieces[at, turn, :folded, group * piece : (group + 1) * piece]
                    for group in range(fold)
                ]
                joined.append(
                    jnp.concatenate(groups + [pieces[at, turn, folded:, :piece]], axis=0)
                )
        return jnp.concatenate(joined, axis=1)

    def join_chunks(merged_refs, chunks):
        rank, _, _ = places()
        for turn, ref in enumerate(merged_refs):
            chunks[rank ^ turn] = ref[...]
        return jnp.concatenate([chunks[at] for at in range(ranks)], axis=1)

    def backward_body(weights_ref, max_ref, *refs):
        state_refs, refs = pages_of(refs[: len(states)]), refs[len(states) :]
        query_refs, refs = refs[:query_devices], refs[query_devices:]
        merged_refs, refs = refs[: len(all_merged)], refs[len(all_merged) :]
        grad_outs, (squares_out, received) = refs[:2], refs[2:]
        if len(states) == CORES:
            joined = join_pieces(merged_refs, received)
        else:
            joined = join_chunks(merged_refs, received)
        residual = joined[:width, :]
        row_max, row_total, row_delta = (
            joined[width + at : width + at + 1, :] for at in range(3)
        )
        all_queries = read_queries(query_refs)
        residual = halves(residual)
        factor = jnp.exp(max_ref[0:1, :] - row_max) / row_total
        ones = jnp.ones((TAIL, query_rows), jnp.bfloat16)
        ones = (ones, jnp.zeros_like(ones))
        squares = [jnp.zeros((1, width), jnp.float32)] * 3
        for at, ref in enumerate(state_refs):
            attention = weights_ref[at * slot_rows : (at + 1) * slot_rows, :] * factor
            grad_values = dot(halves(attention), residual, 1, 1)
            grad_probs = dot(halves(ref[slot_rows : 2 * slot_rows, :]), residual, 1, 0)
            grad_scores = halves(attention * (grad_probs - row_delta))
            grad_keys = dot(grad_scores, all_queries, 1, 0) * score_scale
            grad_bias = row_as_tail(dot(ones, grad_scores, 1, 1)[0:1, :], width)
            grad_outs[at][:slot_rows, :] = grad_keys
            grad_outs[at][slot_rows : 2 * slot_rows, :] = grad_values
            grad_outs[at][2 * slot_rows :, :] = grad_bias
            for which, grad in enumerate((grad_keys, grad_values, grad_bias)):
                squares[which] = squares[which] + jnp.sum(grad * grad, axis=0, keepdims=True)
        tile = jnp.concatenate(squares + [jnp.zeros((TAIL - 3, width), jnp.float32)], axis=0)
        for at in range(devices):
            squares_out[at] = tile

    def mate_body(*refs):
        *state_refs, out_ref = refs
        for at, ref in enumerate(state_refs):
            out_ref[pl.ds(at * packed_rows, packed_rows), :] = part_of(ref, 1)[...]

    out_masks = list(itertools.product(range(query_devices), range(CORES)))

    def to_device(value, **masks):
        masks = {axis: mask for axis, mask in masks.items() if mask}
        return exchange(value, **masks) if masks else value

    for repeat in range(STEPS):
        last = repeat == STEPS - 1
        if repeat == 0:
            chunk_parts = call(
                first_body,
                [chunk_shape] * ranks,
                "forward",
                2 * matmul_cost,
                states + own_queries,
                chunk_scratch,
            )
            weights, maxima = call(
                weights_body, weight_shapes, "weights", matmul_cost, states + query_parts
            )
        else:
            new_state, *chunk_parts, weights, maxima = call(
                next_body,
                [(CORES * packed_rows, width)] + [chunk_shape] * ranks + weight_shapes,
                "update_forward",
                2 * matmul_cost,
                states + query_parts + grads + tiles,
                chunk_scratch,
            )
            states = [new_state]
        arrived = {
            turn: exchange(chunk_parts[turn], page=CORES * turn)
            for turn in reversed(range(1, ranks))
        }
        if repeat:
            new_states = states + [
                exchange(states[0], query=turn) for turn in range(1, query_devices)
            ]
        chunk_parts = [chunk_parts[0]] + list(arrived.values())
        if repeat == 0:
            pieces = call(
                first_merge_body,
                [piece_shape] * query_devices,
                "first_merge",
                2**20,
                own_queries + chunk_parts,
            )
            all_merged = [
                to_device(pieces[turn], page=CORES * shift, query=turn)
                for turn in range(query_devices)
                for shift in range(ranks)
            ]
            received = pltpu.VMEM((ranks, query_devices) + piece_shape, jnp.float32)
        else:
            (merged,) = call(
                merge_body, [chunk_shape], "merge", 2**20, query_parts + chunk_parts
            )
            all_merged = [to_device(merged, page=CORES * shift) for shift in range(ranks)]
            received = chunk_scratch[0]
        if repeat:
            (for_mate,) = call(
                mate_body,
                [(query_devices * packed_rows, width)],
                "mate_parts",
                2**20,
                new_states,
                after=all_merged[1:],
            )
            from_mate = exchange(for_mate, page=1)
        own_grad, mate_grad, squares = call(
            backward_body,
            packed_shapes + [(devices, TAIL, width)],
            "backward",
            3 * matmul_cost,
            [weights, maxima] + states + query_parts + all_merged,
            scratch=[received],
        )
        grads = [own_grad, mate_grad]
        if last:
            all_grads = [
                to_device(grads[flip], page=flip, query=turn) for turn, flip in out_masks
            ]
        tiles = [
            lax.all_to_all(
                squares, ("page", "query", "head"), split_axis=0, concat_axis=0, tiled=True
            )
        ]

    def last_body(*refs):
        state_refs, (mate_ref, *refs) = refs[:query_devices], refs[query_devices:]
        state_refs = [
            part_of(mate_ref, turn) if flip else part_of(state_refs[turn], 0)
            for turn, flip in out_masks
        ]
        grad_refs, refs = refs[:local_heads], refs[local_heads:]
        tile_refs, (keys_out, values_out, bias_out) = refs[: len(tiles)], refs[len(tiles) :]
        _, core, me = places()
        sizes = step_sizes(tile_refs)
        for at, (turn, flip) in enumerate(out_masks):
            keys, values, bias = updated(state_refs[at], grad_refs[at], sizes)
            head = CORES * (me ^ turn) + (core ^ flip)
            keys_out[head] = keys
            values_out[head] = values
            bias_row = jnp.concatenate([bias[row : row + 1] for row in range(bias_rows)], axis=1)
            bias_out[pl.ds(head, 1), :] = bias_row

    return tuple(
        call(
            last_body,
            [compact_keys.shape, compact_values.shape, slot_bias.shape],
            "last_update",
            2**20,
            new_states + [from_mate] + all_grads + tiles,
        )
    )


def from_partner(value, axis, stride):
    mask = 2**stride
    pairs = [(source, source ^ mask) for source in range(lax.axis_size(axis))]
    return lax.ppermute(value, axis, pairs)


def squared_sums(grad_keys, grad_values, grad_bias):
    return jnp.stack(
        [
            jnp.sum(grad_keys * grad_keys),
            jnp.sum(grad_values * grad_values),
            jnp.sum(grad_bias * grad_bias),
        ]
    )


def apply_update(states, grads, totals, entry_count, slot_total):
    key_state, value_state, bias_state = states
    grad_keys, grad_values, grad_bias = grads
    rms_keys = jnp.sqrt(totals[0] / entry_count + EPSILON)
    rms_values = jnp.sqrt(totals[1] / entry_count + EPSILON)
    rms_bias = jnp.sqrt(totals[2] / slot_total + EPSILON)
    return (
        key_state - RATE_KEYS * grad_keys / rms_keys,
        value_state - RATE_VALUES * grad_values / rms_values,
        bias_state - RATE_BIAS * grad_bias / rms_bias,
    )


def local_gradients(queries, targets, visible, compact_keys, compact_values, slot_bias):
    score_scale = 1.0 / math.sqrt(queries.shape[2])
    scores = jnp.einsum("hqd,hsd->hqs", queries, compact_keys, precision=HIGHEST) * score_scale
    scores = jnp.where(visible, scores + slot_bias[:, None, :], MASKED)
    local_max = jnp.max(scores, axis=2)
    row_max = lax.pmax(local_max, "page")
    weights = jnp.where(visible, jnp.exp(scores - row_max[:, :, None]), 0.0)
    local_sum = jnp.einsum("hqs,hsd->hqd", weights, compact_values, precision=HIGHEST)
    row_total, row_sum = lax.psum((jnp.sum(weights, axis=2), local_sum), "page")
    attention = weights / row_total[:, :, None]
    output = row_sum / row_total[:, :, None]
    residual = output - targets
    grad_values = jnp.einsum("hqs,hqd->hsd", attention, residual, precision=HIGHEST)
    row_delta = jnp.sum(residual * output, axis=2)
    grad_probs = jnp.einsum("hqd,hsd->hqs", residual, compact_values, precision=HIGHEST)
    grad_scores = attention * (grad_probs - row_delta[:, :, None])
    grad_bias = jnp.sum(grad_scores, axis=1)
    grad_keys = jnp.einsum("hqs,hqd->hsd", grad_scores, queries, precision=HIGHEST) * score_scale
    return (grad_keys, grad_values, grad_bias)


def per_device(queries, compact_keys, compact_values, slot_bias, targets, positions, assignment):
    page_number = assignment[lax.axis_index("page")]
    local_heads = compact_keys.shape[0]
    slot_total = local_heads * lax.axis_size("head") * compact_keys.shape[1] * lax.axis_size("page")
    entry_count = slot_total * compact_keys.shape[2]
    query_count = lax.axis_size("query")
    heads_kept = max(local_heads // query_count, 1)
    query_parts = max(query_count // local_heads, 1)
    part_rows = queries.shape[1] // query_parts

    def split_items(array):
        width = array.shape[2]
        array = array.reshape(local_heads // heads_kept, heads_kept, query_parts, part_rows, width)
        array = jnp.transpose(array, (0, 2, 1, 3, 4))
        return array.reshape(query_count, heads_kept, part_rows, width)

    def join_items(array):
        width = array.shape[3]
        array = jnp.transpose(array, (1, 0, 2, 3))
        return array.reshape(heads_kept, query_count * part_rows, width)

    position_column = positions.astype(jnp.float32)[:, :, None]
    got_queries, got_targets, got_positions = (
        lax.all_to_all(split_items(queries), "query", split_axis=0, concat_axis=0, tiled=True),
        lax.all_to_all(split_items(targets), "query", split_axis=0, concat_axis=0, tiled=True),
        lax.all_to_all(
            split_items(position_column), "query", split_axis=0, concat_axis=0, tiled=True
        ),
    )
    group_queries = join_items(got_queries)
    group_targets = join_items(got_targets)
    group_positions = join_items(got_positions)[:, :, 0]
    visible = (page_number.astype(jnp.float32) <= jnp.floor(group_positions / PAGE_LEN))[:, :, None]
    query_index = lax.axis_index("query")
    first_head = query_index // query_parts * heads_kept
    key_state = lax.dynamic_slice_in_dim(compact_keys, first_head, heads_kept, 0)
    value_state = lax.dynamic_slice_in_dim(compact_values, first_head, heads_kept, 0)
    bias_state = lax.dynamic_slice_in_dim(slot_bias, first_head, heads_kept, 0)
    counted = (query_index % query_parts == 0).astype(jnp.float32)
    for repeat in range(STEPS):
        grads = local_gradients(
            group_queries, group_targets, visible, key_state, value_state, bias_state
        )
        for bit in range(query_parts.bit_length() - 1):
            partner = from_partner((grads[0], grads[1], grads[2]), "query", bit)
            grads = (grads[0] + partner[0], grads[1] + partner[1], grads[2] + partner[2])
        totals = lax.psum(
            squared_sums(grads[0], grads[1], grads[2]) * counted, ("page", "query", "head")
        )
        key_state, value_state, bias_state = apply_update(
            (key_state, value_state, bias_state), grads, totals, entry_count, slot_total
        )
    all_keys, all_values, all_bias = (
        lax.all_gather(key_state, "query", axis=0, tiled=True),
        lax.all_gather(value_state, "query", axis=0, tiled=True),
        lax.all_gather(bias_state, "query", axis=0, tiled=True),
    )
    slot_rows = compact_keys.shape[1]
    head_width = compact_keys.shape[2]
    all_keys = all_keys.reshape(
        local_heads // heads_kept, query_parts, heads_kept, slot_rows, head_width
    )[:, 0]
    all_values = all_values.reshape(
        local_heads // heads_kept, query_parts, heads_kept, slot_rows, head_width
    )[:, 0]
    all_bias = all_bias.reshape(local_heads // heads_kept, query_parts, heads_kept, slot_rows)[:, 0]
    return (
        all_keys.reshape(local_heads, slot_rows, head_width),
        all_values.reshape(local_heads, slot_rows, head_width),
        all_bias.reshape(local_heads, slot_rows),
    )


def solution(mesh):
    placed = (
        P("head", "query", None),
        P("head", "page", None),
        P("head", "page", None),
        P("head", "page"),
        P("head", "query", None),
        P("head", "query"),
        P(),
    )

    def program(*args):
        plan = direct_per_device if direct_plan_fits(mesh, args[0], args[1]) else per_device
        return jax.shard_map(
            plan,
            mesh=mesh,
            in_specs=placed,
            out_specs=(P("head", "page", None), P("head", "page", None), P("head", "page")),
            check_vma=False,
        )(*args)

    return program
```

```python
import itertools
import math

import jax
import jax.numpy as jnp
from jax import lax
from jax.experimental import pallas as pl
from jax.experimental.pallas import tpu as pltpu
from jax.sharding import PartitionSpec as P

STEPS = 2
PAGE_LEN = 32768


MASKED = -1e30
EPSILON = 1e-06
RATE_KEYS = 0.05
RATE_VALUES = 0.05
RATE_BIAS = 0.2
HIGHEST = lax.Precision.HIGHEST
TAIL = 8
CORES = 2


def exchange(value, **masks):
    axes = tuple(masks)
    sizes = [lax.axis_size(axis) for axis in axes]

    def flat(place):
        index = 0
        for size, at in zip(sizes, place):
            index = index * size + at
        return index

    pairs = [
        (flat(place), flat([at ^ mask for at, mask in zip(place, masks.values())]))
        for place in itertools.product(*map(range, sizes))
    ]
    return lax.ppermute(value, axes, pairs)


def halves(value):
    high = value.astype(jnp.bfloat16)
    return high, (value - high.astype(jnp.float32)).astype(jnp.bfloat16)


def dot(left, right, left_dim, right_dim):
    def one_pass(left_half, right_half):
        return lax.dot_general(
            left_half,
            right_half,
            (((left_dim,), (right_dim,)), ((), ())),
            preferred_element_type=jnp.float32,
        )

    cross = one_pass(left[0], right[1]) + one_pass(left[1], right[0])
    return one_pass(left[0], right[0]) + cross


def call(body, out_shapes, name, cost, operands, scratch=(), after=(), space=pltpu.VMEM,
         out_spaces=None, vmem=32):
    spaces = [space] * len(operands) + [pl.ANY] * len(after)
    out_spaces = out_spaces or [pltpu.VMEM] * len(out_shapes)
    count = len(operands)

    def without_after(*refs):
        body(*refs[:count], *refs[count + len(after) :])

    return pl.pallas_call(
        without_after,
        out_shape=[jax.ShapeDtypeStruct(shape, jnp.float32) for shape in out_shapes],
        in_specs=[pl.BlockSpec(memory_space=space) for space in spaces],
        out_specs=[pl.BlockSpec(memory_space=out_space) for out_space in out_spaces],
        scratch_shapes=scratch,
        compiler_params=pltpu.CompilerParams(vmem_limit_bytes=vmem * 2**20),
        cost_estimate=pl.CostEstimate(flops=cost, bytes_accessed=2**20, transcendentals=0),
        name=name,
    )(*operands, *after)


def row_as_tail(row, width):
    rows = [row[:, at : at + width] for at in range(0, row.shape[1], width)]
    rows.append(jnp.zeros((TAIL - len(rows), width), row.dtype))
    return jnp.concatenate(rows, axis=0)


def tail_as_row(ref, start, count):
    return jnp.concatenate([ref[start + at : start + at + 1, :] for at in range(count)], axis=1)


def row_as_column(row, width):
    parts = []
    for at in range(0, row.shape[1], width):
        parts.append(jnp.broadcast_to(row[:, at : at + width], (width, width)).T)
    return jnp.concatenate(parts, axis=0)


def direct_plan_fits(mesh, queries, compact_keys):
    sizes = [mesh.shape[axis] for axis in ("page", "query", "head")]
    pages, query_devices, head_devices = sizes
    local_heads = queries.shape[0] // head_devices
    part_rows = queries.shape[1] // query_devices
    slot_rows = compact_keys.shape[1] // pages
    width = queries.shape[2]
    if any(size & (size - 1) for size in sizes) or pages < CORES or width % 128:
        return False
    if local_heads != CORES * query_devices:
        return False
    ranks = pages // CORES
    chunk = part_rows * query_devices // ranks
    return (
        part_rows * query_devices % ranks == 0
        and chunk % 128 == 0
        and part_rows % (8 * ranks) == 0
        and slot_rows % width == 0
        and part_rows % width == 0
        and max(slot_rows, part_rows) < TAIL * width
    )


def direct_per_device(
    queries, compact_keys, compact_values, slot_bias, targets, positions, assignment
):
    local_heads, part_rows, width = queries.shape
    slot_rows = compact_keys.shape[1]
    query_devices = lax.axis_size("query")
    head_devices = lax.axis_size("head")
    ranks = lax.axis_size("rank")
    query_rows = part_rows * query_devices
    chunk, piece = query_rows // ranks, part_rows // ranks
    slot_total = local_heads * head_devices * slot_rows * ranks * CORES
    entry_total = slot_total * width
    score_scale = 1.0 / math.sqrt(width)
    slots = CORES * slot_rows
    groups = ranks * query_devices * head_devices
    pos_rows = part_rows // width
    bias_rows = slot_rows // width
    packed_rows = 2 * slot_rows + TAIL
    packed_shapes = [(packed_rows, width)] * 2
    matmul_cost = 3 * 2 * slots * query_rows * width

    def places():
        return lax.axis_index("rank"), lax.axis_index("core"), lax.axis_index("query")

    def pack_queries(head, rank, queries, targets, out):
        rows = pl.ds(pl.multiple_of(rank * piece, piece), piece)
        return [
            (queries.at[head], out.at[pl.ds(0, part_rows)]),
            (targets.at[head, rows], out.at[pl.ds(part_rows, piece)]),
        ]

    def pack_state(head, keys, values, out):
        return [
            (keys.at[head], out.at[pl.ds(0, slot_rows)]),
            (values.at[head], out.at[pl.ds(slot_rows, slot_rows)]),
        ]

    def start_all(copies, sems, first=0):
        copies = [
            pltpu.make_async_copy(source, target, sems.at[first + at])
            for at, (source, target) in enumerate(copies)
        ]
        for copy in copies:
            copy.start()
        return copies

    def position_tail(head, positions_ref):
        return row_as_tail(positions_ref[pl.ds(head, 1), :].astype(jnp.float32), width)

    def state_tail(head, page, bias_ref, assignment_ref):
        page_start = (assignment_ref[page] * PAGE_LEN).astype(jnp.float32)
        tail = row_as_tail(bias_ref[pl.ds(head, 1), :], width)
        return jnp.concatenate(
            [tail[: TAIL - 1], jnp.full((1, width), page_start, jnp.float32)], axis=0
        )

    def send_body(
        queries, keys, values, biases, targets, positions, assignment, state_out, *refs
    ):
        query_outs = refs[: query_devices - 1]
        bias_ref, positions_ref, assignment_ref, sems = refs[query_devices - 1 :]
        rank, core, me = places()
        heads = [CORES * (me ^ turn) + core for turn in range(1, query_devices)]
        mate_head = CORES * me + (core ^ 1)
        small = start_all(
            [(assignment, assignment_ref), (positions, positions_ref), (biases, bias_ref)], sems
        )
        copies = pack_state(mate_head, keys, values, state_out)
        for head, out in zip(heads, query_outs):
            copies += pack_queries(head, rank, queries, targets, out)
        copies = start_all(copies, sems, 3)
        for copy in small:
            copy.wait()
        state_out[2 * slot_rows :, :] = state_tail(
            mate_head, CORES * rank + core, bias_ref, assignment_ref
        )
        for head, out in zip(heads, query_outs):
            out[part_rows + piece :, :] = position_tail(head, positions_ref)
        for copy in copies:
            copy.wait()

    def own_body(
        queries, keys, values, biases, targets, positions, assignment, state_out, query_out, *refs
    ):
        bias_ref, positions_ref, assignment_ref, sems = refs
        rank, core, me = places()
        head = CORES * me + core
        small = start_all(
            [(assignment, assignment_ref), (positions, positions_ref), (biases, bias_ref)], sems
        )
        copies = pack_state(head, keys, values, state_out)
        copies += pack_queries(head, rank, queries, targets, query_out)
        copies = start_all(copies, sems, 3)
        for copy in small:
            copy.wait()
        state_out[2 * slot_rows :, :] = state_tail(
            head, CORES * rank + core, bias_ref, assignment_ref
        )
        query_out[part_rows + piece :, :] = position_tail(head, positions_ref)
        for copy in copies:
            copy.wait()

    state_shape, query_shape = (packed_rows, width), (part_rows + piece + TAIL, width)
    small_scratch = [
        pltpu.VMEM(slot_bias.shape, jnp.float32),
        pltpu.VMEM(positions.shape, jnp.int32),
        pltpu.SMEM(assignment.shape, jnp.int32),
    ]
    arguments = [
        queries, compact_keys, compact_values, slot_bias, targets, positions, assignment
    ]
    mate_state, *sent_queries = call(
        send_body,
        [state_shape] + [query_shape] * (query_devices - 1),
        "pack",
        2**20,
        arguments,
        small_scratch + [pltpu.SemaphoreType.DMA((3 + 2 * query_devices,))],
        space=pl.ANY,
        vmem=60,
    )
    own_state, own_queries = call(
        own_body,
        [state_shape, query_shape],
        "own",
        2**24,
        arguments,
        small_scratch + [pltpu.SemaphoreType.DMA((7,))],
        space=pl.ANY,
    )
    query_parts = [own_queries] + [
        exchange(sent_queries[turn - 1], query=turn) for turn in range(1, query_devices)
    ]
    states = [own_state, exchange(mate_state, core=1)]

    def in_columns(parts, axis):
        return jnp.concatenate(
            [
                lax.slice_in_dim(part, at * piece, (at + 1) * piece, axis=axis)
                for at in range(ranks)
                for part in parts
            ],
            axis=axis,
        )

    def read_queries(query_refs):
        return halves(in_columns([ref[:part_rows, :] for ref in query_refs], 0))

    def part_of(ref, at):
        return ref.at[pl.ds(at * packed_rows, packed_rows)]

    def parts_of(refs):
        return refs if len(refs) == CORES else [part_of(refs[0], at) for at in range(CORES)]

    def step_sizes(tile_refs):
        tile = jnp.sum(tile_refs[0][...], axis=0)
        sums = jnp.sum(tile, axis=1, keepdims=True)
        return (
            RATE_KEYS / jnp.sqrt(sums[0:1] / entry_total + EPSILON),
            RATE_VALUES / jnp.sqrt(sums[1:2] / entry_total + EPSILON),
            RATE_BIAS / jnp.sqrt(sums[2:3] / slot_total + EPSILON),
        )

    def updated(state_ref, grad_ref, sizes):
        key_end, value_end = slot_rows, 2 * slot_rows
        return (
            state_ref[:key_end, :] - sizes[0] * grad_ref[:key_end, :],
            state_ref[key_end:value_end, :] - sizes[1] * grad_ref[key_end:value_end, :],
            state_ref[value_end:, :] - sizes[2] * grad_ref[value_end:, :],
        )

    def forward(state_refs, query_refs, chunk_outs, weights_out, max_out, chunks):
        rank, _, _ = places()
        all_queries = read_queries(query_refs)
        position_row = in_columns(
            [tail_as_row(ref, part_rows + piece, pos_rows) for ref in query_refs], 1
        )
        all_scores, all_visible = [], []
        for at, ref in enumerate(state_refs):
            scores = dot(halves(ref[:slot_rows, :]), all_queries, 1, 1) * score_scale
            bias = row_as_column(tail_as_row(ref, 2 * slot_rows, bias_rows), width)
            scores = scores + jnp.concatenate([bias] * (query_rows // width), axis=1)
            page_start = ref[packed_rows - 1 : packed_rows, 0:1]
            visible = jnp.broadcast_to(position_row >= page_start, scores.shape)
            all_scores.append(jnp.where(visible, scores, MASKED))
            all_visible.append(visible)
        row_max = jnp.max(all_scores[0], axis=0, keepdims=True)
        for scores in all_scores[1:]:
            row_max = jnp.maximum(row_max, jnp.max(scores, axis=0, keepdims=True))
        row_total = jnp.zeros_like(row_max)
        row_sum = jnp.zeros((width, query_rows), jnp.float32)
        for at, ref in enumerate(state_refs):
            weights = jnp.where(all_visible[at], jnp.exp(all_scores[at] - row_max), 0.0)
            weights_out[at * slot_rows : (at + 1) * slot_rows, :] = weights
            row_total = row_total + jnp.sum(weights, axis=0, keepdims=True)
            values = halves(ref[slot_rows : 2 * slot_rows, :])
            row_sum = row_sum + dot(values, halves(weights), 0, 0)
        max_out[...] = jnp.broadcast_to(row_max, (TAIL, query_rows))
        tail = jnp.concatenate(
            [row_max, row_total, jnp.zeros((TAIL - 2, query_rows), jnp.float32)], axis=0
        )
        for at in range(ranks):
            columns = slice(at * chunk, (at + 1) * chunk)
            chunks[at, :width, :] = row_sum[:, columns]
            chunks[at, width:, :] = tail[:, columns]
        for turn in range(ranks):
            chunk_outs[turn][...] = chunks[rank ^ turn]

    chunk_shape = (width + TAIL, chunk)
    forward_shapes = [chunk_shape] * ranks + [(slots, query_rows), (TAIL, query_rows)]
    chunk_scratch = [pltpu.VMEM((ranks,) + chunk_shape, jnp.float32)]

    def first_body(*refs):
        state_refs, refs = refs[:2], refs[2:]
        query_refs, refs = refs[:query_devices], refs[query_devices:]
        chunk_outs, refs = refs[:ranks], refs[ranks:]
        forward(state_refs, query_refs, chunk_outs, *refs)

    def next_body(*refs):
        state_refs, refs = refs[:2], refs[2:]
        query_refs, refs = refs[:query_devices], refs[query_devices:]
        grad_refs, refs = refs[:2], refs[2:]
        tile_refs, refs = refs[: len(tiles)], refs[len(tiles) :]
        state_outs, refs = parts_of(refs[:1]), refs[1:]
        chunk_outs, refs = refs[:ranks], refs[ranks:]
        sizes = step_sizes(tile_refs)
        for at in range(2):
            keys, values, bias = updated(state_refs[at], grad_refs[at], sizes)
            state_outs[at][:slot_rows, :] = keys
            state_outs[at][slot_rows : 2 * slot_rows, :] = values
            state_outs[at][2 * slot_rows :, :] = bias
        forward(state_outs, query_refs, chunk_outs, *refs)

    def merge_body(*refs):
        query_refs, refs = refs[:query_devices], refs[query_devices:]
        chunk_refs, (merged_out,) = refs[:ranks], refs[ranks:]
        targets = jnp.concatenate(
            [ref[part_rows : part_rows + piece, :] for ref in query_refs], axis=0
        )
        row_max = chunk_refs[0][width : width + 1, :]
        for ref in chunk_refs[1:]:
            row_max = jnp.maximum(row_max, ref[width : width + 1, :])
        row_total = jnp.zeros_like(row_max)
        row_sum = jnp.zeros((width, chunk), jnp.float32)
        for ref in chunk_refs:
            factor = jnp.exp(ref[width : width + 1, :] - row_max)
            row_total = row_total + ref[width + 1 : width + 2, :] * factor
            row_sum = row_sum + ref[:width, :] * factor
        output = row_sum / row_total
        residual = output - targets.T
        row_delta = jnp.sum(residual * output, axis=0, keepdims=True)
        merged_out[:width, :] = residual
        merged_out[width:, :] = jnp.concatenate(
            [row_max, row_total, row_delta, jnp.zeros((TAIL - 3, chunk), jnp.float32)], axis=0
        )

    def backward_body(weights_ref, max_ref, *refs):
        state_refs, refs = parts_of(refs[: len(states)]), refs[len(states) :]
        query_refs, refs = refs[:query_devices], refs[query_devices:]
        merged_refs, refs = refs[:ranks], refs[ranks:]
        grad_outs, (squares_out, chunks) = refs[:2], refs[2:]
        rank, _, _ = places()
        for turn in range(ranks):
            chunks[rank ^ turn] = merged_refs[turn][...]
        joined = jnp.concatenate([chunks[at] for at in range(ranks)], axis=1)
        residual = joined[:width, :]
        row_max, row_total, row_delta = (
            joined[width + at : width + at + 1, :] for at in range(3)
        )
        all_queries = read_queries(query_refs)
        residual = halves(residual)
        factor = jnp.exp(max_ref[0:1, :] - row_max) / row_total
        ones = jnp.ones((TAIL, query_rows), jnp.bfloat16)
        ones = (ones, jnp.zeros_like(ones))
        squares = [jnp.zeros((1, width), jnp.float32)] * 3
        for at, ref in enumerate(state_refs):
            attention = weights_ref[at * slot_rows : (at + 1) * slot_rows, :] * factor
            grad_values = dot(halves(attention), residual, 1, 1)
            grad_probs = dot(halves(ref[slot_rows : 2 * slot_rows, :]), residual, 1, 0)
            grad_scores = halves(attention * (grad_probs - row_delta))
            grad_keys = dot(grad_scores, all_queries, 1, 0) * score_scale
            grad_bias = row_as_tail(dot(ones, grad_scores, 1, 1)[0:1, :], width)
            grad_outs[at][:slot_rows, :] = grad_keys
            grad_outs[at][slot_rows : 2 * slot_rows, :] = grad_values
            grad_outs[at][2 * slot_rows :, :] = grad_bias
            for which, grad in enumerate((grad_keys, grad_values, grad_bias)):
                squares[which] = squares[which] + jnp.sum(grad * grad, axis=0, keepdims=True)
        squares_out[...] = jnp.concatenate(
            squares + [jnp.zeros((TAIL - 3, width), jnp.float32)], axis=0
        )

    def spread_body(own_ref, mate_ref, out_ref):
        tile = own_ref[...] + mate_ref[...]
        for at in range(groups):
            out_ref[at] = tile

    def mate_body(*refs):
        *state_refs, out_ref = refs
        for at, ref in enumerate(state_refs):
            out_ref[pl.ds(at * packed_rows, packed_rows), :] = part_of(ref, 1)[...]

    out_masks = list(itertools.product(range(query_devices), range(CORES)))

    def to_output(packs, mask):
        if mask == (0, 0):
            return packs[0]
        return exchange(packs[mask[1]], core=mask[1], query=mask[0])

    for repeat in range(STEPS):
        last = repeat == STEPS - 1
        if repeat == 0:
            *chunk_parts, weights, maxima = call(
                first_body,
                forward_shapes,
                "forward",
                2 * matmul_cost,
                states + query_parts,
                chunk_scratch,
            )
        else:
            new_state, *chunk_parts, weights, maxima = call(
                next_body,
                [(CORES * packed_rows, width)] + forward_shapes,
                "update_forward",
                2 * matmul_cost,
                states + query_parts + grads + tiles,
                chunk_scratch,
            )
            states = [new_state]
        arrived = {
            turn: exchange(chunk_parts[turn], rank=turn)
            for turn in reversed(range(1, ranks))
        }
        if repeat:
            new_states = states + [
                exchange(states[0], query=turn) for turn in range(1, query_devices)
            ]
        (merged,) = call(
            merge_body,
            [chunk_shape],
            "merge",
            2**20,
            query_parts + chunk_parts[:1] + list(arrived.values()),
        )
        all_merged = [merged] + [
            exchange(merged, rank=turn) for turn in range(1, ranks)
        ]
        if repeat:
            (for_mate,) = call(
                mate_body,
                [(query_devices * packed_rows, width)],
                "mate_parts",
                2**20,
                new_states,
                after=all_merged[1:],
            )
            from_mate = exchange(for_mate, core=1)
        own_grad, mate_grad, squares = call(
            backward_body,
            packed_shapes + [(TAIL, width)],
            "backward",
            3 * matmul_cost,
            [weights, maxima] + states + query_parts + all_merged,
            scratch=chunk_scratch,
        )
        grads = [own_grad, mate_grad]
        if last:
            all_grads = [to_output(grads, mask) for mask in out_masks]
        (shared,) = call(
            spread_body,
            [(groups, TAIL, width)],
            "spread",
            2**10,
            [squares, exchange(squares, core=1)],
        )
        tiles = [
            lax.all_to_all(
                shared, ("rank", "query", "head"), split_axis=0, concat_axis=0, tiled=True
            )
        ]

    def last_body(*refs):
        state_refs, (mate_ref, *refs) = refs[:query_devices], refs[query_devices:]
        state_refs = [
            part_of(mate_ref, turn) if flip else part_of(state_refs[turn], 0)
            for turn, flip in out_masks
        ]
        grad_refs, refs = refs[:local_heads], refs[local_heads:]
        tile_refs, refs = refs[: len(tiles)], refs[len(tiles) :]
        keys_out, values_out, bias_out, new_keys, new_values, sems = refs
        _, core, me = places()
        sizes = step_sizes(tile_refs)
        copies = []
        for at, (turn, flip) in enumerate(out_masks):
            keys, values, bias = updated(state_refs[at], grad_refs[at], sizes)
            head = CORES * (me ^ turn) + (core ^ flip)
            new_keys[at] = keys
            new_values[at] = values
            copies += start_all(
                [
                    (new_keys.at[at], keys_out.at[head]),
                    (new_values.at[at], values_out.at[head]),
                ],
                sems,
                len(copies),
            )
            bias_row = jnp.concatenate([bias[row : row + 1] for row in range(bias_rows)], axis=1)
            bias_out[pl.ds(head, 1), :] = bias_row
        for copy in copies:
            copy.wait()

    return tuple(
        call(
            last_body,
            [compact_keys.shape, compact_values.shape, slot_bias.shape],
            "last_update",
            2**20,
            new_states + [from_mate] + all_grads + tiles,
            [
                pltpu.VMEM(compact_keys.shape, jnp.float32),
                pltpu.VMEM(compact_values.shape, jnp.float32),
                pltpu.SemaphoreType.DMA((2 * local_heads,)),
            ],
            out_spaces=[pl.ANY, pl.ANY, pltpu.VMEM],
        )
    )


def from_partner(value, axis, stride):
    mask = 2**stride
    pairs = [(source, source ^ mask) for source in range(lax.axis_size(axis))]
    return lax.ppermute(value, axis, pairs)


def squared_sums(grad_keys, grad_values, grad_bias):
    return jnp.stack(
        [
            jnp.sum(grad_keys * grad_keys),
            jnp.sum(grad_values * grad_values),
            jnp.sum(grad_bias * grad_bias),
        ]
    )


def apply_update(states, grads, totals, entry_count, slot_total):
    key_state, value_state, bias_state = states
    grad_keys, grad_values, grad_bias = grads
    rms_keys = jnp.sqrt(totals[0] / entry_count + EPSILON)
    rms_values = jnp.sqrt(totals[1] / entry_count + EPSILON)
    rms_bias = jnp.sqrt(totals[2] / slot_total + EPSILON)
    return (
        key_state - RATE_KEYS * grad_keys / rms_keys,
        value_state - RATE_VALUES * grad_values / rms_values,
        bias_state - RATE_BIAS * grad_bias / rms_bias,
    )


def local_gradients(queries, targets, visible, compact_keys, compact_values, slot_bias):
    score_scale = 1.0 / math.sqrt(queries.shape[2])
    scores = jnp.einsum("hqd,hsd->hqs", queries, compact_keys, precision=HIGHEST) * score_scale
    scores = jnp.where(visible, scores + slot_bias[:, None, :], MASKED)
    local_max = jnp.max(scores, axis=2)
    row_max = lax.pmax(local_max, "page")
    weights = jnp.where(visible, jnp.exp(scores - row_max[:, :, None]), 0.0)
    local_sum = jnp.einsum("hqs,hsd->hqd", weights, compact_values, precision=HIGHEST)
    row_total, row_sum = lax.psum((jnp.sum(weights, axis=2), local_sum), "page")
    attention = weights / row_total[:, :, None]
    output = row_sum / row_total[:, :, None]
    residual = output - targets
    grad_values = jnp.einsum("hqs,hqd->hsd", attention, residual, precision=HIGHEST)
    row_delta = jnp.sum(residual * output, axis=2)
    grad_probs = jnp.einsum("hqd,hsd->hqs", residual, compact_values, precision=HIGHEST)
    grad_scores = attention * (grad_probs - row_delta[:, :, None])
    grad_bias = jnp.sum(grad_scores, axis=1)
    grad_keys = jnp.einsum("hqs,hqd->hsd", grad_scores, queries, precision=HIGHEST) * score_scale
    return (grad_keys, grad_values, grad_bias)


def per_device(queries, compact_keys, compact_values, slot_bias, targets, positions, assignment):
    page_number = assignment[lax.axis_index("page")]
    local_heads = compact_keys.shape[0]
    slot_total = local_heads * lax.axis_size("head") * compact_keys.shape[1] * lax.axis_size("page")
    entry_count = slot_total * compact_keys.shape[2]
    query_count = lax.axis_size("query")
    heads_kept = max(local_heads // query_count, 1)
    query_parts = max(query_count // local_heads, 1)
    part_rows = queries.shape[1] // query_parts

    def split_items(array):
        width = array.shape[2]
        array = array.reshape(local_heads // heads_kept, heads_kept, query_parts, part_rows, width)
        array = jnp.transpose(array, (0, 2, 1, 3, 4))
        return array.reshape(query_count, heads_kept, part_rows, width)

    def join_items(array):
        width = array.shape[3]
        array = jnp.transpose(array, (1, 0, 2, 3))
        return array.reshape(heads_kept, query_count * part_rows, width)

    position_column = positions.astype(jnp.float32)[:, :, None]
    got_queries, got_targets, got_positions = (
        lax.all_to_all(split_items(queries), "query", split_axis=0, concat_axis=0, tiled=True),
        lax.all_to_all(split_items(targets), "query", split_axis=0, concat_axis=0, tiled=True),
        lax.all_to_all(
            split_items(position_column), "query", split_axis=0, concat_axis=0, tiled=True
        ),
    )
    group_queries = join_items(got_queries)
    group_targets = join_items(got_targets)
    group_positions = join_items(got_positions)[:, :, 0]
    visible = (page_number.astype(jnp.float32) <= jnp.floor(group_positions / PAGE_LEN))[:, :, None]
    query_index = lax.axis_index("query")
    first_head = query_index // query_parts * heads_kept
    key_state = lax.dynamic_slice_in_dim(compact_keys, first_head, heads_kept, 0)
    value_state = lax.dynamic_slice_in_dim(compact_values, first_head, heads_kept, 0)
    bias_state = lax.dynamic_slice_in_dim(slot_bias, first_head, heads_kept, 0)
    counted = (query_index % query_parts == 0).astype(jnp.float32)
    for repeat in range(STEPS):
        grads = local_gradients(
            group_queries, group_targets, visible, key_state, value_state, bias_state
        )
        for bit in range(query_parts.bit_length() - 1):
            partner = from_partner((grads[0], grads[1], grads[2]), "query", bit)
            grads = (grads[0] + partner[0], grads[1] + partner[1], grads[2] + partner[2])
        totals = lax.psum(
            squared_sums(grads[0], grads[1], grads[2]) * counted, ("page", "query", "head")
        )
        key_state, value_state, bias_state = apply_update(
            (key_state, value_state, bias_state), grads, totals, entry_count, slot_total
        )
    all_keys, all_values, all_bias = (
        lax.all_gather(key_state, "query", axis=0, tiled=True),
        lax.all_gather(value_state, "query", axis=0, tiled=True),
        lax.all_gather(bias_state, "query", axis=0, tiled=True),
    )
    slot_rows = compact_keys.shape[1]
    head_width = compact_keys.shape[2]
    all_keys = all_keys.reshape(
        local_heads // heads_kept, query_parts, heads_kept, slot_rows, head_width
    )[:, 0]
    all_values = all_values.reshape(
        local_heads // heads_kept, query_parts, heads_kept, slot_rows, head_width
    )[:, 0]
    all_bias = all_bias.reshape(local_heads // heads_kept, query_parts, heads_kept, slot_rows)[:, 0]
    return (
        all_keys.reshape(local_heads, slot_rows, head_width),
        all_values.reshape(local_heads, slot_rows, head_width),
        all_bias.reshape(local_heads, slot_rows),
    )


def solution(mesh):
    sizes = [mesh.shape[axis] for axis in ("page", "query", "head")]
    if sizes[0] % CORES == 0:
        split = [sizes[0] // CORES, CORES] + sizes[1:]
        split_mesh = jax.sharding.Mesh(
            mesh.devices.reshape(split), ("rank", "core", "query", "head")
        )

    def program(*args):
        direct = direct_plan_fits(mesh, args[0], args[1])
        page = ("rank", "core") if direct else "page"
        placed = (
            P("head", "query", None),
            P("head", page, None),
            P("head", page, None),
            P("head", page),
            P("head", "query", None),
            P("head", "query"),
            P(),
        )
        return jax.shard_map(
            direct_per_device if direct else per_device,
            mesh=split_mesh if direct else mesh,
            in_specs=placed,
            out_specs=(P("head", page, None), P("head", page, None), P("head", page)),
            check_vma=False,
        )(*args)

    return program
```

```python
import itertools
import math

import jax
import jax.numpy as jnp
from jax import lax
from jax.experimental import pallas as pl
from jax.experimental.pallas import tpu as pltpu
from jax.sharding import PartitionSpec as P

STEPS = 2
PAGE_LEN = 32768


MASKED = -1e30
EPSILON = 1e-06
RATE_KEYS = 0.05
RATE_VALUES = 0.05
RATE_BIAS = 0.2
HIGHEST = lax.Precision.HIGHEST
TAIL = 8
CORES = 2


def exchange(value, **masks):
    axes = tuple(masks)
    sizes = [lax.axis_size(axis) for axis in axes]

    def flat(place):
        index = 0
        for size, at in zip(sizes, place):
            index = index * size + at
        return index

    pairs = [
        (flat(place), flat([at ^ mask for at, mask in zip(place, masks.values())]))
        for place in itertools.product(*map(range, sizes))
    ]
    return lax.ppermute(value, axes, pairs)


def halves(value):
    high = value.astype(jnp.bfloat16)
    return high, (value - high.astype(jnp.float32)).astype(jnp.bfloat16)


def dot(left, right, left_dim, right_dim):
    def one_pass(left_half, right_half):
        return lax.dot_general(
            left_half,
            right_half,
            (((left_dim,), (right_dim,)), ((), ())),
            preferred_element_type=jnp.float32,
        )

    cross = one_pass(left[0], right[1]) + one_pass(left[1], right[0])
    return one_pass(left[0], right[0]) + cross


def call(body, out_shapes, name, cost, operands, scratch=(), after=(), space=pltpu.VMEM, vmem=32):
    spaces = [space] * len(operands) + [pl.ANY] * len(after)
    count = len(operands)

    def without_after(*refs):
        body(*refs[:count], *refs[count + len(after) :])

    return pl.pallas_call(
        without_after,
        out_shape=[jax.ShapeDtypeStruct(shape, jnp.float32) for shape in out_shapes],
        in_specs=[pl.BlockSpec(memory_space=space) for space in spaces],
        out_specs=[pl.BlockSpec(memory_space=pltpu.VMEM) for _ in out_shapes],
        scratch_shapes=scratch,
        compiler_params=pltpu.CompilerParams(vmem_limit_bytes=vmem * 2**20),
        cost_estimate=pl.CostEstimate(flops=cost, bytes_accessed=2**20, transcendentals=0),
        name=name,
    )(*operands, *after)


def row_as_tail(row, width):
    rows = [row[:, at : at + width] for at in range(0, row.shape[1], width)]
    rows.append(jnp.zeros((TAIL - len(rows), width), row.dtype))
    return jnp.concatenate(rows, axis=0)


def tail_as_row(ref, start, count):
    return jnp.concatenate([ref[start + at : start + at + 1, :] for at in range(count)], axis=1)


def row_as_column(row, width):
    parts = []
    for at in range(0, row.shape[1], width):
        parts.append(jnp.broadcast_to(row[:, at : at + width], (width, width)).T)
    return jnp.concatenate(parts, axis=0)


def direct_plan_fits(mesh, queries, compact_keys):
    sizes = [mesh.shape[axis] for axis in ("page", "query", "head")]
    pages, query_devices, head_devices = sizes
    local_heads = queries.shape[0] // head_devices
    part_rows = queries.shape[1] // query_devices
    slot_rows = compact_keys.shape[1] // pages
    width = queries.shape[2]
    if any(size & (size - 1) for size in sizes) or pages < CORES or width % 128:
        return False
    if local_heads != CORES * query_devices:
        return False
    ranks = pages // CORES
    chunk = part_rows * query_devices // ranks
    return (
        part_rows * query_devices % ranks == 0
        and chunk % 128 == 0
        and part_rows % (8 * ranks) == 0
        and slot_rows % width == 0
        and part_rows % width == 0
        and max(slot_rows, part_rows) < TAIL * width
    )


def direct_per_device(
    queries, compact_keys, compact_values, slot_bias, targets, positions, assignment
):
    local_heads, part_rows, width = queries.shape
    slot_rows = compact_keys.shape[1]
    query_devices = lax.axis_size("query")
    head_devices = lax.axis_size("head")
    ranks = lax.axis_size("page") // CORES
    query_rows = part_rows * query_devices
    chunk, piece = query_rows // ranks, part_rows // ranks
    slot_total = local_heads * head_devices * slot_rows * lax.axis_size("page")
    entry_total = slot_total * width
    score_scale = 1.0 / math.sqrt(width)
    slots = CORES * slot_rows
    devices = ranks * CORES * query_devices * head_devices
    pos_rows = part_rows // width
    bias_rows = slot_rows // width
    packed_rows = 2 * slot_rows + TAIL
    packed_shapes = [(packed_rows, width)] * 2
    matmul_cost = 3 * 2 * slots * query_rows * width

    def places():
        page = lax.axis_index("page")
        return page // CORES, page % CORES, lax.axis_index("query")

    def to_device(value, **masks):
        masks = {axis: mask for axis, mask in masks.items() if mask}
        return exchange(value, **masks) if masks else value

    def pack_queries(head, rank, queries, targets, out):
        rows = pl.ds(pl.multiple_of(rank * piece, piece), piece)
        return [
            (queries.at[head], out.at[pl.ds(0, part_rows)]),
            (targets.at[head, rows], out.at[pl.ds(part_rows, piece)]),
        ]

    def pack_state(head, keys, values, out):
        return [
            (keys.at[head], out.at[pl.ds(0, slot_rows)]),
            (values.at[head], out.at[pl.ds(slot_rows, slot_rows)]),
        ]

    def start_all(copies, sems, first=0):
        copies = [
            pltpu.make_async_copy(source, target, sems.at[first + at])
            for at, (source, target) in enumerate(copies)
        ]
        for copy in copies:
            copy.start()
        return copies

    def position_tail(head, positions_ref):
        return row_as_tail(positions_ref[pl.ds(head, 1), :].astype(jnp.float32), width)

    def state_tail(head, page, bias_ref, assignment_ref):
        page_start = (assignment_ref[page] * PAGE_LEN).astype(jnp.float32)
        tail = row_as_tail(bias_ref[pl.ds(head, 1), :], width)
        return jnp.concatenate(
            [tail[: TAIL - 1], jnp.full((1, width), page_start, jnp.float32)], axis=0
        )

    def send_body(
        queries, keys, values, biases, targets, positions, assignment, state_out, *refs
    ):
        query_outs = refs[: query_devices - 1]
        bias_ref, positions_ref, assignment_ref, sems = refs[query_devices - 1 :]
        rank, core, me = places()
        heads = [CORES * (me ^ turn) + core for turn in range(1, query_devices)]
        mate_head = CORES * me + (core ^ 1)
        small = start_all(
            [(assignment, assignment_ref), (positions, positions_ref), (biases, bias_ref)], sems
        )
        copies = pack_state(mate_head, keys, values, state_out)
        for head, out in zip(heads, query_outs):
            copies += pack_queries(head, rank, queries, targets, out)
        copies = start_all(copies, sems, 3)
        for copy in small:
            copy.wait()
        state_out[2 * slot_rows :, :] = state_tail(
            mate_head, CORES * rank + core, bias_ref, assignment_ref
        )
        for head, out in zip(heads, query_outs):
            out[part_rows + piece :, :] = position_tail(head, positions_ref)
        for copy in copies:
            copy.wait()

    def own_body(
        queries, keys, values, biases, targets, positions, assignment, state_out, query_out, *refs
    ):
        bias_ref, positions_ref, assignment_ref, sems = refs
        rank, core, me = places()
        head = CORES * me + core
        small = start_all(
            [(assignment, assignment_ref), (positions, positions_ref), (biases, bias_ref)], sems
        )
        copies = pack_state(head, keys, values, state_out)
        copies += pack_queries(head, rank, queries, targets, query_out)
        copies = start_all(copies, sems, 3)
        for copy in small:
            copy.wait()
        state_out[2 * slot_rows :, :] = state_tail(
            head, CORES * rank + core, bias_ref, assignment_ref
        )
        query_out[part_rows + piece :, :] = position_tail(head, positions_ref)
        for copy in copies:
            copy.wait()

    state_shape, query_shape = (packed_rows, width), (part_rows + piece + TAIL, width)
    small_scratch = [
        pltpu.VMEM(slot_bias.shape, jnp.float32),
        pltpu.VMEM(positions.shape, jnp.int32),
        pltpu.SMEM(assignment.shape, jnp.int32),
    ]
    arguments = [
        queries, compact_keys, compact_values, slot_bias, targets, positions, assignment
    ]
    mate_state, *sent_queries = call(
        send_body,
        [state_shape] + [query_shape] * (query_devices - 1),
        "pack",
        2**20,
        arguments,
        small_scratch + [pltpu.SemaphoreType.DMA((3 + 2 * query_devices,))],
        space=pl.ANY,
        vmem=60,
    )
    own_state, own_queries = call(
        own_body,
        [state_shape, query_shape],
        "own",
        2**24,
        arguments,
        small_scratch + [pltpu.SemaphoreType.DMA((7,))],
        space=pl.ANY,
    )
    packs = [own_queries] + list(sent_queries)
    query_parts_of = [
        [to_device(packs[part], query=turn ^ part) for part in range(query_devices)]
        for turn in range(query_devices)
    ]
    query_parts = query_parts_of[0]
    states = [own_state, exchange(mate_state, page=1)]

    def in_columns(parts, axis):
        return jnp.concatenate(
            [
                lax.slice_in_dim(part, at * piece, (at + 1) * piece, axis=axis)
                for at in range(ranks)
                for part in parts
            ],
            axis=axis,
        )

    def read_queries(query_refs):
        return halves(in_columns([ref[:part_rows, :] for ref in query_refs], 0))

    def part_of(ref, at):
        return ref.at[pl.ds(at * packed_rows, packed_rows)]

    def parts_of(refs):
        return refs if len(refs) == CORES else [part_of(refs[0], at) for at in range(CORES)]

    def step_sizes(tile_refs):
        tile = jnp.sum(tile_refs[0][...], axis=0)
        sums = jnp.sum(tile, axis=1, keepdims=True)
        return (
            RATE_KEYS / jnp.sqrt(sums[0:1] / entry_total + EPSILON),
            RATE_VALUES / jnp.sqrt(sums[1:2] / entry_total + EPSILON),
            RATE_BIAS / jnp.sqrt(sums[2:3] / slot_total + EPSILON),
        )

    def updated(state_ref, grad_ref, sizes):
        key_end, value_end = slot_rows, 2 * slot_rows
        return (
            state_ref[:key_end, :] - sizes[0] * grad_ref[:key_end, :],
            state_ref[key_end:value_end, :] - sizes[1] * grad_ref[key_end:value_end, :],
            state_ref[value_end:, :] - sizes[2] * grad_ref[value_end:, :],
        )

    def all_weights(state_refs, query_refs):
        all_queries = read_queries(query_refs)
        position_row = in_columns(
            [tail_as_row(ref, part_rows + piece, pos_rows) for ref in query_refs], 1
        )
        all_scores, all_visible = [], []
        for ref in state_refs:
            scores = dot(halves(ref[:slot_rows, :]), all_queries, 1, 1) * score_scale
            bias = row_as_column(tail_as_row(ref, 2 * slot_rows, bias_rows), width)
            scores = scores + jnp.concatenate([bias] * (query_rows // width), axis=1)
            page_start = ref[packed_rows - 1 : packed_rows, 0:1]
            visible = jnp.broadcast_to(position_row >= page_start, scores.shape)
            all_scores.append(jnp.where(visible, scores, MASKED))
            all_visible.append(visible)
        row_max = jnp.max(all_scores[0], axis=0, keepdims=True)
        for scores in all_scores[1:]:
            row_max = jnp.maximum(row_max, jnp.max(scores, axis=0, keepdims=True))
        weights = [
            jnp.where(visible, jnp.exp(scores - row_max), 0.0)
            for scores, visible in zip(all_scores, all_visible)
        ]
        return weights, row_max

    def store_weights(weights, row_max, weights_out, max_out):
        for at, part in enumerate(weights):
            weights_out[at * slot_rows : (at + 1) * slot_rows, :] = part
        max_out[...] = jnp.broadcast_to(row_max, (TAIL, query_rows))

    def forward(state_refs, query_refs, chunk_outs, weights_out, max_out, chunks):
        rank, _, _ = places()
        weights, row_max = all_weights(state_refs, query_refs)
        store_weights(weights, row_max, weights_out, max_out)
        row_total = jnp.zeros_like(row_max)
        row_sum = jnp.zeros((width, query_rows), jnp.float32)
        for ref, part in zip(state_refs, weights):
            row_total = row_total + jnp.sum(part, axis=0, keepdims=True)
            values = halves(ref[slot_rows : 2 * slot_rows, :])
            row_sum = row_sum + dot(values, halves(part), 0, 0)
        tail = jnp.concatenate(
            [row_max, row_total, jnp.zeros((TAIL - 2, query_rows), jnp.float32)], axis=0
        )
        for at in range(ranks):
            columns = slice(at * chunk, (at + 1) * chunk)
            chunks[at, :width, :] = row_sum[:, columns]
            chunks[at, width:, :] = tail[:, columns]
        for turn in range(ranks):
            chunk_outs[turn][...] = chunks[rank ^ turn]

    chunk_shape = (width + TAIL, chunk)
    weight_shapes = [(slots, query_rows), (TAIL, query_rows)]
    forward_shapes = [chunk_shape] * ranks + weight_shapes
    chunk_scratch = [pltpu.VMEM((ranks,) + chunk_shape, jnp.float32)]

    def first_body(*refs):
        state_refs, refs = refs[:2], refs[2:]
        query_refs, refs = refs[:query_devices], refs[query_devices:]
        chunk_outs, refs = refs[:ranks], refs[ranks:]
        forward(state_refs, query_refs, chunk_outs, *refs)

    def next_body(*refs):
        state_refs, refs = refs[:2], refs[2:]
        query_refs, refs = refs[:query_devices], refs[query_devices:]
        grad_refs, refs = refs[:2], refs[2:]
        tile_refs, refs = refs[: len(tiles)], refs[len(tiles) :]
        state_outs, refs = parts_of(refs[:1]), refs[1:]
        chunk_outs, refs = refs[:ranks], refs[ranks:]
        sizes = step_sizes(tile_refs)
        for at in range(2):
            keys, values, bias = updated(state_refs[at], grad_refs[at], sizes)
            state_outs[at][:slot_rows, :] = keys
            state_outs[at][slot_rows : 2 * slot_rows, :] = values
            state_outs[at][2 * slot_rows :, :] = bias
        forward(state_outs, query_refs, chunk_outs, *refs)

    def merge_body(*refs):
        query_refs, refs = refs[:query_devices], refs[query_devices:]
        chunk_refs, (merged_out,) = refs[:ranks], refs[ranks:]
        targets = jnp.concatenate(
            [ref[part_rows : part_rows + piece, :] for ref in query_refs], axis=0
        )
        row_max = chunk_refs[0][width : width + 1, :]
        for ref in chunk_refs[1:]:
            row_max = jnp.maximum(row_max, ref[width : width + 1, :])
        row_total = jnp.zeros_like(row_max)
        row_sum = jnp.zeros((width, chunk), jnp.float32)
        for ref in chunk_refs:
            factor = jnp.exp(ref[width : width + 1, :] - row_max)
            row_total = row_total + ref[width + 1 : width + 2, :] * factor
            row_sum = row_sum + ref[:width, :] * factor
        output = row_sum / row_total
        residual = output - targets.T
        row_delta = jnp.sum(residual * output, axis=0, keepdims=True)
        merged_out[:width, :] = residual
        merged_out[width:, :] = jnp.concatenate(
            [row_max, row_total, row_delta, jnp.zeros((TAIL - 3, chunk), jnp.float32)], axis=0
        )

    def join_chunks(merged_refs, chunks):
        rank, _, _ = places()
        for turn, ref in enumerate(merged_refs):
            chunks[rank ^ turn] = ref[...]
        return jnp.concatenate([chunks[at] for at in range(ranks)], axis=1)

    def join_body(*refs):
        *merged_refs, joined_out, chunks = refs
        joined_out[...] = join_chunks(merged_refs, chunks)

    def gradients_of(joined, max_ref, query_refs):
        residual = halves(joined[:width, :])
        row_max, row_total, row_delta = (
            joined[width + at : width + at + 1, :] for at in range(3)
        )
        all_queries = read_queries(query_refs)
        factor = jnp.exp(max_ref[0:1, :] - row_max) / row_total
        ones = jnp.ones((TAIL, query_rows), jnp.bfloat16)
        ones = (ones, jnp.zeros_like(ones))

        def gradients(at, state_ref, weights_ref, out):
            attention = weights_ref[at * slot_rows : (at + 1) * slot_rows, :] * factor
            grad_values = dot(halves(attention), residual, 1, 1)
            grad_probs = dot(halves(state_ref[slot_rows : 2 * slot_rows, :]), residual, 1, 0)
            grad_scores = halves(attention * (grad_probs - row_delta))
            grad_keys = dot(grad_scores, all_queries, 1, 0) * score_scale
            grad_bias = row_as_tail(dot(ones, grad_scores, 1, 1)[0:1, :], width)
            out[:slot_rows, :] = grad_keys
            out[slot_rows : 2 * slot_rows, :] = grad_values
            out[2 * slot_rows :, :] = grad_bias
            return [
                jnp.sum(grad * grad, axis=0, keepdims=True)
                for grad in (grad_keys, grad_values, grad_bias)
            ]

        return gradients

    def backward_body(weights_ref, max_ref, *refs):
        state_refs, refs = parts_of(refs[: len(states)]), refs[len(states) :]
        query_refs, refs = refs[:query_devices], refs[query_devices:]
        merged_refs, refs = refs[: len(all_merged)], refs[len(all_merged) :]
        grad_outs, (squares_out, *scratch) = refs[:2], refs[2:]
        joined = join_chunks(merged_refs, *scratch) if scratch else merged_refs[0][...]
        gradients = gradients_of(joined, max_ref, query_refs)
        squares = [
            gradients(at, ref, weights_ref, grad_outs[at]) for at, ref in enumerate(state_refs)
        ]
        tile = jnp.concatenate(
            [sum(parts) for parts in zip(*squares)]
            + [jnp.zeros((TAIL - 3, width), jnp.float32)],
            axis=0,
        )
        for at in range(devices):
            squares_out[at] = tile

    def weights_body(state_ref, *refs):
        query_refs, (weights_out, max_out) = refs[:query_devices], refs[query_devices:]
        weights, row_max = all_weights(parts_of([state_ref]), query_refs)
        store_weights(weights, row_max, weights_out, max_out)

    def page_body(at):
        def body(weights_ref, max_ref, state_ref, joined_ref, *refs):
            query_refs, (grad_out,) = refs[:query_devices], refs[query_devices:]
            gradients = gradients_of(joined_ref[...], max_ref, query_refs)
            gradients(at, part_of(state_ref, at), weights_ref, grad_out)

        return body

    def mate_body(*refs):
        *state_refs, out_ref = refs
        for at, ref in enumerate(state_refs):
            out_ref[pl.ds(at * packed_rows, packed_rows), :] = part_of(ref, 1)[...]

    out_masks = list(itertools.product(range(query_devices), range(CORES)))

    for repeat in range(STEPS):
        last = repeat == STEPS - 1
        if repeat == 0:
            *chunk_parts, weights, maxima = call(
                first_body,
                forward_shapes,
                "forward",
                2 * matmul_cost,
                states + query_parts,
                chunk_scratch,
            )
        else:
            new_state, *chunk_parts, weights, maxima = call(
                next_body,
                [(CORES * packed_rows, width)] + forward_shapes,
                "update_forward",
                2 * matmul_cost,
                states + query_parts + grads + tiles,
                chunk_scratch,
            )
            states = [new_state]
        arrived = {
            turn: exchange(chunk_parts[turn], page=CORES * turn)
            for turn in reversed(range(1, ranks))
        }
        if repeat:
            new_states = states + [
                exchange(states[0], query=turn) for turn in range(1, query_devices)
            ]
        (merged,) = call(
            merge_body,
            [chunk_shape],
            "merge",
            2**20,
            query_parts + chunk_parts[:1] + list(arrived.values()),
        )
        all_merged = [merged] + [
            exchange(merged, page=CORES * turn) for turn in range(1, ranks)
        ]
        if last and repeat:
            other_weights = [
                call(
                    weights_body,
                    weight_shapes,
                    "other_weights",
                    matmul_cost,
                    [new_states[turn]] + query_parts_of[turn],
                )
                for turn in range(1, query_devices)
            ]
            all_merged = call(
                join_body,
                [(width + TAIL, query_rows)],
                "join",
                2**20,
                all_merged,
                chunk_scratch,
                after=[head_weights[1] for head_weights in other_weights],
            )
            all_joined = [
                to_device(all_merged[0], query=turn) for turn in range(query_devices)
            ]
        own_grad, mate_grad, squares = call(
            backward_body,
            packed_shapes + [(devices, TAIL, width)],
            "backward",
            3 * matmul_cost,
            [weights, maxima] + states + query_parts + list(all_merged),
            scratch=() if last and repeat else chunk_scratch,
            after=[part for parts in query_parts_of[1:] for part in parts],
        )
        grads = [own_grad, mate_grad]
        tiles = [
            lax.all_to_all(
                squares, ("page", "query", "head"), split_axis=0, concat_axis=0, tiled=True
            )
        ]

    all_grads = [own_grad, exchange(mate_grad, page=1)]
    for turn in range(1, query_devices):
        operands = list(other_weights[turn - 1]) + [new_states[turn], all_joined[turn]]
        page_grads = [
            call(
                page_body(at),
                [(packed_rows, width)],
                "other_backward",
                3 * matmul_cost // 2,
                operands + query_parts_of[turn],
                after=[squares],
            )[0]
            for at in reversed(range(CORES))
        ]
        all_grads += [page_grads[1], exchange(page_grads[0], page=1)]
    (for_mate,) = call(
        mate_body,
        [(query_devices * packed_rows, width)],
        "mate_parts",
        2**20,
        new_states,
        after=all_joined[1:] + [squares],
    )
    from_mate = exchange(for_mate, page=1)

    def last_body(*refs):
        state_refs, (mate_ref, *refs) = refs[:query_devices], refs[query_devices:]
        state_refs = [
            part_of(mate_ref, turn) if flip else part_of(state_refs[turn], 0)
            for turn, flip in out_masks
        ]
        grad_refs, refs = refs[:local_heads], refs[local_heads:]
        tile_refs, (keys_out, values_out, bias_out) = refs[: len(tiles)], refs[len(tiles) :]
        _, core, me = places()
        sizes = step_sizes(tile_refs)
        for at, (turn, flip) in enumerate(out_masks):
            keys, values, bias = updated(state_refs[at], grad_refs[at], sizes)
            head = CORES * (me ^ turn) + (core ^ flip)
            keys_out[head] = keys
            values_out[head] = values
            bias_row = jnp.concatenate([bias[row : row + 1] for row in range(bias_rows)], axis=1)
            bias_out[pl.ds(head, 1), :] = bias_row

    return tuple(
        call(
            last_body,
            [compact_keys.shape, compact_values.shape, slot_bias.shape],
            "last_update",
            2**20,
            new_states + [from_mate] + all_grads + tiles,
        )
    )


def from_partner(value, axis, stride):
    mask = 2**stride
    pairs = [(source, source ^ mask) for source in range(lax.axis_size(axis))]
    return lax.ppermute(value, axis, pairs)


def squared_sums(grad_keys, grad_values, grad_bias):
    return jnp.stack(
        [
            jnp.sum(grad_keys * grad_keys),
            jnp.sum(grad_values * grad_values),
            jnp.sum(grad_bias * grad_bias),
        ]
    )


def apply_update(states, grads, totals, entry_count, slot_total):
    key_state, value_state, bias_state = states
    grad_keys, grad_values, grad_bias = grads
    rms_keys = jnp.sqrt(totals[0] / entry_count + EPSILON)
    rms_values = jnp.sqrt(totals[1] / entry_count + EPSILON)
    rms_bias = jnp.sqrt(totals[2] / slot_total + EPSILON)
    return (
        key_state - RATE_KEYS * grad_keys / rms_keys,
        value_state - RATE_VALUES * grad_values / rms_values,
        bias_state - RATE_BIAS * grad_bias / rms_bias,
    )


def local_gradients(queries, targets, visible, compact_keys, compact_values, slot_bias):
    score_scale = 1.0 / math.sqrt(queries.shape[2])
    scores = jnp.einsum("hqd,hsd->hqs", queries, compact_keys, precision=HIGHEST) * score_scale
    scores = jnp.where(visible, scores + slot_bias[:, None, :], MASKED)
    local_max = jnp.max(scores, axis=2)
    row_max = lax.pmax(local_max, "page")
    weights = jnp.where(visible, jnp.exp(scores - row_max[:, :, None]), 0.0)
    local_sum = jnp.einsum("hqs,hsd->hqd", weights, compact_values, precision=HIGHEST)
    row_total, row_sum = lax.psum((jnp.sum(weights, axis=2), local_sum), "page")
    attention = weights / row_total[:, :, None]
    output = row_sum / row_total[:, :, None]
    residual = output - targets
    grad_values = jnp.einsum("hqs,hqd->hsd", attention, residual, precision=HIGHEST)
    row_delta = jnp.sum(residual * output, axis=2)
    grad_probs = jnp.einsum("hqd,hsd->hqs", residual, compact_values, precision=HIGHEST)
    grad_scores = attention * (grad_probs - row_delta[:, :, None])
    grad_bias = jnp.sum(grad_scores, axis=1)
    grad_keys = jnp.einsum("hqs,hqd->hsd", grad_scores, queries, precision=HIGHEST) * score_scale
    return (grad_keys, grad_values, grad_bias)


def per_device(queries, compact_keys, compact_values, slot_bias, targets, positions, assignment):
    page_number = assignment[lax.axis_index("page")]
    local_heads = compact_keys.shape[0]
    slot_total = local_heads * lax.axis_size("head") * compact_keys.shape[1] * lax.axis_size("page")
    entry_count = slot_total * compact_keys.shape[2]
    query_count = lax.axis_size("query")
    heads_kept = max(local_heads // query_count, 1)
    query_parts = max(query_count // local_heads, 1)
    part_rows = queries.shape[1] // query_parts

    def split_items(array):
        width = array.shape[2]
        array = array.reshape(local_heads // heads_kept, heads_kept, query_parts, part_rows, width)
        array = jnp.transpose(array, (0, 2, 1, 3, 4))
        return array.reshape(query_count, heads_kept, part_rows, width)

    def join_items(array):
        width = array.shape[3]
        array = jnp.transpose(array, (1, 0, 2, 3))
        return array.reshape(heads_kept, query_count * part_rows, width)

    position_column = positions.astype(jnp.float32)[:, :, None]
    got_queries, got_targets, got_positions = (
        lax.all_to_all(split_items(queries), "query", split_axis=0, concat_axis=0, tiled=True),
        lax.all_to_all(split_items(targets), "query", split_axis=0, concat_axis=0, tiled=True),
        lax.all_to_all(
            split_items(position_column), "query", split_axis=0, concat_axis=0, tiled=True
        ),
    )
    group_queries = join_items(got_queries)
    group_targets = join_items(got_targets)
    group_positions = join_items(got_positions)[:, :, 0]
    visible = (page_number.astype(jnp.float32) <= jnp.floor(group_positions / PAGE_LEN))[:, :, None]
    query_index = lax.axis_index("query")
    first_head = query_index // query_parts * heads_kept
    key_state = lax.dynamic_slice_in_dim(compact_keys, first_head, heads_kept, 0)
    value_state = lax.dynamic_slice_in_dim(compact_values, first_head, heads_kept, 0)
    bias_state = lax.dynamic_slice_in_dim(slot_bias, first_head, heads_kept, 0)
    counted = (query_index % query_parts == 0).astype(jnp.float32)
    for repeat in range(STEPS):
        grads = local_gradients(
            group_queries, group_targets, visible, key_state, value_state, bias_state
        )
        for bit in range(query_parts.bit_length() - 1):
            partner = from_partner((grads[0], grads[1], grads[2]), "query", bit)
            grads = (grads[0] + partner[0], grads[1] + partner[1], grads[2] + partner[2])
        totals = lax.psum(
            squared_sums(grads[0], grads[1], grads[2]) * counted, ("page", "query", "head")
        )
        key_state, value_state, bias_state = apply_update(
            (key_state, value_state, bias_state), grads, totals, entry_count, slot_total
        )
    all_keys, all_values, all_bias = (
        lax.all_gather(key_state, "query", axis=0, tiled=True),
        lax.all_gather(value_state, "query", axis=0, tiled=True),
        lax.all_gather(bias_state, "query", axis=0, tiled=True),
    )
    slot_rows = compact_keys.shape[1]
    head_width = compact_keys.shape[2]
    all_keys = all_keys.reshape(
        local_heads // heads_kept, query_parts, heads_kept, slot_rows, head_width
    )[:, 0]
    all_values = all_values.reshape(
        local_heads // heads_kept, query_parts, heads_kept, slot_rows, head_width
    )[:, 0]
    all_bias = all_bias.reshape(local_heads // heads_kept, query_parts, heads_kept, slot_rows)[:, 0]
    return (
        all_keys.reshape(local_heads, slot_rows, head_width),
        all_values.reshape(local_heads, slot_rows, head_width),
        all_bias.reshape(local_heads, slot_rows),
    )


def solution(mesh):
    placed = (
        P("head", "query", None),
        P("head", "page", None),
        P("head", "page", None),
        P("head", "page"),
        P("head", "query", None),
        P("head", "query"),
        P(),
    )

    def program(*args):
        plan = direct_per_device if direct_plan_fits(mesh, args[0], args[1]) else per_device
        return jax.shard_map(
            plan,
            mesh=mesh,
            in_specs=placed,
            out_specs=(P("head", "page", None), P("head", "page", None), P("head", "page")),
            check_vma=False,
        )(*args)

    return program
```

```python
import itertools
import math

import jax
import jax.numpy as jnp
from jax import lax
from jax.experimental import pallas as pl
from jax.experimental.pallas import tpu as pltpu
from jax.sharding import PartitionSpec as P

STEPS = 2
PAGE_LEN = 32768


MASKED = -1e30
EPSILON = 1e-06
RATE_KEYS = 0.05
RATE_VALUES = 0.05
RATE_BIAS = 0.2
HIGHEST = lax.Precision.HIGHEST
TAIL = 8
CORES = 2


def exchange(value, **masks):
    axes = tuple(masks)
    sizes = [lax.axis_size(axis) for axis in axes]

    def flat(place):
        index = 0
        for size, at in zip(sizes, place):
            index = index * size + at
        return index

    pairs = [
        (flat(place), flat([at ^ mask for at, mask in zip(place, masks.values())]))
        for place in itertools.product(*map(range, sizes))
    ]
    return lax.ppermute(value, axes, pairs)


def halves(value):
    high = value.astype(jnp.bfloat16)
    return high, (value - high.astype(jnp.float32)).astype(jnp.bfloat16)


def dot(left, right, left_dim, right_dim):
    def one_pass(left_half, right_half):
        return lax.dot_general(
            left_half,
            right_half,
            (((left_dim,), (right_dim,)), ((), ())),
            preferred_element_type=jnp.float32,
        )

    cross = one_pass(left[0], right[1]) + one_pass(left[1], right[0])
    return one_pass(left[0], right[0]) + cross


def call(body, out_shapes, name, cost, operands, scratch=(), after=(), space=pltpu.VMEM, vmem=32):
    spaces = [space] * len(operands) + [pl.ANY] * len(after)
    count = len(operands)

    def without_after(*refs):
        body(*refs[:count], *refs[count + len(after) :])

    return pl.pallas_call(
        without_after,
        out_shape=[jax.ShapeDtypeStruct(shape, jnp.float32) for shape in out_shapes],
        in_specs=[pl.BlockSpec(memory_space=space) for space in spaces],
        out_specs=[pl.BlockSpec(memory_space=pltpu.VMEM) for _ in out_shapes],
        scratch_shapes=scratch,
        compiler_params=pltpu.CompilerParams(vmem_limit_bytes=vmem * 2**20),
        cost_estimate=pl.CostEstimate(
            flops=cost, bytes_accessed=min(cost, 2**20), transcendentals=0
        ),
        name=name,
    )(*operands, *after)


def row_as_tail(row, width):
    rows = [row[:, at : at + width] for at in range(0, row.shape[1], width)]
    rows.append(jnp.zeros((TAIL - len(rows), width), row.dtype))
    return jnp.concatenate(rows, axis=0)


def tail_as_row(ref, start, count):
    return jnp.concatenate([ref[start + at : start + at + 1, :] for at in range(count)], axis=1)


def row_as_column(row, width):
    parts = []
    for at in range(0, row.shape[1], width):
        parts.append(jnp.broadcast_to(row[:, at : at + width], (width, width)).T)
    return jnp.concatenate(parts, axis=0)


def direct_plan_fits(mesh, queries, compact_keys):
    sizes = [mesh.shape[axis] for axis in ("page", "query", "head")]
    pages, query_devices, head_devices = sizes
    local_heads = queries.shape[0] // head_devices
    part_rows = queries.shape[1] // query_devices
    slot_rows = compact_keys.shape[1] // pages
    width = queries.shape[2]
    if any(size & (size - 1) for size in sizes) or pages < CORES or width % 128:
        return False
    if local_heads != CORES * query_devices:
        return False
    ranks = pages // CORES
    chunk = part_rows * query_devices // ranks
    return (
        part_rows * query_devices % ranks == 0
        and chunk % 128 == 0
        and part_rows % (8 * ranks) == 0
        and slot_rows % width == 0
        and part_rows % width == 0
        and max(slot_rows, part_rows) < TAIL * width
    )


def direct_per_device(
    queries, compact_keys, compact_values, slot_bias, targets, positions, assignment
):
    local_heads, part_rows, width = queries.shape
    slot_rows = compact_keys.shape[1]
    query_devices = lax.axis_size("query")
    head_devices = lax.axis_size("head")
    ranks = lax.axis_size("page") // CORES
    query_rows = part_rows * query_devices
    chunk, piece = query_rows // ranks, part_rows // ranks
    slot_total = local_heads * head_devices * slot_rows * lax.axis_size("page")
    entry_total = slot_total * width
    score_scale = 1.0 / math.sqrt(width)
    slots = CORES * slot_rows
    devices = ranks * CORES * query_devices * head_devices
    pos_rows = part_rows // width
    bias_rows = slot_rows // width
    packed_rows = 2 * slot_rows + TAIL
    packed_shapes = [(packed_rows, width)] * 2
    matmul_cost = 3 * 2 * slots * query_rows * width

    def places():
        page = lax.axis_index("page")
        return page // CORES, page % CORES, lax.axis_index("query")

    def to_device(value, **masks):
        masks = {axis: mask for axis, mask in masks.items() if mask}
        return exchange(value, **masks) if masks else value

    def pack_queries(head, rank, queries, targets, out):
        rows = pl.ds(pl.multiple_of(rank * piece, piece), piece)
        return [
            (queries.at[head], out.at[pl.ds(0, part_rows)]),
            (targets.at[head, rows], out.at[pl.ds(part_rows, piece)]),
        ]

    def pack_state(head, keys, values, out):
        return [
            (keys.at[head], out.at[pl.ds(0, slot_rows)]),
            (values.at[head], out.at[pl.ds(slot_rows, slot_rows)]),
        ]

    def start_all(copies, sems, first=0):
        copies = [
            pltpu.make_async_copy(source, target, sems.at[first + at])
            for at, (source, target) in enumerate(copies)
        ]
        for copy in copies:
            copy.start()
        return copies

    def position_tail(head, positions_ref):
        return row_as_tail(positions_ref[pl.ds(head, 1), :].astype(jnp.float32), width)

    def state_tail(head, page, bias_ref, assignment_ref):
        page_start = (assignment_ref[page] * PAGE_LEN).astype(jnp.float32)
        tail = row_as_tail(bias_ref[pl.ds(head, 1), :], width)
        return jnp.concatenate(
            [tail[: TAIL - 1], jnp.full((1, width), page_start, jnp.float32)], axis=0
        )

    def send_body(
        queries, keys, values, biases, targets, positions, assignment, state_out, *refs
    ):
        query_outs = refs[: query_devices - 1]
        bias_ref, positions_ref, assignment_ref, sems = refs[query_devices - 1 :]
        rank, core, me = places()
        heads = [CORES * (me ^ turn) + core for turn in range(1, query_devices)]
        mate_head = CORES * me + (core ^ 1)
        small = start_all(
            [(assignment, assignment_ref), (positions, positions_ref), (biases, bias_ref)], sems
        )
        copies = pack_state(mate_head, keys, values, state_out)
        for head, out in zip(heads, query_outs):
            copies += pack_queries(head, rank, queries, targets, out)
        copies = start_all(copies, sems, 3)
        for copy in small:
            copy.wait()
        state_out[2 * slot_rows :, :] = state_tail(
            mate_head, CORES * rank + core, bias_ref, assignment_ref
        )
        for head, out in zip(heads, query_outs):
            out[part_rows + piece :, :] = position_tail(head, positions_ref)
        for copy in copies:
            copy.wait()

    def own_body(
        queries, keys, values, biases, targets, positions, assignment, state_out, query_out, *refs
    ):
        bias_ref, positions_ref, assignment_ref, sems = refs
        rank, core, me = places()
        head = CORES * me + core
        small = start_all(
            [(assignment, assignment_ref), (positions, positions_ref), (biases, bias_ref)], sems
        )
        copies = pack_state(head, keys, values, state_out)
        copies += pack_queries(head, rank, queries, targets, query_out)
        copies = start_all(copies, sems, 3)
        for copy in small:
            copy.wait()
        state_out[2 * slot_rows :, :] = state_tail(
            head, CORES * rank + core, bias_ref, assignment_ref
        )
        query_out[part_rows + piece :, :] = position_tail(head, positions_ref)
        for copy in copies:
            copy.wait()

    state_shape, query_shape = (packed_rows, width), (part_rows + piece + TAIL, width)
    small_scratch = [
        pltpu.VMEM(slot_bias.shape, jnp.float32),
        pltpu.VMEM(positions.shape, jnp.int32),
        pltpu.SMEM(assignment.shape, jnp.int32),
    ]
    arguments = [
        queries, compact_keys, compact_values, slot_bias, targets, positions, assignment
    ]
    mate_state, *sent_queries = call(
        send_body,
        [state_shape] + [query_shape] * (query_devices - 1),
        "pack",
        2**20,
        arguments,
        small_scratch + [pltpu.SemaphoreType.DMA((3 + 2 * query_devices,))],
        space=pl.ANY,
        vmem=60,
    )
    own_state, own_queries = call(
        own_body,
        [state_shape, query_shape],
        "own",
        2**24,
        arguments,
        small_scratch + [pltpu.SemaphoreType.DMA((7,))],
        space=pl.ANY,
    )
    packs = [own_queries] + list(sent_queries)
    query_parts_of = [
        [to_device(packs[part], query=turn ^ part) for part in range(query_devices)]
        for turn in range(query_devices)
    ]
    query_parts = query_parts_of[0]
    states = [own_state, exchange(mate_state, page=1)]

    def in_columns(parts, axis):
        return jnp.concatenate(
            [
                lax.slice_in_dim(part, at * piece, (at + 1) * piece, axis=axis)
                for at in range(ranks)
                for part in parts
            ],
            axis=axis,
        )

    def read_queries(query_refs):
        return halves(in_columns([ref[:part_rows, :] for ref in query_refs], 0))

    def part_of(ref, at):
        return ref.at[pl.ds(at * packed_rows, packed_rows)]

    def parts_of(refs):
        return refs if len(refs) == CORES else [part_of(refs[0], at) for at in range(CORES)]

    def step_sizes(tile_refs):
        tile = jnp.sum(tile_refs[0][...], axis=0)
        sums = jnp.sum(tile, axis=1, keepdims=True)
        return (
            RATE_KEYS / jnp.sqrt(sums[0:1] / entry_total + EPSILON),
            RATE_VALUES / jnp.sqrt(sums[1:2] / entry_total + EPSILON),
            RATE_BIAS / jnp.sqrt(sums[2:3] / slot_total + EPSILON),
        )

    def updated(state_ref, grad_ref, sizes):
        key_end, value_end = slot_rows, 2 * slot_rows
        return (
            state_ref[:key_end, :] - sizes[0] * grad_ref[:key_end, :],
            state_ref[key_end:value_end, :] - sizes[1] * grad_ref[key_end:value_end, :],
            state_ref[value_end:, :] - sizes[2] * grad_ref[value_end:, :],
        )

    def read_positions(query_refs):
        return in_columns(
            [tail_as_row(ref, part_rows + piece, pos_rows) for ref in query_refs], 1
        )

    def page_scores(ref, all_queries, positions):
        scores = dot(halves(ref[:slot_rows, :]), all_queries, 1, 1) * score_scale
        bias = row_as_column(tail_as_row(ref, 2 * slot_rows, bias_rows), width)
        scores = scores + jnp.concatenate([bias] * (query_rows // width), axis=1)
        page_start = ref[packed_rows - 1 : packed_rows, 0:1]
        visible = jnp.broadcast_to(positions >= page_start, scores.shape)
        return jnp.where(visible, scores, MASKED), visible

    def all_weights(state_refs, query_refs):
        all_queries, positions = read_queries(query_refs), read_positions(query_refs)
        pages = [page_scores(ref, all_queries, positions) for ref in state_refs]
        row_max = jnp.max(pages[0][0], axis=0, keepdims=True)
        for scores, _ in pages[1:]:
            row_max = jnp.maximum(row_max, jnp.max(scores, axis=0, keepdims=True))
        weights = [
            jnp.where(visible, jnp.exp(scores - row_max), 0.0) for scores, visible in pages
        ]
        return weights, row_max

    def store_weights(weights, row_max, weights_out, max_out):
        for at, part in enumerate(weights):
            weights_out[at * slot_rows : (at + 1) * slot_rows, :] = part
        max_out[...] = jnp.broadcast_to(row_max, (TAIL, query_rows))

    def forward(state_refs, query_refs, chunk_outs, weights_out, max_out, chunks):
        rank, _, _ = places()
        weights, row_max = all_weights(state_refs, query_refs)
        store_weights(weights, row_max, weights_out, max_out)
        row_total = jnp.zeros_like(row_max)
        row_sum = jnp.zeros((width, query_rows), jnp.float32)
        for ref, part in zip(state_refs, weights):
            row_total = row_total + jnp.sum(part, axis=0, keepdims=True)
            values = halves(ref[slot_rows : 2 * slot_rows, :])
            row_sum = row_sum + dot(values, halves(part), 0, 0)
        tail = jnp.concatenate(
            [row_max, row_total, jnp.zeros((TAIL - 2, query_rows), jnp.float32)], axis=0
        )
        for at in range(ranks):
            columns = slice(at * chunk, (at + 1) * chunk)
            chunks[at, :width, :] = row_sum[:, columns]
            chunks[at, width:, :] = tail[:, columns]
        for turn in range(ranks):
            chunk_outs[turn][...] = chunks[rank ^ turn]

    chunk_shape = (width + TAIL, chunk)
    weight_shapes = [(slots, query_rows), (TAIL, query_rows)]
    forward_shapes = [chunk_shape] * ranks + weight_shapes
    chunk_scratch = [pltpu.VMEM((ranks,) + chunk_shape, jnp.float32)]

    def first_body(*refs):
        state_refs, refs = refs[:2], refs[2:]
        query_refs, refs = refs[:query_devices], refs[query_devices:]
        chunk_outs, refs = refs[:ranks], refs[ranks:]
        forward(state_refs, query_refs, chunk_outs, *refs)

    def next_body(*refs):
        state_refs, refs = refs[:2], refs[2:]
        query_refs, refs = refs[:query_devices], refs[query_devices:]
        grad_refs, refs = refs[:2], refs[2:]
        tile_refs, refs = refs[: len(tiles)], refs[len(tiles) :]
        state_outs, refs = parts_of(refs[:1]), refs[1:]
        chunk_outs, refs = refs[:ranks], refs[ranks:]
        sizes = step_sizes(tile_refs)
        for at in range(2):
            keys, values, bias = updated(state_refs[at], grad_refs[at], sizes)
            state_outs[at][:slot_rows, :] = keys
            state_outs[at][slot_rows : 2 * slot_rows, :] = values
            state_outs[at][2 * slot_rows :, :] = bias
        forward(state_outs, query_refs, chunk_outs, *refs)

    def merge_body(*refs):
        query_refs, refs = refs[:query_devices], refs[query_devices:]
        chunk_refs, (merged_out,) = refs[:ranks], refs[ranks:]
        targets = jnp.concatenate(
            [ref[part_rows : part_rows + piece, :] for ref in query_refs], axis=0
        )
        row_max = chunk_refs[0][width : width + 1, :]
        for ref in chunk_refs[1:]:
            row_max = jnp.maximum(row_max, ref[width : width + 1, :])
        row_total = jnp.zeros_like(row_max)
        row_sum = jnp.zeros((width, chunk), jnp.float32)
        for ref in chunk_refs:
            factor = jnp.exp(ref[width : width + 1, :] - row_max)
            row_total = row_total + ref[width + 1 : width + 2, :] * factor
            row_sum = row_sum + ref[:width, :] * factor
        output = row_sum / row_total
        residual = output - targets.T
        row_delta = jnp.sum(residual * output, axis=0, keepdims=True)
        merged_out[:width, :] = residual
        merged_out[width:, :] = jnp.concatenate(
            [row_max, row_total, row_delta, jnp.zeros((TAIL - 3, chunk), jnp.float32)], axis=0
        )

    def join_chunks(merged_refs, chunks):
        rank, _, _ = places()
        for turn, ref in enumerate(merged_refs):
            chunks[rank ^ turn] = ref[...]
        return jnp.concatenate([chunks[at] for at in range(ranks)], axis=1)

    def join_body(*refs):
        *merged_refs, joined_out, chunks = refs
        joined_out[...] = join_chunks(merged_refs, chunks)

    def page_gradients(weights, factor, state_ref, all_queries, residual, row_delta, out):
        attention = weights * factor
        grad_values = dot(halves(attention), residual, 1, 1)
        grad_probs = dot(halves(state_ref[slot_rows : 2 * slot_rows, :]), residual, 1, 0)
        grad_scores = halves(attention * (grad_probs - row_delta))
        grad_keys = dot(grad_scores, all_queries, 1, 0) * score_scale
        ones = jnp.ones((TAIL, query_rows), jnp.bfloat16)
        grad_bias = dot((ones, jnp.zeros_like(ones)), grad_scores, 1, 1)[0:1, :]
        grad_bias = row_as_tail(grad_bias, width)
        out[:slot_rows, :] = grad_keys
        out[slot_rows : 2 * slot_rows, :] = grad_values
        out[2 * slot_rows :, :] = grad_bias
        return [
            jnp.sum(grad * grad, axis=0, keepdims=True)
            for grad in (grad_keys, grad_values, grad_bias)
        ]

    def split_joined(joined):
        row_max, row_total, row_delta = (
            joined[width + at : width + at + 1, :] for at in range(3)
        )
        return halves(joined[:width, :]), row_max, row_total, row_delta

    def backward_body(weights_ref, max_ref, *refs):
        state_refs, refs = parts_of(refs[: len(states)]), refs[len(states) :]
        query_refs, refs = refs[:query_devices], refs[query_devices:]
        merged_refs, refs = refs[: len(all_merged)], refs[len(all_merged) :]
        grad_outs, (squares_out, *scratch) = refs[:2], refs[2:]
        joined = join_chunks(merged_refs, *scratch) if scratch else merged_refs[0][...]
        residual, row_max, row_total, row_delta = split_joined(joined)
        all_queries = read_queries(query_refs)
        factor = jnp.exp(max_ref[0:1, :] - row_max) / row_total
        squares = []
        for at, (ref, out) in enumerate(zip(state_refs, grad_outs)):
            weights = weights_ref[at * slot_rows : (at + 1) * slot_rows, :]
            squares.append(
                page_gradients(weights, factor, ref, all_queries, residual, row_delta, out)
            )
        tile = jnp.concatenate(
            [sum(parts) for parts in zip(*squares)]
            + [jnp.zeros((TAIL - 3, width), jnp.float32)],
            axis=0,
        )
        for at in range(devices):
            squares_out[at] = tile

    def page_body(at):
        def body(state_ref, joined_ref, *refs):
            query_refs, (grad_out,) = refs[:query_devices], refs[query_devices:]
            residual, row_max, row_total, row_delta = split_joined(joined_ref[...])
            all_queries = read_queries(query_refs)
            ref = part_of(state_ref, at)
            scores, visible = page_scores(ref, all_queries, read_positions(query_refs))
            weights = jnp.where(visible, jnp.exp(scores - row_max), 0.0)
            page_gradients(
                weights, 1.0 / row_total, ref, all_queries, residual, row_delta, grad_out
            )

        return body

    def mate_body(*refs):
        *state_refs, out_ref = refs
        for at, ref in enumerate(state_refs):
            out_ref[pl.ds(at * packed_rows, packed_rows), :] = part_of(ref, 1)[...]

    out_masks = list(itertools.product(range(query_devices), range(CORES)))

    for repeat in range(STEPS):
        last = repeat == STEPS - 1
        if repeat == 0:
            *chunk_parts, weights, maxima = call(
                first_body,
                forward_shapes,
                "forward",
                2 * matmul_cost,
                states + query_parts,
                chunk_scratch,
            )
        else:
            new_state, *chunk_parts, weights, maxima = call(
                next_body,
                [(CORES * packed_rows, width)] + forward_shapes,
                "update_forward",
                2 * matmul_cost,
                states + query_parts + grads + tiles,
                chunk_scratch,
            )
            states = [new_state]
        arrived = {
            turn: exchange(chunk_parts[turn], page=CORES * turn)
            for turn in reversed(range(1, ranks))
        }
        if repeat:
            new_states = states + [
                exchange(states[0], query=turn) for turn in range(1, query_devices)
            ]
        (merged,) = call(
            merge_body,
            [chunk_shape],
            "merge",
            2**20,
            query_parts + chunk_parts[:1] + list(arrived.values()),
        )
        all_merged = [merged] + [
            exchange(merged, page=CORES * turn) for turn in range(1, ranks)
        ]
        if last and repeat:
            all_merged = call(
                join_body, [(width + TAIL, query_rows)], "join", 2**20, all_merged, chunk_scratch
            )
            all_joined = [
                to_device(all_merged[0], query=turn) for turn in range(query_devices)
            ]
        own_grad, mate_grad, squares = call(
            backward_body,
            packed_shapes + [(devices, TAIL, width)],
            "backward",
            3 * matmul_cost,
            [weights, maxima] + states + query_parts + list(all_merged),
            scratch=() if last and repeat else chunk_scratch,
            after=[part for parts in query_parts_of[1:] for part in parts],
        )
        grads = [own_grad, mate_grad]
        tiles = [
            lax.all_to_all(
                squares, ("page", "query", "head"), split_axis=0, concat_axis=0, tiled=True
            )
        ]

    all_grads = [own_grad, exchange(mate_grad, page=1)]
    for turn in range(1, query_devices):
        operands = [new_states[turn], all_joined[turn]]
        page_grads = [
            call(
                page_body(at),
                [(packed_rows, width)],
                "other_backward",
                0,
                operands + query_parts_of[turn],
                after=[squares],
            )[0]
            for at in reversed(range(CORES))
        ]
        all_grads += [page_grads[1], exchange(page_grads[0], page=1)]
    (for_mate,) = call(
        mate_body,
        [(query_devices * packed_rows, width)],
        "mate_parts",
        0,
        new_states,
        after=all_joined[1:] + [squares],
    )
    from_mate = exchange(for_mate, page=1)

    def last_body(*refs):
        state_refs, (mate_ref, *refs) = refs[:query_devices], refs[query_devices:]
        state_refs = [
            part_of(mate_ref, turn) if flip else part_of(state_refs[turn], 0)
            for turn, flip in out_masks
        ]
        grad_refs, refs = refs[:local_heads], refs[local_heads:]
        tile_refs, (keys_out, values_out, bias_out) = refs[: len(tiles)], refs[len(tiles) :]
        _, core, me = places()
        sizes = step_sizes(tile_refs)
        for at, (turn, flip) in enumerate(out_masks):
            keys, values, bias = updated(state_refs[at], grad_refs[at], sizes)
            head = CORES * (me ^ turn) + (core ^ flip)
            keys_out[head] = keys
            values_out[head] = values
            bias_row = jnp.concatenate([bias[row : row + 1] for row in range(bias_rows)], axis=1)
            bias_out[pl.ds(head, 1), :] = bias_row

    return tuple(
        call(
            last_body,
            [compact_keys.shape, compact_values.shape, slot_bias.shape],
            "last_update",
            2**20,
            new_states + [from_mate] + all_grads + tiles,
        )
    )


def from_partner(value, axis, stride):
    mask = 2**stride
    pairs = [(source, source ^ mask) for source in range(lax.axis_size(axis))]
    return lax.ppermute(value, axis, pairs)


def squared_sums(grad_keys, grad_values, grad_bias):
    return jnp.stack(
        [
            jnp.sum(grad_keys * grad_keys),
            jnp.sum(grad_values * grad_values),
            jnp.sum(grad_bias * grad_bias),
        ]
    )


def apply_update(states, grads, totals, entry_count, slot_total):
    key_state, value_state, bias_state = states
    grad_keys, grad_values, grad_bias = grads
    rms_keys = jnp.sqrt(totals[0] / entry_count + EPSILON)
    rms_values = jnp.sqrt(totals[1] / entry_count + EPSILON)
    rms_bias = jnp.sqrt(totals[2] / slot_total + EPSILON)
    return (
        key_state - RATE_KEYS * grad_keys / rms_keys,
        value_state - RATE_VALUES * grad_values / rms_values,
        bias_state - RATE_BIAS * grad_bias / rms_bias,
    )


def local_gradients(queries, targets, visible, compact_keys, compact_values, slot_bias):
    score_scale = 1.0 / math.sqrt(queries.shape[2])
    scores = jnp.einsum("hqd,hsd->hqs", queries, compact_keys, precision=HIGHEST) * score_scale
    scores = jnp.where(visible, scores + slot_bias[:, None, :], MASKED)
    local_max = jnp.max(scores, axis=2)
    row_max = lax.pmax(local_max, "page")
    weights = jnp.where(visible, jnp.exp(scores - row_max[:, :, None]), 0.0)
    local_sum = jnp.einsum("hqs,hsd->hqd", weights, compact_values, precision=HIGHEST)
    row_total, row_sum = lax.psum((jnp.sum(weights, axis=2), local_sum), "page")
    attention = weights / row_total[:, :, None]
    output = row_sum / row_total[:, :, None]
    residual = output - targets
    grad_values = jnp.einsum("hqs,hqd->hsd", attention, residual, precision=HIGHEST)
    row_delta = jnp.sum(residual * output, axis=2)
    grad_probs = jnp.einsum("hqd,hsd->hqs", residual, compact_values, precision=HIGHEST)
    grad_scores = attention * (grad_probs - row_delta[:, :, None])
    grad_bias = jnp.sum(grad_scores, axis=1)
    grad_keys = jnp.einsum("hqs,hqd->hsd", grad_scores, queries, precision=HIGHEST) * score_scale
    return (grad_keys, grad_values, grad_bias)


def per_device(queries, compact_keys, compact_values, slot_bias, targets, positions, assignment):
    page_number = assignment[lax.axis_index("page")]
    local_heads = compact_keys.shape[0]
    slot_total = local_heads * lax.axis_size("head") * compact_keys.shape[1] * lax.axis_size("page")
    entry_count = slot_total * compact_keys.shape[2]
    query_count = lax.axis_size("query")
    heads_kept = max(local_heads // query_count, 1)
    query_parts = max(query_count // local_heads, 1)
    part_rows = queries.shape[1] // query_parts

    def split_items(array):
        width = array.shape[2]
        array = array.reshape(local_heads // heads_kept, heads_kept, query_parts, part_rows, width)
        array = jnp.transpose(array, (0, 2, 1, 3, 4))
        return array.reshape(query_count, heads_kept, part_rows, width)

    def join_items(array):
        width = array.shape[3]
        array = jnp.transpose(array, (1, 0, 2, 3))
        return array.reshape(heads_kept, query_count * part_rows, width)

    position_column = positions.astype(jnp.float32)[:, :, None]
    got_queries, got_targets, got_positions = (
        lax.all_to_all(split_items(queries), "query", split_axis=0, concat_axis=0, tiled=True),
        lax.all_to_all(split_items(targets), "query", split_axis=0, concat_axis=0, tiled=True),
        lax.all_to_all(
            split_items(position_column), "query", split_axis=0, concat_axis=0, tiled=True
        ),
    )
    group_queries = join_items(got_queries)
    group_targets = join_items(got_targets)
    group_positions = join_items(got_positions)[:, :, 0]
    visible = (page_number.astype(jnp.float32) <= jnp.floor(group_positions / PAGE_LEN))[:, :, None]
    query_index = lax.axis_index("query")
    first_head = query_index // query_parts * heads_kept
    key_state = lax.dynamic_slice_in_dim(compact_keys, first_head, heads_kept, 0)
    value_state = lax.dynamic_slice_in_dim(compact_values, first_head, heads_kept, 0)
    bias_state = lax.dynamic_slice_in_dim(slot_bias, first_head, heads_kept, 0)
    counted = (query_index % query_parts == 0).astype(jnp.float32)
    for repeat in range(STEPS):
        grads = local_gradients(
            group_queries, group_targets, visible, key_state, value_state, bias_state
        )
        for bit in range(query_parts.bit_length() - 1):
            partner = from_partner((grads[0], grads[1], grads[2]), "query", bit)
            grads = (grads[0] + partner[0], grads[1] + partner[1], grads[2] + partner[2])
        totals = lax.psum(
            squared_sums(grads[0], grads[1], grads[2]) * counted, ("page", "query", "head")
        )
        key_state, value_state, bias_state = apply_update(
            (key_state, value_state, bias_state), grads, totals, entry_count, slot_total
        )
    all_keys, all_values, all_bias = (
        lax.all_gather(key_state, "query", axis=0, tiled=True),
        lax.all_gather(value_state, "query", axis=0, tiled=True),
        lax.all_gather(bias_state, "query", axis=0, tiled=True),
    )
    slot_rows = compact_keys.shape[1]
    head_width = compact_keys.shape[2]
    all_keys = all_keys.reshape(
        local_heads // heads_kept, query_parts, heads_kept, slot_rows, head_width
    )[:, 0]
    all_values = all_values.reshape(
        local_heads // heads_kept, query_parts, heads_kept, slot_rows, head_width
    )[:, 0]
    all_bias = all_bias.reshape(local_heads // heads_kept, query_parts, heads_kept, slot_rows)[:, 0]
    return (
        all_keys.reshape(local_heads, slot_rows, head_width),
        all_values.reshape(local_heads, slot_rows, head_width),
        all_bias.reshape(local_heads, slot_rows),
    )


def solution(mesh):
    placed = (
        P("head", "query", None),
        P("head", "page", None),
        P("head", "page", None),
        P("head", "page"),
        P("head", "query", None),
        P("head", "query"),
        P(),
    )

    def program(*args):
        plan = direct_per_device if direct_plan_fits(mesh, args[0], args[1]) else per_device
        return jax.shard_map(
            plan,
            mesh=mesh,
            in_specs=placed,
            out_specs=(P("head", "page", None), P("head", "page", None), P("head", "page")),
            check_vma=False,
        )(*args)

    return program
```

```python
import itertools
import math

import jax
import jax.numpy as jnp
from jax import lax
from jax.experimental import pallas as pl
from jax.experimental.pallas import tpu as pltpu
from jax.sharding import PartitionSpec as P

STEPS = 2
PAGE_LEN = 32768


MASKED = -1e30
EPSILON = 1e-06
RATE_KEYS = 0.05
RATE_VALUES = 0.05
RATE_BIAS = 0.2
HIGHEST = lax.Precision.HIGHEST
TAIL = 8
CORES = 2


def exchange(value, **masks):
    axes = tuple(masks)
    sizes = [lax.axis_size(axis) for axis in axes]

    def flat(place):
        index = 0
        for size, at in zip(sizes, place):
            index = index * size + at
        return index

    pairs = [
        (flat(place), flat([at ^ mask for at, mask in zip(place, masks.values())]))
        for place in itertools.product(*map(range, sizes))
    ]
    return lax.ppermute(value, axes, pairs)


def halves(value):
    high = value.astype(jnp.bfloat16)
    return high, (value - high.astype(jnp.float32)).astype(jnp.bfloat16)


def dot(left, right, left_dim, right_dim):
    def one_pass(left_half, right_half):
        return lax.dot_general(
            left_half,
            right_half,
            (((left_dim,), (right_dim,)), ((), ())),
            preferred_element_type=jnp.float32,
        )

    cross = one_pass(left[0], right[1]) + one_pass(left[1], right[0])
    return one_pass(left[0], right[0]) + cross


def call(body, out_shapes, name, cost, operands, scratch=(), after=(), space=pltpu.VMEM, vmem=32):
    spaces = [space] * len(operands) + [pl.ANY] * len(after)
    count = len(operands)

    def without_after(*refs):
        body(*refs[:count], *refs[count + len(after) :])

    return pl.pallas_call(
        without_after,
        out_shape=[
            shape if hasattr(shape, "dtype") else jax.ShapeDtypeStruct(shape, jnp.float32)
            for shape in out_shapes
        ],
        in_specs=[pl.BlockSpec(memory_space=space) for space in spaces],
        out_specs=[pl.BlockSpec(memory_space=pltpu.VMEM) for _ in out_shapes],
        scratch_shapes=scratch,
        compiler_params=pltpu.CompilerParams(vmem_limit_bytes=vmem * 2**20),
        cost_estimate=pl.CostEstimate(
            flops=cost, bytes_accessed=min(cost, 2**20), transcendentals=0
        ),
        name=name,
    )(*operands, *after)


def row_as_tail(row, width):
    rows = [row[:, at : at + width] for at in range(0, row.shape[1], width)]
    rows.append(jnp.zeros((TAIL - len(rows), width), row.dtype))
    return jnp.concatenate(rows, axis=0)


def tail_as_row(ref, start, count):
    return jnp.concatenate([ref[start + at : start + at + 1, :] for at in range(count)], axis=1)


def row_as_column(row, width):
    parts = []
    for at in range(0, row.shape[1], width):
        parts.append(jnp.broadcast_to(row[:, at : at + width], (width, width)).T)
    return jnp.concatenate(parts, axis=0)


def direct_plan_fits(mesh, queries, compact_keys):
    sizes = [mesh.shape[axis] for axis in ("page", "query", "head")]
    pages, query_devices, head_devices = sizes
    local_heads = queries.shape[0] // head_devices
    part_rows = queries.shape[1] // query_devices
    slot_rows = compact_keys.shape[1] // pages
    width = queries.shape[2]
    if any(size & (size - 1) for size in sizes) or pages < CORES or width % 128:
        return False
    if local_heads != CORES * query_devices:
        return False
    ranks = pages // CORES
    chunk = part_rows * query_devices // ranks
    return (
        part_rows * query_devices % ranks == 0
        and chunk % 128 == 0
        and part_rows % (8 * ranks) == 0
        and slot_rows % width == 0
        and part_rows % width == 0
        and max(slot_rows, part_rows) < TAIL * width
    )


def direct_per_device(
    queries, compact_keys, compact_values, slot_bias, targets, positions, assignment
):
    local_heads, part_rows, width = queries.shape
    slot_rows = compact_keys.shape[1]
    query_devices = lax.axis_size("query")
    head_devices = lax.axis_size("head")
    ranks = lax.axis_size("page") // CORES
    query_rows = part_rows * query_devices
    chunk, piece = query_rows // ranks, part_rows // ranks
    slot_total = local_heads * head_devices * slot_rows * lax.axis_size("page")
    entry_total = slot_total * width
    score_scale = 1.0 / math.sqrt(width)
    slots = CORES * slot_rows
    devices = ranks * CORES * query_devices * head_devices
    pos_rows = part_rows // width
    bias_rows = slot_rows // width
    packed_rows = 2 * slot_rows + TAIL
    packed_shapes = [(packed_rows, width)] * 2
    matmul_cost = 3 * 2 * slots * query_rows * width

    def places():
        page = lax.axis_index("page")
        return page // CORES, page % CORES, lax.axis_index("query")

    def to_device(value, **masks):
        masks = {axis: mask for axis, mask in masks.items() if mask}
        return exchange(value, **masks) if masks else value

    def pack_queries(head, rank, queries, targets, out):
        rows = pl.ds(pl.multiple_of(rank * piece, piece), piece)
        return [
            (queries.at[head], out.at[pl.ds(0, part_rows)]),
            (targets.at[head, rows], out.at[pl.ds(part_rows, piece)]),
        ]

    def pack_state(head, keys, values, out):
        return [
            (keys.at[head], out.at[pl.ds(0, slot_rows)]),
            (values.at[head], out.at[pl.ds(slot_rows, slot_rows)]),
        ]

    def start_all(copies, sems, first=0):
        copies = [
            pltpu.make_async_copy(source, target, sems.at[first + at])
            for at, (source, target) in enumerate(copies)
        ]
        for copy in copies:
            copy.start()
        return copies

    def position_tail(head, positions_ref):
        return row_as_tail(positions_ref[pl.ds(head, 1), :].astype(jnp.float32), width)

    def state_tail(head, page, bias_ref, assignment_ref):
        page_start = (assignment_ref[page] * PAGE_LEN).astype(jnp.float32)
        tail = row_as_tail(bias_ref[pl.ds(head, 1), :], width)
        return jnp.concatenate(
            [tail[: TAIL - 1], jnp.full((1, width), page_start, jnp.float32)], axis=0
        )

    def send_body(
        queries, keys, values, biases, targets, positions, assignment, state_out, *refs
    ):
        query_outs = refs[: query_devices - 1]
        bias_ref, positions_ref, assignment_ref, sems = refs[query_devices - 1 :]
        rank, core, me = places()
        heads = [CORES * (me ^ turn) + core for turn in range(1, query_devices)]
        mate_head = CORES * me + (core ^ 1)
        small = start_all(
            [(assignment, assignment_ref), (positions, positions_ref), (biases, bias_ref)], sems
        )
        copies = pack_state(mate_head, keys, values, state_out)
        for head, out in zip(heads, query_outs):
            copies += pack_queries(head, rank, queries, targets, out)
        copies = start_all(copies, sems, 3)
        for copy in small:
            copy.wait()
        state_out[2 * slot_rows :, :] = state_tail(
            mate_head, CORES * rank + core, bias_ref, assignment_ref
        )
        for head, out in zip(heads, query_outs):
            out[part_rows + piece :, :] = position_tail(head, positions_ref)
        for copy in copies:
            copy.wait()

    def own_body(
        queries, keys, values, biases, targets, positions, assignment, state_out, query_out, *refs
    ):
        bias_ref, positions_ref, assignment_ref, sems = refs
        rank, core, me = places()
        head = CORES * me + core
        small = start_all(
            [(assignment, assignment_ref), (positions, positions_ref), (biases, bias_ref)], sems
        )
        copies = pack_state(head, keys, values, state_out)
        copies += pack_queries(head, rank, queries, targets, query_out)
        copies = start_all(copies, sems, 3)
        for copy in small:
            copy.wait()
        state_out[2 * slot_rows :, :] = state_tail(
            head, CORES * rank + core, bias_ref, assignment_ref
        )
        query_out[part_rows + piece :, :] = position_tail(head, positions_ref)
        for copy in copies:
            copy.wait()

    state_shape, query_shape = (packed_rows, width), (part_rows + piece + TAIL, width)
    small_scratch = [
        pltpu.VMEM(slot_bias.shape, jnp.float32),
        pltpu.VMEM(positions.shape, jnp.int32),
        pltpu.SMEM(assignment.shape, jnp.int32),
    ]
    arguments = [
        queries, compact_keys, compact_values, slot_bias, targets, positions, assignment
    ]
    mate_state, *sent_queries = call(
        send_body,
        [state_shape] + [query_shape] * (query_devices - 1),
        "pack",
        2**20,
        arguments,
        small_scratch + [pltpu.SemaphoreType.DMA((3 + 2 * query_devices,))],
        space=pl.ANY,
        vmem=60,
    )
    own_state, own_queries = call(
        own_body,
        [state_shape, query_shape],
        "own",
        2**24,
        arguments,
        small_scratch + [pltpu.SemaphoreType.DMA((7,))],
        space=pl.ANY,
    )
    packs = [own_queries] + list(sent_queries)
    query_parts_of = [
        [to_device(packs[part], query=turn ^ part) for part in range(query_devices)]
        for turn in range(query_devices)
    ]
    query_parts = query_parts_of[0]
    states = [own_state, exchange(mate_state, page=1)]

    def in_columns(parts, axis):
        return jnp.concatenate(
            [
                lax.slice_in_dim(part, at * piece, (at + 1) * piece, axis=axis)
                for at in range(ranks)
                for part in parts
            ],
            axis=axis,
        )

    def read_queries(query_refs):
        return halves(in_columns([ref[:part_rows, :] for ref in query_refs], 0))

    def part_of(ref, at):
        return ref.at[pl.ds(at * packed_rows, packed_rows)]

    def parts_of(refs):
        return refs if len(refs) == CORES else [part_of(refs[0], at) for at in range(CORES)]

    def step_sizes(tile_refs):
        tile = jnp.sum(tile_refs[0][...], axis=0)
        sums = jnp.sum(tile, axis=1, keepdims=True)
        return (
            RATE_KEYS / jnp.sqrt(sums[0:1] / entry_total + EPSILON),
            RATE_VALUES / jnp.sqrt(sums[1:2] / entry_total + EPSILON),
            RATE_BIAS / jnp.sqrt(sums[2:3] / slot_total + EPSILON),
        )

    def updated(state_ref, grad_ref, sizes):
        key_end, value_end = slot_rows, 2 * slot_rows
        return (
            state_ref[:key_end, :] - sizes[0] * grad_ref[:key_end, :],
            state_ref[key_end:value_end, :] - sizes[1] * grad_ref[key_end:value_end, :],
            state_ref[value_end:, :] - sizes[2] * grad_ref[value_end:, :],
        )

    def read_positions(query_refs):
        return in_columns(
            [tail_as_row(ref, part_rows + piece, pos_rows) for ref in query_refs], 1
        )

    def page_scores(ref, all_queries, positions):
        scores = dot(halves(ref[:slot_rows, :]), all_queries, 1, 1) * score_scale
        bias = row_as_column(tail_as_row(ref, 2 * slot_rows, bias_rows), width)
        scores = scores + jnp.concatenate([bias] * (query_rows // width), axis=1)
        page_start = ref[packed_rows - 1 : packed_rows, 0:1]
        visible = jnp.broadcast_to(positions >= page_start, scores.shape)
        return jnp.where(visible, scores, MASKED), visible

    def all_weights(state_refs, all_queries, positions):
        pages = [page_scores(ref, all_queries, positions) for ref in state_refs]
        row_max = jnp.max(pages[0][0], axis=0, keepdims=True)
        for scores, _ in pages[1:]:
            row_max = jnp.maximum(row_max, jnp.max(scores, axis=0, keepdims=True))
        weights = [
            jnp.where(visible, jnp.exp(scores - row_max), 0.0) for scores, visible in pages
        ]
        return weights, row_max

    def store_weights(weights, row_max, weights_out, max_out):
        for at, part in enumerate(weights):
            weights_out[at * slot_rows : (at + 1) * slot_rows, :] = part
        max_out[...] = jnp.broadcast_to(row_max, (TAIL, query_rows))

    def forward(state_refs, all_queries, positions, chunk_outs, weights_out, max_out, chunks):
        rank, _, _ = places()
        weights, row_max = all_weights(state_refs, all_queries, positions)
        store_weights(weights, row_max, weights_out, max_out)
        row_total = jnp.zeros_like(row_max)
        row_sum = jnp.zeros((width, query_rows), jnp.float32)
        for ref, part in zip(state_refs, weights):
            row_total = row_total + jnp.sum(part, axis=0, keepdims=True)
            values = halves(ref[slot_rows : 2 * slot_rows, :])
            row_sum = row_sum + dot(values, halves(part), 0, 0)
        tail = jnp.concatenate(
            [row_max, row_total, jnp.zeros((TAIL - 2, query_rows), jnp.float32)], axis=0
        )
        for at in range(ranks):
            columns = slice(at * chunk, (at + 1) * chunk)
            chunks[at, :width, :] = row_sum[:, columns]
            chunks[at, width:, :] = tail[:, columns]
        for turn in range(ranks):
            chunk_outs[turn][...] = chunks[rank ^ turn]

    chunk_shape = (width + TAIL, chunk)
    weight_shapes = [(slots, query_rows), (TAIL, query_rows)]
    forward_shapes = [chunk_shape] * ranks + weight_shapes
    chunk_scratch = [pltpu.VMEM((ranks,) + chunk_shape, jnp.float32)]

    def first_body(*refs):
        state_refs, refs = refs[:2], refs[2:]
        query_refs, refs = refs[:query_devices], refs[query_devices:]
        chunk_outs, refs = refs[:ranks], refs[ranks:]
        forward(
            state_refs, read_queries(query_refs), read_positions(query_refs), chunk_outs, *refs
        )

    def split_body(*refs):
        query_refs, (high_out, low_out, positions_out) = refs[:query_devices], refs[query_devices:]
        high_out[...], low_out[...] = read_queries(query_refs)
        positions_out[...] = jnp.broadcast_to(read_positions(query_refs), (TAIL, query_rows))

    half_shape = jax.ShapeDtypeStruct((query_rows, width), jnp.bfloat16)
    split_shapes = [half_shape, half_shape, (TAIL, query_rows)]

    def next_body(*refs):
        state_refs, refs = refs[:2], refs[2:]
        (high_ref, low_ref, positions_ref), refs = refs[:3], refs[3:]
        grad_refs, refs = refs[:2], refs[2:]
        tile_refs, refs = refs[: len(tiles)], refs[len(tiles) :]
        state_outs, refs = parts_of(refs[:1]), refs[1:]
        chunk_outs, refs = refs[:ranks], refs[ranks:]
        sizes = step_sizes(tile_refs)
        for at in range(2):
            keys, values, bias = updated(state_refs[at], grad_refs[at], sizes)
            state_outs[at][:slot_rows, :] = keys
            state_outs[at][slot_rows : 2 * slot_rows, :] = values
            state_outs[at][2 * slot_rows :, :] = bias
        forward(
            state_outs, (high_ref[...], low_ref[...]), positions_ref[0:1, :], chunk_outs, *refs
        )

    def merge_body(*refs):
        query_refs, refs = refs[:query_devices], refs[query_devices:]
        chunk_refs, (merged_out,) = refs[:ranks], refs[ranks:]
        targets = jnp.concatenate(
            [ref[part_rows : part_rows + piece, :] for ref in query_refs], axis=0
        )
        row_max = chunk_refs[0][width : width + 1, :]
        for ref in chunk_refs[1:]:
            row_max = jnp.maximum(row_max, ref[width : width + 1, :])
        row_total = jnp.zeros_like(row_max)
        row_sum = jnp.zeros((width, chunk), jnp.float32)
        for ref in chunk_refs:
            factor = jnp.exp(ref[width : width + 1, :] - row_max)
            row_total = row_total + ref[width + 1 : width + 2, :] * factor
            row_sum = row_sum + ref[:width, :] * factor
        output = row_sum / row_total
        residual = output - targets.T
        row_delta = jnp.sum(residual * output, axis=0, keepdims=True)
        merged_out[:width, :] = residual
        merged_out[width:, :] = jnp.concatenate(
            [row_max, row_total, row_delta, jnp.zeros((TAIL - 3, chunk), jnp.float32)], axis=0
        )

    def join_chunks(merged_refs, chunks):
        rank, _, _ = places()
        for turn, ref in enumerate(merged_refs):
            chunks[rank ^ turn] = ref[...]
        return jnp.concatenate([chunks[at] for at in range(ranks)], axis=1)

    def join_body(*refs):
        *merged_refs, joined_out, chunks = refs
        joined_out[...] = join_chunks(merged_refs, chunks)

    def page_gradients(weights, factor, state_ref, all_queries, residual, row_delta, out):
        attention = weights * factor
        grad_values = dot(halves(attention), residual, 1, 1)
        grad_probs = dot(halves(state_ref[slot_rows : 2 * slot_rows, :]), residual, 1, 0)
        grad_scores = halves(attention * (grad_probs - row_delta))
        grad_keys = dot(grad_scores, all_queries, 1, 0) * score_scale
        ones = jnp.ones((TAIL, query_rows), jnp.bfloat16)
        grad_bias = dot((ones, jnp.zeros_like(ones)), grad_scores, 1, 1)[0:1, :]
        grad_bias = row_as_tail(grad_bias, width)
        out[:slot_rows, :] = grad_keys
        out[slot_rows : 2 * slot_rows, :] = grad_values
        out[2 * slot_rows :, :] = grad_bias
        return [
            jnp.sum(grad * grad, axis=0, keepdims=True)
            for grad in (grad_keys, grad_values, grad_bias)
        ]

    def split_joined(joined):
        row_max, row_total, row_delta = (
            joined[width + at : width + at + 1, :] for at in range(3)
        )
        return halves(joined[:width, :]), row_max, row_total, row_delta

    def backward_body(weights_ref, max_ref, *refs):
        state_refs, refs = parts_of(refs[: len(states)]), refs[len(states) :]
        query_refs, refs = refs[: len(head_queries)], refs[len(head_queries) :]
        merged_refs, refs = refs[: len(all_merged)], refs[len(all_merged) :]
        grad_outs, (squares_out, *scratch) = refs[:2], refs[2:]
        joined = join_chunks(merged_refs, *scratch) if scratch else merged_refs[0][...]
        residual, row_max, row_total, row_delta = split_joined(joined)
        if head_queries is query_parts:
            all_queries = read_queries(query_refs)
        else:
            all_queries = (query_refs[0][...], query_refs[1][...])
        factor = jnp.exp(max_ref[0:1, :] - row_max) / row_total
        squares = []
        for at, (ref, out) in enumerate(zip(state_refs, grad_outs)):
            weights = weights_ref[at * slot_rows : (at + 1) * slot_rows, :]
            squares.append(
                page_gradients(weights, factor, ref, all_queries, residual, row_delta, out)
            )
        tile = jnp.concatenate(
            [sum(parts) for parts in zip(*squares)]
            + [jnp.zeros((TAIL - 3, width), jnp.float32)],
            axis=0,
        )
        for at in range(devices):
            squares_out[at] = tile

    def page_body(at):
        def body(state_ref, joined_ref, *refs):
            query_refs, (grad_out,) = refs[:query_devices], refs[query_devices:]
            residual, row_max, row_total, row_delta = split_joined(joined_ref[...])
            all_queries = read_queries(query_refs)
            ref = part_of(state_ref, at)
            scores, visible = page_scores(ref, all_queries, read_positions(query_refs))
            weights = jnp.where(visible, jnp.exp(scores - row_max), 0.0)
            page_gradients(
                weights, 1.0 / row_total, ref, all_queries, residual, row_delta, grad_out
            )

        return body

    def mate_body(*refs):
        *state_refs, out_ref = refs
        for at, ref in enumerate(state_refs):
            out_ref[pl.ds(at * packed_rows, packed_rows), :] = part_of(ref, 1)[...]

    out_masks = list(itertools.product(range(query_devices), range(CORES)))

    for repeat in range(STEPS):
        last = repeat == STEPS - 1
        head_queries = split_queries[:2] if repeat else query_parts
        if repeat == 0:
            *chunk_parts, weights, maxima = call(
                first_body,
                forward_shapes,
                "forward",
                2 * matmul_cost,
                states + query_parts,
                chunk_scratch,
            )
        else:
            new_state, *chunk_parts, weights, maxima = call(
                next_body,
                [(CORES * packed_rows, width)] + forward_shapes,
                "update_forward",
                2 * matmul_cost,
                states + split_queries + grads + tiles,
                chunk_scratch,
            )
            states = [new_state]
        arrived = {
            turn: exchange(chunk_parts[turn], page=CORES * turn)
            for turn in reversed(range(1, ranks))
        }
        if repeat:
            new_states = states + [
                exchange(states[0], query=turn) for turn in range(1, query_devices)
            ]
        (merged,) = call(
            merge_body,
            [chunk_shape],
            "merge",
            2**20,
            query_parts + chunk_parts[:1] + list(arrived.values()),
        )
        all_merged = [merged] + [
            exchange(merged, page=CORES * turn) for turn in range(1, ranks)
        ]
        if last and repeat:
            all_merged = call(
                join_body, [(width + TAIL, query_rows)], "join", 2**20, all_merged, chunk_scratch
            )
            all_joined = [
                to_device(all_merged[0], query=turn) for turn in range(query_devices)
            ]
        own_grad, mate_grad, squares = call(
            backward_body,
            packed_shapes + [(devices, TAIL, width)],
            "backward",
            3 * matmul_cost,
            [weights, maxima] + states + head_queries + list(all_merged),
            scratch=() if last and repeat else chunk_scratch,
            after=[part for parts in query_parts_of[1:] for part in parts],
        )
        grads = [own_grad, mate_grad]
        if repeat == 0:
            split_queries = call(
                split_body, split_shapes, "split_queries", 2**28, query_parts, after=[squares]
            )
            split_queries = list(split_queries)
        tiles = [
            lax.all_to_all(
                squares, ("page", "query", "head"), split_axis=0, concat_axis=0, tiled=True
            )
        ]

    (for_mate,) = call(
        mate_body,
        [(query_devices * packed_rows, width)],
        "mate_parts",
        2**28,
        new_states,
        after=[squares],
    )
    from_mate = exchange(for_mate, page=1)
    all_grads = [own_grad, exchange(mate_grad, page=1)]
    for turn in range(1, query_devices):
        page_grads = [
            call(
                page_body(at),
                [(packed_rows, width)],
                "other_backward",
                3 * matmul_cost // 2,
                [new_states[turn], all_joined[turn]] + query_parts_of[turn],
                after=tiles,
            )[0]
            for at in reversed(range(CORES))
        ]
        all_grads += [page_grads[1], exchange(page_grads[0], page=1)]

    def last_body(*refs):
        state_refs, (mate_ref, *refs) = refs[:query_devices], refs[query_devices:]
        state_refs = [
            part_of(mate_ref, turn) if flip else part_of(state_refs[turn], 0)
            for turn, flip in out_masks
        ]
        grad_refs, refs = refs[:local_heads], refs[local_heads:]
        tile_refs, (keys_out, values_out, bias_out) = refs[: len(tiles)], refs[len(tiles) :]
        _, core, me = places()
        sizes = step_sizes(tile_refs)
        for at, (turn, flip) in enumerate(out_masks):
            keys, values, bias = updated(state_refs[at], grad_refs[at], sizes)
            head = CORES * (me ^ turn) + (core ^ flip)
            keys_out[head] = keys
            values_out[head] = values
            bias_row = jnp.concatenate([bias[row : row + 1] for row in range(bias_rows)], axis=1)
            bias_out[pl.ds(head, 1), :] = bias_row

    return tuple(
        call(
            last_body,
            [compact_keys.shape, compact_values.shape, slot_bias.shape],
            "last_update",
            2**20,
            new_states + [from_mate] + all_grads + tiles,
        )
    )


def from_partner(value, axis, stride):
    mask = 2**stride
    pairs = [(source, source ^ mask) for source in range(lax.axis_size(axis))]
    return lax.ppermute(value, axis, pairs)


def squared_sums(grad_keys, grad_values, grad_bias):
    return jnp.stack(
        [
            jnp.sum(grad_keys * grad_keys),
            jnp.sum(grad_values * grad_values),
            jnp.sum(grad_bias * grad_bias),
        ]
    )


def apply_update(states, grads, totals, entry_count, slot_total):
    key_state, value_state, bias_state = states
    grad_keys, grad_values, grad_bias = grads
    rms_keys = jnp.sqrt(totals[0] / entry_count + EPSILON)
    rms_values = jnp.sqrt(totals[1] / entry_count + EPSILON)
    rms_bias = jnp.sqrt(totals[2] / slot_total + EPSILON)
    return (
        key_state - RATE_KEYS * grad_keys / rms_keys,
        value_state - RATE_VALUES * grad_values / rms_values,
        bias_state - RATE_BIAS * grad_bias / rms_bias,
    )


def local_gradients(queries, targets, visible, compact_keys, compact_values, slot_bias):
    score_scale = 1.0 / math.sqrt(queries.shape[2])
    scores = jnp.einsum("hqd,hsd->hqs", queries, compact_keys, precision=HIGHEST) * score_scale
    scores = jnp.where(visible, scores + slot_bias[:, None, :], MASKED)
    local_max = jnp.max(scores, axis=2)
    row_max = lax.pmax(local_max, "page")
    weights = jnp.where(visible, jnp.exp(scores - row_max[:, :, None]), 0.0)
    local_sum = jnp.einsum("hqs,hsd->hqd", weights, compact_values, precision=HIGHEST)
    row_total, row_sum = lax.psum((jnp.sum(weights, axis=2), local_sum), "page")
    attention = weights / row_total[:, :, None]
    output = row_sum / row_total[:, :, None]
    residual = output - targets
    grad_values = jnp.einsum("hqs,hqd->hsd", attention, residual, precision=HIGHEST)
    row_delta = jnp.sum(residual * output, axis=2)
    grad_probs = jnp.einsum("hqd,hsd->hqs", residual, compact_values, precision=HIGHEST)
    grad_scores = attention * (grad_probs - row_delta[:, :, None])
    grad_bias = jnp.sum(grad_scores, axis=1)
    grad_keys = jnp.einsum("hqs,hqd->hsd", grad_scores, queries, precision=HIGHEST) * score_scale
    return (grad_keys, grad_values, grad_bias)


def per_device(queries, compact_keys, compact_values, slot_bias, targets, positions, assignment):
    page_number = assignment[lax.axis_index("page")]
    local_heads = compact_keys.shape[0]
    slot_total = local_heads * lax.axis_size("head") * compact_keys.shape[1] * lax.axis_size("page")
    entry_count = slot_total * compact_keys.shape[2]
    query_count = lax.axis_size("query")
    heads_kept = max(local_heads // query_count, 1)
    query_parts = max(query_count // local_heads, 1)
    part_rows = queries.shape[1] // query_parts

    def split_items(array):
        width = array.shape[2]
        array = array.reshape(local_heads // heads_kept, heads_kept, query_parts, part_rows, width)
        array = jnp.transpose(array, (0, 2, 1, 3, 4))
        return array.reshape(query_count, heads_kept, part_rows, width)

    def join_items(array):
        width = array.shape[3]
        array = jnp.transpose(array, (1, 0, 2, 3))
        return array.reshape(heads_kept, query_count * part_rows, width)

    position_column = positions.astype(jnp.float32)[:, :, None]
    got_queries, got_targets, got_positions = (
        lax.all_to_all(split_items(queries), "query", split_axis=0, concat_axis=0, tiled=True),
        lax.all_to_all(split_items(targets), "query", split_axis=0, concat_axis=0, tiled=True),
        lax.all_to_all(
            split_items(position_column), "query", split_axis=0, concat_axis=0, tiled=True
        ),
    )
    group_queries = join_items(got_queries)
    group_targets = join_items(got_targets)
    group_positions = join_items(got_positions)[:, :, 0]
    visible = (page_number.astype(jnp.float32) <= jnp.floor(group_positions / PAGE_LEN))[:, :, None]
    query_index = lax.axis_index("query")
    first_head = query_index // query_parts * heads_kept
    key_state = lax.dynamic_slice_in_dim(compact_keys, first_head, heads_kept, 0)
    value_state = lax.dynamic_slice_in_dim(compact_values, first_head, heads_kept, 0)
    bias_state = lax.dynamic_slice_in_dim(slot_bias, first_head, heads_kept, 0)
    counted = (query_index % query_parts == 0).astype(jnp.float32)
    for repeat in range(STEPS):
        grads = local_gradients(
            group_queries, group_targets, visible, key_state, value_state, bias_state
        )
        for bit in range(query_parts.bit_length() - 1):
            partner = from_partner((grads[0], grads[1], grads[2]), "query", bit)
            grads = (grads[0] + partner[0], grads[1] + partner[1], grads[2] + partner[2])
        totals = lax.psum(
            squared_sums(grads[0], grads[1], grads[2]) * counted, ("page", "query", "head")
        )
        key_state, value_state, bias_state = apply_update(
            (key_state, value_state, bias_state), grads, totals, entry_count, slot_total
        )
    all_keys, all_values, all_bias = (
        lax.all_gather(key_state, "query", axis=0, tiled=True),
        lax.all_gather(value_state, "query", axis=0, tiled=True),
        lax.all_gather(bias_state, "query", axis=0, tiled=True),
    )
    slot_rows = compact_keys.shape[1]
    head_width = compact_keys.shape[2]
    all_keys = all_keys.reshape(
        local_heads // heads_kept, query_parts, heads_kept, slot_rows, head_width
    )[:, 0]
    all_values = all_values.reshape(
        local_heads // heads_kept, query_parts, heads_kept, slot_rows, head_width
    )[:, 0]
    all_bias = all_bias.reshape(local_heads // heads_kept, query_parts, heads_kept, slot_rows)[:, 0]
    return (
        all_keys.reshape(local_heads, slot_rows, head_width),
        all_values.reshape(local_heads, slot_rows, head_width),
        all_bias.reshape(local_heads, slot_rows),
    )


def solution(mesh):
    placed = (
        P("head", "query", None),
        P("head", "page", None),
        P("head", "page", None),
        P("head", "page"),
        P("head", "query", None),
        P("head", "query"),
        P(),
    )

    def program(*args):
        plan = direct_per_device if direct_plan_fits(mesh, args[0], args[1]) else per_device
        return jax.shard_map(
            plan,
            mesh=mesh,
            in_specs=placed,
            out_specs=(P("head", "page", None), P("head", "page", None), P("head", "page")),
            check_vma=False,
        )(*args)

    return program
```

```python
import itertools
import math

import jax
import jax.numpy as jnp
from jax import lax
from jax.experimental import pallas as pl
from jax.experimental.pallas import tpu as pltpu
from jax.sharding import PartitionSpec as P

STEPS = 2
PAGE_LEN = 32768


MASKED = -1e30
EPSILON = 1e-06
RATE_KEYS = 0.05
RATE_VALUES = 0.05
RATE_BIAS = 0.2
HIGHEST = lax.Precision.HIGHEST
TAIL = 8
CORES = 2


def exchange(value, **masks):
    axes = tuple(masks)
    sizes = [lax.axis_size(axis) for axis in axes]

    def flat(place):
        index = 0
        for size, at in zip(sizes, place):
            index = index * size + at
        return index

    pairs = [
        (flat(place), flat([at ^ mask for at, mask in zip(place, masks.values())]))
        for place in itertools.product(*map(range, sizes))
    ]
    return lax.ppermute(value, axes, pairs)


def halves(value):
    high = value.astype(jnp.bfloat16)
    return high, (value - high.astype(jnp.float32)).astype(jnp.bfloat16)


def dot(left, right, left_dim, right_dim):
    def one_pass(left_half, right_half):
        return lax.dot_general(
            left_half,
            right_half,
            (((left_dim,), (right_dim,)), ((), ())),
            preferred_element_type=jnp.float32,
        )

    cross = one_pass(left[0], right[1]) + one_pass(left[1], right[0])
    return one_pass(left[0], right[0]) + cross


def call(body, out_shapes, name, cost, operands, scratch=(), after=(), space=pltpu.VMEM, vmem=32):
    spaces = [space] * len(operands) + [pl.ANY] * len(after)
    count = len(operands)

    def without_after(*refs):
        body(*refs[:count], *refs[count + len(after) :])

    return pl.pallas_call(
        without_after,
        out_shape=[jax.ShapeDtypeStruct(shape, jnp.float32) for shape in out_shapes],
        in_specs=[pl.BlockSpec(memory_space=space) for space in spaces],
        out_specs=[pl.BlockSpec(memory_space=pltpu.VMEM) for _ in out_shapes],
        scratch_shapes=scratch,
        compiler_params=pltpu.CompilerParams(vmem_limit_bytes=vmem * 2**20),
        cost_estimate=pl.CostEstimate(flops=cost, bytes_accessed=2**20, transcendentals=0),
        name=name,
    )(*operands, *after)


def row_as_tail(row, width):
    rows = [row[:, at : at + width] for at in range(0, row.shape[1], width)]
    rows.append(jnp.zeros((TAIL - len(rows), width), row.dtype))
    return jnp.concatenate(rows, axis=0)


def tail_as_row(ref, start, count):
    return jnp.concatenate([ref[start + at : start + at + 1, :] for at in range(count)], axis=1)


def row_as_column(row, width):
    parts = []
    for at in range(0, row.shape[1], width):
        parts.append(jnp.broadcast_to(row[:, at : at + width], (width, width)).T)
    return jnp.concatenate(parts, axis=0)


def direct_plan_fits(mesh, queries, compact_keys):
    sizes = [mesh.shape[axis] for axis in ("page", "query", "head")]
    pages, query_devices, head_devices = sizes
    local_heads = queries.shape[0] // head_devices
    part_rows = queries.shape[1] // query_devices
    slot_rows = compact_keys.shape[1] // pages
    width = queries.shape[2]
    if any(size & (size - 1) for size in sizes) or pages < CORES or width % 128:
        return False
    if local_heads != CORES * query_devices:
        return False
    ranks = pages // CORES
    chunk = part_rows * query_devices // ranks
    return (
        part_rows * query_devices % ranks == 0
        and chunk % 128 == 0
        and part_rows % (8 * ranks) == 0
        and slot_rows % width == 0
        and part_rows % width == 0
        and max(slot_rows, part_rows) < TAIL * width
    )


def direct_per_device(
    queries, compact_keys, compact_values, slot_bias, targets, positions, assignment
):
    local_heads, part_rows, width = queries.shape
    slot_rows = compact_keys.shape[1]
    query_devices = lax.axis_size("query")
    head_devices = lax.axis_size("head")
    ranks = lax.axis_size("page") // CORES
    query_rows = part_rows * query_devices
    chunk, piece = query_rows // ranks, part_rows // ranks
    slot_total = local_heads * head_devices * slot_rows * lax.axis_size("page")
    entry_total = slot_total * width
    score_scale = 1.0 / math.sqrt(width)
    slots = CORES * slot_rows
    pos_rows = part_rows // width
    bias_rows = slot_rows // width
    packed_rows = 2 * slot_rows + TAIL
    packed_shapes = [(packed_rows, width)] * 2
    matmul_cost = 3 * 2 * slots * query_rows * width

    def places():
        page = lax.axis_index("page")
        return page // CORES, page % CORES, lax.axis_index("query")

    def pack_queries(head, rank, queries, targets, out):
        rows = pl.ds(pl.multiple_of(rank * piece, piece), piece)
        return [
            (queries.at[head], out.at[pl.ds(0, part_rows)]),
            (targets.at[head, rows], out.at[pl.ds(part_rows, piece)]),
        ]

    def pack_state(head, keys, values, out):
        return [
            (keys.at[head], out.at[pl.ds(0, slot_rows)]),
            (values.at[head], out.at[pl.ds(slot_rows, slot_rows)]),
        ]

    def start_all(copies, sems, first=0):
        copies = [
            pltpu.make_async_copy(source, target, sems.at[first + at])
            for at, (source, target) in enumerate(copies)
        ]
        for copy in copies:
            copy.start()
        return copies

    def position_tail(head, positions_ref):
        return row_as_tail(positions_ref[pl.ds(head, 1), :].astype(jnp.float32), width)

    def state_tail(head, page, bias_ref, assignment_ref):
        page_start = (assignment_ref[page] * PAGE_LEN).astype(jnp.float32)
        tail = row_as_tail(bias_ref[pl.ds(head, 1), :], width)
        return jnp.concatenate(
            [tail[: TAIL - 1], jnp.full((1, width), page_start, jnp.float32)], axis=0
        )

    def send_body(
        queries, keys, values, biases, targets, positions, assignment, state_out, *refs
    ):
        query_outs = refs[: query_devices - 1]
        bias_ref, positions_ref, assignment_ref, sems = refs[query_devices - 1 :]
        rank, core, me = places()
        heads = [CORES * (me ^ turn) + core for turn in range(1, query_devices)]
        mate_head = CORES * me + (core ^ 1)
        small = start_all(
            [(assignment, assignment_ref), (positions, positions_ref), (biases, bias_ref)], sems
        )
        copies = pack_state(mate_head, keys, values, state_out)
        for head, out in zip(heads, query_outs):
            copies += pack_queries(head, rank, queries, targets, out)
        copies = start_all(copies, sems, 3)
        for copy in small:
            copy.wait()
        state_out[2 * slot_rows :, :] = state_tail(
            mate_head, CORES * rank + core, bias_ref, assignment_ref
        )
        for head, out in zip(heads, query_outs):
            out[part_rows + piece :, :] = position_tail(head, positions_ref)
        for copy in copies:
            copy.wait()

    def own_body(
        queries, keys, values, biases, targets, positions, assignment, state_out, query_out, *refs
    ):
        bias_ref, positions_ref, assignment_ref, sems = refs
        rank, core, me = places()
        head = CORES * me + core
        small = start_all(
            [(assignment, assignment_ref), (positions, positions_ref), (biases, bias_ref)], sems
        )
        copies = pack_state(head, keys, values, state_out)
        copies += pack_queries(head, rank, queries, targets, query_out)
        copies = start_all(copies, sems, 3)
        for copy in small:
            copy.wait()
        state_out[2 * slot_rows :, :] = state_tail(
            head, CORES * rank + core, bias_ref, assignment_ref
        )
        query_out[part_rows + piece :, :] = position_tail(head, positions_ref)
        for copy in copies:
            copy.wait()

    state_shape, query_shape = (packed_rows, width), (part_rows + piece + TAIL, width)
    small_scratch = [
        pltpu.VMEM(slot_bias.shape, jnp.float32),
        pltpu.VMEM(positions.shape, jnp.int32),
        pltpu.SMEM(assignment.shape, jnp.int32),
    ]
    arguments = [
        queries, compact_keys, compact_values, slot_bias, targets, positions, assignment
    ]
    mate_state, *sent_queries = call(
        send_body,
        [state_shape] + [query_shape] * (query_devices - 1),
        "pack",
        2**20,
        arguments,
        small_scratch + [pltpu.SemaphoreType.DMA((3 + 2 * query_devices,))],
        space=pl.ANY,
        vmem=60,
    )
    own_state, own_queries = call(
        own_body,
        [state_shape, query_shape],
        "own",
        2**24,
        arguments,
        small_scratch + [pltpu.SemaphoreType.DMA((7,))],
        space=pl.ANY,
    )
    query_parts = [own_queries] + [
        exchange(sent_queries[turn - 1], query=turn) for turn in range(1, query_devices)
    ]
    states = [own_state, exchange(mate_state, page=1)]

    def in_columns(parts, axis):
        return jnp.concatenate(
            [
                lax.slice_in_dim(part, at * piece, (at + 1) * piece, axis=axis)
                for at in range(ranks)
                for part in parts
            ],
            axis=axis,
        )

    def read_queries(query_refs):
        return halves(in_columns([ref[:part_rows, :] for ref in query_refs], 0))

    def part_of(ref, at):
        return ref.at[pl.ds(at * packed_rows, packed_rows)]

    def parts_of(refs):
        return refs if len(refs) == CORES else [part_of(refs[0], at) for at in range(CORES)]

    def step_sizes(tile_refs):
        tile = jnp.sum(tile_refs[0][...], axis=0)
        sums = jnp.sum(tile, axis=1, keepdims=True)
        return (
            RATE_KEYS / jnp.sqrt(sums[0:1] / entry_total + EPSILON),
            RATE_VALUES / jnp.sqrt(sums[1:2] / entry_total + EPSILON),
            RATE_BIAS / jnp.sqrt(sums[2:3] / slot_total + EPSILON),
        )

    def updated(state_ref, grad_ref, sizes):
        key_end, value_end = slot_rows, 2 * slot_rows
        return (
            state_ref[:key_end, :] - sizes[0] * grad_ref[:key_end, :],
            state_ref[key_end:value_end, :] - sizes[1] * grad_ref[key_end:value_end, :],
            state_ref[value_end:, :] - sizes[2] * grad_ref[value_end:, :],
        )

    def forward(state_refs, query_refs, chunk_outs, weights_out, max_out, chunks):
        rank, _, _ = places()
        all_queries = read_queries(query_refs)
        position_row = in_columns(
            [tail_as_row(ref, part_rows + piece, pos_rows) for ref in query_refs], 1
        )
        all_scores, all_visible = [], []
        for at, ref in enumerate(state_refs):
            scores = dot(halves(ref[:slot_rows, :]), all_queries, 1, 1) * score_scale
            bias = row_as_column(tail_as_row(ref, 2 * slot_rows, bias_rows), width)
            scores = scores + jnp.concatenate([bias] * (query_rows // width), axis=1)
            page_start = ref[packed_rows - 1 : packed_rows, 0:1]
            visible = jnp.broadcast_to(position_row >= page_start, scores.shape)
            all_scores.append(jnp.where(visible, scores, MASKED))
            all_visible.append(visible)
        row_max = jnp.max(all_scores[0], axis=0, keepdims=True)
        for scores in all_scores[1:]:
            row_max = jnp.maximum(row_max, jnp.max(scores, axis=0, keepdims=True))
        row_total = jnp.zeros_like(row_max)
        row_sum = jnp.zeros((width, query_rows), jnp.float32)
        for at, ref in enumerate(state_refs):
            weights = jnp.where(all_visible[at], jnp.exp(all_scores[at] - row_max), 0.0)
            weights_out[at * slot_rows : (at + 1) * slot_rows, :] = weights
            row_total = row_total + jnp.sum(weights, axis=0, keepdims=True)
            values = halves(ref[slot_rows : 2 * slot_rows, :])
            row_sum = row_sum + dot(values, halves(weights), 0, 0)
        max_out[...] = jnp.broadcast_to(row_max, (TAIL, query_rows))
        tail = jnp.concatenate(
            [row_max, row_total, jnp.zeros((TAIL - 2, query_rows), jnp.float32)], axis=0
        )
        for at in range(ranks):
            columns = slice(at * chunk, (at + 1) * chunk)
            chunks[at, :width, :] = row_sum[:, columns]
            chunks[at, width:, :] = tail[:, columns]
        for turn in range(ranks):
            chunk_outs[turn][...] = chunks[rank ^ turn]

    chunk_shape = (width + TAIL, chunk)
    forward_shapes = [chunk_shape] * ranks + [(slots, query_rows), (TAIL, query_rows)]
    chunk_scratch = [pltpu.VMEM((ranks,) + chunk_shape, jnp.float32)]

    def first_body(*refs):
        state_refs, refs = refs[:2], refs[2:]
        query_refs, refs = refs[:query_devices], refs[query_devices:]
        chunk_outs, refs = refs[:ranks], refs[ranks:]
        forward(state_refs, query_refs, chunk_outs, *refs)

    def next_body(*refs):
        state_refs, refs = refs[:2], refs[2:]
        query_refs, refs = refs[:query_devices], refs[query_devices:]
        grad_refs, refs = refs[:2], refs[2:]
        tile_refs, refs = refs[: len(tiles)], refs[len(tiles) :]
        state_outs, refs = parts_of(refs[:1]), refs[1:]
        chunk_outs, refs = refs[:ranks], refs[ranks:]
        sizes = step_sizes(tile_refs)
        for at in range(2):
            keys, values, bias = updated(state_refs[at], grad_refs[at], sizes)
            state_outs[at][:slot_rows, :] = keys
            state_outs[at][slot_rows : 2 * slot_rows, :] = values
            state_outs[at][2 * slot_rows :, :] = bias
        forward(state_outs, query_refs, chunk_outs, *refs)

    def merge_body(*refs):
        query_refs, refs = refs[:query_devices], refs[query_devices:]
        chunk_refs, (merged_out,) = refs[:ranks], refs[ranks:]
        targets = jnp.concatenate(
            [ref[part_rows : part_rows + piece, :] for ref in query_refs], axis=0
        )
        row_max = chunk_refs[0][width : width + 1, :]
        for ref in chunk_refs[1:]:
            row_max = jnp.maximum(row_max, ref[width : width + 1, :])
        row_total = jnp.zeros_like(row_max)
        row_sum = jnp.zeros((width, chunk), jnp.float32)
        for ref in chunk_refs:
            factor = jnp.exp(ref[width : width + 1, :] - row_max)
            row_total = row_total + ref[width + 1 : width + 2, :] * factor
            row_sum = row_sum + ref[:width, :] * factor
        output = row_sum / row_total
        residual = output - targets.T
        row_delta = jnp.sum(residual * output, axis=0, keepdims=True)
        merged_out[:width, :] = residual
        merged_out[width:, :] = jnp.concatenate(
            [row_max, row_total, row_delta, jnp.zeros((TAIL - 3, chunk), jnp.float32)], axis=0
        )

    def backward_body(weights_ref, max_ref, *refs):
        state_refs, refs = parts_of(refs[: len(states)]), refs[len(states) :]
        query_refs, refs = refs[:query_devices], refs[query_devices:]
        merged_refs, refs = refs[:ranks], refs[ranks:]
        grad_outs, (squares_out, chunks) = refs[:2], refs[2:]
        rank, _, _ = places()
        for turn in range(ranks):
            chunks[rank ^ turn] = merged_refs[turn][...]
        joined = jnp.concatenate([chunks[at] for at in range(ranks)], axis=1)
        residual = joined[:width, :]
        row_max, row_total, row_delta = (
            joined[width + at : width + at + 1, :] for at in range(3)
        )
        all_queries = read_queries(query_refs)
        residual = halves(residual)
        factor = jnp.exp(max_ref[0:1, :] - row_max) / row_total
        ones = jnp.ones((TAIL, query_rows), jnp.bfloat16)
        ones = (ones, jnp.zeros_like(ones))
        squares = [jnp.zeros((1, width), jnp.float32)] * 3
        for at, ref in enumerate(state_refs):
            attention = weights_ref[at * slot_rows : (at + 1) * slot_rows, :] * factor
            grad_values = dot(halves(attention), residual, 1, 1)
            grad_probs = dot(halves(ref[slot_rows : 2 * slot_rows, :]), residual, 1, 0)
            grad_scores = halves(attention * (grad_probs - row_delta))
            grad_keys = dot(grad_scores, all_queries, 1, 0) * score_scale
            grad_bias = row_as_tail(dot(ones, grad_scores, 1, 1)[0:1, :], width)
            grad_outs[at][:slot_rows, :] = grad_keys
            grad_outs[at][slot_rows : 2 * slot_rows, :] = grad_values
            grad_outs[at][2 * slot_rows :, :] = grad_bias
            for which, grad in enumerate((grad_keys, grad_values, grad_bias)):
                squares[which] = squares[which] + jnp.sum(grad * grad, axis=0, keepdims=True)
        squares_out[...] = jnp.concatenate(
            squares + [jnp.zeros((TAIL - 3, width), jnp.float32)], axis=0
        )

    def mate_body(*refs):
        *state_refs, out_ref = refs
        for at, ref in enumerate(state_refs):
            out_ref[pl.ds(at * packed_rows, packed_rows), :] = part_of(ref, 1)[...]

    out_masks = list(itertools.product(range(query_devices), range(CORES)))

    def to_output(packs, mask):
        if mask == (0, 0):
            return packs[0]
        return exchange(packs[mask[1]], page=mask[1], query=mask[0])

    for repeat in range(STEPS):
        last = repeat == STEPS - 1
        if repeat == 0:
            *chunk_parts, weights, maxima = call(
                first_body,
                forward_shapes,
                "forward",
                2 * matmul_cost,
                states + query_parts,
                chunk_scratch,
            )
        else:
            new_state, *chunk_parts, weights, maxima = call(
                next_body,
                [(CORES * packed_rows, width)] + forward_shapes,
                "update_forward",
                2 * matmul_cost,
                states + query_parts + grads + tiles,
                chunk_scratch,
            )
            states = [new_state]
        arrived = {
            turn: exchange(chunk_parts[turn], page=CORES * turn)
            for turn in reversed(range(1, ranks))
        }
        if repeat:
            new_states = states + [
                exchange(states[0], query=turn) for turn in range(1, query_devices)
            ]
        (merged,) = call(
            merge_body,
            [chunk_shape],
            "merge",
            2**20,
            query_parts + chunk_parts[:1] + list(arrived.values()),
        )
        all_merged = [merged] + [
            exchange(merged, page=CORES * turn) for turn in range(1, ranks)
        ]
        if repeat:
            (for_mate,) = call(
                mate_body,
                [(query_devices * packed_rows, width)],
                "mate_parts",
                2**20,
                new_states,
                after=all_merged[1:],
            )
            from_mate = exchange(for_mate, page=1)
        own_grad, mate_grad, squares = call(
            backward_body,
            packed_shapes + [(TAIL, width)],
            "backward",
            3 * matmul_cost,
            [weights, maxima] + states + query_parts + all_merged,
            scratch=chunk_scratch,
        )
        grads = [own_grad, mate_grad]
        if last:
            all_grads = [to_output(grads, mask) for mask in out_masks]
        tiles = [lax.all_gather(squares, ("page", "query", "head"))]

    def last_body(*refs):
        state_refs, (mate_ref, *refs) = refs[:query_devices], refs[query_devices:]
        state_refs = [
            part_of(mate_ref, turn) if flip else part_of(state_refs[turn], 0)
            for turn, flip in out_masks
        ]
        grad_refs, refs = refs[:local_heads], refs[local_heads:]
        tile_refs, (keys_out, values_out, bias_out) = refs[: len(tiles)], refs[len(tiles) :]
        _, core, me = places()
        sizes = step_sizes(tile_refs)
        for at, (turn, flip) in enumerate(out_masks):
            keys, values, bias = updated(state_refs[at], grad_refs[at], sizes)
            head = CORES * (me ^ turn) + (core ^ flip)
            keys_out[head] = keys
            values_out[head] = values
            bias_row = jnp.concatenate([bias[row : row + 1] for row in range(bias_rows)], axis=1)
            bias_out[pl.ds(head, 1), :] = bias_row

    return tuple(
        call(
            last_body,
            [compact_keys.shape, compact_values.shape, slot_bias.shape],
            "last_update",
            2**20,
            new_states + [from_mate] + all_grads + tiles,
        )
    )


def from_partner(value, axis, stride):
    mask = 2**stride
    pairs = [(source, source ^ mask) for source in range(lax.axis_size(axis))]
    return lax.ppermute(value, axis, pairs)


def squared_sums(grad_keys, grad_values, grad_bias):
    return jnp.stack(
        [
            jnp.sum(grad_keys * grad_keys),
            jnp.sum(grad_values * grad_values),
            jnp.sum(grad_bias * grad_bias),
        ]
    )


def apply_update(states, grads, totals, entry_count, slot_total):
    key_state, value_state, bias_state = states
    grad_keys, grad_values, grad_bias = grads
    rms_keys = jnp.sqrt(totals[0] / entry_count + EPSILON)
    rms_values = jnp.sqrt(totals[1] / entry_count + EPSILON)
    rms_bias = jnp.sqrt(totals[2] / slot_total + EPSILON)
    return (
        key_state - RATE_KEYS * grad_keys / rms_keys,
        value_state - RATE_VALUES * grad_values / rms_values,
        bias_state - RATE_BIAS * grad_bias / rms_bias,
    )


def local_gradients(queries, targets, visible, compact_keys, compact_values, slot_bias):
    score_scale = 1.0 / math.sqrt(queries.shape[2])
    scores = jnp.einsum("hqd,hsd->hqs", queries, compact_keys, precision=HIGHEST) * score_scale
    scores = jnp.where(visible, scores + slot_bias[:, None, :], MASKED)
    local_max = jnp.max(scores, axis=2)
    row_max = lax.pmax(local_max, "page")
    weights = jnp.where(visible, jnp.exp(scores - row_max[:, :, None]), 0.0)
    local_sum = jnp.einsum("hqs,hsd->hqd", weights, compact_values, precision=HIGHEST)
    row_total, row_sum = lax.psum((jnp.sum(weights, axis=2), local_sum), "page")
    attention = weights / row_total[:, :, None]
    output = row_sum / row_total[:, :, None]
    residual = output - targets
    grad_values = jnp.einsum("hqs,hqd->hsd", attention, residual, precision=HIGHEST)
    row_delta = jnp.sum(residual * output, axis=2)
    grad_probs = jnp.einsum("hqd,hsd->hqs", residual, compact_values, precision=HIGHEST)
    grad_scores = attention * (grad_probs - row_delta[:, :, None])
    grad_bias = jnp.sum(grad_scores, axis=1)
    grad_keys = jnp.einsum("hqs,hqd->hsd", grad_scores, queries, precision=HIGHEST) * score_scale
    return (grad_keys, grad_values, grad_bias)


def per_device(queries, compact_keys, compact_values, slot_bias, targets, positions, assignment):
    page_number = assignment[lax.axis_index("page")]
    local_heads = compact_keys.shape[0]
    slot_total = local_heads * lax.axis_size("head") * compact_keys.shape[1] * lax.axis_size("page")
    entry_count = slot_total * compact_keys.shape[2]
    query_count = lax.axis_size("query")
    heads_kept = max(local_heads // query_count, 1)
    query_parts = max(query_count // local_heads, 1)
    part_rows = queries.shape[1] // query_parts

    def split_items(array):
        width = array.shape[2]
        array = array.reshape(local_heads // heads_kept, heads_kept, query_parts, part_rows, width)
        array = jnp.transpose(array, (0, 2, 1, 3, 4))
        return array.reshape(query_count, heads_kept, part_rows, width)

    def join_items(array):
        width = array.shape[3]
        array = jnp.transpose(array, (1, 0, 2, 3))
        return array.reshape(heads_kept, query_count * part_rows, width)

    position_column = positions.astype(jnp.float32)[:, :, None]
    got_queries, got_targets, got_positions = (
        lax.all_to_all(split_items(queries), "query", split_axis=0, concat_axis=0, tiled=True),
        lax.all_to_all(split_items(targets), "query", split_axis=0, concat_axis=0, tiled=True),
        lax.all_to_all(
            split_items(position_column), "query", split_axis=0, concat_axis=0, tiled=True
        ),
    )
    group_queries = join_items(got_queries)
    group_targets = join_items(got_targets)
    group_positions = join_items(got_positions)[:, :, 0]
    visible = (page_number.astype(jnp.float32) <= jnp.floor(group_positions / PAGE_LEN))[:, :, None]
    query_index = lax.axis_index("query")
    first_head = query_index // query_parts * heads_kept
    key_state = lax.dynamic_slice_in_dim(compact_keys, first_head, heads_kept, 0)
    value_state = lax.dynamic_slice_in_dim(compact_values, first_head, heads_kept, 0)
    bias_state = lax.dynamic_slice_in_dim(slot_bias, first_head, heads_kept, 0)
    counted = (query_index % query_parts == 0).astype(jnp.float32)
    for repeat in range(STEPS):
        grads = local_gradients(
            group_queries, group_targets, visible, key_state, value_state, bias_state
        )
        for bit in range(query_parts.bit_length() - 1):
            partner = from_partner((grads[0], grads[1], grads[2]), "query", bit)
            grads = (grads[0] + partner[0], grads[1] + partner[1], grads[2] + partner[2])
        totals = lax.psum(
            squared_sums(grads[0], grads[1], grads[2]) * counted, ("page", "query", "head")
        )
        key_state, value_state, bias_state = apply_update(
            (key_state, value_state, bias_state), grads, totals, entry_count, slot_total
        )
    all_keys, all_values, all_bias = (
        lax.all_gather(key_state, "query", axis=0, tiled=True),
        lax.all_gather(value_state, "query", axis=0, tiled=True),
        lax.all_gather(bias_state, "query", axis=0, tiled=True),
    )
    slot_rows = compact_keys.shape[1]
    head_width = compact_keys.shape[2]
    all_keys = all_keys.reshape(
        local_heads // heads_kept, query_parts, heads_kept, slot_rows, head_width
    )[:, 0]
    all_values = all_values.reshape(
        local_heads // heads_kept, query_parts, heads_kept, slot_rows, head_width
    )[:, 0]
    all_bias = all_bias.reshape(local_heads // heads_kept, query_parts, heads_kept, slot_rows)[:, 0]
    return (
        all_keys.reshape(local_heads, slot_rows, head_width),
        all_values.reshape(local_heads, slot_rows, head_width),
        all_bias.reshape(local_heads, slot_rows),
    )


def solution(mesh):
    placed = (
        P("head", "query", None),
        P("head", "page", None),
        P("head", "page", None),
        P("head", "page"),
        P("head", "query", None),
        P("head", "query"),
        P(),
    )

    def program(*args):
        plan = direct_per_device if direct_plan_fits(mesh, args[0], args[1]) else per_device
        return jax.shard_map(
            plan,
            mesh=mesh,
            in_specs=placed,
            out_specs=(P("head", "page", None), P("head", "page", None), P("head", "page")),
            check_vma=False,
        )(*args)

    return program
```

```python
import itertools
import math

import jax
import jax.numpy as jnp
from jax import lax
from jax.experimental import pallas as pl
from jax.experimental.pallas import tpu as pltpu
from jax.sharding import PartitionSpec as P

STEPS = 2
PAGE_LEN = 32768


MASKED = -1e30
EPSILON = 1e-06
RATE_KEYS = 0.05
RATE_VALUES = 0.05
RATE_BIAS = 0.2
HIGHEST = lax.Precision.HIGHEST
TAIL = 8
CORES = 2


def exchange(value, **masks):
    axes = tuple(masks)
    sizes = [lax.axis_size(axis) for axis in axes]

    def flat(place):
        index = 0
        for size, at in zip(sizes, place):
            index = index * size + at
        return index

    pairs = [
        (flat(place), flat([at ^ mask for at, mask in zip(place, masks.values())]))
        for place in itertools.product(*map(range, sizes))
    ]
    return lax.ppermute(value, axes, pairs)


def halves(value):
    high = value.astype(jnp.bfloat16)
    return high, (value - high.astype(jnp.float32)).astype(jnp.bfloat16)


def dot(left, right, left_dim, right_dim):
    def one_pass(left_half, right_half):
        return lax.dot_general(
            left_half,
            right_half,
            (((left_dim,), (right_dim,)), ((), ())),
            preferred_element_type=jnp.float32,
        )

    cross = one_pass(left[0], right[1]) + one_pass(left[1], right[0])
    return one_pass(left[0], right[0]) + cross


def call(body, out_shapes, name, cost, operands, scratch=(), after=(), space=pltpu.VMEM, vmem=32):
    spaces = [space] * len(operands) + [pl.ANY] * len(after)
    count = len(operands)

    def without_after(*refs):
        body(*refs[:count], *refs[count + len(after) :])

    return pl.pallas_call(
        without_after,
        out_shape=[jax.ShapeDtypeStruct(shape, jnp.float32) for shape in out_shapes],
        in_specs=[pl.BlockSpec(memory_space=space) for space in spaces],
        out_specs=[pl.BlockSpec(memory_space=pltpu.VMEM) for _ in out_shapes],
        scratch_shapes=scratch,
        compiler_params=pltpu.CompilerParams(vmem_limit_bytes=vmem * 2**20),
        cost_estimate=pl.CostEstimate(flops=cost, bytes_accessed=2**20, transcendentals=0),
        name=name,
    )(*operands, *after)


def row_as_tail(row, width):
    rows = [row[:, at : at + width] for at in range(0, row.shape[1], width)]
    rows.append(jnp.zeros((TAIL - len(rows), width), row.dtype))
    return jnp.concatenate(rows, axis=0)


def tail_as_row(ref, start, count):
    return jnp.concatenate([ref[start + at : start + at + 1, :] for at in range(count)], axis=1)


def row_as_column(row, width):
    parts = []
    for at in range(0, row.shape[1], width):
        parts.append(jnp.broadcast_to(row[:, at : at + width], (width, width)).T)
    return jnp.concatenate(parts, axis=0)


def direct_plan_fits(mesh, queries, compact_keys):
    sizes = [mesh.shape[axis] for axis in ("page", "query", "head")]
    pages, query_devices, head_devices = sizes
    local_heads = queries.shape[0] // head_devices
    part_rows = queries.shape[1] // query_devices
    slot_rows = compact_keys.shape[1] // pages
    width = queries.shape[2]
    if any(size & (size - 1) for size in sizes) or pages < CORES or width % 128:
        return False
    if local_heads != CORES * query_devices:
        return False
    ranks = pages // CORES
    chunk = part_rows * query_devices // ranks
    return (
        part_rows * query_devices % ranks == 0
        and chunk % 128 == 0
        and part_rows % (8 * ranks) == 0
        and (part_rows // ranks % 128 == 0 or 1024 % (part_rows // ranks * 8) == 0)
        and slot_rows % width == 0
        and part_rows % width == 0
        and max(slot_rows, part_rows) < TAIL * width
    )


def direct_per_device(
    queries, compact_keys, compact_values, slot_bias, targets, positions, assignment
):
    local_heads, part_rows, width = queries.shape
    slot_rows = compact_keys.shape[1]
    query_devices = lax.axis_size("query")
    head_devices = lax.axis_size("head")
    ranks = lax.axis_size("page") // CORES
    query_rows = part_rows * query_devices
    chunk, piece = query_rows // ranks, part_rows // ranks
    slot_total = local_heads * head_devices * slot_rows * lax.axis_size("page")
    entry_total = slot_total * width
    score_scale = 1.0 / math.sqrt(width)
    slots = CORES * slot_rows
    devices = ranks * CORES * query_devices * head_devices
    pos_rows = part_rows // width
    bias_rows = slot_rows // width
    packed_rows = 2 * slot_rows + TAIL
    packed_shapes = [(packed_rows, width)] * CORES
    matmul_cost = 3 * 2 * slots * query_rows * width

    def places():
        page = lax.axis_index("page")
        return page // CORES, page % CORES, lax.axis_index("query")

    def pack_queries(head, rank, queries, targets, out):
        rows = pl.ds(pl.multiple_of(rank * piece, piece), piece)
        return [
            (queries.at[head], out.at[pl.ds(0, part_rows)]),
            (targets.at[head, rows], out.at[pl.ds(part_rows, piece)]),
        ]

    def pack_state(head, keys, values, out):
        return [
            (keys.at[head], out.at[pl.ds(0, slot_rows)]),
            (values.at[head], out.at[pl.ds(slot_rows, slot_rows)]),
        ]

    def start_all(copies, sems, first=0):
        copies = [
            pltpu.make_async_copy(source, target, sems.at[first + at])
            for at, (source, target) in enumerate(copies)
        ]
        for copy in copies:
            copy.start()
        return copies

    def position_tail(head, positions_ref):
        return row_as_tail(positions_ref[pl.ds(head, 1), :].astype(jnp.float32), width)

    def state_tail(head, page, bias_ref, assignment_ref):
        page_start = (assignment_ref[page] * PAGE_LEN).astype(jnp.float32)
        tail = row_as_tail(bias_ref[pl.ds(head, 1), :], width)
        return jnp.concatenate(
            [tail[: TAIL - 1], jnp.full((1, width), page_start, jnp.float32)], axis=0
        )

    def send_body(
        queries, keys, values, biases, targets, positions, assignment, state_out, *refs
    ):
        query_outs = refs[: query_devices - 1]
        bias_ref, positions_ref, assignment_ref, sems = refs[query_devices - 1 :]
        rank, core, me = places()
        heads = [CORES * (me ^ turn) + core for turn in range(1, query_devices)]
        mate_head = CORES * me + (core ^ 1)
        small = start_all(
            [(assignment, assignment_ref), (positions, positions_ref), (biases, bias_ref)], sems
        )
        copies = pack_state(mate_head, keys, values, state_out)
        for head, out in zip(heads, query_outs):
            copies += pack_queries(head, rank, queries, targets, out)
        copies = start_all(copies, sems, 3)
        for copy in small:
            copy.wait()
        state_out[2 * slot_rows :, :] = state_tail(
            mate_head, CORES * rank + core, bias_ref, assignment_ref
        )
        for head, out in zip(heads, query_outs):
            out[part_rows + piece :, :] = position_tail(head, positions_ref)
        for copy in copies:
            copy.wait()

    def own_body(
        queries, keys, values, biases, targets, positions, assignment, state_out, query_out, *refs
    ):
        bias_ref, positions_ref, assignment_ref, sems = refs
        rank, core, me = places()
        head = CORES * me + core
        small = start_all(
            [(assignment, assignment_ref), (positions, positions_ref), (biases, bias_ref)], sems
        )
        copies = pack_state(head, keys, values, state_out)
        copies += pack_queries(head, rank, queries, targets, query_out)
        copies = start_all(copies, sems, 3)
        for copy in small:
            copy.wait()
        state_out[2 * slot_rows :, :] = state_tail(
            head, CORES * rank + core, bias_ref, assignment_ref
        )
        query_out[part_rows + piece :, :] = position_tail(head, positions_ref)
        for copy in copies:
            copy.wait()

    state_shape, query_shape = (packed_rows, width), (part_rows + piece + TAIL, width)
    small_scratch = [
        pltpu.VMEM(slot_bias.shape, jnp.float32),
        pltpu.VMEM(positions.shape, jnp.int32),
        pltpu.SMEM(assignment.shape, jnp.int32),
    ]
    arguments = [
        queries, compact_keys, compact_values, slot_bias, targets, positions, assignment
    ]
    mate_state, *sent_queries = call(
        send_body,
        [state_shape] + [query_shape] * (query_devices - 1),
        "pack",
        2**20,
        arguments,
        small_scratch + [pltpu.SemaphoreType.DMA((3 + 2 * query_devices,))],
        space=pl.ANY,
        vmem=60,
    )
    own_state, own_queries = call(
        own_body,
        [state_shape, query_shape],
        "own",
        2**24,
        arguments,
        small_scratch + [pltpu.SemaphoreType.DMA((7,))],
        space=pl.ANY,
    )
    query_parts = [own_queries] + [
        exchange(sent_queries[turn - 1], query=turn) for turn in range(1, query_devices)
    ]
    states = [own_state, exchange(mate_state, page=1)]

    def part_of(ref, at):
        return ref.at[pl.ds(at * packed_rows, packed_rows)]

    def parts_of(refs):
        return refs if len(refs) == CORES else [part_of(refs[0], at) for at in range(CORES)]

    def step_sizes(tile_refs):
        tile = jnp.sum(tile_refs[0][...], axis=0)
        sums = jnp.sum(tile, axis=1, keepdims=True)
        return (
            RATE_KEYS / jnp.sqrt(sums[0:1] / entry_total + EPSILON),
            RATE_VALUES / jnp.sqrt(sums[1:2] / entry_total + EPSILON),
            RATE_BIAS / jnp.sqrt(sums[2:3] / slot_total + EPSILON),
        )

    def updated(state_ref, grad_ref, sizes):
        key_end, value_end = slot_rows, 2 * slot_rows
        return (
            state_ref[:key_end, :] - sizes[0] * grad_ref[:key_end, :],
            state_ref[key_end:value_end, :] - sizes[1] * grad_ref[key_end:value_end, :],
            state_ref[value_end:, :] - sizes[2] * grad_ref[value_end:, :],
        )

    fold = max(1, 128 // piece)
    folded, columns = width // fold, fold * piece
    piece_shape = (folded + TAIL, columns)
    piece_scratch = [pltpu.VMEM((ranks,) + piece_shape, jnp.float32)]

    def fold_rows(value):
        groups = [value[at * folded : (at + 1) * folded, :] for at in range(fold)]
        return jnp.concatenate(groups, axis=1)

    def unfold_rows(value):
        groups = [value[:, at * piece : (at + 1) * piece] for at in range(fold)]
        return jnp.concatenate(groups, axis=0)

    def rows_tail(rows):
        empty = jnp.zeros((TAIL - len(rows), columns), jnp.float32)
        return jnp.concatenate(rows + [empty], axis=0)

    def forward(state_refs, query_ref, piece_outs, weights_out, max_out, pieces):
        rank, _, _ = places()
        queries = halves(query_ref[:part_rows, :])
        position_row = tail_as_row(query_ref, part_rows + piece, pos_rows)
        all_scores, all_visible = [], []
        for ref in state_refs:
            scores = dot(halves(ref[:slot_rows, :]), queries, 1, 1) * score_scale
            bias = row_as_column(tail_as_row(ref, 2 * slot_rows, bias_rows), width)
            scores = scores + jnp.concatenate([bias] * (part_rows // width), axis=1)
            page_start = ref[packed_rows - 1 : packed_rows, 0:1]
            visible = jnp.broadcast_to(position_row >= page_start, scores.shape)
            all_scores.append(jnp.where(visible, scores, MASKED))
            all_visible.append(visible)
        row_max = jnp.max(all_scores[0], axis=0, keepdims=True)
        for scores in all_scores[1:]:
            row_max = jnp.maximum(row_max, jnp.max(scores, axis=0, keepdims=True))
        row_total = jnp.zeros_like(row_max)
        row_sum = jnp.zeros((width, part_rows), jnp.float32)
        for at, ref in enumerate(state_refs):
            weights = jnp.where(all_visible[at], jnp.exp(all_scores[at] - row_max), 0.0)
            weights_out[at * slot_rows : (at + 1) * slot_rows, :] = weights
            row_total = row_total + jnp.sum(weights, axis=0, keepdims=True)
            values = halves(ref[slot_rows : 2 * slot_rows, :])
            row_sum = row_sum + dot(values, halves(weights), 0, 0)
        max_out[...] = jnp.broadcast_to(row_max, (TAIL, part_rows))
        for at in range(ranks):
            own = slice(at * piece, (at + 1) * piece)
            pieces[at, :folded, :] = fold_rows(row_sum[:, own])
            pieces[at, folded:, :] = rows_tail(
                [jnp.concatenate([row[:, own]] * fold, axis=1) for row in (row_max, row_total)]
            )
        for turn in range(ranks):
            piece_outs[turn][...] = pieces[rank ^ turn]

    forward_shapes = [piece_shape] * ranks + [(slots, part_rows), (TAIL, part_rows)]

    def forward_body(*refs):
        state_refs, refs = parts_of(refs[: len(states)]), refs[len(states) :]
        query_ref, *refs = refs
        forward(state_refs, query_ref, refs[:ranks], *refs[ranks:])

    def update_body(*refs):
        state_refs, (query_ref, *refs) = refs[:CORES], refs[CORES:]
        grad_refs, refs = refs[:CORES], refs[CORES:]
        tile_refs, refs = refs[: len(tiles)], refs[len(tiles) :]
        state_outs, refs = parts_of(refs[:1]), refs[1:]
        sizes = step_sizes(tile_refs)
        for state_ref, grad_ref, out in zip(state_refs, grad_refs, state_outs):
            keys, values, bias = updated(state_ref, grad_ref, sizes)
            out[:slot_rows, :] = keys
            out[slot_rows : 2 * slot_rows, :] = values
            out[2 * slot_rows :, :] = bias
        forward(state_outs, query_ref, refs[:ranks], *refs[ranks:])

    def merge_body(query_ref, *refs):
        piece_refs, (merged_out,) = refs[:ranks], refs[ranks:]
        targets = fold_rows(query_ref[part_rows : part_rows + piece, :].T)
        row_max = piece_refs[0][folded : folded + 1, :]
        for ref in piece_refs[1:]:
            row_max = jnp.maximum(row_max, ref[folded : folded + 1, :])
        row_total = jnp.zeros_like(row_max)
        row_sum = jnp.zeros((folded, columns), jnp.float32)
        for ref in piece_refs:
            factor = jnp.exp(ref[folded : folded + 1, :] - row_max)
            row_total = row_total + ref[folded + 1 : folded + 2, :] * factor
            row_sum = row_sum + ref[:folded, :] * factor
        output = row_sum / row_total
        residual = output - targets
        row_delta = jnp.sum(residual * output, axis=0, keepdims=True)
        row_delta = sum(row_delta[:, at * piece : (at + 1) * piece] for at in range(fold))
        merged_out[:folded, :] = residual
        merged_out[folded:, :] = rows_tail(
            [row_max, row_total, jnp.concatenate([row_delta] * fold, axis=1)]
        )

    def backward_of(part):
        def body(weights_ref, max_ref, *refs):
            state_refs, refs = parts_of(refs[: len(states)]), refs[len(states) :]
            query_ref, *refs = refs
            merged_refs, refs = refs[:ranks], refs[ranks:]
            before_refs, refs = (refs[:CORES], refs[CORES:]) if part else ([], refs)
            grad_outs, refs = refs[:CORES], refs[CORES:]
            *squares_out, pieces = refs
            rank, _, _ = places()
            for turn, ref in enumerate(merged_refs):
                pieces[rank ^ turn] = ref[...]
            residual = halves(
                jnp.concatenate([unfold_rows(pieces[at, :folded, :]) for at in range(ranks)], 1)
            )
            row_max, row_total, row_delta = (
                jnp.concatenate(
                    [pieces[at, folded + row : folded + row + 1, :piece] for at in range(ranks)], 1
                )
                for row in range(3)
            )
            queries = halves(query_ref[:part_rows, :])
            factor = jnp.exp(max_ref[0:1, :] - row_max) / row_total
            ones = jnp.ones((TAIL, part_rows), jnp.bfloat16)
            ones = (ones, jnp.zeros_like(ones))
            squares = [jnp.zeros((1, width), jnp.float32)] * 3
            for at, ref in enumerate(state_refs):
                attention = weights_ref[at * slot_rows : (at + 1) * slot_rows, :] * factor
                grad_values = dot(halves(attention), residual, 1, 1)
                grad_probs = dot(halves(ref[slot_rows : 2 * slot_rows, :]), residual, 1, 0)
                grad_scores = halves(attention * (grad_probs - row_delta))
                grad_keys = dot(grad_scores, queries, 1, 0) * score_scale
                grad_bias = row_as_tail(dot(ones, grad_scores, 1, 1)[0:1, :], width)
                first, last = 0, 0
                for which, grad in enumerate((grad_keys, grad_values, grad_bias)):
                    first, last = last, last + grad.shape[0]
                    if part:
                        grad = grad + before_refs[at][first:last, :]
                    grad_outs[at][first:last, :] = grad
                    squares[which] = squares[which] + jnp.sum(
                        grad * grad, axis=0, keepdims=True
                    )
            if squares_out:
                tile = jnp.concatenate(
                    squares + [jnp.zeros((TAIL - 3, width), jnp.float32)], axis=0
                )
                for at in range(devices):
                    squares_out[0][at] = tile

        return body

    def mate_body(*refs):
        *state_refs, out_ref = refs
        for at, ref in enumerate(state_refs):
            out_ref[pl.ds(at * packed_rows, packed_rows), :] = part_of(ref, 1)[...]

    out_masks = list(itertools.product(range(query_devices), range(CORES)))

    def to_output(packs, mask):
        if mask == (0, 0):
            return packs[0]
        return exchange(packs[mask[1]], page=mask[1], query=mask[0])

    for repeat in range(STEPS):
        last = repeat == STEPS - 1
        part_sums, all_weights = [], []
        for part, query_part in enumerate(query_parts):
            if repeat and part == 0:
                new_state, *outs = call(
                    update_body,
                    [(CORES * packed_rows, width)] + forward_shapes,
                    "update_forward",
                    2 * matmul_cost // query_devices,
                    states + [query_part] + grads + tiles,
                    piece_scratch,
                )
                states = [new_state]
            else:
                outs = call(
                    forward_body,
                    forward_shapes,
                    "forward",
                    2 * matmul_cost // query_devices,
                    states + [query_part],
                    piece_scratch,
                )
            part_sums.append(
                [
                    exchange(outs[turn], page=CORES * turn) if turn else outs[0]
                    for turn in range(ranks)
                ]
            )
            all_weights.append(list(outs[ranks:]))
        if repeat:
            new_states = states + [
                exchange(states[0], query=turn) for turn in range(1, query_devices)
            ]
        all_merged = []
        for query_part, sums in zip(query_parts, part_sums):
            before = [parts[0] for parts in all_merged[-1:]]
            (merged,) = call(
                merge_body, [piece_shape], "merge", 2**20, [query_part] + sums, after=before
            )
            all_merged.append(
                [
                    exchange(merged, page=CORES * turn) if turn else merged
                    for turn in range(ranks)
                ]
            )
        grads = []
        for part, query_part in enumerate(query_parts):
            ends = part == query_devices - 1
            *grads, squares = list(
                call(
                    backward_of(part),
                    packed_shapes + [(devices, TAIL, width)] * ends,
                    "backward",
                    3 * matmul_cost // query_devices,
                    all_weights[part] + states + [query_part] + all_merged[part] + grads,
                    scratch=piece_scratch,
                )
            ) + [None] * (not ends)
            if repeat and part == 0:
                (for_mate,) = call(
                    mate_body,
                    [(query_devices * packed_rows, width)],
                    "mate_parts",
                    2**20,
                    new_states,
                    after=grads[:1],
                )
                from_mate = exchange(for_mate, page=1)
        if last:
            all_grads = [to_output(grads, mask) for mask in out_masks]
        tiles = [
            lax.all_to_all(
                squares, ("page", "query", "head"), split_axis=0, concat_axis=0, tiled=True
            )
        ]

    def last_body(*refs):
        state_refs, (mate_ref, *refs) = refs[:query_devices], refs[query_devices:]
        state_refs = [
            part_of(mate_ref, turn) if flip else part_of(state_refs[turn], 0)
            for turn, flip in out_masks
        ]
        grad_refs, refs = refs[:local_heads], refs[local_heads:]
        tile_refs, (keys_out, values_out, bias_out) = refs[: len(tiles)], refs[len(tiles) :]
        _, core, me = places()
        sizes = step_sizes(tile_refs)
        for at, (turn, flip) in enumerate(out_masks):
            keys, values, bias = updated(state_refs[at], grad_refs[at], sizes)
            head = CORES * (me ^ turn) + (core ^ flip)
            keys_out[head] = keys
            values_out[head] = values
            bias_row = jnp.concatenate([bias[row : row + 1] for row in range(bias_rows)], axis=1)
            bias_out[pl.ds(head, 1), :] = bias_row

    return tuple(
        call(
            last_body,
            [compact_keys.shape, compact_values.shape, slot_bias.shape],
            "last_update",
            2**20,
            new_states + [from_mate] + all_grads + tiles,
        )
    )


def from_partner(value, axis, stride):
    mask = 2**stride
    pairs = [(source, source ^ mask) for source in range(lax.axis_size(axis))]
    return lax.ppermute(value, axis, pairs)


def squared_sums(grad_keys, grad_values, grad_bias):
    return jnp.stack(
        [
            jnp.sum(grad_keys * grad_keys),
            jnp.sum(grad_values * grad_values),
            jnp.sum(grad_bias * grad_bias),
        ]
    )


def apply_update(states, grads, totals, entry_count, slot_total):
    key_state, value_state, bias_state = states
    grad_keys, grad_values, grad_bias = grads
    rms_keys = jnp.sqrt(totals[0] / entry_count + EPSILON)
    rms_values = jnp.sqrt(totals[1] / entry_count + EPSILON)
    rms_bias = jnp.sqrt(totals[2] / slot_total + EPSILON)
    return (
        key_state - RATE_KEYS * grad_keys / rms_keys,
        value_state - RATE_VALUES * grad_values / rms_values,
        bias_state - RATE_BIAS * grad_bias / rms_bias,
    )


def local_gradients(queries, targets, visible, compact_keys, compact_values, slot_bias):
    score_scale = 1.0 / math.sqrt(queries.shape[2])
    scores = jnp.einsum("hqd,hsd->hqs", queries, compact_keys, precision=HIGHEST) * score_scale
    scores = jnp.where(visible, scores + slot_bias[:, None, :], MASKED)
    local_max = jnp.max(scores, axis=2)
    row_max = lax.pmax(local_max, "page")
    weights = jnp.where(visible, jnp.exp(scores - row_max[:, :, None]), 0.0)
    local_sum = jnp.einsum("hqs,hsd->hqd", weights, compact_values, precision=HIGHEST)
    row_total, row_sum = lax.psum((jnp.sum(weights, axis=2), local_sum), "page")
    attention = weights / row_total[:, :, None]
    output = row_sum / row_total[:, :, None]
    residual = output - targets
    grad_values = jnp.einsum("hqs,hqd->hsd", attention, residual, precision=HIGHEST)
    row_delta = jnp.sum(residual * output, axis=2)
    grad_probs = jnp.einsum("hqd,hsd->hqs", residual, compact_values, precision=HIGHEST)
    grad_scores = attention * (grad_probs - row_delta[:, :, None])
    grad_bias = jnp.sum(grad_scores, axis=1)
    grad_keys = jnp.einsum("hqs,hqd->hsd", grad_scores, queries, precision=HIGHEST) * score_scale
    return (grad_keys, grad_values, grad_bias)


def per_device(queries, compact_keys, compact_values, slot_bias, targets, positions, assignment):
    page_number = assignment[lax.axis_index("page")]
    local_heads = compact_keys.shape[0]
    slot_total = local_heads * lax.axis_size("head") * compact_keys.shape[1] * lax.axis_size("page")
    entry_count = slot_total * compact_keys.shape[2]
    query_count = lax.axis_size("query")
    heads_kept = max(local_heads // query_count, 1)
    query_parts = max(query_count // local_heads, 1)
    part_rows = queries.shape[1] // query_parts

    def split_items(array):
        width = array.shape[2]
        array = array.reshape(local_heads // heads_kept, heads_kept, query_parts, part_rows, width)
        array = jnp.transpose(array, (0, 2, 1, 3, 4))
        return array.reshape(query_count, heads_kept, part_rows, width)

    def join_items(array):
        width = array.shape[3]
        array = jnp.transpose(array, (1, 0, 2, 3))
        return array.reshape(heads_kept, query_count * part_rows, width)

    position_column = positions.astype(jnp.float32)[:, :, None]
    got_queries, got_targets, got_positions = (
        lax.all_to_all(split_items(queries), "query", split_axis=0, concat_axis=0, tiled=True),
        lax.all_to_all(split_items(targets), "query", split_axis=0, concat_axis=0, tiled=True),
        lax.all_to_all(
            split_items(position_column), "query", split_axis=0, concat_axis=0, tiled=True
        ),
    )
    group_queries = join_items(got_queries)
    group_targets = join_items(got_targets)
    group_positions = join_items(got_positions)[:, :, 0]
    visible = (page_number.astype(jnp.float32) <= jnp.floor(group_positions / PAGE_LEN))[:, :, None]
    query_index = lax.axis_index("query")
    first_head = query_index // query_parts * heads_kept
    key_state = lax.dynamic_slice_in_dim(compact_keys, first_head, heads_kept, 0)
    value_state = lax.dynamic_slice_in_dim(compact_values, first_head, heads_kept, 0)
    bias_state = lax.dynamic_slice_in_dim(slot_bias, first_head, heads_kept, 0)
    counted = (query_index % query_parts == 0).astype(jnp.float32)
    for repeat in range(STEPS):
        grads = local_gradients(
            group_queries, group_targets, visible, key_state, value_state, bias_state
        )
        for bit in range(query_parts.bit_length() - 1):
            partner = from_partner((grads[0], grads[1], grads[2]), "query", bit)
            grads = (grads[0] + partner[0], grads[1] + partner[1], grads[2] + partner[2])
        totals = lax.psum(
            squared_sums(grads[0], grads[1], grads[2]) * counted, ("page", "query", "head")
        )
        key_state, value_state, bias_state = apply_update(
            (key_state, value_state, bias_state), grads, totals, entry_count, slot_total
        )
    all_keys, all_values, all_bias = (
        lax.all_gather(key_state, "query", axis=0, tiled=True),
        lax.all_gather(value_state, "query", axis=0, tiled=True),
        lax.all_gather(bias_state, "query", axis=0, tiled=True),
    )
    slot_rows = compact_keys.shape[1]
    head_width = compact_keys.shape[2]
    all_keys = all_keys.reshape(
        local_heads // heads_kept, query_parts, heads_kept, slot_rows, head_width
    )[:, 0]
    all_values = all_values.reshape(
        local_heads // heads_kept, query_parts, heads_kept, slot_rows, head_width
    )[:, 0]
    all_bias = all_bias.reshape(local_heads // heads_kept, query_parts, heads_kept, slot_rows)[:, 0]
    return (
        all_keys.reshape(local_heads, slot_rows, head_width),
        all_values.reshape(local_heads, slot_rows, head_width),
        all_bias.reshape(local_heads, slot_rows),
    )


def solution(mesh):
    placed = (
        P("head", "query", None),
        P("head", "page", None),
        P("head", "page", None),
        P("head", "page"),
        P("head", "query", None),
        P("head", "query"),
        P(),
    )

    def program(*args):
        plan = direct_per_device if direct_plan_fits(mesh, args[0], args[1]) else per_device
        return jax.shard_map(
            plan,
            mesh=mesh,
            in_specs=placed,
            out_specs=(P("head", "page", None), P("head", "page", None), P("head", "page")),
            check_vma=False,
        )(*args)

    return program
```

```python
import itertools
import math

import jax
import jax.numpy as jnp
from jax import lax
from jax.experimental import pallas as pl
from jax.experimental.pallas import tpu as pltpu
from jax.sharding import PartitionSpec as P

STEPS = 2
PAGE_LEN = 32768


MASKED = -1e30
EPSILON = 1e-06
RATE_KEYS = 0.05
RATE_VALUES = 0.05
RATE_BIAS = 0.2
HIGHEST = lax.Precision.HIGHEST
TAIL = 8
CORES = 2


def exchange(value, **masks):
    axes = tuple(masks)
    sizes = [lax.axis_size(axis) for axis in axes]

    def flat(place):
        index = 0
        for size, at in zip(sizes, place):
            index = index * size + at
        return index

    pairs = [
        (flat(place), flat([at ^ mask for at, mask in zip(place, masks.values())]))
        for place in itertools.product(*map(range, sizes))
    ]
    return lax.ppermute(value, axes, pairs)


def halves(value):
    high = value.astype(jnp.bfloat16)
    return high, (value - high.astype(jnp.float32)).astype(jnp.bfloat16)


def dot(left, right, left_dim, right_dim):
    def one_pass(left_half, right_half):
        return lax.dot_general(
            left_half,
            right_half,
            (((left_dim,), (right_dim,)), ((), ())),
            preferred_element_type=jnp.float32,
        )

    cross = one_pass(left[0], right[1]) + one_pass(left[1], right[0])
    return one_pass(left[0], right[0]) + cross


def call(body, out_shapes, name, cost, operands, scratch=(), after=(), space=pltpu.VMEM, vmem=32):
    spaces = [space] * len(operands) + [pl.ANY] * len(after)
    count = len(operands)

    def without_after(*refs):
        body(*refs[:count], *refs[count + len(after) :])

    return pl.pallas_call(
        without_after,
        out_shape=[jax.ShapeDtypeStruct(shape, jnp.float32) for shape in out_shapes],
        in_specs=[pl.BlockSpec(memory_space=space) for space in spaces],
        out_specs=[pl.BlockSpec(memory_space=pltpu.VMEM) for _ in out_shapes],
        scratch_shapes=scratch,
        compiler_params=pltpu.CompilerParams(vmem_limit_bytes=vmem * 2**20),
        cost_estimate=pl.CostEstimate(flops=cost, bytes_accessed=2**20, transcendentals=0),
        name=name,
    )(*operands, *after)


def row_as_tail(row, width):
    rows = [row[:, at : at + width] for at in range(0, row.shape[1], width)]
    rows.append(jnp.zeros((TAIL - len(rows), width), row.dtype))
    return jnp.concatenate(rows, axis=0)


def tail_as_row(ref, start, count):
    return jnp.concatenate([ref[start + at : start + at + 1, :] for at in range(count)], axis=1)


def row_as_column(row, width):
    parts = []
    for at in range(0, row.shape[1], width):
        parts.append(jnp.broadcast_to(row[:, at : at + width], (width, width)).T)
    return jnp.concatenate(parts, axis=0)


def direct_plan_fits(mesh, queries, compact_keys):
    sizes = [mesh.shape[axis] for axis in ("page", "query", "head")]
    pages, query_devices, head_devices = sizes
    local_heads = queries.shape[0] // head_devices
    part_rows = queries.shape[1] // query_devices
    slot_rows = compact_keys.shape[1] // pages
    width = queries.shape[2]
    if any(size & (size - 1) for size in sizes) or pages < CORES or width % 128:
        return False
    if local_heads != CORES * query_devices:
        return False
    ranks = pages // CORES
    chunk = part_rows * query_devices // ranks
    return (
        part_rows * query_devices % ranks == 0
        and chunk % 128 == 0
        and part_rows % (8 * ranks) == 0
        and (part_rows // ranks % 128 == 0 or 1024 % (part_rows // ranks * 8) == 0)
        and slot_rows % width == 0
        and part_rows % width == 0
        and max(slot_rows, part_rows) < TAIL * width
    )


def direct_per_device(
    queries, compact_keys, compact_values, slot_bias, targets, positions, assignment
):
    local_heads, part_rows, width = queries.shape
    slot_rows = compact_keys.shape[1]
    query_devices = lax.axis_size("query")
    head_devices = lax.axis_size("head")
    ranks = lax.axis_size("page") // CORES
    query_rows = part_rows * query_devices
    chunk, piece = query_rows // ranks, part_rows // ranks
    slot_total = local_heads * head_devices * slot_rows * lax.axis_size("page")
    entry_total = slot_total * width
    score_scale = 1.0 / math.sqrt(width)
    slots = CORES * slot_rows
    devices = ranks * CORES * query_devices * head_devices
    pos_rows = part_rows // width
    bias_rows = slot_rows // width
    packed_rows = 2 * slot_rows + TAIL
    packed_shapes = [(packed_rows, width)] * 2
    matmul_cost = 3 * 2 * slots * query_rows * width

    def places():
        page = lax.axis_index("page")
        return page // CORES, page % CORES, lax.axis_index("query")

    def pack_queries(head, rank, queries, targets, out):
        rows = pl.ds(pl.multiple_of(rank * piece, piece), piece)
        return [
            (queries.at[head], out.at[pl.ds(0, part_rows)]),
            (targets.at[head, rows], out.at[pl.ds(part_rows, piece)]),
        ]

    def pack_state(head, keys, values, out):
        return [
            (keys.at[head], out.at[pl.ds(0, slot_rows)]),
            (values.at[head], out.at[pl.ds(slot_rows, slot_rows)]),
        ]

    def start_all(copies, sems, first=0):
        copies = [
            pltpu.make_async_copy(source, target, sems.at[first + at])
            for at, (source, target) in enumerate(copies)
        ]
        for copy in copies:
            copy.start()
        return copies

    def position_tail(head, positions_ref):
        return row_as_tail(positions_ref[pl.ds(head, 1), :].astype(jnp.float32), width)

    def state_tail(head, page, bias_ref, assignment_ref):
        page_start = (assignment_ref[page] * PAGE_LEN).astype(jnp.float32)
        tail = row_as_tail(bias_ref[pl.ds(head, 1), :], width)
        return jnp.concatenate(
            [tail[: TAIL - 1], jnp.full((1, width), page_start, jnp.float32)], axis=0
        )

    def send_body(
        queries, keys, values, biases, targets, positions, assignment, state_out, *refs
    ):
        query_outs = refs[: query_devices - 1]
        bias_ref, positions_ref, assignment_ref, sems = refs[query_devices - 1 :]
        rank, core, me = places()
        heads = [CORES * (me ^ turn) + core for turn in range(1, query_devices)]
        mate_head = CORES * me + (core ^ 1)
        small = start_all(
            [(assignment, assignment_ref), (positions, positions_ref), (biases, bias_ref)], sems
        )
        copies = pack_state(mate_head, keys, values, state_out)
        for head, out in zip(heads, query_outs):
            copies += pack_queries(head, rank, queries, targets, out)
        copies = start_all(copies, sems, 3)
        for copy in small:
            copy.wait()
        state_out[2 * slot_rows :, :] = state_tail(
            mate_head, CORES * rank + core, bias_ref, assignment_ref
        )
        for head, out in zip(heads, query_outs):
            out[part_rows + piece :, :] = position_tail(head, positions_ref)
        for copy in copies:
            copy.wait()

    def own_body(
        queries, keys, values, biases, targets, positions, assignment, state_out, query_out, *refs
    ):
        bias_ref, positions_ref, assignment_ref, sems = refs
        rank, core, me = places()
        head = CORES * me + core
        small = start_all(
            [(assignment, assignment_ref), (positions, positions_ref), (biases, bias_ref)], sems
        )
        copies = pack_state(head, keys, values, state_out)
        copies += pack_queries(head, rank, queries, targets, query_out)
        copies = start_all(copies, sems, 3)
        for copy in small:
            copy.wait()
        state_out[2 * slot_rows :, :] = state_tail(
            head, CORES * rank + core, bias_ref, assignment_ref
        )
        query_out[part_rows + piece :, :] = position_tail(head, positions_ref)
        for copy in copies:
            copy.wait()

    state_shape, query_shape = (packed_rows, width), (part_rows + piece + TAIL, width)
    small_scratch = [
        pltpu.VMEM(slot_bias.shape, jnp.float32),
        pltpu.VMEM(positions.shape, jnp.int32),
        pltpu.SMEM(assignment.shape, jnp.int32),
    ]
    arguments = [
        queries, compact_keys, compact_values, slot_bias, targets, positions, assignment
    ]
    mate_state, *sent_queries = call(
        send_body,
        [state_shape] + [query_shape] * (query_devices - 1),
        "pack",
        2**20,
        arguments,
        small_scratch + [pltpu.SemaphoreType.DMA((3 + 2 * query_devices,))],
        space=pl.ANY,
        vmem=60,
    )
    own_state, own_queries = call(
        own_body,
        [state_shape, query_shape],
        "own",
        2**24,
        arguments,
        small_scratch + [pltpu.SemaphoreType.DMA((7,))],
        space=pl.ANY,
    )
    query_parts = [own_queries] + [
        exchange(sent_queries[turn - 1], query=turn) for turn in range(1, query_devices)
    ]
    states = [own_state, exchange(mate_state, page=1)]

    def in_columns(parts, axis):
        return jnp.concatenate(
            [
                lax.slice_in_dim(part, at * piece, (at + 1) * piece, axis=axis)
                for at in range(ranks)
                for part in parts
            ],
            axis=axis,
        )

    def read_queries(query_refs):
        return halves(in_columns([ref[:part_rows, :] for ref in query_refs], 0))

    def part_of(ref, at):
        return ref.at[pl.ds(at * packed_rows, packed_rows)]

    def parts_of(refs):
        return refs if len(refs) == CORES else [part_of(refs[0], at) for at in range(CORES)]

    def step_sizes(tile_refs):
        tile = jnp.sum(tile_refs[0][...], axis=0)
        sums = jnp.sum(tile, axis=1, keepdims=True)
        return (
            RATE_KEYS / jnp.sqrt(sums[0:1] / entry_total + EPSILON),
            RATE_VALUES / jnp.sqrt(sums[1:2] / entry_total + EPSILON),
            RATE_BIAS / jnp.sqrt(sums[2:3] / slot_total + EPSILON),
        )

    def updated(state_ref, grad_ref, sizes):
        key_end, value_end = slot_rows, 2 * slot_rows
        return (
            state_ref[:key_end, :] - sizes[0] * grad_ref[:key_end, :],
            state_ref[key_end:value_end, :] - sizes[1] * grad_ref[key_end:value_end, :],
            state_ref[value_end:, :] - sizes[2] * grad_ref[value_end:, :],
        )

    def forward(state_refs, query_refs, chunk_outs, weights_out, max_out, chunks):
        rank, _, _ = places()
        all_queries = read_queries(query_refs)
        position_row = in_columns(
            [tail_as_row(ref, part_rows + piece, pos_rows) for ref in query_refs], 1
        )
        all_scores, all_visible = [], []
        for at, ref in enumerate(state_refs):
            scores = dot(halves(ref[:slot_rows, :]), all_queries, 1, 1) * score_scale
            bias = row_as_column(tail_as_row(ref, 2 * slot_rows, bias_rows), width)
            scores = scores + jnp.concatenate([bias] * (query_rows // width), axis=1)
            page_start = ref[packed_rows - 1 : packed_rows, 0:1]
            visible = jnp.broadcast_to(position_row >= page_start, scores.shape)
            all_scores.append(jnp.where(visible, scores, MASKED))
            all_visible.append(visible)
        row_max = jnp.max(all_scores[0], axis=0, keepdims=True)
        for scores in all_scores[1:]:
            row_max = jnp.maximum(row_max, jnp.max(scores, axis=0, keepdims=True))
        row_total = jnp.zeros_like(row_max)
        row_sum = jnp.zeros((width, query_rows), jnp.float32)
        for at, ref in enumerate(state_refs):
            weights = jnp.where(all_visible[at], jnp.exp(all_scores[at] - row_max), 0.0)
            weights_out[at * slot_rows : (at + 1) * slot_rows, :] = weights
            row_total = row_total + jnp.sum(weights, axis=0, keepdims=True)
            values = halves(ref[slot_rows : 2 * slot_rows, :])
            row_sum = row_sum + dot(values, halves(weights), 0, 0)
        max_out[...] = jnp.broadcast_to(row_max, (TAIL, query_rows))
        tail = jnp.concatenate(
            [row_max, row_total, jnp.zeros((TAIL - 2, query_rows), jnp.float32)], axis=0
        )
        for at in range(ranks):
            columns = slice(at * chunk, (at + 1) * chunk)
            chunks[at, :width, :] = row_sum[:, columns]
            chunks[at, width:, :] = tail[:, columns]
        for turn in range(ranks):
            chunk_outs[turn][...] = chunks[rank ^ turn]

    chunk_shape = (width + TAIL, chunk)
    forward_shapes = [chunk_shape] * ranks + [(slots, query_rows), (TAIL, query_rows)]
    chunk_scratch = [pltpu.VMEM((ranks,) + chunk_shape, jnp.float32)]

    fold = max(1, 128 // piece)
    folded, columns = width // fold, fold * piece
    piece_shape = (folded + TAIL, columns)
    piece_scratch = [pltpu.VMEM((ranks,) + piece_shape, jnp.float32)]

    def fold_rows(value):
        groups = [value[at * folded : (at + 1) * folded, :] for at in range(fold)]
        return jnp.concatenate(groups, axis=1)

    def unfold_rows(value):
        groups = [value[:, at * piece : (at + 1) * piece] for at in range(fold)]
        return jnp.concatenate(groups, axis=0)

    def rows_tail(rows):
        empty = jnp.zeros((TAIL - len(rows), columns), jnp.float32)
        return jnp.concatenate(rows + [empty], axis=0)

    def part_body(*refs):
        state_refs, (query_ref, *refs) = refs[:CORES], refs[CORES:]
        piece_outs, (weights_out, max_out, pieces) = refs[:ranks], refs[ranks:]
        rank, _, _ = places()
        queries = halves(query_ref[:part_rows, :])
        position_row = tail_as_row(query_ref, part_rows + piece, pos_rows)
        all_scores, all_visible = [], []
        for ref in state_refs:
            scores = dot(halves(ref[:slot_rows, :]), queries, 1, 1) * score_scale
            bias = row_as_column(tail_as_row(ref, 2 * slot_rows, bias_rows), width)
            scores = scores + jnp.concatenate([bias] * (part_rows // width), axis=1)
            page_start = ref[packed_rows - 1 : packed_rows, 0:1]
            visible = jnp.broadcast_to(position_row >= page_start, scores.shape)
            all_scores.append(jnp.where(visible, scores, MASKED))
            all_visible.append(visible)
        row_max = jnp.max(all_scores[0], axis=0, keepdims=True)
        for scores in all_scores[1:]:
            row_max = jnp.maximum(row_max, jnp.max(scores, axis=0, keepdims=True))
        row_total = jnp.zeros_like(row_max)
        row_sum = jnp.zeros((width, part_rows), jnp.float32)
        for at, ref in enumerate(state_refs):
            weights = jnp.where(all_visible[at], jnp.exp(all_scores[at] - row_max), 0.0)
            weights_out[at * slot_rows : (at + 1) * slot_rows, :] = weights
            row_total = row_total + jnp.sum(weights, axis=0, keepdims=True)
            values = halves(ref[slot_rows : 2 * slot_rows, :])
            row_sum = row_sum + dot(values, halves(weights), 0, 0)
        max_out[...] = jnp.broadcast_to(row_max, (TAIL, part_rows))
        for at in range(ranks):
            own = slice(at * piece, (at + 1) * piece)
            pieces[at, :folded, :] = fold_rows(row_sum[:, own])
            pieces[at, folded:, :] = rows_tail(
                [jnp.concatenate([row[:, own]] * fold, axis=1) for row in (row_max, row_total)]
            )
        for turn in range(ranks):
            piece_outs[turn][...] = pieces[rank ^ turn]

    part_shapes = [piece_shape] * ranks + [(slots, part_rows), (TAIL, part_rows)]

    def next_body(*refs):
        state_refs, refs = refs[:2], refs[2:]
        query_refs, refs = refs[:query_devices], refs[query_devices:]
        grad_refs, refs = refs[:2], refs[2:]
        tile_refs, refs = refs[: len(tiles)], refs[len(tiles) :]
        state_outs, refs = parts_of(refs[:1]), refs[1:]
        chunk_outs, refs = refs[:ranks], refs[ranks:]
        sizes = step_sizes(tile_refs)
        for at in range(2):
            keys, values, bias = updated(state_refs[at], grad_refs[at], sizes)
            state_outs[at][:slot_rows, :] = keys
            state_outs[at][slot_rows : 2 * slot_rows, :] = values
            state_outs[at][2 * slot_rows :, :] = bias
        forward(state_outs, query_refs, chunk_outs, *refs)

    def merged_chunk(query_refs, sums, maxima, totals, out):
        targets = jnp.concatenate(
            [ref[part_rows : part_rows + piece, :] for ref in query_refs], axis=0
        )
        row_max = maxima[0]
        for other in maxima[1:]:
            row_max = jnp.maximum(row_max, other)
        row_total = jnp.zeros_like(row_max)
        row_sum = jnp.zeros((width, chunk), jnp.float32)
        for part_sum, part_max, part_total in zip(sums, maxima, totals):
            factor = jnp.exp(part_max - row_max)
            row_total = row_total + part_total * factor
            row_sum = row_sum + part_sum * factor
        output = row_sum / row_total
        residual = output - targets.T
        row_delta = jnp.sum(residual * output, axis=0, keepdims=True)
        out[:width, :] = residual
        out[width:, :] = jnp.concatenate(
            [row_max, row_total, row_delta, jnp.zeros((TAIL - 3, chunk), jnp.float32)], axis=0
        )

    def first_merge_body(*refs):
        query_refs, (*piece_refs, merged_out) = refs[:query_devices], refs[query_devices:]

        def joined(read):
            return [
                jnp.concatenate([read(ref) for ref in piece_refs[turn::ranks]], axis=1)
                for turn in range(ranks)
            ]

        merged_chunk(
            query_refs,
            joined(lambda ref: unfold_rows(ref[:folded, :])),
            joined(lambda ref: ref[folded : folded + 1, :piece]),
            joined(lambda ref: ref[folded + 1 : folded + 2, :piece]),
            merged_out,
        )

    def merge_body(*refs):
        query_refs, (*chunk_refs, merged_out) = refs[:query_devices], refs[query_devices:]
        merged_chunk(
            query_refs,
            [ref[:width, :] for ref in chunk_refs],
            [ref[width : width + 1, :] for ref in chunk_refs],
            [ref[width + 1 : width + 2, :] for ref in chunk_refs],
            merged_out,
        )

    def backward_body(*refs):
        weights_refs, refs = refs[: len(weights)], refs[len(weights) :]
        max_refs, refs = refs[: len(weights)], refs[len(weights) :]
        state_refs, refs = parts_of(refs[: len(states)]), refs[len(states) :]
        query_refs, refs = refs[:query_devices], refs[query_devices:]
        merged_refs, refs = refs[:ranks], refs[ranks:]
        grad_outs, (squares_out, chunks) = refs[:2], refs[2:]
        rank, _, _ = places()
        for turn in range(ranks):
            chunks[rank ^ turn] = merged_refs[turn][...]
        if len(weights_refs) == 1:
            joined = jnp.concatenate([chunks[at] for at in range(ranks)], axis=1)
            all_queries = read_queries(query_refs)
        else:
            joined = jnp.concatenate(
                [
                    chunks[at, :, part * piece : (part + 1) * piece]
                    for part in range(query_devices)
                    for at in range(ranks)
                ],
                axis=1,
            )
            all_queries = halves(
                jnp.concatenate([ref[:part_rows, :] for ref in query_refs], axis=0)
            )
        residual = joined[:width, :]
        row_max, row_total, row_delta = (
            joined[width + at : width + at + 1, :] for at in range(3)
        )
        residual = halves(residual)
        maxima = jnp.concatenate([ref[0:1, :] for ref in max_refs], axis=1)
        factor = jnp.exp(maxima - row_max) / row_total
        ones = jnp.ones((TAIL, query_rows), jnp.bfloat16)
        ones = (ones, jnp.zeros_like(ones))
        squares = [jnp.zeros((1, width), jnp.float32)] * 3
        for at, ref in enumerate(state_refs):
            rows = slice(at * slot_rows, (at + 1) * slot_rows)
            attention = jnp.concatenate([part[rows, :] for part in weights_refs], axis=1) * factor
            grad_values = dot(halves(attention), residual, 1, 1)
            grad_probs = dot(halves(ref[slot_rows : 2 * slot_rows, :]), residual, 1, 0)
            grad_scores = halves(attention * (grad_probs - row_delta))
            grad_keys = dot(grad_scores, all_queries, 1, 0) * score_scale
            grad_bias = row_as_tail(dot(ones, grad_scores, 1, 1)[0:1, :], width)
            grad_outs[at][:slot_rows, :] = grad_keys
            grad_outs[at][slot_rows : 2 * slot_rows, :] = grad_values
            grad_outs[at][2 * slot_rows :, :] = grad_bias
            for which, grad in enumerate((grad_keys, grad_values, grad_bias)):
                squares[which] = squares[which] + jnp.sum(grad * grad, axis=0, keepdims=True)
        tile = jnp.concatenate(squares + [jnp.zeros((TAIL - 3, width), jnp.float32)], axis=0)
        for at in range(devices):
            squares_out[at] = tile

    def mate_body(*refs):
        *state_refs, out_ref = refs
        for at, ref in enumerate(state_refs):
            out_ref[pl.ds(at * packed_rows, packed_rows), :] = part_of(ref, 1)[...]

    out_masks = list(itertools.product(range(query_devices), range(CORES)))

    def to_output(packs, mask):
        if mask == (0, 0):
            return packs[0]
        return exchange(packs[mask[1]], page=mask[1], query=mask[0])

    for repeat in range(STEPS):
        last = repeat == STEPS - 1
        if repeat == 0:
            sums, weights, maxima = [], [], []
            for query_part in query_parts:
                *pieces, part_weights, part_max = call(
                    part_body,
                    part_shapes,
                    "forward",
                    2 * matmul_cost // query_devices,
                    states + [query_part],
                    piece_scratch,
                    after=maxima[-1:],
                )
                sums += pieces[:1] + [
                    exchange(pieces[turn], page=CORES * turn) for turn in range(1, ranks)
                ]
                weights.append(part_weights)
                maxima.append(part_max)
        else:
            new_state, *chunk_parts, part_weights, part_max = call(
                next_body,
                [(CORES * packed_rows, width)] + forward_shapes,
                "update_forward",
                2 * matmul_cost,
                states + query_parts + grads + tiles,
                chunk_scratch,
            )
            states, weights, maxima = [new_state], [part_weights], [part_max]
            arrived = {
                turn: exchange(chunk_parts[turn], page=CORES * turn)
                for turn in reversed(range(1, ranks))
            }
            sums = chunk_parts[:1] + list(arrived.values())
            new_states = states + [
                exchange(states[0], query=turn) for turn in range(1, query_devices)
            ]
        (merged,) = call(
            merge_body if repeat else first_merge_body,
            [chunk_shape],
            "merge",
            2**20,
            query_parts + sums,
        )
        all_merged = [merged] + [
            exchange(merged, page=CORES * turn) for turn in range(1, ranks)
        ]
        if repeat:
            (for_mate,) = call(
                mate_body,
                [(query_devices * packed_rows, width)],
                "mate_parts",
                2**20,
                new_states,
                after=all_merged[1:],
            )
            from_mate = exchange(for_mate, page=1)
        own_grad, mate_grad, squares = call(
            backward_body,
            packed_shapes + [(devices, TAIL, width)],
            "backward",
            3 * matmul_cost,
            weights + maxima + states + query_parts + all_merged,
            scratch=chunk_scratch,
        )
        grads = [own_grad, mate_grad]
        if last:
            all_grads = [to_output(grads, mask) for mask in out_masks]
        tiles = [
            lax.all_to_all(
                squares, ("page", "query", "head"), split_axis=0, concat_axis=0, tiled=True
            )
        ]

    def last_body(*refs):
        state_refs, (mate_ref, *refs) = refs[:query_devices], refs[query_devices:]
        state_refs = [
            part_of(mate_ref, turn) if flip else part_of(state_refs[turn], 0)
            for turn, flip in out_masks
        ]
        grad_refs, refs = refs[:local_heads], refs[local_heads:]
        tile_refs, (keys_out, values_out, bias_out) = refs[: len(tiles)], refs[len(tiles) :]
        _, core, me = places()
        sizes = step_sizes(tile_refs)
        for at, (turn, flip) in enumerate(out_masks):
            keys, values, bias = updated(state_refs[at], grad_refs[at], sizes)
            head = CORES * (me ^ turn) + (core ^ flip)
            keys_out[head] = keys
            values_out[head] = values
            bias_row = jnp.concatenate([bias[row : row + 1] for row in range(bias_rows)], axis=1)
            bias_out[pl.ds(head, 1), :] = bias_row

    return tuple(
        call(
            last_body,
            [compact_keys.shape, compact_values.shape, slot_bias.shape],
            "last_update",
            2**20,
            new_states + [from_mate] + all_grads + tiles,
        )
    )


def from_partner(value, axis, stride):
    mask = 2**stride
    pairs = [(source, source ^ mask) for source in range(lax.axis_size(axis))]
    return lax.ppermute(value, axis, pairs)


def squared_sums(grad_keys, grad_values, grad_bias):
    return jnp.stack(
        [
            jnp.sum(grad_keys * grad_keys),
            jnp.sum(grad_values * grad_values),
            jnp.sum(grad_bias * grad_bias),
        ]
    )


def apply_update(states, grads, totals, entry_count, slot_total):
    key_state, value_state, bias_state = states
    grad_keys, grad_values, grad_bias = grads
    rms_keys = jnp.sqrt(totals[0] / entry_count + EPSILON)
    rms_values = jnp.sqrt(totals[1] / entry_count + EPSILON)
    rms_bias = jnp.sqrt(totals[2] / slot_total + EPSILON)
    return (
        key_state - RATE_KEYS * grad_keys / rms_keys,
        value_state - RATE_VALUES * grad_values / rms_values,
        bias_state - RATE_BIAS * grad_bias / rms_bias,
    )


def local_gradients(queries, targets, visible, compact_keys, compact_values, slot_bias):
    score_scale = 1.0 / math.sqrt(queries.shape[2])
    scores = jnp.einsum("hqd,hsd->hqs", queries, compact_keys, precision=HIGHEST) * score_scale
    scores = jnp.where(visible, scores + slot_bias[:, None, :], MASKED)
    local_max = jnp.max(scores, axis=2)
    row_max = lax.pmax(local_max, "page")
    weights = jnp.where(visible, jnp.exp(scores - row_max[:, :, None]), 0.0)
    local_sum = jnp.einsum("hqs,hsd->hqd", weights, compact_values, precision=HIGHEST)
    row_total, row_sum = lax.psum((jnp.sum(weights, axis=2), local_sum), "page")
    attention = weights / row_total[:, :, None]
    output = row_sum / row_total[:, :, None]
    residual = output - targets
    grad_values = jnp.einsum("hqs,hqd->hsd", attention, residual, precision=HIGHEST)
    row_delta = jnp.sum(residual * output, axis=2)
    grad_probs = jnp.einsum("hqd,hsd->hqs", residual, compact_values, precision=HIGHEST)
    grad_scores = attention * (grad_probs - row_delta[:, :, None])
    grad_bias = jnp.sum(grad_scores, axis=1)
    grad_keys = jnp.einsum("hqs,hqd->hsd", grad_scores, queries, precision=HIGHEST) * score_scale
    return (grad_keys, grad_values, grad_bias)


def per_device(queries, compact_keys, compact_values, slot_bias, targets, positions, assignment):
    page_number = assignment[lax.axis_index("page")]
    local_heads = compact_keys.shape[0]
    slot_total = local_heads * lax.axis_size("head") * compact_keys.shape[1] * lax.axis_size("page")
    entry_count = slot_total * compact_keys.shape[2]
    query_count = lax.axis_size("query")
    heads_kept = max(local_heads // query_count, 1)
    query_parts = max(query_count // local_heads, 1)
    part_rows = queries.shape[1] // query_parts

    def split_items(array):
        width = array.shape[2]
        array = array.reshape(local_heads // heads_kept, heads_kept, query_parts, part_rows, width)
        array = jnp.transpose(array, (0, 2, 1, 3, 4))
        return array.reshape(query_count, heads_kept, part_rows, width)

    def join_items(array):
        width = array.shape[3]
        array = jnp.transpose(array, (1, 0, 2, 3))
        return array.reshape(heads_kept, query_count * part_rows, width)

    position_column = positions.astype(jnp.float32)[:, :, None]
    got_queries, got_targets, got_positions = (
        lax.all_to_all(split_items(queries), "query", split_axis=0, concat_axis=0, tiled=True),
        lax.all_to_all(split_items(targets), "query", split_axis=0, concat_axis=0, tiled=True),
        lax.all_to_all(
            split_items(position_column), "query", split_axis=0, concat_axis=0, tiled=True
        ),
    )
    group_queries = join_items(got_queries)
    group_targets = join_items(got_targets)
    group_positions = join_items(got_positions)[:, :, 0]
    visible = (page_number.astype(jnp.float32) <= jnp.floor(group_positions / PAGE_LEN))[:, :, None]
    query_index = lax.axis_index("query")
    first_head = query_index // query_parts * heads_kept
    key_state = lax.dynamic_slice_in_dim(compact_keys, first_head, heads_kept, 0)
    value_state = lax.dynamic_slice_in_dim(compact_values, first_head, heads_kept, 0)
    bias_state = lax.dynamic_slice_in_dim(slot_bias, first_head, heads_kept, 0)
    counted = (query_index % query_parts == 0).astype(jnp.float32)
    for repeat in range(STEPS):
        grads = local_gradients(
            group_queries, group_targets, visible, key_state, value_state, bias_state
        )
        for bit in range(query_parts.bit_length() - 1):
            partner = from_partner((grads[0], grads[1], grads[2]), "query", bit)
            grads = (grads[0] + partner[0], grads[1] + partner[1], grads[2] + partner[2])
        totals = lax.psum(
            squared_sums(grads[0], grads[1], grads[2]) * counted, ("page", "query", "head")
        )
        key_state, value_state, bias_state = apply_update(
            (key_state, value_state, bias_state), grads, totals, entry_count, slot_total
        )
    all_keys, all_values, all_bias = (
        lax.all_gather(key_state, "query", axis=0, tiled=True),
        lax.all_gather(value_state, "query", axis=0, tiled=True),
        lax.all_gather(bias_state, "query", axis=0, tiled=True),
    )
    slot_rows = compact_keys.shape[1]
    head_width = compact_keys.shape[2]
    all_keys = all_keys.reshape(
        local_heads // heads_kept, query_parts, heads_kept, slot_rows, head_width
    )[:, 0]
    all_values = all_values.reshape(
        local_heads // heads_kept, query_parts, heads_kept, slot_rows, head_width
    )[:, 0]
    all_bias = all_bias.reshape(local_heads // heads_kept, query_parts, heads_kept, slot_rows)[:, 0]
    return (
        all_keys.reshape(local_heads, slot_rows, head_width),
        all_values.reshape(local_heads, slot_rows, head_width),
        all_bias.reshape(local_heads, slot_rows),
    )


def solution(mesh):
    placed = (
        P("head", "query", None),
        P("head", "page", None),
        P("head", "page", None),
        P("head", "page"),
        P("head", "query", None),
        P("head", "query"),
        P(),
    )

    def program(*args):
        plan = direct_per_device if direct_plan_fits(mesh, args[0], args[1]) else per_device
        return jax.shard_map(
            plan,
            mesh=mesh,
            in_specs=placed,
            out_specs=(P("head", "page", None), P("head", "page", None), P("head", "page")),
            check_vma=False,
        )(*args)

    return program
```

```python
import itertools
import math

import jax
import jax.numpy as jnp
from jax import lax
from jax.experimental import pallas as pl
from jax.experimental.pallas import tpu as pltpu
from jax.sharding import PartitionSpec as P

STEPS = 2
PAGE_LEN = 32768


MASKED = -1e30
EPSILON = 1e-06
RATE_KEYS = 0.05
RATE_VALUES = 0.05
RATE_BIAS = 0.2
HIGHEST = lax.Precision.HIGHEST
TAIL = 8
CORES = 2


def exchange(value, **masks):
    axes = tuple(masks)
    sizes = [lax.axis_size(axis) for axis in axes]

    def flat(place):
        index = 0
        for size, at in zip(sizes, place):
            index = index * size + at
        return index

    pairs = [
        (flat(place), flat([at ^ mask for at, mask in zip(place, masks.values())]))
        for place in itertools.product(*map(range, sizes))
    ]
    return lax.ppermute(value, axes, pairs)


def halves(value):
    high = value.astype(jnp.bfloat16)
    return high, (value - high.astype(jnp.float32)).astype(jnp.bfloat16)


def dot(left, right, left_dim, right_dim):
    def one_pass(left_half, right_half):
        return lax.dot_general(
            left_half,
            right_half,
            (((left_dim,), (right_dim,)), ((), ())),
            preferred_element_type=jnp.float32,
        )

    cross = one_pass(left[0], right[1]) + one_pass(left[1], right[0])
    return one_pass(left[0], right[0]) + cross


def call(body, out_shapes, name, cost, operands, scratch=(), after=(), space=pltpu.VMEM, vmem=32):
    spaces = [space] * len(operands) + [pl.ANY] * len(after)
    count = len(operands)

    def without_after(*refs):
        body(*refs[:count], *refs[count + len(after) :])

    return pl.pallas_call(
        without_after,
        out_shape=[jax.ShapeDtypeStruct(shape, jnp.float32) for shape in out_shapes],
        in_specs=[pl.BlockSpec(memory_space=space) for space in spaces],
        out_specs=[pl.BlockSpec(memory_space=pltpu.VMEM) for _ in out_shapes],
        scratch_shapes=scratch,
        compiler_params=pltpu.CompilerParams(vmem_limit_bytes=vmem * 2**20),
        cost_estimate=pl.CostEstimate(flops=cost, bytes_accessed=2**20, transcendentals=0),
        name=name,
    )(*operands, *after)


def row_as_tail(row, width):
    rows = [row[:, at : at + width] for at in range(0, row.shape[1], width)]
    rows.append(jnp.zeros((TAIL - len(rows), width), row.dtype))
    return jnp.concatenate(rows, axis=0)


def tail_as_row(ref, start, count):
    return jnp.concatenate([ref[start + at : start + at + 1, :] for at in range(count)], axis=1)


def row_as_column(row, width):
    parts = []
    for at in range(0, row.shape[1], width):
        parts.append(jnp.broadcast_to(row[:, at : at + width], (width, width)).T)
    return jnp.concatenate(parts, axis=0)


def direct_plan_fits(mesh, queries, compact_keys):
    sizes = [mesh.shape[axis] for axis in ("page", "query", "head")]
    pages, query_devices, head_devices = sizes
    local_heads = queries.shape[0] // head_devices
    part_rows = queries.shape[1] // query_devices
    slot_rows = compact_keys.shape[1] // pages
    width = queries.shape[2]
    if any(size & (size - 1) for size in sizes) or pages < CORES or width % 128:
        return False
    if local_heads != CORES * query_devices:
        return False
    ranks = pages // CORES
    chunk = part_rows * query_devices // ranks
    return (
        part_rows * query_devices % ranks == 0
        and chunk % 128 == 0
        and part_rows % (8 * ranks) == 0
        and (part_rows // ranks % 128 == 0 or 1024 % (part_rows // ranks * 8) == 0)
        and slot_rows % width == 0
        and part_rows % width == 0
        and max(slot_rows, part_rows) < TAIL * width
    )


def direct_per_device(
    queries, compact_keys, compact_values, slot_bias, targets, positions, assignment
):
    local_heads, part_rows, width = queries.shape
    slot_rows = compact_keys.shape[1]
    query_devices = lax.axis_size("query")
    head_devices = lax.axis_size("head")
    ranks = lax.axis_size("page") // CORES
    query_rows = part_rows * query_devices
    chunk, piece = query_rows // ranks, part_rows // ranks
    slot_total = local_heads * head_devices * slot_rows * lax.axis_size("page")
    entry_total = slot_total * width
    score_scale = 1.0 / math.sqrt(width)
    slots = CORES * slot_rows
    devices = ranks * CORES * query_devices * head_devices
    pos_rows = part_rows // width
    bias_rows = slot_rows // width
    packed_rows = 2 * slot_rows + TAIL
    packed_shapes = [(packed_rows, width)] * 2
    matmul_cost = 3 * 2 * slots * query_rows * width

    def places():
        page = lax.axis_index("page")
        return page // CORES, page % CORES, lax.axis_index("query")

    def pack_queries(head, rank, queries, targets, out):
        rows = pl.ds(pl.multiple_of(rank * piece, piece), piece)
        return [
            (queries.at[head], out.at[pl.ds(0, part_rows)]),
            (targets.at[head, rows], out.at[pl.ds(part_rows, piece)]),
        ]

    def pack_state(head, keys, values, out):
        return [
            (keys.at[head], out.at[pl.ds(0, slot_rows)]),
            (values.at[head], out.at[pl.ds(slot_rows, slot_rows)]),
        ]

    def start_all(copies, sems, first=0):
        copies = [
            pltpu.make_async_copy(source, target, sems.at[first + at])
            for at, (source, target) in enumerate(copies)
        ]
        for copy in copies:
            copy.start()
        return copies

    def position_tail(head, positions_ref):
        return row_as_tail(positions_ref[pl.ds(head, 1), :].astype(jnp.float32), width)

    def state_tail(head, page, bias_ref, assignment_ref):
        page_start = (assignment_ref[page] * PAGE_LEN).astype(jnp.float32)
        tail = row_as_tail(bias_ref[pl.ds(head, 1), :], width)
        return jnp.concatenate(
            [tail[: TAIL - 1], jnp.full((1, width), page_start, jnp.float32)], axis=0
        )

    def send_body(
        queries, keys, values, biases, targets, positions, assignment, state_out, *refs
    ):
        query_outs = refs[: query_devices - 1]
        bias_ref, positions_ref, assignment_ref, sems = refs[query_devices - 1 :]
        rank, core, me = places()
        heads = [CORES * (me ^ turn) + core for turn in range(1, query_devices)]
        mate_head = CORES * me + (core ^ 1)
        small = start_all(
            [(assignment, assignment_ref), (positions, positions_ref), (biases, bias_ref)], sems
        )
        copies = pack_state(mate_head, keys, values, state_out)
        for head, out in zip(heads, query_outs):
            copies += pack_queries(head, rank, queries, targets, out)
        copies = start_all(copies, sems, 3)
        for copy in small:
            copy.wait()
        state_out[2 * slot_rows :, :] = state_tail(
            mate_head, CORES * rank + core, bias_ref, assignment_ref
        )
        for head, out in zip(heads, query_outs):
            out[part_rows + piece :, :] = position_tail(head, positions_ref)
        for copy in copies:
            copy.wait()

    def own_body(
        queries, keys, values, biases, targets, positions, assignment, state_out, query_out, *refs
    ):
        bias_ref, positions_ref, assignment_ref, sems = refs
        rank, core, me = places()
        head = CORES * me + core
        small = start_all(
            [(assignment, assignment_ref), (positions, positions_ref), (biases, bias_ref)], sems
        )
        copies = pack_state(head, keys, values, state_out)
        copies += pack_queries(head, rank, queries, targets, query_out)
        copies = start_all(copies, sems, 3)
        for copy in small:
            copy.wait()
        state_out[2 * slot_rows :, :] = state_tail(
            head, CORES * rank + core, bias_ref, assignment_ref
        )
        query_out[part_rows + piece :, :] = position_tail(head, positions_ref)
        for copy in copies:
            copy.wait()

    state_shape, query_shape = (packed_rows, width), (part_rows + piece + TAIL, width)
    small_scratch = [
        pltpu.VMEM(slot_bias.shape, jnp.float32),
        pltpu.VMEM(positions.shape, jnp.int32),
        pltpu.SMEM(assignment.shape, jnp.int32),
    ]
    arguments = [
        queries, compact_keys, compact_values, slot_bias, targets, positions, assignment
    ]
    mate_state, *sent_queries = call(
        send_body,
        [state_shape] + [query_shape] * (query_devices - 1),
        "pack",
        2**20,
        arguments,
        small_scratch + [pltpu.SemaphoreType.DMA((3 + 2 * query_devices,))],
        space=pl.ANY,
        vmem=60,
    )
    own_state, own_queries = call(
        own_body,
        [state_shape, query_shape],
        "own",
        2**24,
        arguments,
        small_scratch + [pltpu.SemaphoreType.DMA((7,))],
        space=pl.ANY,
    )
    query_parts = [own_queries] + [
        exchange(sent_queries[turn - 1], query=turn) for turn in range(1, query_devices)
    ]
    states = [own_state, exchange(mate_state, page=1)]

    def in_columns(parts, axis):
        return jnp.concatenate(
            [
                lax.slice_in_dim(part, at * piece, (at + 1) * piece, axis=axis)
                for at in range(ranks)
                for part in parts
            ],
            axis=axis,
        )

    def read_queries(query_refs):
        return halves(in_columns([ref[:part_rows, :] for ref in query_refs], 0))

    def part_of(ref, at):
        return ref.at[pl.ds(at * packed_rows, packed_rows)]

    def parts_of(refs):
        return refs if len(refs) == CORES else [part_of(refs[0], at) for at in range(CORES)]

    def step_sizes(tile_refs):
        tile = jnp.sum(tile_refs[0][...], axis=0)
        sums = jnp.sum(tile, axis=1, keepdims=True)
        return (
            RATE_KEYS / jnp.sqrt(sums[0:1] / entry_total + EPSILON),
            RATE_VALUES / jnp.sqrt(sums[1:2] / entry_total + EPSILON),
            RATE_BIAS / jnp.sqrt(sums[2:3] / slot_total + EPSILON),
        )

    def updated(state_ref, grad_ref, sizes):
        key_end, value_end = slot_rows, 2 * slot_rows
        return (
            state_ref[:key_end, :] - sizes[0] * grad_ref[:key_end, :],
            state_ref[key_end:value_end, :] - sizes[1] * grad_ref[key_end:value_end, :],
            state_ref[value_end:, :] - sizes[2] * grad_ref[value_end:, :],
        )

    def forward(state_refs, query_refs, chunk_outs, weights_out, max_out, chunks):
        rank, _, _ = places()
        all_queries = read_queries(query_refs)
        position_row = in_columns(
            [tail_as_row(ref, part_rows + piece, pos_rows) for ref in query_refs], 1
        )
        all_scores, all_visible = [], []
        for at, ref in enumerate(state_refs):
            scores = dot(halves(ref[:slot_rows, :]), all_queries, 1, 1) * score_scale
            bias = row_as_column(tail_as_row(ref, 2 * slot_rows, bias_rows), width)
            scores = scores + jnp.concatenate([bias] * (query_rows // width), axis=1)
            page_start = ref[packed_rows - 1 : packed_rows, 0:1]
            visible = jnp.broadcast_to(position_row >= page_start, scores.shape)
            all_scores.append(jnp.where(visible, scores, MASKED))
            all_visible.append(visible)
        row_max = jnp.max(all_scores[0], axis=0, keepdims=True)
        for scores in all_scores[1:]:
            row_max = jnp.maximum(row_max, jnp.max(scores, axis=0, keepdims=True))
        row_total = jnp.zeros_like(row_max)
        row_sum = jnp.zeros((width, query_rows), jnp.float32)
        for at, ref in enumerate(state_refs):
            weights = jnp.where(all_visible[at], jnp.exp(all_scores[at] - row_max), 0.0)
            weights_out[at * slot_rows : (at + 1) * slot_rows, :] = weights
            row_total = row_total + jnp.sum(weights, axis=0, keepdims=True)
            values = halves(ref[slot_rows : 2 * slot_rows, :])
            row_sum = row_sum + dot(values, halves(weights), 0, 0)
        max_out[...] = jnp.broadcast_to(row_max, (TAIL, query_rows))
        tail = jnp.concatenate(
            [row_max, row_total, jnp.zeros((TAIL - 2, query_rows), jnp.float32)], axis=0
        )
        for at in range(ranks):
            columns = slice(at * chunk, (at + 1) * chunk)
            chunks[at, :width, :] = row_sum[:, columns]
            chunks[at, width:, :] = tail[:, columns]
        for turn in range(ranks):
            chunk_outs[turn][...] = chunks[rank ^ turn]

    chunk_shape = (width + TAIL, chunk)
    forward_shapes = [chunk_shape] * ranks + [(slots, query_rows), (TAIL, query_rows)]
    chunk_scratch = [pltpu.VMEM((ranks,) + chunk_shape, jnp.float32)]

    fold = max(1, 128 // piece)
    folded, columns = width // fold, fold * piece
    piece_shape = (folded + TAIL, columns)
    piece_scratch = [pltpu.VMEM((ranks,) + piece_shape, jnp.float32)]

    def fold_rows(value):
        groups = [value[at * folded : (at + 1) * folded, :] for at in range(fold)]
        return jnp.concatenate(groups, axis=1)

    def unfold_rows(value):
        groups = [value[:, at * piece : (at + 1) * piece] for at in range(fold)]
        return jnp.concatenate(groups, axis=0)

    def rows_tail(rows):
        empty = jnp.zeros((TAIL - len(rows), columns), jnp.float32)
        return jnp.concatenate(rows + [empty], axis=0)

    def part_body(*refs):
        state_refs, (query_ref, *refs) = refs[:CORES], refs[CORES:]
        piece_outs, (weights_out, max_out, pieces) = refs[:ranks], refs[ranks:]
        rank, _, _ = places()
        queries = halves(query_ref[:part_rows, :])
        position_row = tail_as_row(query_ref, part_rows + piece, pos_rows)
        all_scores, all_visible = [], []
        for ref in state_refs:
            scores = dot(halves(ref[:slot_rows, :]), queries, 1, 1) * score_scale
            bias = row_as_column(tail_as_row(ref, 2 * slot_rows, bias_rows), width)
            scores = scores + jnp.concatenate([bias] * (part_rows // width), axis=1)
            page_start = ref[packed_rows - 1 : packed_rows, 0:1]
            visible = jnp.broadcast_to(position_row >= page_start, scores.shape)
            all_scores.append(jnp.where(visible, scores, MASKED))
            all_visible.append(visible)
        row_max = jnp.max(all_scores[0], axis=0, keepdims=True)
        for scores in all_scores[1:]:
            row_max = jnp.maximum(row_max, jnp.max(scores, axis=0, keepdims=True))
        row_total = jnp.zeros_like(row_max)
        row_sum = jnp.zeros((width, part_rows), jnp.float32)
        for at, ref in enumerate(state_refs):
            weights = jnp.where(all_visible[at], jnp.exp(all_scores[at] - row_max), 0.0)
            weights_out[at * slot_rows : (at + 1) * slot_rows, :] = weights
            row_total = row_total + jnp.sum(weights, axis=0, keepdims=True)
            values = halves(ref[slot_rows : 2 * slot_rows, :])
            row_sum = row_sum + dot(values, halves(weights), 0, 0)
        max_out[...] = jnp.broadcast_to(row_max, (TAIL, part_rows))
        for at in range(ranks):
            own = slice(at * piece, (at + 1) * piece)
            pieces[at, :folded, :] = fold_rows(row_sum[:, own])
            pieces[at, folded:, :] = rows_tail(
                [jnp.concatenate([row[:, own]] * fold, axis=1) for row in (row_max, row_total)]
            )
        for turn in range(ranks):
            piece_outs[turn][...] = pieces[rank ^ turn]

    part_shapes = [piece_shape] * ranks + [(slots, part_rows), (TAIL, part_rows)]

    def next_body(*refs):
        state_refs, refs = refs[:2], refs[2:]
        query_refs, refs = refs[:query_devices], refs[query_devices:]
        grad_refs, refs = refs[:2], refs[2:]
        tile_refs, refs = refs[: len(tiles)], refs[len(tiles) :]
        state_outs, refs = parts_of(refs[:1]), refs[1:]
        chunk_outs, refs = refs[:ranks], refs[ranks:]
        sizes = step_sizes(tile_refs)
        for at in range(2):
            keys, values, bias = updated(state_refs[at], grad_refs[at], sizes)
            state_outs[at][:slot_rows, :] = keys
            state_outs[at][slot_rows : 2 * slot_rows, :] = values
            state_outs[at][2 * slot_rows :, :] = bias
        forward(state_outs, query_refs, chunk_outs, *refs)

    def merged_chunk(query_refs, sums, maxima, totals, out):
        targets = jnp.concatenate(
            [ref[part_rows : part_rows + piece, :] for ref in query_refs], axis=0
        )
        row_max = maxima[0]
        for other in maxima[1:]:
            row_max = jnp.maximum(row_max, other)
        row_total = jnp.zeros_like(row_max)
        row_sum = jnp.zeros((width, chunk), jnp.float32)
        for part_sum, part_max, part_total in zip(sums, maxima, totals):
            factor = jnp.exp(part_max - row_max)
            row_total = row_total + part_total * factor
            row_sum = row_sum + part_sum * factor
        output = row_sum / row_total
        residual = output - targets.T
        row_delta = jnp.sum(residual * output, axis=0, keepdims=True)
        out[:width, :] = residual
        out[width:, :] = jnp.concatenate(
            [row_max, row_total, row_delta, jnp.zeros((TAIL - 3, chunk), jnp.float32)], axis=0
        )

    def first_merge_body(*refs):
        query_refs, (*piece_refs, merged_out) = refs[:query_devices], refs[query_devices:]

        def joined(read):
            return [
                jnp.concatenate([read(ref) for ref in piece_refs[turn::ranks]], axis=1)
                for turn in range(ranks)
            ]

        merged_chunk(
            query_refs,
            joined(lambda ref: unfold_rows(ref[:folded, :])),
            joined(lambda ref: ref[folded : folded + 1, :piece]),
            joined(lambda ref: ref[folded + 1 : folded + 2, :piece]),
            merged_out,
        )

    def merge_body(*refs):
        query_refs, (*chunk_refs, merged_out) = refs[:query_devices], refs[query_devices:]
        merged_chunk(
            query_refs,
            [ref[:width, :] for ref in chunk_refs],
            [ref[width : width + 1, :] for ref in chunk_refs],
            [ref[width + 1 : width + 2, :] for ref in chunk_refs],
            merged_out,
        )

    def backward_body(*refs):
        weights_refs, refs = refs[: len(weights)], refs[len(weights) :]
        max_refs, refs = refs[: len(weights)], refs[len(weights) :]
        state_refs, refs = parts_of(refs[: len(states)]), refs[len(states) :]
        query_refs, refs = refs[:query_devices], refs[query_devices:]
        merged_refs, refs = refs[:ranks], refs[ranks:]
        grad_outs, (squares_out, chunks) = refs[:2], refs[2:]
        rank, _, _ = places()
        for turn in range(ranks):
            chunks[rank ^ turn] = merged_refs[turn][...]
        if len(weights_refs) == 1:
            joined = jnp.concatenate([chunks[at] for at in range(ranks)], axis=1)
            all_queries = read_queries(query_refs)
        else:
            joined = jnp.concatenate(
                [
                    chunks[at, :, part * piece : (part + 1) * piece]
                    for part in range(query_devices)
                    for at in range(ranks)
                ],
                axis=1,
            )
            all_queries = halves(
                jnp.concatenate([ref[:part_rows, :] for ref in query_refs], axis=0)
            )
        residual = joined[:width, :]
        row_max, row_total, row_delta = (
            joined[width + at : width + at + 1, :] for at in range(3)
        )
        residual = halves(residual)
        maxima = jnp.concatenate([ref[0:1, :] for ref in max_refs], axis=1)
        factor = jnp.exp(maxima - row_max) / row_total
        ones = jnp.ones((TAIL, query_rows), jnp.bfloat16)
        ones = (ones, jnp.zeros_like(ones))
        squares = [jnp.zeros((1, width), jnp.float32)] * 3
        for at, (ref, out) in enumerate(zip(state_refs, grad_outs)):
            rows = slice(at * slot_rows, (at + 1) * slot_rows)
            attention = jnp.concatenate([part[rows, :] for part in weights_refs], axis=1) * factor
            grad_values = dot(halves(attention), residual, 1, 1)
            grad_probs = dot(halves(ref[slot_rows : 2 * slot_rows, :]), residual, 1, 0)
            grad_scores = halves(attention * (grad_probs - row_delta))
            grad_keys = dot(grad_scores, all_queries, 1, 0) * score_scale
            grad_bias = row_as_tail(dot(ones, grad_scores, 1, 1)[0:1, :], width)
            out[:slot_rows, :] = grad_keys
            out[slot_rows : 2 * slot_rows, :] = grad_values
            out[2 * slot_rows :, :] = grad_bias
            for which, grad in enumerate((grad_keys, grad_values, grad_bias)):
                squares[which] = squares[which] + jnp.sum(grad * grad, axis=0, keepdims=True)
        tile = jnp.concatenate(squares + [jnp.zeros((TAIL - 3, width), jnp.float32)], axis=0)
        for at in range(devices):
            squares_out[at] = tile

    def mate_body(*refs):
        *state_refs, out_ref = refs
        for at, ref in enumerate(state_refs):
            out_ref[pl.ds(at * packed_rows, packed_rows), :] = part_of(ref, 1)[...]

    out_masks = list(itertools.product(range(query_devices), range(CORES)))

    def to_output(packs, mask):
        if mask == (0, 0):
            return packs[0]
        return exchange(packs[mask[1]], page=mask[1], query=mask[0])

    for repeat in range(STEPS):
        last = repeat == STEPS - 1
        if repeat == 0:
            sums, weights, maxima = [], [], []
            for query_part in query_parts:
                *pieces, part_weights, part_max = call(
                    part_body,
                    part_shapes,
                    "forward",
                    2 * matmul_cost // query_devices,
                    states + [query_part],
                    piece_scratch,
                    after=maxima[-1:],
                )
                arrived = {
                    turn: exchange(pieces[turn], page=CORES * turn)
                    for turn in reversed(range(1, ranks))
                }
                sums += list(arrived.values()) + pieces[:1]
                weights.append(part_weights)
                maxima.append(part_max)
        else:
            new_state, *chunk_parts, part_weights, part_max = call(
                next_body,
                [(CORES * packed_rows, width)] + forward_shapes,
                "update_forward",
                2 * matmul_cost,
                states + query_parts + grads + tiles,
                chunk_scratch,
            )
            states, weights, maxima = [new_state], [part_weights], [part_max]
            arrived = {
                turn: exchange(chunk_parts[turn], page=CORES * turn)
                for turn in reversed(range(1, ranks))
            }
            sums = chunk_parts[:1] + list(arrived.values())
            new_states = states + [
                exchange(states[0], query=turn) for turn in range(1, query_devices)
            ]
        (merged,) = call(
            merge_body if repeat else first_merge_body,
            [chunk_shape],
            "merge",
            2**20,
            query_parts + sums,
        )
        all_merged = [merged] + [
            exchange(merged, page=CORES * turn) for turn in range(1, ranks)
        ]
        if repeat:
            (for_mate,) = call(
                mate_body,
                [(query_devices * packed_rows, width)],
                "mate_parts",
                2**20,
                new_states,
                after=all_merged[1:],
            )
            from_mate = exchange(for_mate, page=1)
        own_grad, mate_grad, squares = call(
            backward_body,
            packed_shapes + [(devices, TAIL, width)],
            "backward",
            3 * matmul_cost,
            weights + maxima + states + query_parts + all_merged,
            scratch=chunk_scratch,
        )
        grads = [own_grad, mate_grad]
        if last:
            all_grads = [to_output(grads, mask) for mask in out_masks]
        tiles = [
            lax.all_to_all(
                squares, ("page", "query", "head"), split_axis=0, concat_axis=0, tiled=True
            )
        ]

    def last_body(*refs):
        state_refs, (mate_ref, *refs) = refs[:query_devices], refs[query_devices:]
        state_refs = [
            part_of(mate_ref, turn) if flip else part_of(state_refs[turn], 0)
            for turn, flip in out_masks
        ]
        grad_refs, refs = refs[:local_heads], refs[local_heads:]
        tile_refs, (keys_out, values_out, bias_out) = refs[: len(tiles)], refs[len(tiles) :]
        _, core, me = places()
        sizes = step_sizes(tile_refs)
        for at, (turn, flip) in enumerate(out_masks):
            keys, values, bias = updated(state_refs[at], grad_refs[at], sizes)
            head = CORES * (me ^ turn) + (core ^ flip)
            keys_out[head] = keys
            values_out[head] = values
            bias_row = jnp.concatenate([bias[row : row + 1] for row in range(bias_rows)], axis=1)
            bias_out[pl.ds(head, 1), :] = bias_row

    return tuple(
        call(
            last_body,
            [compact_keys.shape, compact_values.shape, slot_bias.shape],
            "last_update",
            2**20,
            new_states + [from_mate] + all_grads + tiles,
        )
    )


def from_partner(value, axis, stride):
    mask = 2**stride
    pairs = [(source, source ^ mask) for source in range(lax.axis_size(axis))]
    return lax.ppermute(value, axis, pairs)


def squared_sums(grad_keys, grad_values, grad_bias):
    return jnp.stack(
        [
            jnp.sum(grad_keys * grad_keys),
            jnp.sum(grad_values * grad_values),
            jnp.sum(grad_bias * grad_bias),
        ]
    )


def apply_update(states, grads, totals, entry_count, slot_total):
    key_state, value_state, bias_state = states
    grad_keys, grad_values, grad_bias = grads
    rms_keys = jnp.sqrt(totals[0] / entry_count + EPSILON)
    rms_values = jnp.sqrt(totals[1] / entry_count + EPSILON)
    rms_bias = jnp.sqrt(totals[2] / slot_total + EPSILON)
    return (
        key_state - RATE_KEYS * grad_keys / rms_keys,
        value_state - RATE_VALUES * grad_values / rms_values,
        bias_state - RATE_BIAS * grad_bias / rms_bias,
    )


def local_gradients(queries, targets, visible, compact_keys, compact_values, slot_bias):
    score_scale = 1.0 / math.sqrt(queries.shape[2])
    scores = jnp.einsum("hqd,hsd->hqs", queries, compact_keys, precision=HIGHEST) * score_scale
    scores = jnp.where(visible, scores + slot_bias[:, None, :], MASKED)
    local_max = jnp.max(scores, axis=2)
    row_max = lax.pmax(local_max, "page")
    weights = jnp.where(visible, jnp.exp(scores - row_max[:, :, None]), 0.0)
    local_sum = jnp.einsum("hqs,hsd->hqd", weights, compact_values, precision=HIGHEST)
    row_total, row_sum = lax.psum((jnp.sum(weights, axis=2), local_sum), "page")
    attention = weights / row_total[:, :, None]
    output = row_sum / row_total[:, :, None]
    residual = output - targets
    grad_values = jnp.einsum("hqs,hqd->hsd", attention, residual, precision=HIGHEST)
    row_delta = jnp.sum(residual * output, axis=2)
    grad_probs = jnp.einsum("hqd,hsd->hqs", residual, compact_values, precision=HIGHEST)
    grad_scores = attention * (grad_probs - row_delta[:, :, None])
    grad_bias = jnp.sum(grad_scores, axis=1)
    grad_keys = jnp.einsum("hqs,hqd->hsd", grad_scores, queries, precision=HIGHEST) * score_scale
    return (grad_keys, grad_values, grad_bias)


def per_device(queries, compact_keys, compact_values, slot_bias, targets, positions, assignment):
    page_number = assignment[lax.axis_index("page")]
    local_heads = compact_keys.shape[0]
    slot_total = local_heads * lax.axis_size("head") * compact_keys.shape[1] * lax.axis_size("page")
    entry_count = slot_total * compact_keys.shape[2]
    query_count = lax.axis_size("query")
    heads_kept = max(local_heads // query_count, 1)
    query_parts = max(query_count // local_heads, 1)
    part_rows = queries.shape[1] // query_parts

    def split_items(array):
        width = array.shape[2]
        array = array.reshape(local_heads // heads_kept, heads_kept, query_parts, part_rows, width)
        array = jnp.transpose(array, (0, 2, 1, 3, 4))
        return array.reshape(query_count, heads_kept, part_rows, width)

    def join_items(array):
        width = array.shape[3]
        array = jnp.transpose(array, (1, 0, 2, 3))
        return array.reshape(heads_kept, query_count * part_rows, width)

    position_column = positions.astype(jnp.float32)[:, :, None]
    got_queries, got_targets, got_positions = (
        lax.all_to_all(split_items(queries), "query", split_axis=0, concat_axis=0, tiled=True),
        lax.all_to_all(split_items(targets), "query", split_axis=0, concat_axis=0, tiled=True),
        lax.all_to_all(
            split_items(position_column), "query", split_axis=0, concat_axis=0, tiled=True
        ),
    )
    group_queries = join_items(got_queries)
    group_targets = join_items(got_targets)
    group_positions = join_items(got_positions)[:, :, 0]
    visible = (page_number.astype(jnp.float32) <= jnp.floor(group_positions / PAGE_LEN))[:, :, None]
    query_index = lax.axis_index("query")
    first_head = query_index // query_parts * heads_kept
    key_state = lax.dynamic_slice_in_dim(compact_keys, first_head, heads_kept, 0)
    value_state = lax.dynamic_slice_in_dim(compact_values, first_head, heads_kept, 0)
    bias_state = lax.dynamic_slice_in_dim(slot_bias, first_head, heads_kept, 0)
    counted = (query_index % query_parts == 0).astype(jnp.float32)
    for repeat in range(STEPS):
        grads = local_gradients(
            group_queries, group_targets, visible, key_state, value_state, bias_state
        )
        for bit in range(query_parts.bit_length() - 1):
            partner = from_partner((grads[0], grads[1], grads[2]), "query", bit)
            grads = (grads[0] + partner[0], grads[1] + partner[1], grads[2] + partner[2])
        totals = lax.psum(
            squared_sums(grads[0], grads[1], grads[2]) * counted, ("page", "query", "head")
        )
        key_state, value_state, bias_state = apply_update(
            (key_state, value_state, bias_state), grads, totals, entry_count, slot_total
        )
    all_keys, all_values, all_bias = (
        lax.all_gather(key_state, "query", axis=0, tiled=True),
        lax.all_gather(value_state, "query", axis=0, tiled=True),
        lax.all_gather(bias_state, "query", axis=0, tiled=True),
    )
    slot_rows = compact_keys.shape[1]
    head_width = compact_keys.shape[2]
    all_keys = all_keys.reshape(
        local_heads // heads_kept, query_parts, heads_kept, slot_rows, head_width
    )[:, 0]
    all_values = all_values.reshape(
        local_heads // heads_kept, query_parts, heads_kept, slot_rows, head_width
    )[:, 0]
    all_bias = all_bias.reshape(local_heads // heads_kept, query_parts, heads_kept, slot_rows)[:, 0]
    return (
        all_keys.reshape(local_heads, slot_rows, head_width),
        all_values.reshape(local_heads, slot_rows, head_width),
        all_bias.reshape(local_heads, slot_rows),
    )


def solution(mesh):
    placed = (
        P("head", "query", None),
        P("head", "page", None),
        P("head", "page", None),
        P("head", "page"),
        P("head", "query", None),
        P("head", "query"),
        P(),
    )

    def program(*args):
        plan = direct_per_device if direct_plan_fits(mesh, args[0], args[1]) else per_device
        return jax.shard_map(
            plan,
            mesh=mesh,
            in_specs=placed,
            out_specs=(P("head", "page", None), P("head", "page", None), P("head", "page")),
            check_vma=False,
        )(*args)

    return program
```

```python
import itertools
import math

import jax
import jax.numpy as jnp
from jax import lax
from jax.experimental import pallas as pl
from jax.experimental.pallas import tpu as pltpu
from jax.sharding import PartitionSpec as P

STEPS = 2
PAGE_LEN = 32768


MASKED = -1e30
EPSILON = 1e-06
RATE_KEYS = 0.05
RATE_VALUES = 0.05
RATE_BIAS = 0.2
HIGHEST = lax.Precision.HIGHEST
TAIL = 8
CORES = 2


def exchange(value, **masks):
    axes = tuple(masks)
    sizes = [lax.axis_size(axis) for axis in axes]

    def flat(place):
        index = 0
        for size, at in zip(sizes, place):
            index = index * size + at
        return index

    pairs = [
        (flat(place), flat([at ^ mask for at, mask in zip(place, masks.values())]))
        for place in itertools.product(*map(range, sizes))
    ]
    return lax.ppermute(value, axes, pairs)


def halves(value):
    high = value.astype(jnp.bfloat16)
    return high, (value - high.astype(jnp.float32)).astype(jnp.bfloat16)


def dot(left, right, left_dim, right_dim):
    def one_pass(left_half, right_half):
        return lax.dot_general(
            left_half,
            right_half,
            (((left_dim,), (right_dim,)), ((), ())),
            preferred_element_type=jnp.float32,
        )

    cross = one_pass(left[0], right[1]) + one_pass(left[1], right[0])
    return one_pass(left[0], right[0]) + cross


def call(body, out_shapes, name, cost, operands, scratch=(), after=(), space=pltpu.VMEM, vmem=32):
    spaces = [space] * len(operands) + [pl.ANY] * len(after)
    count = len(operands)

    def without_after(*refs):
        body(*refs[:count], *refs[count + len(after) :])

    return pl.pallas_call(
        without_after,
        out_shape=[jax.ShapeDtypeStruct(shape, jnp.float32) for shape in out_shapes],
        in_specs=[pl.BlockSpec(memory_space=space) for space in spaces],
        out_specs=[pl.BlockSpec(memory_space=pltpu.VMEM) for _ in out_shapes],
        scratch_shapes=scratch,
        compiler_params=pltpu.CompilerParams(vmem_limit_bytes=vmem * 2**20),
        cost_estimate=pl.CostEstimate(flops=cost, bytes_accessed=2**20, transcendentals=0),
        name=name,
    )(*operands, *after)


def row_as_tail(row, width):
    rows = [row[:, at : at + width] for at in range(0, row.shape[1], width)]
    rows.append(jnp.zeros((TAIL - len(rows), width), row.dtype))
    return jnp.concatenate(rows, axis=0)


def tail_as_row(ref, start, count):
    return jnp.concatenate([ref[start + at : start + at + 1, :] for at in range(count)], axis=1)


def row_as_column(row, width):
    parts = []
    for at in range(0, row.shape[1], width):
        parts.append(jnp.broadcast_to(row[:, at : at + width], (width, width)).T)
    return jnp.concatenate(parts, axis=0)


def direct_plan_fits(mesh, queries, compact_keys):
    sizes = [mesh.shape[axis] for axis in ("page", "query", "head")]
    pages, query_devices, head_devices = sizes
    local_heads = queries.shape[0] // head_devices
    part_rows = queries.shape[1] // query_devices
    slot_rows = compact_keys.shape[1] // pages
    width = queries.shape[2]
    if any(size & (size - 1) for size in sizes) or pages < CORES or width % 128:
        return False
    if local_heads != CORES * query_devices:
        return False
    ranks = pages // CORES
    chunk = part_rows * query_devices // ranks
    return (
        part_rows * query_devices % ranks == 0
        and chunk % 128 == 0
        and part_rows % (8 * ranks) == 0
        and (part_rows // ranks % 128 == 0 or 1024 % (part_rows // ranks * 8) == 0)
        and slot_rows % width == 0
        and part_rows % width == 0
        and max(slot_rows, part_rows) < TAIL * width
    )


def direct_per_device(
    queries, compact_keys, compact_values, slot_bias, targets, positions, assignment
):
    local_heads, part_rows, width = queries.shape
    slot_rows = compact_keys.shape[1]
    query_devices = lax.axis_size("query")
    head_devices = lax.axis_size("head")
    ranks = lax.axis_size("page") // CORES
    query_rows = part_rows * query_devices
    chunk, piece = query_rows // ranks, part_rows // ranks
    slot_total = local_heads * head_devices * slot_rows * lax.axis_size("page")
    entry_total = slot_total * width
    score_scale = 1.0 / math.sqrt(width)
    slots = CORES * slot_rows
    devices = ranks * CORES * query_devices * head_devices
    pos_rows = part_rows // width
    bias_rows = slot_rows // width
    packed_rows = 2 * slot_rows + TAIL
    packed_shapes = [(packed_rows, width)] * 2
    matmul_cost = 3 * 2 * slots * query_rows * width

    def places():
        page = lax.axis_index("page")
        return page // CORES, page % CORES, lax.axis_index("query")

    def pack_queries(head, rank, queries, targets, out):
        rows = pl.ds(pl.multiple_of(rank * piece, piece), piece)
        return [
            (queries.at[head], out.at[pl.ds(0, part_rows)]),
            (targets.at[head, rows], out.at[pl.ds(part_rows, piece)]),
        ]

    def pack_state(head, keys, values, out):
        return [
            (keys.at[head], out.at[pl.ds(0, slot_rows)]),
            (values.at[head], out.at[pl.ds(slot_rows, slot_rows)]),
        ]

    def start_all(copies, sems, first=0):
        copies = [
            pltpu.make_async_copy(source, target, sems.at[first + at])
            for at, (source, target) in enumerate(copies)
        ]
        for copy in copies:
            copy.start()
        return copies

    def position_tail(head, positions_ref):
        return row_as_tail(positions_ref[pl.ds(head, 1), :].astype(jnp.float32), width)

    def state_tail(head, page, bias_ref, assignment_ref):
        page_start = (assignment_ref[page] * PAGE_LEN).astype(jnp.float32)
        tail = row_as_tail(bias_ref[pl.ds(head, 1), :], width)
        return jnp.concatenate(
            [tail[: TAIL - 1], jnp.full((1, width), page_start, jnp.float32)], axis=0
        )

    def send_body(
        queries, keys, values, biases, targets, positions, assignment, state_out, *refs
    ):
        query_outs = refs[: query_devices - 1]
        bias_ref, positions_ref, assignment_ref, sems = refs[query_devices - 1 :]
        rank, core, me = places()
        heads = [CORES * (me ^ turn) + core for turn in range(1, query_devices)]
        mate_head = CORES * me + (core ^ 1)
        small = start_all(
            [(assignment, assignment_ref), (positions, positions_ref), (biases, bias_ref)], sems
        )
        copies = pack_state(mate_head, keys, values, state_out)
        for head, out in zip(heads, query_outs):
            copies += pack_queries(head, rank, queries, targets, out)
        copies = start_all(copies, sems, 3)
        for copy in small:
            copy.wait()
        state_out[2 * slot_rows :, :] = state_tail(
            mate_head, CORES * rank + core, bias_ref, assignment_ref
        )
        for head, out in zip(heads, query_outs):
            out[part_rows + piece :, :] = position_tail(head, positions_ref)
        for copy in copies:
            copy.wait()

    def own_body(
        queries, keys, values, biases, targets, positions, assignment, state_out, query_out, *refs
    ):
        bias_ref, positions_ref, assignment_ref, sems = refs
        rank, core, me = places()
        head = CORES * me + core
        small = start_all(
            [(assignment, assignment_ref), (positions, positions_ref), (biases, bias_ref)], sems
        )
        copies = pack_state(head, keys, values, state_out)
        copies += pack_queries(head, rank, queries, targets, query_out)
        copies = start_all(copies, sems, 3)
        for copy in small:
            copy.wait()
        state_out[2 * slot_rows :, :] = state_tail(
            head, CORES * rank + core, bias_ref, assignment_ref
        )
        query_out[part_rows + piece :, :] = position_tail(head, positions_ref)
        for copy in copies:
            copy.wait()

    state_shape, query_shape = (packed_rows, width), (part_rows + piece + TAIL, width)
    small_scratch = [
        pltpu.VMEM(slot_bias.shape, jnp.float32),
        pltpu.VMEM(positions.shape, jnp.int32),
        pltpu.SMEM(assignment.shape, jnp.int32),
    ]
    arguments = [
        queries, compact_keys, compact_values, slot_bias, targets, positions, assignment
    ]
    mate_state, *sent_queries = call(
        send_body,
        [state_shape] + [query_shape] * (query_devices - 1),
        "pack",
        2**20,
        arguments,
        small_scratch + [pltpu.SemaphoreType.DMA((3 + 2 * query_devices,))],
        space=pl.ANY,
        vmem=60,
    )
    own_state, own_queries = call(
        own_body,
        [state_shape, query_shape],
        "own",
        2**24,
        arguments,
        small_scratch + [pltpu.SemaphoreType.DMA((7,))],
        space=pl.ANY,
    )
    query_parts = [own_queries] + [
        exchange(sent_queries[turn - 1], query=turn) for turn in range(1, query_devices)
    ]
    states = [own_state, exchange(mate_state, page=1)]

    def in_columns(parts, axis):
        return jnp.concatenate(
            [
                lax.slice_in_dim(part, at * piece, (at + 1) * piece, axis=axis)
                for at in range(ranks)
                for part in parts
            ],
            axis=axis,
        )

    def read_queries(query_refs):
        return halves(in_columns([ref[:part_rows, :] for ref in query_refs], 0))

    def part_of(ref, at):
        return ref.at[pl.ds(at * packed_rows, packed_rows)]

    def parts_of(refs):
        return refs if len(refs) == CORES else [part_of(refs[0], at) for at in range(CORES)]

    def step_sizes(tile_refs):
        row = jnp.sum(tile_refs[0][...], axis=0)
        return (
            RATE_KEYS / jnp.sqrt(row[:, 0:1] / entry_total + EPSILON),
            RATE_VALUES / jnp.sqrt(row[:, 1:2] / entry_total + EPSILON),
            RATE_BIAS / jnp.sqrt(row[:, 2:3] / slot_total + EPSILON),
        )

    def updated(state_ref, grad_ref, sizes):
        key_end, value_end = slot_rows, 2 * slot_rows
        return (
            state_ref[:key_end, :] - sizes[0] * grad_ref[:key_end, :],
            state_ref[key_end:value_end, :] - sizes[1] * grad_ref[key_end:value_end, :],
            state_ref[value_end:, :] - sizes[2] * grad_ref[value_end:, :],
        )

    def forward(state_refs, query_refs, chunk_outs, weights_out, max_out, chunks):
        rank, _, _ = places()
        all_queries = read_queries(query_refs)
        position_row = in_columns(
            [tail_as_row(ref, part_rows + piece, pos_rows) for ref in query_refs], 1
        )
        all_scores, all_visible = [], []
        for at, ref in enumerate(state_refs):
            scores = dot(halves(ref[:slot_rows, :]), all_queries, 1, 1) * score_scale
            bias = row_as_column(tail_as_row(ref, 2 * slot_rows, bias_rows), width)
            scores = scores + jnp.concatenate([bias] * (query_rows // width), axis=1)
            page_start = ref[packed_rows - 1 : packed_rows, 0:1]
            visible = jnp.broadcast_to(position_row >= page_start, scores.shape)
            all_scores.append(jnp.where(visible, scores, MASKED))
            all_visible.append(visible)
        row_max = jnp.max(all_scores[0], axis=0, keepdims=True)
        for scores in all_scores[1:]:
            row_max = jnp.maximum(row_max, jnp.max(scores, axis=0, keepdims=True))
        row_total = jnp.zeros_like(row_max)
        row_sum = jnp.zeros((width, query_rows), jnp.float32)
        for at, ref in enumerate(state_refs):
            weights = jnp.where(all_visible[at], jnp.exp(all_scores[at] - row_max), 0.0)
            weights_out[at * slot_rows : (at + 1) * slot_rows, :] = weights
            row_total = row_total + jnp.sum(weights, axis=0, keepdims=True)
            values = halves(ref[slot_rows : 2 * slot_rows, :])
            row_sum = row_sum + dot(values, halves(weights), 0, 0)
        max_out[...] = jnp.broadcast_to(row_max, (TAIL, query_rows))
        tail = jnp.concatenate(
            [row_max, row_total, jnp.zeros((TAIL - 2, query_rows), jnp.float32)], axis=0
        )
        for at in range(ranks):
            columns = slice(at * chunk, (at + 1) * chunk)
            chunks[at, :width, :] = row_sum[:, columns]
            chunks[at, width:, :] = tail[:, columns]
        for turn in range(ranks):
            chunk_outs[turn][...] = chunks[rank ^ turn]

    chunk_shape = (width + TAIL, chunk)
    forward_shapes = [chunk_shape] * ranks + [(slots, query_rows), (TAIL, query_rows)]
    chunk_scratch = [pltpu.VMEM((ranks,) + chunk_shape, jnp.float32)]

    fold = max(1, 128 // piece)
    folded, columns = width // fold, fold * piece
    piece_shape = (folded + TAIL, columns)
    piece_scratch = [pltpu.VMEM((ranks,) + piece_shape, jnp.float32)]

    def fold_rows(value):
        groups = [value[at * folded : (at + 1) * folded, :] for at in range(fold)]
        return jnp.concatenate(groups, axis=1)

    def unfold_rows(value):
        groups = [value[:, at * piece : (at + 1) * piece] for at in range(fold)]
        return jnp.concatenate(groups, axis=0)

    def rows_tail(rows):
        empty = jnp.zeros((TAIL - len(rows), columns), jnp.float32)
        return jnp.concatenate(rows + [empty], axis=0)

    def part_body(*refs):
        state_refs, (query_ref, *refs) = refs[:CORES], refs[CORES:]
        piece_outs, (weights_out, max_out, pieces) = refs[:ranks], refs[ranks:]
        rank, _, _ = places()
        queries = halves(query_ref[:part_rows, :])
        position_row = tail_as_row(query_ref, part_rows + piece, pos_rows)
        all_scores, all_visible = [], []
        for ref in state_refs:
            scores = dot(halves(ref[:slot_rows, :]), queries, 1, 1) * score_scale
            bias = row_as_column(tail_as_row(ref, 2 * slot_rows, bias_rows), width)
            scores = scores + jnp.concatenate([bias] * (part_rows // width), axis=1)
            page_start = ref[packed_rows - 1 : packed_rows, 0:1]
            visible = jnp.broadcast_to(position_row >= page_start, scores.shape)
            all_scores.append(jnp.where(visible, scores, MASKED))
            all_visible.append(visible)
        row_max = jnp.max(all_scores[0], axis=0, keepdims=True)
        for scores in all_scores[1:]:
            row_max = jnp.maximum(row_max, jnp.max(scores, axis=0, keepdims=True))
        row_total = jnp.zeros_like(row_max)
        row_sum = jnp.zeros((width, part_rows), jnp.float32)
        for at, ref in enumerate(state_refs):
            weights = jnp.where(all_visible[at], jnp.exp(all_scores[at] - row_max), 0.0)
            weights_out[at * slot_rows : (at + 1) * slot_rows, :] = weights
            row_total = row_total + jnp.sum(weights, axis=0, keepdims=True)
            values = halves(ref[slot_rows : 2 * slot_rows, :])
            row_sum = row_sum + dot(values, halves(weights), 0, 0)
        max_out[...] = jnp.broadcast_to(row_max, (TAIL, part_rows))
        for at in range(ranks):
            own = slice(at * piece, (at + 1) * piece)
            pieces[at, :folded, :] = fold_rows(row_sum[:, own])
            pieces[at, folded:, :] = rows_tail(
                [jnp.concatenate([row[:, own]] * fold, axis=1) for row in (row_max, row_total)]
            )
        for turn in range(ranks):
            piece_outs[turn][...] = pieces[rank ^ turn]

    part_shapes = [piece_shape] * ranks + [(slots, part_rows), (TAIL, part_rows)]

    def next_body(*refs):
        state_refs, refs = refs[:2], refs[2:]
        query_refs, refs = refs[:query_devices], refs[query_devices:]
        grad_refs, refs = refs[:2], refs[2:]
        tile_refs, refs = refs[: len(tiles)], refs[len(tiles) :]
        state_outs, refs = parts_of(refs[:1]), refs[1:]
        chunk_outs, refs = refs[:ranks], refs[ranks:]
        sizes = step_sizes(tile_refs)
        for at in range(2):
            keys, values, bias = updated(state_refs[at], grad_refs[at], sizes)
            state_outs[at][:slot_rows, :] = keys
            state_outs[at][slot_rows : 2 * slot_rows, :] = values
            state_outs[at][2 * slot_rows :, :] = bias
        forward(state_outs, query_refs, chunk_outs, *refs)

    def merged_chunk(query_refs, sums, maxima, totals, out):
        targets = jnp.concatenate(
            [ref[part_rows : part_rows + piece, :] for ref in query_refs], axis=0
        )
        row_max = maxima[0]
        for other in maxima[1:]:
            row_max = jnp.maximum(row_max, other)
        row_total = jnp.zeros_like(row_max)
        row_sum = jnp.zeros((width, chunk), jnp.float32)
        for part_sum, part_max, part_total in zip(sums, maxima, totals):
            factor = jnp.exp(part_max - row_max)
            row_total = row_total + part_total * factor
            row_sum = row_sum + part_sum * factor
        output = row_sum / row_total
        residual = output - targets.T
        row_delta = jnp.sum(residual * output, axis=0, keepdims=True)
        out[:width, :] = residual
        out[width:, :] = jnp.concatenate(
            [row_max, row_total, row_delta, jnp.zeros((TAIL - 3, chunk), jnp.float32)], axis=0
        )

    def first_merge_body(*refs):
        query_refs, (*piece_refs, merged_out) = refs[:query_devices], refs[query_devices:]

        def joined(read):
            return [
                jnp.concatenate([read(ref) for ref in piece_refs[turn::ranks]], axis=1)
                for turn in range(ranks)
            ]

        merged_chunk(
            query_refs,
            joined(lambda ref: unfold_rows(ref[:folded, :])),
            joined(lambda ref: ref[folded : folded + 1, :piece]),
            joined(lambda ref: ref[folded + 1 : folded + 2, :piece]),
            merged_out,
        )

    def merge_body(*refs):
        query_refs, (*chunk_refs, merged_out) = refs[:query_devices], refs[query_devices:]
        merged_chunk(
            query_refs,
            [ref[:width, :] for ref in chunk_refs],
            [ref[width : width + 1, :] for ref in chunk_refs],
            [ref[width + 1 : width + 2, :] for ref in chunk_refs],
            merged_out,
        )

    def backward_body(*refs):
        weights_refs, refs = refs[: len(weights)], refs[len(weights) :]
        max_refs, refs = refs[: len(weights)], refs[len(weights) :]
        state_refs, refs = parts_of(refs[: len(states)]), refs[len(states) :]
        query_refs, refs = refs[:query_devices], refs[query_devices:]
        merged_refs, refs = refs[:ranks], refs[ranks:]
        grad_outs, (squares_out, chunks) = refs[:2], refs[2:]
        rank, _, _ = places()
        for turn in range(ranks):
            chunks[rank ^ turn] = merged_refs[turn][...]
        if len(weights_refs) == 1:
            joined = jnp.concatenate([chunks[at] for at in range(ranks)], axis=1)
            all_queries = read_queries(query_refs)
        else:
            joined = jnp.concatenate(
                [
                    chunks[at, :, part * piece : (part + 1) * piece]
                    for part in range(query_devices)
                    for at in range(ranks)
                ],
                axis=1,
            )
            all_queries = halves(
                jnp.concatenate([ref[:part_rows, :] for ref in query_refs], axis=0)
            )
        residual = joined[:width, :]
        row_max, row_total, row_delta = (
            joined[width + at : width + at + 1, :] for at in range(3)
        )
        residual = halves(residual)
        maxima = jnp.concatenate([ref[0:1, :] for ref in max_refs], axis=1)
        factor = jnp.exp(maxima - row_max) / row_total
        ones = jnp.ones((TAIL, query_rows), jnp.bfloat16)
        ones = (ones, jnp.zeros_like(ones))
        squares = [jnp.zeros((1, width), jnp.float32)] * 3
        for at, (ref, out) in enumerate(zip(state_refs, grad_outs)):
            rows = slice(at * slot_rows, (at + 1) * slot_rows)
            attention = jnp.concatenate([part[rows, :] for part in weights_refs], axis=1) * factor
            grad_values = dot(halves(attention), residual, 1, 1)
            grad_probs = dot(halves(ref[slot_rows : 2 * slot_rows, :]), residual, 1, 0)
            grad_scores = halves(attention * (grad_probs - row_delta))
            grad_keys = dot(grad_scores, all_queries, 1, 0) * score_scale
            grad_bias = row_as_tail(dot(ones, grad_scores, 1, 1)[0:1, :], width)
            out[:slot_rows, :] = grad_keys
            out[slot_rows : 2 * slot_rows, :] = grad_values
            out[2 * slot_rows :, :] = grad_bias
            for which, grad in enumerate((grad_keys, grad_values, grad_bias)):
                squares[which] = squares[which] + jnp.sum(grad * grad, axis=0, keepdims=True)
        lanes = lax.broadcasted_iota(jnp.int32, (1, width), 1)
        row = jnp.zeros((1, width), jnp.float32)
        for which, square in enumerate(squares):
            row = jnp.where(lanes == which, jnp.sum(square, axis=1, keepdims=True), row)
        for at in range(devices):
            squares_out[at] = row

    def mate_body(*refs):
        *state_refs, out_ref = refs
        for at, ref in enumerate(state_refs):
            out_ref[pl.ds(at * packed_rows, packed_rows), :] = part_of(ref, 1)[...]

    out_masks = list(itertools.product(range(query_devices), range(CORES)))

    def to_output(packs, mask):
        if mask == (0, 0):
            return packs[0]
        return exchange(packs[mask[1]], page=mask[1], query=mask[0])

    for repeat in range(STEPS):
        last = repeat == STEPS - 1
        if repeat == 0:
            sums, weights, maxima = [], [], []
            for query_part in query_parts:
                *pieces, part_weights, part_max = call(
                    part_body,
                    part_shapes,
                    "forward",
                    2 * matmul_cost // query_devices,
                    states + [query_part],
                    piece_scratch,
                    after=maxima[-1:],
                )
                arrived = {
                    turn: exchange(pieces[turn], page=CORES * turn)
                    for turn in reversed(range(1, ranks))
                }
                sums += list(arrived.values()) + pieces[:1]
                weights.append(part_weights)
                maxima.append(part_max)
        else:
            new_state, *chunk_parts, part_weights, part_max = call(
                next_body,
                [(CORES * packed_rows, width)] + forward_shapes,
                "update_forward",
                2 * matmul_cost,
                states + query_parts + grads + tiles,
                chunk_scratch,
            )
            states, weights, maxima = [new_state], [part_weights], [part_max]
            arrived = {
                turn: exchange(chunk_parts[turn], page=CORES * turn)
                for turn in reversed(range(1, ranks))
            }
            sums = chunk_parts[:1] + list(arrived.values())
            new_states = states + [
                exchange(states[0], query=turn) for turn in range(1, query_devices)
            ]
        (merged,) = call(
            merge_body if repeat else first_merge_body,
            [chunk_shape],
            "merge",
            2**20,
            query_parts + sums,
        )
        all_merged = [merged] + [
            exchange(merged, page=CORES * turn) for turn in range(1, ranks)
        ]
        if repeat:
            (for_mate,) = call(
                mate_body,
                [(query_devices * packed_rows, width)],
                "mate_parts",
                2**20,
                new_states,
                after=all_merged[1:],
            )
            from_mate = exchange(for_mate, page=1)
        own_grad, mate_grad, squares = call(
            backward_body,
            packed_shapes + [(devices, 1, width)],
            "backward",
            3 * matmul_cost,
            weights + maxima + states + query_parts + all_merged,
            scratch=chunk_scratch,
        )
        grads = [own_grad, mate_grad]
        if last:
            all_grads = [to_output(grads, mask) for mask in out_masks]
        tiles = [
            lax.all_to_all(
                squares, ("page", "query", "head"), split_axis=0, concat_axis=0, tiled=True
            )
        ]

    def last_body(*refs):
        state_refs, (mate_ref, *refs) = refs[:query_devices], refs[query_devices:]
        state_refs = [
            part_of(mate_ref, turn) if flip else part_of(state_refs[turn], 0)
            for turn, flip in out_masks
        ]
        grad_refs, refs = refs[:local_heads], refs[local_heads:]
        tile_refs, (keys_out, values_out, bias_out) = refs[: len(tiles)], refs[len(tiles) :]
        _, core, me = places()
        sizes = step_sizes(tile_refs)
        for at, (turn, flip) in enumerate(out_masks):
            keys, values, bias = updated(state_refs[at], grad_refs[at], sizes)
            head = CORES * (me ^ turn) + (core ^ flip)
            keys_out[head] = keys
            values_out[head] = values
            bias_row = jnp.concatenate([bias[row : row + 1] for row in range(bias_rows)], axis=1)
            bias_out[pl.ds(head, 1), :] = bias_row

    return tuple(
        call(
            last_body,
            [compact_keys.shape, compact_values.shape, slot_bias.shape],
            "last_update",
            2**20,
            new_states + [from_mate] + all_grads + tiles,
        )
    )


def from_partner(value, axis, stride):
    mask = 2**stride
    pairs = [(source, source ^ mask) for source in range(lax.axis_size(axis))]
    return lax.ppermute(value, axis, pairs)


def squared_sums(grad_keys, grad_values, grad_bias):
    return jnp.stack(
        [
            jnp.sum(grad_keys * grad_keys),
            jnp.sum(grad_values * grad_values),
            jnp.sum(grad_bias * grad_bias),
        ]
    )


def apply_update(states, grads, totals, entry_count, slot_total):
    key_state, value_state, bias_state = states
    grad_keys, grad_values, grad_bias = grads
    rms_keys = jnp.sqrt(totals[0] / entry_count + EPSILON)
    rms_values = jnp.sqrt(totals[1] / entry_count + EPSILON)
    rms_bias = jnp.sqrt(totals[2] / slot_total + EPSILON)
    return (
        key_state - RATE_KEYS * grad_keys / rms_keys,
        value_state - RATE_VALUES * grad_values / rms_values,
        bias_state - RATE_BIAS * grad_bias / rms_bias,
    )


def local_gradients(queries, targets, visible, compact_keys, compact_values, slot_bias):
    score_scale = 1.0 / math.sqrt(queries.shape[2])
    scores = jnp.einsum("hqd,hsd->hqs", queries, compact_keys, precision=HIGHEST) * score_scale
    scores = jnp.where(visible, scores + slot_bias[:, None, :], MASKED)
    local_max = jnp.max(scores, axis=2)
    row_max = lax.pmax(local_max, "page")
    weights = jnp.where(visible, jnp.exp(scores - row_max[:, :, None]), 0.0)
    local_sum = jnp.einsum("hqs,hsd->hqd", weights, compact_values, precision=HIGHEST)
    row_total, row_sum = lax.psum((jnp.sum(weights, axis=2), local_sum), "page")
    attention = weights / row_total[:, :, None]
    output = row_sum / row_total[:, :, None]
    residual = output - targets
    grad_values = jnp.einsum("hqs,hqd->hsd", attention, residual, precision=HIGHEST)
    row_delta = jnp.sum(residual * output, axis=2)
    grad_probs = jnp.einsum("hqd,hsd->hqs", residual, compact_values, precision=HIGHEST)
    grad_scores = attention * (grad_probs - row_delta[:, :, None])
    grad_bias = jnp.sum(grad_scores, axis=1)
    grad_keys = jnp.einsum("hqs,hqd->hsd", grad_scores, queries, precision=HIGHEST) * score_scale
    return (grad_keys, grad_values, grad_bias)


def per_device(queries, compact_keys, compact_values, slot_bias, targets, positions, assignment):
    page_number = assignment[lax.axis_index("page")]
    local_heads = compact_keys.shape[0]
    slot_total = local_heads * lax.axis_size("head") * compact_keys.shape[1] * lax.axis_size("page")
    entry_count = slot_total * compact_keys.shape[2]
    query_count = lax.axis_size("query")
    heads_kept = max(local_heads // query_count, 1)
    query_parts = max(query_count // local_heads, 1)
    part_rows = queries.shape[1] // query_parts

    def split_items(array):
        width = array.shape[2]
        array = array.reshape(local_heads // heads_kept, heads_kept, query_parts, part_rows, width)
        array = jnp.transpose(array, (0, 2, 1, 3, 4))
        return array.reshape(query_count, heads_kept, part_rows, width)

    def join_items(array):
        width = array.shape[3]
        array = jnp.transpose(array, (1, 0, 2, 3))
        return array.reshape(heads_kept, query_count * part_rows, width)

    position_column = positions.astype(jnp.float32)[:, :, None]
    got_queries, got_targets, got_positions = (
        lax.all_to_all(split_items(queries), "query", split_axis=0, concat_axis=0, tiled=True),
        lax.all_to_all(split_items(targets), "query", split_axis=0, concat_axis=0, tiled=True),
        lax.all_to_all(
            split_items(position_column), "query", split_axis=0, concat_axis=0, tiled=True
        ),
    )
    group_queries = join_items(got_queries)
    group_targets = join_items(got_targets)
    group_positions = join_items(got_positions)[:, :, 0]
    visible = (page_number.astype(jnp.float32) <= jnp.floor(group_positions / PAGE_LEN))[:, :, None]
    query_index = lax.axis_index("query")
    first_head = query_index // query_parts * heads_kept
    key_state = lax.dynamic_slice_in_dim(compact_keys, first_head, heads_kept, 0)
    value_state = lax.dynamic_slice_in_dim(compact_values, first_head, heads_kept, 0)
    bias_state = lax.dynamic_slice_in_dim(slot_bias, first_head, heads_kept, 0)
    counted = (query_index % query_parts == 0).astype(jnp.float32)
    for repeat in range(STEPS):
        grads = local_gradients(
            group_queries, group_targets, visible, key_state, value_state, bias_state
        )
        for bit in range(query_parts.bit_length() - 1):
            partner = from_partner((grads[0], grads[1], grads[2]), "query", bit)
            grads = (grads[0] + partner[0], grads[1] + partner[1], grads[2] + partner[2])
        totals = lax.psum(
            squared_sums(grads[0], grads[1], grads[2]) * counted, ("page", "query", "head")
        )
        key_state, value_state, bias_state = apply_update(
            (key_state, value_state, bias_state), grads, totals, entry_count, slot_total
        )
    all_keys, all_values, all_bias = (
        lax.all_gather(key_state, "query", axis=0, tiled=True),
        lax.all_gather(value_state, "query", axis=0, tiled=True),
        lax.all_gather(bias_state, "query", axis=0, tiled=True),
    )
    slot_rows = compact_keys.shape[1]
    head_width = compact_keys.shape[2]
    all_keys = all_keys.reshape(
        local_heads // heads_kept, query_parts, heads_kept, slot_rows, head_width
    )[:, 0]
    all_values = all_values.reshape(
        local_heads // heads_kept, query_parts, heads_kept, slot_rows, head_width
    )[:, 0]
    all_bias = all_bias.reshape(local_heads // heads_kept, query_parts, heads_kept, slot_rows)[:, 0]
    return (
        all_keys.reshape(local_heads, slot_rows, head_width),
        all_values.reshape(local_heads, slot_rows, head_width),
        all_bias.reshape(local_heads, slot_rows),
    )


def solution(mesh):
    placed = (
        P("head", "query", None),
        P("head", "page", None),
        P("head", "page", None),
        P("head", "page"),
        P("head", "query", None),
        P("head", "query"),
        P(),
    )

    def program(*args):
        plan = direct_per_device if direct_plan_fits(mesh, args[0], args[1]) else per_device
        return jax.shard_map(
            plan,
            mesh=mesh,
            in_specs=placed,
            out_specs=(P("head", "page", None), P("head", "page", None), P("head", "page")),
            check_vma=False,
        )(*args)

    return program
```

```python
import itertools
import math

import jax
import jax.numpy as jnp
from jax import lax
from jax.experimental import pallas as pl
from jax.experimental.pallas import tpu as pltpu
from jax.sharding import PartitionSpec as P

STEPS = 2
PAGE_LEN = 32768


MASKED = -1e30
EPSILON = 1e-06
RATE_KEYS = 0.05
RATE_VALUES = 0.05
RATE_BIAS = 0.2
HIGHEST = lax.Precision.HIGHEST
TAIL = 8
CORES = 2


def exchange(value, **masks):
    axes = tuple(masks)
    sizes = [lax.axis_size(axis) for axis in axes]

    def flat(place):
        index = 0
        for size, at in zip(sizes, place):
            index = index * size + at
        return index

    pairs = [
        (flat(place), flat([at ^ mask for at, mask in zip(place, masks.values())]))
        for place in itertools.product(*map(range, sizes))
    ]
    return lax.ppermute(value, axes, pairs)


def halves(value):
    high = value.astype(jnp.bfloat16)
    return high, (value - high.astype(jnp.float32)).astype(jnp.bfloat16)


def dot(left, right, left_dim, right_dim):
    def one_pass(left_half, right_half):
        return lax.dot_general(
            left_half,
            right_half,
            (((left_dim,), (right_dim,)), ((), ())),
            preferred_element_type=jnp.float32,
        )

    cross = one_pass(left[0], right[1]) + one_pass(left[1], right[0])
    return one_pass(left[0], right[0]) + cross


def call(body, out_shapes, name, cost, operands, scratch=(), after=(), space=pltpu.VMEM, vmem=32):
    spaces = [space] * len(operands) + [pl.ANY] * len(after)
    count = len(operands)

    def without_after(*refs):
        body(*refs[:count], *refs[count + len(after) :])

    return pl.pallas_call(
        without_after,
        out_shape=[jax.ShapeDtypeStruct(shape, jnp.float32) for shape in out_shapes],
        in_specs=[pl.BlockSpec(memory_space=space) for space in spaces],
        out_specs=[pl.BlockSpec(memory_space=pltpu.VMEM) for _ in out_shapes],
        scratch_shapes=scratch,
        compiler_params=pltpu.CompilerParams(vmem_limit_bytes=vmem * 2**20),
        cost_estimate=pl.CostEstimate(flops=cost, bytes_accessed=2**20, transcendentals=0),
        name=name,
    )(*operands, *after)


def row_as_tail(row, width):
    rows = [row[:, at : at + width] for at in range(0, row.shape[1], width)]
    rows.append(jnp.zeros((TAIL - len(rows), width), row.dtype))
    return jnp.concatenate(rows, axis=0)


def tail_as_row(ref, start, count):
    return jnp.concatenate([ref[start + at : start + at + 1, :] for at in range(count)], axis=1)


def row_as_column(row, width):
    parts = []
    for at in range(0, row.shape[1], width):
        parts.append(jnp.broadcast_to(row[:, at : at + width], (width, width)).T)
    return jnp.concatenate(parts, axis=0)


def direct_plan_fits(mesh, queries, compact_keys):
    sizes = [mesh.shape[axis] for axis in ("page", "query", "head")]
    pages, query_devices, head_devices = sizes
    local_heads = queries.shape[0] // head_devices
    part_rows = queries.shape[1] // query_devices
    slot_rows = compact_keys.shape[1] // pages
    width = queries.shape[2]
    if any(size & (size - 1) for size in sizes) or pages < CORES or width % 128:
        return False
    if local_heads != CORES * query_devices:
        return False
    ranks = pages // CORES
    chunk = part_rows * query_devices // ranks
    return (
        part_rows * query_devices % ranks == 0
        and chunk % 128 == 0
        and part_rows % (8 * ranks) == 0
        and (part_rows // ranks % 128 == 0 or 1024 % (part_rows // ranks * 8) == 0)
        and slot_rows % width == 0
        and part_rows % width == 0
        and max(slot_rows, part_rows) < TAIL * width
    )


def direct_per_device(
    queries, compact_keys, compact_values, slot_bias, targets, positions, assignment
):
    local_heads, part_rows, width = queries.shape
    slot_rows = compact_keys.shape[1]
    query_devices = lax.axis_size("query")
    head_devices = lax.axis_size("head")
    ranks = lax.axis_size("page") // CORES
    query_rows = part_rows * query_devices
    chunk, piece = query_rows // ranks, part_rows // ranks
    slot_total = local_heads * head_devices * slot_rows * lax.axis_size("page")
    entry_total = slot_total * width
    score_scale = 1.0 / math.sqrt(width)
    slots = CORES * slot_rows
    devices = ranks * CORES * query_devices * head_devices
    pos_rows = part_rows // width
    bias_rows = slot_rows // width
    packed_rows = 2 * slot_rows + TAIL
    packed_shapes = [(packed_rows, width)] * 2
    matmul_cost = 3 * 2 * slots * query_rows * width

    def places():
        page = lax.axis_index("page")
        return page // CORES, page % CORES, lax.axis_index("query")

    def to_device(value, **masks):
        masks = {axis: mask for axis, mask in masks.items() if mask}
        return exchange(value, **masks) if masks else value

    def pack_queries(head, rank, queries, targets, out):
        rows = pl.ds(pl.multiple_of(rank * piece, piece), piece)
        return [
            (queries.at[head], out.at[pl.ds(0, part_rows)]),
            (targets.at[head, rows], out.at[pl.ds(part_rows, piece)]),
        ]

    def pack_state(head, keys, values, out):
        return [
            (keys.at[head], out.at[pl.ds(0, slot_rows)]),
            (values.at[head], out.at[pl.ds(slot_rows, slot_rows)]),
        ]

    def start_all(copies, sems, first=0):
        copies = [
            pltpu.make_async_copy(source, target, sems.at[first + at])
            for at, (source, target) in enumerate(copies)
        ]
        for copy in copies:
            copy.start()
        return copies

    def position_tail(head, positions_ref):
        return row_as_tail(positions_ref[pl.ds(head, 1), :].astype(jnp.float32), width)

    def state_tail(head, page, bias_ref, assignment_ref):
        page_start = (assignment_ref[page] * PAGE_LEN).astype(jnp.float32)
        tail = row_as_tail(bias_ref[pl.ds(head, 1), :], width)
        return jnp.concatenate(
            [tail[: TAIL - 1], jnp.full((1, width), page_start, jnp.float32)], axis=0
        )

    def send_body(
        queries, keys, values, biases, targets, positions, assignment, state_out, *refs
    ):
        query_outs = refs[: query_devices - 1]
        bias_ref, positions_ref, assignment_ref, sems = refs[query_devices - 1 :]
        rank, core, me = places()
        heads = [CORES * (me ^ turn) + core for turn in range(1, query_devices)]
        mate_head = CORES * me + (core ^ 1)
        small = start_all(
            [(assignment, assignment_ref), (positions, positions_ref), (biases, bias_ref)], sems
        )
        copies = pack_state(mate_head, keys, values, state_out)
        for head, out in zip(heads, query_outs):
            copies += pack_queries(head, rank, queries, targets, out)
        copies = start_all(copies, sems, 3)
        for copy in small:
            copy.wait()
        state_out[2 * slot_rows :, :] = state_tail(
            mate_head, CORES * rank + core, bias_ref, assignment_ref
        )
        for head, out in zip(heads, query_outs):
            out[part_rows + piece :, :] = position_tail(head, positions_ref)
        for copy in copies:
            copy.wait()

    def own_body(
        queries, keys, values, biases, targets, positions, assignment, state_out, query_out, *refs
    ):
        bias_ref, positions_ref, assignment_ref, sems = refs
        rank, core, me = places()
        head = CORES * me + core
        small = start_all(
            [(assignment, assignment_ref), (positions, positions_ref), (biases, bias_ref)], sems
        )
        copies = pack_state(head, keys, values, state_out)
        copies += pack_queries(head, rank, queries, targets, query_out)
        copies = start_all(copies, sems, 3)
        for copy in small:
            copy.wait()
        state_out[2 * slot_rows :, :] = state_tail(
            head, CORES * rank + core, bias_ref, assignment_ref
        )
        query_out[part_rows + piece :, :] = position_tail(head, positions_ref)
        for copy in copies:
            copy.wait()

    state_shape, query_shape = (packed_rows, width), (part_rows + piece + TAIL, width)
    small_scratch = [
        pltpu.VMEM(slot_bias.shape, jnp.float32),
        pltpu.VMEM(positions.shape, jnp.int32),
        pltpu.SMEM(assignment.shape, jnp.int32),
    ]
    arguments = [
        queries, compact_keys, compact_values, slot_bias, targets, positions, assignment
    ]
    mate_state, *sent_queries = call(
        send_body,
        [state_shape] + [query_shape] * (query_devices - 1),
        "pack",
        2**20,
        arguments,
        small_scratch + [pltpu.SemaphoreType.DMA((3 + 2 * query_devices,))],
        space=pl.ANY,
        vmem=60,
    )
    own_state, own_queries = call(
        own_body,
        [state_shape, query_shape],
        "own",
        2**24,
        arguments,
        small_scratch + [pltpu.SemaphoreType.DMA((7,))],
        space=pl.ANY,
    )
    packs = [own_queries] + list(sent_queries)

    def query_part(turn, part):
        return to_device(packs[part], query=turn ^ part)

    query_parts = [query_part(0, part) for part in range(query_devices)]
    states = [own_state, exchange(mate_state, page=1)]

    def in_columns(parts, axis):
        return jnp.concatenate(
            [
                lax.slice_in_dim(part, at * piece, (at + 1) * piece, axis=axis)
                for at in range(ranks)
                for part in parts
            ],
            axis=axis,
        )

    def read_queries(query_refs):
        return halves(in_columns([ref[:part_rows, :] for ref in query_refs], 0))

    def part_of(ref, at):
        return ref.at[pl.ds(at * packed_rows, packed_rows)]

    def parts_of(refs):
        return refs if len(refs) == CORES else [part_of(refs[0], at) for at in range(CORES)]

    def step_sizes(tile_refs):
        row = jnp.sum(tile_refs[0][...], axis=0)
        return (
            RATE_KEYS / jnp.sqrt(row[:, 0:1] / entry_total + EPSILON),
            RATE_VALUES / jnp.sqrt(row[:, 1:2] / entry_total + EPSILON),
            RATE_BIAS / jnp.sqrt(row[:, 2:3] / slot_total + EPSILON),
        )

    def updated(state_ref, grad_ref, sizes):
        key_end, value_end = slot_rows, 2 * slot_rows
        return (
            state_ref[:key_end, :] - sizes[0] * grad_ref[:key_end, :],
            state_ref[key_end:value_end, :] - sizes[1] * grad_ref[key_end:value_end, :],
            state_ref[value_end:, :] - sizes[2] * grad_ref[value_end:, :],
        )

    def page_scores(ref, queries, positions):
        scores = dot(halves(ref[:slot_rows, :]), queries, 1, 1) * score_scale
        bias = row_as_column(tail_as_row(ref, 2 * slot_rows, bias_rows), width)
        scores = scores + jnp.concatenate([bias] * (positions.shape[1] // width), axis=1)
        page_start = ref[packed_rows - 1 : packed_rows, 0:1]
        visible = jnp.broadcast_to(positions >= page_start, scores.shape)
        return jnp.where(visible, scores, MASKED), visible

    def read_positions(query_refs):
        return in_columns(
            [tail_as_row(ref, part_rows + piece, pos_rows) for ref in query_refs], 1
        )

    def forward(state_refs, query_refs, chunk_outs, weights_out, max_out, chunks):
        rank, _, _ = places()
        all_queries, positions = read_queries(query_refs), read_positions(query_refs)
        all_scores, all_visible = [], []
        for at, ref in enumerate(state_refs):
            scores, visible = page_scores(ref, all_queries, positions)
            all_scores.append(scores)
            all_visible.append(visible)
        row_max = jnp.max(all_scores[0], axis=0, keepdims=True)
        for scores in all_scores[1:]:
            row_max = jnp.maximum(row_max, jnp.max(scores, axis=0, keepdims=True))
        row_total = jnp.zeros_like(row_max)
        row_sum = jnp.zeros((width, query_rows), jnp.float32)
        for at, ref in enumerate(state_refs):
            weights = jnp.where(all_visible[at], jnp.exp(all_scores[at] - row_max), 0.0)
            weights_out[at * slot_rows : (at + 1) * slot_rows, :] = weights
            row_total = row_total + jnp.sum(weights, axis=0, keepdims=True)
            values = halves(ref[slot_rows : 2 * slot_rows, :])
            row_sum = row_sum + dot(values, halves(weights), 0, 0)
        max_out[...] = jnp.broadcast_to(row_max, (TAIL, query_rows))
        tail = jnp.concatenate(
            [row_max, row_total, jnp.zeros((TAIL - 2, query_rows), jnp.float32)], axis=0
        )
        for at in range(ranks):
            columns = slice(at * chunk, (at + 1) * chunk)
            chunks[at, :width, :] = row_sum[:, columns]
            chunks[at, width:, :] = tail[:, columns]
        for turn in range(ranks):
            chunk_outs[turn][...] = chunks[rank ^ turn]

    chunk_shape = (width + TAIL, chunk)
    forward_shapes = [chunk_shape] * ranks + [(slots, query_rows), (TAIL, query_rows)]
    chunk_scratch = [pltpu.VMEM((ranks,) + chunk_shape, jnp.float32)]

    fold = max(1, 128 // piece)
    folded, columns = width // fold, fold * piece
    piece_shape = (folded + TAIL, columns)
    piece_scratch = [pltpu.VMEM((ranks,) + piece_shape, jnp.float32)]

    def fold_rows(value):
        groups = [value[at * folded : (at + 1) * folded, :] for at in range(fold)]
        return jnp.concatenate(groups, axis=1)

    def unfold_rows(value):
        groups = [value[:, at * piece : (at + 1) * piece] for at in range(fold)]
        return jnp.concatenate(groups, axis=0)

    def rows_tail(rows):
        empty = jnp.zeros((TAIL - len(rows), columns), jnp.float32)
        return jnp.concatenate(rows + [empty], axis=0)

    def part_body(*refs):
        state_refs, (query_ref, *refs) = refs[:CORES], refs[CORES:]
        piece_outs, (weights_out, max_out, pieces) = refs[:ranks], refs[ranks:]
        rank, _, _ = places()
        queries = halves(query_ref[:part_rows, :])
        position_row = tail_as_row(query_ref, part_rows + piece, pos_rows)
        all_scores, all_visible = [], []
        for ref in state_refs:
            scores, visible = page_scores(ref, queries, position_row)
            all_scores.append(scores)
            all_visible.append(visible)
        row_max = jnp.max(all_scores[0], axis=0, keepdims=True)
        for scores in all_scores[1:]:
            row_max = jnp.maximum(row_max, jnp.max(scores, axis=0, keepdims=True))
        row_total = jnp.zeros_like(row_max)
        row_sum = jnp.zeros((width, part_rows), jnp.float32)
        for at, ref in enumerate(state_refs):
            weights = jnp.where(all_visible[at], jnp.exp(all_scores[at] - row_max), 0.0)
            weights_out[at * slot_rows : (at + 1) * slot_rows, :] = weights
            row_total = row_total + jnp.sum(weights, axis=0, keepdims=True)
            values = halves(ref[slot_rows : 2 * slot_rows, :])
            row_sum = row_sum + dot(values, halves(weights), 0, 0)
        max_out[...] = jnp.broadcast_to(row_max, (TAIL, part_rows))
        for at in range(ranks):
            own = slice(at * piece, (at + 1) * piece)
            pieces[at, :folded, :] = fold_rows(row_sum[:, own])
            pieces[at, folded:, :] = rows_tail(
                [jnp.concatenate([row[:, own]] * fold, axis=1) for row in (row_max, row_total)]
            )
        for turn in range(ranks):
            piece_outs[turn][...] = pieces[rank ^ turn]

    part_shapes = [piece_shape] * ranks + [(slots, part_rows), (TAIL, part_rows)]

    def next_body(*refs):
        state_refs, refs = refs[:2], refs[2:]
        query_refs, refs = refs[:query_devices], refs[query_devices:]
        grad_refs, refs = refs[:2], refs[2:]
        tile_refs, refs = refs[: len(tiles)], refs[len(tiles) :]
        refs[0][CORES * packed_rows :, :] = query_refs[0][...]
        state_outs, refs = parts_of(refs[:1]), refs[1:]
        chunk_outs, refs = refs[:ranks], refs[ranks:]
        sizes = step_sizes(tile_refs)
        for at in range(2):
            keys, values, bias = updated(state_refs[at], grad_refs[at], sizes)
            state_outs[at][:slot_rows, :] = keys
            state_outs[at][slot_rows : 2 * slot_rows, :] = values
            state_outs[at][2 * slot_rows :, :] = bias
        forward(state_outs, query_refs, chunk_outs, *refs)

    def merged_chunk(query_refs, sums, maxima, totals, out):
        targets = jnp.concatenate(
            [ref[part_rows : part_rows + piece, :] for ref in query_refs], axis=0
        )
        row_max = maxima[0]
        for other in maxima[1:]:
            row_max = jnp.maximum(row_max, other)
        row_total = jnp.zeros_like(row_max)
        row_sum = jnp.zeros((width, chunk), jnp.float32)
        for part_sum, part_max, part_total in zip(sums, maxima, totals):
            factor = jnp.exp(part_max - row_max)
            row_total = row_total + part_total * factor
            row_sum = row_sum + part_sum * factor
        output = row_sum / row_total
        residual = output - targets.T
        row_delta = jnp.sum(residual * output, axis=0, keepdims=True)
        out[:width, :] = residual
        out[width:, :] = jnp.concatenate(
            [row_max, row_total, row_delta, jnp.zeros((TAIL - 3, chunk), jnp.float32)], axis=0
        )

    def first_merge_body(*refs):
        query_refs, (*piece_refs, merged_out) = refs[:query_devices], refs[query_devices:]

        def joined(read):
            return [
                jnp.concatenate([read(ref) for ref in piece_refs[turn::ranks]], axis=1)
                for turn in range(ranks)
            ]

        merged_chunk(
            query_refs,
            joined(lambda ref: unfold_rows(ref[:folded, :])),
            joined(lambda ref: ref[folded : folded + 1, :piece]),
            joined(lambda ref: ref[folded + 1 : folded + 2, :piece]),
            merged_out,
        )

    def merge_body(*refs):
        query_refs, (*chunk_refs, merged_out) = refs[:query_devices], refs[query_devices:]
        merged_chunk(
            query_refs,
            [ref[:width, :] for ref in chunk_refs],
            [ref[width : width + 1, :] for ref in chunk_refs],
            [ref[width + 1 : width + 2, :] for ref in chunk_refs],
            merged_out,
        )

    def page_gradients(weights, factor, state_ref, all_queries, residual, row_delta, out):
        attention = weights * factor
        grad_values = dot(halves(attention), residual, 1, 1)
        grad_probs = dot(halves(state_ref[slot_rows : 2 * slot_rows, :]), residual, 1, 0)
        grad_scores = halves(attention * (grad_probs - row_delta))
        grad_keys = dot(grad_scores, all_queries, 1, 0) * score_scale
        ones = jnp.ones((TAIL, query_rows), jnp.bfloat16)
        grad_bias = dot((ones, jnp.zeros_like(ones)), grad_scores, 1, 1)[0:1, :]
        grad_bias = row_as_tail(grad_bias, width)
        out[:slot_rows, :] = grad_keys
        out[slot_rows : 2 * slot_rows, :] = grad_values
        out[2 * slot_rows :, :] = grad_bias
        return grad_keys, grad_values, grad_bias

    def split_merged(joined):
        row_max, row_total, row_delta = (
            joined[width + at : width + at + 1, :] for at in range(3)
        )
        return halves(joined[:width, :]), row_max, row_total, row_delta

    def read_chunks(merged_refs, chunks):
        rank, _, _ = places()
        for turn, ref in enumerate(merged_refs):
            chunks[rank ^ turn] = ref[...]
        return [chunks[at] for at in range(ranks)]

    def join_body(*refs):
        *merged_refs, joined_out, chunks = refs
        joined_out[...] = jnp.concatenate(read_chunks(merged_refs, chunks), axis=1)

    def backward_body(*refs):
        weights_refs, refs = refs[: len(weights)], refs[len(weights) :]
        max_refs, refs = refs[: len(weights)], refs[len(weights) :]
        state_refs, refs = parts_of(refs[: len(states)]), refs[len(states) :]
        query_refs, refs = refs[:query_devices], refs[query_devices:]
        merged_refs, refs = refs[: len(all_merged)], refs[len(all_merged) :]
        grad_outs, (squares_out, *scratch) = refs[:2], refs[2:]
        if len(states) < CORES:
            joined = merged_refs[0][...]
            all_queries = read_queries(query_refs)
        else:
            chunks = read_chunks(merged_refs, *scratch)
            joined = jnp.concatenate(
                [
                    value[:, part * piece : (part + 1) * piece]
                    for part in range(query_devices)
                    for value in chunks
                ],
                axis=1,
            )
            all_queries = halves(
                jnp.concatenate([ref[:part_rows, :] for ref in query_refs], axis=0)
            )
        residual, row_max, row_total, row_delta = split_merged(joined)
        maxima = jnp.concatenate([ref[0:1, :] for ref in max_refs], axis=1)
        factor = jnp.exp(maxima - row_max) / row_total
        squares = [jnp.zeros((1, width), jnp.float32)] * 3
        for at, (ref, out) in enumerate(zip(state_refs, grad_outs)):
            rows = slice(at * slot_rows, (at + 1) * slot_rows)
            page_weights = jnp.concatenate([part[rows, :] for part in weights_refs], axis=1)
            grads = page_gradients(
                page_weights, factor, ref, all_queries, residual, row_delta, out
            )
            for which, grad in enumerate(grads):
                squares[which] = squares[which] + jnp.sum(grad * grad, axis=0, keepdims=True)
        lanes = lax.broadcasted_iota(jnp.int32, (1, width), 1)
        row = jnp.zeros((1, width), jnp.float32)
        for which, square in enumerate(squares):
            row = jnp.where(lanes == which, jnp.sum(square, axis=1, keepdims=True), row)
        for at in range(devices):
            squares_out[at] = row

    def page_body(turn, at):
        def body(state_ref, joined_ref, *refs):
            *pack_refs, grad_out = refs
            query_refs = [state_ref.at[pl.ds(CORES * packed_rows, query_shape[0])]] + pack_refs
            residual, row_max, row_total, row_delta = split_merged(joined_ref[...])
            all_queries = read_queries(query_refs)
            ref = part_of(state_ref, at)
            scores, visible = page_scores(ref, all_queries, read_positions(query_refs))
            weights = jnp.where(visible, jnp.exp(scores - row_max), 0.0)
            page_gradients(
                weights, 1.0 / row_total, ref, all_queries, residual, row_delta, grad_out
            )

        return body

    def mate_body(*refs):
        *state_refs, out_ref = refs
        for at, ref in enumerate(state_refs):
            out_ref[pl.ds(at * packed_rows, packed_rows), :] = part_of(ref, 1)[...]

    for repeat in range(STEPS):
        last = repeat == STEPS - 1
        if repeat == 0:
            sums, weights, maxima = [], [], []
            for query_pack in query_parts:
                *pieces, part_weights, part_max = call(
                    part_body,
                    part_shapes,
                    "forward",
                    2 * matmul_cost // query_devices,
                    states + [query_pack],
                    piece_scratch,
                    after=maxima[-1:],
                )
                arrived = {
                    turn: exchange(pieces[turn], page=CORES * turn)
                    for turn in reversed(range(1, ranks))
                }
                sums += list(arrived.values()) + pieces[:1]
                weights.append(part_weights)
                maxima.append(part_max)
        else:
            new_state, *chunk_parts, part_weights, part_max = call(
                next_body,
                [(CORES * packed_rows + query_shape[0], width)] + forward_shapes,
                "update_forward",
                2 * matmul_cost,
                states + query_parts + grads + tiles,
                chunk_scratch,
            )
            states, weights, maxima = [new_state], [part_weights], [part_max]
            arrived = {
                turn: exchange(chunk_parts[turn], page=CORES * turn)
                for turn in reversed(range(1, ranks))
            }
            sums = chunk_parts[:1] + list(arrived.values())
            new_states = states + [
                exchange(states[0], query=turn) for turn in range(1, query_devices)
            ]
        (merged,) = call(
            merge_body if repeat else first_merge_body,
            [chunk_shape],
            "merge",
            2**20,
            query_parts + sums,
        )
        all_merged = [merged] + [
            exchange(merged, page=CORES * turn) for turn in range(1, ranks)
        ]
        if last:
            all_merged = call(
                join_body, [(width + TAIL, query_rows)], "join", 2**20, all_merged, chunk_scratch
            )
            all_joined = [
                to_device(all_merged[0], query=turn) for turn in range(query_devices)
            ]
        own_grad, mate_grad, squares = call(
            backward_body,
            packed_shapes + [(devices, 1, width)],
            "backward",
            3 * matmul_cost,
            weights + maxima + states + query_parts + list(all_merged),
            scratch=() if last else chunk_scratch,
        )
        grads = [own_grad, mate_grad]
        tiles = [
            lax.all_to_all(
                squares, ("page", "query", "head"), split_axis=0, concat_axis=0, tiled=True
            )
        ]

    (for_mate,) = call(
        mate_body,
        [(query_devices * packed_rows, width)],
        "mate_parts",
        2**20,
        new_states,
        after=tiles,
    )
    from_mate = exchange(for_mate, page=1)
    all_grads = [own_grad, exchange(mate_grad, page=1)]
    for turn in range(1, query_devices):
        parts = [
            packs[part] if part == turn else query_part(turn, part)
            for part in range(1, query_devices)
        ]
        page_grads = [
            call(
                page_body(turn, at),
                packed_shapes[:1],
                "other_backward",
                3 * matmul_cost // 2,
                [new_states[turn], all_joined[turn]] + parts,
                after=tiles,
            )[0]
            for at in reversed(range(CORES))
        ]
        all_grads += [page_grads[1], exchange(page_grads[0], page=1)]
    out_masks = list(itertools.product(range(query_devices), range(CORES)))

    def last_body(*refs):
        state_refs, (mate_ref, *refs) = refs[:query_devices], refs[query_devices:]
        state_refs = [
            part_of(mate_ref, turn) if flip else part_of(state_refs[turn], 0)
            for turn, flip in out_masks
        ]
        grad_refs, refs = refs[:local_heads], refs[local_heads:]
        tile_refs, (keys_out, values_out, bias_out) = refs[: len(tiles)], refs[len(tiles) :]
        _, core, me = places()
        sizes = step_sizes(tile_refs)
        for at, (turn, flip) in enumerate(out_masks):
            keys, values, bias = updated(state_refs[at], grad_refs[at], sizes)
            head = CORES * (me ^ turn) + (core ^ flip)
            keys_out[head] = keys
            values_out[head] = values
            bias_row = jnp.concatenate([bias[row : row + 1] for row in range(bias_rows)], axis=1)
            bias_out[pl.ds(head, 1), :] = bias_row

    return tuple(
        call(
            last_body,
            [compact_keys.shape, compact_values.shape, slot_bias.shape],
            "last_update",
            2**20,
            new_states + [from_mate] + all_grads + tiles,
        )
    )


def from_partner(value, axis, stride):
    mask = 2**stride
    pairs = [(source, source ^ mask) for source in range(lax.axis_size(axis))]
    return lax.ppermute(value, axis, pairs)


def squared_sums(grad_keys, grad_values, grad_bias):
    return jnp.stack(
        [
            jnp.sum(grad_keys * grad_keys),
            jnp.sum(grad_values * grad_values),
            jnp.sum(grad_bias * grad_bias),
        ]
    )


def apply_update(states, grads, totals, entry_count, slot_total):
    key_state, value_state, bias_state = states
    grad_keys, grad_values, grad_bias = grads
    rms_keys = jnp.sqrt(totals[0] / entry_count + EPSILON)
    rms_values = jnp.sqrt(totals[1] / entry_count + EPSILON)
    rms_bias = jnp.sqrt(totals[2] / slot_total + EPSILON)
    return (
        key_state - RATE_KEYS * grad_keys / rms_keys,
        value_state - RATE_VALUES * grad_values / rms_values,
        bias_state - RATE_BIAS * grad_bias / rms_bias,
    )


def local_gradients(queries, targets, visible, compact_keys, compact_values, slot_bias):
    score_scale = 1.0 / math.sqrt(queries.shape[2])
    scores = jnp.einsum("hqd,hsd->hqs", queries, compact_keys, precision=HIGHEST) * score_scale
    scores = jnp.where(visible, scores + slot_bias[:, None, :], MASKED)
    local_max = jnp.max(scores, axis=2)
    row_max = lax.pmax(local_max, "page")
    weights = jnp.where(visible, jnp.exp(scores - row_max[:, :, None]), 0.0)
    local_sum = jnp.einsum("hqs,hsd->hqd", weights, compact_values, precision=HIGHEST)
    row_total, row_sum = lax.psum((jnp.sum(weights, axis=2), local_sum), "page")
    attention = weights / row_total[:, :, None]
    output = row_sum / row_total[:, :, None]
    residual = output - targets
    grad_values = jnp.einsum("hqs,hqd->hsd", attention, residual, precision=HIGHEST)
    row_delta = jnp.sum(residual * output, axis=2)
    grad_probs = jnp.einsum("hqd,hsd->hqs", residual, compact_values, precision=HIGHEST)
    grad_scores = attention * (grad_probs - row_delta[:, :, None])
    grad_bias = jnp.sum(grad_scores, axis=1)
    grad_keys = jnp.einsum("hqs,hqd->hsd", grad_scores, queries, precision=HIGHEST) * score_scale
    return (grad_keys, grad_values, grad_bias)


def per_device(queries, compact_keys, compact_values, slot_bias, targets, positions, assignment):
    page_number = assignment[lax.axis_index("page")]
    local_heads = compact_keys.shape[0]
    slot_total = local_heads * lax.axis_size("head") * compact_keys.shape[1] * lax.axis_size("page")
    entry_count = slot_total * compact_keys.shape[2]
    query_count = lax.axis_size("query")
    heads_kept = max(local_heads // query_count, 1)
    query_parts = max(query_count // local_heads, 1)
    part_rows = queries.shape[1] // query_parts

    def split_items(array):
        width = array.shape[2]
        array = array.reshape(local_heads // heads_kept, heads_kept, query_parts, part_rows, width)
        array = jnp.transpose(array, (0, 2, 1, 3, 4))
        return array.reshape(query_count, heads_kept, part_rows, width)

    def join_items(array):
        width = array.shape[3]
        array = jnp.transpose(array, (1, 0, 2, 3))
        return array.reshape(heads_kept, query_count * part_rows, width)

    position_column = positions.astype(jnp.float32)[:, :, None]
    got_queries, got_targets, got_positions = (
        lax.all_to_all(split_items(queries), "query", split_axis=0, concat_axis=0, tiled=True),
        lax.all_to_all(split_items(targets), "query", split_axis=0, concat_axis=0, tiled=True),
        lax.all_to_all(
            split_items(position_column), "query", split_axis=0, concat_axis=0, tiled=True
        ),
    )
    group_queries = join_items(got_queries)
    group_targets = join_items(got_targets)
    group_positions = join_items(got_positions)[:, :, 0]
    visible = (page_number.astype(jnp.float32) <= jnp.floor(group_positions / PAGE_LEN))[:, :, None]
    query_index = lax.axis_index("query")
    first_head = query_index // query_parts * heads_kept
    key_state = lax.dynamic_slice_in_dim(compact_keys, first_head, heads_kept, 0)
    value_state = lax.dynamic_slice_in_dim(compact_values, first_head, heads_kept, 0)
    bias_state = lax.dynamic_slice_in_dim(slot_bias, first_head, heads_kept, 0)
    counted = (query_index % query_parts == 0).astype(jnp.float32)
    for repeat in range(STEPS):
        grads = local_gradients(
            group_queries, group_targets, visible, key_state, value_state, bias_state
        )
        for bit in range(query_parts.bit_length() - 1):
            partner = from_partner((grads[0], grads[1], grads[2]), "query", bit)
            grads = (grads[0] + partner[0], grads[1] + partner[1], grads[2] + partner[2])
        totals = lax.psum(
            squared_sums(grads[0], grads[1], grads[2]) * counted, ("page", "query", "head")
        )
        key_state, value_state, bias_state = apply_update(
            (key_state, value_state, bias_state), grads, totals, entry_count, slot_total
        )
    all_keys, all_values, all_bias = (
        lax.all_gather(key_state, "query", axis=0, tiled=True),
        lax.all_gather(value_state, "query", axis=0, tiled=True),
        lax.all_gather(bias_state, "query", axis=0, tiled=True),
    )
    slot_rows = compact_keys.shape[1]
    head_width = compact_keys.shape[2]
    all_keys = all_keys.reshape(
        local_heads // heads_kept, query_parts, heads_kept, slot_rows, head_width
    )[:, 0]
    all_values = all_values.reshape(
        local_heads // heads_kept, query_parts, heads_kept, slot_rows, head_width
    )[:, 0]
    all_bias = all_bias.reshape(local_heads // heads_kept, query_parts, heads_kept, slot_rows)[:, 0]
    return (
        all_keys.reshape(local_heads, slot_rows, head_width),
        all_values.reshape(local_heads, slot_rows, head_width),
        all_bias.reshape(local_heads, slot_rows),
    )


def solution(mesh):
    placed = (
        P("head", "query", None),
        P("head", "page", None),
        P("head", "page", None),
        P("head", "page"),
        P("head", "query", None),
        P("head", "query"),
        P(),
    )

    def program(*args):
        plan = direct_per_device if direct_plan_fits(mesh, args[0], args[1]) else per_device
        return jax.shard_map(
            plan,
            mesh=mesh,
            in_specs=placed,
            out_specs=(P("head", "page", None), P("head", "page", None), P("head", "page")),
            check_vma=False,
        )(*args)

    return program
```

```python
import itertools
import math

import jax
import jax.numpy as jnp
from jax import lax
from jax.experimental import pallas as pl
from jax.experimental.pallas import tpu as pltpu
from jax.sharding import PartitionSpec as P

STEPS = 2
PAGE_LEN = 32768


MASKED = -1e30
EPSILON = 1e-06
RATE_KEYS = 0.05
RATE_VALUES = 0.05
RATE_BIAS = 0.2
HIGHEST = lax.Precision.HIGHEST
TAIL = 8
CORES = 2


def exchange(value, **masks):
    axes = tuple(masks)
    sizes = [lax.axis_size(axis) for axis in axes]

    def flat(place):
        index = 0
        for size, at in zip(sizes, place):
            index = index * size + at
        return index

    pairs = [
        (flat(place), flat([at ^ mask for at, mask in zip(place, masks.values())]))
        for place in itertools.product(*map(range, sizes))
    ]
    return lax.ppermute(value, axes, pairs)


def halves(value):
    high = value.astype(jnp.bfloat16)
    return high, (value - high.astype(jnp.float32)).astype(jnp.bfloat16)


def dot(left, right, left_dim, right_dim):
    def one_pass(left_half, right_half):
        return lax.dot_general(
            left_half,
            right_half,
            (((left_dim,), (right_dim,)), ((), ())),
            preferred_element_type=jnp.float32,
        )

    cross = one_pass(left[0], right[1]) + one_pass(left[1], right[0])
    return one_pass(left[0], right[0]) + cross


def call(body, out_shapes, name, cost, operands, scratch=(), after=(), space=pltpu.VMEM, vmem=32):
    spaces = [space] * len(operands) + [pl.ANY] * len(after)
    count = len(operands)

    def without_after(*refs):
        body(*refs[:count], *refs[count + len(after) :])

    return pl.pallas_call(
        without_after,
        out_shape=[jax.ShapeDtypeStruct(shape, jnp.float32) for shape in out_shapes],
        in_specs=[pl.BlockSpec(memory_space=space) for space in spaces],
        out_specs=[pl.BlockSpec(memory_space=pltpu.VMEM) for _ in out_shapes],
        scratch_shapes=scratch,
        compiler_params=pltpu.CompilerParams(vmem_limit_bytes=vmem * 2**20),
        cost_estimate=pl.CostEstimate(flops=cost, bytes_accessed=2**20, transcendentals=0),
        name=name,
    )(*operands, *after)


def row_as_tail(row, width):
    rows = [row[:, at : at + width] for at in range(0, row.shape[1], width)]
    rows.append(jnp.zeros((TAIL - len(rows), width), row.dtype))
    return jnp.concatenate(rows, axis=0)


def tail_as_row(ref, start, count):
    return jnp.concatenate([ref[start + at : start + at + 1, :] for at in range(count)], axis=1)


def row_as_column(row, width):
    parts = []
    for at in range(0, row.shape[1], width):
        parts.append(jnp.broadcast_to(row[:, at : at + width], (width, width)).T)
    return jnp.concatenate(parts, axis=0)


def direct_plan_fits(mesh, queries, compact_keys):
    sizes = [mesh.shape[axis] for axis in ("page", "query", "head")]
    pages, query_devices, head_devices = sizes
    local_heads = queries.shape[0] // head_devices
    part_rows = queries.shape[1] // query_devices
    slot_rows = compact_keys.shape[1] // pages
    width = queries.shape[2]
    if any(size & (size - 1) for size in sizes) or pages < CORES or width % 128:
        return False
    if local_heads != CORES * query_devices:
        return False
    ranks = pages // CORES
    chunk = part_rows * query_devices // ranks
    return (
        part_rows * query_devices % ranks == 0
        and chunk % 128 == 0
        and part_rows % (8 * ranks) == 0
        and (part_rows // ranks % 128 == 0 or 1024 % (part_rows // ranks * 8) == 0)
        and slot_rows % width == 0
        and part_rows % width == 0
        and max(slot_rows, part_rows) < TAIL * width
    )


def direct_per_device(
    queries, compact_keys, compact_values, slot_bias, targets, positions, assignment
):
    local_heads, part_rows, width = queries.shape
    slot_rows = compact_keys.shape[1]
    query_devices = lax.axis_size("query")
    head_devices = lax.axis_size("head")
    ranks = lax.axis_size("page") // CORES
    query_rows = part_rows * query_devices
    chunk, piece = query_rows // ranks, part_rows // ranks
    slot_total = local_heads * head_devices * slot_rows * lax.axis_size("page")
    entry_total = slot_total * width
    score_scale = 1.0 / math.sqrt(width)
    slots = CORES * slot_rows
    devices = ranks * CORES * query_devices * head_devices
    pos_rows = part_rows // width
    bias_rows = slot_rows // width
    packed_rows = 2 * slot_rows + TAIL
    packed_shapes = [(packed_rows, width)] * 2
    matmul_cost = 3 * 2 * slots * query_rows * width

    def places():
        page = lax.axis_index("page")
        return page // CORES, page % CORES, lax.axis_index("query")

    def to_device(value, **masks):
        masks = {axis: mask for axis, mask in masks.items() if mask}
        return exchange(value, **masks) if masks else value

    def pack_queries(head, rank, queries, targets, out):
        rows = pl.ds(pl.multiple_of(rank * piece, piece), piece)
        return [
            (queries.at[head], out.at[pl.ds(0, part_rows)]),
            (targets.at[head, rows], out.at[pl.ds(part_rows, piece)]),
        ]

    def pack_state(head, keys, values, out):
        return [
            (keys.at[head], out.at[pl.ds(0, slot_rows)]),
            (values.at[head], out.at[pl.ds(slot_rows, slot_rows)]),
        ]

    def start_all(copies, sems, first=0):
        copies = [
            pltpu.make_async_copy(source, target, sems.at[first + at])
            for at, (source, target) in enumerate(copies)
        ]
        for copy in copies:
            copy.start()
        return copies

    def position_tail(head, positions_ref):
        return row_as_tail(positions_ref[pl.ds(head, 1), :].astype(jnp.float32), width)

    def state_tail(head, page, bias_ref, assignment_ref):
        page_start = (assignment_ref[page] * PAGE_LEN).astype(jnp.float32)
        tail = row_as_tail(bias_ref[pl.ds(head, 1), :], width)
        return jnp.concatenate(
            [tail[: TAIL - 1], jnp.full((1, width), page_start, jnp.float32)], axis=0
        )

    def send_body(
        queries, keys, values, biases, targets, positions, assignment, state_out, *refs
    ):
        query_outs = refs[: query_devices - 1]
        bias_ref, positions_ref, assignment_ref, sems = refs[query_devices - 1 :]
        rank, core, me = places()
        heads = [CORES * (me ^ turn) + core for turn in range(1, query_devices)]
        mate_head = CORES * me + (core ^ 1)
        small = start_all(
            [(assignment, assignment_ref), (positions, positions_ref), (biases, bias_ref)], sems
        )
        copies = pack_state(mate_head, keys, values, state_out)
        for head, out in zip(heads, query_outs):
            copies += pack_queries(head, rank, queries, targets, out)
        copies = start_all(copies, sems, 3)
        for copy in small:
            copy.wait()
        state_out[2 * slot_rows :, :] = state_tail(
            mate_head, CORES * rank + core, bias_ref, assignment_ref
        )
        for head, out in zip(heads, query_outs):
            out[part_rows + piece :, :] = position_tail(head, positions_ref)
        for copy in copies:
            copy.wait()

    def own_body(
        queries, keys, values, biases, targets, positions, assignment, state_out, query_out, *refs
    ):
        bias_ref, positions_ref, assignment_ref, sems = refs
        rank, core, me = places()
        head = CORES * me + core
        small = start_all(
            [(assignment, assignment_ref), (positions, positions_ref), (biases, bias_ref)], sems
        )
        copies = pack_state(head, keys, values, state_out)
        copies += pack_queries(head, rank, queries, targets, query_out)
        copies = start_all(copies, sems, 3)
        for copy in small:
            copy.wait()
        state_out[2 * slot_rows :, :] = state_tail(
            head, CORES * rank + core, bias_ref, assignment_ref
        )
        query_out[part_rows + piece :, :] = position_tail(head, positions_ref)
        for copy in copies:
            copy.wait()

    state_shape, query_shape = (packed_rows, width), (part_rows + piece + TAIL, width)
    small_scratch = [
        pltpu.VMEM(slot_bias.shape, jnp.float32),
        pltpu.VMEM(positions.shape, jnp.int32),
        pltpu.SMEM(assignment.shape, jnp.int32),
    ]
    arguments = [
        queries, compact_keys, compact_values, slot_bias, targets, positions, assignment
    ]
    mate_state, *sent_queries = call(
        send_body,
        [state_shape] + [query_shape] * (query_devices - 1),
        "pack",
        2**20,
        arguments,
        small_scratch + [pltpu.SemaphoreType.DMA((3 + 2 * query_devices,))],
        space=pl.ANY,
        vmem=60,
    )
    own_state, own_queries = call(
        own_body,
        [state_shape, query_shape],
        "own",
        2**24,
        arguments,
        small_scratch + [pltpu.SemaphoreType.DMA((7,))],
        space=pl.ANY,
    )
    packs = [own_queries] + list(sent_queries)

    def query_part(turn, part):
        return to_device(packs[part], query=turn ^ part)

    query_parts = [query_part(0, part) for part in range(query_devices)]
    states = [own_state, exchange(mate_state, page=1)]

    def in_columns(parts, axis):
        return jnp.concatenate(
            [
                lax.slice_in_dim(part, at * piece, (at + 1) * piece, axis=axis)
                for at in range(ranks)
                for part in parts
            ],
            axis=axis,
        )

    def read_queries(query_refs):
        return halves(in_columns([ref[:part_rows, :] for ref in query_refs], 0))

    def part_of(ref, at):
        return ref.at[pl.ds(at * packed_rows, packed_rows)]

    def parts_of(refs):
        return refs if len(refs) == CORES else [part_of(refs[0], at) for at in range(CORES)]

    def step_sizes(tile_refs):
        row = jnp.sum(tile_refs[0][...], axis=0)
        return (
            RATE_KEYS / jnp.sqrt(row[:, 0:1] / entry_total + EPSILON),
            RATE_VALUES / jnp.sqrt(row[:, 1:2] / entry_total + EPSILON),
            RATE_BIAS / jnp.sqrt(row[:, 2:3] / slot_total + EPSILON),
        )

    def read_pack(ref):
        return ref[:slot_rows, :], ref[slot_rows : 2 * slot_rows, :], ref[2 * slot_rows :, :]

    def store_pack(ref, values):
        ref[:slot_rows, :] = values[0]
        ref[slot_rows : 2 * slot_rows, :] = values[1]
        ref[2 * slot_rows :, :] = values[2]

    def updated(state, grads, sizes):
        return [value - size * grad for value, grad, size in zip(state, grads, sizes)]

    def page_scores(ref, queries, positions):
        scores = dot(halves(ref[:slot_rows, :]), queries, 1, 1) * score_scale
        bias = row_as_column(tail_as_row(ref, 2 * slot_rows, bias_rows), width)
        scores = scores + jnp.concatenate([bias] * (positions.shape[1] // width), axis=1)
        page_start = ref[packed_rows - 1 : packed_rows, 0:1]
        visible = jnp.broadcast_to(positions >= page_start, scores.shape)
        return jnp.where(visible, scores, MASKED), visible

    def read_positions(query_refs):
        return in_columns(
            [tail_as_row(ref, part_rows + piece, pos_rows) for ref in query_refs], 1
        )

    def forward(state_refs, query_refs, chunk_outs, weights_out, max_out, chunks):
        rank, _, _ = places()
        all_queries, positions = read_queries(query_refs), read_positions(query_refs)
        all_scores, all_visible = [], []
        for at, ref in enumerate(state_refs):
            scores, visible = page_scores(ref, all_queries, positions)
            all_scores.append(scores)
            all_visible.append(visible)
        row_max = jnp.max(all_scores[0], axis=0, keepdims=True)
        for scores in all_scores[1:]:
            row_max = jnp.maximum(row_max, jnp.max(scores, axis=0, keepdims=True))
        row_total = jnp.zeros_like(row_max)
        row_sum = jnp.zeros((width, query_rows), jnp.float32)
        for at, ref in enumerate(state_refs):
            weights = jnp.where(all_visible[at], jnp.exp(all_scores[at] - row_max), 0.0)
            weights_out[at * slot_rows : (at + 1) * slot_rows, :] = weights
            row_total = row_total + jnp.sum(weights, axis=0, keepdims=True)
            values = halves(ref[slot_rows : 2 * slot_rows, :])
            row_sum = row_sum + dot(values, halves(weights), 0, 0)
        max_out[...] = jnp.broadcast_to(row_max, (TAIL, query_rows))
        tail = jnp.concatenate(
            [row_max, row_total, jnp.zeros((TAIL - 2, query_rows), jnp.float32)], axis=0
        )
        for at in range(ranks):
            columns = slice(at * chunk, (at + 1) * chunk)
            chunks[at, :width, :] = row_sum[:, columns]
            chunks[at, width:, :] = tail[:, columns]
        for turn in range(ranks):
            chunk_outs[turn][...] = chunks[rank ^ turn]

    chunk_shape = (width + TAIL, chunk)
    forward_shapes = [chunk_shape] * ranks + [(slots, query_rows), (TAIL, query_rows)]
    chunk_scratch = [pltpu.VMEM((ranks,) + chunk_shape, jnp.float32)]

    fold = max(1, 128 // piece)
    folded, columns = width // fold, fold * piece
    piece_shape = (folded + TAIL, columns)
    piece_scratch = [pltpu.VMEM((ranks,) + piece_shape, jnp.float32)]

    def fold_rows(value):
        groups = [value[at * folded : (at + 1) * folded, :] for at in range(fold)]
        return jnp.concatenate(groups, axis=1)

    def unfold_rows(value):
        groups = [value[:, at * piece : (at + 1) * piece] for at in range(fold)]
        return jnp.concatenate(groups, axis=0)

    def rows_tail(rows):
        empty = jnp.zeros((TAIL - len(rows), columns), jnp.float32)
        return jnp.concatenate(rows + [empty], axis=0)

    def part_body(*refs):
        state_refs, (query_ref, *refs) = refs[:CORES], refs[CORES:]
        piece_outs, (weights_out, max_out, pieces) = refs[:ranks], refs[ranks:]
        rank, _, _ = places()
        queries = halves(query_ref[:part_rows, :])
        position_row = tail_as_row(query_ref, part_rows + piece, pos_rows)
        all_scores, all_visible = [], []
        for ref in state_refs:
            scores, visible = page_scores(ref, queries, position_row)
            all_scores.append(scores)
            all_visible.append(visible)
        row_max = jnp.max(all_scores[0], axis=0, keepdims=True)
        for scores in all_scores[1:]:
            row_max = jnp.maximum(row_max, jnp.max(scores, axis=0, keepdims=True))
        row_total = jnp.zeros_like(row_max)
        row_sum = jnp.zeros((width, part_rows), jnp.float32)
        for at, ref in enumerate(state_refs):
            weights = jnp.where(all_visible[at], jnp.exp(all_scores[at] - row_max), 0.0)
            weights_out[at * slot_rows : (at + 1) * slot_rows, :] = weights
            row_total = row_total + jnp.sum(weights, axis=0, keepdims=True)
            values = halves(ref[slot_rows : 2 * slot_rows, :])
            row_sum = row_sum + dot(values, halves(weights), 0, 0)
        max_out[...] = jnp.broadcast_to(row_max, (TAIL, part_rows))
        for at in range(ranks):
            own = slice(at * piece, (at + 1) * piece)
            pieces[at, :folded, :] = fold_rows(row_sum[:, own])
            pieces[at, folded:, :] = rows_tail(
                [jnp.concatenate([row[:, own]] * fold, axis=1) for row in (row_max, row_total)]
            )
        for turn in range(ranks):
            piece_outs[turn][...] = pieces[rank ^ turn]

    part_shapes = [piece_shape] * ranks + [(slots, part_rows), (TAIL, part_rows)]

    def next_body(*refs):
        state_refs, refs = refs[:2], refs[2:]
        query_refs, refs = refs[:query_devices], refs[query_devices:]
        grad_refs, refs = refs[:2], refs[2:]
        tile_refs, refs = refs[: len(tiles)], refs[len(tiles) :]
        refs[0][CORES * packed_rows :, :] = query_refs[0][...]
        state_outs, refs = parts_of(refs[:1]), refs[1:]
        chunk_outs, refs = refs[:ranks], refs[ranks:]
        sizes = step_sizes(tile_refs)
        for at in range(2):
            state = read_pack(state_refs[at])
            store_pack(state_outs[at], updated(state, read_pack(grad_refs[at]), sizes))
        forward(state_outs, query_refs, chunk_outs, *refs)

    def merged_chunk(query_refs, sums, maxima, totals, out):
        targets = jnp.concatenate(
            [ref[part_rows : part_rows + piece, :] for ref in query_refs], axis=0
        )
        row_max = maxima[0]
        for other in maxima[1:]:
            row_max = jnp.maximum(row_max, other)
        row_total = jnp.zeros_like(row_max)
        row_sum = jnp.zeros((width, chunk), jnp.float32)
        for part_sum, part_max, part_total in zip(sums, maxima, totals):
            factor = jnp.exp(part_max - row_max)
            row_total = row_total + part_total * factor
            row_sum = row_sum + part_sum * factor
        output = row_sum / row_total
        residual = output - targets.T
        row_delta = jnp.sum(residual * output, axis=0, keepdims=True)
        out[:width, :] = residual
        out[width:, :] = jnp.concatenate(
            [row_max, row_total, row_delta, jnp.zeros((TAIL - 3, chunk), jnp.float32)], axis=0
        )

    def first_merge_body(*refs):
        query_refs, (*piece_refs, merged_out) = refs[:query_devices], refs[query_devices:]

        def joined(read):
            return [
                jnp.concatenate([read(ref) for ref in piece_refs[turn::ranks]], axis=1)
                for turn in range(ranks)
            ]

        merged_chunk(
            query_refs,
            joined(lambda ref: unfold_rows(ref[:folded, :])),
            joined(lambda ref: ref[folded : folded + 1, :piece]),
            joined(lambda ref: ref[folded + 1 : folded + 2, :piece]),
            merged_out,
        )

    def merge_body(*refs):
        query_refs, (*chunk_refs, merged_out) = refs[:query_devices], refs[query_devices:]
        merged_chunk(
            query_refs,
            [ref[:width, :] for ref in chunk_refs],
            [ref[width : width + 1, :] for ref in chunk_refs],
            [ref[width + 1 : width + 2, :] for ref in chunk_refs],
            merged_out,
        )

    def page_gradients(weights, factor, state_ref, all_queries, residual, row_delta):
        attention = weights * factor
        grad_values = dot(halves(attention), residual, 1, 1)
        grad_probs = dot(halves(state_ref[slot_rows : 2 * slot_rows, :]), residual, 1, 0)
        grad_scores = halves(attention * (grad_probs - row_delta))
        grad_keys = dot(grad_scores, all_queries, 1, 0) * score_scale
        ones = jnp.ones((TAIL, query_rows), jnp.bfloat16)
        grad_bias = dot((ones, jnp.zeros_like(ones)), grad_scores, 1, 1)[0:1, :]
        return grad_keys, grad_values, row_as_tail(grad_bias, width)

    def split_merged(joined):
        row_max, row_total, row_delta = (
            joined[width + at : width + at + 1, :] for at in range(3)
        )
        return halves(joined[:width, :]), row_max, row_total, row_delta

    def read_chunks(merged_refs, chunks):
        rank, _, _ = places()
        for turn, ref in enumerate(merged_refs):
            chunks[rank ^ turn] = ref[...]
        return [chunks[at] for at in range(ranks)]

    def join_body(*refs):
        *merged_refs, joined_out, chunks = refs
        joined_out[...] = jnp.concatenate(read_chunks(merged_refs, chunks), axis=1)

    def backward_body(*refs):
        weights_refs, refs = refs[: len(weights)], refs[len(weights) :]
        max_refs, refs = refs[: len(weights)], refs[len(weights) :]
        state_refs, refs = parts_of(refs[: len(states)]), refs[len(states) :]
        query_refs, refs = refs[:query_devices], refs[query_devices:]
        merged_refs, refs = refs[: len(all_merged)], refs[len(all_merged) :]
        grad_outs, (squares_out, *scratch) = refs[:2], refs[2:]
        if len(states) < CORES:
            joined = merged_refs[0][...]
            all_queries = read_queries(query_refs)
        else:
            chunks = read_chunks(merged_refs, *scratch)
            joined = jnp.concatenate(
                [
                    value[:, part * piece : (part + 1) * piece]
                    for part in range(query_devices)
                    for value in chunks
                ],
                axis=1,
            )
            all_queries = halves(
                jnp.concatenate([ref[:part_rows, :] for ref in query_refs], axis=0)
            )
        residual, row_max, row_total, row_delta = split_merged(joined)
        maxima = jnp.concatenate([ref[0:1, :] for ref in max_refs], axis=1)
        factor = jnp.exp(maxima - row_max) / row_total
        squares = [jnp.zeros((1, width), jnp.float32)] * 3
        for at, (ref, out) in enumerate(zip(state_refs, grad_outs)):
            rows = slice(at * slot_rows, (at + 1) * slot_rows)
            page_weights = jnp.concatenate([part[rows, :] for part in weights_refs], axis=1)
            grads = page_gradients(page_weights, factor, ref, all_queries, residual, row_delta)
            store_pack(out, grads)
            for which, grad in enumerate(grads):
                squares[which] = squares[which] + jnp.sum(grad * grad, axis=0, keepdims=True)
        lanes = lax.broadcasted_iota(jnp.int32, (1, width), 1)
        row = jnp.zeros((1, width), jnp.float32)
        for which, square in enumerate(squares):
            row = jnp.where(lanes == which, jnp.sum(square, axis=1, keepdims=True), row)
        for at in range(devices):
            squares_out[at] = row

    def page_body(at):
        def body(tile_ref, grad_ref, own_state_ref, *refs):
            state_refs, refs = refs[: query_devices - 1], refs[query_devices - 1 :]
            joined_refs, (*pack_refs, out) = refs[: query_devices - 1], refs[query_devices - 1 :]
            sizes = step_sizes([tile_ref])
            state = read_pack(part_of(own_state_ref, at))
            store_pack(part_of(out, 0), updated(state, read_pack(grad_ref), sizes))
            for turn, (state_ref, joined_ref) in enumerate(zip(state_refs, joined_refs), 1):
                query_refs = [state_ref.at[pl.ds(CORES * packed_rows, query_shape[0])]]
                query_refs += pack_refs[(turn - 1) * (query_devices - 1) :][: query_devices - 1]
                residual, row_max, row_total, row_delta = split_merged(joined_ref[...])
                all_queries = read_queries(query_refs)
                ref = part_of(state_ref, at)
                scores, visible = page_scores(ref, all_queries, read_positions(query_refs))
                weights = jnp.where(visible, jnp.exp(scores - row_max), 0.0)
                grads = page_gradients(
                    weights, 1.0 / row_total, ref, all_queries, residual, row_delta
                )
                store_pack(part_of(out, turn), updated(read_pack(ref), grads, sizes))

        return body

    for repeat in range(STEPS):
        last = repeat == STEPS - 1
        if repeat == 0:
            sums, weights, maxima = [], [], []
            for query_pack in query_parts:
                *pieces, part_weights, part_max = call(
                    part_body,
                    part_shapes,
                    "forward",
                    2 * matmul_cost // query_devices,
                    states + [query_pack],
                    piece_scratch,
                    after=maxima[-1:],
                )
                arrived = {
                    turn: exchange(pieces[turn], page=CORES * turn)
                    for turn in reversed(range(1, ranks))
                }
                sums += list(arrived.values()) + pieces[:1]
                weights.append(part_weights)
                maxima.append(part_max)
        else:
            new_state, *chunk_parts, part_weights, part_max = call(
                next_body,
                [(CORES * packed_rows + query_shape[0], width)] + forward_shapes,
                "update_forward",
                2 * matmul_cost,
                states + query_parts + grads + tiles,
                chunk_scratch,
            )
            states, weights, maxima = [new_state], [part_weights], [part_max]
            arrived = {
                turn: exchange(chunk_parts[turn], page=CORES * turn)
                for turn in reversed(range(1, ranks))
            }
            sums = chunk_parts[:1] + list(arrived.values())
            new_states = states + [
                exchange(states[0], query=turn) for turn in range(1, query_devices)
            ]
        (merged,) = call(
            merge_body if repeat else first_merge_body,
            [chunk_shape],
            "merge",
            2**20,
            query_parts + sums,
        )
        all_merged = [merged] + [
            exchange(merged, page=CORES * turn) for turn in range(1, ranks)
        ]
        if last:
            all_merged = call(
                join_body, [(width + TAIL, query_rows)], "join", 2**20, all_merged, chunk_scratch
            )
            all_joined = [
                to_device(all_merged[0], query=turn) for turn in range(query_devices)
            ]
        own_grad, mate_grad, squares = call(
            backward_body,
            packed_shapes + [(devices, 1, width)],
            "backward",
            3 * matmul_cost,
            weights + maxima + states + query_parts + list(all_merged),
            scratch=() if last else chunk_scratch,
        )
        grads = [own_grad, mate_grad]
        tiles = [
            lax.all_to_all(
                squares, ("page", "query", "head"), split_axis=0, concat_axis=0, tiled=True
            )
        ]

    other_packs = [
        packs[part] if part == turn else query_part(turn, part)
        for turn in range(1, query_devices)
        for part in range(1, query_devices)
    ]
    operands = new_states + all_joined[1:] + other_packs
    pages = []
    for at, grad in ((1, mate_grad), (0, own_grad)):
        pages += call(
            page_body(at),
            [(query_devices * packed_rows, width)],
            "page_update",
            3 * matmul_cost // 2,
            tiles + [grad] + operands,
            after=pages,
        )
    pages = [pages[1], exchange(pages[0], page=1)]

    def last_body(*refs):
        page_refs, (keys_out, values_out, bias_out) = refs[:CORES], refs[CORES:]
        _, core, me = places()
        for turn, flip in itertools.product(range(query_devices), range(CORES)):
            keys, values, bias = read_pack(part_of(page_refs[flip], turn))
            head = CORES * (me ^ turn) + (core ^ flip)
            keys_out[head] = keys
            values_out[head] = values
            bias_row = jnp.concatenate([bias[row : row + 1] for row in range(bias_rows)], axis=1)
            bias_out[pl.ds(head, 1), :] = bias_row

    return tuple(
        call(
            last_body,
            [compact_keys.shape, compact_values.shape, slot_bias.shape],
            "unpack",
            2**20,
            pages,
        )
    )


def from_partner(value, axis, stride):
    mask = 2**stride
    pairs = [(source, source ^ mask) for source in range(lax.axis_size(axis))]
    return lax.ppermute(value, axis, pairs)


def squared_sums(grad_keys, grad_values, grad_bias):
    return jnp.stack(
        [
            jnp.sum(grad_keys * grad_keys),
            jnp.sum(grad_values * grad_values),
            jnp.sum(grad_bias * grad_bias),
        ]
    )


def apply_update(states, grads, totals, entry_count, slot_total):
    key_state, value_state, bias_state = states
    grad_keys, grad_values, grad_bias = grads
    rms_keys = jnp.sqrt(totals[0] / entry_count + EPSILON)
    rms_values = jnp.sqrt(totals[1] / entry_count + EPSILON)
    rms_bias = jnp.sqrt(totals[2] / slot_total + EPSILON)
    return (
        key_state - RATE_KEYS * grad_keys / rms_keys,
        value_state - RATE_VALUES * grad_values / rms_values,
        bias_state - RATE_BIAS * grad_bias / rms_bias,
    )


def local_gradients(queries, targets, visible, compact_keys, compact_values, slot_bias):
    score_scale = 1.0 / math.sqrt(queries.shape[2])
    scores = jnp.einsum("hqd,hsd->hqs", queries, compact_keys, precision=HIGHEST) * score_scale
    scores = jnp.where(visible, scores + slot_bias[:, None, :], MASKED)
    local_max = jnp.max(scores, axis=2)
    row_max = lax.pmax(local_max, "page")
    weights = jnp.where(visible, jnp.exp(scores - row_max[:, :, None]), 0.0)
    local_sum = jnp.einsum("hqs,hsd->hqd", weights, compact_values, precision=HIGHEST)
    row_total, row_sum = lax.psum((jnp.sum(weights, axis=2), local_sum), "page")
    attention = weights / row_total[:, :, None]
    output = row_sum / row_total[:, :, None]
    residual = output - targets
    grad_values = jnp.einsum("hqs,hqd->hsd", attention, residual, precision=HIGHEST)
    row_delta = jnp.sum(residual * output, axis=2)
    grad_probs = jnp.einsum("hqd,hsd->hqs", residual, compact_values, precision=HIGHEST)
    grad_scores = attention * (grad_probs - row_delta[:, :, None])
    grad_bias = jnp.sum(grad_scores, axis=1)
    grad_keys = jnp.einsum("hqs,hqd->hsd", grad_scores, queries, precision=HIGHEST) * score_scale
    return (grad_keys, grad_values, grad_bias)


def per_device(queries, compact_keys, compact_values, slot_bias, targets, positions, assignment):
    page_number = assignment[lax.axis_index("page")]
    local_heads = compact_keys.shape[0]
    slot_total = local_heads * lax.axis_size("head") * compact_keys.shape[1] * lax.axis_size("page")
    entry_count = slot_total * compact_keys.shape[2]
    query_count = lax.axis_size("query")
    heads_kept = max(local_heads // query_count, 1)
    query_parts = max(query_count // local_heads, 1)
    part_rows = queries.shape[1] // query_parts

    def split_items(array):
        width = array.shape[2]
        array = array.reshape(local_heads // heads_kept, heads_kept, query_parts, part_rows, width)
        array = jnp.transpose(array, (0, 2, 1, 3, 4))
        return array.reshape(query_count, heads_kept, part_rows, width)

    def join_items(array):
        width = array.shape[3]
        array = jnp.transpose(array, (1, 0, 2, 3))
        return array.reshape(heads_kept, query_count * part_rows, width)

    position_column = positions.astype(jnp.float32)[:, :, None]
    got_queries, got_targets, got_positions = (
        lax.all_to_all(split_items(queries), "query", split_axis=0, concat_axis=0, tiled=True),
        lax.all_to_all(split_items(targets), "query", split_axis=0, concat_axis=0, tiled=True),
        lax.all_to_all(
            split_items(position_column), "query", split_axis=0, concat_axis=0, tiled=True
        ),
    )
    group_queries = join_items(got_queries)
    group_targets = join_items(got_targets)
    group_positions = join_items(got_positions)[:, :, 0]
    visible = (page_number.astype(jnp.float32) <= jnp.floor(group_positions / PAGE_LEN))[:, :, None]
    query_index = lax.axis_index("query")
    first_head = query_index // query_parts * heads_kept
    key_state = lax.dynamic_slice_in_dim(compact_keys, first_head, heads_kept, 0)
    value_state = lax.dynamic_slice_in_dim(compact_values, first_head, heads_kept, 0)
    bias_state = lax.dynamic_slice_in_dim(slot_bias, first_head, heads_kept, 0)
    counted = (query_index % query_parts == 0).astype(jnp.float32)
    for repeat in range(STEPS):
        grads = local_gradients(
            group_queries, group_targets, visible, key_state, value_state, bias_state
        )
        for bit in range(query_parts.bit_length() - 1):
            partner = from_partner((grads[0], grads[1], grads[2]), "query", bit)
            grads = (grads[0] + partner[0], grads[1] + partner[1], grads[2] + partner[2])
        totals = lax.psum(
            squared_sums(grads[0], grads[1], grads[2]) * counted, ("page", "query", "head")
        )
        key_state, value_state, bias_state = apply_update(
            (key_state, value_state, bias_state), grads, totals, entry_count, slot_total
        )
    all_keys, all_values, all_bias = (
        lax.all_gather(key_state, "query", axis=0, tiled=True),
        lax.all_gather(value_state, "query", axis=0, tiled=True),
        lax.all_gather(bias_state, "query", axis=0, tiled=True),
    )
    slot_rows = compact_keys.shape[1]
    head_width = compact_keys.shape[2]
    all_keys = all_keys.reshape(
        local_heads // heads_kept, query_parts, heads_kept, slot_rows, head_width
    )[:, 0]
    all_values = all_values.reshape(
        local_heads // heads_kept, query_parts, heads_kept, slot_rows, head_width
    )[:, 0]
    all_bias = all_bias.reshape(local_heads // heads_kept, query_parts, heads_kept, slot_rows)[:, 0]
    return (
        all_keys.reshape(local_heads, slot_rows, head_width),
        all_values.reshape(local_heads, slot_rows, head_width),
        all_bias.reshape(local_heads, slot_rows),
    )


def solution(mesh):
    placed = (
        P("head", "query", None),
        P("head", "page", None),
        P("head", "page", None),
        P("head", "page"),
        P("head", "query", None),
        P("head", "query"),
        P(),
    )

    def program(*args):
        plan = direct_per_device if direct_plan_fits(mesh, args[0], args[1]) else per_device
        return jax.shard_map(
            plan,
            mesh=mesh,
            in_specs=placed,
            out_specs=(P("head", "page", None), P("head", "page", None), P("head", "page")),
            check_vma=False,
        )(*args)

    return program
```

```python
import itertools
import math

import jax
import jax.numpy as jnp
from jax import lax
from jax.experimental import pallas as pl
from jax.experimental.pallas import tpu as pltpu
from jax.sharding import PartitionSpec as P

STEPS = 2
PAGE_LEN = 32768


MASKED = -1e30
EPSILON = 1e-06
RATE_KEYS = 0.05
RATE_VALUES = 0.05
RATE_BIAS = 0.2
HIGHEST = lax.Precision.HIGHEST
TAIL = 8
CORES = 2


def exchange(value, **masks):
    axes = tuple(masks)
    sizes = [lax.axis_size(axis) for axis in axes]

    def flat(place):
        index = 0
        for size, at in zip(sizes, place):
            index = index * size + at
        return index

    pairs = [
        (flat(place), flat([at ^ mask for at, mask in zip(place, masks.values())]))
        for place in itertools.product(*map(range, sizes))
    ]
    return lax.ppermute(value, axes, pairs)


def halves(value):
    high = value.astype(jnp.bfloat16)
    return high, (value - high.astype(jnp.float32)).astype(jnp.bfloat16)


def one_pass(left, right, left_dim, right_dim):
    return lax.dot_general(
        left,
        right,
        (((left_dim,), (right_dim,)), ((), ())),
        preferred_element_type=jnp.float32,
    )


def dot_deep(left, right, left_dim, right_dim):
    left = jnp.concatenate([left[0], left[1], left[0]], axis=left_dim)
    right = jnp.concatenate([right[0], right[0], right[1]], axis=right_dim)
    return one_pass(left, right, left_dim, right_dim)


def dot_narrow(left, right, left_dim, right_dim):
    both = one_pass(
        left[0], jnp.concatenate(right, axis=1 - right_dim), left_dim, right_dim
    )
    count = both.shape[1] // 2
    cross = both[:, count:] + one_pass(left[1], right[0], left_dim, right_dim)
    return both[:, :count] + cross


def dot_low(left, right, left_dim, right_dim):
    both = one_pass(jnp.concatenate(left, axis=1 - left_dim), right[0], left_dim, right_dim)
    count = both.shape[0] // 2
    cross = both[count:, :] + one_pass(left[0], right[1], left_dim, right_dim)
    return both[:count, :] + cross


def call(body, out_shapes, name, cost, operands, scratch=(), after=(), space=pltpu.VMEM, vmem=32):
    spaces = [space] * len(operands) + [pl.ANY] * len(after)
    count = len(operands)

    def without_after(*refs):
        body(*refs[:count], *refs[count + len(after) :])

    return pl.pallas_call(
        without_after,
        out_shape=[jax.ShapeDtypeStruct(shape, jnp.float32) for shape in out_shapes],
        in_specs=[pl.BlockSpec(memory_space=space) for space in spaces],
        out_specs=[pl.BlockSpec(memory_space=pltpu.VMEM) for _ in out_shapes],
        scratch_shapes=scratch,
        compiler_params=pltpu.CompilerParams(vmem_limit_bytes=vmem * 2**20),
        cost_estimate=pl.CostEstimate(flops=cost, bytes_accessed=2**20, transcendentals=0),
        name=name,
    )(*operands, *after)


def row_as_tail(row, width):
    rows = [row[:, at : at + width] for at in range(0, row.shape[1], width)]
    rows.append(jnp.zeros((TAIL - len(rows), width), row.dtype))
    return jnp.concatenate(rows, axis=0)


def tail_as_row(ref, start, count):
    return jnp.concatenate([ref[start + at : start + at + 1, :] for at in range(count)], axis=1)


def row_as_column(row, width):
    parts = []
    for at in range(0, row.shape[1], width):
        parts.append(jnp.broadcast_to(row[:, at : at + width], (width, width)).T)
    return jnp.concatenate(parts, axis=0)


def column_sums(value, width):
    groups = [value[:, at : at + width] for at in range(0, value.shape[1], width)]
    partial = sum(groups[1:], groups[0])
    blocks = [
        jnp.sum(partial[at : at + width, :].T, axis=0, keepdims=True)
        for at in range(0, value.shape[0], width)
    ]
    return jnp.concatenate(blocks, axis=1)


def direct_plan_fits(mesh, queries, compact_keys):
    sizes = [mesh.shape[axis] for axis in ("page", "query", "head")]
    pages, query_devices, head_devices = sizes
    local_heads = queries.shape[0] // head_devices
    part_rows = queries.shape[1] // query_devices
    slot_rows = compact_keys.shape[1] // pages
    width = queries.shape[2]
    if any(size & (size - 1) for size in sizes) or pages < CORES or width % 128:
        return False
    if local_heads != CORES * query_devices:
        return False
    ranks = pages // CORES
    chunk = part_rows * query_devices // ranks
    return (
        part_rows * query_devices % ranks == 0
        and chunk % 128 == 0
        and part_rows % (8 * ranks) == 0
        and (part_rows // ranks % 128 == 0 or 1024 % (part_rows // ranks * 8) == 0)
        and slot_rows % width == 0
        and part_rows % width == 0
        and max(slot_rows, part_rows) < TAIL * width
    )


def direct_per_device(
    queries, compact_keys, compact_values, slot_bias, targets, positions, assignment
):
    local_heads, part_rows, width = queries.shape
    slot_rows = compact_keys.shape[1]
    query_devices = lax.axis_size("query")
    head_devices = lax.axis_size("head")
    ranks = lax.axis_size("page") // CORES
    query_rows = part_rows * query_devices
    chunk, piece = query_rows // ranks, part_rows // ranks
    slot_total = local_heads * head_devices * slot_rows * lax.axis_size("page")
    entry_total = slot_total * width
    score_scale = 1.0 / math.sqrt(width)
    slots = CORES * slot_rows
    devices = ranks * CORES * query_devices * head_devices
    pos_rows = part_rows // width
    bias_rows = slot_rows // width
    packed_rows = 2 * slot_rows + TAIL
    packed_shapes = [(packed_rows, width)] * 2
    matmul_cost = 3 * 2 * slots * query_rows * width

    def places():
        page = lax.axis_index("page")
        return page // CORES, page % CORES, lax.axis_index("query")

    def to_device(value, **masks):
        masks = {axis: mask for axis, mask in masks.items() if mask}
        return exchange(value, **masks) if masks else value

    def pack_queries(head, rank, queries, targets, out):
        rows = pl.ds(pl.multiple_of(rank * piece, piece), piece)
        return [
            (queries.at[head], out.at[pl.ds(0, part_rows)]),
            (targets.at[head, rows], out.at[pl.ds(part_rows, piece)]),
        ]

    def pack_state(head, keys, values, out):
        return [
            (keys.at[head], out.at[pl.ds(0, slot_rows)]),
            (values.at[head], out.at[pl.ds(slot_rows, slot_rows)]),
        ]

    def start_all(copies, sems, first=0):
        copies = [
            pltpu.make_async_copy(source, target, sems.at[first + at])
            for at, (source, target) in enumerate(copies)
        ]
        for copy in copies:
            copy.start()
        return copies

    def position_tail(head, positions_ref):
        return row_as_tail(positions_ref[pl.ds(head, 1), :].astype(jnp.float32), width)

    def state_tail(head, page, bias_ref, assignment_ref):
        page_start = (assignment_ref[page] * PAGE_LEN).astype(jnp.float32)
        tail = row_as_tail(bias_ref[pl.ds(head, 1), :], width)
        return jnp.concatenate(
            [tail[: TAIL - 1], jnp.full((1, width), page_start, jnp.float32)], axis=0
        )

    def send_body(
        queries, keys, values, biases, targets, positions, assignment, state_out, *refs
    ):
        query_outs = refs[: query_devices - 1]
        bias_ref, positions_ref, assignment_ref, sems = refs[query_devices - 1 :]
        rank, core, me = places()
        heads = [CORES * (me ^ turn) + core for turn in range(1, query_devices)]
        mate_head = CORES * me + (core ^ 1)
        small = start_all(
            [(assignment, assignment_ref), (positions, positions_ref), (biases, bias_ref)], sems
        )
        copies = pack_state(mate_head, keys, values, state_out)
        for head, out in zip(heads, query_outs):
            copies += pack_queries(head, rank, queries, targets, out)
        copies = start_all(copies, sems, 3)
        for copy in small:
            copy.wait()
        state_out[2 * slot_rows :, :] = state_tail(
            mate_head, CORES * rank + core, bias_ref, assignment_ref
        )
        for head, out in zip(heads, query_outs):
            out[part_rows + piece :, :] = position_tail(head, positions_ref)
        for copy in copies:
            copy.wait()

    def own_body(
        queries, keys, values, biases, targets, positions, assignment, state_out, query_out, *refs
    ):
        bias_ref, positions_ref, assignment_ref, sems = refs
        rank, core, me = places()
        head = CORES * me + core
        small = start_all(
            [(assignment, assignment_ref), (positions, positions_ref), (biases, bias_ref)], sems
        )
        copies = pack_state(head, keys, values, state_out)
        copies += pack_queries(head, rank, queries, targets, query_out)
        copies = start_all(copies, sems, 3)
        for copy in small:
            copy.wait()
        state_out[2 * slot_rows :, :] = state_tail(
            head, CORES * rank + core, bias_ref, assignment_ref
        )
        query_out[part_rows + piece :, :] = position_tail(head, positions_ref)
        for copy in copies:
            copy.wait()

    state_shape, query_shape = (packed_rows, width), (part_rows + piece + TAIL, width)
    small_scratch = [
        pltpu.VMEM(slot_bias.shape, jnp.float32),
        pltpu.VMEM(positions.shape, jnp.int32),
        pltpu.SMEM(assignment.shape, jnp.int32),
    ]
    arguments = [
        queries, compact_keys, compact_values, slot_bias, targets, positions, assignment
    ]
    mate_state, *sent_queries = call(
        send_body,
        [state_shape] + [query_shape] * (query_devices - 1),
        "pack",
        2**20,
        arguments,
        small_scratch + [pltpu.SemaphoreType.DMA((3 + 2 * query_devices,))],
        space=pl.ANY,
        vmem=60,
    )
    own_state, own_queries = call(
        own_body,
        [state_shape, query_shape],
        "own",
        2**24,
        arguments,
        small_scratch + [pltpu.SemaphoreType.DMA((7,))],
        space=pl.ANY,
    )
    packs = [own_queries] + list(sent_queries)

    def query_part(turn, part):
        return to_device(packs[part], query=turn ^ part)

    query_parts = [query_part(0, part) for part in range(query_devices)]
    states = [own_state, exchange(mate_state, page=1)]

    def in_columns(parts, axis):
        return jnp.concatenate(
            [
                lax.slice_in_dim(part, at * piece, (at + 1) * piece, axis=axis)
                for at in range(ranks)
                for part in parts
            ],
            axis=axis,
        )

    def read_queries(query_refs):
        return halves(in_columns([ref[:part_rows, :] for ref in query_refs], 0))

    def part_of(ref, at):
        return ref.at[pl.ds(at * packed_rows, packed_rows)]

    def parts_of(refs):
        return refs if len(refs) == CORES else [part_of(refs[0], at) for at in range(CORES)]

    def step_sizes(tile_refs):
        row = jnp.sum(tile_refs[0][...], axis=0)
        return (
            RATE_KEYS / jnp.sqrt(row[:, 0:1] / entry_total + EPSILON),
            RATE_VALUES / jnp.sqrt(row[:, 1:2] / entry_total + EPSILON),
            RATE_BIAS / jnp.sqrt(row[:, 2:3] / slot_total + EPSILON),
        )

    def read_pack(ref):
        return ref[:slot_rows, :], ref[slot_rows : 2 * slot_rows, :], ref[2 * slot_rows :, :]

    def store_pack(ref, values):
        ref[:slot_rows, :] = values[0]
        ref[slot_rows : 2 * slot_rows, :] = values[1]
        ref[2 * slot_rows :, :] = values[2]

    def updated(state, grads, sizes):
        return [value - size * grad for value, grad, size in zip(state, grads, sizes)]

    def page_scores(ref, queries, positions):
        scores = dot_deep(halves(ref[:slot_rows, :]), queries, 1, 1) * score_scale
        bias = row_as_column(tail_as_row(ref, 2 * slot_rows, bias_rows), width)
        scores = scores + jnp.concatenate([bias] * (positions.shape[1] // width), axis=1)
        page_start = ref[packed_rows - 1 : packed_rows, 0:1]
        visible = jnp.broadcast_to(positions >= page_start, scores.shape)
        return jnp.where(visible, scores, MASKED), visible

    def read_positions(query_refs):
        return in_columns(
            [tail_as_row(ref, part_rows + piece, pos_rows) for ref in query_refs], 1
        )

    def forward(state_refs, query_refs, chunk_outs, weights_out, max_out, chunks):
        rank, _, _ = places()
        all_queries, positions = read_queries(query_refs), read_positions(query_refs)
        all_scores, all_visible = [], []
        for at, ref in enumerate(state_refs):
            scores, visible = page_scores(ref, all_queries, positions)
            all_scores.append(scores)
            all_visible.append(visible)
        row_max = jnp.max(all_scores[0], axis=0, keepdims=True)
        for scores in all_scores[1:]:
            row_max = jnp.maximum(row_max, jnp.max(scores, axis=0, keepdims=True))
        row_total = jnp.zeros_like(row_max)
        row_sum = jnp.zeros((width, query_rows), jnp.float32)
        for at, ref in enumerate(state_refs):
            weights = jnp.where(all_visible[at], jnp.exp(all_scores[at] - row_max), 0.0)
            weights_out[at * slot_rows : (at + 1) * slot_rows, :] = weights
            row_total = row_total + jnp.sum(weights, axis=0, keepdims=True)
            values = halves(ref[slot_rows : 2 * slot_rows, :])
            row_sum = row_sum + dot_low(values, halves(weights), 0, 0)
        max_out[...] = jnp.broadcast_to(row_max, (TAIL, query_rows))
        tail = jnp.concatenate(
            [row_max, row_total, jnp.zeros((TAIL - 2, query_rows), jnp.float32)], axis=0
        )
        for at in range(ranks):
            columns = slice(at * chunk, (at + 1) * chunk)
            chunks[at, :width, :] = row_sum[:, columns]
            chunks[at, width:, :] = tail[:, columns]
        for turn in range(ranks):
            chunk_outs[turn][...] = chunks[rank ^ turn]

    chunk_shape = (width + TAIL, chunk)
    forward_shapes = [chunk_shape] * ranks + [(slots, query_rows), (TAIL, query_rows)]
    chunk_scratch = [pltpu.VMEM((ranks,) + chunk_shape, jnp.float32)]

    fold = max(1, 128 // piece)
    folded, columns = width // fold, fold * piece
    piece_shape = (folded + TAIL, columns)
    piece_scratch = [pltpu.VMEM((ranks,) + piece_shape, jnp.float32)]

    def fold_rows(value):
        groups = [value[at * folded : (at + 1) * folded, :] for at in range(fold)]
        return jnp.concatenate(groups, axis=1)

    def unfold_rows(value):
        groups = [value[:, at * piece : (at + 1) * piece] for at in range(fold)]
        return jnp.concatenate(groups, axis=0)

    def rows_tail(rows):
        empty = jnp.zeros((TAIL - len(rows), columns), jnp.float32)
        return jnp.concatenate(rows + [empty], axis=0)

    def part_body(*refs):
        state_refs, (query_ref, *refs) = refs[:CORES], refs[CORES:]
        piece_outs, (weights_out, max_out, pieces) = refs[:ranks], refs[ranks:]
        rank, _, _ = places()
        queries = halves(query_ref[:part_rows, :])
        position_row = tail_as_row(query_ref, part_rows + piece, pos_rows)
        all_scores, all_visible = [], []
        for ref in state_refs:
            scores, visible = page_scores(ref, queries, position_row)
            all_scores.append(scores)
            all_visible.append(visible)
        row_max = jnp.max(all_scores[0], axis=0, keepdims=True)
        for scores in all_scores[1:]:
            row_max = jnp.maximum(row_max, jnp.max(scores, axis=0, keepdims=True))
        row_total = jnp.zeros_like(row_max)
        row_sum = jnp.zeros((width, part_rows), jnp.float32)
        for at, ref in enumerate(state_refs):
            weights = jnp.where(all_visible[at], jnp.exp(all_scores[at] - row_max), 0.0)
            weights_out[at * slot_rows : (at + 1) * slot_rows, :] = weights
            row_total = row_total + jnp.sum(weights, axis=0, keepdims=True)
            values = halves(ref[slot_rows : 2 * slot_rows, :])
            row_sum = row_sum + dot_low(values, halves(weights), 0, 0)
        max_out[...] = jnp.broadcast_to(row_max, (TAIL, part_rows))
        for at in range(ranks):
            own = slice(at * piece, (at + 1) * piece)
            pieces[at, :folded, :] = fold_rows(row_sum[:, own])
            pieces[at, folded:, :] = rows_tail(
                [jnp.concatenate([row[:, own]] * fold, axis=1) for row in (row_max, row_total)]
            )
        for turn in range(ranks):
            piece_outs[turn][...] = pieces[rank ^ turn]

    part_shapes = [piece_shape] * ranks + [(slots, part_rows), (TAIL, part_rows)]

    def next_body(*refs):
        state_refs, refs = refs[:2], refs[2:]
        query_refs, refs = refs[:query_devices], refs[query_devices:]
        grad_refs, refs = refs[:2], refs[2:]
        tile_refs, refs = refs[: len(tiles)], refs[len(tiles) :]
        refs[0][CORES * packed_rows :, :] = query_refs[0][...]
        state_outs, refs = parts_of(refs[:1]), refs[1:]
        chunk_outs, refs = refs[:ranks], refs[ranks:]
        sizes = step_sizes(tile_refs)
        for at in range(2):
            state = read_pack(state_refs[at])
            store_pack(state_outs[at], updated(state, read_pack(grad_refs[at]), sizes))
        forward(state_outs, query_refs, chunk_outs, *refs)

    def merged_chunk(query_refs, sums, maxima, totals, out):
        targets = jnp.concatenate(
            [ref[part_rows : part_rows + piece, :] for ref in query_refs], axis=0
        )
        row_max = maxima[0]
        for other in maxima[1:]:
            row_max = jnp.maximum(row_max, other)
        row_total = jnp.zeros_like(row_max)
        row_sum = jnp.zeros((width, chunk), jnp.float32)
        for part_sum, part_max, part_total in zip(sums, maxima, totals):
            factor = jnp.exp(part_max - row_max)
            row_total = row_total + part_total * factor
            row_sum = row_sum + part_sum * factor
        output = row_sum / row_total
        residual = output - targets.T
        row_delta = jnp.sum(residual * output, axis=0, keepdims=True)
        out[:width, :] = residual
        out[width:, :] = jnp.concatenate(
            [row_max, row_total, row_delta, jnp.zeros((TAIL - 3, chunk), jnp.float32)], axis=0
        )

    def first_merge_body(*refs):
        query_refs, (*piece_refs, merged_out) = refs[:query_devices], refs[query_devices:]

        def joined(read):
            return [
                jnp.concatenate([read(ref) for ref in piece_refs[turn::ranks]], axis=1)
                for turn in range(ranks)
            ]

        merged_chunk(
            query_refs,
            joined(lambda ref: unfold_rows(ref[:folded, :])),
            joined(lambda ref: ref[folded : folded + 1, :piece]),
            joined(lambda ref: ref[folded + 1 : folded + 2, :piece]),
            merged_out,
        )

    def merge_body(*refs):
        query_refs, (*chunk_refs, merged_out) = refs[:query_devices], refs[query_devices:]
        merged_chunk(
            query_refs,
            [ref[:width, :] for ref in chunk_refs],
            [ref[width : width + 1, :] for ref in chunk_refs],
            [ref[width + 1 : width + 2, :] for ref in chunk_refs],
            merged_out,
        )

    def page_gradients(weights, factor, state_ref, all_queries, residual, row_delta):
        attention = weights * factor
        grad_values = dot_narrow(halves(attention), residual, 1, 1)
        grad_probs = dot_deep(halves(state_ref[slot_rows : 2 * slot_rows, :]), residual, 1, 0)
        grad_scores = attention * (grad_probs - row_delta)
        grad_keys = dot_narrow(halves(grad_scores), all_queries, 1, 0) * score_scale
        grad_bias = column_sums(grad_scores, width)
        return grad_keys, grad_values, row_as_tail(grad_bias, width)

    def split_merged(joined):
        row_max, row_total, row_delta = (
            joined[width + at : width + at + 1, :] for at in range(3)
        )
        return halves(joined[:width, :]), row_max, row_total, row_delta

    def read_chunks(merged_refs, chunks):
        rank, _, _ = places()
        for turn, ref in enumerate(merged_refs):
            chunks[rank ^ turn] = ref[...]
        return [chunks[at] for at in range(ranks)]

    def join_body(*refs):
        *merged_refs, joined_out, chunks = refs
        joined_out[...] = jnp.concatenate(read_chunks(merged_refs, chunks), axis=1)

    def backward_body(*refs):
        weights_refs, refs = refs[: len(weights)], refs[len(weights) :]
        max_refs, refs = refs[: len(weights)], refs[len(weights) :]
        state_refs, refs = parts_of(refs[: len(states)]), refs[len(states) :]
        query_refs, refs = refs[:query_devices], refs[query_devices:]
        merged_refs, refs = refs[: len(all_merged)], refs[len(all_merged) :]
        grad_outs, (squares_out, *scratch) = refs[:2], refs[2:]
        if len(states) < CORES:
            joined = merged_refs[0][...]
            all_queries = read_queries(query_refs)
        else:
            chunks = read_chunks(merged_refs, *scratch)
            joined = jnp.concatenate(
                [
                    value[:, part * piece : (part + 1) * piece]
                    for part in range(query_devices)
                    for value in chunks
                ],
                axis=1,
            )
            all_queries = halves(
                jnp.concatenate([ref[:part_rows, :] for ref in query_refs], axis=0)
            )
        residual, row_max, row_total, row_delta = split_merged(joined)
        maxima = jnp.concatenate([ref[0:1, :] for ref in max_refs], axis=1)
        factor = jnp.exp(maxima - row_max) / row_total
        squares = [jnp.zeros((1, width), jnp.float32)] * 3
        for at, (ref, out) in enumerate(zip(state_refs, grad_outs)):
            rows = slice(at * slot_rows, (at + 1) * slot_rows)
            page_weights = jnp.concatenate([part[rows, :] for part in weights_refs], axis=1)
            grads = page_gradients(page_weights, factor, ref, all_queries, residual, row_delta)
            store_pack(out, grads)
            for which, grad in enumerate(grads):
                squares[which] = squares[which] + jnp.sum(grad * grad, axis=0, keepdims=True)
        lanes = lax.broadcasted_iota(jnp.int32, (1, width), 1)
        row = jnp.zeros((1, width), jnp.float32)
        for which, square in enumerate(squares):
            row = jnp.where(lanes == which, jnp.sum(square, axis=1, keepdims=True), row)
        for at in range(devices):
            squares_out[at] = row

    def page_body(at):
        def body(tile_ref, grad_ref, own_state_ref, *refs):
            state_refs, refs = refs[: query_devices - 1], refs[query_devices - 1 :]
            joined_refs, (*pack_refs, out) = refs[: query_devices - 1], refs[query_devices - 1 :]
            sizes = step_sizes([tile_ref])
            state = read_pack(part_of(own_state_ref, at))
            store_pack(part_of(out, 0), updated(state, read_pack(grad_ref), sizes))
            for turn, (state_ref, joined_ref) in enumerate(zip(state_refs, joined_refs), 1):
                query_refs = [state_ref.at[pl.ds(CORES * packed_rows, query_shape[0])]]
                query_refs += pack_refs[(turn - 1) * (query_devices - 1) :][: query_devices - 1]
                residual, row_max, row_total, row_delta = split_merged(joined_ref[...])
                all_queries = read_queries(query_refs)
                ref = part_of(state_ref, at)
                scores, visible = page_scores(ref, all_queries, read_positions(query_refs))
                weights = jnp.where(visible, jnp.exp(scores - row_max), 0.0)
                grads = page_gradients(
                    weights, 1.0 / row_total, ref, all_queries, residual, row_delta
                )
                store_pack(part_of(out, turn), updated(read_pack(ref), grads, sizes))

        return body

    for repeat in range(STEPS):
        last = repeat == STEPS - 1
        if repeat == 0:
            sums, weights, maxima = [], [], []
            for query_pack in query_parts:
                *pieces, part_weights, part_max = call(
                    part_body,
                    part_shapes,
                    "forward",
                    2 * matmul_cost // query_devices,
                    states + [query_pack],
                    piece_scratch,
                    after=maxima[-1:],
                )
                arrived = {
                    turn: exchange(pieces[turn], page=CORES * turn)
                    for turn in reversed(range(1, ranks))
                }
                sums += list(arrived.values()) + pieces[:1]
                weights.append(part_weights)
                maxima.append(part_max)
        else:
            new_state, *chunk_parts, part_weights, part_max = call(
                next_body,
                [(CORES * packed_rows + query_shape[0], width)] + forward_shapes,
                "update_forward",
                2 * matmul_cost,
                states + query_parts + grads + tiles,
                chunk_scratch,
            )
            states, weights, maxima = [new_state], [part_weights], [part_max]
            arrived = {
                turn: exchange(chunk_parts[turn], page=CORES * turn)
                for turn in reversed(range(1, ranks))
            }
            sums = chunk_parts[:1] + list(arrived.values())
            new_states = states + [
                exchange(states[0], query=turn) for turn in range(1, query_devices)
            ]
        (merged,) = call(
            merge_body if repeat else first_merge_body,
            [chunk_shape],
            "merge",
            2**20,
            query_parts + sums,
        )
        all_merged = [merged] + [
            exchange(merged, page=CORES * turn) for turn in range(1, ranks)
        ]
        if last:
            all_merged = call(
                join_body, [(width + TAIL, query_rows)], "join", 2**20, all_merged, chunk_scratch
            )
            all_joined = [
                to_device(all_merged[0], query=turn) for turn in range(query_devices)
            ]
        own_grad, mate_grad, squares = call(
            backward_body,
            packed_shapes + [(devices, 1, width)],
            "backward",
            3 * matmul_cost,
            weights + maxima + states + query_parts + list(all_merged),
            scratch=() if last else chunk_scratch,
        )
        grads = [own_grad, mate_grad]
        tiles = [
            lax.all_to_all(
                squares, ("page", "query", "head"), split_axis=0, concat_axis=0, tiled=True
            )
        ]

    other_packs = [
        packs[part] if part == turn else query_part(turn, part)
        for turn in range(1, query_devices)
        for part in range(1, query_devices)
    ]
    operands = new_states + all_joined[1:] + other_packs
    pages = []
    for at, grad in ((1, mate_grad), (0, own_grad)):
        pages += call(
            page_body(at),
            [(query_devices * packed_rows, width)],
            "page_update",
            3 * matmul_cost // 2,
            tiles + [grad] + operands,
            after=pages,
        )
    pages = [pages[1], exchange(pages[0], page=1)]

    def last_body(*refs):
        page_refs, (keys_out, values_out, bias_out) = refs[:CORES], refs[CORES:]
        _, core, me = places()
        for turn, flip in itertools.product(range(query_devices), range(CORES)):
            keys, values, bias = read_pack(part_of(page_refs[flip], turn))
            head = CORES * (me ^ turn) + (core ^ flip)
            keys_out[head] = keys
            values_out[head] = values
            bias_row = jnp.concatenate([bias[row : row + 1] for row in range(bias_rows)], axis=1)
            bias_out[pl.ds(head, 1), :] = bias_row

    return tuple(
        call(
            last_body,
            [compact_keys.shape, compact_values.shape, slot_bias.shape],
            "unpack",
            2**20,
            pages,
        )
    )


def from_partner(value, axis, stride):
    mask = 2**stride
    pairs = [(source, source ^ mask) for source in range(lax.axis_size(axis))]
    return lax.ppermute(value, axis, pairs)


def squared_sums(grad_keys, grad_values, grad_bias):
    return jnp.stack(
        [
            jnp.sum(grad_keys * grad_keys),
            jnp.sum(grad_values * grad_values),
            jnp.sum(grad_bias * grad_bias),
        ]
    )


def apply_update(states, grads, totals, entry_count, slot_total):
    key_state, value_state, bias_state = states
    grad_keys, grad_values, grad_bias = grads
    rms_keys = jnp.sqrt(totals[0] / entry_count + EPSILON)
    rms_values = jnp.sqrt(totals[1] / entry_count + EPSILON)
    rms_bias = jnp.sqrt(totals[2] / slot_total + EPSILON)
    return (
        key_state - RATE_KEYS * grad_keys / rms_keys,
        value_state - RATE_VALUES * grad_values / rms_values,
        bias_state - RATE_BIAS * grad_bias / rms_bias,
    )


def local_gradients(queries, targets, visible, compact_keys, compact_values, slot_bias):
    score_scale = 1.0 / math.sqrt(queries.shape[2])
    scores = jnp.einsum("hqd,hsd->hqs", queries, compact_keys, precision=HIGHEST) * score_scale
    scores = jnp.where(visible, scores + slot_bias[:, None, :], MASKED)
    local_max = jnp.max(scores, axis=2)
    row_max = lax.pmax(local_max, "page")
    weights = jnp.where(visible, jnp.exp(scores - row_max[:, :, None]), 0.0)
    local_sum = jnp.einsum("hqs,hsd->hqd", weights, compact_values, precision=HIGHEST)
    row_total, row_sum = lax.psum((jnp.sum(weights, axis=2), local_sum), "page")
    attention = weights / row_total[:, :, None]
    output = row_sum / row_total[:, :, None]
    residual = output - targets
    grad_values = jnp.einsum("hqs,hqd->hsd", attention, residual, precision=HIGHEST)
    row_delta = jnp.sum(residual * output, axis=2)
    grad_probs = jnp.einsum("hqd,hsd->hqs", residual, compact_values, precision=HIGHEST)
    grad_scores = attention * (grad_probs - row_delta[:, :, None])
    grad_bias = jnp.sum(grad_scores, axis=1)
    grad_keys = jnp.einsum("hqs,hqd->hsd", grad_scores, queries, precision=HIGHEST) * score_scale
    return (grad_keys, grad_values, grad_bias)


def per_device(queries, compact_keys, compact_values, slot_bias, targets, positions, assignment):
    page_number = assignment[lax.axis_index("page")]
    local_heads = compact_keys.shape[0]
    slot_total = local_heads * lax.axis_size("head") * compact_keys.shape[1] * lax.axis_size("page")
    entry_count = slot_total * compact_keys.shape[2]
    query_count = lax.axis_size("query")
    heads_kept = max(local_heads // query_count, 1)
    query_parts = max(query_count // local_heads, 1)
    part_rows = queries.shape[1] // query_parts

    def split_items(array):
        width = array.shape[2]
        array = array.reshape(local_heads // heads_kept, heads_kept, query_parts, part_rows, width)
        array = jnp.transpose(array, (0, 2, 1, 3, 4))
        return array.reshape(query_count, heads_kept, part_rows, width)

    def join_items(array):
        width = array.shape[3]
        array = jnp.transpose(array, (1, 0, 2, 3))
        return array.reshape(heads_kept, query_count * part_rows, width)

    position_column = positions.astype(jnp.float32)[:, :, None]
    got_queries, got_targets, got_positions = (
        lax.all_to_all(split_items(queries), "query", split_axis=0, concat_axis=0, tiled=True),
        lax.all_to_all(split_items(targets), "query", split_axis=0, concat_axis=0, tiled=True),
        lax.all_to_all(
            split_items(position_column), "query", split_axis=0, concat_axis=0, tiled=True
        ),
    )
    group_queries = join_items(got_queries)
    group_targets = join_items(got_targets)
    group_positions = join_items(got_positions)[:, :, 0]
    visible = (page_number.astype(jnp.float32) <= jnp.floor(group_positions / PAGE_LEN))[:, :, None]
    query_index = lax.axis_index("query")
    first_head = query_index // query_parts * heads_kept
    key_state = lax.dynamic_slice_in_dim(compact_keys, first_head, heads_kept, 0)
    value_state = lax.dynamic_slice_in_dim(compact_values, first_head, heads_kept, 0)
    bias_state = lax.dynamic_slice_in_dim(slot_bias, first_head, heads_kept, 0)
    counted = (query_index % query_parts == 0).astype(jnp.float32)
    for repeat in range(STEPS):
        grads = local_gradients(
            group_queries, group_targets, visible, key_state, value_state, bias_state
        )
        for bit in range(query_parts.bit_length() - 1):
            partner = from_partner((grads[0], grads[1], grads[2]), "query", bit)
            grads = (grads[0] + partner[0], grads[1] + partner[1], grads[2] + partner[2])
        totals = lax.psum(
            squared_sums(grads[0], grads[1], grads[2]) * counted, ("page", "query", "head")
        )
        key_state, value_state, bias_state = apply_update(
            (key_state, value_state, bias_state), grads, totals, entry_count, slot_total
        )
    all_keys, all_values, all_bias = (
        lax.all_gather(key_state, "query", axis=0, tiled=True),
        lax.all_gather(value_state, "query", axis=0, tiled=True),
        lax.all_gather(bias_state, "query", axis=0, tiled=True),
    )
    slot_rows = compact_keys.shape[1]
    head_width = compact_keys.shape[2]
    all_keys = all_keys.reshape(
        local_heads // heads_kept, query_parts, heads_kept, slot_rows, head_width
    )[:, 0]
    all_values = all_values.reshape(
        local_heads // heads_kept, query_parts, heads_kept, slot_rows, head_width
    )[:, 0]
    all_bias = all_bias.reshape(local_heads // heads_kept, query_parts, heads_kept, slot_rows)[:, 0]
    return (
        all_keys.reshape(local_heads, slot_rows, head_width),
        all_values.reshape(local_heads, slot_rows, head_width),
        all_bias.reshape(local_heads, slot_rows),
    )


def solution(mesh):
    placed = (
        P("head", "query", None),
        P("head", "page", None),
        P("head", "page", None),
        P("head", "page"),
        P("head", "query", None),
        P("head", "query"),
        P(),
    )

    def program(*args):
        plan = direct_per_device if direct_plan_fits(mesh, args[0], args[1]) else per_device
        return jax.shard_map(
            plan,
            mesh=mesh,
            in_specs=placed,
            out_specs=(P("head", "page", None), P("head", "page", None), P("head", "page")),
            check_vma=False,
        )(*args)

    return program
```

```python
import itertools
import math

import jax
import jax.numpy as jnp
from jax import lax
from jax.experimental import pallas as pl
from jax.experimental.pallas import tpu as pltpu
from jax.sharding import PartitionSpec as P

STEPS = 2
PAGE_LEN = 32768


MASKED = -1e30
EPSILON = 1e-06
RATE_KEYS = 0.05
RATE_VALUES = 0.05
RATE_BIAS = 0.2
HIGHEST = lax.Precision.HIGHEST
TAIL = 8
CORES = 2


def exchange(value, **masks):
    axes = tuple(masks)
    sizes = [lax.axis_size(axis) for axis in axes]

    def flat(place):
        index = 0
        for size, at in zip(sizes, place):
            index = index * size + at
        return index

    pairs = [
        (flat(place), flat([at ^ mask for at, mask in zip(place, masks.values())]))
        for place in itertools.product(*map(range, sizes))
    ]
    return lax.ppermute(value, axes, pairs)


def halves(value):
    high = value.astype(jnp.bfloat16)
    return high, (value - high.astype(jnp.float32)).astype(jnp.bfloat16)


def one_pass(left, right, left_dim, right_dim):
    return lax.dot_general(
        left,
        right,
        (((left_dim,), (right_dim,)), ((), ())),
        preferred_element_type=jnp.float32,
    )


def dot_deep(left, right, left_dim, right_dim):
    left = jnp.concatenate([left[0], left[1], left[0]], axis=left_dim)
    right = jnp.concatenate([right[0], right[0], right[1]], axis=right_dim)
    return one_pass(left, right, left_dim, right_dim)


def dot_narrow(left, right, left_dim, right_dim):
    both = one_pass(
        left[0], jnp.concatenate(right, axis=1 - right_dim), left_dim, right_dim
    )
    count = both.shape[1] // 2
    cross = both[:, count:] + one_pass(left[1], right[0], left_dim, right_dim)
    return both[:, :count] + cross


def dot_low(left, right, left_dim, right_dim):
    both = one_pass(jnp.concatenate(left, axis=1 - left_dim), right[0], left_dim, right_dim)
    count = both.shape[0] // 2
    cross = both[count:, :] + one_pass(left[0], right[1], left_dim, right_dim)
    return both[:count, :] + cross


def call(body, out_shapes, name, cost, operands, scratch=(), after=(), space=pltpu.VMEM, vmem=32):
    spaces = [space] * len(operands) + [pl.ANY] * len(after)
    count = len(operands)

    def without_after(*refs):
        body(*refs[:count], *refs[count + len(after) :])

    return pl.pallas_call(
        without_after,
        out_shape=[jax.ShapeDtypeStruct(shape, jnp.float32) for shape in out_shapes],
        in_specs=[pl.BlockSpec(memory_space=space) for space in spaces],
        out_specs=[pl.BlockSpec(memory_space=pltpu.VMEM) for _ in out_shapes],
        scratch_shapes=scratch,
        compiler_params=pltpu.CompilerParams(vmem_limit_bytes=int(vmem * 2**20)),
        cost_estimate=pl.CostEstimate(flops=cost, bytes_accessed=2**20, transcendentals=0),
        name=name,
    )(*operands, *after)


def row_as_tail(row, width):
    rows = [row[:, at : at + width] for at in range(0, row.shape[1], width)]
    rows.append(jnp.zeros((TAIL - len(rows), width), row.dtype))
    return jnp.concatenate(rows, axis=0)


def tail_as_row(ref, start, count):
    return jnp.concatenate([ref[start + at : start + at + 1, :] for at in range(count)], axis=1)


def row_as_column(row, width):
    parts = []
    for at in range(0, row.shape[1], width):
        parts.append(jnp.broadcast_to(row[:, at : at + width], (width, width)).T)
    return jnp.concatenate(parts, axis=0)


def column_sums(value, width):
    groups = [value[:, at : at + width] for at in range(0, value.shape[1], width)]
    partial = sum(groups[1:], groups[0])
    blocks = [
        jnp.sum(partial[at : at + width, :].T, axis=0, keepdims=True)
        for at in range(0, value.shape[0], width)
    ]
    return jnp.concatenate(blocks, axis=1)


def direct_plan_fits(mesh, queries, compact_keys):
    sizes = [mesh.shape[axis] for axis in ("page", "query", "head")]
    pages, query_devices, head_devices = sizes
    local_heads = queries.shape[0] // head_devices
    part_rows = queries.shape[1] // query_devices
    slot_rows = compact_keys.shape[1] // pages
    width = queries.shape[2]
    if any(size & (size - 1) for size in sizes) or pages < CORES or width % 128:
        return False
    if local_heads != CORES * query_devices:
        return False
    ranks = pages // CORES
    if ranks < 4 or query_devices != 2:
        return False
    chunk = part_rows * query_devices // ranks
    return (
        part_rows * query_devices % ranks == 0
        and chunk % 128 == 0
        and part_rows % (8 * ranks) == 0
        and (part_rows // ranks % 128 == 0 or 1024 % (part_rows // ranks * 8) == 0)
        and slot_rows % width == 0
        and part_rows % width == 0
        and max(slot_rows, part_rows) < TAIL * width
    )


def direct_per_device(
    queries, compact_keys, compact_values, slot_bias, targets, positions, assignment
):
    local_heads, part_rows, width = queries.shape
    slot_rows = compact_keys.shape[1]
    query_devices = lax.axis_size("query")
    head_devices = lax.axis_size("head")
    ranks = lax.axis_size("page") // CORES
    query_rows = part_rows * query_devices
    chunk, piece = query_rows // ranks, part_rows // ranks
    slot_total = local_heads * head_devices * slot_rows * lax.axis_size("page")
    entry_total = slot_total * width
    score_scale = 1.0 / math.sqrt(width)
    slots = CORES * slot_rows
    devices = ranks * CORES * query_devices * head_devices
    pos_rows = part_rows // width
    bias_rows = slot_rows // width
    packed_rows = 2 * slot_rows + TAIL
    packed_shapes = [(packed_rows, width)] * 2
    matmul_cost = 3 * 2 * slots * query_rows * width

    def places():
        page = lax.axis_index("page")
        return page // CORES, page % CORES, lax.axis_index("query")

    def to_device(value, **masks):
        masks = {axis: mask for axis, mask in masks.items() if mask}
        return exchange(value, **masks) if masks else value

    def target_rows(head, rank, targets, out):
        return (targets.at[head, pl.ds(pl.multiple_of(rank * piece, piece), piece)], out)

    def pack_state(head, keys, values, out):
        return [
            (keys.at[head], out.at[pl.ds(0, slot_rows)]),
            (values.at[head], out.at[pl.ds(slot_rows, slot_rows)]),
        ]

    def start_all(copies, sems, first=0):
        copies = [
            pltpu.make_async_copy(source, target, sems.at[first + at])
            for at, (source, target) in enumerate(copies)
        ]
        for copy in copies:
            copy.start()
        return copies

    def position_tail(head, positions_ref):
        return row_as_tail(positions_ref[pl.ds(head, 1), :].astype(jnp.float32), width)

    def state_tail(head, page, bias_ref, assignment_ref):
        page_start = (assignment_ref[page] * PAGE_LEN).astype(jnp.float32)
        tail = row_as_tail(bias_ref[pl.ds(head, 1), :], width)
        return jnp.concatenate(
            [tail[: TAIL - 1], jnp.full((1, width), page_start, jnp.float32)], axis=0
        )

    def send_body(queries, keys, values, state_out, *refs):
        query_outs, (sems,) = refs[: query_devices - 1], refs[query_devices - 1 :]
        _, core, me = places()
        copies = [
            (queries.at[CORES * (me ^ turn) + core], out) for turn, out in enumerate(query_outs, 1)
        ]
        copies += pack_state(CORES * me + (core ^ 1), keys, values, state_out)
        for copy in start_all(copies, sems):
            copy.wait()

    def own_body(
        queries, keys, values, biases, targets, positions, assignment, state_out, query_out,
        mate_tail_out, *refs
    ):
        rest_outs, refs = refs[: query_devices - 1], refs[query_devices - 1 :]
        bias_ref, positions_ref, assignment_ref, sems = refs
        rank, core, me = places()
        head, page = CORES * me + core, CORES * rank + core
        small = start_all(
            [(assignment, assignment_ref), (positions, positions_ref), (biases, bias_ref)], sems
        )
        copies = pack_state(head, keys, values, state_out)
        copies.append((queries.at[head], query_out.at[pl.ds(0, part_rows)]))
        copies.append(target_rows(head, rank, targets, query_out.at[pl.ds(part_rows, piece)]))
        for turn, out in enumerate(rest_outs, 1):
            other = CORES * (me ^ turn) + core
            copies.append(target_rows(other, rank, targets, out.at[pl.ds(0, piece)]))
        copies = start_all(copies, sems, 3)
        for copy in small:
            copy.wait()
        state_out[2 * slot_rows :, :] = state_tail(head, page, bias_ref, assignment_ref)
        mate_tail_out[...] = state_tail(head ^ 1, page, bias_ref, assignment_ref)
        query_out[part_rows + piece :, :] = position_tail(head, positions_ref)
        for turn, out in enumerate(rest_outs, 1):
            other = CORES * (me ^ turn) + core
            out[piece:, :] = position_tail(other, positions_ref)
        for copy in copies:
            copy.wait()

    state_shape, query_shape = (packed_rows, width), (part_rows + piece + TAIL, width)
    rest_shape = (piece + TAIL, width)
    mate_slots, *sent_queries = call(
        send_body,
        [(2 * slot_rows, width)] + [(part_rows, width)] * (query_devices - 1),
        "pack",
        2**20,
        [queries, compact_keys, compact_values],
        [pltpu.SemaphoreType.DMA((query_devices + 1,))],
        after=[slot_bias, targets, positions, assignment],
        space=pl.ANY,
        vmem=60,
    )
    own_state, own_queries, mate_tail, *sent_rests = call(
        own_body,
        [state_shape, query_shape, (TAIL, width)] + [rest_shape] * (query_devices - 1),
        "own",
        2**24,
        [queries, compact_keys, compact_values, slot_bias, targets, positions, assignment],
        [
            pltpu.VMEM(slot_bias.shape, jnp.float32),
            pltpu.VMEM(positions.shape, jnp.int32),
            pltpu.SMEM(assignment.shape, jnp.int32),
            pltpu.SemaphoreType.DMA((6 + query_devices,)),
        ],
        space=pl.ANY,
    )
    arrived_queries = [
        exchange(sent_queries[turn - 1], query=turn) for turn in range(1, query_devices)
    ]
    arrived_rests = [
        exchange(sent_rests[turn - 1], query=turn) for turn in range(1, query_devices)
    ]
    mate_parts = [exchange(mate_slots, page=1), exchange(mate_tail, page=1)]

    def in_columns(parts, axis):
        return jnp.concatenate(
            [
                lax.slice_in_dim(part, at * piece, (at + 1) * piece, axis=axis)
                for at in range(ranks)
                for part in parts
            ],
            axis=axis,
        )

    def read_queries(query_refs):
        return halves(in_columns([ref[:part_rows, :] for ref in query_refs], 0))

    def part_of(ref, at):
        return ref.at[pl.ds(at * packed_rows, packed_rows)]

    def parts_of(refs):
        return refs if len(refs) == CORES else [part_of(refs[0], at) for at in range(CORES)]

    def step_sizes(tile_refs):
        row = jnp.sum(tile_refs[0][...], axis=0)
        return (
            RATE_KEYS / jnp.sqrt(row[:, 0:1] / entry_total + EPSILON),
            RATE_VALUES / jnp.sqrt(row[:, 1:2] / entry_total + EPSILON),
            RATE_BIAS / jnp.sqrt(row[:, 2:3] / slot_total + EPSILON),
        )

    def read_pack(ref):
        return ref[:slot_rows, :], ref[slot_rows : 2 * slot_rows, :], ref[2 * slot_rows :, :]

    def store_pack(ref, values):
        ref[:slot_rows, :] = values[0]
        ref[slot_rows : 2 * slot_rows, :] = values[1]
        ref[2 * slot_rows :, :] = values[2]

    def updated(state, grads, sizes):
        return [value - size * grad for value, grad, size in zip(state, grads, sizes)]

    def page_scores(ref, queries, positions):
        scores = dot_deep(halves(ref[:slot_rows, :]), queries, 1, 1) * score_scale
        bias = row_as_column(tail_as_row(ref, 2 * slot_rows, bias_rows), width)
        scores = scores + jnp.concatenate([bias] * (positions.shape[1] // width), axis=1)
        page_start = ref[packed_rows - 1 : packed_rows, 0:1]
        visible = jnp.broadcast_to(positions >= page_start, scores.shape)
        return jnp.where(visible, scores, MASKED), visible

    def read_positions(query_refs):
        return in_columns(
            [tail_as_row(ref, part_rows + piece, pos_rows) for ref in query_refs], 1
        )

    def forward(state_refs, query_refs, chunk_outs, weights_out, max_out, chunks):
        rank, _, _ = places()
        all_queries, positions = read_queries(query_refs), read_positions(query_refs)
        all_scores, all_visible = [], []
        for at, ref in enumerate(state_refs):
            scores, visible = page_scores(ref, all_queries, positions)
            all_scores.append(scores)
            all_visible.append(visible)
        row_max = jnp.max(all_scores[0], axis=0, keepdims=True)
        for scores in all_scores[1:]:
            row_max = jnp.maximum(row_max, jnp.max(scores, axis=0, keepdims=True))
        row_total = jnp.zeros_like(row_max)
        row_sum = jnp.zeros((width, query_rows), jnp.float32)
        for at, ref in enumerate(state_refs):
            weights = jnp.where(all_visible[at], jnp.exp(all_scores[at] - row_max), 0.0)
            weights_out[at * slot_rows : (at + 1) * slot_rows, :] = weights
            row_total = row_total + jnp.sum(weights, axis=0, keepdims=True)
            values = halves(ref[slot_rows : 2 * slot_rows, :])
            row_sum = row_sum + dot_low(values, halves(weights), 0, 0)
        max_out[...] = jnp.broadcast_to(row_max, (TAIL, query_rows))
        tail = jnp.concatenate(
            [row_max, row_total, jnp.zeros((TAIL - 2, query_rows), jnp.float32)], axis=0
        )
        for at in range(ranks):
            columns = slice(at * chunk, (at + 1) * chunk)
            chunks[at, :width, :] = row_sum[:, columns]
            chunks[at, width:, :] = tail[:, columns]
        for turn in range(ranks):
            chunk_outs[turn][...] = chunks[rank ^ turn]

    chunk_shape = (width + TAIL, chunk)
    forward_shapes = [chunk_shape] * ranks + [(slots, query_rows), (TAIL, query_rows)]
    chunk_scratch = [pltpu.VMEM((ranks,) + chunk_shape, jnp.float32)]

    fold = max(1, 128 // piece)
    folded, columns = width // fold, fold * piece
    piece_shape = (folded + TAIL, columns)
    piece_scratch = [pltpu.VMEM((ranks,) + piece_shape, jnp.float32)]

    def fold_rows(value):
        groups = [value[at * folded : (at + 1) * folded, :] for at in range(fold)]
        return jnp.concatenate(groups, axis=1)

    def unfold_rows(value):
        groups = [value[:, at * piece : (at + 1) * piece] for at in range(fold)]
        return jnp.concatenate(groups, axis=0)

    def rows_tail(rows):
        empty = jnp.zeros((TAIL - len(rows), columns), jnp.float32)
        return jnp.concatenate(rows + [empty], axis=0)

    def part_body(part):
        def body(own_ref, *refs):
            if part:
                (mate_ref, query_rows_ref, rest_ref), refs = refs[:3], refs[3:]
            else:
                (slots_ref, tail_ref, query_ref), refs = refs[:3], refs[3:]
            before_refs, refs = refs[: len(before)], refs[len(before) :]
            piece_outs, (weights_out, max_out, joined_out, pieces) = refs[:ranks], refs[ranks:]
            if part:
                query_ref = joined_out
                query_ref[:part_rows, :] = query_rows_ref[...]
                query_ref[part_rows:, :] = rest_ref[...]
            else:
                mate_ref = joined_out
                mate_ref[: 2 * slot_rows, :] = slots_ref[...]
                mate_ref[2 * slot_rows :, :] = tail_ref[...]
            part_forward(
                [own_ref, mate_ref], query_ref, before_refs, piece_outs, weights_out, max_out, pieces
            )

        return body

    def part_forward(
        state_refs, query_ref, before_refs, piece_outs, weights_out, max_out, pieces
    ):
        rank, _, _ = places()
        queries = halves(query_ref[:part_rows, :])
        position_row = tail_as_row(query_ref, part_rows + piece, pos_rows)
        all_scores, all_visible = [], []
        for ref in state_refs:
            scores, visible = page_scores(ref, queries, position_row)
            all_scores.append(scores)
            all_visible.append(visible)
        row_max = jnp.max(all_scores[0], axis=0, keepdims=True)
        for scores in all_scores[1:]:
            row_max = jnp.maximum(row_max, jnp.max(scores, axis=0, keepdims=True))
        row_total = jnp.zeros_like(row_max)
        row_sum = jnp.zeros((width, part_rows), jnp.float32)
        for at, ref in enumerate(state_refs):
            weights = jnp.where(all_visible[at], jnp.exp(all_scores[at] - row_max), 0.0)
            weights_out[at * slot_rows : (at + 1) * slot_rows, :] = weights
            row_total = row_total + jnp.sum(weights, axis=0, keepdims=True)
            values = halves(ref[slot_rows : 2 * slot_rows, :])
            row_sum = row_sum + dot_low(values, halves(weights), 0, 0)
        max_out[...] = jnp.broadcast_to(row_max, (TAIL, part_rows))
        for at in range(ranks):
            own = slice(at * piece, (at + 1) * piece)
            pieces[at, :folded, :] = fold_rows(row_sum[:, own])
            pieces[at, folded:, :] = rows_tail(
                [jnp.concatenate([row[:, own]] * fold, axis=1) for row in (row_max, row_total)]
            )
        for turn, out in enumerate(piece_outs):
            out[out.shape[0] - piece_shape[0] :, :] = pieces[rank ^ turn]
        for at, ref in enumerate(before_refs):
            out, first = piece_outs[1 + at % (ranks - 2)], at // (ranks - 2) * piece_shape[0]
            out[first : first + piece_shape[0], :] = ref[...]


    def next_body(*refs):
        state_refs, refs = refs[:2], refs[2:]
        query_refs, refs = refs[:query_devices], refs[query_devices:]
        grad_refs, refs = refs[:2], refs[2:]
        tile_refs, refs = refs[: len(tiles)], refs[len(tiles) :]
        refs[0][CORES * packed_rows :, :] = query_refs[0][...]
        state_outs, refs = parts_of(refs[:1]), refs[1:]
        chunk_outs, refs = refs[:ranks], refs[ranks:]
        sizes = step_sizes(tile_refs)
        for at in range(2):
            state = read_pack(state_refs[at])
            store_pack(state_outs[at], updated(state, read_pack(grad_refs[at]), sizes))
        forward(state_outs, query_refs, chunk_outs, *refs)

    def merged_chunk(query_refs, sums, maxima, totals, out):
        targets = jnp.concatenate(
            [ref[part_rows : part_rows + piece, :] for ref in query_refs], axis=0
        )
        row_max = maxima[0]
        for other in maxima[1:]:
            row_max = jnp.maximum(row_max, other)
        row_total = jnp.zeros_like(row_max)
        row_sum = jnp.zeros((width, chunk), jnp.float32)
        for part_sum, part_max, part_total in zip(sums, maxima, totals):
            factor = jnp.exp(part_max - row_max)
            row_total = row_total + part_total * factor
            row_sum = row_sum + part_sum * factor
        output = row_sum / row_total
        residual = output - targets.T
        row_delta = jnp.sum(residual * output, axis=0, keepdims=True)
        out[:width, :] = residual
        out[width:, :] = jnp.concatenate(
            [row_max, row_total, row_delta, jnp.zeros((TAIL - 3, chunk), jnp.float32)], axis=0
        )

    def first_merge_body(*refs):
        query_refs, (*piece_refs, merged_out) = refs[:query_devices], refs[query_devices:]
        single, joint = piece_refs[: 2 * query_devices], piece_refs[2 * query_devices :]
        groups = [single[0::2], single[1::2]]
        for ref in joint:
            groups.append(
                [
                    ref.at[pl.ds(part * piece_shape[0], piece_shape[0])]
                    for part in range(query_devices)
                ]
            )

        def joined(read):
            return [jnp.concatenate([read(ref) for ref in group], axis=1) for group in groups]

        merged_chunk(
            query_refs,
            joined(lambda ref: unfold_rows(ref[:folded, :])),
            joined(lambda ref: ref[folded : folded + 1, :piece]),
            joined(lambda ref: ref[folded + 1 : folded + 2, :piece]),
            merged_out,
        )

    def merge_body(*refs):
        query_refs, (*chunk_refs, merged_out) = refs[:query_devices], refs[query_devices:]
        merged_chunk(
            query_refs,
            [ref[:width, :] for ref in chunk_refs],
            [ref[width : width + 1, :] for ref in chunk_refs],
            [ref[width + 1 : width + 2, :] for ref in chunk_refs],
            merged_out,
        )

    def page_gradients(weights, factor, state_ref, all_queries, residual, row_delta):
        attention = weights * factor
        grad_values = dot_narrow(halves(attention), residual, 1, 1)
        grad_probs = dot_deep(halves(state_ref[slot_rows : 2 * slot_rows, :]), residual, 1, 0)
        grad_scores = attention * (grad_probs - row_delta)
        grad_keys = dot_narrow(halves(grad_scores), all_queries, 1, 0) * score_scale
        grad_bias = column_sums(grad_scores, width)
        return grad_keys, grad_values, row_as_tail(grad_bias, width)

    def split_merged(joined):
        row_max, row_total, row_delta = (
            joined[width + at : width + at + 1, :] for at in range(3)
        )
        return halves(joined[:width, :]), row_max, row_total, row_delta

    def read_chunks(merged_refs, chunks):
        rank, _, _ = places()
        for turn, ref in enumerate(merged_refs):
            chunks[rank ^ turn] = ref[...]
        return [chunks[at] for at in range(ranks)]

    def join_body(*refs):
        *merged_refs, joined_out, chunks = refs
        joined_out[...] = jnp.concatenate(read_chunks(merged_refs, chunks), axis=1)

    def backward_body(*refs):
        weights_refs, refs = refs[: len(weights)], refs[len(weights) :]
        max_refs, refs = refs[: len(weights)], refs[len(weights) :]
        state_refs, refs = parts_of(refs[: len(states)]), refs[len(states) :]
        query_refs, refs = refs[:query_devices], refs[query_devices:]
        merged_refs, refs = refs[: len(all_merged)], refs[len(all_merged) :]
        grad_outs, (squares_out, *scratch) = refs[:2], refs[2:]
        if len(states) < CORES:
            joined = merged_refs[0][...]
            all_queries = read_queries(query_refs)
        else:
            chunks = read_chunks(merged_refs, *scratch)
            joined = jnp.concatenate(
                [
                    value[:, part * piece : (part + 1) * piece]
                    for part in range(query_devices)
                    for value in chunks
                ],
                axis=1,
            )
            all_queries = halves(
                jnp.concatenate([ref[:part_rows, :] for ref in query_refs], axis=0)
            )
        residual, row_max, row_total, row_delta = split_merged(joined)
        maxima = jnp.concatenate([ref[0:1, :] for ref in max_refs], axis=1)
        factor = jnp.exp(maxima - row_max) / row_total
        squares = [jnp.zeros((1, width), jnp.float32)] * 3
        for at, (ref, out) in enumerate(zip(state_refs, grad_outs)):
            rows = slice(at * slot_rows, (at + 1) * slot_rows)
            page_weights = jnp.concatenate([part[rows, :] for part in weights_refs], axis=1)
            grads = page_gradients(page_weights, factor, ref, all_queries, residual, row_delta)
            store_pack(out, grads)
            for which, grad in enumerate(grads):
                squares[which] = squares[which] + jnp.sum(grad * grad, axis=0, keepdims=True)
        lanes = lax.broadcasted_iota(jnp.int32, (1, width), 1)
        row = jnp.zeros((1, width), jnp.float32)
        for which, square in enumerate(squares):
            row = jnp.where(lanes == which, jnp.sum(square, axis=1, keepdims=True), row)
        for at in range(devices):
            squares_out[at] = row

    def page_body(at):
        def body(tile_ref, grad_ref, own_state_ref, *refs):
            state_refs, refs = refs[: query_devices - 1], refs[query_devices - 1 :]
            joined_refs, (*pack_refs, out) = refs[: query_devices - 1], refs[query_devices - 1 :]
            sizes = step_sizes([tile_ref])
            state = read_pack(part_of(own_state_ref, at))
            store_pack(part_of(out, 0), updated(state, read_pack(grad_ref), sizes))
            for turn, (state_ref, joined_ref) in enumerate(zip(state_refs, joined_refs), 1):
                query_ref = state_ref.at[pl.ds(CORES * packed_rows, query_shape[0])]
                rows_ref, rest_ref = pack_refs[2 * turn - 2 : 2 * turn]
                query_rows = [query_ref[:part_rows, :], rows_ref[...]]
                positions = [
                    tail_as_row(query_ref, part_rows + piece, pos_rows),
                    tail_as_row(rest_ref, piece, pos_rows),
                ]
                residual, row_max, row_total, row_delta = split_merged(joined_ref[...])
                all_queries = halves(in_columns(query_rows, 0))
                ref = part_of(state_ref, at)
                scores, visible = page_scores(ref, all_queries, in_columns(positions, 1))
                weights = jnp.where(visible, jnp.exp(scores - row_max), 0.0)
                grads = page_gradients(
                    weights, 1.0 / row_total, ref, all_queries, residual, row_delta
                )
                store_pack(part_of(out, turn), updated(read_pack(ref), grads, sizes))

        return body

    for repeat in range(STEPS):
        last = repeat == STEPS - 1
        if repeat == 0:
            sums, weights, maxima, nearer, far = [], [], [], [], []
            for part in range(query_devices):
                before = nearer if part == query_devices - 1 else []
                joined_rows = 1 + len(before) // (ranks - 2)
                near_shape = (joined_rows * piece_shape[0], columns)
                if part:
                    inputs = [states[1], arrived_queries[part - 1], arrived_rests[part - 1]]
                else:
                    inputs = mate_parts + [own_queries]
                *pieces, part_weights, part_max, joined = call(
                    part_body(part),
                    [piece_shape]
                    + [near_shape] * (ranks - 2)
                    + [piece_shape, (slots, part_rows), (TAIL, part_rows)]
                    + [query_shape if part else state_shape],
                    "forward",
                    2 * matmul_cost // query_devices,
                    [own_state] + inputs + before,
                    piece_scratch,
                    after=maxima[-1:] + far,
                )
                if part:
                    query_parts.append(joined)
                else:
                    states, query_parts = [own_state, joined], [own_queries]
                far = [exchange(pieces[-1], page=CORES * (ranks - 1))]
                nearer = nearer + pieces[1:-1]
                sums += [pieces[0]] + far
                weights.append(part_weights)
                maxima.append(part_max)
            sums += [
                exchange(pieces[turn], page=CORES * turn) for turn in reversed(range(1, ranks - 1))
            ]
        else:
            new_state, *chunk_parts, part_weights, part_max = call(
                next_body,
                [(CORES * packed_rows + query_shape[0], width)] + forward_shapes,
                "update_forward",
                2 * matmul_cost,
                states + query_parts + grads + tiles,
                chunk_scratch,
            )
            states, weights, maxima = [new_state], [part_weights], [part_max]
            arrived = {
                turn: exchange(chunk_parts[turn], page=CORES * turn)
                for turn in reversed(range(1, ranks))
            }
            sums = chunk_parts[:1] + list(arrived.values())
            new_states = states + [
                exchange(states[0], query=turn) for turn in range(1, query_devices)
            ]
        (merged,) = call(
            merge_body if repeat else first_merge_body,
            [chunk_shape],
            "merge",
            2**20,
            query_parts + sums,
        )
        all_merged = [merged] + [
            exchange(merged, page=CORES * turn) for turn in range(1, ranks)
        ]
        if last:
            all_merged = call(
                join_body, [(width + TAIL, query_rows)], "join", 2**20, all_merged, chunk_scratch
            )
            all_joined = [
                to_device(all_merged[0], query=turn) for turn in range(query_devices)
            ]
        own_grad, mate_grad, squares = call(
            backward_body,
            packed_shapes + [(devices, 1, width)],
            "backward",
            3 * matmul_cost,
            weights + maxima + states + query_parts + list(all_merged),
            scratch=() if last else chunk_scratch,
        )
        grads = [own_grad, mate_grad]
        tiles = [
            lax.all_to_all(
                squares, ("page", "query", "head"), split_axis=0, concat_axis=0, tiled=True
            )
        ]

    other_packs = [
        part for turn in range(1, query_devices) for part in (sent_queries[turn - 1], sent_rests[turn - 1])
    ]
    operands = new_states + all_joined[1:] + other_packs
    pages = []
    for at, grad in ((1, mate_grad), (0, own_grad)):
        pages += call(
            page_body(at),
            [(query_devices * packed_rows, width)],
            "page_update",
            3 * matmul_cost // 2,
            tiles + [grad] + operands,
            after=pages,
        )
    pages = [pages[1], exchange(pages[0], page=1)]

    def last_body(*refs):
        page_refs, (keys_out, values_out, bias_out) = refs[:CORES], refs[CORES:]
        _, core, me = places()
        for turn, flip in itertools.product(range(query_devices), range(CORES)):
            keys, values, bias = read_pack(part_of(page_refs[flip], turn))
            head = CORES * (me ^ turn) + (core ^ flip)
            keys_out[head] = keys
            values_out[head] = values
            bias_row = jnp.concatenate([bias[row : row + 1] for row in range(bias_rows)], axis=1)
            bias_out[pl.ds(head, 1), :] = bias_row

    return tuple(
        call(
            last_body,
            [compact_keys.shape, compact_values.shape, slot_bias.shape],
            "unpack",
            2**20,
            pages,
        )
    )


def from_partner(value, axis, stride):
    mask = 2**stride
    pairs = [(source, source ^ mask) for source in range(lax.axis_size(axis))]
    return lax.ppermute(value, axis, pairs)


def squared_sums(grad_keys, grad_values, grad_bias):
    return jnp.stack(
        [
            jnp.sum(grad_keys * grad_keys),
            jnp.sum(grad_values * grad_values),
            jnp.sum(grad_bias * grad_bias),
        ]
    )


def apply_update(states, grads, totals, entry_count, slot_total):
    key_state, value_state, bias_state = states
    grad_keys, grad_values, grad_bias = grads
    rms_keys = jnp.sqrt(totals[0] / entry_count + EPSILON)
    rms_values = jnp.sqrt(totals[1] / entry_count + EPSILON)
    rms_bias = jnp.sqrt(totals[2] / slot_total + EPSILON)
    return (
        key_state - RATE_KEYS * grad_keys / rms_keys,
        value_state - RATE_VALUES * grad_values / rms_values,
        bias_state - RATE_BIAS * grad_bias / rms_bias,
    )


def local_gradients(queries, targets, visible, compact_keys, compact_values, slot_bias):
    score_scale = 1.0 / math.sqrt(queries.shape[2])
    scores = jnp.einsum("hqd,hsd->hqs", queries, compact_keys, precision=HIGHEST) * score_scale
    scores = jnp.where(visible, scores + slot_bias[:, None, :], MASKED)
    local_max = jnp.max(scores, axis=2)
    row_max = lax.pmax(local_max, "page")
    weights = jnp.where(visible, jnp.exp(scores - row_max[:, :, None]), 0.0)
    local_sum = jnp.einsum("hqs,hsd->hqd", weights, compact_values, precision=HIGHEST)
    row_total, row_sum = lax.psum((jnp.sum(weights, axis=2), local_sum), "page")
    attention = weights / row_total[:, :, None]
    output = row_sum / row_total[:, :, None]
    residual = output - targets
    grad_values = jnp.einsum("hqs,hqd->hsd", attention, residual, precision=HIGHEST)
    row_delta = jnp.sum(residual * output, axis=2)
    grad_probs = jnp.einsum("hqd,hsd->hqs", residual, compact_values, precision=HIGHEST)
    grad_scores = attention * (grad_probs - row_delta[:, :, None])
    grad_bias = jnp.sum(grad_scores, axis=1)
    grad_keys = jnp.einsum("hqs,hqd->hsd", grad_scores, queries, precision=HIGHEST) * score_scale
    return (grad_keys, grad_values, grad_bias)


def per_device(queries, compact_keys, compact_values, slot_bias, targets, positions, assignment):
    page_number = assignment[lax.axis_index("page")]
    local_heads = compact_keys.shape[0]
    slot_total = local_heads * lax.axis_size("head") * compact_keys.shape[1] * lax.axis_size("page")
    entry_count = slot_total * compact_keys.shape[2]
    query_count = lax.axis_size("query")
    heads_kept = max(local_heads // query_count, 1)
    query_parts = max(query_count // local_heads, 1)
    part_rows = queries.shape[1] // query_parts

    def split_items(array):
        width = array.shape[2]
        array = array.reshape(local_heads // heads_kept, heads_kept, query_parts, part_rows, width)
        array = jnp.transpose(array, (0, 2, 1, 3, 4))
        return array.reshape(query_count, heads_kept, part_rows, width)

    def join_items(array):
        width = array.shape[3]
        array = jnp.transpose(array, (1, 0, 2, 3))
        return array.reshape(heads_kept, query_count * part_rows, width)

    position_column = positions.astype(jnp.float32)[:, :, None]
    got_queries, got_targets, got_positions = (
        lax.all_to_all(split_items(queries), "query", split_axis=0, concat_axis=0, tiled=True),
        lax.all_to_all(split_items(targets), "query", split_axis=0, concat_axis=0, tiled=True),
        lax.all_to_all(
            split_items(position_column), "query", split_axis=0, concat_axis=0, tiled=True
        ),
    )
    group_queries = join_items(got_queries)
    group_targets = join_items(got_targets)
    group_positions = join_items(got_positions)[:, :, 0]
    visible = (page_number.astype(jnp.float32) <= jnp.floor(group_positions / PAGE_LEN))[:, :, None]
    query_index = lax.axis_index("query")
    first_head = query_index // query_parts * heads_kept
    key_state = lax.dynamic_slice_in_dim(compact_keys, first_head, heads_kept, 0)
    value_state = lax.dynamic_slice_in_dim(compact_values, first_head, heads_kept, 0)
    bias_state = lax.dynamic_slice_in_dim(slot_bias, first_head, heads_kept, 0)
    counted = (query_index % query_parts == 0).astype(jnp.float32)
    for repeat in range(STEPS):
        grads = local_gradients(
            group_queries, group_targets, visible, key_state, value_state, bias_state
        )
        for bit in range(query_parts.bit_length() - 1):
            partner = from_partner((grads[0], grads[1], grads[2]), "query", bit)
            grads = (grads[0] + partner[0], grads[1] + partner[1], grads[2] + partner[2])
        totals = lax.psum(
            squared_sums(grads[0], grads[1], grads[2]) * counted, ("page", "query", "head")
        )
        key_state, value_state, bias_state = apply_update(
            (key_state, value_state, bias_state), grads, totals, entry_count, slot_total
        )
    all_keys, all_values, all_bias = (
        lax.all_gather(key_state, "query", axis=0, tiled=True),
        lax.all_gather(value_state, "query", axis=0, tiled=True),
        lax.all_gather(bias_state, "query", axis=0, tiled=True),
    )
    slot_rows = compact_keys.shape[1]
    head_width = compact_keys.shape[2]
    all_keys = all_keys.reshape(
        local_heads // heads_kept, query_parts, heads_kept, slot_rows, head_width
    )[:, 0]
    all_values = all_values.reshape(
        local_heads // heads_kept, query_parts, heads_kept, slot_rows, head_width
    )[:, 0]
    all_bias = all_bias.reshape(local_heads // heads_kept, query_parts, heads_kept, slot_rows)[:, 0]
    return (
        all_keys.reshape(local_heads, slot_rows, head_width),
        all_values.reshape(local_heads, slot_rows, head_width),
        all_bias.reshape(local_heads, slot_rows),
    )


def solution(mesh):
    placed = (
        P("head", "query", None),
        P("head", "page", None),
        P("head", "page", None),
        P("head", "page"),
        P("head", "query", None),
        P("head", "query"),
        P(),
    )

    def program(*args):
        plan = direct_per_device if direct_plan_fits(mesh, args[0], args[1]) else per_device
        return jax.shard_map(
            plan,
            mesh=mesh,
            in_specs=placed,
            out_specs=(P("head", "page", None), P("head", "page", None), P("head", "page")),
            check_vma=False,
        )(*args)

    return program
```

```python
import itertools
import math

import jax
import jax.numpy as jnp
from jax import lax
from jax.experimental import pallas as pl
from jax.experimental.pallas import tpu as pltpu
from jax.sharding import PartitionSpec as P

STEPS = 2
PAGE_LEN = 32768


MASKED = -1e30
EPSILON = 1e-06
RATE_KEYS = 0.05
RATE_VALUES = 0.05
RATE_BIAS = 0.2
HIGHEST = lax.Precision.HIGHEST
TAIL = 8
CORES = 2


def exchange(value, **masks):
    axes = tuple(masks)
    sizes = [lax.axis_size(axis) for axis in axes]

    def flat(place):
        index = 0
        for size, at in zip(sizes, place):
            index = index * size + at
        return index

    pairs = [
        (flat(place), flat([at ^ mask for at, mask in zip(place, masks.values())]))
        for place in itertools.product(*map(range, sizes))
    ]
    return lax.ppermute(value, axes, pairs)


def halves(value):
    high = value.astype(jnp.bfloat16)
    return high, (value - high.astype(jnp.float32)).astype(jnp.bfloat16)


def one_pass(left, right, left_dim, right_dim):
    return lax.dot_general(
        left,
        right,
        (((left_dim,), (right_dim,)), ((), ())),
        preferred_element_type=jnp.float32,
    )


def dot_deep(left, right, left_dim, right_dim):
    left = jnp.concatenate([left[0], left[1], left[0]], axis=left_dim)
    right = jnp.concatenate([right[0], right[0], right[1]], axis=right_dim)
    return one_pass(left, right, left_dim, right_dim)


def dot_narrow(left, right, left_dim, right_dim):
    both = one_pass(
        left[0], jnp.concatenate(right, axis=1 - right_dim), left_dim, right_dim
    )
    count = both.shape[1] // 2
    cross = both[:, count:] + one_pass(left[1], right[0], left_dim, right_dim)
    return both[:, :count] + cross


def dot_low(left, right, left_dim, right_dim):
    both = one_pass(jnp.concatenate(left, axis=1 - left_dim), right[0], left_dim, right_dim)
    count = both.shape[0] // 2
    cross = both[count:, :] + one_pass(left[0], right[1], left_dim, right_dim)
    return both[:count, :] + cross


def call(body, out_shapes, name, cost, operands, scratch=(), after=(), space=pltpu.VMEM, vmem=32):
    spaces = [space] * len(operands) + [pl.ANY] * len(after)
    count = len(operands)

    def without_after(*refs):
        body(*refs[:count], *refs[count + len(after) :])

    return pl.pallas_call(
        without_after,
        out_shape=[jax.ShapeDtypeStruct(shape, jnp.float32) for shape in out_shapes],
        in_specs=[pl.BlockSpec(memory_space=space) for space in spaces],
        out_specs=[pl.BlockSpec(memory_space=pltpu.VMEM) for _ in out_shapes],
        scratch_shapes=scratch,
        compiler_params=pltpu.CompilerParams(vmem_limit_bytes=vmem * 2**20),
        cost_estimate=pl.CostEstimate(flops=cost, bytes_accessed=2**20, transcendentals=0),
        name=name,
    )(*operands, *after)


def row_as_tail(row, width):
    rows = [row[:, at : at + width] for at in range(0, row.shape[1], width)]
    rows.append(jnp.zeros((TAIL - len(rows), width), row.dtype))
    return jnp.concatenate(rows, axis=0)


def tail_as_row(ref, start, count):
    return jnp.concatenate([ref[start + at : start + at + 1, :] for at in range(count)], axis=1)


def row_as_column(row, width):
    parts = []
    for at in range(0, row.shape[1], width):
        parts.append(jnp.broadcast_to(row[:, at : at + width], (width, width)).T)
    return jnp.concatenate(parts, axis=0)


def column_sums(value, width):
    groups = [value[:, at : at + width] for at in range(0, value.shape[1], width)]
    partial = sum(groups[1:], groups[0])
    blocks = [
        jnp.sum(partial[at : at + width, :].T, axis=0, keepdims=True)
        for at in range(0, value.shape[0], width)
    ]
    return jnp.concatenate(blocks, axis=1)


def direct_plan_fits(mesh, queries, compact_keys):
    sizes = [mesh.shape[axis] for axis in ("page", "query", "head")]
    pages, query_devices, head_devices = sizes
    local_heads = queries.shape[0] // head_devices
    part_rows = queries.shape[1] // query_devices
    slot_rows = compact_keys.shape[1] // pages
    width = queries.shape[2]
    if any(size & (size - 1) for size in sizes) or pages < CORES or width % 128:
        return False
    if local_heads != CORES * query_devices:
        return False
    ranks = pages // CORES
    chunk = part_rows * query_devices // ranks
    return (
        part_rows * query_devices % ranks == 0
        and chunk % 128 == 0
        and part_rows % (8 * ranks) == 0
        and (part_rows // ranks % 128 == 0 or 1024 % (part_rows // ranks * 8) == 0)
        and slot_rows % width == 0
        and part_rows % width == 0
        and max(slot_rows, part_rows) < TAIL * width
    )


def direct_per_device(
    queries, compact_keys, compact_values, slot_bias, targets, positions, assignment
):
    local_heads, part_rows, width = queries.shape
    slot_rows = compact_keys.shape[1]
    query_devices = lax.axis_size("query")
    head_devices = lax.axis_size("head")
    ranks = lax.axis_size("page") // CORES
    query_rows = part_rows * query_devices
    chunk, piece = query_rows // ranks, part_rows // ranks
    turns = [ranks // 2] + [turn for turn in reversed(range(1, ranks)) if turn != ranks // 2]
    slot_total = local_heads * head_devices * slot_rows * lax.axis_size("page")
    entry_total = slot_total * width
    score_scale = 1.0 / math.sqrt(width)
    slots = CORES * slot_rows
    devices = ranks * CORES * query_devices * head_devices
    pos_rows = part_rows // width
    bias_rows = slot_rows // width
    packed_rows = 2 * slot_rows + TAIL
    packed_shapes = [(packed_rows, width)] * 2
    matmul_cost = 3 * 2 * slots * query_rows * width

    def places():
        page = lax.axis_index("page")
        return page // CORES, page % CORES, lax.axis_index("query")

    def to_device(value, **masks):
        masks = {axis: mask for axis, mask in masks.items() if mask}
        return exchange(value, **masks) if masks else value

    def pack_queries(head, rank, queries, targets, out):
        rows = pl.ds(pl.multiple_of(rank * piece, piece), piece)
        return [
            (queries.at[head], out.at[pl.ds(0, part_rows)]),
            (targets.at[head, rows], out.at[pl.ds(part_rows, piece)]),
        ]

    def pack_state(head, keys, values, out):
        return [
            (keys.at[head], out.at[pl.ds(0, slot_rows)]),
            (values.at[head], out.at[pl.ds(slot_rows, slot_rows)]),
        ]

    def start_all(copies, sems, first=0):
        copies = [
            pltpu.make_async_copy(source, target, sems.at[first + at])
            for at, (source, target) in enumerate(copies)
        ]
        for copy in copies:
            copy.start()
        return copies

    def position_tail(head, positions_ref):
        return row_as_tail(positions_ref[pl.ds(head, 1), :].astype(jnp.float32), width)

    def state_tail(head, page, bias_ref, assignment_ref):
        page_start = (assignment_ref[page] * PAGE_LEN).astype(jnp.float32)
        tail = row_as_tail(bias_ref[pl.ds(head, 1), :], width)
        return jnp.concatenate(
            [tail[: TAIL - 1], jnp.full((1, width), page_start, jnp.float32)], axis=0
        )

    def send_body(
        queries, keys, values, biases, targets, positions, assignment, state_out, *refs
    ):
        query_outs = refs[: query_devices - 1]
        bias_ref, positions_ref, assignment_ref, sems = refs[query_devices - 1 :]
        rank, core, me = places()
        heads = [CORES * (me ^ turn) + core for turn in range(1, query_devices)]
        mate_head = CORES * me + (core ^ 1)
        small = start_all(
            [(assignment, assignment_ref), (positions, positions_ref), (biases, bias_ref)], sems
        )
        copies = pack_state(mate_head, keys, values, state_out)
        for head, out in zip(heads, query_outs):
            copies += pack_queries(head, rank, queries, targets, out)
        copies = start_all(copies, sems, 3)
        for copy in small:
            copy.wait()
        state_out[2 * slot_rows :, :] = state_tail(
            mate_head, CORES * rank + core, bias_ref, assignment_ref
        )
        for head, out in zip(heads, query_outs):
            out[part_rows + piece :, :] = position_tail(head, positions_ref)
        for copy in copies:
            copy.wait()

    def own_body(
        queries, keys, values, biases, targets, positions, assignment, state_out, query_out, *refs
    ):
        bias_ref, positions_ref, assignment_ref, sems = refs
        rank, core, me = places()
        head = CORES * me + core
        small = start_all(
            [(assignment, assignment_ref), (positions, positions_ref), (biases, bias_ref)], sems
        )
        copies = pack_state(head, keys, values, state_out)
        copies += pack_queries(head, rank, queries, targets, query_out)
        copies = start_all(copies, sems, 3)
        for copy in small:
            copy.wait()
        state_out[2 * slot_rows :, :] = state_tail(
            head, CORES * rank + core, bias_ref, assignment_ref
        )
        query_out[part_rows + piece :, :] = position_tail(head, positions_ref)
        for copy in copies:
            copy.wait()

    state_shape, query_shape = (packed_rows, width), (part_rows + piece + TAIL, width)
    small_scratch = [
        pltpu.VMEM(slot_bias.shape, jnp.float32),
        pltpu.VMEM(positions.shape, jnp.int32),
        pltpu.SMEM(assignment.shape, jnp.int32),
    ]
    arguments = [
        queries, compact_keys, compact_values, slot_bias, targets, positions, assignment
    ]
    mate_state, *sent_queries = call(
        send_body,
        [state_shape] + [query_shape] * (query_devices - 1),
        "pack",
        2**20,
        arguments,
        small_scratch + [pltpu.SemaphoreType.DMA((3 + 2 * query_devices,))],
        space=pl.ANY,
        vmem=60,
    )
    own_state, own_queries = call(
        own_body,
        [state_shape, query_shape],
        "own",
        2**24,
        arguments,
        small_scratch + [pltpu.SemaphoreType.DMA((7,))],
        space=pl.ANY,
    )
    packs = [own_queries] + list(sent_queries)

    def query_part(turn, part):
        return to_device(packs[part], query=turn ^ part)

    query_parts = [query_part(0, part) for part in range(query_devices)]
    states = [own_state, exchange(mate_state, page=1)]

    def in_columns(parts, axis):
        return jnp.concatenate(
            [
                lax.slice_in_dim(part, at * piece, (at + 1) * piece, axis=axis)
                for at in range(ranks)
                for part in parts
            ],
            axis=axis,
        )

    def read_queries(query_refs):
        return halves(in_columns([ref[:part_rows, :] for ref in query_refs], 0))

    def part_of(ref, at):
        return ref.at[pl.ds(at * packed_rows, packed_rows)]

    def parts_of(refs):
        return refs if len(refs) == CORES else [part_of(refs[0], at) for at in range(CORES)]

    def step_sizes(tile_refs):
        row = jnp.sum(tile_refs[0][...], axis=0)
        return (
            RATE_KEYS / jnp.sqrt(row[:, 0:1] / entry_total + EPSILON),
            RATE_VALUES / jnp.sqrt(row[:, 1:2] / entry_total + EPSILON),
            RATE_BIAS / jnp.sqrt(row[:, 2:3] / slot_total + EPSILON),
        )

    def read_pack(ref):
        return ref[:slot_rows, :], ref[slot_rows : 2 * slot_rows, :], ref[2 * slot_rows :, :]

    def store_pack(ref, values):
        ref[:slot_rows, :] = values[0]
        ref[slot_rows : 2 * slot_rows, :] = values[1]
        ref[2 * slot_rows :, :] = values[2]

    def updated(state, grads, sizes):
        return [value - size * grad for value, grad, size in zip(state, grads, sizes)]

    def page_scores(ref, queries, positions):
        scores = dot_deep(halves(ref[:slot_rows, :]), queries, 1, 1) * score_scale
        bias = row_as_column(tail_as_row(ref, 2 * slot_rows, bias_rows), width)
        scores = scores + jnp.concatenate([bias] * (positions.shape[1] // width), axis=1)
        page_start = ref[packed_rows - 1 : packed_rows, 0:1]
        visible = jnp.broadcast_to(positions >= page_start, scores.shape)
        return jnp.where(visible, scores, MASKED), visible

    def read_positions(query_refs):
        return in_columns(
            [tail_as_row(ref, part_rows + piece, pos_rows) for ref in query_refs], 1
        )

    def forward(state_refs, query_refs, chunk_outs, weights_out, max_out, chunks):
        rank, _, _ = places()
        all_queries, positions = read_queries(query_refs), read_positions(query_refs)
        all_scores, all_visible = [], []
        for at, ref in enumerate(state_refs):
            scores, visible = page_scores(ref, all_queries, positions)
            all_scores.append(scores)
            all_visible.append(visible)
        row_max = jnp.max(all_scores[0], axis=0, keepdims=True)
        for scores in all_scores[1:]:
            row_max = jnp.maximum(row_max, jnp.max(scores, axis=0, keepdims=True))
        row_total = jnp.zeros_like(row_max)
        row_sum = jnp.zeros((width, query_rows), jnp.float32)
        for at, ref in enumerate(state_refs):
            weights = jnp.where(all_visible[at], jnp.exp(all_scores[at] - row_max), 0.0)
            weights_out[at * slot_rows : (at + 1) * slot_rows, :] = weights
            row_total = row_total + jnp.sum(weights, axis=0, keepdims=True)
            values = halves(ref[slot_rows : 2 * slot_rows, :])
            row_sum = row_sum + dot_low(values, halves(weights), 0, 0)
        max_out[...] = jnp.broadcast_to(row_max, (TAIL, query_rows))
        tail = jnp.concatenate(
            [row_max, row_total, jnp.zeros((TAIL - 2, query_rows), jnp.float32)], axis=0
        )
        for at in range(ranks):
            columns = slice(at * chunk, (at + 1) * chunk)
            chunks[at, :width, :] = row_sum[:, columns]
            chunks[at, width:, :] = tail[:, columns]
        for turn in range(ranks):
            chunk_outs[turn][...] = chunks[rank ^ turn]

    chunk_shape = (width + TAIL, chunk)
    forward_shapes = [chunk_shape] * ranks + [(slots, query_rows), (TAIL, query_rows)]
    chunk_scratch = [pltpu.VMEM((ranks,) + chunk_shape, jnp.float32)]

    fold = max(1, 128 // piece)
    folded, columns = width // fold, fold * piece
    piece_shape = (folded + TAIL, columns)
    piece_scratch = [pltpu.VMEM((ranks,) + piece_shape, jnp.float32)]

    def fold_rows(value):
        groups = [value[at * folded : (at + 1) * folded, :] for at in range(fold)]
        return jnp.concatenate(groups, axis=1)

    def unfold_rows(value):
        groups = [value[:, at * piece : (at + 1) * piece] for at in range(fold)]
        return jnp.concatenate(groups, axis=0)

    def rows_tail(rows):
        empty = jnp.zeros((TAIL - len(rows), columns), jnp.float32)
        return jnp.concatenate(rows + [empty], axis=0)

    def part_body(*refs):
        state_refs, (query_ref, *refs) = refs[:CORES], refs[CORES:]
        piece_outs, (weights_out, max_out, pieces) = refs[:ranks], refs[ranks:]
        rank, _, _ = places()
        queries = halves(query_ref[:part_rows, :])
        position_row = tail_as_row(query_ref, part_rows + piece, pos_rows)
        all_scores, all_visible = [], []
        for ref in state_refs:
            scores, visible = page_scores(ref, queries, position_row)
            all_scores.append(scores)
            all_visible.append(visible)
        row_max = jnp.max(all_scores[0], axis=0, keepdims=True)
        for scores in all_scores[1:]:
            row_max = jnp.maximum(row_max, jnp.max(scores, axis=0, keepdims=True))
        row_total = jnp.zeros_like(row_max)
        row_sum = jnp.zeros((width, part_rows), jnp.float32)
        for at, ref in enumerate(state_refs):
            weights = jnp.where(all_visible[at], jnp.exp(all_scores[at] - row_max), 0.0)
            weights_out[at * slot_rows : (at + 1) * slot_rows, :] = weights
            row_total = row_total + jnp.sum(weights, axis=0, keepdims=True)
            values = halves(ref[slot_rows : 2 * slot_rows, :])
            row_sum = row_sum + dot_low(values, halves(weights), 0, 0)
        max_out[...] = jnp.broadcast_to(row_max, (TAIL, part_rows))
        for at in range(ranks):
            own = slice(at * piece, (at + 1) * piece)
            pieces[at, :folded, :] = fold_rows(row_sum[:, own])
            pieces[at, folded:, :] = rows_tail(
                [jnp.concatenate([row[:, own]] * fold, axis=1) for row in (row_max, row_total)]
            )
        for turn in range(ranks):
            piece_outs[turn][...] = pieces[rank ^ turn]

    part_shapes = [piece_shape] * ranks + [(slots, part_rows), (TAIL, part_rows)]

    def next_body(*refs):
        state_refs, refs = refs[:2], refs[2:]
        query_refs, refs = refs[:query_devices], refs[query_devices:]
        grad_refs, refs = refs[:2], refs[2:]
        tile_refs, refs = refs[: len(tiles)], refs[len(tiles) :]
        refs[0][CORES * packed_rows :, :] = query_refs[0][...]
        state_outs, refs = parts_of(refs[:1]), refs[1:]
        chunk_outs, refs = refs[:ranks], refs[ranks:]
        sizes = step_sizes(tile_refs)
        for at in range(2):
            state = read_pack(state_refs[at])
            store_pack(state_outs[at], updated(state, read_pack(grad_refs[at]), sizes))
        forward(state_outs, query_refs, chunk_outs, *refs)

    def merged_chunk(query_refs, sums, maxima, totals, out):
        targets = jnp.concatenate(
            [ref[part_rows : part_rows + piece, :] for ref in query_refs], axis=0
        )
        row_max = maxima[0]
        for other in maxima[1:]:
            row_max = jnp.maximum(row_max, other)
        row_total = jnp.zeros_like(row_max)
        row_sum = jnp.zeros((width, chunk), jnp.float32)
        for part_sum, part_max, part_total in zip(sums, maxima, totals):
            factor = jnp.exp(part_max - row_max)
            row_total = row_total + part_total * factor
            row_sum = row_sum + part_sum * factor
        output = row_sum / row_total
        residual = output - targets.T
        row_delta = jnp.sum(residual * output, axis=0, keepdims=True)
        out[:width, :] = residual
        out[width:, :] = jnp.concatenate(
            [row_max, row_total, row_delta, jnp.zeros((TAIL - 3, chunk), jnp.float32)], axis=0
        )

    def first_merge_body(*refs):
        query_refs, (*piece_refs, merged_out) = refs[:query_devices], refs[query_devices:]

        def joined(read):
            return [
                jnp.concatenate([read(ref) for ref in piece_refs[turn::ranks]], axis=1)
                for turn in range(ranks)
            ]

        merged_chunk(
            query_refs,
            joined(lambda ref: unfold_rows(ref[:folded, :])),
            joined(lambda ref: ref[folded : folded + 1, :piece]),
            joined(lambda ref: ref[folded + 1 : folded + 2, :piece]),
            merged_out,
        )

    def merge_body(*refs):
        query_refs, (*chunk_refs, merged_out) = refs[:query_devices], refs[query_devices:]
        merged_chunk(
            query_refs,
            [ref[:width, :] for ref in chunk_refs],
            [ref[width : width + 1, :] for ref in chunk_refs],
            [ref[width + 1 : width + 2, :] for ref in chunk_refs],
            merged_out,
        )

    def page_gradients(weights, factor, state_ref, all_queries, residual, row_delta):
        attention = weights * factor
        grad_values = dot_narrow(halves(attention), residual, 1, 1)
        grad_probs = dot_deep(halves(state_ref[slot_rows : 2 * slot_rows, :]), residual, 1, 0)
        grad_scores = attention * (grad_probs - row_delta)
        grad_keys = dot_narrow(halves(grad_scores), all_queries, 1, 0) * score_scale
        grad_bias = column_sums(grad_scores, width)
        return grad_keys, grad_values, row_as_tail(grad_bias, width)

    def split_merged(joined):
        row_max, row_total, row_delta = (
            joined[width + at : width + at + 1, :] for at in range(3)
        )
        return halves(joined[:width, :]), row_max, row_total, row_delta

    def read_chunks(merged_refs, chunks):
        rank, _, _ = places()
        for turn, ref in zip([0] + turns[::-1], merged_refs):
            chunks[rank ^ turn] = ref[...]
        return [chunks[at] for at in range(ranks)]

    def join_body(*refs):
        *merged_refs, joined_out, chunks = refs
        joined_out[...] = jnp.concatenate(read_chunks(merged_refs, chunks), axis=1)

    def backward_body(*refs):
        weights_refs, refs = refs[: len(weights)], refs[len(weights) :]
        max_refs, refs = refs[: len(weights)], refs[len(weights) :]
        state_refs, refs = parts_of(refs[: len(states)]), refs[len(states) :]
        query_refs, refs = refs[:query_devices], refs[query_devices:]
        merged_refs, refs = refs[: len(all_merged)], refs[len(all_merged) :]
        grad_outs, (squares_out, *scratch) = refs[:2], refs[2:]
        if len(states) < CORES:
            joined = merged_refs[0][...]
            all_queries = read_queries(query_refs)
        else:
            chunks = read_chunks(merged_refs, *scratch)
            joined = jnp.concatenate(
                [
                    value[:, part * piece : (part + 1) * piece]
                    for part in range(query_devices)
                    for value in chunks
                ],
                axis=1,
            )
            all_queries = halves(
                jnp.concatenate([ref[:part_rows, :] for ref in query_refs], axis=0)
            )
        residual, row_max, row_total, row_delta = split_merged(joined)
        maxima = jnp.concatenate([ref[0:1, :] for ref in max_refs], axis=1)
        factor = jnp.exp(maxima - row_max) / row_total
        squares = [jnp.zeros((1, width), jnp.float32)] * 3
        for at, (ref, out) in enumerate(zip(state_refs, grad_outs)):
            rows = slice(at * slot_rows, (at + 1) * slot_rows)
            page_weights = jnp.concatenate([part[rows, :] for part in weights_refs], axis=1)
            grads = page_gradients(page_weights, factor, ref, all_queries, residual, row_delta)
            store_pack(out, grads)
            for which, grad in enumerate(grads):
                squares[which] = squares[which] + jnp.sum(grad * grad, axis=0, keepdims=True)
        lanes = lax.broadcasted_iota(jnp.int32, (1, width), 1)
        row = jnp.zeros((1, width), jnp.float32)
        for which, square in enumerate(squares):
            row = jnp.where(lanes == which, jnp.sum(square, axis=1, keepdims=True), row)
        for at in range(devices):
            squares_out[at] = row

    def page_body(at):
        def body(tile_ref, grad_ref, own_state_ref, *refs):
            state_refs, refs = refs[: query_devices - 1], refs[query_devices - 1 :]
            joined_refs, (*pack_refs, out) = refs[: query_devices - 1], refs[query_devices - 1 :]
            sizes = step_sizes([tile_ref])
            state = read_pack(part_of(own_state_ref, at))
            store_pack(part_of(out, 0), updated(state, read_pack(grad_ref), sizes))
            for turn, (state_ref, joined_ref) in enumerate(zip(state_refs, joined_refs), 1):
                query_refs = [state_ref.at[pl.ds(CORES * packed_rows, query_shape[0])]]
                query_refs += pack_refs[(turn - 1) * (query_devices - 1) :][: query_devices - 1]
                residual, row_max, row_total, row_delta = split_merged(joined_ref[...])
                all_queries = read_queries(query_refs)
                ref = part_of(state_ref, at)
                scores, visible = page_scores(ref, all_queries, read_positions(query_refs))
                weights = jnp.where(visible, jnp.exp(scores - row_max), 0.0)
                grads = page_gradients(
                    weights, 1.0 / row_total, ref, all_queries, residual, row_delta
                )
                store_pack(part_of(out, turn), updated(read_pack(ref), grads, sizes))

        return body

    for repeat in range(STEPS):
        last = repeat == STEPS - 1
        if repeat == 0:
            sums, weights, maxima = [], [], []
            for query_pack in query_parts:
                *pieces, part_weights, part_max = call(
                    part_body,
                    part_shapes,
                    "forward",
                    2 * matmul_cost // query_devices,
                    states + [query_pack],
                    piece_scratch,
                    after=maxima[-1:],
                )
                arrived = {
                    turn: exchange(pieces[turn], page=CORES * turn)
                    for turn in turns
                }
                sums += list(arrived.values()) + pieces[:1]
                weights.append(part_weights)
                maxima.append(part_max)
        else:
            new_state, *chunk_parts, part_weights, part_max = call(
                next_body,
                [(CORES * packed_rows + query_shape[0], width)] + forward_shapes,
                "update_forward",
                2 * matmul_cost,
                states + query_parts + grads + tiles,
                chunk_scratch,
            )
            states, weights, maxima = [new_state], [part_weights], [part_max]
            arrived = {
                turn: exchange(chunk_parts[turn], page=CORES * turn)
                for turn in turns
            }
            sums = chunk_parts[:1] + list(arrived.values())
            new_states = states + [
                exchange(states[0], query=turn) for turn in range(1, query_devices)
            ]
        (merged,) = call(
            merge_body if repeat else first_merge_body,
            [chunk_shape],
            "merge",
            2**20,
            query_parts + sums,
        )
        all_merged = [merged] + [exchange(merged, page=CORES * turn) for turn in reversed(turns)]
        if last:
            all_merged = call(
                join_body, [(width + TAIL, query_rows)], "join", 2**20, all_merged, chunk_scratch
            )
            all_joined = [
                to_device(all_merged[0], query=turn) for turn in range(query_devices)
            ]
        own_grad, mate_grad, squares = call(
            backward_body,
            packed_shapes + [(devices, 1, width)],
            "backward",
            3 * matmul_cost,
            weights + maxima + states + query_parts + list(all_merged),
            scratch=() if last else chunk_scratch,
        )
        grads = [own_grad, mate_grad]
        tiles = [
            lax.all_to_all(
                squares, ("page", "query", "head"), split_axis=0, concat_axis=0, tiled=True
            )
        ]

    other_packs = [
        packs[part] if part == turn else query_part(turn, part)
        for turn in range(1, query_devices)
        for part in range(1, query_devices)
    ]
    operands = new_states + all_joined[1:] + other_packs
    pages = []
    for at, grad in ((1, mate_grad), (0, own_grad)):
        pages += call(
            page_body(at),
            [(query_devices * packed_rows, width)],
            "page_update",
            3 * matmul_cost // 2,
            tiles + [grad] + operands,
            after=pages,
        )
    pages = [pages[1], exchange(pages[0], page=1)]

    def last_body(*refs):
        page_refs, (keys_out, values_out, bias_out) = refs[:CORES], refs[CORES:]
        _, core, me = places()
        for turn, flip in itertools.product(range(query_devices), range(CORES)):
            keys, values, bias = read_pack(part_of(page_refs[flip], turn))
            head = CORES * (me ^ turn) + (core ^ flip)
            keys_out[head] = keys
            values_out[head] = values
            bias_row = jnp.concatenate([bias[row : row + 1] for row in range(bias_rows)], axis=1)
            bias_out[pl.ds(head, 1), :] = bias_row

    return tuple(
        call(
            last_body,
            [compact_keys.shape, compact_values.shape, slot_bias.shape],
            "unpack",
            2**20,
            pages,
        )
    )


def from_partner(value, axis, stride):
    mask = 2**stride
    pairs = [(source, source ^ mask) for source in range(lax.axis_size(axis))]
    return lax.ppermute(value, axis, pairs)


def squared_sums(grad_keys, grad_values, grad_bias):
    return jnp.stack(
        [
            jnp.sum(grad_keys * grad_keys),
            jnp.sum(grad_values * grad_values),
            jnp.sum(grad_bias * grad_bias),
        ]
    )


def apply_update(states, grads, totals, entry_count, slot_total):
    key_state, value_state, bias_state = states
    grad_keys, grad_values, grad_bias = grads
    rms_keys = jnp.sqrt(totals[0] / entry_count + EPSILON)
    rms_values = jnp.sqrt(totals[1] / entry_count + EPSILON)
    rms_bias = jnp.sqrt(totals[2] / slot_total + EPSILON)
    return (
        key_state - RATE_KEYS * grad_keys / rms_keys,
        value_state - RATE_VALUES * grad_values / rms_values,
        bias_state - RATE_BIAS * grad_bias / rms_bias,
    )


def local_gradients(queries, targets, visible, compact_keys, compact_values, slot_bias):
    score_scale = 1.0 / math.sqrt(queries.shape[2])
    scores = jnp.einsum("hqd,hsd->hqs", queries, compact_keys, precision=HIGHEST) * score_scale
    scores = jnp.where(visible, scores + slot_bias[:, None, :], MASKED)
    local_max = jnp.max(scores, axis=2)
    row_max = lax.pmax(local_max, "page")
    weights = jnp.where(visible, jnp.exp(scores - row_max[:, :, None]), 0.0)
    local_sum = jnp.einsum("hqs,hsd->hqd", weights, compact_values, precision=HIGHEST)
    row_total, row_sum = lax.psum((jnp.sum(weights, axis=2), local_sum), "page")
    attention = weights / row_total[:, :, None]
    output = row_sum / row_total[:, :, None]
    residual = output - targets
    grad_values = jnp.einsum("hqs,hqd->hsd", attention, residual, precision=HIGHEST)
    row_delta = jnp.sum(residual * output, axis=2)
    grad_probs = jnp.einsum("hqd,hsd->hqs", residual, compact_values, precision=HIGHEST)
    grad_scores = attention * (grad_probs - row_delta[:, :, None])
    grad_bias = jnp.sum(grad_scores, axis=1)
    grad_keys = jnp.einsum("hqs,hqd->hsd", grad_scores, queries, precision=HIGHEST) * score_scale
    return (grad_keys, grad_values, grad_bias)


def per_device(queries, compact_keys, compact_values, slot_bias, targets, positions, assignment):
    page_number = assignment[lax.axis_index("page")]
    local_heads = compact_keys.shape[0]
    slot_total = local_heads * lax.axis_size("head") * compact_keys.shape[1] * lax.axis_size("page")
    entry_count = slot_total * compact_keys.shape[2]
    query_count = lax.axis_size("query")
    heads_kept = max(local_heads // query_count, 1)
    query_parts = max(query_count // local_heads, 1)
    part_rows = queries.shape[1] // query_parts

    def split_items(array):
        width = array.shape[2]
        array = array.reshape(local_heads // heads_kept, heads_kept, query_parts, part_rows, width)
        array = jnp.transpose(array, (0, 2, 1, 3, 4))
        return array.reshape(query_count, heads_kept, part_rows, width)

    def join_items(array):
        width = array.shape[3]
        array = jnp.transpose(array, (1, 0, 2, 3))
        return array.reshape(heads_kept, query_count * part_rows, width)

    position_column = positions.astype(jnp.float32)[:, :, None]
    got_queries, got_targets, got_positions = (
        lax.all_to_all(split_items(queries), "query", split_axis=0, concat_axis=0, tiled=True),
        lax.all_to_all(split_items(targets), "query", split_axis=0, concat_axis=0, tiled=True),
        lax.all_to_all(
            split_items(position_column), "query", split_axis=0, concat_axis=0, tiled=True
        ),
    )
    group_queries = join_items(got_queries)
    group_targets = join_items(got_targets)
    group_positions = join_items(got_positions)[:, :, 0]
    visible = (page_number.astype(jnp.float32) <= jnp.floor(group_positions / PAGE_LEN))[:, :, None]
    query_index = lax.axis_index("query")
    first_head = query_index // query_parts * heads_kept
    key_state = lax.dynamic_slice_in_dim(compact_keys, first_head, heads_kept, 0)
    value_state = lax.dynamic_slice_in_dim(compact_values, first_head, heads_kept, 0)
    bias_state = lax.dynamic_slice_in_dim(slot_bias, first_head, heads_kept, 0)
    counted = (query_index % query_parts == 0).astype(jnp.float32)
    for repeat in range(STEPS):
        grads = local_gradients(
            group_queries, group_targets, visible, key_state, value_state, bias_state
        )
        for bit in range(query_parts.bit_length() - 1):
            partner = from_partner((grads[0], grads[1], grads[2]), "query", bit)
            grads = (grads[0] + partner[0], grads[1] + partner[1], grads[2] + partner[2])
        totals = lax.psum(
            squared_sums(grads[0], grads[1], grads[2]) * counted, ("page", "query", "head")
        )
        key_state, value_state, bias_state = apply_update(
            (key_state, value_state, bias_state), grads, totals, entry_count, slot_total
        )
    all_keys, all_values, all_bias = (
        lax.all_gather(key_state, "query", axis=0, tiled=True),
        lax.all_gather(value_state, "query", axis=0, tiled=True),
        lax.all_gather(bias_state, "query", axis=0, tiled=True),
    )
    slot_rows = compact_keys.shape[1]
    head_width = compact_keys.shape[2]
    all_keys = all_keys.reshape(
        local_heads // heads_kept, query_parts, heads_kept, slot_rows, head_width
    )[:, 0]
    all_values = all_values.reshape(
        local_heads // heads_kept, query_parts, heads_kept, slot_rows, head_width
    )[:, 0]
    all_bias = all_bias.reshape(local_heads // heads_kept, query_parts, heads_kept, slot_rows)[:, 0]
    return (
        all_keys.reshape(local_heads, slot_rows, head_width),
        all_values.reshape(local_heads, slot_rows, head_width),
        all_bias.reshape(local_heads, slot_rows),
    )


def solution(mesh):
    placed = (
        P("head", "query", None),
        P("head", "page", None),
        P("head", "page", None),
        P("head", "page"),
        P("head", "query", None),
        P("head", "query"),
        P(),
    )

    def program(*args):
        plan = direct_per_device if direct_plan_fits(mesh, args[0], args[1]) else per_device
        return jax.shard_map(
            plan,
            mesh=mesh,
            in_specs=placed,
            out_specs=(P("head", "page", None), P("head", "page", None), P("head", "page")),
            check_vma=False,
        )(*args)

    return program
```

```python
import itertools
import math

import jax
import jax.numpy as jnp
from jax import lax
from jax.experimental import pallas as pl
from jax.experimental.pallas import tpu as pltpu
from jax.sharding import PartitionSpec as P

STEPS = 2
PAGE_LEN = 32768


MASKED = -1e30
EPSILON = 1e-06
RATE_KEYS = 0.05
RATE_VALUES = 0.05
RATE_BIAS = 0.2
HIGHEST = lax.Precision.HIGHEST
TAIL = 8
CORES = 2


def exchange(value, **masks):
    axes = tuple(masks)
    sizes = [lax.axis_size(axis) for axis in axes]

    def flat(place):
        index = 0
        for size, at in zip(sizes, place):
            index = index * size + at
        return index

    pairs = [
        (flat(place), flat([at ^ mask for at, mask in zip(place, masks.values())]))
        for place in itertools.product(*map(range, sizes))
    ]
    return lax.ppermute(value, axes, pairs)


def halves(value):
    high = value.astype(jnp.bfloat16)
    return high, (value - high.astype(jnp.float32)).astype(jnp.bfloat16)


def one_pass(left, right, left_dim, right_dim):
    return lax.dot_general(
        left,
        right,
        (((left_dim,), (right_dim,)), ((), ())),
        preferred_element_type=jnp.float32,
    )


def dot_deep(left, right, left_dim, right_dim):
    left = jnp.concatenate([left[0], left[1], left[0]], axis=left_dim)
    right = jnp.concatenate([right[0], right[0], right[1]], axis=right_dim)
    return one_pass(left, right, left_dim, right_dim)


def dot_narrow(left, right, left_dim, right_dim):
    both = one_pass(
        left[0], jnp.concatenate(right, axis=1 - right_dim), left_dim, right_dim
    )
    count = both.shape[1] // 2
    cross = both[:, count:] + one_pass(left[1], right[0], left_dim, right_dim)
    return both[:, :count] + cross


def dot_low(left, right, left_dim, right_dim):
    both = one_pass(jnp.concatenate(left, axis=1 - left_dim), right[0], left_dim, right_dim)
    count = both.shape[0] // 2
    cross = both[count:, :] + one_pass(left[0], right[1], left_dim, right_dim)
    return both[:count, :] + cross


def call(body, out_shapes, name, cost, operands, scratch=(), after=(), space=pltpu.VMEM, vmem=32):
    spaces = [space] * len(operands) + [pl.ANY] * len(after)
    count = len(operands)

    def without_after(*refs):
        body(*refs[:count], *refs[count + len(after) :])

    return pl.pallas_call(
        without_after,
        out_shape=[jax.ShapeDtypeStruct(shape, jnp.float32) for shape in out_shapes],
        in_specs=[pl.BlockSpec(memory_space=space) for space in spaces],
        out_specs=[pl.BlockSpec(memory_space=pltpu.VMEM) for _ in out_shapes],
        scratch_shapes=scratch,
        compiler_params=pltpu.CompilerParams(vmem_limit_bytes=vmem * 2**20),
        cost_estimate=pl.CostEstimate(flops=cost, bytes_accessed=2**20, transcendentals=0),
        name=name,
    )(*operands, *after)


def row_as_tail(row, width):
    rows = [row[:, at : at + width] for at in range(0, row.shape[1], width)]
    rows.append(jnp.zeros((TAIL - len(rows), width), row.dtype))
    return jnp.concatenate(rows, axis=0)


def tail_as_row(ref, start, count):
    return jnp.concatenate([ref[start + at : start + at + 1, :] for at in range(count)], axis=1)


def row_as_column(row, width):
    parts = []
    for at in range(0, row.shape[1], width):
        parts.append(jnp.broadcast_to(row[:, at : at + width], (width, width)).T)
    return jnp.concatenate(parts, axis=0)


def column_sums(value, width):
    groups = [value[:, at : at + width] for at in range(0, value.shape[1], width)]
    partial = sum(groups[1:], groups[0])
    blocks = [
        jnp.sum(partial[at : at + width, :].T, axis=0, keepdims=True)
        for at in range(0, value.shape[0], width)
    ]
    return jnp.concatenate(blocks, axis=1)


def direct_plan_fits(mesh, queries, compact_keys):
    sizes = [mesh.shape[axis] for axis in ("page", "query", "head")]
    pages, query_devices, head_devices = sizes
    local_heads = queries.shape[0] // head_devices
    part_rows = queries.shape[1] // query_devices
    slot_rows = compact_keys.shape[1] // pages
    width = queries.shape[2]
    if any(size & (size - 1) for size in sizes) or pages < CORES or width % 128:
        return False
    if local_heads != CORES * query_devices:
        return False
    ranks = pages // CORES
    chunk = part_rows * query_devices // ranks
    return (
        part_rows * query_devices % ranks == 0
        and chunk % 128 == 0
        and part_rows % (8 * ranks) == 0
        and (part_rows // ranks % 128 == 0 or 1024 % (part_rows // ranks * 8) == 0)
        and slot_rows % width == 0
        and part_rows % width == 0
        and max(slot_rows, part_rows) < TAIL * width
    )


def direct_per_device(
    queries, compact_keys, compact_values, slot_bias, targets, positions, assignment
):
    local_heads, part_rows, width = queries.shape
    slot_rows = compact_keys.shape[1]
    query_devices = lax.axis_size("query")
    head_devices = lax.axis_size("head")
    ranks = lax.axis_size("page") // CORES
    query_rows = part_rows * query_devices
    chunk, piece = query_rows // ranks, part_rows // ranks
    turns = [ranks // 2] + [turn for turn in range(1, ranks) if turn != ranks // 2]
    slot_total = local_heads * head_devices * slot_rows * lax.axis_size("page")
    entry_total = slot_total * width
    score_scale = 1.0 / math.sqrt(width)
    slots = CORES * slot_rows
    devices = ranks * CORES * query_devices * head_devices
    pos_rows = part_rows // width
    bias_rows = slot_rows // width
    packed_rows = 2 * slot_rows + TAIL
    packed_shapes = [(packed_rows, width)] * 2
    matmul_cost = 3 * 2 * slots * query_rows * width

    def places():
        page = lax.axis_index("page")
        return page // CORES, page % CORES, lax.axis_index("query")

    def to_device(value, **masks):
        masks = {axis: mask for axis, mask in masks.items() if mask}
        return exchange(value, **masks) if masks else value

    def pack_queries(head, rank, queries, targets, out):
        rows = pl.ds(pl.multiple_of(rank * piece, piece), piece)
        return [
            (queries.at[head], out.at[pl.ds(0, part_rows)]),
            (targets.at[head, rows], out.at[pl.ds(part_rows, piece)]),
        ]

    def pack_state(head, keys, values, out):
        return [
            (keys.at[head], out.at[pl.ds(0, slot_rows)]),
            (values.at[head], out.at[pl.ds(slot_rows, slot_rows)]),
        ]

    def start_all(copies, sems, first=0):
        copies = [
            pltpu.make_async_copy(source, target, sems.at[first + at])
            for at, (source, target) in enumerate(copies)
        ]
        for copy in copies:
            copy.start()
        return copies

    def position_tail(head, positions_ref):
        return row_as_tail(positions_ref[pl.ds(head, 1), :].astype(jnp.float32), width)

    def state_tail(head, page, bias_ref, assignment_ref):
        page_start = (assignment_ref[page] * PAGE_LEN).astype(jnp.float32)
        tail = row_as_tail(bias_ref[pl.ds(head, 1), :], width)
        return jnp.concatenate(
            [tail[: TAIL - 1], jnp.full((1, width), page_start, jnp.float32)], axis=0
        )

    def send_body(
        queries, keys, values, biases, targets, positions, assignment, state_out, *refs
    ):
        query_outs = refs[: query_devices - 1]
        bias_ref, positions_ref, assignment_ref, sems = refs[query_devices - 1 :]
        rank, core, me = places()
        heads = [CORES * (me ^ turn) + core for turn in range(1, query_devices)]
        mate_head = CORES * me + (core ^ 1)
        small = start_all(
            [(assignment, assignment_ref), (positions, positions_ref), (biases, bias_ref)], sems
        )
        copies = pack_state(mate_head, keys, values, state_out)
        for head, out in zip(heads, query_outs):
            copies += pack_queries(head, rank, queries, targets, out)
        copies = start_all(copies, sems, 3)
        for copy in small:
            copy.wait()
        state_out[2 * slot_rows :, :] = state_tail(
            mate_head, CORES * rank + core, bias_ref, assignment_ref
        )
        for head, out in zip(heads, query_outs):
            out[part_rows + piece :, :] = position_tail(head, positions_ref)
        for copy in copies:
            copy.wait()

    def own_body(
        queries, keys, values, biases, targets, positions, assignment, state_out, query_out, *refs
    ):
        bias_ref, positions_ref, assignment_ref, sems = refs
        rank, core, me = places()
        head = CORES * me + core
        small = start_all(
            [(assignment, assignment_ref), (positions, positions_ref), (biases, bias_ref)], sems
        )
        copies = pack_state(head, keys, values, state_out)
        copies += pack_queries(head, rank, queries, targets, query_out)
        copies = start_all(copies, sems, 3)
        for copy in small:
            copy.wait()
        state_out[2 * slot_rows :, :] = state_tail(
            head, CORES * rank + core, bias_ref, assignment_ref
        )
        query_out[part_rows + piece :, :] = position_tail(head, positions_ref)
        for copy in copies:
            copy.wait()

    state_shape, query_shape = (packed_rows, width), (part_rows + piece + TAIL, width)
    small_scratch = [
        pltpu.VMEM(slot_bias.shape, jnp.float32),
        pltpu.VMEM(positions.shape, jnp.int32),
        pltpu.SMEM(assignment.shape, jnp.int32),
    ]
    arguments = [
        queries, compact_keys, compact_values, slot_bias, targets, positions, assignment
    ]
    mate_state, *sent_queries = call(
        send_body,
        [state_shape] + [query_shape] * (query_devices - 1),
        "pack",
        2**20,
        arguments,
        small_scratch + [pltpu.SemaphoreType.DMA((3 + 2 * query_devices,))],
        space=pl.ANY,
        vmem=60,
    )
    own_state, own_queries = call(
        own_body,
        [state_shape, query_shape],
        "own",
        2**24,
        arguments,
        small_scratch + [pltpu.SemaphoreType.DMA((7,))],
        space=pl.ANY,
    )
    packs = [own_queries] + list(sent_queries)

    def query_part(turn, part):
        return to_device(packs[part], query=turn ^ part)

    query_parts = [query_part(0, part) for part in range(query_devices)]
    states = [own_state, exchange(mate_state, page=1)]

    def in_columns(parts, axis):
        return jnp.concatenate(
            [
                lax.slice_in_dim(part, at * piece, (at + 1) * piece, axis=axis)
                for at in range(ranks)
                for part in parts
            ],
            axis=axis,
        )

    def read_queries(query_refs):
        return halves(in_columns([ref[:part_rows, :] for ref in query_refs], 0))

    def part_of(ref, at):
        return ref.at[pl.ds(at * packed_rows, packed_rows)]

    def parts_of(refs):
        return refs if len(refs) == CORES else [part_of(refs[0], at) for at in range(CORES)]

    def step_sizes(tile_refs):
        row = jnp.sum(tile_refs[0][...], axis=0)
        return (
            RATE_KEYS / jnp.sqrt(row[:, 0:1] / entry_total + EPSILON),
            RATE_VALUES / jnp.sqrt(row[:, 1:2] / entry_total + EPSILON),
            RATE_BIAS / jnp.sqrt(row[:, 2:3] / slot_total + EPSILON),
        )

    def read_pack(ref):
        return ref[:slot_rows, :], ref[slot_rows : 2 * slot_rows, :], ref[2 * slot_rows :, :]

    def store_pack(ref, values):
        ref[:slot_rows, :] = values[0]
        ref[slot_rows : 2 * slot_rows, :] = values[1]
        ref[2 * slot_rows :, :] = values[2]

    def updated(state, grads, sizes):
        return [value - size * grad for value, grad, size in zip(state, grads, sizes)]

    def page_scores(ref, queries, positions):
        scores = dot_deep(halves(ref[:slot_rows, :]), queries, 1, 1) * score_scale
        bias = row_as_column(tail_as_row(ref, 2 * slot_rows, bias_rows), width)
        scores = scores + jnp.concatenate([bias] * (positions.shape[1] // width), axis=1)
        page_start = ref[packed_rows - 1 : packed_rows, 0:1]
        visible = jnp.broadcast_to(positions >= page_start, scores.shape)
        return jnp.where(visible, scores, MASKED), visible

    def read_positions(query_refs):
        return in_columns(
            [tail_as_row(ref, part_rows + piece, pos_rows) for ref in query_refs], 1
        )

    def forward(state_refs, query_refs, chunk_outs, weights_out, max_out, chunks):
        rank, _, _ = places()
        all_queries, positions = read_queries(query_refs), read_positions(query_refs)
        all_scores, all_visible = [], []
        for at, ref in enumerate(state_refs):
            scores, visible = page_scores(ref, all_queries, positions)
            all_scores.append(scores)
            all_visible.append(visible)
        row_max = jnp.max(all_scores[0], axis=0, keepdims=True)
        for scores in all_scores[1:]:
            row_max = jnp.maximum(row_max, jnp.max(scores, axis=0, keepdims=True))
        row_total = jnp.zeros_like(row_max)
        row_sum = jnp.zeros((width, query_rows), jnp.float32)
        for at, ref in enumerate(state_refs):
            weights = jnp.where(all_visible[at], jnp.exp(all_scores[at] - row_max), 0.0)
            weights_out[at * slot_rows : (at + 1) * slot_rows, :] = weights
            row_total = row_total + jnp.sum(weights, axis=0, keepdims=True)
            values = halves(ref[slot_rows : 2 * slot_rows, :])
            row_sum = row_sum + dot_low(values, halves(weights), 0, 0)
        max_out[...] = jnp.broadcast_to(row_max, (TAIL, query_rows))
        tail = jnp.concatenate(
            [row_max, row_total, jnp.zeros((TAIL - 2, query_rows), jnp.float32)], axis=0
        )
        for at in range(ranks):
            columns = slice(at * chunk, (at + 1) * chunk)
            chunks[at, :width, :] = row_sum[:, columns]
            chunks[at, width:, :] = tail[:, columns]
        for turn in range(ranks):
            chunk_outs[turn][...] = chunks[rank ^ turn]

    chunk_shape = (width + TAIL, chunk)
    forward_shapes = [chunk_shape] * ranks + [(slots, query_rows), (TAIL, query_rows)]
    chunk_scratch = [pltpu.VMEM((ranks,) + chunk_shape, jnp.float32)]

    fold = max(1, 128 // piece)
    folded, columns = width // fold, fold * piece
    piece_shape = (folded + TAIL, columns)
    piece_scratch = [pltpu.VMEM((ranks,) + piece_shape, jnp.float32)]

    def fold_rows(value):
        groups = [value[at * folded : (at + 1) * folded, :] for at in range(fold)]
        return jnp.concatenate(groups, axis=1)

    def unfold_rows(value):
        groups = [value[:, at * piece : (at + 1) * piece] for at in range(fold)]
        return jnp.concatenate(groups, axis=0)

    def rows_tail(rows):
        empty = jnp.zeros((TAIL - len(rows), columns), jnp.float32)
        return jnp.concatenate(rows + [empty], axis=0)

    def part_body(*refs):
        state_refs, (query_ref, *refs) = refs[:CORES], refs[CORES:]
        piece_outs, (weights_out, max_out, pieces) = refs[:ranks], refs[ranks:]
        rank, _, _ = places()
        queries = halves(query_ref[:part_rows, :])
        position_row = tail_as_row(query_ref, part_rows + piece, pos_rows)
        all_scores, all_visible = [], []
        for ref in state_refs:
            scores, visible = page_scores(ref, queries, position_row)
            all_scores.append(scores)
            all_visible.append(visible)
        row_max = jnp.max(all_scores[0], axis=0, keepdims=True)
        for scores in all_scores[1:]:
            row_max = jnp.maximum(row_max, jnp.max(scores, axis=0, keepdims=True))
        row_total = jnp.zeros_like(row_max)
        row_sum = jnp.zeros((width, part_rows), jnp.float32)
        for at, ref in enumerate(state_refs):
            weights = jnp.where(all_visible[at], jnp.exp(all_scores[at] - row_max), 0.0)
            weights_out[at * slot_rows : (at + 1) * slot_rows, :] = weights
            row_total = row_total + jnp.sum(weights, axis=0, keepdims=True)
            values = halves(ref[slot_rows : 2 * slot_rows, :])
            row_sum = row_sum + dot_low(values, halves(weights), 0, 0)
        max_out[...] = jnp.broadcast_to(row_max, (TAIL, part_rows))
        for at in range(ranks):
            own = slice(at * piece, (at + 1) * piece)
            pieces[at, :folded, :] = fold_rows(row_sum[:, own])
            pieces[at, folded:, :] = rows_tail(
                [jnp.concatenate([row[:, own]] * fold, axis=1) for row in (row_max, row_total)]
            )
        for turn in range(ranks):
            piece_outs[turn][...] = pieces[rank ^ turn]

    part_shapes = [piece_shape] * ranks + [(slots, part_rows), (TAIL, part_rows)]

    def next_body(*refs):
        state_refs, refs = refs[:2], refs[2:]
        query_refs, refs = refs[:query_devices], refs[query_devices:]
        grad_refs, refs = refs[:2], refs[2:]
        tile_refs, refs = refs[: len(tiles)], refs[len(tiles) :]
        refs[0][CORES * packed_rows :, :] = query_refs[0][...]
        state_outs, refs = parts_of(refs[:1]), refs[1:]
        chunk_outs, refs = refs[:ranks], refs[ranks:]
        sizes = step_sizes(tile_refs)
        for at in range(2):
            state = read_pack(state_refs[at])
            store_pack(state_outs[at], updated(state, read_pack(grad_refs[at]), sizes))
        forward(state_outs, query_refs, chunk_outs, *refs)

    def merged_chunk(query_refs, sums, maxima, totals, out):
        targets = jnp.concatenate(
            [ref[part_rows : part_rows + piece, :] for ref in query_refs], axis=0
        )
        row_max = maxima[0]
        for other in maxima[1:]:
            row_max = jnp.maximum(row_max, other)
        row_total = jnp.zeros_like(row_max)
        row_sum = jnp.zeros((width, chunk), jnp.float32)
        for part_sum, part_max, part_total in zip(sums, maxima, totals):
            factor = jnp.exp(part_max - row_max)
            row_total = row_total + part_total * factor
            row_sum = row_sum + part_sum * factor
        output = row_sum / row_total
        residual = output - targets.T
        row_delta = jnp.sum(residual * output, axis=0, keepdims=True)
        out[:width, :] = residual
        out[width:, :] = jnp.concatenate(
            [row_max, row_total, row_delta, jnp.zeros((TAIL - 3, chunk), jnp.float32)], axis=0
        )

    def first_merge_body(*refs):
        query_refs, (*piece_refs, merged_out) = refs[:query_devices], refs[query_devices:]

        def joined(read):
            return [
                jnp.concatenate([read(ref) for ref in piece_refs[turn::ranks]], axis=1)
                for turn in range(ranks)
            ]

        merged_chunk(
            query_refs,
            joined(lambda ref: unfold_rows(ref[:folded, :])),
            joined(lambda ref: ref[folded : folded + 1, :piece]),
            joined(lambda ref: ref[folded + 1 : folded + 2, :piece]),
            merged_out,
        )

    def merge_body(*refs):
        query_refs, (*chunk_refs, merged_out) = refs[:query_devices], refs[query_devices:]
        merged_chunk(
            query_refs,
            [ref[:width, :] for ref in chunk_refs],
            [ref[width : width + 1, :] for ref in chunk_refs],
            [ref[width + 1 : width + 2, :] for ref in chunk_refs],
            merged_out,
        )

    def page_gradients(weights, factor, state_ref, all_queries, residual, row_delta):
        attention = weights * factor
        grad_values = dot_narrow(halves(attention), residual, 1, 1)
        grad_probs = dot_deep(halves(state_ref[slot_rows : 2 * slot_rows, :]), residual, 1, 0)
        grad_scores = attention * (grad_probs - row_delta)
        grad_keys = dot_narrow(halves(grad_scores), all_queries, 1, 0) * score_scale
        grad_bias = column_sums(grad_scores, width)
        return grad_keys, grad_values, row_as_tail(grad_bias, width)

    def split_merged(joined):
        row_max, row_total, row_delta = (
            joined[width + at : width + at + 1, :] for at in range(3)
        )
        return halves(joined[:width, :]), row_max, row_total, row_delta

    def read_chunks(merged_refs, chunks):
        rank, _, _ = places()
        for turn, ref in zip([0] + turns[::-1], merged_refs):
            chunks[rank ^ turn] = ref[...]
        return [chunks[at] for at in range(ranks)]

    def join_body(*refs):
        *merged_refs, joined_out, chunks = refs
        joined_out[...] = jnp.concatenate(read_chunks(merged_refs, chunks), axis=1)

    def backward_body(*refs):
        weights_refs, refs = refs[: len(weights)], refs[len(weights) :]
        max_refs, refs = refs[: len(weights)], refs[len(weights) :]
        state_refs, refs = parts_of(refs[: len(states)]), refs[len(states) :]
        query_refs, refs = refs[:query_devices], refs[query_devices:]
        merged_refs, refs = refs[: len(all_merged)], refs[len(all_merged) :]
        grad_outs, (squares_out, *scratch) = refs[:2], refs[2:]
        if len(states) < CORES:
            joined = merged_refs[0][...]
            all_queries = read_queries(query_refs)
        else:
            chunks = read_chunks(merged_refs, *scratch)
            joined = jnp.concatenate(
                [
                    value[:, part * piece : (part + 1) * piece]
                    for part in range(query_devices)
                    for value in chunks
                ],
                axis=1,
            )
            all_queries = halves(
                jnp.concatenate([ref[:part_rows, :] for ref in query_refs], axis=0)
            )
        residual, row_max, row_total, row_delta = split_merged(joined)
        maxima = jnp.concatenate([ref[0:1, :] for ref in max_refs], axis=1)
        factor = jnp.exp(maxima - row_max) / row_total
        squares = [jnp.zeros((1, width), jnp.float32)] * 3
        for at, (ref, out) in enumerate(zip(state_refs, grad_outs)):
            rows = slice(at * slot_rows, (at + 1) * slot_rows)
            page_weights = jnp.concatenate([part[rows, :] for part in weights_refs], axis=1)
            grads = page_gradients(page_weights, factor, ref, all_queries, residual, row_delta)
            store_pack(out, grads)
            for which, grad in enumerate(grads):
                squares[which] = squares[which] + jnp.sum(grad * grad, axis=0, keepdims=True)
        lanes = lax.broadcasted_iota(jnp.int32, (1, width), 1)
        row = jnp.zeros((1, width), jnp.float32)
        for which, square in enumerate(squares):
            row = jnp.where(lanes == which, jnp.sum(square, axis=1, keepdims=True), row)
        for at in range(devices):
            squares_out[at] = row

    def page_body(at):
        def body(tile_ref, grad_ref, own_state_ref, *refs):
            state_refs, refs = refs[: query_devices - 1], refs[query_devices - 1 :]
            joined_refs, (*pack_refs, out) = refs[: query_devices - 1], refs[query_devices - 1 :]
            sizes = step_sizes([tile_ref])
            state = read_pack(part_of(own_state_ref, at))
            store_pack(part_of(out, 0), updated(state, read_pack(grad_ref), sizes))
            for turn, (state_ref, joined_ref) in enumerate(zip(state_refs, joined_refs), 1):
                query_refs = [state_ref.at[pl.ds(CORES * packed_rows, query_shape[0])]]
                query_refs += pack_refs[(turn - 1) * (query_devices - 1) :][: query_devices - 1]
                residual, row_max, row_total, row_delta = split_merged(joined_ref[...])
                all_queries = read_queries(query_refs)
                ref = part_of(state_ref, at)
                scores, visible = page_scores(ref, all_queries, read_positions(query_refs))
                weights = jnp.where(visible, jnp.exp(scores - row_max), 0.0)
                grads = page_gradients(
                    weights, 1.0 / row_total, ref, all_queries, residual, row_delta
                )
                store_pack(part_of(out, turn), updated(read_pack(ref), grads, sizes))

        return body

    for repeat in range(STEPS):
        last = repeat == STEPS - 1
        if repeat == 0:
            sums, weights, maxima = [], [], []
            for query_pack in query_parts:
                *pieces, part_weights, part_max = call(
                    part_body,
                    part_shapes,
                    "forward",
                    2 * matmul_cost // query_devices,
                    states + [query_pack],
                    piece_scratch,
                    after=maxima[-1:],
                )
                arrived = {
                    turn: exchange(pieces[turn], page=CORES * turn)
                    for turn in turns
                }
                sums += list(arrived.values()) + pieces[:1]
                weights.append(part_weights)
                maxima.append(part_max)
        else:
            new_state, *chunk_parts, part_weights, part_max = call(
                next_body,
                [(CORES * packed_rows + query_shape[0], width)] + forward_shapes,
                "update_forward",
                2 * matmul_cost,
                states + query_parts + grads + tiles,
                chunk_scratch,
            )
            states, weights, maxima = [new_state], [part_weights], [part_max]
            arrived = {
                turn: exchange(chunk_parts[turn], page=CORES * turn)
                for turn in turns
            }
            sums = chunk_parts[:1] + list(arrived.values())
            new_states = states + [
                exchange(states[0], query=turn) for turn in range(1, query_devices)
            ]
        (merged,) = call(
            merge_body if repeat else first_merge_body,
            [chunk_shape],
            "merge",
            2**20,
            query_parts + sums,
        )
        all_merged = [merged] + [exchange(merged, page=CORES * turn) for turn in reversed(turns)]
        if last:
            all_merged = call(
                join_body, [(width + TAIL, query_rows)], "join", 2**20, all_merged, chunk_scratch
            )
            all_joined = [
                to_device(all_merged[0], query=turn) for turn in range(query_devices)
            ]
        own_grad, mate_grad, squares = call(
            backward_body,
            packed_shapes + [(devices, 1, width)],
            "backward",
            3 * matmul_cost,
            weights + maxima + states + query_parts + list(all_merged),
            scratch=() if last else chunk_scratch,
        )
        grads = [own_grad, mate_grad]
        tiles = [
            lax.all_to_all(
                squares, ("page", "query", "head"), split_axis=0, concat_axis=0, tiled=True
            )
        ]

    other_packs = [
        packs[part] if part == turn else query_part(turn, part)
        for turn in range(1, query_devices)
        for part in range(1, query_devices)
    ]
    operands = new_states + all_joined[1:] + other_packs
    pages = []
    for at, grad in ((1, mate_grad), (0, own_grad)):
        pages += call(
            page_body(at),
            [(query_devices * packed_rows, width)],
            "page_update",
            3 * matmul_cost // 2,
            tiles + [grad] + operands,
            after=pages,
        )
    pages = [pages[1], exchange(pages[0], page=1)]

    def last_body(*refs):
        page_refs, (keys_out, values_out, bias_out) = refs[:CORES], refs[CORES:]
        _, core, me = places()
        for turn, flip in itertools.product(range(query_devices), range(CORES)):
            keys, values, bias = read_pack(part_of(page_refs[flip], turn))
            head = CORES * (me ^ turn) + (core ^ flip)
            keys_out[head] = keys
            values_out[head] = values
            bias_row = jnp.concatenate([bias[row : row + 1] for row in range(bias_rows)], axis=1)
            bias_out[pl.ds(head, 1), :] = bias_row

    return tuple(
        call(
            last_body,
            [compact_keys.shape, compact_values.shape, slot_bias.shape],
            "unpack",
            2**20,
            pages,
        )
    )


def from_partner(value, axis, stride):
    mask = 2**stride
    pairs = [(source, source ^ mask) for source in range(lax.axis_size(axis))]
    return lax.ppermute(value, axis, pairs)


def squared_sums(grad_keys, grad_values, grad_bias):
    return jnp.stack(
        [
            jnp.sum(grad_keys * grad_keys),
            jnp.sum(grad_values * grad_values),
            jnp.sum(grad_bias * grad_bias),
        ]
    )


def apply_update(states, grads, totals, entry_count, slot_total):
    key_state, value_state, bias_state = states
    grad_keys, grad_values, grad_bias = grads
    rms_keys = jnp.sqrt(totals[0] / entry_count + EPSILON)
    rms_values = jnp.sqrt(totals[1] / entry_count + EPSILON)
    rms_bias = jnp.sqrt(totals[2] / slot_total + EPSILON)
    return (
        key_state - RATE_KEYS * grad_keys / rms_keys,
        value_state - RATE_VALUES * grad_values / rms_values,
        bias_state - RATE_BIAS * grad_bias / rms_bias,
    )


def local_gradients(queries, targets, visible, compact_keys, compact_values, slot_bias):
    score_scale = 1.0 / math.sqrt(queries.shape[2])
    scores = jnp.einsum("hqd,hsd->hqs", queries, compact_keys, precision=HIGHEST) * score_scale
    scores = jnp.where(visible, scores + slot_bias[:, None, :], MASKED)
    local_max = jnp.max(scores, axis=2)
    row_max = lax.pmax(local_max, "page")
    weights = jnp.where(visible, jnp.exp(scores - row_max[:, :, None]), 0.0)
    local_sum = jnp.einsum("hqs,hsd->hqd", weights, compact_values, precision=HIGHEST)
    row_total, row_sum = lax.psum((jnp.sum(weights, axis=2), local_sum), "page")
    attention = weights / row_total[:, :, None]
    output = row_sum / row_total[:, :, None]
    residual = output - targets
    grad_values = jnp.einsum("hqs,hqd->hsd", attention, residual, precision=HIGHEST)
    row_delta = jnp.sum(residual * output, axis=2)
    grad_probs = jnp.einsum("hqd,hsd->hqs", residual, compact_values, precision=HIGHEST)
    grad_scores = attention * (grad_probs - row_delta[:, :, None])
    grad_bias = jnp.sum(grad_scores, axis=1)
    grad_keys = jnp.einsum("hqs,hqd->hsd", grad_scores, queries, precision=HIGHEST) * score_scale
    return (grad_keys, grad_values, grad_bias)


def per_device(queries, compact_keys, compact_values, slot_bias, targets, positions, assignment):
    page_number = assignment[lax.axis_index("page")]
    local_heads = compact_keys.shape[0]
    slot_total = local_heads * lax.axis_size("head") * compact_keys.shape[1] * lax.axis_size("page")
    entry_count = slot_total * compact_keys.shape[2]
    query_count = lax.axis_size("query")
    heads_kept = max(local_heads // query_count, 1)
    query_parts = max(query_count // local_heads, 1)
    part_rows = queries.shape[1] // query_parts

    def split_items(array):
        width = array.shape[2]
        array = array.reshape(local_heads // heads_kept, heads_kept, query_parts, part_rows, width)
        array = jnp.transpose(array, (0, 2, 1, 3, 4))
        return array.reshape(query_count, heads_kept, part_rows, width)

    def join_items(array):
        width = array.shape[3]
        array = jnp.transpose(array, (1, 0, 2, 3))
        return array.reshape(heads_kept, query_count * part_rows, width)

    position_column = positions.astype(jnp.float32)[:, :, None]
    got_queries, got_targets, got_positions = (
        lax.all_to_all(split_items(queries), "query", split_axis=0, concat_axis=0, tiled=True),
        lax.all_to_all(split_items(targets), "query", split_axis=0, concat_axis=0, tiled=True),
        lax.all_to_all(
            split_items(position_column), "query", split_axis=0, concat_axis=0, tiled=True
        ),
    )
    group_queries = join_items(got_queries)
    group_targets = join_items(got_targets)
    group_positions = join_items(got_positions)[:, :, 0]
    visible = (page_number.astype(jnp.float32) <= jnp.floor(group_positions / PAGE_LEN))[:, :, None]
    query_index = lax.axis_index("query")
    first_head = query_index // query_parts * heads_kept
    key_state = lax.dynamic_slice_in_dim(compact_keys, first_head, heads_kept, 0)
    value_state = lax.dynamic_slice_in_dim(compact_values, first_head, heads_kept, 0)
    bias_state = lax.dynamic_slice_in_dim(slot_bias, first_head, heads_kept, 0)
    counted = (query_index % query_parts == 0).astype(jnp.float32)
    for repeat in range(STEPS):
        grads = local_gradients(
            group_queries, group_targets, visible, key_state, value_state, bias_state
        )
        for bit in range(query_parts.bit_length() - 1):
            partner = from_partner((grads[0], grads[1], grads[2]), "query", bit)
            grads = (grads[0] + partner[0], grads[1] + partner[1], grads[2] + partner[2])
        totals = lax.psum(
            squared_sums(grads[0], grads[1], grads[2]) * counted, ("page", "query", "head")
        )
        key_state, value_state, bias_state = apply_update(
            (key_state, value_state, bias_state), grads, totals, entry_count, slot_total
        )
    all_keys, all_values, all_bias = (
        lax.all_gather(key_state, "query", axis=0, tiled=True),
        lax.all_gather(value_state, "query", axis=0, tiled=True),
        lax.all_gather(bias_state, "query", axis=0, tiled=True),
    )
    slot_rows = compact_keys.shape[1]
    head_width = compact_keys.shape[2]
    all_keys = all_keys.reshape(
        local_heads // heads_kept, query_parts, heads_kept, slot_rows, head_width
    )[:, 0]
    all_values = all_values.reshape(
        local_heads // heads_kept, query_parts, heads_kept, slot_rows, head_width
    )[:, 0]
    all_bias = all_bias.reshape(local_heads // heads_kept, query_parts, heads_kept, slot_rows)[:, 0]
    return (
        all_keys.reshape(local_heads, slot_rows, head_width),
        all_values.reshape(local_heads, slot_rows, head_width),
        all_bias.reshape(local_heads, slot_rows),
    )


def solution(mesh):
    placed = (
        P("head", "query", None),
        P("head", "page", None),
        P("head", "page", None),
        P("head", "page"),
        P("head", "query", None),
        P("head", "query"),
        P(),
    )

    def program(*args):
        plan = direct_per_device if direct_plan_fits(mesh, args[0], args[1]) else per_device
        return jax.shard_map(
            plan,
            mesh=mesh,
            in_specs=placed,
            out_specs=(P("head", "page", None), P("head", "page", None), P("head", "page")),
            check_vma=False,
        )(*args)

    return program
```

```python
import itertools
import math

import jax
import jax.numpy as jnp
from jax import lax
from jax.experimental import pallas as pl
from jax.experimental.pallas import tpu as pltpu
from jax.sharding import PartitionSpec as P

STEPS = 2
PAGE_LEN = 32768


MASKED = -1e30
EPSILON = 1e-06
RATE_KEYS = 0.05
RATE_VALUES = 0.05
RATE_BIAS = 0.2
HIGHEST = lax.Precision.HIGHEST
TAIL = 8
CORES = 2


def exchange(value, **masks):
    axes = tuple(masks)
    sizes = [lax.axis_size(axis) for axis in axes]

    def flat(place):
        index = 0
        for size, at in zip(sizes, place):
            index = index * size + at
        return index

    pairs = [
        (flat(place), flat([at ^ mask for at, mask in zip(place, masks.values())]))
        for place in itertools.product(*map(range, sizes))
    ]
    return lax.ppermute(value, axes, pairs)


def halves(value):
    high = value.astype(jnp.bfloat16)
    return high, (value - high.astype(jnp.float32)).astype(jnp.bfloat16)


def one_pass(left, right, left_dim, right_dim):
    return lax.dot_general(
        left,
        right,
        (((left_dim,), (right_dim,)), ((), ())),
        preferred_element_type=jnp.float32,
    )


def dot_deep(left, right, left_dim, right_dim):
    left = jnp.concatenate([left[0], left[1], left[0]], axis=left_dim)
    right = jnp.concatenate([right[0], right[0], right[1]], axis=right_dim)
    return one_pass(left, right, left_dim, right_dim)


def dot_narrow(left, right, left_dim, right_dim):
    both = one_pass(
        left[0], jnp.concatenate(right, axis=1 - right_dim), left_dim, right_dim
    )
    count = both.shape[1] // 2
    cross = both[:, count:] + one_pass(left[1], right[0], left_dim, right_dim)
    return both[:, :count] + cross


def dot_low(left, right, left_dim, right_dim):
    both = one_pass(jnp.concatenate(left, axis=1 - left_dim), right[0], left_dim, right_dim)
    count = both.shape[0] // 2
    cross = both[count:, :] + one_pass(left[0], right[1], left_dim, right_dim)
    return both[:count, :] + cross


def call(body, out_shapes, name, cost, operands, scratch=(), after=(), space=pltpu.VMEM, vmem=32):
    spaces = [space] * len(operands) + [pl.ANY] * len(after)
    count = len(operands)

    def without_after(*refs):
        body(*refs[:count], *refs[count + len(after) :])

    return pl.pallas_call(
        without_after,
        out_shape=[jax.ShapeDtypeStruct(shape, jnp.float32) for shape in out_shapes],
        in_specs=[pl.BlockSpec(memory_space=space) for space in spaces],
        out_specs=[pl.BlockSpec(memory_space=pltpu.VMEM) for _ in out_shapes],
        scratch_shapes=scratch,
        compiler_params=pltpu.CompilerParams(vmem_limit_bytes=vmem * 2**20),
        cost_estimate=pl.CostEstimate(flops=cost, bytes_accessed=2**20, transcendentals=0),
        name=name,
    )(*operands, *after)


def row_as_tail(row, width):
    rows = [row[:, at : at + width] for at in range(0, row.shape[1], width)]
    rows.append(jnp.zeros((TAIL - len(rows), width), row.dtype))
    return jnp.concatenate(rows, axis=0)


def tail_as_row(ref, start, count):
    return jnp.concatenate([ref[start + at : start + at + 1, :] for at in range(count)], axis=1)


def row_as_column(row, width):
    parts = []
    for at in range(0, row.shape[1], width):
        parts.append(jnp.broadcast_to(row[:, at : at + width], (width, width)).T)
    return jnp.concatenate(parts, axis=0)


def column_sums(value, width):
    groups = [value[:, at : at + width] for at in range(0, value.shape[1], width)]
    partial = sum(groups[1:], groups[0])
    blocks = [
        jnp.sum(partial[at : at + width, :].T, axis=0, keepdims=True)
        for at in range(0, value.shape[0], width)
    ]
    return jnp.concatenate(blocks, axis=1)


def direct_plan_fits(mesh, queries, compact_keys):
    sizes = [mesh.shape[axis] for axis in ("page", "query", "head")]
    pages, query_devices, head_devices = sizes
    local_heads = queries.shape[0] // head_devices
    part_rows = queries.shape[1] // query_devices
    slot_rows = compact_keys.shape[1] // pages
    width = queries.shape[2]
    if any(size & (size - 1) for size in sizes) or pages < CORES or width % 128:
        return False
    if local_heads != CORES * query_devices or query_devices < 2:
        return False
    ranks = pages // CORES
    chunk = part_rows * query_devices // ranks
    return (
        part_rows * query_devices % ranks == 0
        and chunk % 128 == 0
        and part_rows % (8 * ranks) == 0
        and (part_rows // ranks % 128 == 0 or 1024 % (part_rows // ranks * 8) == 0)
        and slot_rows % width == 0
        and part_rows % width == 0
        and max(slot_rows, part_rows) < TAIL * width
    )


def direct_per_device(
    queries, compact_keys, compact_values, slot_bias, targets, positions, assignment
):
    local_heads, part_rows, width = queries.shape
    slot_rows = compact_keys.shape[1]
    query_devices = lax.axis_size("query")
    head_devices = lax.axis_size("head")
    ranks = lax.axis_size("page") // CORES
    query_rows = part_rows * query_devices
    chunk, piece = query_rows // ranks, part_rows // ranks
    turns = [ranks // 2] + [turn for turn in reversed(range(1, ranks)) if turn != ranks // 2]
    slot_total = local_heads * head_devices * slot_rows * lax.axis_size("page")
    entry_total = slot_total * width
    score_scale = 1.0 / math.sqrt(width)
    slots = CORES * slot_rows
    devices = ranks * CORES * query_devices * head_devices
    pos_rows = part_rows // width
    bias_rows = slot_rows // width
    packed_rows = 2 * slot_rows + TAIL
    packed_shapes = [(packed_rows, width)] * 2
    matmul_cost = 3 * 2 * slots * query_rows * width

    def places():
        page = lax.axis_index("page")
        return page // CORES, page % CORES, lax.axis_index("query")

    def to_device(value, **masks):
        masks = {axis: mask for axis, mask in masks.items() if mask}
        return exchange(value, **masks) if masks else value

    def pack_queries(head, rank, queries, targets, out):
        rows = pl.ds(pl.multiple_of(rank * piece, piece), piece)
        return [
            (queries.at[head], out.at[pl.ds(0, part_rows)]),
            (targets.at[head, rows], out.at[pl.ds(part_rows, piece)]),
        ]

    def pack_state(head, keys, values, out):
        return [
            (keys.at[head], out.at[pl.ds(0, slot_rows)]),
            (values.at[head], out.at[pl.ds(slot_rows, slot_rows)]),
        ]

    def start_all(copies, sems, first=0):
        copies = [
            pltpu.make_async_copy(source, target, sems.at[first + at])
            for at, (source, target) in enumerate(copies)
        ]
        for copy in copies:
            copy.start()
        return copies

    def position_tail(head, positions_ref):
        return row_as_tail(positions_ref[pl.ds(head, 1), :].astype(jnp.float32), width)

    def state_tail(head, page, bias_ref, assignment_ref):
        page_start = (assignment_ref[page] * PAGE_LEN).astype(jnp.float32)
        tail = row_as_tail(bias_ref[pl.ds(head, 1), :], width)
        return jnp.concatenate(
            [tail[: TAIL - 1], jnp.full((1, width), page_start, jnp.float32)], axis=0
        )

    def send_body(
        queries, keys, values, biases, targets, positions, assignment, state_out, *refs
    ):
        query_outs = refs[: query_devices - 1]
        bias_ref, positions_ref, assignment_ref, sems = refs[query_devices - 1 :]
        rank, core, me = places()
        heads = [CORES * (me ^ turn) + core for turn in range(1, query_devices)]
        mate_head = CORES * me + (core ^ 1)
        small = start_all(
            [(assignment, assignment_ref), (positions, positions_ref), (biases, bias_ref)], sems
        )
        copies = pack_state(mate_head, keys, values, state_out)
        for head, out in zip(heads, query_outs):
            copies += pack_queries(head, rank, queries, targets, out)
        copies = start_all(copies, sems, 3)
        for copy in small:
            copy.wait()
        state_out[2 * slot_rows :, :] = state_tail(
            mate_head, CORES * rank + core, bias_ref, assignment_ref
        )
        for head, out in zip(heads, query_outs):
            out[part_rows + piece :, :] = position_tail(head, positions_ref)
        for copy in copies:
            copy.wait()

    def own_body(
        queries, keys, values, biases, targets, positions, assignment, state_out, query_out, *refs
    ):
        bias_ref, positions_ref, assignment_ref, sems = refs
        rank, core, me = places()
        head = CORES * me + core
        small = start_all(
            [(assignment, assignment_ref), (positions, positions_ref), (biases, bias_ref)], sems
        )
        copies = pack_state(head, keys, values, state_out)
        copies += pack_queries(head, rank, queries, targets, query_out)
        copies = start_all(copies, sems, 3)
        for copy in small:
            copy.wait()
        state_out[2 * slot_rows :, :] = state_tail(
            head, CORES * rank + core, bias_ref, assignment_ref
        )
        query_out[part_rows + piece :, :] = position_tail(head, positions_ref)
        for copy in copies:
            copy.wait()

    state_shape, query_shape = (packed_rows, width), (part_rows + piece + TAIL, width)
    small_scratch = [
        pltpu.VMEM(slot_bias.shape, jnp.float32),
        pltpu.VMEM(positions.shape, jnp.int32),
        pltpu.SMEM(assignment.shape, jnp.int32),
    ]
    arguments = [
        queries, compact_keys, compact_values, slot_bias, targets, positions, assignment
    ]
    mate_state, *sent_queries = call(
        send_body,
        [state_shape] + [query_shape] * (query_devices - 1),
        "pack",
        2**20,
        arguments,
        small_scratch + [pltpu.SemaphoreType.DMA((3 + 2 * query_devices,))],
        space=pl.ANY,
        vmem=60,
    )
    own_state, own_queries = call(
        own_body,
        [state_shape, query_shape],
        "own",
        2**24,
        arguments,
        small_scratch + [pltpu.SemaphoreType.DMA((7,))],
        space=pl.ANY,
    )
    packs = [own_queries] + list(sent_queries)

    def query_part(turn, part):
        return to_device(packs[part], query=turn ^ part)

    query_parts = [query_part(0, part) for part in range(query_devices)]
    states = [own_state, exchange(mate_state, page=1)]

    def in_columns(parts, axis):
        return jnp.concatenate(
            [
                lax.slice_in_dim(part, at * piece, (at + 1) * piece, axis=axis)
                for at in range(ranks)
                for part in parts
            ],
            axis=axis,
        )

    def read_queries(query_refs):
        return halves(in_columns([ref[:part_rows, :] for ref in query_refs], 0))

    def part_of(ref, at):
        return ref.at[pl.ds(at * packed_rows, packed_rows)]

    def parts_of(refs):
        return refs if len(refs) == CORES else [part_of(refs[0], at) for at in range(CORES)]

    def step_sizes(tile_refs):
        row = jnp.sum(tile_refs[0][...], axis=0)
        return (
            RATE_KEYS / jnp.sqrt(row[:, 0:1] / entry_total + EPSILON),
            RATE_VALUES / jnp.sqrt(row[:, 1:2] / entry_total + EPSILON),
            RATE_BIAS / jnp.sqrt(row[:, 2:3] / slot_total + EPSILON),
        )

    def read_pack(ref):
        return ref[:slot_rows, :], ref[slot_rows : 2 * slot_rows, :], ref[2 * slot_rows :, :]

    def store_pack(ref, values):
        ref[:slot_rows, :] = values[0]
        ref[slot_rows : 2 * slot_rows, :] = values[1]
        ref[2 * slot_rows :, :] = values[2]

    def updated(state, grads, sizes):
        return [value - size * grad for value, grad, size in zip(state, grads, sizes)]

    def page_scores(ref, queries, positions):
        scores = dot_deep(halves(ref[:slot_rows, :]), queries, 1, 1) * score_scale
        bias = row_as_column(tail_as_row(ref, 2 * slot_rows, bias_rows), width)
        scores = scores + jnp.concatenate([bias] * (positions.shape[1] // width), axis=1)
        page_start = ref[packed_rows - 1 : packed_rows, 0:1]
        visible = jnp.broadcast_to(positions >= page_start, scores.shape)
        return jnp.where(visible, scores, MASKED), visible

    def read_positions(query_refs):
        return in_columns(
            [tail_as_row(ref, part_rows + piece, pos_rows) for ref in query_refs], 1
        )

    def forward(state_refs, query_refs, chunk_outs, weights_out, max_out, chunks):
        rank, _, _ = places()
        all_queries, positions = read_queries(query_refs), read_positions(query_refs)
        all_scores, all_visible = [], []
        for at, ref in enumerate(state_refs):
            scores, visible = page_scores(ref, all_queries, positions)
            all_scores.append(scores)
            all_visible.append(visible)
        row_max = jnp.max(all_scores[0], axis=0, keepdims=True)
        for scores in all_scores[1:]:
            row_max = jnp.maximum(row_max, jnp.max(scores, axis=0, keepdims=True))
        row_total = jnp.zeros_like(row_max)
        row_sum = jnp.zeros((width, query_rows), jnp.float32)
        for at, ref in enumerate(state_refs):
            weights = jnp.where(all_visible[at], jnp.exp(all_scores[at] - row_max), 0.0)
            weights_out[at * slot_rows : (at + 1) * slot_rows, :] = weights
            row_total = row_total + jnp.sum(weights, axis=0, keepdims=True)
            values = halves(ref[slot_rows : 2 * slot_rows, :])
            row_sum = row_sum + dot_low(values, halves(weights), 0, 0)
        max_out[...] = jnp.broadcast_to(row_max, (TAIL, query_rows))
        tail = jnp.concatenate(
            [row_max, row_total, jnp.zeros((TAIL - 2, query_rows), jnp.float32)], axis=0
        )
        for at in range(ranks):
            columns = slice(at * chunk, (at + 1) * chunk)
            chunks[at, :width, :] = row_sum[:, columns]
            chunks[at, width:, :] = tail[:, columns]
        for turn in range(ranks):
            chunk_outs[turn][...] = chunks[rank ^ turn]

    chunk_shape = (width + TAIL, chunk)
    forward_shapes = [chunk_shape] * ranks + [(slots, query_rows), (TAIL, query_rows)]
    chunk_scratch = [pltpu.VMEM((ranks,) + chunk_shape, jnp.float32)]

    fold = max(1, 128 // piece)
    folded, columns = width // fold, fold * piece
    piece_shape = (folded + TAIL, columns)
    piece_scratch = [pltpu.VMEM((ranks,) + piece_shape, jnp.float32)]

    def fold_rows(value):
        groups = [value[at * folded : (at + 1) * folded, :] for at in range(fold)]
        return jnp.concatenate(groups, axis=1)

    def unfold_rows(value):
        groups = [value[:, at * piece : (at + 1) * piece] for at in range(fold)]
        return jnp.concatenate(groups, axis=0)

    def rows_tail(rows):
        empty = jnp.zeros((TAIL - len(rows), columns), jnp.float32)
        return jnp.concatenate(rows + [empty], axis=0)

    def part_body(*refs):
        state_refs, (query_ref, *refs) = refs[:CORES], refs[CORES:]
        piece_outs, (weights_out, max_out, pieces) = refs[:ranks], refs[ranks:]
        rank, _, _ = places()
        queries = halves(query_ref[:part_rows, :])
        position_row = tail_as_row(query_ref, part_rows + piece, pos_rows)
        all_scores, all_visible = [], []
        for ref in state_refs:
            scores, visible = page_scores(ref, queries, position_row)
            all_scores.append(scores)
            all_visible.append(visible)
        row_max = jnp.max(all_scores[0], axis=0, keepdims=True)
        for scores in all_scores[1:]:
            row_max = jnp.maximum(row_max, jnp.max(scores, axis=0, keepdims=True))
        row_total = jnp.zeros_like(row_max)
        row_sum = jnp.zeros((width, part_rows), jnp.float32)
        for at, ref in enumerate(state_refs):
            weights = jnp.where(all_visible[at], jnp.exp(all_scores[at] - row_max), 0.0)
            weights_out[at * slot_rows : (at + 1) * slot_rows, :] = weights
            row_total = row_total + jnp.sum(weights, axis=0, keepdims=True)
            values = halves(ref[slot_rows : 2 * slot_rows, :])
            row_sum = row_sum + dot_low(values, halves(weights), 0, 0)
        max_out[...] = jnp.broadcast_to(row_max, (TAIL, part_rows))
        for at in range(ranks):
            own = slice(at * piece, (at + 1) * piece)
            pieces[at, :folded, :] = fold_rows(row_sum[:, own])
            pieces[at, folded:, :] = rows_tail(
                [jnp.concatenate([row[:, own]] * fold, axis=1) for row in (row_max, row_total)]
            )
        for turn in range(ranks):
            piece_outs[turn][...] = pieces[rank ^ turn]

    part_shapes = [piece_shape] * ranks + [(slots, part_rows), (TAIL, part_rows)]

    def next_body(*refs):
        state_refs, refs = refs[:2], refs[2:]
        query_refs, refs = refs[:query_devices], refs[query_devices:]
        grad_refs, refs = refs[:2], refs[2:]
        tile_refs, refs = refs[: len(tiles)], refs[len(tiles) :]
        refs[0][CORES * packed_rows :, :] = query_refs[0][...]
        state_outs, refs = parts_of(refs[:1]), refs[1:]
        chunk_outs, refs = refs[:ranks], refs[ranks:]
        sizes = step_sizes(tile_refs)
        for at in range(2):
            state = read_pack(state_refs[at])
            store_pack(state_outs[at], updated(state, read_pack(grad_refs[at]), sizes))
        forward(state_outs, query_refs, chunk_outs, *refs)

    def merged_chunk(query_refs, sums, maxima, totals, out):
        targets = jnp.concatenate(
            [ref[part_rows : part_rows + piece, :] for ref in query_refs], axis=0
        )
        row_max = maxima[0]
        for other in maxima[1:]:
            row_max = jnp.maximum(row_max, other)
        row_total = jnp.zeros_like(row_max)
        row_sum = jnp.zeros((width, chunk), jnp.float32)
        for part_sum, part_max, part_total in zip(sums, maxima, totals):
            factor = jnp.exp(part_max - row_max)
            row_total = row_total + part_total * factor
            row_sum = row_sum + part_sum * factor
        output = row_sum / row_total
        residual = output - targets.T
        row_delta = jnp.sum(residual * output, axis=0, keepdims=True)
        out[:width, :] = residual
        out[width:, :] = jnp.concatenate(
            [row_max, row_total, row_delta, jnp.zeros((TAIL - 3, chunk), jnp.float32)], axis=0
        )

    def first_merge_body(*refs):
        query_refs, (*piece_refs, merged_out) = refs[:query_devices], refs[query_devices:]

        def joined(read):
            return [
                jnp.concatenate([read(ref) for ref in piece_refs[turn::ranks]], axis=1)
                for turn in range(ranks)
            ]

        merged_chunk(
            query_refs,
            joined(lambda ref: unfold_rows(ref[:folded, :])),
            joined(lambda ref: ref[folded : folded + 1, :piece]),
            joined(lambda ref: ref[folded + 1 : folded + 2, :piece]),
            merged_out,
        )

    def merge_body(*refs):
        query_refs, (*chunk_refs, merged_out) = refs[:query_devices], refs[query_devices:]
        merged_chunk(
            query_refs,
            [ref[:width, :] for ref in chunk_refs],
            [ref[width : width + 1, :] for ref in chunk_refs],
            [ref[width + 1 : width + 2, :] for ref in chunk_refs],
            merged_out,
        )

    def page_gradients(weights, factor, state_ref, all_queries, residual, row_delta):
        attention = weights * factor
        grad_values = dot_narrow(halves(attention), residual, 1, 1)
        grad_probs = dot_deep(halves(state_ref[slot_rows : 2 * slot_rows, :]), residual, 1, 0)
        grad_scores = attention * (grad_probs - row_delta)
        grad_keys = dot_narrow(halves(grad_scores), all_queries, 1, 0) * score_scale
        grad_bias = column_sums(grad_scores, width)
        return grad_keys, grad_values, row_as_tail(grad_bias, width)

    def split_merged(joined):
        row_max, row_total, row_delta = (
            joined[width + at : width + at + 1, :] for at in range(3)
        )
        return halves(joined[:width, :]), row_max, row_total, row_delta

    def read_chunks(merged_refs, chunks):
        rank, _, _ = places()
        for turn, ref in zip([0] + turns[::-1], merged_refs):
            chunks[rank ^ turn] = ref[...]
        return [chunks[at] for at in range(ranks)]

    def join_body(*refs):
        *merged_refs, joined_out, chunks = refs
        joined_out[...] = jnp.concatenate(read_chunks(merged_refs, chunks), axis=1)

    def backward_body(*refs):
        weights_refs, refs = refs[: len(weights)], refs[len(weights) :]
        max_refs, refs = refs[: len(weights)], refs[len(weights) :]
        state_refs, refs = parts_of(refs[: len(states)]), refs[len(states) :]
        query_refs, refs = refs[:query_devices], refs[query_devices:]
        merged_refs, refs = refs[: len(all_merged)], refs[len(all_merged) :]
        grad_outs, (squares_out, *scratch) = refs[:2], refs[2:]
        if len(states) < CORES:
            joined = merged_refs[0][...]
            all_queries = read_queries(query_refs)
        else:
            chunks = read_chunks(merged_refs, *scratch)
            joined = jnp.concatenate(
                [
                    value[:, part * piece : (part + 1) * piece]
                    for part in range(query_devices)
                    for value in chunks
                ],
                axis=1,
            )
            all_queries = halves(
                jnp.concatenate([ref[:part_rows, :] for ref in query_refs], axis=0)
            )
        residual, row_max, row_total, row_delta = split_merged(joined)
        maxima = jnp.concatenate([ref[0:1, :] for ref in max_refs], axis=1)
        factor = jnp.exp(maxima - row_max) / row_total
        squares = [jnp.zeros((1, width), jnp.float32)] * 3
        for at, (ref, out) in enumerate(zip(state_refs, grad_outs)):
            rows = slice(at * slot_rows, (at + 1) * slot_rows)
            page_weights = jnp.concatenate([part[rows, :] for part in weights_refs], axis=1)
            grads = page_gradients(page_weights, factor, ref, all_queries, residual, row_delta)
            store_pack(out, grads)
            for which, grad in enumerate(grads):
                squares[which] = squares[which] + jnp.sum(grad * grad, axis=0, keepdims=True)
        lanes = lax.broadcasted_iota(jnp.int32, (1, width), 1)
        row = jnp.zeros((1, width), jnp.float32)
        for which, square in enumerate(squares):
            row = jnp.where(lanes == which, jnp.sum(square, axis=1, keepdims=True), row)
        for at in range(devices):
            squares_out[at] = row

    def own_update(tile_ref, state_ref, grad_ref, at):
        state = read_pack(part_of(state_ref, at))
        return updated(state, read_pack(grad_ref), step_sizes([tile_ref]))

    def own_page_body(tile_ref, state_ref, grad_ref, out):
        store_pack(out, own_update(tile_ref, state_ref, grad_ref, 1))

    def other_page_body(at):
        def body(tile_ref, *refs):
            state_refs, refs = refs[: query_devices - 1], refs[query_devices - 1 :]
            joined_refs, (*pack_refs, out) = refs[: query_devices - 1], refs[query_devices - 1 :]
            sizes = step_sizes([tile_ref])
            for other, (state_ref, joined_ref) in enumerate(zip(state_refs, joined_refs)):
                query_refs = [state_ref.at[pl.ds(CORES * packed_rows, query_shape[0])]]
                query_refs += pack_refs[other * (query_devices - 1) :][: query_devices - 1]
                residual, row_max, row_total, row_delta = split_merged(joined_ref[...])
                all_queries = read_queries(query_refs)
                ref = part_of(state_ref, at)
                scores, visible = page_scores(ref, all_queries, read_positions(query_refs))
                weights = jnp.where(visible, jnp.exp(scores - row_max), 0.0)
                grads = page_gradients(
                    weights, 1.0 / row_total, ref, all_queries, residual, row_delta
                )
                store_pack(part_of(out, other), updated(read_pack(ref), grads, sizes))

        return body

    for repeat in range(STEPS):
        last = repeat == STEPS - 1
        if repeat == 0:
            sums, weights, maxima = [], [], []
            for query_pack in query_parts:
                *pieces, part_weights, part_max = call(
                    part_body,
                    part_shapes,
                    "forward",
                    2 * matmul_cost // query_devices,
                    states + [query_pack],
                    piece_scratch,
                    after=maxima[-1:],
                )
                arrived = {
                    turn: exchange(pieces[turn], page=CORES * turn)
                    for turn in turns
                }
                sums += list(arrived.values()) + pieces[:1]
                weights.append(part_weights)
                maxima.append(part_max)
        else:
            new_state, *chunk_parts, part_weights, part_max = call(
                next_body,
                [(CORES * packed_rows + query_shape[0], width)] + forward_shapes,
                "update_forward",
                2 * matmul_cost,
                states + query_parts + grads + tiles,
                chunk_scratch,
            )
            states, weights, maxima = [new_state], [part_weights], [part_max]
            arrived = {
                turn: exchange(chunk_parts[turn], page=CORES * turn)
                for turn in turns
            }
            sums = chunk_parts[:1] + list(arrived.values())
            new_states = states + [
                exchange(states[0], query=turn) for turn in range(1, query_devices)
            ]
        (merged,) = call(
            merge_body if repeat else first_merge_body,
            [chunk_shape],
            "merge",
            2**20,
            query_parts + sums,
        )
        all_merged = [merged] + [exchange(merged, page=CORES * turn) for turn in reversed(turns)]
        if last:
            all_merged = call(
                join_body, [(width + TAIL, query_rows)], "join", 2**20, all_merged, chunk_scratch
            )
            all_joined = [
                to_device(all_merged[0], query=turn) for turn in range(query_devices)
            ]
        own_grad, mate_grad, squares = call(
            backward_body,
            packed_shapes + [(devices, 1, width)],
            "backward",
            3 * matmul_cost,
            weights + maxima + states + query_parts + list(all_merged),
            scratch=() if last else chunk_scratch,
        )
        grads = [own_grad, mate_grad]
        tiles = [
            lax.all_to_all(
                squares, ("page", "query", "head"), split_axis=0, concat_axis=0, tiled=True
            )
        ]

    other_packs = [
        packs[part] if part == turn else query_part(turn, part)
        for turn in range(1, query_devices)
        for part in range(1, query_devices)
    ]
    (own_for_mate,) = call(
        own_page_body, packed_shapes[:1], "own_update", 2**20, tiles + states + [mate_grad]
    )
    before, others = [own_for_mate], []
    for at in reversed(range(CORES)):
        others += call(
            other_page_body(at),
            [((query_devices - 1) * packed_rows, width)],
            "other_update",
            3 * matmul_cost // 2,
            tiles + new_states[1:] + all_joined[1:] + other_packs,
            after=before,
        )
        before = others[-1:]
    others_for_mate, own_page_others = others
    from_mate = [exchange(own_for_mate, page=1), exchange(others_for_mate, page=1)]

    def last_body(tile_ref, state_ref, grad_ref, *refs):
        others_ref, mate_ref, mate_others_ref, keys_out, values_out, bias_out = refs
        _, core, me = places()
        for turn, flip in itertools.product(range(query_devices), range(CORES)):
            if turn:
                values = read_pack(part_of(mate_others_ref if flip else others_ref, turn - 1))
            elif flip:
                values = read_pack(mate_ref)
            else:
                values = own_update(tile_ref, state_ref, grad_ref, 0)
            head = CORES * (me ^ turn) + (core ^ flip)
            keys_out[head] = values[0]
            values_out[head] = values[1]
            bias_row = [values[2][row : row + 1] for row in range(bias_rows)]
            bias_out[pl.ds(head, 1), :] = jnp.concatenate(bias_row, axis=1)

    return tuple(
        call(
            last_body,
            [compact_keys.shape, compact_values.shape, slot_bias.shape],
            "unpack",
            2**20,
            tiles + states + [own_grad, own_page_others] + from_mate,
        )
    )


def from_partner(value, axis, stride):
    mask = 2**stride
    pairs = [(source, source ^ mask) for source in range(lax.axis_size(axis))]
    return lax.ppermute(value, axis, pairs)


def squared_sums(grad_keys, grad_values, grad_bias):
    return jnp.stack(
        [
            jnp.sum(grad_keys * grad_keys),
            jnp.sum(grad_values * grad_values),
            jnp.sum(grad_bias * grad_bias),
        ]
    )


def apply_update(states, grads, totals, entry_count, slot_total):
    key_state, value_state, bias_state = states
    grad_keys, grad_values, grad_bias = grads
    rms_keys = jnp.sqrt(totals[0] / entry_count + EPSILON)
    rms_values = jnp.sqrt(totals[1] / entry_count + EPSILON)
    rms_bias = jnp.sqrt(totals[2] / slot_total + EPSILON)
    return (
        key_state - RATE_KEYS * grad_keys / rms_keys,
        value_state - RATE_VALUES * grad_values / rms_values,
        bias_state - RATE_BIAS * grad_bias / rms_bias,
    )


def local_gradients(queries, targets, visible, compact_keys, compact_values, slot_bias):
    score_scale = 1.0 / math.sqrt(queries.shape[2])
    scores = jnp.einsum("hqd,hsd->hqs", queries, compact_keys, precision=HIGHEST) * score_scale
    scores = jnp.where(visible, scores + slot_bias[:, None, :], MASKED)
    local_max = jnp.max(scores, axis=2)
    row_max = lax.pmax(local_max, "page")
    weights = jnp.where(visible, jnp.exp(scores - row_max[:, :, None]), 0.0)
    local_sum = jnp.einsum("hqs,hsd->hqd", weights, compact_values, precision=HIGHEST)
    row_total, row_sum = lax.psum((jnp.sum(weights, axis=2), local_sum), "page")
    attention = weights / row_total[:, :, None]
    output = row_sum / row_total[:, :, None]
    residual = output - targets
    grad_values = jnp.einsum("hqs,hqd->hsd", attention, residual, precision=HIGHEST)
    row_delta = jnp.sum(residual * output, axis=2)
    grad_probs = jnp.einsum("hqd,hsd->hqs", residual, compact_values, precision=HIGHEST)
    grad_scores = attention * (grad_probs - row_delta[:, :, None])
    grad_bias = jnp.sum(grad_scores, axis=1)
    grad_keys = jnp.einsum("hqs,hqd->hsd", grad_scores, queries, precision=HIGHEST) * score_scale
    return (grad_keys, grad_values, grad_bias)


def per_device(queries, compact_keys, compact_values, slot_bias, targets, positions, assignment):
    page_number = assignment[lax.axis_index("page")]
    local_heads = compact_keys.shape[0]
    slot_total = local_heads * lax.axis_size("head") * compact_keys.shape[1] * lax.axis_size("page")
    entry_count = slot_total * compact_keys.shape[2]
    query_count = lax.axis_size("query")
    heads_kept = max(local_heads // query_count, 1)
    query_parts = max(query_count // local_heads, 1)
    part_rows = queries.shape[1] // query_parts

    def split_items(array):
        width = array.shape[2]
        array = array.reshape(local_heads // heads_kept, heads_kept, query_parts, part_rows, width)
        array = jnp.transpose(array, (0, 2, 1, 3, 4))
        return array.reshape(query_count, heads_kept, part_rows, width)

    def join_items(array):
        width = array.shape[3]
        array = jnp.transpose(array, (1, 0, 2, 3))
        return array.reshape(heads_kept, query_count * part_rows, width)

    position_column = positions.astype(jnp.float32)[:, :, None]
    got_queries, got_targets, got_positions = (
        lax.all_to_all(split_items(queries), "query", split_axis=0, concat_axis=0, tiled=True),
        lax.all_to_all(split_items(targets), "query", split_axis=0, concat_axis=0, tiled=True),
        lax.all_to_all(
            split_items(position_column), "query", split_axis=0, concat_axis=0, tiled=True
        ),
    )
    group_queries = join_items(got_queries)
    group_targets = join_items(got_targets)
    group_positions = join_items(got_positions)[:, :, 0]
    visible = (page_number.astype(jnp.float32) <= jnp.floor(group_positions / PAGE_LEN))[:, :, None]
    query_index = lax.axis_index("query")
    first_head = query_index // query_parts * heads_kept
    key_state = lax.dynamic_slice_in_dim(compact_keys, first_head, heads_kept, 0)
    value_state = lax.dynamic_slice_in_dim(compact_values, first_head, heads_kept, 0)
    bias_state = lax.dynamic_slice_in_dim(slot_bias, first_head, heads_kept, 0)
    counted = (query_index % query_parts == 0).astype(jnp.float32)
    for repeat in range(STEPS):
        grads = local_gradients(
            group_queries, group_targets, visible, key_state, value_state, bias_state
        )
        for bit in range(query_parts.bit_length() - 1):
            partner = from_partner((grads[0], grads[1], grads[2]), "query", bit)
            grads = (grads[0] + partner[0], grads[1] + partner[1], grads[2] + partner[2])
        totals = lax.psum(
            squared_sums(grads[0], grads[1], grads[2]) * counted, ("page", "query", "head")
        )
        key_state, value_state, bias_state = apply_update(
            (key_state, value_state, bias_state), grads, totals, entry_count, slot_total
        )
    all_keys, all_values, all_bias = (
        lax.all_gather(key_state, "query", axis=0, tiled=True),
        lax.all_gather(value_state, "query", axis=0, tiled=True),
        lax.all_gather(bias_state, "query", axis=0, tiled=True),
    )
    slot_rows = compact_keys.shape[1]
    head_width = compact_keys.shape[2]
    all_keys = all_keys.reshape(
        local_heads // heads_kept, query_parts, heads_kept, slot_rows, head_width
    )[:, 0]
    all_values = all_values.reshape(
        local_heads // heads_kept, query_parts, heads_kept, slot_rows, head_width
    )[:, 0]
    all_bias = all_bias.reshape(local_heads // heads_kept, query_parts, heads_kept, slot_rows)[:, 0]
    return (
        all_keys.reshape(local_heads, slot_rows, head_width),
        all_values.reshape(local_heads, slot_rows, head_width),
        all_bias.reshape(local_heads, slot_rows),
    )


def solution(mesh):
    placed = (
        P("head", "query", None),
        P("head", "page", None),
        P("head", "page", None),
        P("head", "page"),
        P("head", "query", None),
        P("head", "query"),
        P(),
    )

    def program(*args):
        plan = direct_per_device if direct_plan_fits(mesh, args[0], args[1]) else per_device
        return jax.shard_map(
            plan,
            mesh=mesh,
            in_specs=placed,
            out_specs=(P("head", "page", None), P("head", "page", None), P("head", "page")),
            check_vma=False,
        )(*args)

    return program
```

```python
import itertools
import math

import jax
import jax.numpy as jnp
from jax import lax
from jax.experimental import pallas as pl
from jax.experimental.pallas import tpu as pltpu
from jax.sharding import PartitionSpec as P

STEPS = 2
PAGE_LEN = 32768


MASKED = -1e30
EPSILON = 1e-06
RATE_KEYS = 0.05
RATE_VALUES = 0.05
RATE_BIAS = 0.2
HIGHEST = lax.Precision.HIGHEST
TAIL = 8
CORES = 2


def exchange(value, **masks):
    axes = tuple(masks)
    sizes = [lax.axis_size(axis) for axis in axes]

    def flat(place):
        index = 0
        for size, at in zip(sizes, place):
            index = index * size + at
        return index

    pairs = [
        (flat(place), flat([at ^ mask for at, mask in zip(place, masks.values())]))
        for place in itertools.product(*map(range, sizes))
    ]
    return lax.ppermute(value, axes, pairs)


def halves(value):
    high = value.astype(jnp.bfloat16)
    return high, (value - high.astype(jnp.float32)).astype(jnp.bfloat16)


def one_pass(left, right, left_dim, right_dim):
    return lax.dot_general(
        left,
        right,
        (((left_dim,), (right_dim,)), ((), ())),
        preferred_element_type=jnp.float32,
    )


def dot_deep(left, right, left_dim, right_dim):
    left = jnp.concatenate([left[0], left[1], left[0]], axis=left_dim)
    right = jnp.concatenate([right[0], right[0], right[1]], axis=right_dim)
    return one_pass(left, right, left_dim, right_dim)


def dot_narrow(left, right, left_dim, right_dim):
    both = one_pass(
        left[0], jnp.concatenate(right, axis=1 - right_dim), left_dim, right_dim
    )
    count = both.shape[1] // 2
    cross = both[:, count:] + one_pass(left[1], right[0], left_dim, right_dim)
    return both[:, :count] + cross


def dot_low(left, right, left_dim, right_dim):
    both = one_pass(jnp.concatenate(left, axis=1 - left_dim), right[0], left_dim, right_dim)
    count = both.shape[0] // 2
    cross = both[count:, :] + one_pass(left[0], right[1], left_dim, right_dim)
    return both[:count, :] + cross


def call(body, out_shapes, name, cost, operands, scratch=(), after=(), space=pltpu.VMEM,
         spaces=None, out_spaces=None, aliases=None, vmem=32):
    spaces = (spaces or [space] * len(operands)) + [pl.ANY] * len(after)
    out_spaces = out_spaces or [pltpu.VMEM] * len(out_shapes)
    count = len(operands)

    def without_after(*refs):
        body(*refs[:count], *refs[count + len(after) :])

    return pl.pallas_call(
        without_after,
        out_shape=[jax.ShapeDtypeStruct(shape, jnp.float32) for shape in out_shapes],
        in_specs=[pl.BlockSpec(memory_space=space) for space in spaces],
        out_specs=[pl.BlockSpec(memory_space=out_space) for out_space in out_spaces],
        input_output_aliases=aliases or {},
        scratch_shapes=scratch,
        compiler_params=pltpu.CompilerParams(vmem_limit_bytes=vmem * 2**20),
        cost_estimate=pl.CostEstimate(flops=cost, bytes_accessed=2**20, transcendentals=0),
        name=name,
    )(*operands, *after)


def row_as_tail(row, width):
    rows = [row[:, at : at + width] for at in range(0, row.shape[1], width)]
    rows.append(jnp.zeros((TAIL - len(rows), width), row.dtype))
    return jnp.concatenate(rows, axis=0)


def tail_as_row(ref, start, count):
    return jnp.concatenate([ref[start + at : start + at + 1, :] for at in range(count)], axis=1)


def row_as_column(row, width):
    parts = []
    for at in range(0, row.shape[1], width):
        parts.append(jnp.broadcast_to(row[:, at : at + width], (width, width)).T)
    return jnp.concatenate(parts, axis=0)


def column_sums(value, width):
    groups = [value[:, at : at + width] for at in range(0, value.shape[1], width)]
    partial = sum(groups[1:], groups[0])
    blocks = [
        jnp.sum(partial[at : at + width, :].T, axis=0, keepdims=True)
        for at in range(0, value.shape[0], width)
    ]
    return jnp.concatenate(blocks, axis=1)


def direct_plan_fits(mesh, queries, compact_keys):
    sizes = [mesh.shape[axis] for axis in ("page", "query", "head")]
    pages, query_devices, head_devices = sizes
    local_heads = queries.shape[0] // head_devices
    part_rows = queries.shape[1] // query_devices
    slot_rows = compact_keys.shape[1] // pages
    width = queries.shape[2]
    if any(size & (size - 1) for size in sizes) or pages < CORES or width % 128:
        return False
    if local_heads != CORES * query_devices:
        return False
    ranks = pages // CORES
    chunk = part_rows * query_devices // ranks
    return (
        part_rows * query_devices % ranks == 0
        and chunk % 128 == 0
        and part_rows % (8 * ranks) == 0
        and (part_rows // ranks % 128 == 0 or 1024 % (part_rows // ranks * 8) == 0)
        and slot_rows % width == 0
        and part_rows % width == 0
        and max(slot_rows, part_rows) < TAIL * width
    )


def direct_per_device(
    queries, compact_keys, compact_values, slot_bias, targets, positions, assignment
):
    local_heads, part_rows, width = queries.shape
    slot_rows = compact_keys.shape[1]
    query_devices = lax.axis_size("query")
    head_devices = lax.axis_size("head")
    ranks = lax.axis_size("page") // CORES
    query_rows = part_rows * query_devices
    chunk, piece = query_rows // ranks, part_rows // ranks
    turns = [ranks // 2] + [turn for turn in reversed(range(1, ranks)) if turn != ranks // 2]
    slot_total = local_heads * head_devices * slot_rows * lax.axis_size("page")
    entry_total = slot_total * width
    score_scale = 1.0 / math.sqrt(width)
    slots = CORES * slot_rows
    devices = ranks * CORES * query_devices * head_devices
    pos_rows = part_rows // width
    bias_rows = slot_rows // width
    packed_rows = 2 * slot_rows + TAIL
    packed_shapes = [(packed_rows, width)] * 2
    matmul_cost = 3 * 2 * slots * query_rows * width

    def places():
        page = lax.axis_index("page")
        return page // CORES, page % CORES, lax.axis_index("query")

    def to_device(value, **masks):
        masks = {axis: mask for axis, mask in masks.items() if mask}
        return exchange(value, **masks) if masks else value

    def pack_queries(head, rank, queries, targets, out):
        rows = pl.ds(pl.multiple_of(rank * piece, piece), piece)
        return [
            (queries.at[head], out.at[pl.ds(0, part_rows)]),
            (targets.at[head, rows], out.at[pl.ds(part_rows, piece)]),
        ]

    def pack_state(head, keys, values, out):
        return [
            (keys.at[head], out.at[pl.ds(0, slot_rows)]),
            (values.at[head], out.at[pl.ds(slot_rows, slot_rows)]),
        ]

    def start_all(copies, sems, first=0):
        copies = [
            pltpu.make_async_copy(source, target, sems.at[first + at])
            for at, (source, target) in enumerate(copies)
        ]
        for copy in copies:
            copy.start()
        return copies

    def position_tail(head, positions_ref):
        return row_as_tail(positions_ref[pl.ds(head, 1), :].astype(jnp.float32), width)

    def state_tail(head, page, bias_ref, assignment_ref):
        page_start = (assignment_ref[page] * PAGE_LEN).astype(jnp.float32)
        tail = row_as_tail(bias_ref[pl.ds(head, 1), :], width)
        return jnp.concatenate(
            [tail[: TAIL - 1], jnp.full((1, width), page_start, jnp.float32)], axis=0
        )

    def send_body(
        queries, keys, values, biases, targets, positions, assignment, state_out, *refs
    ):
        query_outs = refs[: query_devices - 1]
        bias_ref, positions_ref, assignment_ref, sems = refs[query_devices - 1 :]
        rank, core, me = places()
        heads = [CORES * (me ^ turn) + core for turn in range(1, query_devices)]
        mate_head = CORES * me + (core ^ 1)
        small = start_all(
            [(assignment, assignment_ref), (positions, positions_ref), (biases, bias_ref)], sems
        )
        copies = pack_state(mate_head, keys, values, state_out)
        for head, out in zip(heads, query_outs):
            copies += pack_queries(head, rank, queries, targets, out)
        copies = start_all(copies, sems, 3)
        for copy in small:
            copy.wait()
        state_out[2 * slot_rows :, :] = state_tail(
            mate_head, CORES * rank + core, bias_ref, assignment_ref
        )
        for head, out in zip(heads, query_outs):
            out[part_rows + piece :, :] = position_tail(head, positions_ref)
        for copy in copies:
            copy.wait()

    def own_body(
        queries, keys, values, biases, targets, positions, assignment, state_out, query_out, *refs
    ):
        bias_ref, positions_ref, assignment_ref, sems = refs
        rank, core, me = places()
        head = CORES * me + core
        small = start_all(
            [(assignment, assignment_ref), (positions, positions_ref), (biases, bias_ref)], sems
        )
        copies = pack_state(head, keys, values, state_out)
        copies += pack_queries(head, rank, queries, targets, query_out)
        copies = start_all(copies, sems, 3)
        for copy in small:
            copy.wait()
        state_out[2 * slot_rows :, :] = state_tail(
            head, CORES * rank + core, bias_ref, assignment_ref
        )
        query_out[part_rows + piece :, :] = position_tail(head, positions_ref)
        for copy in copies:
            copy.wait()

    state_shape, query_shape = (packed_rows, width), (part_rows + piece + TAIL, width)
    small_scratch = [
        pltpu.VMEM(slot_bias.shape, jnp.float32),
        pltpu.VMEM(positions.shape, jnp.int32),
        pltpu.SMEM(assignment.shape, jnp.int32),
    ]
    arguments = [
        queries, compact_keys, compact_values, slot_bias, targets, positions, assignment
    ]
    mate_state, *sent_queries = call(
        send_body,
        [state_shape] + [query_shape] * (query_devices - 1),
        "pack",
        2**20,
        arguments,
        small_scratch + [pltpu.SemaphoreType.DMA((3 + 2 * query_devices,))],
        space=pl.ANY,
        vmem=60,
    )
    own_state, own_queries = call(
        own_body,
        [state_shape, query_shape],
        "own",
        2**24,
        arguments,
        small_scratch + [pltpu.SemaphoreType.DMA((7,))],
        space=pl.ANY,
    )
    packs = [own_queries] + list(sent_queries)

    def query_part(turn, part):
        return to_device(packs[part], query=turn ^ part)

    query_parts = [query_part(0, part) for part in range(query_devices)]
    states = [own_state, exchange(mate_state, page=1)]

    def in_columns(parts, axis):
        return jnp.concatenate(
            [
                lax.slice_in_dim(part, at * piece, (at + 1) * piece, axis=axis)
                for at in range(ranks)
                for part in parts
            ],
            axis=axis,
        )

    def read_queries(query_refs):
        return halves(in_columns([ref[:part_rows, :] for ref in query_refs], 0))

    def part_of(ref, at):
        return ref.at[pl.ds(at * packed_rows, packed_rows)]

    def parts_of(refs):
        return refs if len(refs) == CORES else [part_of(refs[0], at) for at in range(CORES)]

    def step_sizes(tile_refs):
        row = jnp.sum(tile_refs[0][...], axis=0)
        return (
            RATE_KEYS / jnp.sqrt(row[:, 0:1] / entry_total + EPSILON),
            RATE_VALUES / jnp.sqrt(row[:, 1:2] / entry_total + EPSILON),
            RATE_BIAS / jnp.sqrt(row[:, 2:3] / slot_total + EPSILON),
        )

    def read_pack(ref):
        return ref[:slot_rows, :], ref[slot_rows : 2 * slot_rows, :], ref[2 * slot_rows :, :]

    def store_pack(ref, values):
        ref[:slot_rows, :] = values[0]
        ref[slot_rows : 2 * slot_rows, :] = values[1]
        ref[2 * slot_rows :, :] = values[2]

    def updated(state, grads, sizes):
        return [value - size * grad for value, grad, size in zip(state, grads, sizes)]

    def page_scores(ref, queries, positions):
        scores = dot_deep(halves(ref[:slot_rows, :]), queries, 1, 1) * score_scale
        bias = row_as_column(tail_as_row(ref, 2 * slot_rows, bias_rows), width)
        scores = scores + jnp.concatenate([bias] * (positions.shape[1] // width), axis=1)
        page_start = ref[packed_rows - 1 : packed_rows, 0:1]
        visible = jnp.broadcast_to(positions >= page_start, scores.shape)
        return jnp.where(visible, scores, MASKED), visible

    def read_positions(query_refs):
        return in_columns(
            [tail_as_row(ref, part_rows + piece, pos_rows) for ref in query_refs], 1
        )

    def forward(state_refs, query_refs, chunk_outs, weights_out, max_out, chunks):
        rank, _, _ = places()
        all_queries, positions = read_queries(query_refs), read_positions(query_refs)
        all_scores, all_visible = [], []
        for at, ref in enumerate(state_refs):
            scores, visible = page_scores(ref, all_queries, positions)
            all_scores.append(scores)
            all_visible.append(visible)
        row_max = jnp.max(all_scores[0], axis=0, keepdims=True)
        for scores in all_scores[1:]:
            row_max = jnp.maximum(row_max, jnp.max(scores, axis=0, keepdims=True))
        row_total = jnp.zeros_like(row_max)
        row_sum = jnp.zeros((width, query_rows), jnp.float32)
        for at, ref in enumerate(state_refs):
            weights = jnp.where(all_visible[at], jnp.exp(all_scores[at] - row_max), 0.0)
            weights_out[at * slot_rows : (at + 1) * slot_rows, :] = weights
            row_total = row_total + jnp.sum(weights, axis=0, keepdims=True)
            values = halves(ref[slot_rows : 2 * slot_rows, :])
            row_sum = row_sum + dot_low(values, halves(weights), 0, 0)
        max_out[...] = jnp.broadcast_to(row_max, (TAIL, query_rows))
        tail = jnp.concatenate(
            [row_max, row_total, jnp.zeros((TAIL - 2, query_rows), jnp.float32)], axis=0
        )
        for at in range(ranks):
            columns = slice(at * chunk, (at + 1) * chunk)
            chunks[at, :width, :] = row_sum[:, columns]
            chunks[at, width:, :] = tail[:, columns]
        for turn in range(ranks):
            chunk_outs[turn][...] = chunks[rank ^ turn]

    chunk_shape = (width + TAIL, chunk)
    forward_shapes = [chunk_shape] * ranks + [(slots, query_rows), (TAIL, query_rows)]
    chunk_scratch = [pltpu.VMEM((ranks,) + chunk_shape, jnp.float32)]

    fold = max(1, 128 // piece)
    folded, columns = width // fold, fold * piece
    piece_shape = (folded + TAIL, columns)
    piece_scratch = [pltpu.VMEM((ranks,) + piece_shape, jnp.float32)]

    def fold_rows(value):
        groups = [value[at * folded : (at + 1) * folded, :] for at in range(fold)]
        return jnp.concatenate(groups, axis=1)

    def unfold_rows(value):
        groups = [value[:, at * piece : (at + 1) * piece] for at in range(fold)]
        return jnp.concatenate(groups, axis=0)

    def rows_tail(rows):
        empty = jnp.zeros((TAIL - len(rows), columns), jnp.float32)
        return jnp.concatenate(rows + [empty], axis=0)

    def part_body(*refs):
        state_refs, (query_ref, *refs) = refs[:CORES], refs[CORES:]
        piece_outs, (weights_out, max_out, pieces) = refs[:ranks], refs[ranks:]
        rank, _, _ = places()
        queries = halves(query_ref[:part_rows, :])
        position_row = tail_as_row(query_ref, part_rows + piece, pos_rows)
        all_scores, all_visible = [], []
        for ref in state_refs:
            scores, visible = page_scores(ref, queries, position_row)
            all_scores.append(scores)
            all_visible.append(visible)
        row_max = jnp.max(all_scores[0], axis=0, keepdims=True)
        for scores in all_scores[1:]:
            row_max = jnp.maximum(row_max, jnp.max(scores, axis=0, keepdims=True))
        row_total = jnp.zeros_like(row_max)
        row_sum = jnp.zeros((width, part_rows), jnp.float32)
        for at, ref in enumerate(state_refs):
            weights = jnp.where(all_visible[at], jnp.exp(all_scores[at] - row_max), 0.0)
            weights_out[at * slot_rows : (at + 1) * slot_rows, :] = weights
            row_total = row_total + jnp.sum(weights, axis=0, keepdims=True)
            values = halves(ref[slot_rows : 2 * slot_rows, :])
            row_sum = row_sum + dot_low(values, halves(weights), 0, 0)
        max_out[...] = jnp.broadcast_to(row_max, (TAIL, part_rows))
        for at in range(ranks):
            own = slice(at * piece, (at + 1) * piece)
            pieces[at, :folded, :] = fold_rows(row_sum[:, own])
            pieces[at, folded:, :] = rows_tail(
                [jnp.concatenate([row[:, own]] * fold, axis=1) for row in (row_max, row_total)]
            )
        for turn in range(ranks):
            piece_outs[turn][...] = pieces[rank ^ turn]

    part_shapes = [piece_shape] * ranks + [(slots, part_rows), (TAIL, part_rows)]

    def next_body(*refs):
        state_refs, refs = refs[:2], refs[2:]
        query_refs, refs = refs[:query_devices], refs[query_devices:]
        grad_refs, refs = refs[:2], refs[2:]
        tile_refs, refs = refs[: len(tiles)], refs[len(tiles) :]
        refs[0][CORES * packed_rows :, :] = query_refs[0][...]
        state_outs, refs = parts_of(refs[:1]), refs[1:]
        chunk_outs, refs = refs[:ranks], refs[ranks:]
        sizes = step_sizes(tile_refs)
        for at in range(2):
            state = read_pack(state_refs[at])
            store_pack(state_outs[at], updated(state, read_pack(grad_refs[at]), sizes))
        forward(state_outs, query_refs, chunk_outs, *refs)

    def merged_chunk(query_refs, sums, maxima, totals, out):
        targets = jnp.concatenate(
            [ref[part_rows : part_rows + piece, :] for ref in query_refs], axis=0
        )
        row_max = maxima[0]
        for other in maxima[1:]:
            row_max = jnp.maximum(row_max, other)
        row_total = jnp.zeros_like(row_max)
        row_sum = jnp.zeros((width, chunk), jnp.float32)
        for part_sum, part_max, part_total in zip(sums, maxima, totals):
            factor = jnp.exp(part_max - row_max)
            row_total = row_total + part_total * factor
            row_sum = row_sum + part_sum * factor
        output = row_sum / row_total
        residual = output - targets.T
        row_delta = jnp.sum(residual * output, axis=0, keepdims=True)
        out[:width, :] = residual
        out[width:, :] = jnp.concatenate(
            [row_max, row_total, row_delta, jnp.zeros((TAIL - 3, chunk), jnp.float32)], axis=0
        )

    def first_merge_body(*refs):
        query_refs, (*piece_refs, merged_out) = refs[:query_devices], refs[query_devices:]

        def joined(read):
            return [
                jnp.concatenate([read(ref) for ref in piece_refs[turn::ranks]], axis=1)
                for turn in range(ranks)
            ]

        merged_chunk(
            query_refs,
            joined(lambda ref: unfold_rows(ref[:folded, :])),
            joined(lambda ref: ref[folded : folded + 1, :piece]),
            joined(lambda ref: ref[folded + 1 : folded + 2, :piece]),
            merged_out,
        )

    def merge_body(*refs):
        query_refs, (*chunk_refs, merged_out) = refs[:query_devices], refs[query_devices:]
        merged_chunk(
            query_refs,
            [ref[:width, :] for ref in chunk_refs],
            [ref[width : width + 1, :] for ref in chunk_refs],
            [ref[width + 1 : width + 2, :] for ref in chunk_refs],
            merged_out,
        )

    def page_gradients(weights, factor, state_ref, all_queries, residual, row_delta):
        attention = weights * factor
        grad_values = dot_narrow(halves(attention), residual, 1, 1)
        grad_probs = dot_deep(halves(state_ref[slot_rows : 2 * slot_rows, :]), residual, 1, 0)
        grad_scores = attention * (grad_probs - row_delta)
        grad_keys = dot_narrow(halves(grad_scores), all_queries, 1, 0) * score_scale
        grad_bias = column_sums(grad_scores, width)
        return grad_keys, grad_values, row_as_tail(grad_bias, width)

    def split_merged(joined):
        row_max, row_total, row_delta = (
            joined[width + at : width + at + 1, :] for at in range(3)
        )
        return halves(joined[:width, :]), row_max, row_total, row_delta

    def read_chunks(merged_refs, chunks):
        rank, _, _ = places()
        for turn, ref in zip([0] + turns[::-1], merged_refs):
            chunks[rank ^ turn] = ref[...]
        return [chunks[at] for at in range(ranks)]

    def join_body(*refs):
        *merged_refs, joined_out, chunks = refs
        joined_out[...] = jnp.concatenate(read_chunks(merged_refs, chunks), axis=1)

    def backward_body(*refs):
        weights_refs, refs = refs[: len(weights)], refs[len(weights) :]
        max_refs, refs = refs[: len(weights)], refs[len(weights) :]
        state_refs, refs = parts_of(refs[: len(states)]), refs[len(states) :]
        query_refs, refs = refs[:query_devices], refs[query_devices:]
        merged_refs, refs = refs[: len(all_merged)], refs[len(all_merged) :]
        grad_outs, (squares_out, *scratch) = refs[:2], refs[2:]
        if len(states) < CORES:
            joined = merged_refs[0][...]
            all_queries = read_queries(query_refs)
        else:
            chunks = read_chunks(merged_refs, *scratch)
            joined = jnp.concatenate(
                [
                    value[:, part * piece : (part + 1) * piece]
                    for part in range(query_devices)
                    for value in chunks
                ],
                axis=1,
            )
            all_queries = halves(
                jnp.concatenate([ref[:part_rows, :] for ref in query_refs], axis=0)
            )
        residual, row_max, row_total, row_delta = split_merged(joined)
        maxima = jnp.concatenate([ref[0:1, :] for ref in max_refs], axis=1)
        factor = jnp.exp(maxima - row_max) / row_total
        squares = [jnp.zeros((1, width), jnp.float32)] * 3
        for at, (ref, out) in enumerate(zip(state_refs, grad_outs)):
            rows = slice(at * slot_rows, (at + 1) * slot_rows)
            page_weights = jnp.concatenate([part[rows, :] for part in weights_refs], axis=1)
            grads = page_gradients(page_weights, factor, ref, all_queries, residual, row_delta)
            store_pack(out, grads)
            for which, grad in enumerate(grads):
                squares[which] = squares[which] + jnp.sum(grad * grad, axis=0, keepdims=True)
        lanes = lax.broadcasted_iota(jnp.int32, (1, width), 1)
        row = jnp.zeros((1, width), jnp.float32)
        for which, square in enumerate(squares):
            row = jnp.where(lanes == which, jnp.sum(square, axis=1, keepdims=True), row)
        for at in range(devices):
            squares_out[at] = row

    def page_body(at):
        def body(tile_ref, grad_ref, own_state_ref, *refs):
            state_refs, refs = refs[: query_devices - 1], refs[query_devices - 1 :]
            joined_refs, (*pack_refs, out) = refs[: query_devices - 1], refs[query_devices - 1 :]
            sizes = step_sizes([tile_ref])
            state = read_pack(part_of(own_state_ref, at))
            store_pack(part_of(out, 0), updated(state, read_pack(grad_ref), sizes))
            for turn, (state_ref, joined_ref) in enumerate(zip(state_refs, joined_refs), 1):
                query_refs = [state_ref.at[pl.ds(CORES * packed_rows, query_shape[0])]]
                query_refs += pack_refs[(turn - 1) * (query_devices - 1) :][: query_devices - 1]
                residual, row_max, row_total, row_delta = split_merged(joined_ref[...])
                all_queries = read_queries(query_refs)
                ref = part_of(state_ref, at)
                scores, visible = page_scores(ref, all_queries, read_positions(query_refs))
                weights = jnp.where(visible, jnp.exp(scores - row_max), 0.0)
                grads = page_gradients(
                    weights, 1.0 / row_total, ref, all_queries, residual, row_delta
                )
                store_pack(part_of(out, turn), updated(read_pack(ref), grads, sizes))

        return body

    for repeat in range(STEPS):
        last = repeat == STEPS - 1
        if repeat == 0:
            sums, weights, maxima = [], [], []
            for query_pack in query_parts:
                *pieces, part_weights, part_max = call(
                    part_body,
                    part_shapes,
                    "forward",
                    2 * matmul_cost // query_devices,
                    states + [query_pack],
                    piece_scratch,
                    after=maxima[-1:],
                )
                arrived = {
                    turn: exchange(pieces[turn], page=CORES * turn)
                    for turn in turns
                }
                sums += list(arrived.values()) + pieces[:1]
                weights.append(part_weights)
                maxima.append(part_max)
        else:
            new_state, *chunk_parts, part_weights, part_max = call(
                next_body,
                [(CORES * packed_rows + query_shape[0], width)] + forward_shapes,
                "update_forward",
                2 * matmul_cost,
                states + query_parts + grads + tiles,
                chunk_scratch,
            )
            states, weights, maxima = [new_state], [part_weights], [part_max]
            arrived = {
                turn: exchange(chunk_parts[turn], page=CORES * turn)
                for turn in turns
            }
            sums = chunk_parts[:1] + list(arrived.values())
            new_states = states + [
                exchange(states[0], query=turn) for turn in range(1, query_devices)
            ]
        (merged,) = call(
            merge_body if repeat else first_merge_body,
            [chunk_shape],
            "merge",
            2**20,
            query_parts + sums,
        )
        all_merged = [merged] + [exchange(merged, page=CORES * turn) for turn in reversed(turns)]
        if last:
            all_merged = call(
                join_body, [(width + TAIL, query_rows)], "join", 2**20, all_merged, chunk_scratch
            )
            all_joined = [
                to_device(all_merged[0], query=turn) for turn in range(query_devices)
            ]
        own_grad, mate_grad, squares = call(
            backward_body,
            packed_shapes + [(devices, 1, width)],
            "backward",
            3 * matmul_cost,
            weights + maxima + states + query_parts + list(all_merged),
            scratch=() if last else chunk_scratch,
        )
        grads = [own_grad, mate_grad]
        tiles = [
            lax.all_to_all(
                squares, ("page", "query", "head"), split_axis=0, concat_axis=0, tiled=True
            )
        ]

    other_packs = [
        packs[part] if part == turn else query_part(turn, part)
        for turn in range(1, query_devices)
        for part in range(1, query_devices)
    ]
    operands = new_states + all_joined[1:] + other_packs
    pages = []
    for at, grad in ((1, mate_grad), (0, own_grad)):
        pages += call(
            page_body(at),
            [(query_devices * packed_rows, width)],
            "page_update",
            3 * matmul_cost // 2,
            tiles + [grad] + operands,
            after=pages,
        )
    mate_page, own_page = exchange(pages[0], page=1), pages[1]

    def write_page(page_ref, flip, keys_out, values_out, sems):
        _, core, me = places()
        copies = []
        for turn in range(query_devices):
            keys, values = (
                page_ref.at[pl.ds(turn * packed_rows + at * slot_rows, slot_rows)]
                for at in range(2)
            )
            head = CORES * (me ^ turn) + (core ^ flip)
            copies += [(keys, keys_out.at[head]), (values, values_out.at[head])]
        return start_all(copies, sems)

    def own_unpack_body(page_ref, keys_out, values_out, sems):
        for copy in write_page(page_ref, 0, keys_out, values_out, sems):
            copy.wait()

    def unpack_body(own_ref, mate_ref, _keys, _values, keys_out, values_out, bias_out, sems):
        copies = write_page(mate_ref, 1, keys_out, values_out, sems)
        _, core, me = places()
        for flip, page_ref in enumerate((own_ref, mate_ref)):
            for turn in range(query_devices):
                first = turn * packed_rows + 2 * slot_rows
                head = CORES * (me ^ turn) + (core ^ flip)
                bias_out[pl.ds(head, 1), :] = tail_as_row(page_ref, first, bias_rows)
        for copy in copies:
            copy.wait()

    result_shapes = [compact_keys.shape, compact_values.shape]
    unpack_sems = [pltpu.SemaphoreType.DMA((2 * query_devices,))]
    results = call(
        own_unpack_body,
        result_shapes,
        "unpack_own",
        2**10,
        [own_page],
        unpack_sems,
        out_spaces=[pl.ANY] * 2,
    )
    return tuple(
        call(
            unpack_body,
            result_shapes + [slot_bias.shape],
            "unpack",
            2**20,
            [own_page, mate_page] + list(results),
            unpack_sems,
            spaces=[pltpu.VMEM] * 2 + [pl.ANY] * 2,
            out_spaces=[pl.ANY] * 2 + [pltpu.VMEM],
            aliases={2: 0, 3: 1},
        )
    )


def from_partner(value, axis, stride):
    mask = 2**stride
    pairs = [(source, source ^ mask) for source in range(lax.axis_size(axis))]
    return lax.ppermute(value, axis, pairs)


def squared_sums(grad_keys, grad_values, grad_bias):
    return jnp.stack(
        [
            jnp.sum(grad_keys * grad_keys),
            jnp.sum(grad_values * grad_values),
            jnp.sum(grad_bias * grad_bias),
        ]
    )


def apply_update(states, grads, totals, entry_count, slot_total):
    key_state, value_state, bias_state = states
    grad_keys, grad_values, grad_bias = grads
    rms_keys = jnp.sqrt(totals[0] / entry_count + EPSILON)
    rms_values = jnp.sqrt(totals[1] / entry_count + EPSILON)
    rms_bias = jnp.sqrt(totals[2] / slot_total + EPSILON)
    return (
        key_state - RATE_KEYS * grad_keys / rms_keys,
        value_state - RATE_VALUES * grad_values / rms_values,
        bias_state - RATE_BIAS * grad_bias / rms_bias,
    )


def local_gradients(queries, targets, visible, compact_keys, compact_values, slot_bias):
    score_scale = 1.0 / math.sqrt(queries.shape[2])
    scores = jnp.einsum("hqd,hsd->hqs", queries, compact_keys, precision=HIGHEST) * score_scale
    scores = jnp.where(visible, scores + slot_bias[:, None, :], MASKED)
    local_max = jnp.max(scores, axis=2)
    row_max = lax.pmax(local_max, "page")
    weights = jnp.where(visible, jnp.exp(scores - row_max[:, :, None]), 0.0)
    local_sum = jnp.einsum("hqs,hsd->hqd", weights, compact_values, precision=HIGHEST)
    row_total, row_sum = lax.psum((jnp.sum(weights, axis=2), local_sum), "page")
    attention = weights / row_total[:, :, None]
    output = row_sum / row_total[:, :, None]
    residual = output - targets
    grad_values = jnp.einsum("hqs,hqd->hsd", attention, residual, precision=HIGHEST)
    row_delta = jnp.sum(residual * output, axis=2)
    grad_probs = jnp.einsum("hqd,hsd->hqs", residual, compact_values, precision=HIGHEST)
    grad_scores = attention * (grad_probs - row_delta[:, :, None])
    grad_bias = jnp.sum(grad_scores, axis=1)
    grad_keys = jnp.einsum("hqs,hqd->hsd", grad_scores, queries, precision=HIGHEST) * score_scale
    return (grad_keys, grad_values, grad_bias)


def per_device(queries, compact_keys, compact_values, slot_bias, targets, positions, assignment):
    page_number = assignment[lax.axis_index("page")]
    local_heads = compact_keys.shape[0]
    slot_total = local_heads * lax.axis_size("head") * compact_keys.shape[1] * lax.axis_size("page")
    entry_count = slot_total * compact_keys.shape[2]
    query_count = lax.axis_size("query")
    heads_kept = max(local_heads // query_count, 1)
    query_parts = max(query_count // local_heads, 1)
    part_rows = queries.shape[1] // query_parts

    def split_items(array):
        width = array.shape[2]
        array = array.reshape(local_heads // heads_kept, heads_kept, query_parts, part_rows, width)
        array = jnp.transpose(array, (0, 2, 1, 3, 4))
        return array.reshape(query_count, heads_kept, part_rows, width)

    def join_items(array):
        width = array.shape[3]
        array = jnp.transpose(array, (1, 0, 2, 3))
        return array.reshape(heads_kept, query_count * part_rows, width)

    position_column = positions.astype(jnp.float32)[:, :, None]
    got_queries, got_targets, got_positions = (
        lax.all_to_all(split_items(queries), "query", split_axis=0, concat_axis=0, tiled=True),
        lax.all_to_all(split_items(targets), "query", split_axis=0, concat_axis=0, tiled=True),
        lax.all_to_all(
            split_items(position_column), "query", split_axis=0, concat_axis=0, tiled=True
        ),
    )
    group_queries = join_items(got_queries)
    group_targets = join_items(got_targets)
    group_positions = join_items(got_positions)[:, :, 0]
    visible = (page_number.astype(jnp.float32) <= jnp.floor(group_positions / PAGE_LEN))[:, :, None]
    query_index = lax.axis_index("query")
    first_head = query_index // query_parts * heads_kept
    key_state = lax.dynamic_slice_in_dim(compact_keys, first_head, heads_kept, 0)
    value_state = lax.dynamic_slice_in_dim(compact_values, first_head, heads_kept, 0)
    bias_state = lax.dynamic_slice_in_dim(slot_bias, first_head, heads_kept, 0)
    counted = (query_index % query_parts == 0).astype(jnp.float32)
    for repeat in range(STEPS):
        grads = local_gradients(
            group_queries, group_targets, visible, key_state, value_state, bias_state
        )
        for bit in range(query_parts.bit_length() - 1):
            partner = from_partner((grads[0], grads[1], grads[2]), "query", bit)
            grads = (grads[0] + partner[0], grads[1] + partner[1], grads[2] + partner[2])
        totals = lax.psum(
            squared_sums(grads[0], grads[1], grads[2]) * counted, ("page", "query", "head")
        )
        key_state, value_state, bias_state = apply_update(
            (key_state, value_state, bias_state), grads, totals, entry_count, slot_total
        )
    all_keys, all_values, all_bias = (
        lax.all_gather(key_state, "query", axis=0, tiled=True),
        lax.all_gather(value_state, "query", axis=0, tiled=True),
        lax.all_gather(bias_state, "query", axis=0, tiled=True),
    )
    slot_rows = compact_keys.shape[1]
    head_width = compact_keys.shape[2]
    all_keys = all_keys.reshape(
        local_heads // heads_kept, query_parts, heads_kept, slot_rows, head_width
    )[:, 0]
    all_values = all_values.reshape(
        local_heads // heads_kept, query_parts, heads_kept, slot_rows, head_width
    )[:, 0]
    all_bias = all_bias.reshape(local_heads // heads_kept, query_parts, heads_kept, slot_rows)[:, 0]
    return (
        all_keys.reshape(local_heads, slot_rows, head_width),
        all_values.reshape(local_heads, slot_rows, head_width),
        all_bias.reshape(local_heads, slot_rows),
    )


def solution(mesh):
    placed = (
        P("head", "query", None),
        P("head", "page", None),
        P("head", "page", None),
        P("head", "page"),
        P("head", "query", None),
        P("head", "query"),
        P(),
    )

    def program(*args):
        plan = direct_per_device if direct_plan_fits(mesh, args[0], args[1]) else per_device
        return jax.shard_map(
            plan,
            mesh=mesh,
            in_specs=placed,
            out_specs=(P("head", "page", None), P("head", "page", None), P("head", "page")),
            check_vma=False,
        )(*args)

    return program
```

```python
import itertools
import math

import jax
import jax.numpy as jnp
from jax import lax
from jax.experimental import pallas as pl
from jax.experimental.pallas import tpu as pltpu
from jax.sharding import PartitionSpec as P

STEPS = 2
PAGE_LEN = 32768


MASKED = -1e30
EPSILON = 1e-06
RATE_KEYS = 0.05
RATE_VALUES = 0.05
RATE_BIAS = 0.2
HIGHEST = lax.Precision.HIGHEST
TAIL = 8
CORES = 2


def exchange(value, **masks):
    axes = tuple(masks)
    sizes = [lax.axis_size(axis) for axis in axes]

    def flat(place):
        index = 0
        for size, at in zip(sizes, place):
            index = index * size + at
        return index

    pairs = [
        (flat(place), flat([at ^ mask for at, mask in zip(place, masks.values())]))
        for place in itertools.product(*map(range, sizes))
    ]
    return lax.ppermute(value, axes, pairs)


def halves(value):
    high = value.astype(jnp.bfloat16)
    return high, (value - high.astype(jnp.float32)).astype(jnp.bfloat16)


def one_pass(left, right, left_dim, right_dim):
    return lax.dot_general(
        left,
        right,
        (((left_dim,), (right_dim,)), ((), ())),
        preferred_element_type=jnp.float32,
    )


def dot_deep(left, right, left_dim, right_dim):
    left = jnp.concatenate([left[0], left[1], left[0]], axis=left_dim)
    right = jnp.concatenate([right[0], right[0], right[1]], axis=right_dim)
    return one_pass(left, right, left_dim, right_dim)


def dot_narrow(left, right, left_dim, right_dim):
    both = one_pass(
        left[0], jnp.concatenate(right, axis=1 - right_dim), left_dim, right_dim
    )
    count = both.shape[1] // 2
    cross = both[:, count:] + one_pass(left[1], right[0], left_dim, right_dim)
    return both[:, :count] + cross


def dot_low(left, right, left_dim, right_dim):
    both = one_pass(jnp.concatenate(left, axis=1 - left_dim), right[0], left_dim, right_dim)
    count = both.shape[0] // 2
    cross = both[count:, :] + one_pass(left[0], right[1], left_dim, right_dim)
    return both[:count, :] + cross


def call(body, out_shapes, name, cost, operands, scratch=(), after=(), space=pltpu.VMEM, vmem=32):
    spaces = [space] * len(operands) + [pl.ANY] * len(after)
    count = len(operands)

    def without_after(*refs):
        body(*refs[:count], *refs[count + len(after) :])

    return pl.pallas_call(
        without_after,
        out_shape=[jax.ShapeDtypeStruct(shape, jnp.float32) for shape in out_shapes],
        in_specs=[pl.BlockSpec(memory_space=space) for space in spaces],
        out_specs=[pl.BlockSpec(memory_space=pltpu.VMEM) for _ in out_shapes],
        scratch_shapes=scratch,
        compiler_params=pltpu.CompilerParams(vmem_limit_bytes=vmem * 2**20),
        cost_estimate=pl.CostEstimate(flops=cost, bytes_accessed=2**20, transcendentals=0),
        name=name,
    )(*operands, *after)


def row_as_tail(row, width):
    rows = [row[:, at : at + width] for at in range(0, row.shape[1], width)]
    rows.append(jnp.zeros((TAIL - len(rows), width), row.dtype))
    return jnp.concatenate(rows, axis=0)


def tail_as_row(ref, start, count):
    return jnp.concatenate([ref[start + at : start + at + 1, :] for at in range(count)], axis=1)


def row_as_column(row, width):
    parts = []
    for at in range(0, row.shape[1], width):
        parts.append(jnp.broadcast_to(row[:, at : at + width], (width, width)).T)
    return jnp.concatenate(parts, axis=0)


def column_sums(value, width):
    groups = [value[:, at : at + width] for at in range(0, value.shape[1], width)]
    partial = sum(groups[1:], groups[0])
    blocks = [
        jnp.sum(partial[at : at + width, :].T, axis=0, keepdims=True)
        for at in range(0, value.shape[0], width)
    ]
    return jnp.concatenate(blocks, axis=1)


def direct_plan_fits(mesh, queries, compact_keys):
    sizes = [mesh.shape[axis] for axis in ("page", "query", "head")]
    pages, query_devices, head_devices = sizes
    local_heads = queries.shape[0] // head_devices
    part_rows = queries.shape[1] // query_devices
    slot_rows = compact_keys.shape[1] // pages
    width = queries.shape[2]
    if any(size & (size - 1) for size in sizes) or pages < CORES or width % 128:
        return False
    if local_heads != CORES * query_devices:
        return False
    ranks = pages // CORES
    chunk = part_rows * query_devices // ranks
    return (
        part_rows * query_devices % ranks == 0
        and chunk % 128 == 0
        and part_rows % (8 * ranks) == 0
        and (part_rows // ranks % 128 == 0 or 1024 % (part_rows // ranks * 8) == 0)
        and slot_rows % width == 0
        and part_rows % width == 0
        and max(slot_rows, part_rows) < TAIL * width
    )


def direct_per_device(
    queries, compact_keys, compact_values, slot_bias, targets, positions, assignment
):
    local_heads, part_rows, width = queries.shape
    slot_rows = compact_keys.shape[1]
    query_devices = lax.axis_size("query")
    head_devices = lax.axis_size("head")
    ranks = lax.axis_size("page") // CORES
    query_rows = part_rows * query_devices
    chunk, piece = query_rows // ranks, part_rows // ranks
    turns = [ranks // 2] + [turn for turn in reversed(range(1, ranks)) if turn != ranks // 2]
    slot_total = local_heads * head_devices * slot_rows * lax.axis_size("page")
    entry_total = slot_total * width
    score_scale = 1.0 / math.sqrt(width)
    slots = CORES * slot_rows
    devices = ranks * CORES * query_devices * head_devices
    pos_rows = part_rows // width
    bias_rows = slot_rows // width
    packed_rows = 2 * slot_rows + TAIL
    packed_shapes = [(packed_rows, width)] * 2
    matmul_cost = 3 * 2 * slots * query_rows * width

    def places():
        page = lax.axis_index("page")
        return page // CORES, page % CORES, lax.axis_index("query")

    def to_device(value, **masks):
        masks = {axis: mask for axis, mask in masks.items() if mask}
        return exchange(value, **masks) if masks else value

    def pack_state(head, keys, values, out):
        return [
            (keys.at[head], out.at[pl.ds(0, slot_rows)]),
            (values.at[head], out.at[pl.ds(slot_rows, slot_rows)]),
        ]

    def start_all(copies, sems, first=0):
        copies = [
            pltpu.make_async_copy(source, target, sems.at[first + at])
            for at, (source, target) in enumerate(copies)
        ]
        for copy in copies:
            copy.start()
        return copies

    def position_tail(head, positions_ref):
        return row_as_tail(positions_ref[pl.ds(head, 1), :].astype(jnp.float32), width)

    def state_tail(head, page, bias_ref, assignment_ref):
        page_start = (assignment_ref[page] * PAGE_LEN).astype(jnp.float32)
        tail = row_as_tail(bias_ref[pl.ds(head, 1), :], width)
        return jnp.concatenate(
            [tail[: TAIL - 1], jnp.full((1, width), page_start, jnp.float32)], axis=0
        )

    def send_body(
        queries, keys, values, biases, targets, positions, assignment, state_out, *refs
    ):
        query_outs = refs[: query_devices - 1]
        bias_ref, positions_ref, assignment_ref, sems = refs[query_devices - 1 :]
        rank, core, me = places()
        heads = [CORES * (me ^ turn) + core for turn in range(1, query_devices)]
        mate_head = CORES * me + (core ^ 1)
        small = start_all(
            [(assignment, assignment_ref), (positions, positions_ref), (biases, bias_ref)], sems
        )
        copies = pack_state(mate_head, keys, values, state_out)
        for head, out in zip(heads, query_outs):
            copies.append((queries.at[head], out.at[pl.ds(0, part_rows)]))
        copies = start_all(copies, sems, 3)
        for copy in small:
            copy.wait()
        state_out[2 * slot_rows :, :] = state_tail(
            mate_head, CORES * rank + core, bias_ref, assignment_ref
        )
        for head, out in zip(heads, query_outs):
            out[part_rows:, :] = position_tail(head, positions_ref)
        for copy in copies:
            copy.wait()

    def own_body(
        queries, keys, values, biases, targets, positions, assignment, state_out, query_out, *refs
    ):
        target_outs, refs = refs[:query_devices], refs[query_devices:]
        bias_ref, positions_ref, assignment_ref, sems = refs
        rank, core, me = places()
        head = CORES * me + core
        small = start_all(
            [(assignment, assignment_ref), (positions, positions_ref), (biases, bias_ref)], sems
        )
        copies = pack_state(head, keys, values, state_out)
        copies.append((queries.at[head], query_out.at[pl.ds(0, part_rows)]))
        rows = pl.ds(pl.multiple_of(rank * piece, piece), piece)
        for turn, out in enumerate(target_outs):
            copies.append((targets.at[CORES * (me ^ turn) + core, rows], out))
        copies = start_all(copies, sems, 3)
        for copy in small:
            copy.wait()
        state_out[2 * slot_rows :, :] = state_tail(
            head, CORES * rank + core, bias_ref, assignment_ref
        )
        query_out[part_rows:, :] = position_tail(head, positions_ref)
        for copy in copies:
            copy.wait()

    state_shape, query_shape = (packed_rows, width), (part_rows + TAIL, width)
    small_scratch = [
        pltpu.VMEM(slot_bias.shape, jnp.float32),
        pltpu.VMEM(positions.shape, jnp.int32),
        pltpu.SMEM(assignment.shape, jnp.int32),
    ]
    arguments = [
        queries, compact_keys, compact_values, slot_bias, targets, positions, assignment
    ]
    mate_state, *sent_queries = call(
        send_body,
        [state_shape] + [query_shape] * (query_devices - 1),
        "pack",
        2**20,
        arguments,
        small_scratch + [pltpu.SemaphoreType.DMA((3 + 2 * query_devices,))],
        space=pl.ANY,
        vmem=60,
    )
    own_state, own_queries, own_targets, *sent_targets = call(
        own_body,
        [state_shape, query_shape] + [(piece, width)] * query_devices,
        "own",
        2**24,
        arguments,
        small_scratch + [pltpu.SemaphoreType.DMA((6 + query_devices,))],
        space=pl.ANY,
    )
    packs = [own_queries] + list(sent_queries)

    def query_part(turn, part):
        return to_device(packs[part], query=turn ^ part)

    query_parts = [query_part(0, part) for part in range(query_devices)]
    states = [own_state, exchange(mate_state, page=1)]

    def in_columns(parts, axis):
        return jnp.concatenate(
            [
                lax.slice_in_dim(part, at * piece, (at + 1) * piece, axis=axis)
                for at in range(ranks)
                for part in parts
            ],
            axis=axis,
        )

    def read_queries(query_refs):
        return halves(in_columns([ref[:part_rows, :] for ref in query_refs], 0))

    def part_of(ref, at):
        return ref.at[pl.ds(at * packed_rows, packed_rows)]

    def parts_of(refs):
        return refs if len(refs) == CORES else [part_of(refs[0], at) for at in range(CORES)]

    def step_sizes(tile_refs):
        row = jnp.sum(tile_refs[0][...], axis=0)
        return (
            RATE_KEYS / jnp.sqrt(row[:, 0:1] / entry_total + EPSILON),
            RATE_VALUES / jnp.sqrt(row[:, 1:2] / entry_total + EPSILON),
            RATE_BIAS / jnp.sqrt(row[:, 2:3] / slot_total + EPSILON),
        )

    def read_pack(ref):
        return ref[:slot_rows, :], ref[slot_rows : 2 * slot_rows, :], ref[2 * slot_rows :, :]

    def store_pack(ref, values):
        ref[:slot_rows, :] = values[0]
        ref[slot_rows : 2 * slot_rows, :] = values[1]
        ref[2 * slot_rows :, :] = values[2]

    def updated(state, grads, sizes):
        return [value - size * grad for value, grad, size in zip(state, grads, sizes)]

    def page_scores(ref, queries, positions):
        scores = dot_deep(halves(ref[:slot_rows, :]), queries, 1, 1) * score_scale
        bias = row_as_column(tail_as_row(ref, 2 * slot_rows, bias_rows), width)
        scores = scores + jnp.concatenate([bias] * (positions.shape[1] // width), axis=1)
        page_start = ref[packed_rows - 1 : packed_rows, 0:1]
        visible = jnp.broadcast_to(positions >= page_start, scores.shape)
        return jnp.where(visible, scores, MASKED), visible

    def read_positions(query_refs):
        return in_columns(
            [tail_as_row(ref, part_rows, pos_rows) for ref in query_refs], 1
        )

    def forward(state_refs, query_refs, chunk_outs, weights_out, max_out, chunks):
        rank, _, _ = places()
        all_queries, positions = read_queries(query_refs), read_positions(query_refs)
        all_scores, all_visible = [], []
        for at, ref in enumerate(state_refs):
            scores, visible = page_scores(ref, all_queries, positions)
            all_scores.append(scores)
            all_visible.append(visible)
        row_max = jnp.max(all_scores[0], axis=0, keepdims=True)
        for scores in all_scores[1:]:
            row_max = jnp.maximum(row_max, jnp.max(scores, axis=0, keepdims=True))
        row_total = jnp.zeros_like(row_max)
        row_sum = jnp.zeros((width, query_rows), jnp.float32)
        for at, ref in enumerate(state_refs):
            weights = jnp.where(all_visible[at], jnp.exp(all_scores[at] - row_max), 0.0)
            weights_out[at * slot_rows : (at + 1) * slot_rows, :] = weights
            row_total = row_total + jnp.sum(weights, axis=0, keepdims=True)
            values = halves(ref[slot_rows : 2 * slot_rows, :])
            row_sum = row_sum + dot_low(values, halves(weights), 0, 0)
        max_out[...] = jnp.broadcast_to(row_max, (TAIL, query_rows))
        tail = jnp.concatenate(
            [row_max, row_total, jnp.zeros((TAIL - 2, query_rows), jnp.float32)], axis=0
        )
        for at in range(ranks):
            columns = slice(at * chunk, (at + 1) * chunk)
            chunks[at, :width, :] = row_sum[:, columns]
            chunks[at, width:, :] = tail[:, columns]
        for turn in range(ranks):
            chunk_outs[turn][...] = chunks[rank ^ turn]

    chunk_shape = (width + TAIL, chunk)
    forward_shapes = [chunk_shape] * ranks + [(slots, query_rows), (TAIL, query_rows)]
    chunk_scratch = [pltpu.VMEM((ranks,) + chunk_shape, jnp.float32)]

    fold = max(1, 128 // piece)
    folded, columns = width // fold, fold * piece
    piece_shape = (folded + TAIL, columns)
    piece_scratch = [pltpu.VMEM((ranks,) + piece_shape, jnp.float32)]

    def fold_rows(value):
        groups = [value[at * folded : (at + 1) * folded, :] for at in range(fold)]
        return jnp.concatenate(groups, axis=1)

    def unfold_rows(value):
        groups = [value[:, at * piece : (at + 1) * piece] for at in range(fold)]
        return jnp.concatenate(groups, axis=0)

    def rows_tail(rows):
        empty = jnp.zeros((TAIL - len(rows), columns), jnp.float32)
        return jnp.concatenate(rows + [empty], axis=0)

    def part_body(*refs):
        state_refs, (query_ref, *refs) = refs[:CORES], refs[CORES:]
        target_refs, refs = refs[: len(passed)], refs[len(passed) :]
        piece_outs, (weights_out, max_out, *refs) = refs[:ranks], refs[ranks:]
        *target_outs, pieces = refs
        for ref, out in zip(target_refs, target_outs):
            out[...] = ref[...]
        rank, _, _ = places()
        queries = halves(query_ref[:part_rows, :])
        position_row = tail_as_row(query_ref, part_rows, pos_rows)
        all_scores, all_visible = [], []
        for ref in state_refs:
            scores, visible = page_scores(ref, queries, position_row)
            all_scores.append(scores)
            all_visible.append(visible)
        row_max = jnp.max(all_scores[0], axis=0, keepdims=True)
        for scores in all_scores[1:]:
            row_max = jnp.maximum(row_max, jnp.max(scores, axis=0, keepdims=True))
        row_total = jnp.zeros_like(row_max)
        row_sum = jnp.zeros((width, part_rows), jnp.float32)
        for at, ref in enumerate(state_refs):
            weights = jnp.where(all_visible[at], jnp.exp(all_scores[at] - row_max), 0.0)
            weights_out[at * slot_rows : (at + 1) * slot_rows, :] = weights
            row_total = row_total + jnp.sum(weights, axis=0, keepdims=True)
            values = halves(ref[slot_rows : 2 * slot_rows, :])
            row_sum = row_sum + dot_low(values, halves(weights), 0, 0)
        max_out[...] = jnp.broadcast_to(row_max, (TAIL, part_rows))
        for at in range(ranks):
            own = slice(at * piece, (at + 1) * piece)
            pieces[at, :folded, :] = fold_rows(row_sum[:, own])
            pieces[at, folded:, :] = rows_tail(
                [jnp.concatenate([row[:, own]] * fold, axis=1) for row in (row_max, row_total)]
            )
        for turn in range(ranks):
            piece_outs[turn][...] = pieces[rank ^ turn]

    part_shapes = [piece_shape] * ranks + [(slots, part_rows), (TAIL, part_rows)]

    def next_body(*refs):
        state_refs, refs = refs[:2], refs[2:]
        query_refs, refs = refs[:query_devices], refs[query_devices:]
        grad_refs, refs = refs[:2], refs[2:]
        tile_refs, refs = refs[: len(tiles)], refs[len(tiles) :]
        refs[0][CORES * packed_rows :, :] = query_refs[0][...]
        state_outs, refs = parts_of(refs[:1]), refs[1:]
        chunk_outs, refs = refs[:ranks], refs[ranks:]
        sizes = step_sizes(tile_refs)
        for at in range(2):
            state = read_pack(state_refs[at])
            store_pack(state_outs[at], updated(state, read_pack(grad_refs[at]), sizes))
        forward(state_outs, query_refs, chunk_outs, *refs)

    def merged_chunk(target_refs, sums, maxima, totals, out):
        targets = jnp.concatenate([ref[...] for ref in target_refs], axis=0)
        row_max = maxima[0]
        for other in maxima[1:]:
            row_max = jnp.maximum(row_max, other)
        row_total = jnp.zeros_like(row_max)
        row_sum = jnp.zeros((width, chunk), jnp.float32)
        for part_sum, part_max, part_total in zip(sums, maxima, totals):
            factor = jnp.exp(part_max - row_max)
            row_total = row_total + part_total * factor
            row_sum = row_sum + part_sum * factor
        output = row_sum / row_total
        residual = output - targets.T
        row_delta = jnp.sum(residual * output, axis=0, keepdims=True)
        out[:width, :] = residual
        out[width:, :] = jnp.concatenate(
            [row_max, row_total, row_delta, jnp.zeros((TAIL - 3, chunk), jnp.float32)], axis=0
        )

    def first_merge_body(*refs):
        target_refs, (*piece_refs, merged_out) = refs[:query_devices], refs[query_devices:]

        def joined(read):
            return [
                jnp.concatenate([read(ref) for ref in piece_refs[turn::ranks]], axis=1)
                for turn in range(ranks)
            ]

        merged_chunk(
            target_refs,
            joined(lambda ref: unfold_rows(ref[:folded, :])),
            joined(lambda ref: ref[folded : folded + 1, :piece]),
            joined(lambda ref: ref[folded + 1 : folded + 2, :piece]),
            merged_out,
        )

    def merge_body(*refs):
        target_refs, (*chunk_refs, merged_out) = refs[:query_devices], refs[query_devices:]
        merged_chunk(
            target_refs,
            [ref[:width, :] for ref in chunk_refs],
            [ref[width : width + 1, :] for ref in chunk_refs],
            [ref[width + 1 : width + 2, :] for ref in chunk_refs],
            merged_out,
        )

    def page_gradients(weights, factor, state_ref, all_queries, residual, row_delta):
        attention = weights * factor
        grad_values = dot_narrow(halves(attention), residual, 1, 1)
        grad_probs = dot_deep(halves(state_ref[slot_rows : 2 * slot_rows, :]), residual, 1, 0)
        grad_scores = attention * (grad_probs - row_delta)
        grad_keys = dot_narrow(halves(grad_scores), all_queries, 1, 0) * score_scale
        grad_bias = column_sums(grad_scores, width)
        return grad_keys, grad_values, row_as_tail(grad_bias, width)

    def split_merged(joined):
        row_max, row_total, row_delta = (
            joined[width + at : width + at + 1, :] for at in range(3)
        )
        return halves(joined[:width, :]), row_max, row_total, row_delta

    def read_chunks(merged_refs, chunks):
        rank, _, _ = places()
        for turn, ref in zip([0] + turns[::-1], merged_refs):
            chunks[rank ^ turn] = ref[...]
        return [chunks[at] for at in range(ranks)]

    def join_body(*refs):
        *merged_refs, joined_out, chunks = refs
        joined_out[...] = jnp.concatenate(read_chunks(merged_refs, chunks), axis=1)

    def backward_body(*refs):
        weights_refs, refs = refs[: len(weights)], refs[len(weights) :]
        max_refs, refs = refs[: len(weights)], refs[len(weights) :]
        state_refs, refs = parts_of(refs[: len(states)]), refs[len(states) :]
        query_refs, refs = refs[:query_devices], refs[query_devices:]
        merged_refs, refs = refs[: len(all_merged)], refs[len(all_merged) :]
        grad_outs, (squares_out, *scratch) = refs[:2], refs[2:]
        if len(states) < CORES:
            joined = merged_refs[0][...]
            all_queries = read_queries(query_refs)
        else:
            chunks = read_chunks(merged_refs, *scratch)
            joined = jnp.concatenate(
                [
                    value[:, part * piece : (part + 1) * piece]
                    for part in range(query_devices)
                    for value in chunks
                ],
                axis=1,
            )
            all_queries = halves(
                jnp.concatenate([ref[:part_rows, :] for ref in query_refs], axis=0)
            )
        residual, row_max, row_total, row_delta = split_merged(joined)
        maxima = jnp.concatenate([ref[0:1, :] for ref in max_refs], axis=1)
        factor = jnp.exp(maxima - row_max) / row_total
        squares = [jnp.zeros((1, width), jnp.float32)] * 3
        for at, (ref, out) in enumerate(zip(state_refs, grad_outs)):
            rows = slice(at * slot_rows, (at + 1) * slot_rows)
            page_weights = jnp.concatenate([part[rows, :] for part in weights_refs], axis=1)
            grads = page_gradients(page_weights, factor, ref, all_queries, residual, row_delta)
            store_pack(out, grads)
            for which, grad in enumerate(grads):
                squares[which] = squares[which] + jnp.sum(grad * grad, axis=0, keepdims=True)
        lanes = lax.broadcasted_iota(jnp.int32, (1, width), 1)
        row = jnp.zeros((1, width), jnp.float32)
        for which, square in enumerate(squares):
            row = jnp.where(lanes == which, jnp.sum(square, axis=1, keepdims=True), row)
        for at in range(devices):
            squares_out[at] = row

    def page_body(at):
        def body(tile_ref, grad_ref, own_state_ref, *refs):
            state_refs, refs = refs[: query_devices - 1], refs[query_devices - 1 :]
            joined_refs, (*pack_refs, out) = refs[: query_devices - 1], refs[query_devices - 1 :]
            sizes = step_sizes([tile_ref])
            state = read_pack(part_of(own_state_ref, at))
            store_pack(part_of(out, 0), updated(state, read_pack(grad_ref), sizes))
            for turn, (state_ref, joined_ref) in enumerate(zip(state_refs, joined_refs), 1):
                query_refs = [state_ref.at[pl.ds(CORES * packed_rows, query_shape[0])]]
                query_refs += pack_refs[(turn - 1) * (query_devices - 1) :][: query_devices - 1]
                residual, row_max, row_total, row_delta = split_merged(joined_ref[...])
                all_queries = read_queries(query_refs)
                ref = part_of(state_ref, at)
                scores, visible = page_scores(ref, all_queries, read_positions(query_refs))
                weights = jnp.where(visible, jnp.exp(scores - row_max), 0.0)
                grads = page_gradients(
                    weights, 1.0 / row_total, ref, all_queries, residual, row_delta
                )
                store_pack(part_of(out, turn), updated(read_pack(ref), grads, sizes))

        return body

    for repeat in range(STEPS):
        last = repeat == STEPS - 1
        if repeat == 0:
            sums, weights, maxima = [], [], []
            for part, query_pack in enumerate(query_parts):
                passed = list(sent_targets) if part == query_devices - 1 else []
                outs = call(
                    part_body,
                    part_shapes + [(piece, width)] * len(passed),
                    "forward",
                    2 * matmul_cost // query_devices,
                    states + [query_pack] + passed,
                    piece_scratch,
                    after=maxima[-1:] + sums[:1],
                )
                pieces, (part_weights, part_max, *leaving) = list(outs[:ranks]), outs[ranks:]
                arrived = {
                    turn: exchange(pieces[turn], page=CORES * turn)
                    for turn in turns
                }
                sums += list(arrived.values()) + pieces[:1]
                weights.append(part_weights)
                maxima.append(part_max)
            target_parts = [own_targets] + [
                exchange(rows, query=turn) for turn, rows in enumerate(leaving, 1)
            ]
        else:
            new_state, *chunk_parts, part_weights, part_max = call(
                next_body,
                [(CORES * packed_rows + query_shape[0], width)] + forward_shapes,
                "update_forward",
                2 * matmul_cost,
                states + query_parts + grads + tiles,
                chunk_scratch,
            )
            states, weights, maxima = [new_state], [part_weights], [part_max]
            arrived = {
                turn: exchange(chunk_parts[turn], page=CORES * turn)
                for turn in turns
            }
            sums = chunk_parts[:1] + list(arrived.values())
            new_states = states + [
                exchange(states[0], query=turn) for turn in range(1, query_devices)
            ]
        (merged,) = call(
            merge_body if repeat else first_merge_body,
            [chunk_shape],
            "merge",
            2**20,
            target_parts + sums,
        )
        all_merged = [merged] + [exchange(merged, page=CORES * turn) for turn in reversed(turns)]
        if last:
            all_merged = call(
                join_body, [(width + TAIL, query_rows)], "join", 2**20, all_merged, chunk_scratch
            )
            all_joined = [
                to_device(all_merged[0], query=turn) for turn in range(query_devices)
            ]
        own_grad, mate_grad, squares = call(
            backward_body,
            packed_shapes + [(devices, 1, width)],
            "backward",
            3 * matmul_cost,
            weights + maxima + states + query_parts + list(all_merged),
            scratch=() if last else chunk_scratch,
        )
        grads = [own_grad, mate_grad]
        tiles = [
            lax.all_to_all(
                squares, ("page", "query", "head"), split_axis=0, concat_axis=0, tiled=True
            )
        ]

    other_packs = [
        packs[part] if part == turn else query_part(turn, part)
        for turn in range(1, query_devices)
        for part in range(1, query_devices)
    ]
    operands = new_states + all_joined[1:] + other_packs
    pages = []
    for at, grad in ((1, mate_grad), (0, own_grad)):
        pages += call(
            page_body(at),
            [(query_devices * packed_rows, width)],
            "page_update",
            3 * matmul_cost // 2,
            tiles + [grad] + operands,
            after=pages,
        )
    pages = [pages[1], exchange(pages[0], page=1)]

    def last_body(*refs):
        page_refs, (keys_out, values_out, bias_out) = refs[:CORES], refs[CORES:]
        _, core, me = places()
        for turn, flip in itertools.product(range(query_devices), range(CORES)):
            keys, values, bias = read_pack(part_of(page_refs[flip], turn))
            head = CORES * (me ^ turn) + (core ^ flip)
            keys_out[head] = keys
            values_out[head] = values
            bias_row = jnp.concatenate([bias[row : row + 1] for row in range(bias_rows)], axis=1)
            bias_out[pl.ds(head, 1), :] = bias_row

    return tuple(
        call(
            last_body,
            [compact_keys.shape, compact_values.shape, slot_bias.shape],
            "unpack",
            2**20,
            pages,
        )
    )


def from_partner(value, axis, stride):
    mask = 2**stride
    pairs = [(source, source ^ mask) for source in range(lax.axis_size(axis))]
    return lax.ppermute(value, axis, pairs)


def squared_sums(grad_keys, grad_values, grad_bias):
    return jnp.stack(
        [
            jnp.sum(grad_keys * grad_keys),
            jnp.sum(grad_values * grad_values),
            jnp.sum(grad_bias * grad_bias),
        ]
    )


def apply_update(states, grads, totals, entry_count, slot_total):
    key_state, value_state, bias_state = states
    grad_keys, grad_values, grad_bias = grads
    rms_keys = jnp.sqrt(totals[0] / entry_count + EPSILON)
    rms_values = jnp.sqrt(totals[1] / entry_count + EPSILON)
    rms_bias = jnp.sqrt(totals[2] / slot_total + EPSILON)
    return (
        key_state - RATE_KEYS * grad_keys / rms_keys,
        value_state - RATE_VALUES * grad_values / rms_values,
        bias_state - RATE_BIAS * grad_bias / rms_bias,
    )


def local_gradients(queries, targets, visible, compact_keys, compact_values, slot_bias):
    score_scale = 1.0 / math.sqrt(queries.shape[2])
    scores = jnp.einsum("hqd,hsd->hqs", queries, compact_keys, precision=HIGHEST) * score_scale
    scores = jnp.where(visible, scores + slot_bias[:, None, :], MASKED)
    local_max = jnp.max(scores, axis=2)
    row_max = lax.pmax(local_max, "page")
    weights = jnp.where(visible, jnp.exp(scores - row_max[:, :, None]), 0.0)
    local_sum = jnp.einsum("hqs,hsd->hqd", weights, compact_values, precision=HIGHEST)
    row_total, row_sum = lax.psum((jnp.sum(weights, axis=2), local_sum), "page")
    attention = weights / row_total[:, :, None]
    output = row_sum / row_total[:, :, None]
    residual = output - targets
    grad_values = jnp.einsum("hqs,hqd->hsd", attention, residual, precision=HIGHEST)
    row_delta = jnp.sum(residual * output, axis=2)
    grad_probs = jnp.einsum("hqd,hsd->hqs", residual, compact_values, precision=HIGHEST)
    grad_scores = attention * (grad_probs - row_delta[:, :, None])
    grad_bias = jnp.sum(grad_scores, axis=1)
    grad_keys = jnp.einsum("hqs,hqd->hsd", grad_scores, queries, precision=HIGHEST) * score_scale
    return (grad_keys, grad_values, grad_bias)


def per_device(queries, compact_keys, compact_values, slot_bias, targets, positions, assignment):
    page_number = assignment[lax.axis_index("page")]
    local_heads = compact_keys.shape[0]
    slot_total = local_heads * lax.axis_size("head") * compact_keys.shape[1] * lax.axis_size("page")
    entry_count = slot_total * compact_keys.shape[2]
    query_count = lax.axis_size("query")
    heads_kept = max(local_heads // query_count, 1)
    query_parts = max(query_count // local_heads, 1)
    part_rows = queries.shape[1] // query_parts

    def split_items(array):
        width = array.shape[2]
        array = array.reshape(local_heads // heads_kept, heads_kept, query_parts, part_rows, width)
        array = jnp.transpose(array, (0, 2, 1, 3, 4))
        return array.reshape(query_count, heads_kept, part_rows, width)

    def join_items(array):
        width = array.shape[3]
        array = jnp.transpose(array, (1, 0, 2, 3))
        return array.reshape(heads_kept, query_count * part_rows, width)

    position_column = positions.astype(jnp.float32)[:, :, None]
    got_queries, got_targets, got_positions = (
        lax.all_to_all(split_items(queries), "query", split_axis=0, concat_axis=0, tiled=True),
        lax.all_to_all(split_items(targets), "query", split_axis=0, concat_axis=0, tiled=True),
        lax.all_to_all(
            split_items(position_column), "query", split_axis=0, concat_axis=0, tiled=True
        ),
    )
    group_queries = join_items(got_queries)
    group_targets = join_items(got_targets)
    group_positions = join_items(got_positions)[:, :, 0]
    visible = (page_number.astype(jnp.float32) <= jnp.floor(group_positions / PAGE_LEN))[:, :, None]
    query_index = lax.axis_index("query")
    first_head = query_index // query_parts * heads_kept
    key_state = lax.dynamic_slice_in_dim(compact_keys, first_head, heads_kept, 0)
    value_state = lax.dynamic_slice_in_dim(compact_values, first_head, heads_kept, 0)
    bias_state = lax.dynamic_slice_in_dim(slot_bias, first_head, heads_kept, 0)
    counted = (query_index % query_parts == 0).astype(jnp.float32)
    for repeat in range(STEPS):
        grads = local_gradients(
            group_queries, group_targets, visible, key_state, value_state, bias_state
        )
        for bit in range(query_parts.bit_length() - 1):
            partner = from_partner((grads[0], grads[1], grads[2]), "query", bit)
            grads = (grads[0] + partner[0], grads[1] + partner[1], grads[2] + partner[2])
        totals = lax.psum(
            squared_sums(grads[0], grads[1], grads[2]) * counted, ("page", "query", "head")
        )
        key_state, value_state, bias_state = apply_update(
            (key_state, value_state, bias_state), grads, totals, entry_count, slot_total
        )
    all_keys, all_values, all_bias = (
        lax.all_gather(key_state, "query", axis=0, tiled=True),
        lax.all_gather(value_state, "query", axis=0, tiled=True),
        lax.all_gather(bias_state, "query", axis=0, tiled=True),
    )
    slot_rows = compact_keys.shape[1]
    head_width = compact_keys.shape[2]
    all_keys = all_keys.reshape(
        local_heads // heads_kept, query_parts, heads_kept, slot_rows, head_width
    )[:, 0]
    all_values = all_values.reshape(
        local_heads // heads_kept, query_parts, heads_kept, slot_rows, head_width
    )[:, 0]
    all_bias = all_bias.reshape(local_heads // heads_kept, query_parts, heads_kept, slot_rows)[:, 0]
    return (
        all_keys.reshape(local_heads, slot_rows, head_width),
        all_values.reshape(local_heads, slot_rows, head_width),
        all_bias.reshape(local_heads, slot_rows),
    )


def solution(mesh):
    placed = (
        P("head", "query", None),
        P("head", "page", None),
        P("head", "page", None),
        P("head", "page"),
        P("head", "query", None),
        P("head", "query"),
        P(),
    )

    def program(*args):
        plan = direct_per_device if direct_plan_fits(mesh, args[0], args[1]) else per_device
        return jax.shard_map(
            plan,
            mesh=mesh,
            in_specs=placed,
            out_specs=(P("head", "page", None), P("head", "page", None), P("head", "page")),
            check_vma=False,
        )(*args)

    return program
```

```python
import itertools
import math

import jax
import jax.numpy as jnp
from jax import lax
from jax.experimental import pallas as pl
from jax.experimental.pallas import tpu as pltpu
from jax.sharding import PartitionSpec as P

STEPS = 2
PAGE_LEN = 32768


MASKED = -1e30
EPSILON = 1e-06
RATE_KEYS = 0.05
RATE_VALUES = 0.05
RATE_BIAS = 0.2
HIGHEST = lax.Precision.HIGHEST
TAIL = 8
CORES = 2


def exchange(value, **masks):
    axes = tuple(masks)
    sizes = [lax.axis_size(axis) for axis in axes]

    def flat(place):
        index = 0
        for size, at in zip(sizes, place):
            index = index * size + at
        return index

    pairs = [
        (flat(place), flat([at ^ mask for at, mask in zip(place, masks.values())]))
        for place in itertools.product(*map(range, sizes))
    ]
    return lax.ppermute(value, axes, pairs)


def halves(value):
    high = value.astype(jnp.bfloat16)
    return high, (value - high.astype(jnp.float32)).astype(jnp.bfloat16)


def one_pass(left, right, left_dim, right_dim):
    return lax.dot_general(
        left,
        right,
        (((left_dim,), (right_dim,)), ((), ())),
        preferred_element_type=jnp.float32,
    )


def dot_deep(left, right, left_dim, right_dim):
    left = jnp.concatenate([left[0], left[1], left[0]], axis=left_dim)
    right = jnp.concatenate([right[0], right[0], right[1]], axis=right_dim)
    return one_pass(left, right, left_dim, right_dim)


def dot_narrow(left, right, left_dim, right_dim):
    both = one_pass(
        left[0], jnp.concatenate(right, axis=1 - right_dim), left_dim, right_dim
    )
    count = both.shape[1] // 2
    cross = both[:, count:] + one_pass(left[1], right[0], left_dim, right_dim)
    return both[:, :count] + cross


def dot_low(left, right, left_dim, right_dim):
    both = one_pass(jnp.concatenate(left, axis=1 - left_dim), right[0], left_dim, right_dim)
    count = both.shape[0] // 2
    cross = both[count:, :] + one_pass(left[0], right[1], left_dim, right_dim)
    return both[:count, :] + cross


def call(body, out_shapes, name, cost, operands, scratch=(), after=(), space=pltpu.VMEM, vmem=32):
    spaces = [space] * len(operands) + [pl.ANY] * len(after)
    count = len(operands)

    def without_after(*refs):
        body(*refs[:count], *refs[count + len(after) :])

    return pl.pallas_call(
        without_after,
        out_shape=[jax.ShapeDtypeStruct(shape, jnp.float32) for shape in out_shapes],
        in_specs=[pl.BlockSpec(memory_space=space) for space in spaces],
        out_specs=[pl.BlockSpec(memory_space=pltpu.VMEM) for _ in out_shapes],
        scratch_shapes=scratch,
        compiler_params=pltpu.CompilerParams(vmem_limit_bytes=vmem * 2**20),
        cost_estimate=pl.CostEstimate(flops=cost, bytes_accessed=2**20, transcendentals=0),
        name=name,
    )(*operands, *after)


def row_as_tail(row, width):
    rows = [row[:, at : at + width] for at in range(0, row.shape[1], width)]
    rows.append(jnp.zeros((TAIL - len(rows), width), row.dtype))
    return jnp.concatenate(rows, axis=0)


def tail_as_row(ref, start, count):
    return jnp.concatenate([ref[start + at : start + at + 1, :] for at in range(count)], axis=1)


def row_as_column(row, width):
    parts = []
    for at in range(0, row.shape[1], width):
        parts.append(jnp.broadcast_to(row[:, at : at + width], (width, width)).T)
    return jnp.concatenate(parts, axis=0)


def column_sums(value, width):
    groups = [value[:, at : at + width] for at in range(0, value.shape[1], width)]
    partial = sum(groups[1:], groups[0])
    blocks = [
        jnp.sum(partial[at : at + width, :].T, axis=0, keepdims=True)
        for at in range(0, value.shape[0], width)
    ]
    return jnp.concatenate(blocks, axis=1)


def direct_plan_fits(mesh, queries, compact_keys):
    sizes = [mesh.shape[axis] for axis in ("page", "query", "head")]
    pages, query_devices, head_devices = sizes
    local_heads = queries.shape[0] // head_devices
    part_rows = queries.shape[1] // query_devices
    slot_rows = compact_keys.shape[1] // pages
    width = queries.shape[2]
    if any(size & (size - 1) for size in sizes) or pages < CORES or width % 128:
        return False
    if local_heads != CORES * query_devices:
        return False
    ranks = pages // CORES
    chunk = part_rows * query_devices // ranks
    return (
        part_rows * query_devices % ranks == 0
        and chunk % 128 == 0
        and part_rows % (8 * ranks) == 0
        and (part_rows // ranks % 128 == 0 or 1024 % (part_rows // ranks * 8) == 0)
        and slot_rows % width == 0
        and part_rows % width == 0
        and max(slot_rows, part_rows) < TAIL * width
    )


def direct_per_device(
    queries, compact_keys, compact_values, slot_bias, targets, positions, assignment
):
    local_heads, part_rows, width = queries.shape
    slot_rows = compact_keys.shape[1]
    query_devices = lax.axis_size("query")
    head_devices = lax.axis_size("head")
    ranks = lax.axis_size("page") // CORES
    query_rows = part_rows * query_devices
    chunk, piece = query_rows // ranks, part_rows // ranks
    turns = [ranks // 2] + [turn for turn in reversed(range(1, ranks)) if turn != ranks // 2]
    slot_total = local_heads * head_devices * slot_rows * lax.axis_size("page")
    entry_total = slot_total * width
    score_scale = 1.0 / math.sqrt(width)
    slots = CORES * slot_rows
    devices = ranks * CORES * query_devices * head_devices
    pos_rows = part_rows // width
    bias_rows = slot_rows // width
    packed_rows = 2 * slot_rows + TAIL
    packed_shapes = [(packed_rows, width)] * 2
    matmul_cost = 3 * 2 * slots * query_rows * width

    def places():
        page = lax.axis_index("page")
        return page // CORES, page % CORES, lax.axis_index("query")

    def to_device(value, **masks):
        masks = {axis: mask for axis, mask in masks.items() if mask}
        return exchange(value, **masks) if masks else value

    def pack_queries(head, rank, queries, targets, out):
        rows = pl.ds(pl.multiple_of(rank * piece, piece), piece)
        return [
            (queries.at[head], out.at[pl.ds(0, part_rows)]),
            (targets.at[head, rows], out.at[pl.ds(part_rows, piece)]),
        ]

    def pack_state(head, keys, values, out):
        return [
            (keys.at[head], out.at[pl.ds(0, slot_rows)]),
            (values.at[head], out.at[pl.ds(slot_rows, slot_rows)]),
        ]

    def start_all(copies, sems, first=0):
        copies = [
            pltpu.make_async_copy(source, target, sems.at[first + at])
            for at, (source, target) in enumerate(copies)
        ]
        for copy in copies:
            copy.start()
        return copies

    def position_tail(head, positions_ref):
        return row_as_tail(positions_ref[pl.ds(head, 1), :].astype(jnp.float32), width)

    def state_tail(head, page, bias_ref, assignment_ref):
        page_start = (assignment_ref[page] * PAGE_LEN).astype(jnp.float32)
        tail = row_as_tail(bias_ref[pl.ds(head, 1), :], width)
        return jnp.concatenate(
            [tail[: TAIL - 1], jnp.full((1, width), page_start, jnp.float32)], axis=0
        )

    def send_body(
        queries, keys, values, biases, targets, positions, assignment, state_out, *refs
    ):
        query_outs = refs[: query_devices - 1]
        bias_ref, positions_ref, assignment_ref, sems = refs[query_devices - 1 :]
        rank, core, me = places()
        heads = [CORES * (me ^ turn) + core for turn in range(1, query_devices)]
        mate_head = CORES * me + (core ^ 1)
        small = start_all(
            [(assignment, assignment_ref), (positions, positions_ref), (biases, bias_ref)], sems
        )
        copies = pack_state(mate_head, keys, values, state_out)
        for head, out in zip(heads, query_outs):
            copies += pack_queries(head, rank, queries, targets, out)
        copies = start_all(copies, sems, 3)
        for copy in small:
            copy.wait()
        state_out[2 * slot_rows :, :] = state_tail(
            mate_head, CORES * rank + core, bias_ref, assignment_ref
        )
        for head, out in zip(heads, query_outs):
            out[part_rows + piece :, :] = position_tail(head, positions_ref)
        for copy in copies:
            copy.wait()

    def own_body(
        queries, keys, values, biases, targets, positions, assignment, state_out, query_out, *refs
    ):
        bias_ref, positions_ref, assignment_ref, sems = refs
        rank, core, me = places()
        head = CORES * me + core
        small = start_all(
            [(assignment, assignment_ref), (positions, positions_ref), (biases, bias_ref)], sems
        )
        copies = pack_state(head, keys, values, state_out)
        copies += pack_queries(head, rank, queries, targets, query_out)
        copies = start_all(copies, sems, 3)
        for copy in small:
            copy.wait()
        state_out[2 * slot_rows :, :] = state_tail(
            head, CORES * rank + core, bias_ref, assignment_ref
        )
        query_out[part_rows + piece :, :] = position_tail(head, positions_ref)
        for copy in copies:
            copy.wait()

    state_shape, query_shape = (packed_rows, width), (part_rows + piece + TAIL, width)
    small_scratch = [
        pltpu.VMEM(slot_bias.shape, jnp.float32),
        pltpu.VMEM(positions.shape, jnp.int32),
        pltpu.SMEM(assignment.shape, jnp.int32),
    ]
    arguments = [
        queries, compact_keys, compact_values, slot_bias, targets, positions, assignment
    ]
    mate_state, *sent_queries = call(
        send_body,
        [state_shape] + [query_shape] * (query_devices - 1),
        "pack",
        2**20,
        arguments,
        small_scratch + [pltpu.SemaphoreType.DMA((3 + 2 * query_devices,))],
        space=pl.ANY,
        vmem=60,
    )
    own_state, own_queries = call(
        own_body,
        [state_shape, query_shape],
        "own",
        2**24,
        arguments,
        small_scratch + [pltpu.SemaphoreType.DMA((7,))],
        space=pl.ANY,
    )
    packs = [own_queries] + list(sent_queries)

    def query_part(turn, part):
        return to_device(packs[part], query=turn ^ part)

    query_parts = [query_part(0, part) for part in range(query_devices)]
    states = [own_state, exchange(mate_state, page=1)]

    def in_columns(parts, axis):
        return jnp.concatenate(
            [
                lax.slice_in_dim(part, at * piece, (at + 1) * piece, axis=axis)
                for at in range(ranks)
                for part in parts
            ],
            axis=axis,
        )

    def read_queries(query_refs):
        return halves(in_columns([ref[:part_rows, :] for ref in query_refs], 0))

    def part_of(ref, at):
        return ref.at[pl.ds(at * packed_rows, packed_rows)]

    def parts_of(refs):
        return refs if len(refs) == CORES else [part_of(refs[0], at) for at in range(CORES)]

    def step_sizes(tile_refs):
        row = jnp.sum(tile_refs[0][...], axis=0)
        return (
            RATE_KEYS / jnp.sqrt(row[:, 0:1] / entry_total + EPSILON),
            RATE_VALUES / jnp.sqrt(row[:, 1:2] / entry_total + EPSILON),
            RATE_BIAS / jnp.sqrt(row[:, 2:3] / slot_total + EPSILON),
        )

    def read_pack(ref):
        return ref[:slot_rows, :], ref[slot_rows : 2 * slot_rows, :], ref[2 * slot_rows :, :]

    def store_pack(ref, values):
        ref[:slot_rows, :] = values[0]
        ref[slot_rows : 2 * slot_rows, :] = values[1]
        ref[2 * slot_rows :, :] = values[2]

    def updated(state, grads, sizes):
        return [value - size * grad for value, grad, size in zip(state, grads, sizes)]

    def page_scores(ref, queries, positions):
        scores = dot_deep(halves(ref[:slot_rows, :]), queries, 1, 1) * score_scale
        bias = row_as_column(tail_as_row(ref, 2 * slot_rows, bias_rows), width)
        scores = scores + jnp.concatenate([bias] * (positions.shape[1] // width), axis=1)
        page_start = ref[packed_rows - 1 : packed_rows, 0:1]
        visible = jnp.broadcast_to(positions >= page_start, scores.shape)
        return jnp.where(visible, scores, MASKED), visible

    def read_positions(query_refs):
        return in_columns(
            [tail_as_row(ref, part_rows + piece, pos_rows) for ref in query_refs], 1
        )

    def forward(state_refs, query_refs, chunk_outs, weights_out, max_out, chunks):
        rank, _, _ = places()
        all_queries, positions = read_queries(query_refs), read_positions(query_refs)
        all_scores, all_visible = [], []
        for at, ref in enumerate(state_refs):
            scores, visible = page_scores(ref, all_queries, positions)
            all_scores.append(scores)
            all_visible.append(visible)
        row_max = jnp.max(all_scores[0], axis=0, keepdims=True)
        for scores in all_scores[1:]:
            row_max = jnp.maximum(row_max, jnp.max(scores, axis=0, keepdims=True))
        row_total = jnp.zeros_like(row_max)
        row_sum = jnp.zeros((width, query_rows), jnp.float32)
        for at, ref in enumerate(state_refs):
            weights = jnp.where(all_visible[at], jnp.exp(all_scores[at] - row_max), 0.0)
            weights_out[at * slot_rows : (at + 1) * slot_rows, :] = weights
            row_total = row_total + jnp.sum(weights, axis=0, keepdims=True)
            values = halves(ref[slot_rows : 2 * slot_rows, :])
            row_sum = row_sum + dot_low(values, halves(weights), 0, 0)
        max_out[...] = jnp.broadcast_to(row_max, (TAIL, query_rows))
        tail = jnp.concatenate(
            [row_max, row_total, jnp.zeros((TAIL - 2, query_rows), jnp.float32)], axis=0
        )
        for at in range(ranks):
            columns = slice(at * chunk, (at + 1) * chunk)
            chunks[at, :width, :] = row_sum[:, columns]
            chunks[at, width:, :] = tail[:, columns]
        for turn in range(ranks):
            chunk_outs[turn][...] = chunks[rank ^ turn]

    chunk_shape = (width + TAIL, chunk)
    forward_shapes = [chunk_shape] * ranks + [(slots, query_rows), (TAIL, query_rows)]
    chunk_scratch = [pltpu.VMEM((ranks,) + chunk_shape, jnp.float32)]

    fold = max(1, 128 // piece)
    folded, columns = width // fold, fold * piece
    piece_shape = (folded + TAIL, columns)
    piece_scratch = [pltpu.VMEM((ranks,) + piece_shape, jnp.float32)]

    def fold_rows(value):
        groups = [value[at * folded : (at + 1) * folded, :] for at in range(fold)]
        return jnp.concatenate(groups, axis=1)

    def unfold_rows(value):
        groups = [value[:, at * piece : (at + 1) * piece] for at in range(fold)]
        return jnp.concatenate(groups, axis=0)

    def rows_tail(rows):
        empty = jnp.zeros((TAIL - len(rows), columns), jnp.float32)
        return jnp.concatenate(rows + [empty], axis=0)

    def part_body(*refs):
        state_refs, (query_ref, *refs) = refs[:CORES], refs[CORES:]
        piece_outs, (weights_out, max_out, pieces) = refs[:ranks], refs[ranks:]
        rank, _, _ = places()
        queries = halves(query_ref[:part_rows, :])
        position_row = tail_as_row(query_ref, part_rows + piece, pos_rows)
        all_scores, all_visible = [], []
        for ref in state_refs:
            scores, visible = page_scores(ref, queries, position_row)
            all_scores.append(scores)
            all_visible.append(visible)
        row_max = jnp.max(all_scores[0], axis=0, keepdims=True)
        for scores in all_scores[1:]:
            row_max = jnp.maximum(row_max, jnp.max(scores, axis=0, keepdims=True))
        row_total = jnp.zeros_like(row_max)
        row_sum = jnp.zeros((width, part_rows), jnp.float32)
        for at, ref in enumerate(state_refs):
            weights = jnp.where(all_visible[at], jnp.exp(all_scores[at] - row_max), 0.0)
            weights_out[at * slot_rows : (at + 1) * slot_rows, :] = weights
            row_total = row_total + jnp.sum(weights, axis=0, keepdims=True)
            values = halves(ref[slot_rows : 2 * slot_rows, :])
            row_sum = row_sum + dot_low(values, halves(weights), 0, 0)
        max_out[...] = jnp.broadcast_to(row_max, (TAIL, part_rows))
        for at in range(ranks):
            own = slice(at * piece, (at + 1) * piece)
            pieces[at, :folded, :] = fold_rows(row_sum[:, own])
            pieces[at, folded:, :] = rows_tail(
                [jnp.concatenate([row[:, own]] * fold, axis=1) for row in (row_max, row_total)]
            )
        for turn in range(ranks):
            piece_outs[turn][...] = pieces[rank ^ turn]

    part_shapes = [piece_shape] * ranks + [(slots, part_rows), (TAIL, part_rows)]

    def next_body(*refs):
        state_refs, refs = refs[:2], refs[2:]
        query_refs, refs = refs[:query_devices], refs[query_devices:]
        grad_refs, refs = refs[:2], refs[2:]
        tile_refs, refs = refs[: len(tiles)], refs[len(tiles) :]
        refs[0][CORES * packed_rows :, :] = query_refs[0][...]
        state_outs, refs = parts_of(refs[:1]), refs[1:]
        chunk_outs, refs = refs[:ranks], refs[ranks:]
        sizes = step_sizes(tile_refs)
        for at in range(2):
            state = read_pack(state_refs[at])
            store_pack(state_outs[at], updated(state, read_pack(grad_refs[at]), sizes))
        forward(state_outs, query_refs, chunk_outs, *refs)

    def merged_chunk(query_refs, sums, maxima, totals, out):
        targets = jnp.concatenate(
            [ref[part_rows : part_rows + piece, :] for ref in query_refs], axis=0
        )
        row_max = maxima[0]
        for other in maxima[1:]:
            row_max = jnp.maximum(row_max, other)
        row_total = jnp.zeros_like(row_max)
        row_sum = jnp.zeros((width, chunk), jnp.float32)
        for part_sum, part_max, part_total in zip(sums, maxima, totals):
            factor = jnp.exp(part_max - row_max)
            row_total = row_total + part_total * factor
            row_sum = row_sum + part_sum * factor
        output = row_sum / row_total
        residual = output - targets.T
        row_delta = jnp.sum(residual * output, axis=0, keepdims=True)
        out[:width, :] = residual
        out[width:, :] = jnp.concatenate(
            [row_max, row_total, row_delta, jnp.zeros((TAIL - 3, chunk), jnp.float32)], axis=0
        )

    def first_merge_body(*refs):
        query_refs, (*piece_refs, merged_out) = refs[:query_devices], refs[query_devices:]

        def joined(read):
            return [
                jnp.concatenate([read(ref) for ref in piece_refs[turn::ranks]], axis=1)
                for turn in range(ranks)
            ]

        merged_chunk(
            query_refs,
            joined(lambda ref: unfold_rows(ref[:folded, :])),
            joined(lambda ref: ref[folded : folded + 1, :piece]),
            joined(lambda ref: ref[folded + 1 : folded + 2, :piece]),
            merged_out,
        )

    def merge_body(*refs):
        query_refs, (*chunk_refs, merged_out) = refs[:query_devices], refs[query_devices:]
        merged_chunk(
            query_refs,
            [ref[:width, :] for ref in chunk_refs],
            [ref[width : width + 1, :] for ref in chunk_refs],
            [ref[width + 1 : width + 2, :] for ref in chunk_refs],
            merged_out,
        )

    def page_gradients(weights, factor, state_ref, all_queries, residual, row_delta):
        attention = weights * factor
        grad_values = dot_narrow(halves(attention), residual, 1, 1)
        grad_probs = dot_deep(halves(state_ref[slot_rows : 2 * slot_rows, :]), residual, 1, 0)
        grad_scores = attention * (grad_probs - row_delta)
        grad_keys = dot_narrow(halves(grad_scores), all_queries, 1, 0) * score_scale
        grad_bias = column_sums(grad_scores, width)
        return grad_keys, grad_values, row_as_tail(grad_bias, width)

    def split_merged(joined):
        row_max, row_total, row_delta = (
            joined[width + at : width + at + 1, :] for at in range(3)
        )
        return halves(joined[:width, :]), row_max, row_total, row_delta

    def read_chunks(merged_refs, chunks):
        rank, _, _ = places()
        for turn, ref in zip([0] + turns[::-1], merged_refs):
            chunks[rank ^ turn] = ref[...]
        return [chunks[at] for at in range(ranks)]

    def join_body(*refs):
        *merged_refs, joined_out, chunks = refs
        joined_out[...] = jnp.concatenate(read_chunks(merged_refs, chunks), axis=1)

    def backward_body(*refs):
        weights_refs, refs = refs[: len(weights)], refs[len(weights) :]
        max_refs, refs = refs[: len(weights)], refs[len(weights) :]
        state_refs, refs = parts_of(refs[: len(states)]), refs[len(states) :]
        query_refs, refs = refs[:query_devices], refs[query_devices:]
        merged_refs, refs = refs[: len(all_merged)], refs[len(all_merged) :]
        grad_outs, (squares_out, *scratch) = refs[:2], refs[2:]
        if len(states) < CORES:
            joined = merged_refs[0][...]
            all_queries = read_queries(query_refs)
        else:
            chunks = read_chunks(merged_refs, *scratch)
            joined = jnp.concatenate(
                [
                    value[:, part * piece : (part + 1) * piece]
                    for part in range(query_devices)
                    for value in chunks
                ],
                axis=1,
            )
            all_queries = halves(
                jnp.concatenate([ref[:part_rows, :] for ref in query_refs], axis=0)
            )
        residual, row_max, row_total, row_delta = split_merged(joined)
        maxima = jnp.concatenate([ref[0:1, :] for ref in max_refs], axis=1)
        factor = jnp.exp(maxima - row_max) / row_total
        squares = [jnp.zeros((1, width), jnp.float32)] * 3
        for at, (ref, out) in enumerate(zip(state_refs, grad_outs)):
            rows = slice(at * slot_rows, (at + 1) * slot_rows)
            page_weights = jnp.concatenate([part[rows, :] for part in weights_refs], axis=1)
            grads = page_gradients(page_weights, factor, ref, all_queries, residual, row_delta)
            store_pack(out, grads)
            for which, grad in enumerate(grads):
                squares[which] = squares[which] + jnp.sum(grad * grad, axis=0, keepdims=True)
        lanes = lax.broadcasted_iota(jnp.int32, (1, width), 1)
        row = jnp.zeros((1, width), jnp.float32)
        for which, square in enumerate(squares):
            row = jnp.where(lanes == which, jnp.sum(square, axis=1, keepdims=True), row)
        for at in range(devices):
            squares_out[at] = row

    def page_body(at):
        def body(tile_ref, grad_ref, own_state_ref, *refs):
            state_refs, refs = refs[: query_devices - 1], refs[query_devices - 1 :]
            joined_refs, (*pack_refs, out) = refs[: query_devices - 1], refs[query_devices - 1 :]
            sizes = step_sizes([tile_ref])
            state = read_pack(part_of(own_state_ref, at))
            store_pack(part_of(out, 0), updated(state, read_pack(grad_ref), sizes))
            for turn, (state_ref, joined_ref) in enumerate(zip(state_refs, joined_refs), 1):
                query_refs = [state_ref.at[pl.ds(CORES * packed_rows, query_shape[0])]]
                query_refs += pack_refs[(turn - 1) * (query_devices - 1) :][: query_devices - 1]
                residual, row_max, row_total, row_delta = split_merged(joined_ref[...])
                all_queries = read_queries(query_refs)
                ref = part_of(state_ref, at)
                scores, visible = page_scores(ref, all_queries, read_positions(query_refs))
                weights = jnp.where(visible, jnp.exp(scores - row_max), 0.0)
                grads = page_gradients(
                    weights, 1.0 / row_total, ref, all_queries, residual, row_delta
                )
                store_pack(part_of(out, turn), updated(read_pack(ref), grads, sizes))

        return body

    for repeat in range(STEPS):
        last = repeat == STEPS - 1
        if repeat == 0:
            sums, weights, maxima = [], [], []
            for query_pack in query_parts:
                *pieces, part_weights, part_max = call(
                    part_body,
                    part_shapes,
                    "forward",
                    2 * matmul_cost // query_devices,
                    states + [query_pack],
                    piece_scratch,
                    after=maxima[-1:],
                )
                arrived = {
                    turn: exchange(pieces[turn], page=CORES * turn)
                    for turn in turns
                }
                sums += list(arrived.values()) + pieces[:1]
                weights.append(part_weights)
                maxima.append(part_max)
        else:
            new_state, *chunk_parts, part_weights, part_max = call(
                next_body,
                [(CORES * packed_rows + query_shape[0], width)] + forward_shapes,
                "update_forward",
                2 * matmul_cost,
                states + query_parts + grads + tiles,
                chunk_scratch,
            )
            states, weights, maxima = [new_state], [part_weights], [part_max]
            arrived = {
                turn: exchange(chunk_parts[turn], page=CORES * turn)
                for turn in turns
            }
            sums = chunk_parts[:1] + list(arrived.values())
            new_states = states + [
                exchange(states[0], query=turn) for turn in range(1, query_devices)
            ]
        (merged,) = call(
            merge_body if repeat else first_merge_body,
            [chunk_shape],
            "merge",
            2**20,
            query_parts + sums,
        )
        all_merged = [merged] + [exchange(merged, page=CORES * turn) for turn in reversed(turns)]
        if last:
            all_merged = call(
                join_body, [(width + TAIL, query_rows)], "join", 2**20, all_merged, chunk_scratch
            )
            all_joined = [
                to_device(all_merged[0], query=turn) for turn in range(query_devices)
            ]
        own_grad, mate_grad, squares = call(
            backward_body,
            packed_shapes + [(devices, 1, width)],
            "backward",
            3 * matmul_cost,
            weights + maxima + states + query_parts + list(all_merged),
            scratch=() if last else chunk_scratch,
        )
        grads = [own_grad, mate_grad]
        tiles = [
            lax.all_to_all(
                squares, ("head", "query", "page"), split_axis=0, concat_axis=0, tiled=True
            )
        ]

    other_packs = [
        packs[part] if part == turn else query_part(turn, part)
        for turn in range(1, query_devices)
        for part in range(1, query_devices)
    ]
    operands = new_states + all_joined[1:] + other_packs
    pages = []
    for at, grad in ((1, mate_grad), (0, own_grad)):
        pages += call(
            page_body(at),
            [(query_devices * packed_rows, width)],
            "page_update",
            3 * matmul_cost // 2,
            tiles + [grad] + operands,
            after=pages,
        )
    pages = [pages[1], exchange(pages[0], page=1)]

    def last_body(*refs):
        page_refs, (keys_out, values_out, bias_out) = refs[:CORES], refs[CORES:]
        _, core, me = places()
        for turn, flip in itertools.product(range(query_devices), range(CORES)):
            keys, values, bias = read_pack(part_of(page_refs[flip], turn))
            head = CORES * (me ^ turn) + (core ^ flip)
            keys_out[head] = keys
            values_out[head] = values
            bias_row = jnp.concatenate([bias[row : row + 1] for row in range(bias_rows)], axis=1)
            bias_out[pl.ds(head, 1), :] = bias_row

    return tuple(
        call(
            last_body,
            [compact_keys.shape, compact_values.shape, slot_bias.shape],
            "unpack",
            2**20,
            pages,
        )
    )


def from_partner(value, axis, stride):
    mask = 2**stride
    pairs = [(source, source ^ mask) for source in range(lax.axis_size(axis))]
    return lax.ppermute(value, axis, pairs)


def squared_sums(grad_keys, grad_values, grad_bias):
    return jnp.stack(
        [
            jnp.sum(grad_keys * grad_keys),
            jnp.sum(grad_values * grad_values),
            jnp.sum(grad_bias * grad_bias),
        ]
    )


def apply_update(states, grads, totals, entry_count, slot_total):
    key_state, value_state, bias_state = states
    grad_keys, grad_values, grad_bias = grads
    rms_keys = jnp.sqrt(totals[0] / entry_count + EPSILON)
    rms_values = jnp.sqrt(totals[1] / entry_count + EPSILON)
    rms_bias = jnp.sqrt(totals[2] / slot_total + EPSILON)
    return (
        key_state - RATE_KEYS * grad_keys / rms_keys,
        value_state - RATE_VALUES * grad_values / rms_values,
        bias_state - RATE_BIAS * grad_bias / rms_bias,
    )


def local_gradients(queries, targets, visible, compact_keys, compact_values, slot_bias):
    score_scale = 1.0 / math.sqrt(queries.shape[2])
    scores = jnp.einsum("hqd,hsd->hqs", queries, compact_keys, precision=HIGHEST) * score_scale
    scores = jnp.where(visible, scores + slot_bias[:, None, :], MASKED)
    local_max = jnp.max(scores, axis=2)
    row_max = lax.pmax(local_max, "page")
    weights = jnp.where(visible, jnp.exp(scores - row_max[:, :, None]), 0.0)
    local_sum = jnp.einsum("hqs,hsd->hqd", weights, compact_values, precision=HIGHEST)
    row_total, row_sum = lax.psum((jnp.sum(weights, axis=2), local_sum), "page")
    attention = weights / row_total[:, :, None]
    output = row_sum / row_total[:, :, None]
    residual = output - targets
    grad_values = jnp.einsum("hqs,hqd->hsd", attention, residual, precision=HIGHEST)
    row_delta = jnp.sum(residual * output, axis=2)
    grad_probs = jnp.einsum("hqd,hsd->hqs", residual, compact_values, precision=HIGHEST)
    grad_scores = attention * (grad_probs - row_delta[:, :, None])
    grad_bias = jnp.sum(grad_scores, axis=1)
    grad_keys = jnp.einsum("hqs,hqd->hsd", grad_scores, queries, precision=HIGHEST) * score_scale
    return (grad_keys, grad_values, grad_bias)


def per_device(queries, compact_keys, compact_values, slot_bias, targets, positions, assignment):
    page_number = assignment[lax.axis_index("page")]
    local_heads = compact_keys.shape[0]
    slot_total = local_heads * lax.axis_size("head") * compact_keys.shape[1] * lax.axis_size("page")
    entry_count = slot_total * compact_keys.shape[2]
    query_count = lax.axis_size("query")
    heads_kept = max(local_heads // query_count, 1)
    query_parts = max(query_count // local_heads, 1)
    part_rows = queries.shape[1] // query_parts

    def split_items(array):
        width = array.shape[2]
        array = array.reshape(local_heads // heads_kept, heads_kept, query_parts, part_rows, width)
        array = jnp.transpose(array, (0, 2, 1, 3, 4))
        return array.reshape(query_count, heads_kept, part_rows, width)

    def join_items(array):
        width = array.shape[3]
        array = jnp.transpose(array, (1, 0, 2, 3))
        return array.reshape(heads_kept, query_count * part_rows, width)

    position_column = positions.astype(jnp.float32)[:, :, None]
    got_queries, got_targets, got_positions = (
        lax.all_to_all(split_items(queries), "query", split_axis=0, concat_axis=0, tiled=True),
        lax.all_to_all(split_items(targets), "query", split_axis=0, concat_axis=0, tiled=True),
        lax.all_to_all(
            split_items(position_column), "query", split_axis=0, concat_axis=0, tiled=True
        ),
    )
    group_queries = join_items(got_queries)
    group_targets = join_items(got_targets)
    group_positions = join_items(got_positions)[:, :, 0]
    visible = (page_number.astype(jnp.float32) <= jnp.floor(group_positions / PAGE_LEN))[:, :, None]
    query_index = lax.axis_index("query")
    first_head = query_index // query_parts * heads_kept
    key_state = lax.dynamic_slice_in_dim(compact_keys, first_head, heads_kept, 0)
    value_state = lax.dynamic_slice_in_dim(compact_values, first_head, heads_kept, 0)
    bias_state = lax.dynamic_slice_in_dim(slot_bias, first_head, heads_kept, 0)
    counted = (query_index % query_parts == 0).astype(jnp.float32)
    for repeat in range(STEPS):
        grads = local_gradients(
            group_queries, group_targets, visible, key_state, value_state, bias_state
        )
        for bit in range(query_parts.bit_length() - 1):
            partner = from_partner((grads[0], grads[1], grads[2]), "query", bit)
            grads = (grads[0] + partner[0], grads[1] + partner[1], grads[2] + partner[2])
        totals = lax.psum(
            squared_sums(grads[0], grads[1], grads[2]) * counted, ("page", "query", "head")
        )
        key_state, value_state, bias_state = apply_update(
            (key_state, value_state, bias_state), grads, totals, entry_count, slot_total
        )
    all_keys, all_values, all_bias = (
        lax.all_gather(key_state, "query", axis=0, tiled=True),
        lax.all_gather(value_state, "query", axis=0, tiled=True),
        lax.all_gather(bias_state, "query", axis=0, tiled=True),
    )
    slot_rows = compact_keys.shape[1]
    head_width = compact_keys.shape[2]
    all_keys = all_keys.reshape(
        local_heads // heads_kept, query_parts, heads_kept, slot_rows, head_width
    )[:, 0]
    all_values = all_values.reshape(
        local_heads // heads_kept, query_parts, heads_kept, slot_rows, head_width
    )[:, 0]
    all_bias = all_bias.reshape(local_heads // heads_kept, query_parts, heads_kept, slot_rows)[:, 0]
    return (
        all_keys.reshape(local_heads, slot_rows, head_width),
        all_values.reshape(local_heads, slot_rows, head_width),
        all_bias.reshape(local_heads, slot_rows),
    )


def solution(mesh):
    placed = (
        P("head", "query", None),
        P("head", "page", None),
        P("head", "page", None),
        P("head", "page"),
        P("head", "query", None),
        P("head", "query"),
        P(),
    )

    def program(*args):
        plan = direct_per_device if direct_plan_fits(mesh, args[0], args[1]) else per_device
        return jax.shard_map(
            plan,
            mesh=mesh,
            in_specs=placed,
            out_specs=(P("head", "page", None), P("head", "page", None), P("head", "page")),
            check_vma=False,
        )(*args)

    return program
```

```python
import itertools
import math

import jax
import jax.numpy as jnp
from jax import lax
from jax.experimental import pallas as pl
from jax.experimental.pallas import tpu as pltpu
from jax.sharding import PartitionSpec as P

STEPS = 2
PAGE_LEN = 32768


MASKED = -1e30
EPSILON = 1e-06
RATE_KEYS = 0.05
RATE_VALUES = 0.05
RATE_BIAS = 0.2
HIGHEST = lax.Precision.HIGHEST
TAIL = 8
CORES = 2


def exchange(value, **masks):
    axes = tuple(masks)
    sizes = [lax.axis_size(axis) for axis in axes]

    def flat(place):
        index = 0
        for size, at in zip(sizes, place):
            index = index * size + at
        return index

    pairs = [
        (flat(place), flat([at ^ mask for at, mask in zip(place, masks.values())]))
        for place in itertools.product(*map(range, sizes))
    ]
    return lax.ppermute(value, axes, pairs)


def halves(value):
    high = value.astype(jnp.bfloat16)
    return high, (value - high.astype(jnp.float32)).astype(jnp.bfloat16)


def one_pass(left, right, left_dim, right_dim):
    return lax.dot_general(
        left,
        right,
        (((left_dim,), (right_dim,)), ((), ())),
        preferred_element_type=jnp.float32,
    )


def dot_deep(left, right, left_dim, right_dim):
    left = jnp.concatenate([left[0], left[1], left[0]], axis=left_dim)
    right = jnp.concatenate([right[0], right[0], right[1]], axis=right_dim)
    return one_pass(left, right, left_dim, right_dim)


def dot_narrow(left, right, left_dim, right_dim):
    both = one_pass(
        left[0], jnp.concatenate(right, axis=1 - right_dim), left_dim, right_dim
    )
    count = both.shape[1] // 2
    cross = both[:, count:] + one_pass(left[1], right[0], left_dim, right_dim)
    return both[:, :count] + cross


def dot_low(left, right, left_dim, right_dim):
    both = one_pass(jnp.concatenate(left, axis=1 - left_dim), right[0], left_dim, right_dim)
    count = both.shape[0] // 2
    cross = both[count:, :] + one_pass(left[0], right[1], left_dim, right_dim)
    return both[:count, :] + cross


def call(body, out_shapes, name, cost, operands, scratch=(), after=(), space=pltpu.VMEM, vmem=32):
    spaces = [space] * len(operands) + [pl.ANY] * len(after)
    count = len(operands)

    def without_after(*refs):
        body(*refs[:count], *refs[count + len(after) :])

    return pl.pallas_call(
        without_after,
        out_shape=[
            shape if hasattr(shape, "dtype") else jax.ShapeDtypeStruct(shape, jnp.float32)
            for shape in out_shapes
        ],
        in_specs=[pl.BlockSpec(memory_space=space) for space in spaces],
        out_specs=[pl.BlockSpec(memory_space=pltpu.VMEM) for _ in out_shapes],
        scratch_shapes=scratch,
        compiler_params=pltpu.CompilerParams(vmem_limit_bytes=vmem * 2**20),
        cost_estimate=pl.CostEstimate(flops=cost, bytes_accessed=2**20, transcendentals=0),
        name=name,
    )(*operands, *after)


def row_as_tail(row, width):
    rows = [row[:, at : at + width] for at in range(0, row.shape[1], width)]
    rows.append(jnp.zeros((TAIL - len(rows), width), row.dtype))
    return jnp.concatenate(rows, axis=0)


def tail_as_row(ref, start, count):
    return jnp.concatenate([ref[start + at : start + at + 1, :] for at in range(count)], axis=1)


def row_as_column(row, width):
    parts = []
    for at in range(0, row.shape[1], width):
        parts.append(jnp.broadcast_to(row[:, at : at + width], (width, width)).T)
    return jnp.concatenate(parts, axis=0)


def column_sums(value, width):
    groups = [value[:, at : at + width] for at in range(0, value.shape[1], width)]
    partial = sum(groups[1:], groups[0])
    blocks = [
        jnp.sum(partial[at : at + width, :].T, axis=0, keepdims=True)
        for at in range(0, value.shape[0], width)
    ]
    return jnp.concatenate(blocks, axis=1)


def direct_plan_fits(mesh, queries, compact_keys):
    sizes = [mesh.shape[axis] for axis in ("page", "query", "head")]
    pages, query_devices, head_devices = sizes
    local_heads = queries.shape[0] // head_devices
    part_rows = queries.shape[1] // query_devices
    slot_rows = compact_keys.shape[1] // pages
    width = queries.shape[2]
    if any(size & (size - 1) for size in sizes) or pages < CORES or width % 128:
        return False
    if local_heads != CORES * query_devices:
        return False
    ranks = pages // CORES
    chunk = part_rows * query_devices // ranks
    return (
        part_rows * query_devices % ranks == 0
        and chunk % 128 == 0
        and part_rows % (8 * ranks) == 0
        and (part_rows // ranks % 128 == 0 or 1024 % (part_rows // ranks * 8) == 0)
        and slot_rows % width == 0
        and part_rows % width == 0
        and max(slot_rows, part_rows) < TAIL * width
    )


def direct_per_device(
    queries, compact_keys, compact_values, slot_bias, targets, positions, assignment
):
    local_heads, part_rows, width = queries.shape
    slot_rows = compact_keys.shape[1]
    query_devices = lax.axis_size("query")
    head_devices = lax.axis_size("head")
    ranks = lax.axis_size("page") // CORES
    query_rows = part_rows * query_devices
    chunk, piece = query_rows // ranks, part_rows // ranks
    turns = [ranks // 2] + [turn for turn in reversed(range(1, ranks)) if turn != ranks // 2]
    slot_total = local_heads * head_devices * slot_rows * lax.axis_size("page")
    entry_total = slot_total * width
    score_scale = 1.0 / math.sqrt(width)
    slots = CORES * slot_rows
    devices = ranks * CORES * query_devices * head_devices
    pos_rows = part_rows // width
    bias_rows = slot_rows // width
    packed_rows = 2 * slot_rows + TAIL
    packed_shapes = [(packed_rows, width)] * 2
    matmul_cost = 3 * 2 * slots * query_rows * width

    def places():
        page = lax.axis_index("page")
        return page // CORES, page % CORES, lax.axis_index("query")

    def to_device(value, **masks):
        masks = {axis: mask for axis, mask in masks.items() if mask}
        return exchange(value, **masks) if masks else value

    def pack_queries(head, rank, queries, targets, out):
        rows = pl.ds(pl.multiple_of(rank * piece, piece), piece)
        return [
            (queries.at[head], out.at[pl.ds(0, part_rows)]),
            (targets.at[head, rows], out.at[pl.ds(part_rows, piece)]),
        ]

    def pack_state(head, keys, values, out):
        return [
            (keys.at[head], out.at[pl.ds(0, slot_rows)]),
            (values.at[head], out.at[pl.ds(slot_rows, slot_rows)]),
        ]

    def start_all(copies, sems, first=0):
        copies = [
            pltpu.make_async_copy(source, target, sems.at[first + at])
            for at, (source, target) in enumerate(copies)
        ]
        for copy in copies:
            copy.start()
        return copies

    def position_tail(head, positions_ref):
        return row_as_tail(positions_ref[pl.ds(head, 1), :].astype(jnp.float32), width)

    def state_tail(head, page, bias_ref, assignment_ref):
        page_start = (assignment_ref[page] * PAGE_LEN).astype(jnp.float32)
        tail = row_as_tail(bias_ref[pl.ds(head, 1), :], width)
        return jnp.concatenate(
            [tail[: TAIL - 1], jnp.full((1, width), page_start, jnp.float32)], axis=0
        )

    def send_body(
        queries, keys, values, biases, targets, positions, assignment, state_out, *refs
    ):
        query_outs = refs[: query_devices - 1]
        bias_ref, positions_ref, assignment_ref, sems = refs[query_devices - 1 :]
        rank, core, me = places()
        heads = [CORES * (me ^ turn) + core for turn in range(1, query_devices)]
        mate_head = CORES * me + (core ^ 1)
        small = start_all(
            [(assignment, assignment_ref), (positions, positions_ref), (biases, bias_ref)], sems
        )
        copies = pack_state(mate_head, keys, values, state_out)
        for head, out in zip(heads, query_outs):
            copies += pack_queries(head, rank, queries, targets, out)
        copies = start_all(copies, sems, 3)
        for copy in small:
            copy.wait()
        state_out[2 * slot_rows :, :] = state_tail(
            mate_head, CORES * rank + core, bias_ref, assignment_ref
        )
        for head, out in zip(heads, query_outs):
            out[part_rows + piece :, :] = position_tail(head, positions_ref)
        for copy in copies:
            copy.wait()

    def own_body(
        queries, keys, values, biases, targets, positions, assignment, state_out, query_out, *refs
    ):
        bias_ref, positions_ref, assignment_ref, sems = refs
        rank, core, me = places()
        head = CORES * me + core
        small = start_all(
            [(assignment, assignment_ref), (positions, positions_ref), (biases, bias_ref)], sems
        )
        copies = pack_state(head, keys, values, state_out)
        copies += pack_queries(head, rank, queries, targets, query_out)
        copies = start_all(copies, sems, 3)
        for copy in small:
            copy.wait()
        state_out[2 * slot_rows :, :] = state_tail(
            head, CORES * rank + core, bias_ref, assignment_ref
        )
        query_out[part_rows + piece :, :] = position_tail(head, positions_ref)
        for copy in copies:
            copy.wait()

    state_shape, query_shape = (packed_rows, width), (part_rows + piece + TAIL, width)
    small_scratch = [
        pltpu.VMEM(slot_bias.shape, jnp.float32),
        pltpu.VMEM(positions.shape, jnp.int32),
        pltpu.SMEM(assignment.shape, jnp.int32),
    ]
    arguments = [
        queries, compact_keys, compact_values, slot_bias, targets, positions, assignment
    ]
    mate_state, *sent_queries = call(
        send_body,
        [state_shape] + [query_shape] * (query_devices - 1),
        "pack",
        2**20,
        arguments,
        small_scratch + [pltpu.SemaphoreType.DMA((3 + 2 * query_devices,))],
        space=pl.ANY,
        vmem=60,
    )
    own_state, own_queries = call(
        own_body,
        [state_shape, query_shape],
        "own",
        2**24,
        arguments,
        small_scratch + [pltpu.SemaphoreType.DMA((7,))],
        space=pl.ANY,
    )
    packs = [own_queries] + list(sent_queries)

    def query_part(turn, part):
        return to_device(packs[part], query=turn ^ part)

    query_parts = [query_part(0, part) for part in range(query_devices)]
    states = [own_state, exchange(mate_state, page=1)]

    def in_columns(parts, axis):
        return jnp.concatenate(
            [
                lax.slice_in_dim(part, at * piece, (at + 1) * piece, axis=axis)
                for at in range(ranks)
                for part in parts
            ],
            axis=axis,
        )

    def read_queries(query_refs):
        return halves(in_columns([ref[:part_rows, :] for ref in query_refs], 0))

    def part_of(ref, at):
        return ref.at[pl.ds(at * packed_rows, packed_rows)]

    def parts_of(refs):
        return refs if len(refs) == CORES else [part_of(refs[0], at) for at in range(CORES)]

    def step_sizes(tile_refs):
        row = jnp.sum(tile_refs[0][...], axis=0)
        return (
            RATE_KEYS / jnp.sqrt(row[:, 0:1] / entry_total + EPSILON),
            RATE_VALUES / jnp.sqrt(row[:, 1:2] / entry_total + EPSILON),
            RATE_BIAS / jnp.sqrt(row[:, 2:3] / slot_total + EPSILON),
        )

    def read_pack(ref):
        return ref[:slot_rows, :], ref[slot_rows : 2 * slot_rows, :], ref[2 * slot_rows :, :]

    def store_pack(ref, values):
        ref[:slot_rows, :] = values[0]
        ref[slot_rows : 2 * slot_rows, :] = values[1]
        ref[2 * slot_rows :, :] = values[2]

    def updated(state, grads, sizes):
        return [value - size * grad for value, grad, size in zip(state, grads, sizes)]

    def page_scores(ref, queries, positions):
        scores = dot_deep(halves(ref[:slot_rows, :]), queries, 1, 1) * score_scale
        bias = row_as_column(tail_as_row(ref, 2 * slot_rows, bias_rows), width)
        scores = scores + jnp.concatenate([bias] * (positions.shape[1] // width), axis=1)
        page_start = ref[packed_rows - 1 : packed_rows, 0:1]
        visible = jnp.broadcast_to(positions >= page_start, scores.shape)
        return jnp.where(visible, scores, MASKED), visible

    def read_positions(query_refs):
        return in_columns(
            [tail_as_row(ref, part_rows + piece, pos_rows) for ref in query_refs], 1
        )

    def split_body(*refs):
        query_refs, (halves_out, positions_out) = refs[:query_devices], refs[query_devices:]
        halves_out[...] = jnp.concatenate(read_queries(query_refs), axis=1)
        positions_out[...] = jnp.broadcast_to(read_positions(query_refs), (TAIL, query_rows))

    def read_halves(ref):
        return ref[:, :width], ref[:, width:]

    def forward(state_refs, split_refs, chunk_outs, weights_out, max_out, chunks):
        rank, _, _ = places()
        all_queries, positions = read_halves(split_refs[0]), split_refs[1][0:1, :]
        all_scores, all_visible = [], []
        for at, ref in enumerate(state_refs):
            scores, visible = page_scores(ref, all_queries, positions)
            all_scores.append(scores)
            all_visible.append(visible)
        row_max = jnp.max(all_scores[0], axis=0, keepdims=True)
        for scores in all_scores[1:]:
            row_max = jnp.maximum(row_max, jnp.max(scores, axis=0, keepdims=True))
        row_total = jnp.zeros_like(row_max)
        row_sum = jnp.zeros((width, query_rows), jnp.float32)
        for at, ref in enumerate(state_refs):
            weights = jnp.where(all_visible[at], jnp.exp(all_scores[at] - row_max), 0.0)
            weights_out[at * slot_rows : (at + 1) * slot_rows, :] = weights
            row_total = row_total + jnp.sum(weights, axis=0, keepdims=True)
            values = halves(ref[slot_rows : 2 * slot_rows, :])
            row_sum = row_sum + dot_low(values, halves(weights), 0, 0)
        max_out[...] = jnp.broadcast_to(row_max, (TAIL, query_rows))
        tail = jnp.concatenate(
            [row_max, row_total, jnp.zeros((TAIL - 2, query_rows), jnp.float32)], axis=0
        )
        for at in range(ranks):
            columns = slice(at * chunk, (at + 1) * chunk)
            chunks[at, :width, :] = row_sum[:, columns]
            chunks[at, width:, :] = tail[:, columns]
        for turn in range(ranks):
            chunk_outs[turn][...] = chunks[rank ^ turn]

    chunk_shape = (width + TAIL, chunk)
    forward_shapes = [chunk_shape] * ranks + [(slots, query_rows), (TAIL, query_rows)]
    chunk_scratch = [pltpu.VMEM((ranks,) + chunk_shape, jnp.float32)]

    fold = max(1, 128 // piece)
    folded, columns = width // fold, fold * piece
    piece_shape = (folded + TAIL, columns)
    piece_scratch = [pltpu.VMEM((ranks,) + piece_shape, jnp.float32)]

    def fold_rows(value):
        groups = [value[at * folded : (at + 1) * folded, :] for at in range(fold)]
        return jnp.concatenate(groups, axis=1)

    def unfold_rows(value):
        groups = [value[:, at * piece : (at + 1) * piece] for at in range(fold)]
        return jnp.concatenate(groups, axis=0)

    def rows_tail(rows):
        empty = jnp.zeros((TAIL - len(rows), columns), jnp.float32)
        return jnp.concatenate(rows + [empty], axis=0)

    def part_body(*refs):
        state_refs, (query_ref, *refs) = refs[:CORES], refs[CORES:]
        piece_outs, (weights_out, max_out, pieces) = refs[:ranks], refs[ranks:]
        rank, _, _ = places()
        queries = halves(query_ref[:part_rows, :])
        position_row = tail_as_row(query_ref, part_rows + piece, pos_rows)
        all_scores, all_visible = [], []
        for ref in state_refs:
            scores, visible = page_scores(ref, queries, position_row)
            all_scores.append(scores)
            all_visible.append(visible)
        row_max = jnp.max(all_scores[0], axis=0, keepdims=True)
        for scores in all_scores[1:]:
            row_max = jnp.maximum(row_max, jnp.max(scores, axis=0, keepdims=True))
        row_total = jnp.zeros_like(row_max)
        row_sum = jnp.zeros((width, part_rows), jnp.float32)
        for at, ref in enumerate(state_refs):
            weights = jnp.where(all_visible[at], jnp.exp(all_scores[at] - row_max), 0.0)
            weights_out[at * slot_rows : (at + 1) * slot_rows, :] = weights
            row_total = row_total + jnp.sum(weights, axis=0, keepdims=True)
            values = halves(ref[slot_rows : 2 * slot_rows, :])
            row_sum = row_sum + dot_low(values, halves(weights), 0, 0)
        max_out[...] = jnp.broadcast_to(row_max, (TAIL, part_rows))
        for at in range(ranks):
            own = slice(at * piece, (at + 1) * piece)
            pieces[at, :folded, :] = fold_rows(row_sum[:, own])
            pieces[at, folded:, :] = rows_tail(
                [jnp.concatenate([row[:, own]] * fold, axis=1) for row in (row_max, row_total)]
            )
        for turn in range(ranks):
            piece_outs[turn][...] = pieces[rank ^ turn]

    part_shapes = [piece_shape] * ranks + [(slots, part_rows), (TAIL, part_rows)]

    def next_body(*refs):
        state_refs, refs = refs[:2], refs[2:]
        split_refs, (pack_ref, *refs) = refs[:2], refs[2:]
        grad_refs, refs = refs[:2], refs[2:]
        tile_refs, refs = refs[: len(tiles)], refs[len(tiles) :]
        refs[0][CORES * packed_rows :, :] = pack_ref[...]
        state_outs, refs = parts_of(refs[:1]), refs[1:]
        chunk_outs, refs = refs[:ranks], refs[ranks:]
        sizes = step_sizes(tile_refs)
        for at in range(2):
            state = read_pack(state_refs[at])
            store_pack(state_outs[at], updated(state, read_pack(grad_refs[at]), sizes))
        forward(state_outs, split_refs, chunk_outs, *refs)

    def merged_chunk(query_refs, sums, maxima, totals, out):
        targets = jnp.concatenate(
            [ref[part_rows : part_rows + piece, :] for ref in query_refs], axis=0
        )
        row_max = maxima[0]
        for other in maxima[1:]:
            row_max = jnp.maximum(row_max, other)
        row_total = jnp.zeros_like(row_max)
        row_sum = jnp.zeros((width, chunk), jnp.float32)
        for part_sum, part_max, part_total in zip(sums, maxima, totals):
            factor = jnp.exp(part_max - row_max)
            row_total = row_total + part_total * factor
            row_sum = row_sum + part_sum * factor
        output = row_sum / row_total
        residual = output - targets.T
        row_delta = jnp.sum(residual * output, axis=0, keepdims=True)
        out[:width, :] = residual
        out[width:, :] = jnp.concatenate(
            [row_max, row_total, row_delta, jnp.zeros((TAIL - 3, chunk), jnp.float32)], axis=0
        )

    def first_merge_body(*refs):
        query_refs, (*piece_refs, merged_out) = refs[:query_devices], refs[query_devices:]

        def joined(read):
            return [
                jnp.concatenate([read(ref) for ref in piece_refs[turn::ranks]], axis=1)
                for turn in range(ranks)
            ]

        merged_chunk(
            query_refs,
            joined(lambda ref: unfold_rows(ref[:folded, :])),
            joined(lambda ref: ref[folded : folded + 1, :piece]),
            joined(lambda ref: ref[folded + 1 : folded + 2, :piece]),
            merged_out,
        )

    def merge_body(*refs):
        query_refs, (*chunk_refs, merged_out) = refs[:query_devices], refs[query_devices:]
        merged_chunk(
            query_refs,
            [ref[:width, :] for ref in chunk_refs],
            [ref[width : width + 1, :] for ref in chunk_refs],
            [ref[width + 1 : width + 2, :] for ref in chunk_refs],
            merged_out,
        )

    def page_gradients(weights, factor, state_ref, all_queries, residual, row_delta):
        attention = weights * factor
        grad_values = dot_narrow(halves(attention), residual, 1, 1)
        grad_probs = dot_deep(halves(state_ref[slot_rows : 2 * slot_rows, :]), residual, 1, 0)
        grad_scores = attention * (grad_probs - row_delta)
        grad_keys = dot_narrow(halves(grad_scores), all_queries, 1, 0) * score_scale
        grad_bias = column_sums(grad_scores, width)
        return grad_keys, grad_values, row_as_tail(grad_bias, width)

    def split_merged(joined):
        row_max, row_total, row_delta = (
            joined[width + at : width + at + 1, :] for at in range(3)
        )
        return halves(joined[:width, :]), row_max, row_total, row_delta

    def read_chunks(merged_refs, chunks):
        rank, _, _ = places()
        for turn, ref in zip([0] + turns[::-1], merged_refs):
            chunks[rank ^ turn] = ref[...]
        return [chunks[at] for at in range(ranks)]

    def join_body(*refs):
        *merged_refs, joined_out, chunks = refs
        joined_out[...] = jnp.concatenate(read_chunks(merged_refs, chunks), axis=1)

    def backward_body(*refs):
        weights_refs, refs = refs[: len(weights)], refs[len(weights) :]
        max_refs, refs = refs[: len(weights)], refs[len(weights) :]
        state_refs, refs = parts_of(refs[: len(states)]), refs[len(states) :]
        query_refs, refs = refs[: len(head_queries)], refs[len(head_queries) :]
        merged_refs, refs = refs[: len(all_merged)], refs[len(all_merged) :]
        grad_outs, (squares_out, *scratch) = refs[:2], refs[2:]
        if len(states) < CORES:
            joined = merged_refs[0][...]
            all_queries = read_halves(query_refs[0])
        else:
            chunks = read_chunks(merged_refs, *scratch)
            joined = jnp.concatenate(
                [
                    value[:, part * piece : (part + 1) * piece]
                    for part in range(query_devices)
                    for value in chunks
                ],
                axis=1,
            )
            all_queries = halves(
                jnp.concatenate([ref[:part_rows, :] for ref in query_refs], axis=0)
            )
        residual, row_max, row_total, row_delta = split_merged(joined)
        maxima = jnp.concatenate([ref[0:1, :] for ref in max_refs], axis=1)
        factor = jnp.exp(maxima - row_max) / row_total
        squares = [jnp.zeros((1, width), jnp.float32)] * 3
        for at, (ref, out) in enumerate(zip(state_refs, grad_outs)):
            rows = slice(at * slot_rows, (at + 1) * slot_rows)
            page_weights = jnp.concatenate([part[rows, :] for part in weights_refs], axis=1)
            grads = page_gradients(page_weights, factor, ref, all_queries, residual, row_delta)
            store_pack(out, grads)
            for which, grad in enumerate(grads):
                squares[which] = squares[which] + jnp.sum(grad * grad, axis=0, keepdims=True)
        lanes = lax.broadcasted_iota(jnp.int32, (1, width), 1)
        row = jnp.zeros((1, width), jnp.float32)
        for which, square in enumerate(squares):
            row = jnp.where(lanes == which, jnp.sum(square, axis=1, keepdims=True), row)
        for at in range(devices):
            squares_out[at] = row

    def page_body(at):
        def body(tile_ref, grad_ref, own_state_ref, *refs):
            state_refs, refs = refs[: query_devices - 1], refs[query_devices - 1 :]
            joined_refs, (*pack_refs, out) = refs[: query_devices - 1], refs[query_devices - 1 :]
            sizes = step_sizes([tile_ref])
            state = read_pack(part_of(own_state_ref, at))
            store_pack(part_of(out, 0), updated(state, read_pack(grad_ref), sizes))
            for turn, (state_ref, joined_ref) in enumerate(zip(state_refs, joined_refs), 1):
                query_refs = [state_ref.at[pl.ds(CORES * packed_rows, query_shape[0])]]
                query_refs += pack_refs[(turn - 1) * (query_devices - 1) :][: query_devices - 1]
                residual, row_max, row_total, row_delta = split_merged(joined_ref[...])
                all_queries = read_queries(query_refs)
                ref = part_of(state_ref, at)
                scores, visible = page_scores(ref, all_queries, read_positions(query_refs))
                weights = jnp.where(visible, jnp.exp(scores - row_max), 0.0)
                grads = page_gradients(
                    weights, 1.0 / row_total, ref, all_queries, residual, row_delta
                )
                store_pack(part_of(out, turn), updated(read_pack(ref), grads, sizes))

        return body

    for repeat in range(STEPS):
        last = repeat == STEPS - 1
        if repeat == 0:
            sums, weights, maxima = [], [], []
            for query_pack in query_parts:
                *pieces, part_weights, part_max = call(
                    part_body,
                    part_shapes,
                    "forward",
                    2 * matmul_cost // query_devices,
                    states + [query_pack],
                    piece_scratch,
                    after=maxima[-1:],
                )
                arrived = {
                    turn: exchange(pieces[turn], page=CORES * turn)
                    for turn in turns
                }
                sums += list(arrived.values()) + pieces[:1]
                weights.append(part_weights)
                maxima.append(part_max)
        else:
            new_state, *chunk_parts, part_weights, part_max = call(
                next_body,
                [(CORES * packed_rows + query_shape[0], width)] + forward_shapes,
                "update_forward",
                2 * matmul_cost,
                states + split_queries + [own_queries] + grads + tiles,
                chunk_scratch,
            )
            states, weights, maxima = [new_state], [part_weights], [part_max]
            arrived = {
                turn: exchange(chunk_parts[turn], page=CORES * turn)
                for turn in turns
            }
            sums = chunk_parts[:1] + list(arrived.values())
            new_states = states + [
                exchange(states[0], query=turn) for turn in range(1, query_devices)
            ]
        (merged,) = call(
            merge_body if repeat else first_merge_body,
            [chunk_shape],
            "merge",
            2**20,
            query_parts + sums,
        )
        all_merged = [merged] + [exchange(merged, page=CORES * turn) for turn in reversed(turns)]
        if last:
            all_merged = call(
                join_body, [(width + TAIL, query_rows)], "join", 2**20, all_merged, chunk_scratch
            )
            all_joined = [
                to_device(all_merged[0], query=turn) for turn in range(query_devices)
            ]
        before_backward = []
        if repeat == 0:
            half_shape = jax.ShapeDtypeStruct((query_rows, 2 * width), jnp.bfloat16)
            split_queries = call(
                split_body,
                [half_shape, (TAIL, query_rows)],
                "split_queries",
                2**20,
                query_parts,
            )
            split_queries = list(split_queries)
            before_backward = split_queries[1:]
        head_queries = split_queries[:1] if repeat else query_parts
        own_grad, mate_grad, squares = call(
            backward_body,
            packed_shapes + [(devices, 1, width)],
            "backward",
            3 * matmul_cost,
            weights + maxima + states + head_queries + list(all_merged),
            scratch=() if last else chunk_scratch,
            after=before_backward,
        )
        grads = [own_grad, mate_grad]
        tiles = [
            lax.all_to_all(
                squares, ("head", "query", "page"), split_axis=0, concat_axis=0, tiled=True
            )
        ]

    other_packs = [
        packs[part] if part == turn else query_part(turn, part)
        for turn in range(1, query_devices)
        for part in range(1, query_devices)
    ]
    operands = new_states + all_joined[1:] + other_packs
    pages = []
    for at, grad in ((1, mate_grad), (0, own_grad)):
        pages += call(
            page_body(at),
            [(query_devices * packed_rows, width)],
            "page_update",
            3 * matmul_cost // 2,
            tiles + [grad] + operands,
            after=pages,
        )
    pages = [pages[1], exchange(pages[0], page=1)]

    def last_body(*refs):
        page_refs, (keys_out, values_out, bias_out) = refs[:CORES], refs[CORES:]
        _, core, me = places()
        for turn, flip in itertools.product(range(query_devices), range(CORES)):
            keys, values, bias = read_pack(part_of(page_refs[flip], turn))
            head = CORES * (me ^ turn) + (core ^ flip)
            keys_out[head] = keys
            values_out[head] = values
            bias_row = jnp.concatenate([bias[row : row + 1] for row in range(bias_rows)], axis=1)
            bias_out[pl.ds(head, 1), :] = bias_row

    return tuple(
        call(
            last_body,
            [compact_keys.shape, compact_values.shape, slot_bias.shape],
            "unpack",
            2**20,
            pages,
        )
    )


def from_partner(value, axis, stride):
    mask = 2**stride
    pairs = [(source, source ^ mask) for source in range(lax.axis_size(axis))]
    return lax.ppermute(value, axis, pairs)


def squared_sums(grad_keys, grad_values, grad_bias):
    return jnp.stack(
        [
            jnp.sum(grad_keys * grad_keys),
            jnp.sum(grad_values * grad_values),
            jnp.sum(grad_bias * grad_bias),
        ]
    )


def apply_update(states, grads, totals, entry_count, slot_total):
    key_state, value_state, bias_state = states
    grad_keys, grad_values, grad_bias = grads
    rms_keys = jnp.sqrt(totals[0] / entry_count + EPSILON)
    rms_values = jnp.sqrt(totals[1] / entry_count + EPSILON)
    rms_bias = jnp.sqrt(totals[2] / slot_total + EPSILON)
    return (
        key_state - RATE_KEYS * grad_keys / rms_keys,
        value_state - RATE_VALUES * grad_values / rms_values,
        bias_state - RATE_BIAS * grad_bias / rms_bias,
    )


def local_gradients(queries, targets, visible, compact_keys, compact_values, slot_bias):
    score_scale = 1.0 / math.sqrt(queries.shape[2])
    scores = jnp.einsum("hqd,hsd->hqs", queries, compact_keys, precision=HIGHEST) * score_scale
    scores = jnp.where(visible, scores + slot_bias[:, None, :], MASKED)
    local_max = jnp.max(scores, axis=2)
    row_max = lax.pmax(local_max, "page")
    weights = jnp.where(visible, jnp.exp(scores - row_max[:, :, None]), 0.0)
    local_sum = jnp.einsum("hqs,hsd->hqd", weights, compact_values, precision=HIGHEST)
    row_total, row_sum = lax.psum((jnp.sum(weights, axis=2), local_sum), "page")
    attention = weights / row_total[:, :, None]
    output = row_sum / row_total[:, :, None]
    residual = output - targets
    grad_values = jnp.einsum("hqs,hqd->hsd", attention, residual, precision=HIGHEST)
    row_delta = jnp.sum(residual * output, axis=2)
    grad_probs = jnp.einsum("hqd,hsd->hqs", residual, compact_values, precision=HIGHEST)
    grad_scores = attention * (grad_probs - row_delta[:, :, None])
    grad_bias = jnp.sum(grad_scores, axis=1)
    grad_keys = jnp.einsum("hqs,hqd->hsd", grad_scores, queries, precision=HIGHEST) * score_scale
    return (grad_keys, grad_values, grad_bias)


def per_device(queries, compact_keys, compact_values, slot_bias, targets, positions, assignment):
    page_number = assignment[lax.axis_index("page")]
    local_heads = compact_keys.shape[0]
    slot_total = local_heads * lax.axis_size("head") * compact_keys.shape[1] * lax.axis_size("page")
    entry_count = slot_total * compact_keys.shape[2]
    query_count = lax.axis_size("query")
    heads_kept = max(local_heads // query_count, 1)
    query_parts = max(query_count // local_heads, 1)
    part_rows = queries.shape[1] // query_parts

    def split_items(array):
        width = array.shape[2]
        array = array.reshape(local_heads // heads_kept, heads_kept, query_parts, part_rows, width)
        array = jnp.transpose(array, (0, 2, 1, 3, 4))
        return array.reshape(query_count, heads_kept, part_rows, width)

    def join_items(array):
        width = array.shape[3]
        array = jnp.transpose(array, (1, 0, 2, 3))
        return array.reshape(heads_kept, query_count * part_rows, width)

    position_column = positions.astype(jnp.float32)[:, :, None]
    got_queries, got_targets, got_positions = (
        lax.all_to_all(split_items(queries), "query", split_axis=0, concat_axis=0, tiled=True),
        lax.all_to_all(split_items(targets), "query", split_axis=0, concat_axis=0, tiled=True),
        lax.all_to_all(
            split_items(position_column), "query", split_axis=0, concat_axis=0, tiled=True
        ),
    )
    group_queries = join_items(got_queries)
    group_targets = join_items(got_targets)
    group_positions = join_items(got_positions)[:, :, 0]
    visible = (page_number.astype(jnp.float32) <= jnp.floor(group_positions / PAGE_LEN))[:, :, None]
    query_index = lax.axis_index("query")
    first_head = query_index // query_parts * heads_kept
    key_state = lax.dynamic_slice_in_dim(compact_keys, first_head, heads_kept, 0)
    value_state = lax.dynamic_slice_in_dim(compact_values, first_head, heads_kept, 0)
    bias_state = lax.dynamic_slice_in_dim(slot_bias, first_head, heads_kept, 0)
    counted = (query_index % query_parts == 0).astype(jnp.float32)
    for repeat in range(STEPS):
        grads = local_gradients(
            group_queries, group_targets, visible, key_state, value_state, bias_state
        )
        for bit in range(query_parts.bit_length() - 1):
            partner = from_partner((grads[0], grads[1], grads[2]), "query", bit)
            grads = (grads[0] + partner[0], grads[1] + partner[1], grads[2] + partner[2])
        totals = lax.psum(
            squared_sums(grads[0], grads[1], grads[2]) * counted, ("page", "query", "head")
        )
        key_state, value_state, bias_state = apply_update(
            (key_state, value_state, bias_state), grads, totals, entry_count, slot_total
        )
    all_keys, all_values, all_bias = (
        lax.all_gather(key_state, "query", axis=0, tiled=True),
        lax.all_gather(value_state, "query", axis=0, tiled=True),
        lax.all_gather(bias_state, "query", axis=0, tiled=True),
    )
    slot_rows = compact_keys.shape[1]
    head_width = compact_keys.shape[2]
    all_keys = all_keys.reshape(
        local_heads // heads_kept, query_parts, heads_kept, slot_rows, head_width
    )[:, 0]
    all_values = all_values.reshape(
        local_heads // heads_kept, query_parts, heads_kept, slot_rows, head_width
    )[:, 0]
    all_bias = all_bias.reshape(local_heads // heads_kept, query_parts, heads_kept, slot_rows)[:, 0]
    return (
        all_keys.reshape(local_heads, slot_rows, head_width),
        all_values.reshape(local_heads, slot_rows, head_width),
        all_bias.reshape(local_heads, slot_rows),
    )


def solution(mesh):
    placed = (
        P("head", "query", None),
        P("head", "page", None),
        P("head", "page", None),
        P("head", "page"),
        P("head", "query", None),
        P("head", "query"),
        P(),
    )

    def program(*args):
        plan = direct_per_device if direct_plan_fits(mesh, args[0], args[1]) else per_device
        return jax.shard_map(
            plan,
            mesh=mesh,
            in_specs=placed,
            out_specs=(P("head", "page", None), P("head", "page", None), P("head", "page")),
            check_vma=False,
        )(*args)

    return program
```

```python
import itertools
import math

import jax
import jax.numpy as jnp
from jax import lax
from jax.experimental import pallas as pl
from jax.experimental.pallas import tpu as pltpu
from jax.sharding import PartitionSpec as P

STEPS = 2
PAGE_LEN = 32768


MASKED = -1e30
EPSILON = 1e-06
RATE_KEYS = 0.05
RATE_VALUES = 0.05
RATE_BIAS = 0.2
HIGHEST = lax.Precision.HIGHEST
TAIL = 8
CORES = 2


def exchange(value, **masks):
    axes = tuple(masks)
    sizes = [lax.axis_size(axis) for axis in axes]

    def flat(place):
        index = 0
        for size, at in zip(sizes, place):
            index = index * size + at
        return index

    pairs = [
        (flat(place), flat([at ^ mask for at, mask in zip(place, masks.values())]))
        for place in itertools.product(*map(range, sizes))
    ]
    return lax.ppermute(value, axes, pairs)


def halves(value):
    high = value.astype(jnp.bfloat16)
    return high, (value - high.astype(jnp.float32)).astype(jnp.bfloat16)


def one_pass(left, right, left_dim, right_dim):
    return lax.dot_general(
        left,
        right,
        (((left_dim,), (right_dim,)), ((), ())),
        preferred_element_type=jnp.float32,
    )


def dot_deep(left, right, left_dim, right_dim):
    left = jnp.concatenate([left[0], left[1], left[0]], axis=left_dim)
    right = jnp.concatenate([right[0], right[0], right[1]], axis=right_dim)
    return one_pass(left, right, left_dim, right_dim)


def dot_narrow(left, right, left_dim, right_dim):
    both = one_pass(
        left[0], jnp.concatenate(right, axis=1 - right_dim), left_dim, right_dim
    )
    count = both.shape[1] // 2
    cross = both[:, count:] + one_pass(left[1], right[0], left_dim, right_dim)
    return both[:, :count] + cross


def dot_low(left, right, left_dim, right_dim):
    both = one_pass(jnp.concatenate(left, axis=1 - left_dim), right[0], left_dim, right_dim)
    count = both.shape[0] // 2
    cross = both[count:, :] + one_pass(left[0], right[1], left_dim, right_dim)
    return both[:count, :] + cross


def call(body, out_shapes, name, cost, operands, scratch=(), after=(), space=pltpu.VMEM, vmem=32):
    spaces = [space] * len(operands) + [pl.ANY] * len(after)
    count = len(operands)

    def without_after(*refs):
        body(*refs[:count], *refs[count + len(after) :])

    return pl.pallas_call(
        without_after,
        out_shape=[
            shape if hasattr(shape, "dtype") else jax.ShapeDtypeStruct(shape, jnp.float32)
            for shape in out_shapes
        ],
        in_specs=[pl.BlockSpec(memory_space=space) for space in spaces],
        out_specs=[pl.BlockSpec(memory_space=pltpu.VMEM) for _ in out_shapes],
        scratch_shapes=scratch,
        compiler_params=pltpu.CompilerParams(vmem_limit_bytes=vmem * 2**20),
        cost_estimate=pl.CostEstimate(flops=cost, bytes_accessed=2**20, transcendentals=0),
        name=name,
    )(*operands, *after)


def row_as_tail(row, width):
    rows = [row[:, at : at + width] for at in range(0, row.shape[1], width)]
    rows.append(jnp.zeros((TAIL - len(rows), width), row.dtype))
    return jnp.concatenate(rows, axis=0)


def tail_as_row(ref, start, count):
    return jnp.concatenate([ref[start + at : start + at + 1, :] for at in range(count)], axis=1)


def row_as_column(row, width):
    parts = []
    for at in range(0, row.shape[1], width):
        parts.append(jnp.broadcast_to(row[:, at : at + width], (width, width)).T)
    return jnp.concatenate(parts, axis=0)


def column_sums(value, width):
    groups = [value[:, at : at + width] for at in range(0, value.shape[1], width)]
    partial = sum(groups[1:], groups[0])
    blocks = [
        jnp.sum(partial[at : at + width, :].T, axis=0, keepdims=True)
        for at in range(0, value.shape[0], width)
    ]
    return jnp.concatenate(blocks, axis=1)


def direct_plan_fits(mesh, queries, compact_keys):
    sizes = [mesh.shape[axis] for axis in ("page", "query", "head")]
    pages, query_devices, head_devices = sizes
    local_heads = queries.shape[0] // head_devices
    part_rows = queries.shape[1] // query_devices
    slot_rows = compact_keys.shape[1] // pages
    width = queries.shape[2]
    if any(size & (size - 1) for size in sizes) or pages < CORES or width % 128:
        return False
    if local_heads != CORES * query_devices:
        return False
    ranks = pages // CORES
    chunk = part_rows * query_devices // ranks
    return (
        part_rows * query_devices % ranks == 0
        and chunk % 128 == 0
        and part_rows % (8 * ranks) == 0
        and (part_rows // ranks % 128 == 0 or 1024 % (part_rows // ranks * 8) == 0)
        and slot_rows % width == 0
        and part_rows % width == 0
        and max(slot_rows, part_rows) < TAIL * width
    )


def direct_per_device(
    queries, compact_keys, compact_values, slot_bias, targets, positions, assignment
):
    local_heads, part_rows, width = queries.shape
    slot_rows = compact_keys.shape[1]
    query_devices = lax.axis_size("query")
    head_devices = lax.axis_size("head")
    ranks = lax.axis_size("page") // CORES
    query_rows = part_rows * query_devices
    chunk, piece = query_rows // ranks, part_rows // ranks
    turns = [ranks // 2] + [turn for turn in reversed(range(1, ranks)) if turn != ranks // 2]
    slot_total = local_heads * head_devices * slot_rows * lax.axis_size("page")
    entry_total = slot_total * width
    score_scale = 1.0 / math.sqrt(width)
    slots = CORES * slot_rows
    devices = ranks * CORES * query_devices * head_devices
    pos_rows = part_rows // width
    bias_rows = slot_rows // width
    packed_rows = 2 * slot_rows + TAIL
    packed_shapes = [(packed_rows, width)] * 2
    matmul_cost = 3 * 2 * slots * query_rows * width

    def places():
        page = lax.axis_index("page")
        return page // CORES, page % CORES, lax.axis_index("query")

    def to_device(value, **masks):
        masks = {axis: mask for axis, mask in masks.items() if mask}
        return exchange(value, **masks) if masks else value

    def pack_queries(head, rank, queries, targets, out):
        rows = pl.ds(pl.multiple_of(rank * piece, piece), piece)
        return [
            (queries.at[head], out.at[pl.ds(0, part_rows)]),
            (targets.at[head, rows], out.at[pl.ds(part_rows, piece)]),
        ]

    def pack_state(head, keys, values, out):
        return [
            (keys.at[head], out.at[pl.ds(0, slot_rows)]),
            (values.at[head], out.at[pl.ds(slot_rows, slot_rows)]),
        ]

    def start_all(copies, sems, first=0):
        copies = [
            pltpu.make_async_copy(source, target, sems.at[first + at])
            for at, (source, target) in enumerate(copies)
        ]
        for copy in copies:
            copy.start()
        return copies

    def position_tail(head, positions_ref):
        return row_as_tail(positions_ref[pl.ds(head, 1), :].astype(jnp.float32), width)

    def state_tail(head, page, bias_ref, assignment_ref):
        page_start = (assignment_ref[page] * PAGE_LEN).astype(jnp.float32)
        tail = row_as_tail(bias_ref[pl.ds(head, 1), :], width)
        return jnp.concatenate(
            [tail[: TAIL - 1], jnp.full((1, width), page_start, jnp.float32)], axis=0
        )

    def send_body(
        queries, keys, values, biases, targets, positions, assignment, state_out, *refs
    ):
        query_outs = refs[: query_devices - 1]
        bias_ref, positions_ref, assignment_ref, sems = refs[query_devices - 1 :]
        rank, core, me = places()
        heads = [CORES * (me ^ turn) + core for turn in range(1, query_devices)]
        mate_head = CORES * me + (core ^ 1)
        small = start_all(
            [(assignment, assignment_ref), (positions, positions_ref), (biases, bias_ref)], sems
        )
        copies = pack_state(mate_head, keys, values, state_out)
        for head, out in zip(heads, query_outs):
            copies += pack_queries(head, rank, queries, targets, out)
        copies = start_all(copies, sems, 3)
        for copy in small:
            copy.wait()
        state_out[2 * slot_rows :, :] = state_tail(
            mate_head, CORES * rank + core, bias_ref, assignment_ref
        )
        for head, out in zip(heads, query_outs):
            out[part_rows + piece :, :] = position_tail(head, positions_ref)
        for copy in copies:
            copy.wait()

    def own_body(
        queries, keys, values, biases, targets, positions, assignment, state_out, query_out, *refs
    ):
        bias_ref, positions_ref, assignment_ref, sems = refs
        rank, core, me = places()
        head = CORES * me + core
        small = start_all(
            [(assignment, assignment_ref), (positions, positions_ref), (biases, bias_ref)], sems
        )
        copies = pack_state(head, keys, values, state_out)
        copies += pack_queries(head, rank, queries, targets, query_out)
        copies = start_all(copies, sems, 3)
        for copy in small:
            copy.wait()
        state_out[2 * slot_rows :, :] = state_tail(
            head, CORES * rank + core, bias_ref, assignment_ref
        )
        query_out[part_rows + piece :, :] = position_tail(head, positions_ref)
        for copy in copies:
            copy.wait()

    state_shape, query_shape = (packed_rows, width), (part_rows + piece + TAIL, width)
    small_scratch = [
        pltpu.VMEM(slot_bias.shape, jnp.float32),
        pltpu.VMEM(positions.shape, jnp.int32),
        pltpu.SMEM(assignment.shape, jnp.int32),
    ]
    arguments = [
        queries, compact_keys, compact_values, slot_bias, targets, positions, assignment
    ]
    mate_state, *sent_queries = call(
        send_body,
        [state_shape] + [query_shape] * (query_devices - 1),
        "pack",
        2**20,
        arguments,
        small_scratch + [pltpu.SemaphoreType.DMA((3 + 2 * query_devices,))],
        space=pl.ANY,
        vmem=60,
    )
    own_state, own_queries = call(
        own_body,
        [state_shape, query_shape],
        "own",
        2**24,
        arguments,
        small_scratch + [pltpu.SemaphoreType.DMA((7,))],
        space=pl.ANY,
    )
    packs = [own_queries] + list(sent_queries)

    def query_part(turn, part):
        return to_device(packs[part], query=turn ^ part)

    query_parts = [query_part(0, part) for part in range(query_devices)]
    states = [own_state, exchange(mate_state, page=1)]

    def in_columns(parts, axis):
        return jnp.concatenate(
            [
                lax.slice_in_dim(part, at * piece, (at + 1) * piece, axis=axis)
                for at in range(ranks)
                for part in parts
            ],
            axis=axis,
        )

    def read_queries(query_refs):
        return halves(in_columns([ref[:part_rows, :] for ref in query_refs], 0))

    def part_of(ref, at):
        return ref.at[pl.ds(at * packed_rows, packed_rows)]

    def parts_of(refs):
        return refs if len(refs) == CORES else [part_of(refs[0], at) for at in range(CORES)]

    def step_sizes(tile_refs):
        row = jnp.sum(tile_refs[0][...], axis=0)
        return (
            RATE_KEYS / jnp.sqrt(row[:, 0:1] / entry_total + EPSILON),
            RATE_VALUES / jnp.sqrt(row[:, 1:2] / entry_total + EPSILON),
            RATE_BIAS / jnp.sqrt(row[:, 2:3] / slot_total + EPSILON),
        )

    def read_pack(ref):
        return ref[:slot_rows, :], ref[slot_rows : 2 * slot_rows, :], ref[2 * slot_rows :, :]

    def store_pack(ref, values):
        ref[:slot_rows, :] = values[0]
        ref[slot_rows : 2 * slot_rows, :] = values[1]
        ref[2 * slot_rows :, :] = values[2]

    def updated(state, grads, sizes):
        return [value - size * grad for value, grad, size in zip(state, grads, sizes)]

    def page_bias(ref):
        return row_as_column(tail_as_row(ref, 2 * slot_rows, bias_rows), width)

    def page_scores(ref, queries, positions, keys=None, bias=None):
        keys = halves(ref[:slot_rows, :]) if keys is None else keys
        bias = page_bias(ref) if bias is None else bias
        scores = dot_deep(keys, queries, 1, 1) * score_scale
        scores = scores + jnp.concatenate([bias] * (positions.shape[1] // width), axis=1)
        page_start = ref[packed_rows - 1 : packed_rows, 0:1]
        visible = jnp.broadcast_to(positions >= page_start, scores.shape)
        return jnp.where(visible, scores, MASKED), visible

    def read_positions(query_refs):
        return in_columns(
            [tail_as_row(ref, part_rows + piece, pos_rows) for ref in query_refs], 1
        )

    def forward(state_refs, query_refs, chunk_outs, weights_out, max_out, chunks):
        rank, _, _ = places()
        all_queries, positions = read_queries(query_refs), read_positions(query_refs)
        all_scores, all_visible = [], []
        for at, ref in enumerate(state_refs):
            scores, visible = page_scores(ref, all_queries, positions)
            all_scores.append(scores)
            all_visible.append(visible)
        row_max = jnp.max(all_scores[0], axis=0, keepdims=True)
        for scores in all_scores[1:]:
            row_max = jnp.maximum(row_max, jnp.max(scores, axis=0, keepdims=True))
        row_total = jnp.zeros_like(row_max)
        row_sum = jnp.zeros((width, query_rows), jnp.float32)
        for at, ref in enumerate(state_refs):
            weights = jnp.where(all_visible[at], jnp.exp(all_scores[at] - row_max), 0.0)
            weights_out[at * slot_rows : (at + 1) * slot_rows, :] = weights
            row_total = row_total + jnp.sum(weights, axis=0, keepdims=True)
            values = halves(ref[slot_rows : 2 * slot_rows, :])
            row_sum = row_sum + dot_low(values, halves(weights), 0, 0)
        max_out[...] = jnp.broadcast_to(row_max, (TAIL, query_rows))
        tail = jnp.concatenate(
            [row_max, row_total, jnp.zeros((TAIL - 2, query_rows), jnp.float32)], axis=0
        )
        for at in range(ranks):
            columns = slice(at * chunk, (at + 1) * chunk)
            chunks[at, :width, :] = row_sum[:, columns]
            chunks[at, width:, :] = tail[:, columns]
        for turn in range(ranks):
            chunk_outs[turn][...] = chunks[rank ^ turn]

    chunk_shape = (width + TAIL, chunk)
    forward_shapes = [chunk_shape] * ranks + [(slots, query_rows), (TAIL, query_rows)]
    chunk_scratch = [pltpu.VMEM((ranks,) + chunk_shape, jnp.float32)]

    fold = max(1, 128 // piece)
    folded, columns = width // fold, fold * piece
    piece_shape = (folded + TAIL, columns)
    piece_scratch = [pltpu.VMEM((ranks,) + piece_shape, jnp.float32)]

    def fold_rows(value):
        groups = [value[at * folded : (at + 1) * folded, :] for at in range(fold)]
        return jnp.concatenate(groups, axis=1)

    def unfold_rows(value):
        groups = [value[:, at * piece : (at + 1) * piece] for at in range(fold)]
        return jnp.concatenate(groups, axis=0)

    def rows_tail(rows):
        empty = jnp.zeros((TAIL - len(rows), columns), jnp.float32)
        return jnp.concatenate(rows + [empty], axis=0)

    def part_body(*refs):
        state_refs, (query_ref, *refs) = refs[:CORES], refs[CORES:]
        if ready:
            (split_ref, bias_ref), refs = refs[:2], refs[2:]
            piece_outs, (weights_out, max_out, pieces) = refs[:ranks], refs[ranks:]
        else:
            piece_outs, refs = refs[:ranks], refs[ranks:]
            weights_out, max_out, split_ref, bias_ref, pieces = refs
            for at, ref in enumerate(state_refs):
                rows = slice(at * slot_rows, (at + 1) * slot_rows)
                both = halves(ref[:slot_rows, :]) + halves(ref[slot_rows : 2 * slot_rows, :])
                for which, half in enumerate(both):
                    split_ref[rows, which * width : (which + 1) * width] = half
                bias_ref[rows, :] = page_bias(ref)

        def read_split(at, first):
            rows = slice(at * slot_rows, (at + 1) * slot_rows)
            return tuple(
                split_ref[rows, which * width : (which + 1) * width]
                for which in (first, first + 1)
            )

        rank, _, _ = places()
        queries = halves(query_ref[:part_rows, :])
        position_row = tail_as_row(query_ref, part_rows + piece, pos_rows)
        all_scores, all_visible = [], []
        for at, ref in enumerate(state_refs):
            bias = bias_ref[at * slot_rows : (at + 1) * slot_rows, :]
            scores, visible = page_scores(ref, queries, position_row, read_split(at, 0), bias)
            all_scores.append(scores)
            all_visible.append(visible)
        row_max = jnp.max(all_scores[0], axis=0, keepdims=True)
        for scores in all_scores[1:]:
            row_max = jnp.maximum(row_max, jnp.max(scores, axis=0, keepdims=True))
        row_total = jnp.zeros_like(row_max)
        row_sum = jnp.zeros((width, part_rows), jnp.float32)
        for at, ref in enumerate(state_refs):
            weights = jnp.where(all_visible[at], jnp.exp(all_scores[at] - row_max), 0.0)
            weights_out[at * slot_rows : (at + 1) * slot_rows, :] = weights
            row_total = row_total + jnp.sum(weights, axis=0, keepdims=True)
            row_sum = row_sum + dot_low(read_split(at, 2), halves(weights), 0, 0)
        max_out[...] = jnp.broadcast_to(row_max, (TAIL, part_rows))
        for at in range(ranks):
            own = slice(at * piece, (at + 1) * piece)
            pieces[at, :folded, :] = fold_rows(row_sum[:, own])
            pieces[at, folded:, :] = rows_tail(
                [jnp.concatenate([row[:, own]] * fold, axis=1) for row in (row_max, row_total)]
            )
        for turn in range(ranks):
            piece_outs[turn][...] = pieces[rank ^ turn]

    part_shapes = [piece_shape] * ranks + [(slots, part_rows), (TAIL, part_rows)]

    def next_body(*refs):
        state_refs, refs = refs[:2], refs[2:]
        query_refs, refs = refs[:query_devices], refs[query_devices:]
        grad_refs, refs = refs[:2], refs[2:]
        tile_refs, refs = refs[: len(tiles)], refs[len(tiles) :]
        refs[0][CORES * packed_rows :, :] = query_refs[0][...]
        state_outs, refs = parts_of(refs[:1]), refs[1:]
        chunk_outs, refs = refs[:ranks], refs[ranks:]
        sizes = step_sizes(tile_refs)
        for at in range(2):
            state = read_pack(state_refs[at])
            store_pack(state_outs[at], updated(state, read_pack(grad_refs[at]), sizes))
        forward(state_outs, query_refs, chunk_outs, *refs)

    def merged_chunk(query_refs, sums, maxima, totals, out):
        targets = jnp.concatenate(
            [ref[part_rows : part_rows + piece, :] for ref in query_refs], axis=0
        )
        row_max = maxima[0]
        for other in maxima[1:]:
            row_max = jnp.maximum(row_max, other)
        row_total = jnp.zeros_like(row_max)
        row_sum = jnp.zeros((width, chunk), jnp.float32)
        for part_sum, part_max, part_total in zip(sums, maxima, totals):
            factor = jnp.exp(part_max - row_max)
            row_total = row_total + part_total * factor
            row_sum = row_sum + part_sum * factor
        output = row_sum / row_total
        residual = output - targets.T
        row_delta = jnp.sum(residual * output, axis=0, keepdims=True)
        out[:width, :] = residual
        out[width:, :] = jnp.concatenate(
            [row_max, row_total, row_delta, jnp.zeros((TAIL - 3, chunk), jnp.float32)], axis=0
        )

    def first_merge_body(*refs):
        query_refs, (*piece_refs, merged_out) = refs[:query_devices], refs[query_devices:]

        def joined(read):
            return [
                jnp.concatenate([read(ref) for ref in piece_refs[turn::ranks]], axis=1)
                for turn in range(ranks)
            ]

        merged_chunk(
            query_refs,
            joined(lambda ref: unfold_rows(ref[:folded, :])),
            joined(lambda ref: ref[folded : folded + 1, :piece]),
            joined(lambda ref: ref[folded + 1 : folded + 2, :piece]),
            merged_out,
        )

    def merge_body(*refs):
        query_refs, (*chunk_refs, merged_out) = refs[:query_devices], refs[query_devices:]
        merged_chunk(
            query_refs,
            [ref[:width, :] for ref in chunk_refs],
            [ref[width : width + 1, :] for ref in chunk_refs],
            [ref[width + 1 : width + 2, :] for ref in chunk_refs],
            merged_out,
        )

    def page_gradients(weights, factor, state_ref, all_queries, residual, row_delta):
        attention = weights * factor
        grad_values = dot_narrow(halves(attention), residual, 1, 1)
        grad_probs = dot_deep(halves(state_ref[slot_rows : 2 * slot_rows, :]), residual, 1, 0)
        grad_scores = attention * (grad_probs - row_delta)
        grad_keys = dot_narrow(halves(grad_scores), all_queries, 1, 0) * score_scale
        grad_bias = column_sums(grad_scores, width)
        return grad_keys, grad_values, row_as_tail(grad_bias, width)

    def split_merged(joined):
        row_max, row_total, row_delta = (
            joined[width + at : width + at + 1, :] for at in range(3)
        )
        return halves(joined[:width, :]), row_max, row_total, row_delta

    def read_chunks(merged_refs, chunks):
        rank, _, _ = places()
        for turn, ref in zip([0] + turns[::-1], merged_refs):
            chunks[rank ^ turn] = ref[...]
        return [chunks[at] for at in range(ranks)]

    def join_body(*refs):
        *merged_refs, joined_out, chunks = refs
        joined_out[...] = jnp.concatenate(read_chunks(merged_refs, chunks), axis=1)

    def backward_body(*refs):
        weights_refs, refs = refs[: len(weights)], refs[len(weights) :]
        max_refs, refs = refs[: len(weights)], refs[len(weights) :]
        state_refs, refs = parts_of(refs[: len(states)]), refs[len(states) :]
        query_refs, refs = refs[:query_devices], refs[query_devices:]
        merged_refs, refs = refs[: len(all_merged)], refs[len(all_merged) :]
        grad_outs, (squares_out, *scratch) = refs[:2], refs[2:]
        if len(states) < CORES:
            joined = merged_refs[0][...]
            all_queries = read_queries(query_refs)
        else:
            chunks = read_chunks(merged_refs, *scratch)
            joined = jnp.concatenate(
                [
                    value[:, part * piece : (part + 1) * piece]
                    for part in range(query_devices)
                    for value in chunks
                ],
                axis=1,
            )
            all_queries = halves(
                jnp.concatenate([ref[:part_rows, :] for ref in query_refs], axis=0)
            )
        residual, row_max, row_total, row_delta = split_merged(joined)
        maxima = jnp.concatenate([ref[0:1, :] for ref in max_refs], axis=1)
        factor = jnp.exp(maxima - row_max) / row_total
        squares = [jnp.zeros((1, width), jnp.float32)] * 3
        for at, (ref, out) in enumerate(zip(state_refs, grad_outs)):
            rows = slice(at * slot_rows, (at + 1) * slot_rows)
            page_weights = jnp.concatenate([part[rows, :] for part in weights_refs], axis=1)
            grads = page_gradients(page_weights, factor, ref, all_queries, residual, row_delta)
            store_pack(out, grads)
            for which, grad in enumerate(grads):
                squares[which] = squares[which] + jnp.sum(grad * grad, axis=0, keepdims=True)
        lanes = lax.broadcasted_iota(jnp.int32, (1, width), 1)
        row = jnp.zeros((1, width), jnp.float32)
        for which, square in enumerate(squares):
            row = jnp.where(lanes == which, jnp.sum(square, axis=1, keepdims=True), row)
        for at in range(devices):
            squares_out[at] = row

    def page_body(at):
        def body(tile_ref, grad_ref, own_state_ref, *refs):
            state_refs, refs = refs[: query_devices - 1], refs[query_devices - 1 :]
            joined_refs, (*pack_refs, out) = refs[: query_devices - 1], refs[query_devices - 1 :]
            sizes = step_sizes([tile_ref])
            state = read_pack(part_of(own_state_ref, at))
            store_pack(part_of(out, 0), updated(state, read_pack(grad_ref), sizes))
            for turn, (state_ref, joined_ref) in enumerate(zip(state_refs, joined_refs), 1):
                query_refs = [state_ref.at[pl.ds(CORES * packed_rows, query_shape[0])]]
                query_refs += pack_refs[(turn - 1) * (query_devices - 1) :][: query_devices - 1]
                residual, row_max, row_total, row_delta = split_merged(joined_ref[...])
                all_queries = read_queries(query_refs)
                ref = part_of(state_ref, at)
                scores, visible = page_scores(ref, all_queries, read_positions(query_refs))
                weights = jnp.where(visible, jnp.exp(scores - row_max), 0.0)
                grads = page_gradients(
                    weights, 1.0 / row_total, ref, all_queries, residual, row_delta
                )
                store_pack(part_of(out, turn), updated(read_pack(ref), grads, sizes))

        return body

    for repeat in range(STEPS):
        last = repeat == STEPS - 1
        if repeat == 0:
            sums, weights, maxima = [], [], []
            split_shape = jax.ShapeDtypeStruct((slots, 4 * width), jnp.bfloat16)
            ready = []
            for query_pack in query_parts:
                outs = call(
                    part_body,
                    part_shapes + ([] if ready else [split_shape, (slots, width)]),
                    "forward",
                    2 * matmul_cost // query_devices,
                    states + [query_pack] + ready,
                    piece_scratch,
                    after=maxima[-1:],
                )
                pieces, (part_weights, part_max, *handed) = list(outs[:ranks]), outs[ranks:]
                ready = ready or handed
                arrived = {
                    turn: exchange(pieces[turn], page=CORES * turn)
                    for turn in turns
                }
                sums += list(arrived.values()) + pieces[:1]
                weights.append(part_weights)
                maxima.append(part_max)
        else:
            new_state, *chunk_parts, part_weights, part_max = call(
                next_body,
                [(CORES * packed_rows + query_shape[0], width)] + forward_shapes,
                "update_forward",
                2 * matmul_cost,
                states + query_parts + grads + tiles,
                chunk_scratch,
            )
            states, weights, maxima = [new_state], [part_weights], [part_max]
            arrived = {
                turn: exchange(chunk_parts[turn], page=CORES * turn)
                for turn in turns
            }
            sums = chunk_parts[:1] + list(arrived.values())
            new_states = states + [
                exchange(states[0], query=turn) for turn in range(1, query_devices)
            ]
        (merged,) = call(
            merge_body if repeat else first_merge_body,
            [chunk_shape],
            "merge",
            2**20,
            query_parts + sums,
        )
        all_merged = [merged] + [exchange(merged, page=CORES * turn) for turn in reversed(turns)]
        if last:
            all_merged = call(
                join_body, [(width + TAIL, query_rows)], "join", 2**20, all_merged, chunk_scratch
            )
            all_joined = [
                to_device(all_merged[0], query=turn) for turn in range(query_devices)
            ]
        own_grad, mate_grad, squares = call(
            backward_body,
            packed_shapes + [(devices, 1, width)],
            "backward",
            3 * matmul_cost,
            weights + maxima + states + query_parts + list(all_merged),
            scratch=() if last else chunk_scratch,
        )
        grads = [own_grad, mate_grad]
        tiles = [
            lax.all_to_all(
                squares, ("head", "query", "page"), split_axis=0, concat_axis=0, tiled=True
            )
        ]

    other_packs = [
        packs[part] if part == turn else query_part(turn, part)
        for turn in range(1, query_devices)
        for part in range(1, query_devices)
    ]
    operands = new_states + all_joined[1:] + other_packs
    pages = []
    for at, grad in ((1, mate_grad), (0, own_grad)):
        pages += call(
            page_body(at),
            [(query_devices * packed_rows, width)],
            "page_update",
            3 * matmul_cost // 2,
            tiles + [grad] + operands,
            after=pages,
        )
    pages = [pages[1], exchange(pages[0], page=1)]

    def last_body(*refs):
        page_refs, (keys_out, values_out, bias_out) = refs[:CORES], refs[CORES:]
        _, core, me = places()
        for turn, flip in itertools.product(range(query_devices), range(CORES)):
            keys, values, bias = read_pack(part_of(page_refs[flip], turn))
            head = CORES * (me ^ turn) + (core ^ flip)
            keys_out[head] = keys
            values_out[head] = values
            bias_row = jnp.concatenate([bias[row : row + 1] for row in range(bias_rows)], axis=1)
            bias_out[pl.ds(head, 1), :] = bias_row

    return tuple(
        call(
            last_body,
            [compact_keys.shape, compact_values.shape, slot_bias.shape],
            "unpack",
            2**20,
            pages,
        )
    )


def from_partner(value, axis, stride):
    mask = 2**stride
    pairs = [(source, source ^ mask) for source in range(lax.axis_size(axis))]
    return lax.ppermute(value, axis, pairs)


def squared_sums(grad_keys, grad_values, grad_bias):
    return jnp.stack(
        [
            jnp.sum(grad_keys * grad_keys),
            jnp.sum(grad_values * grad_values),
            jnp.sum(grad_bias * grad_bias),
        ]
    )


def apply_update(states, grads, totals, entry_count, slot_total):
    key_state, value_state, bias_state = states
    grad_keys, grad_values, grad_bias = grads
    rms_keys = jnp.sqrt(totals[0] / entry_count + EPSILON)
    rms_values = jnp.sqrt(totals[1] / entry_count + EPSILON)
    rms_bias = jnp.sqrt(totals[2] / slot_total + EPSILON)
    return (
        key_state - RATE_KEYS * grad_keys / rms_keys,
        value_state - RATE_VALUES * grad_values / rms_values,
        bias_state - RATE_BIAS * grad_bias / rms_bias,
    )


def local_gradients(queries, targets, visible, compact_keys, compact_values, slot_bias):
    score_scale = 1.0 / math.sqrt(queries.shape[2])
    scores = jnp.einsum("hqd,hsd->hqs", queries, compact_keys, precision=HIGHEST) * score_scale
    scores = jnp.where(visible, scores + slot_bias[:, None, :], MASKED)
    local_max = jnp.max(scores, axis=2)
    row_max = lax.pmax(local_max, "page")
    weights = jnp.where(visible, jnp.exp(scores - row_max[:, :, None]), 0.0)
    local_sum = jnp.einsum("hqs,hsd->hqd", weights, compact_values, precision=HIGHEST)
    row_total, row_sum = lax.psum((jnp.sum(weights, axis=2), local_sum), "page")
    attention = weights / row_total[:, :, None]
    output = row_sum / row_total[:, :, None]
    residual = output - targets
    grad_values = jnp.einsum("hqs,hqd->hsd", attention, residual, precision=HIGHEST)
    row_delta = jnp.sum(residual * output, axis=2)
    grad_probs = jnp.einsum("hqd,hsd->hqs", residual, compact_values, precision=HIGHEST)
    grad_scores = attention * (grad_probs - row_delta[:, :, None])
    grad_bias = jnp.sum(grad_scores, axis=1)
    grad_keys = jnp.einsum("hqs,hqd->hsd", grad_scores, queries, precision=HIGHEST) * score_scale
    return (grad_keys, grad_values, grad_bias)


def per_device(queries, compact_keys, compact_values, slot_bias, targets, positions, assignment):
    page_number = assignment[lax.axis_index("page")]
    local_heads = compact_keys.shape[0]
    slot_total = local_heads * lax.axis_size("head") * compact_keys.shape[1] * lax.axis_size("page")
    entry_count = slot_total * compact_keys.shape[2]
    query_count = lax.axis_size("query")
    heads_kept = max(local_heads // query_count, 1)
    query_parts = max(query_count // local_heads, 1)
    part_rows = queries.shape[1] // query_parts

    def split_items(array):
        width = array.shape[2]
        array = array.reshape(local_heads // heads_kept, heads_kept, query_parts, part_rows, width)
        array = jnp.transpose(array, (0, 2, 1, 3, 4))
        return array.reshape(query_count, heads_kept, part_rows, width)

    def join_items(array):
        width = array.shape[3]
        array = jnp.transpose(array, (1, 0, 2, 3))
        return array.reshape(heads_kept, query_count * part_rows, width)

    position_column = positions.astype(jnp.float32)[:, :, None]
    got_queries, got_targets, got_positions = (
        lax.all_to_all(split_items(queries), "query", split_axis=0, concat_axis=0, tiled=True),
        lax.all_to_all(split_items(targets), "query", split_axis=0, concat_axis=0, tiled=True),
        lax.all_to_all(
            split_items(position_column), "query", split_axis=0, concat_axis=0, tiled=True
        ),
    )
    group_queries = join_items(got_queries)
    group_targets = join_items(got_targets)
    group_positions = join_items(got_positions)[:, :, 0]
    visible = (page_number.astype(jnp.float32) <= jnp.floor(group_positions / PAGE_LEN))[:, :, None]
    query_index = lax.axis_index("query")
    first_head = query_index // query_parts * heads_kept
    key_state = lax.dynamic_slice_in_dim(compact_keys, first_head, heads_kept, 0)
    value_state = lax.dynamic_slice_in_dim(compact_values, first_head, heads_kept, 0)
    bias_state = lax.dynamic_slice_in_dim(slot_bias, first_head, heads_kept, 0)
    counted = (query_index % query_parts == 0).astype(jnp.float32)
    for repeat in range(STEPS):
        grads = local_gradients(
            group_queries, group_targets, visible, key_state, value_state, bias_state
        )
        for bit in range(query_parts.bit_length() - 1):
            partner = from_partner((grads[0], grads[1], grads[2]), "query", bit)
            grads = (grads[0] + partner[0], grads[1] + partner[1], grads[2] + partner[2])
        totals = lax.psum(
            squared_sums(grads[0], grads[1], grads[2]) * counted, ("page", "query", "head")
        )
        key_state, value_state, bias_state = apply_update(
            (key_state, value_state, bias_state), grads, totals, entry_count, slot_total
        )
    all_keys, all_values, all_bias = (
        lax.all_gather(key_state, "query", axis=0, tiled=True),
        lax.all_gather(value_state, "query", axis=0, tiled=True),
        lax.all_gather(bias_state, "query", axis=0, tiled=True),
    )
    slot_rows = compact_keys.shape[1]
    head_width = compact_keys.shape[2]
    all_keys = all_keys.reshape(
        local_heads // heads_kept, query_parts, heads_kept, slot_rows, head_width
    )[:, 0]
    all_values = all_values.reshape(
        local_heads // heads_kept, query_parts, heads_kept, slot_rows, head_width
    )[:, 0]
    all_bias = all_bias.reshape(local_heads // heads_kept, query_parts, heads_kept, slot_rows)[:, 0]
    return (
        all_keys.reshape(local_heads, slot_rows, head_width),
        all_values.reshape(local_heads, slot_rows, head_width),
        all_bias.reshape(local_heads, slot_rows),
    )


def solution(mesh):
    placed = (
        P("head", "query", None),
        P("head", "page", None),
        P("head", "page", None),
        P("head", "page"),
        P("head", "query", None),
        P("head", "query"),
        P(),
    )

    def program(*args):
        plan = direct_per_device if direct_plan_fits(mesh, args[0], args[1]) else per_device
        return jax.shard_map(
            plan,
            mesh=mesh,
            in_specs=placed,
            out_specs=(P("head", "page", None), P("head", "page", None), P("head", "page")),
            check_vma=False,
        )(*args)

    return program
```

```python
import itertools
import math

import jax
import jax.numpy as jnp
from jax import lax
from jax.experimental import pallas as pl
from jax.experimental.pallas import tpu as pltpu
from jax.sharding import PartitionSpec as P

STEPS = 2
PAGE_LEN = 32768


MASKED = -1e30
EPSILON = 1e-06
RATE_KEYS = 0.05
RATE_VALUES = 0.05
RATE_BIAS = 0.2
HIGHEST = lax.Precision.HIGHEST
TAIL = 8
CORES = 2


def exchange(value, **masks):
    axes = tuple(masks)
    sizes = [lax.axis_size(axis) for axis in axes]

    def flat(place):
        index = 0
        for size, at in zip(sizes, place):
            index = index * size + at
        return index

    pairs = [
        (flat(place), flat([at ^ mask for at, mask in zip(place, masks.values())]))
        for place in itertools.product(*map(range, sizes))
    ]
    return lax.ppermute(value, axes, pairs)


def halves(value):
    high = value.astype(jnp.bfloat16)
    return high, (value - high.astype(jnp.float32)).astype(jnp.bfloat16)


def one_pass(left, right, left_dim, right_dim):
    return lax.dot_general(
        left,
        right,
        (((left_dim,), (right_dim,)), ((), ())),
        preferred_element_type=jnp.float32,
    )


def dot_deep(left, right, left_dim, right_dim):
    left = jnp.concatenate([left[0], left[1], left[0]], axis=left_dim)
    right = jnp.concatenate([right[0], right[0], right[1]], axis=right_dim)
    return one_pass(left, right, left_dim, right_dim)


def dot_narrow(left, right, left_dim, right_dim):
    both = one_pass(
        left[0], jnp.concatenate(right, axis=1 - right_dim), left_dim, right_dim
    )
    count = both.shape[1] // 2
    cross = both[:, count:] + one_pass(left[1], right[0], left_dim, right_dim)
    return both[:, :count] + cross


def dot_low(left, right, left_dim, right_dim):
    both = one_pass(jnp.concatenate(left, axis=1 - left_dim), right[0], left_dim, right_dim)
    count = both.shape[0] // 2
    cross = both[count:, :] + one_pass(left[0], right[1], left_dim, right_dim)
    return both[:count, :] + cross


def call(body, out_shapes, name, cost, operands, scratch=(), after=(), space=pltpu.VMEM, vmem=32):
    spaces = [space] * len(operands) + [pl.ANY] * len(after)
    count = len(operands)

    def without_after(*refs):
        body(*refs[:count], *refs[count + len(after) :])

    return pl.pallas_call(
        without_after,
        out_shape=[jax.ShapeDtypeStruct(shape, jnp.float32) for shape in out_shapes],
        in_specs=[pl.BlockSpec(memory_space=space) for space in spaces],
        out_specs=[pl.BlockSpec(memory_space=pltpu.VMEM) for _ in out_shapes],
        scratch_shapes=scratch,
        compiler_params=pltpu.CompilerParams(vmem_limit_bytes=vmem * 2**20),
        cost_estimate=pl.CostEstimate(flops=cost, bytes_accessed=2**20, transcendentals=0),
        name=name,
    )(*operands, *after)


def row_as_tail(row, width):
    rows = [row[:, at : at + width] for at in range(0, row.shape[1], width)]
    rows.append(jnp.zeros((TAIL - len(rows), width), row.dtype))
    return jnp.concatenate(rows, axis=0)


def tail_as_row(ref, start, count):
    return jnp.concatenate([ref[start + at : start + at + 1, :] for at in range(count)], axis=1)


def row_as_column(row, width):
    parts = []
    for at in range(0, row.shape[1], width):
        parts.append(jnp.broadcast_to(row[:, at : at + width], (width, width)).T)
    return jnp.concatenate(parts, axis=0)


def column_sums(value, width):
    groups = [value[:, at : at + width] for at in range(0, value.shape[1], width)]
    partial = sum(groups[1:], groups[0])
    blocks = [
        jnp.sum(partial[at : at + width, :].T, axis=0, keepdims=True)
        for at in range(0, value.shape[0], width)
    ]
    return jnp.concatenate(blocks, axis=1)


def direct_plan_fits(mesh, queries, compact_keys):
    sizes = [mesh.shape[axis] for axis in ("page", "query", "head")]
    pages, query_devices, head_devices = sizes
    local_heads = queries.shape[0] // head_devices
    part_rows = queries.shape[1] // query_devices
    slot_rows = compact_keys.shape[1] // pages
    width = queries.shape[2]
    if any(size & (size - 1) for size in sizes) or pages < CORES or width % 128:
        return False
    if local_heads != CORES * query_devices:
        return False
    ranks = pages // CORES
    chunk = part_rows * query_devices // ranks
    return (
        part_rows * query_devices % ranks == 0
        and chunk % 128 == 0
        and part_rows % (8 * ranks) == 0
        and (part_rows // ranks % 128 == 0 or 1024 % (part_rows // ranks * 8) == 0)
        and slot_rows % width == 0
        and part_rows % width == 0
        and max(slot_rows, part_rows) < TAIL * width
    )


def direct_per_device(
    queries, compact_keys, compact_values, slot_bias, targets, positions, assignment
):
    local_heads, part_rows, width = queries.shape
    slot_rows = compact_keys.shape[1]
    query_devices = lax.axis_size("query")
    head_devices = lax.axis_size("head")
    ranks = lax.axis_size("page") // CORES
    query_rows = part_rows * query_devices
    chunk, piece = query_rows // ranks, part_rows // ranks
    turns = [ranks // 2] + [turn for turn in reversed(range(1, ranks)) if turn != ranks // 2]
    slot_total = local_heads * head_devices * slot_rows * lax.axis_size("page")
    entry_total = slot_total * width
    score_scale = 1.0 / math.sqrt(width)
    slots = CORES * slot_rows
    devices = ranks * CORES * query_devices * head_devices
    pos_rows = part_rows // width
    bias_rows = slot_rows // width
    packed_rows = 2 * slot_rows + TAIL
    packed_shapes = [(packed_rows, width)] * 2
    matmul_cost = 3 * 2 * slots * query_rows * width

    def places():
        page = lax.axis_index("page")
        return page // CORES, page % CORES, lax.axis_index("query")

    def to_device(value, **masks):
        masks = {axis: mask for axis, mask in masks.items() if mask}
        return exchange(value, **masks) if masks else value

    def pack_queries(head, rank, queries, targets, out):
        rows = pl.ds(pl.multiple_of(rank * piece, piece), piece)
        return [
            (queries.at[head], out.at[pl.ds(0, part_rows)]),
            (targets.at[head, rows], out.at[pl.ds(part_rows, piece)]),
        ]

    def pack_state(head, keys, values, out):
        return [
            (keys.at[head], out.at[pl.ds(0, slot_rows)]),
            (values.at[head], out.at[pl.ds(slot_rows, slot_rows)]),
        ]

    def start_all(copies, sems, first=0):
        copies = [
            pltpu.make_async_copy(source, target, sems.at[first + at])
            for at, (source, target) in enumerate(copies)
        ]
        for copy in copies:
            copy.start()
        return copies

    def position_tail(head, positions_ref):
        return row_as_tail(positions_ref[pl.ds(head, 1), :].astype(jnp.float32), width)

    def state_tail(head, page, bias_ref, assignment_ref):
        page_start = (assignment_ref[page] * PAGE_LEN).astype(jnp.float32)
        tail = row_as_tail(bias_ref[pl.ds(head, 1), :], width)
        return jnp.concatenate(
            [tail[: TAIL - 1], jnp.full((1, width), page_start, jnp.float32)], axis=0
        )

    def send_body(
        queries, keys, values, biases, targets, positions, assignment, state_out, *refs
    ):
        query_outs = refs[: query_devices - 1]
        bias_ref, positions_ref, assignment_ref, sems = refs[query_devices - 1 :]
        rank, core, me = places()
        heads = [CORES * (me ^ turn) + core for turn in range(1, query_devices)]
        mate_head = CORES * me + (core ^ 1)
        small = start_all(
            [(assignment, assignment_ref), (positions, positions_ref), (biases, bias_ref)], sems
        )
        copies = pack_state(mate_head, keys, values, state_out)
        for head, out in zip(heads, query_outs):
            copies += pack_queries(head, rank, queries, targets, out)
        copies = start_all(copies, sems, 3)
        for copy in small:
            copy.wait()
        state_out[2 * slot_rows :, :] = state_tail(
            mate_head, CORES * rank + core, bias_ref, assignment_ref
        )
        for head, out in zip(heads, query_outs):
            out[part_rows + piece :, :] = position_tail(head, positions_ref)
        for copy in copies:
            copy.wait()

    def own_body(
        queries, keys, values, biases, targets, positions, assignment, state_out, query_out, *refs
    ):
        bias_ref, positions_ref, assignment_ref, sems = refs
        rank, core, me = places()
        head = CORES * me + core
        small = start_all(
            [(assignment, assignment_ref), (positions, positions_ref), (biases, bias_ref)], sems
        )
        copies = pack_state(head, keys, values, state_out)
        copies += pack_queries(head, rank, queries, targets, query_out)
        copies = start_all(copies, sems, 3)
        for copy in small:
            copy.wait()
        state_out[2 * slot_rows :, :] = state_tail(
            head, CORES * rank + core, bias_ref, assignment_ref
        )
        query_out[part_rows + piece :, :] = position_tail(head, positions_ref)
        for copy in copies:
            copy.wait()

    state_shape, query_shape = (packed_rows, width), (part_rows + piece + TAIL, width)
    small_scratch = [
        pltpu.VMEM(slot_bias.shape, jnp.float32),
        pltpu.VMEM(positions.shape, jnp.int32),
        pltpu.SMEM(assignment.shape, jnp.int32),
    ]
    arguments = [
        queries, compact_keys, compact_values, slot_bias, targets, positions, assignment
    ]
    mate_state, *sent_queries = call(
        send_body,
        [state_shape] + [query_shape] * (query_devices - 1),
        "pack",
        2**20,
        arguments,
        small_scratch + [pltpu.SemaphoreType.DMA((3 + 2 * query_devices,))],
        space=pl.ANY,
        vmem=60,
    )
    own_state, own_queries = call(
        own_body,
        [state_shape, query_shape],
        "own",
        2**24,
        arguments,
        small_scratch + [pltpu.SemaphoreType.DMA((7,))],
        space=pl.ANY,
    )
    packs = [own_queries] + list(sent_queries)

    def query_part(turn, part):
        return to_device(packs[part], query=turn ^ part)

    query_parts = [query_part(0, part) for part in range(query_devices)]
    states = [own_state, exchange(mate_state, page=1)]

    def in_columns(parts, axis):
        return jnp.concatenate(
            [
                lax.slice_in_dim(part, at * piece, (at + 1) * piece, axis=axis)
                for at in range(ranks)
                for part in parts
            ],
            axis=axis,
        )

    def read_queries(query_refs):
        return halves(in_columns([ref[:part_rows, :] for ref in query_refs], 0))

    def part_of(ref, at):
        return ref.at[pl.ds(at * packed_rows, packed_rows)]

    def parts_of(refs):
        return refs if len(refs) == CORES else [part_of(refs[0], at) for at in range(CORES)]

    def step_sizes(tile_refs):
        row = jnp.sum(tile_refs[0][...], axis=0)
        return (
            RATE_KEYS / jnp.sqrt(row[:, 0:1] / entry_total + EPSILON),
            RATE_VALUES / jnp.sqrt(row[:, 1:2] / entry_total + EPSILON),
            RATE_BIAS / jnp.sqrt(row[:, 2:3] / slot_total + EPSILON),
        )

    def read_pack(ref):
        return ref[:slot_rows, :], ref[slot_rows : 2 * slot_rows, :], ref[2 * slot_rows :, :]

    def store_pack(ref, values):
        ref[:slot_rows, :] = values[0]
        ref[slot_rows : 2 * slot_rows, :] = values[1]
        ref[2 * slot_rows :, :] = values[2]

    def updated(state, grads, sizes):
        return [value - size * grad for value, grad, size in zip(state, grads, sizes)]

    def page_scores(ref, queries, positions):
        scores = dot_deep(halves(ref[:slot_rows, :]), queries, 1, 1) * score_scale
        bias = row_as_column(tail_as_row(ref, 2 * slot_rows, bias_rows), width)
        scores = scores + jnp.concatenate([bias] * (positions.shape[1] // width), axis=1)
        page_start = ref[packed_rows - 1 : packed_rows, 0:1]
        visible = jnp.broadcast_to(positions >= page_start, scores.shape)
        return jnp.where(visible, scores, MASKED), visible

    def read_positions(query_refs):
        return in_columns(
            [tail_as_row(ref, part_rows + piece, pos_rows) for ref in query_refs], 1
        )

    def forward(state_refs, query_refs, chunk_outs, weights_out, max_out, chunks):
        rank, _, _ = places()
        all_queries, positions = read_queries(query_refs), read_positions(query_refs)
        all_scores, all_visible = [], []
        for at, ref in enumerate(state_refs):
            scores, visible = page_scores(ref, all_queries, positions)
            all_scores.append(scores)
            all_visible.append(visible)
        row_max = jnp.max(all_scores[0], axis=0, keepdims=True)
        for scores in all_scores[1:]:
            row_max = jnp.maximum(row_max, jnp.max(scores, axis=0, keepdims=True))
        row_total = jnp.zeros_like(row_max)
        row_sum = jnp.zeros((width, query_rows), jnp.float32)
        for at, ref in enumerate(state_refs):
            weights = jnp.where(all_visible[at], jnp.exp(all_scores[at] - row_max), 0.0)
            weights_out[at * slot_rows : (at + 1) * slot_rows, :] = weights
            row_total = row_total + jnp.sum(weights, axis=0, keepdims=True)
            values = halves(ref[slot_rows : 2 * slot_rows, :])
            row_sum = row_sum + dot_low(values, halves(weights), 0, 0)
        max_out[...] = jnp.broadcast_to(row_max, (TAIL, query_rows))
        tail = jnp.concatenate(
            [row_max, row_total, jnp.zeros((TAIL - 2, query_rows), jnp.float32)], axis=0
        )
        for at in range(ranks):
            columns = slice(at * chunk, (at + 1) * chunk)
            chunks[at, :width, :] = row_sum[:, columns]
            chunks[at, width:, :] = tail[:, columns]
        for turn in range(ranks):
            chunk_outs[turn][...] = chunks[rank ^ turn]

    chunk_shape = (width + TAIL, chunk)
    forward_shapes = [chunk_shape] * ranks + [(slots, query_rows), (TAIL, query_rows)]
    chunk_scratch = [pltpu.VMEM((ranks,) + chunk_shape, jnp.float32)]

    fold = max(1, 128 // piece)
    folded, columns = width // fold, fold * piece
    piece_shape = (folded + TAIL, columns)
    piece_scratch = [pltpu.VMEM((ranks,) + piece_shape, jnp.float32)]

    def fold_rows(value):
        groups = [value[at * folded : (at + 1) * folded, :] for at in range(fold)]
        return jnp.concatenate(groups, axis=1)

    def unfold_rows(value):
        groups = [value[:, at * piece : (at + 1) * piece] for at in range(fold)]
        return jnp.concatenate(groups, axis=0)

    def rows_tail(rows):
        empty = jnp.zeros((TAIL - len(rows), columns), jnp.float32)
        return jnp.concatenate(rows + [empty], axis=0)

    def part_body(*refs):
        state_refs, (query_ref, *refs) = refs[:CORES], refs[CORES:]
        piece_outs, (weights_out, max_out, pieces) = refs[:ranks], refs[ranks:]
        rank, _, _ = places()
        queries = halves(query_ref[:part_rows, :])
        position_row = tail_as_row(query_ref, part_rows + piece, pos_rows)
        all_scores, all_visible = [], []
        for ref in state_refs:
            scores, visible = page_scores(ref, queries, position_row)
            all_scores.append(scores)
            all_visible.append(visible)
        row_max = jnp.max(all_scores[0], axis=0, keepdims=True)
        for scores in all_scores[1:]:
            row_max = jnp.maximum(row_max, jnp.max(scores, axis=0, keepdims=True))
        row_total = jnp.zeros_like(row_max)
        row_sum = jnp.zeros((width, part_rows), jnp.float32)
        for at, ref in enumerate(state_refs):
            weights = jnp.where(all_visible[at], jnp.exp(all_scores[at] - row_max), 0.0)
            weights_out[at * slot_rows : (at + 1) * slot_rows, :] = weights
            row_total = row_total + jnp.sum(weights, axis=0, keepdims=True)
            values = halves(ref[slot_rows : 2 * slot_rows, :])
            row_sum = row_sum + dot_low(values, halves(weights), 0, 0)
        max_out[...] = jnp.broadcast_to(row_max, (TAIL, part_rows))
        for at in range(ranks):
            own = slice(at * piece, (at + 1) * piece)
            pieces[at, :folded, :] = fold_rows(row_sum[:, own])
            pieces[at, folded:, :] = rows_tail(
                [jnp.concatenate([row[:, own]] * fold, axis=1) for row in (row_max, row_total)]
            )
        for turn in range(ranks):
            piece_outs[turn][...] = pieces[rank ^ turn]

    part_shapes = [piece_shape] * ranks + [(slots, part_rows), (TAIL, part_rows)]

    def next_body(*refs):
        state_refs, refs = refs[:2], refs[2:]
        query_refs, refs = refs[:query_devices], refs[query_devices:]
        grad_refs, refs = refs[:2], refs[2:]
        tile_refs, refs = refs[: len(tiles)], refs[len(tiles) :]
        refs[0][CORES * packed_rows :, :] = query_refs[0][...]
        state_outs, refs = parts_of(refs[:1]), refs[1:]
        chunk_outs, refs = refs[:ranks], refs[ranks:]
        sizes = step_sizes(tile_refs)
        for at in range(2):
            state = read_pack(state_refs[at])
            store_pack(state_outs[at], updated(state, read_pack(grad_refs[at]), sizes))
        forward(state_outs, query_refs, chunk_outs, *refs)

    def merged_sums(sums, maxima, totals):
        row_max = maxima[0]
        for other in maxima[1:]:
            row_max = jnp.maximum(row_max, other)
        row_total, row_sum = jnp.zeros_like(row_max), jnp.zeros_like(sums[0])
        for part_sum, part_max, part_total in zip(sums, maxima, totals):
            factor = jnp.exp(part_max - row_max)
            row_total = row_total + part_total * factor
            row_sum = row_sum + part_sum * factor
        return row_sum / row_total, row_max, row_total

    def store_chunk(query_refs, output, row_max, row_total, out):
        targets = jnp.concatenate(
            [ref[part_rows : part_rows + piece, :] for ref in query_refs], axis=0
        )
        residual = output - targets.T
        row_delta = jnp.sum(residual * output, axis=0, keepdims=True)
        out[:width, :] = residual
        out[width:, :] = jnp.concatenate(
            [row_max, row_total, row_delta, jnp.zeros((TAIL - 3, chunk), jnp.float32)], axis=0
        )

    def read_sums(refs, rows):
        return [
            [ref[:rows, :] for ref in refs],
            [ref[rows : rows + 1, :] for ref in refs],
            [ref[rows + 1 : rows + 2, :] for ref in refs],
        ]

    def first_merge_body(*refs):
        query_refs, (*piece_refs, merged_out) = refs[:query_devices], refs[query_devices:]
        parts = []
        for part in range(query_devices):
            group = piece_refs[part * ranks : (part + 1) * ranks]
            output, row_max, row_total = merged_sums(*read_sums(group, folded))
            parts.append((unfold_rows(output), row_max[:, :piece], row_total[:, :piece]))
        joined = [jnp.concatenate(values, axis=1) for values in zip(*parts)]
        store_chunk(query_refs, *joined, merged_out)

    def merge_body(*refs):
        query_refs, (*chunk_refs, merged_out) = refs[:query_devices], refs[query_devices:]
        store_chunk(query_refs, *merged_sums(*read_sums(chunk_refs, width)), merged_out)

    def page_gradients(weights, factor, state_ref, all_queries, residual, row_delta):
        attention = weights * factor
        grad_values = dot_narrow(halves(attention), residual, 1, 1)
        grad_probs = dot_deep(halves(state_ref[slot_rows : 2 * slot_rows, :]), residual, 1, 0)
        grad_scores = attention * (grad_probs - row_delta)
        grad_keys = dot_narrow(halves(grad_scores), all_queries, 1, 0) * score_scale
        grad_bias = column_sums(grad_scores, width)
        return grad_keys, grad_values, row_as_tail(grad_bias, width)

    def split_merged(joined):
        row_max, row_total, row_delta = (
            joined[width + at : width + at + 1, :] for at in range(3)
        )
        return halves(joined[:width, :]), row_max, row_total, row_delta

    def read_chunks(merged_refs, chunks):
        rank, _, _ = places()
        for turn, ref in zip([0] + turns[::-1], merged_refs):
            chunks[rank ^ turn] = ref[...]
        return [chunks[at] for at in range(ranks)]

    def join_body(*refs):
        *merged_refs, joined_out, chunks = refs
        joined_out[...] = jnp.concatenate(read_chunks(merged_refs, chunks), axis=1)

    def backward_body(*refs):
        weights_refs, refs = refs[: len(weights)], refs[len(weights) :]
        max_refs, refs = refs[: len(weights)], refs[len(weights) :]
        state_refs, refs = parts_of(refs[: len(states)]), refs[len(states) :]
        query_refs, refs = refs[:query_devices], refs[query_devices:]
        merged_refs, refs = refs[: len(all_merged)], refs[len(all_merged) :]
        grad_outs, (squares_out, *scratch) = refs[:2], refs[2:]
        if len(states) < CORES:
            joined = merged_refs[0][...]
            all_queries = read_queries(query_refs)
        else:
            chunks = read_chunks(merged_refs, *scratch)
            joined = jnp.concatenate(
                [
                    value[:, part * piece : (part + 1) * piece]
                    for part in range(query_devices)
                    for value in chunks
                ],
                axis=1,
            )
            all_queries = halves(
                jnp.concatenate([ref[:part_rows, :] for ref in query_refs], axis=0)
            )
        residual, row_max, row_total, row_delta = split_merged(joined)
        maxima = jnp.concatenate([ref[0:1, :] for ref in max_refs], axis=1)
        factor = jnp.exp(maxima - row_max) / row_total
        squares = [jnp.zeros((1, width), jnp.float32)] * 3
        for at, (ref, out) in enumerate(zip(state_refs, grad_outs)):
            rows = slice(at * slot_rows, (at + 1) * slot_rows)
            page_weights = jnp.concatenate([part[rows, :] for part in weights_refs], axis=1)
            grads = page_gradients(page_weights, factor, ref, all_queries, residual, row_delta)
            store_pack(out, grads)
            for which, grad in enumerate(grads):
                squares[which] = squares[which] + jnp.sum(grad * grad, axis=0, keepdims=True)
        lanes = lax.broadcasted_iota(jnp.int32, (1, width), 1)
        row = jnp.zeros((1, width), jnp.float32)
        for which, square in enumerate(squares):
            row = jnp.where(lanes == which, jnp.sum(square, axis=1, keepdims=True), row)
        for at in range(devices):
            squares_out[at] = row

    def page_body(at):
        def body(tile_ref, grad_ref, own_state_ref, *refs):
            state_refs, refs = refs[: query_devices - 1], refs[query_devices - 1 :]
            joined_refs, (*pack_refs, out) = refs[: query_devices - 1], refs[query_devices - 1 :]
            sizes = step_sizes([tile_ref])
            state = read_pack(part_of(own_state_ref, at))
            store_pack(part_of(out, 0), updated(state, read_pack(grad_ref), sizes))
            for turn, (state_ref, joined_ref) in enumerate(zip(state_refs, joined_refs), 1):
                query_refs = [state_ref.at[pl.ds(CORES * packed_rows, query_shape[0])]]
                query_refs += pack_refs[(turn - 1) * (query_devices - 1) :][: query_devices - 1]
                residual, row_max, row_total, row_delta = split_merged(joined_ref[...])
                all_queries = read_queries(query_refs)
                ref = part_of(state_ref, at)
                scores, visible = page_scores(ref, all_queries, read_positions(query_refs))
                weights = jnp.where(visible, jnp.exp(scores - row_max), 0.0)
                grads = page_gradients(
                    weights, 1.0 / row_total, ref, all_queries, residual, row_delta
                )
                store_pack(part_of(out, turn), updated(read_pack(ref), grads, sizes))

        return body

    for repeat in range(STEPS):
        last = repeat == STEPS - 1
        if repeat == 0:
            sums, weights, maxima = [], [], []
            for query_pack in query_parts:
                *pieces, part_weights, part_max = call(
                    part_body,
                    part_shapes,
                    "forward",
                    2 * matmul_cost // query_devices,
                    states + [query_pack],
                    piece_scratch,
                    after=maxima[-1:],
                )
                arrived = {
                    turn: exchange(pieces[turn], page=CORES * turn)
                    for turn in turns
                }
                sums += list(arrived.values()) + pieces[:1]
                weights.append(part_weights)
                maxima.append(part_max)
        else:
            new_state, *chunk_parts, part_weights, part_max = call(
                next_body,
                [(CORES * packed_rows + query_shape[0], width)] + forward_shapes,
                "update_forward",
                2 * matmul_cost,
                states + query_parts + grads + tiles,
                chunk_scratch,
            )
            states, weights, maxima = [new_state], [part_weights], [part_max]
            arrived = {
                turn: exchange(chunk_parts[turn], page=CORES * turn)
                for turn in turns
            }
            sums = chunk_parts[:1] + list(arrived.values())
            new_states = states + [
                exchange(states[0], query=turn) for turn in range(1, query_devices)
            ]
        (merged,) = call(
            merge_body if repeat else first_merge_body,
            [chunk_shape],
            "merge",
            2**20,
            query_parts + sums,
        )
        all_merged = [merged] + [exchange(merged, page=CORES * turn) for turn in reversed(turns)]
        if last:
            all_merged = call(
                join_body, [(width + TAIL, query_rows)], "join", 2**20, all_merged, chunk_scratch
            )
            all_joined = [
                to_device(all_merged[0], query=turn) for turn in range(query_devices)
            ]
        own_grad, mate_grad, squares = call(
            backward_body,
            packed_shapes + [(devices, 1, width)],
            "backward",
            3 * matmul_cost,
            weights + maxima + states + query_parts + list(all_merged),
            scratch=() if last else chunk_scratch,
        )
        grads = [own_grad, mate_grad]
        tiles = [
            lax.all_to_all(
                squares, ("head", "query", "page"), split_axis=0, concat_axis=0, tiled=True
            )
        ]

    other_packs = [
        packs[part] if part == turn else query_part(turn, part)
        for turn in range(1, query_devices)
        for part in range(1, query_devices)
    ]
    operands = new_states + all_joined[1:] + other_packs
    pages = []
    for at, grad in ((1, mate_grad), (0, own_grad)):
        pages += call(
            page_body(at),
            [(query_devices * packed_rows, width)],
            "page_update",
            3 * matmul_cost // 2,
            tiles + [grad] + operands,
            after=pages,
        )
    pages = [pages[1], exchange(pages[0], page=1)]

    def last_body(*refs):
        page_refs, (keys_out, values_out, bias_out) = refs[:CORES], refs[CORES:]
        _, core, me = places()
        for turn, flip in itertools.product(range(query_devices), range(CORES)):
            keys, values, bias = read_pack(part_of(page_refs[flip], turn))
            head = CORES * (me ^ turn) + (core ^ flip)
            keys_out[head] = keys
            values_out[head] = values
            bias_row = jnp.concatenate([bias[row : row + 1] for row in range(bias_rows)], axis=1)
            bias_out[pl.ds(head, 1), :] = bias_row

    return tuple(
        call(
            last_body,
            [compact_keys.shape, compact_values.shape, slot_bias.shape],
            "unpack",
            2**20,
            pages,
        )
    )


def from_partner(value, axis, stride):
    mask = 2**stride
    pairs = [(source, source ^ mask) for source in range(lax.axis_size(axis))]
    return lax.ppermute(value, axis, pairs)


def squared_sums(grad_keys, grad_values, grad_bias):
    return jnp.stack(
        [
            jnp.sum(grad_keys * grad_keys),
            jnp.sum(grad_values * grad_values),
            jnp.sum(grad_bias * grad_bias),
        ]
    )


def apply_update(states, grads, totals, entry_count, slot_total):
    key_state, value_state, bias_state = states
    grad_keys, grad_values, grad_bias = grads
    rms_keys = jnp.sqrt(totals[0] / entry_count + EPSILON)
    rms_values = jnp.sqrt(totals[1] / entry_count + EPSILON)
    rms_bias = jnp.sqrt(totals[2] / slot_total + EPSILON)
    return (
        key_state - RATE_KEYS * grad_keys / rms_keys,
        value_state - RATE_VALUES * grad_values / rms_values,
        bias_state - RATE_BIAS * grad_bias / rms_bias,
    )


def local_gradients(queries, targets, visible, compact_keys, compact_values, slot_bias):
    score_scale = 1.0 / math.sqrt(queries.shape[2])
    scores = jnp.einsum("hqd,hsd->hqs", queries, compact_keys, precision=HIGHEST) * score_scale
    scores = jnp.where(visible, scores + slot_bias[:, None, :], MASKED)
    local_max = jnp.max(scores, axis=2)
    row_max = lax.pmax(local_max, "page")
    weights = jnp.where(visible, jnp.exp(scores - row_max[:, :, None]), 0.0)
    local_sum = jnp.einsum("hqs,hsd->hqd", weights, compact_values, precision=HIGHEST)
    row_total, row_sum = lax.psum((jnp.sum(weights, axis=2), local_sum), "page")
    attention = weights / row_total[:, :, None]
    output = row_sum / row_total[:, :, None]
    residual = output - targets
    grad_values = jnp.einsum("hqs,hqd->hsd", attention, residual, precision=HIGHEST)
    row_delta = jnp.sum(residual * output, axis=2)
    grad_probs = jnp.einsum("hqd,hsd->hqs", residual, compact_values, precision=HIGHEST)
    grad_scores = attention * (grad_probs - row_delta[:, :, None])
    grad_bias = jnp.sum(grad_scores, axis=1)
    grad_keys = jnp.einsum("hqs,hqd->hsd", grad_scores, queries, precision=HIGHEST) * score_scale
    return (grad_keys, grad_values, grad_bias)


def per_device(queries, compact_keys, compact_values, slot_bias, targets, positions, assignment):
    page_number = assignment[lax.axis_index("page")]
    local_heads = compact_keys.shape[0]
    slot_total = local_heads * lax.axis_size("head") * compact_keys.shape[1] * lax.axis_size("page")
    entry_count = slot_total * compact_keys.shape[2]
    query_count = lax.axis_size("query")
    heads_kept = max(local_heads // query_count, 1)
    query_parts = max(query_count // local_heads, 1)
    part_rows = queries.shape[1] // query_parts

    def split_items(array):
        width = array.shape[2]
        array = array.reshape(local_heads // heads_kept, heads_kept, query_parts, part_rows, width)
        array = jnp.transpose(array, (0, 2, 1, 3, 4))
        return array.reshape(query_count, heads_kept, part_rows, width)

    def join_items(array):
        width = array.shape[3]
        array = jnp.transpose(array, (1, 0, 2, 3))
        return array.reshape(heads_kept, query_count * part_rows, width)

    position_column = positions.astype(jnp.float32)[:, :, None]
    got_queries, got_targets, got_positions = (
        lax.all_to_all(split_items(queries), "query", split_axis=0, concat_axis=0, tiled=True),
        lax.all_to_all(split_items(targets), "query", split_axis=0, concat_axis=0, tiled=True),
        lax.all_to_all(
            split_items(position_column), "query", split_axis=0, concat_axis=0, tiled=True
        ),
    )
    group_queries = join_items(got_queries)
    group_targets = join_items(got_targets)
    group_positions = join_items(got_positions)[:, :, 0]
    visible = (page_number.astype(jnp.float32) <= jnp.floor(group_positions / PAGE_LEN))[:, :, None]
    query_index = lax.axis_index("query")
    first_head = query_index // query_parts * heads_kept
    key_state = lax.dynamic_slice_in_dim(compact_keys, first_head, heads_kept, 0)
    value_state = lax.dynamic_slice_in_dim(compact_values, first_head, heads_kept, 0)
    bias_state = lax.dynamic_slice_in_dim(slot_bias, first_head, heads_kept, 0)
    counted = (query_index % query_parts == 0).astype(jnp.float32)
    for repeat in range(STEPS):
        grads = local_gradients(
            group_queries, group_targets, visible, key_state, value_state, bias_state
        )
        for bit in range(query_parts.bit_length() - 1):
            partner = from_partner((grads[0], grads[1], grads[2]), "query", bit)
            grads = (grads[0] + partner[0], grads[1] + partner[1], grads[2] + partner[2])
        totals = lax.psum(
            squared_sums(grads[0], grads[1], grads[2]) * counted, ("page", "query", "head")
        )
        key_state, value_state, bias_state = apply_update(
            (key_state, value_state, bias_state), grads, totals, entry_count, slot_total
        )
    all_keys, all_values, all_bias = (
        lax.all_gather(key_state, "query", axis=0, tiled=True),
        lax.all_gather(value_state, "query", axis=0, tiled=True),
        lax.all_gather(bias_state, "query", axis=0, tiled=True),
    )
    slot_rows = compact_keys.shape[1]
    head_width = compact_keys.shape[2]
    all_keys = all_keys.reshape(
        local_heads // heads_kept, query_parts, heads_kept, slot_rows, head_width
    )[:, 0]
    all_values = all_values.reshape(
        local_heads // heads_kept, query_parts, heads_kept, slot_rows, head_width
    )[:, 0]
    all_bias = all_bias.reshape(local_heads // heads_kept, query_parts, heads_kept, slot_rows)[:, 0]
    return (
        all_keys.reshape(local_heads, slot_rows, head_width),
        all_values.reshape(local_heads, slot_rows, head_width),
        all_bias.reshape(local_heads, slot_rows),
    )


def solution(mesh):
    placed = (
        P("head", "query", None),
        P("head", "page", None),
        P("head", "page", None),
        P("head", "page"),
        P("head", "query", None),
        P("head", "query"),
        P(),
    )

    def program(*args):
        plan = direct_per_device if direct_plan_fits(mesh, args[0], args[1]) else per_device
        return jax.shard_map(
            plan,
            mesh=mesh,
            in_specs=placed,
            out_specs=(P("head", "page", None), P("head", "page", None), P("head", "page")),
            check_vma=False,
        )(*args)

    return program
```
